32 devices in a mesh: seq: 4 (over z), fsdp: 8 (over y, x, core).
Axes of the slice: x: 2, y: 2, z: 4, core: 2. Of those that a mesh axis runs over, the one named last changes fastest.
Arguments:
- tokens: bfloat16 [4096, 1536], P(('seq', 'fsdp')), may hold values from -6 to 6
- teacher: bfloat16 [4096, 1536], P(('seq', 'fsdp')), may hold values from -6 to 6
- valid: int32 [4096], P(('seq', 'fsdp')), may hold values from 0 to 1
- routes: int32 [4096, 2], P(('seq', 'fsdp')), may hold values from 0 to 3, as said below
- slots: int32 [4096, 2], P(('seq', 'fsdp')), may hold values from 0 to 127, as said below
- gain_attn: bfloat16 [1536], P('fsdp'), may hold values from 0.5 to 1.5
- w_query: bfloat16 [1536, 1536], P('fsdp'), may hold values from -0.15625 to 0.15625
- w_keyval: bfloat16 [1536, 1024], P('fsdp'), may hold values from -0.15625 to 0.15625
- w_out: bfloat16 [1536, 1536], P(None, 'fsdp'), may hold values from -6 to 6
- gain_ffn: bfloat16 [1536], P('fsdp'), may hold values from 0.5 to 1.5
- w_router: bfloat16 [1536, 4], P('fsdp'), may hold values from -0.3125 to 0.3125
- w_gate_up: bfloat16 [4, 1536, 2048], P(None, 'fsdp'), may hold values from -0.15625 to 0.15625
- w_down: bfloat16 [4, 1024, 1536], P(None, None, 'fsdp'), may hold values from -0.1875 to 0.1875
Outputs:
- mixed: bfloat16 [4096, 1536], P(('seq', 'fsdp'))
- loss: float32 [], replicated
- grad_tokens: float32 [4096, 1536], P(('seq', 'fsdp'))
- grad_gain_attn: float32 [1536], P('fsdp')
- grad_query: float32 [1536, 1536], P('fsdp')
- grad_keyval: float32 [1536, 1024], P('fsdp')
- grad_out: float32 [1536, 1536], P(None, 'fsdp')
- grad_gain_ffn: float32 [1536], P('fsdp')
- grad_router: float32 [1536, 4], P('fsdp')
- grad_gate_up: float32 [4, 1536, 2048], P(None, 'fsdp')
- grad_down: float32 [4, 1024, 1536], P(None, None, 'fsdp')
The draws below stay inside these ranges and needn't reach their ends.
Inputs may be any that keep to these rules, and one draw needn't show every extreme that they name: `routes`: each row names 2 different experts. In each aligned block of 128 rows (the rows of one device) some expert is named by every row. In each aligned block of 128 rows, the rows that name an expert carry the slots 0, 1, ... up to their number - 1 for it, each once.
All inputs are finite; a program needn't handle non-finite values.
Results may differ from the reference program's by a relative error of at most 0.018.
Values may be sent and summed in bfloat16 or wider, within the bound.
No kernel may reach another device: no remote copies, remote signals or barrier semaphores. Data moves between devices by JAX's collectives and lax.ppermute only.
A program may use at most 256 MiB of HBM per device.

```python
import math
import jax
import jax.numpy as jnp
from jax import lax

D = 1536
HEADS = 24
KVH = 8
HD = 64
FF = 1024
EXP = 4
TOP = 2
TOK_DEV = 128
SEQ_LEN = 4096
CAP = 96
LOSS_SCALE = 786432


def route_table(key):
    blocks_count = SEQ_LEN // TOK_DEV
    block_keys = jax.random.split(key, blocks_count)

    def one_block(block_key):
        sub_keys = jax.random.split(block_key, 4)
        busiest = jax.random.randint(sub_keys[0], (), 0, EXP)
        cut_points = jnp.sort(jax.random.randint(sub_keys[1], (EXP - 2,), 0, TOK_DEV + 1))
        bounds = jnp.concatenate([jnp.zeros((1,), jnp.int32), cut_points.astype(jnp.int32), jnp.full((1,), TOK_DEV, jnp.int32)])
        others = bounds[1:] - bounds[:-1]
        other_ids = (busiest + 1 + jnp.arange(EXP - 1, dtype=jnp.int32)) % EXP
        expert_loads = jnp.zeros((EXP,), jnp.int32).at[busiest].set(TOK_DEV).at[other_ids].set(others)
        run_ends = jnp.cumsum(expert_loads)
        starts = run_ends - expert_loads
        places = jnp.arange(2 * TOK_DEV, dtype=jnp.int32)
        owners = jnp.sum((run_ends[None, :] <= places[:, None]).astype(jnp.int32), axis=1)
        slot_ranks = places - jnp.take(starts, owners)
        route_pair = jnp.stack([owners[:TOK_DEV], owners[TOK_DEV:]], axis=1)
        slot_pair = jnp.stack([slot_ranks[:TOK_DEV], slot_ranks[TOK_DEV:]], axis=1)
        shuffle = jax.random.permutation(sub_keys[2], TOK_DEV)
        route_pair = route_pair[shuffle]
        slot_pair = slot_pair[shuffle]
        swapped = jax.random.randint(sub_keys[3], (TOK_DEV, 1), 0, 2) == 1
        route_pair = jnp.where(swapped, route_pair[:, ::-1], route_pair)
        slot_pair = jnp.where(swapped, slot_pair[:, ::-1], slot_pair)
        return (route_pair, slot_pair)
    route_blocks, slot_blocks = jax.vmap(one_block)(block_keys)
    return (route_blocks.reshape(SEQ_LEN, 2).astype(jnp.int32), slot_blocks.reshape(SEQ_LEN, 2).astype(jnp.int32))


def draw_routes(key, part):
    route_rows, slot_rows = route_table(key)
    return route_rows


def draw_slots(key, part):
    route_rows, slot_rows = route_table(key)
    return slot_rows


def draw_valid(key, part):
    key = jax.random.fold_in(key, 7)
    positions = jnp.arange(SEQ_LEN, dtype=jnp.int32)
    thresholds = 300 + 600 * positions // SEQ_LEN
    samples = jax.random.randint(key, (SEQ_LEN,), 0, 1000)
    return (samples < thresholds).astype(jnp.int32)


def level_of(stream_key, shape, pieces, least, largest):
    loudness = 1.0
    for position, shards_of in pieces:
        draws = jax.random.uniform(jax.random.fold_in(jax.random.fold_in(stream_key, 6), position), (shards_of,), jnp.float32, least / len(pieces), largest / len(pieces))
        loudness = loudness * jnp.repeat(jnp.exp(draws), shape[position] // shards_of).reshape((-1,) + (1,) * (len(shape) - 1 - position))
    return loudness


def bell_draw(rng, shape, width, limit, cuts=(), held_as=jnp.bfloat16):
    drawn = width * jax.random.normal(rng, shape, jnp.float32)
    if cuts:
        drawn = drawn * level_of(rng, shape, cuts, -0.22, 0.18)
    return jnp.clip(drawn, -limit, limit).astype(held_as)


def setup_inputs(seed: int = 0) -> dict:
    key_list = jax.random.split(jax.random.key(seed), 14)
    return {
        "tokens": bell_draw(key_list[0], (SEQ_LEN, D), 1.0, 6.0, ((0, 32),)),
        "teacher": bell_draw(key_list[1], (SEQ_LEN, D), 1.0, 6.0, ((0, 32),)),
        "valid": draw_valid(jax.random.fold_in(key_list[13], 71), 0),
        "routes": draw_routes(jax.random.fold_in(key_list[13], 71), 0),
        "slots": draw_slots(jax.random.fold_in(key_list[13], 71), 0),
        "gain_attn": jnp.clip(1.0 + 0.1 * jax.random.normal(key_list[5], (D,), jnp.float32), 0.5, 1.5).astype(jnp.bfloat16),
        "w_query": bell_draw(key_list[6], (D, HEADS * HD), D ** -0.5, 0.15625, ((0, 8),)),
        "w_keyval": bell_draw(key_list[7], (D, 2 * KVH * HD), D ** -0.5, 0.15625, ((0, 8),)),
        "w_out": bell_draw(key_list[8], (HEADS * HD, D), ((SEQ_LEN // (9 * HEADS * HD) + 1) ** 0.5), 6.0, ((1, 8),)),
        "gain_ffn": jnp.clip(1.0 + 0.1 * jax.random.normal(key_list[9], (D,), jnp.float32), 0.5, 1.5).astype(jnp.bfloat16),
        "w_router": bell_draw(key_list[10], (D, EXP), 0.02, 0.3125, ((0, 8),)),
        "w_gate_up": bell_draw(key_list[11], (EXP, D, 2 * FF), D ** -0.5, 0.15625, ((1, 8),)),
        "w_down": bell_draw(key_list[12], (EXP, FF, D), FF ** -0.5, 0.1875, ((2, 8),)),
    }


EPSILON = 1e-06
FLOOR_SCORE = -1e+30
PRECISE = lax.Precision.HIGHEST

@jax.custom_vjp
def low(v):
    return lax.optimization_barrier(v.astype(jnp.bfloat16)).astype(jnp.float32)

@jax.custom_vjp
def low_back(v):
    return v

def low_keep(v):
    return (low(v), None)

def low_pass(kept, grad):
    return (grad,)

def back_keep(v):
    return (v, None)

def back_low(kept, grad):
    return (low(grad),)
low.defvjp(low_keep, low_pass)
low_back.defvjp(back_keep, back_low)

def norm_rows(values, gain_row):
    return values * lax.rsqrt(lax.optimization_barrier(jnp.mean(values * values, axis=-1, keepdims=True)) + EPSILON) * gain_row

def attend(queries, key_rows, value_rows, valid_row):
    length = queries.shape[0]
    block_rows = math.gcd(length, 256)
    number = length // block_rows
    key_pos = jnp.arange(length, dtype=jnp.int32)
    score_scale = HD ** (-0.5)

    def one_block(inputs):
        query_block, offset = inputs
        query_pos = offset + jnp.arange(block_rows, dtype=jnp.int32)
        scores = jnp.einsum('rkgd,jkd->rkgj', query_block, key_rows, precision=PRECISE) * score_scale
        scores = low_back(scores)
        causal = key_pos[None, :] <= query_pos[:, None]
        usable = (valid_row[None, :] > 0) | (key_pos[None, :] == query_pos[:, None])
        visible = (causal & usable)[:, None, None, :]
        masked = jnp.where(visible, scores, FLOOR_SCORE)
        row_max = lax.optimization_barrier(jnp.max(masked, axis=-1, keepdims=True))
        exp_terms = jnp.where(visible, jnp.exp(masked - row_max), 0.0)
        denominator = lax.optimization_barrier(jnp.sum(exp_terms, axis=-1))
        summed = low_back(jnp.einsum('rkgj,jkd->rkgd', low(exp_terms), value_rows, precision=PRECISE))
        return summed / denominator[..., None]
    blocks = queries.reshape(number, block_rows, queries.shape[1], queries.shape[2], queries.shape[3])
    offsets = jnp.arange(number, dtype=jnp.int32) * block_rows
    block_outputs = lax.map(jax.checkpoint(one_block), (blocks, offsets))
    return block_outputs.reshape(queries.shape)

def reference(tokens, teacher, valid, routes, slots, gain_attn, w_query, w_keyval, w_out, gain_ffn, w_router, w_gate_up, w_down):
    length = SEQ_LEN
    groups = HEADS // KVH
    blocks_count = SEQ_LEN // TOK_DEV
    teacher_rows = teacher.astype(jnp.float32)
    valid_rows = valid.astype(jnp.float32)
    picked = (routes[:, :, None] == jnp.arange(EXP, dtype=jnp.int32)).astype(jnp.float32)
    slot_hot = (slots[:, :, None] == jnp.arange(CAP, dtype=jnp.int32)).astype(jnp.float32)
    placed = (picked[:, :, :, None] * slot_hot[:, :, None, :]).reshape(blocks_count, TOK_DEV, TOP, EXP, CAP)
    dispatch = lax.optimization_barrier(jnp.sum(placed, axis=2))

    def forward(inputs, gain_one, query_weight, keyval_weight, out_weight, gain_two, router_weight, gate_up_weight, down_weight):
        normed = low(norm_rows(inputs, gain_one))
        queries = low(low_back(jnp.dot(normed, query_weight, precision=PRECISE)))
        keyvals = low(low_back(jnp.dot(normed, keyval_weight, precision=PRECISE)))
        queries = queries.reshape(length, KVH, groups, HD)
        keyvals = keyvals.reshape(length, KVH, 2, HD)
        attended = attend(queries, keyvals[:, :, 0], keyvals[:, :, 1], valid)
        attended = low(low_back(attended)).reshape(length, HEADS * HD)
        branch = low_back(jnp.dot(attended, out_weight, precision=PRECISE))
        residual = inputs + branch
        normed_two = low(norm_rows(residual, gain_two))
        logits = jnp.dot(normed_two, router_weight, precision=PRECISE)
        chosen = lax.optimization_barrier(jnp.sum(picked * logits[:, None, :], axis=-1))
        gating = jax.nn.softmax(chosen, axis=-1)
        expert_rows = low(low_back(jnp.einsum('btec,btd->becd', dispatch, normed_two.reshape(blocks_count, TOK_DEV, D), precision=PRECISE)))
        gate_up = low_back(jnp.einsum('becd,edf->becf', expert_rows, gate_up_weight, precision=PRECISE))
        hidden = low(jax.nn.silu(gate_up[..., :FF]) * gate_up[..., FF:])
        expert_out = low(low_back(jnp.einsum('becf,efd->becd', hidden, down_weight, precision=PRECISE)))
        selected = jnp.einsum('btkec,becd->btkd', placed, expert_out, precision=PRECISE).reshape(length, TOP, D)
        return residual + lax.optimization_barrier(jnp.sum(gating[:, :, None] * selected, axis=1))

    def scaled(inputs, gain_one, query_weight, keyval_weight, out_weight, gain_two, router_weight, gate_up_weight, down_weight):
        mixed_exact = forward(inputs, gain_one, query_weight, keyval_weight, out_weight, gain_two, router_weight, gate_up_weight, down_weight)
        errors = (mixed_exact - teacher_rows) * valid_rows[:, None]
        squares = jnp.sum(errors * errors)
        valid_count = jnp.sum(valid_rows)
        return (squares * (LOSS_SCALE / (D * valid_count)), (mixed_exact, squares / (D * valid_count)))
    scaled_loss, pullback, side_outputs = jax.vjp(scaled, tokens.astype(jnp.float32), gain_attn.astype(jnp.float32), w_query.astype(jnp.float32), w_keyval.astype(jnp.float32), w_out.astype(jnp.float32), gain_ffn.astype(jnp.float32), w_router.astype(jnp.float32), w_gate_up.astype(jnp.float32), w_down.astype(jnp.float32), has_aux=True)
    gradients = pullback(jnp.ones_like(scaled_loss))
    mixed_exact, loss_value = side_outputs
    return (mixed_exact.astype(jnp.bfloat16), loss_value, gradients[0], gradients[1], gradients[2], gradients[3], gradients[4], gradients[5], gradients[6], gradients[7], gradients[8])
```

```python
import math

import jax
import jax.numpy as jnp
from jax import lax
from jax.sharding import PartitionSpec as P

HEADS = 24
KVH = 8
HD = 64
CAP = 96
EPSILON = 1e-06
FLOOR_SCORE = -1e30
BF = jnp.bfloat16
F32 = jnp.float32


def token_place(row_index, rows_tok, shard_count, local_rows):
    owner_shard = row_index // local_rows
    within = row_index % local_rows
    return (within // rows_tok * shard_count + owner_shard) * rows_tok + within % rows_tok


def score_block(queries, key_rows, query_place, key_place, key_valid, score_scale):
    scores = (
        jnp.einsum("rkgd,jkd->rkgj", queries, key_rows, preferred_element_type=jnp.float32)
        * score_scale
    )
    causal = key_place[None, :] <= query_place[:, None]
    usable = (key_valid[None, :] > 0) | (key_place[None, :] == query_place[:, None])
    visible = (causal & usable)[:, None, None, :]
    return (jnp.where(visible, scores, FLOOR_SCORE), visible)


def attend_forward(head_queries, kv_piece, valid_row, query_place, place):
    local_rows, local_kv, groups, head_size = head_queries.shape
    score_scale = head_size ** (-0.5)
    fold = math.gcd(kv_piece.shape[0], 1024)
    number = kv_piece.shape[0] // fold
    kv_blocks = kv_piece.reshape(number, fold, local_kv, 2 * head_size)
    valid_blocks = valid_row.reshape(number, fold)
    starts = jnp.arange(number, dtype=jnp.int32) * fold

    def advance(state, block):
        kv_block, valid_block, first_row = block
        row_max, denominator, summed = state
        key_place = place(first_row + jnp.arange(fold, dtype=jnp.int32))
        masked, visible = score_block(
            head_queries,
            kv_block[..., :head_size],
            query_place,
            key_place,
            valid_block,
            score_scale,
        )
        new_max = jnp.maximum(row_max, jnp.max(masked, axis=-1))
        exp_terms = jnp.where(visible, jnp.exp(masked - new_max[..., None]), 0.0)
        factor = jnp.exp(row_max - new_max)
        denominator = denominator * factor + jnp.sum(exp_terms, axis=-1)
        summed = summed * factor[..., None] + jnp.einsum(
            "rkgj,jkd->rkgd",
            exp_terms.astype(BF),
            kv_block[..., head_size:],
            preferred_element_type=F32,
        )
        return ((new_max, denominator, summed), None)

    start = (
        jnp.full((local_rows, local_kv, groups), FLOOR_SCORE, F32),
        jnp.zeros((local_rows, local_kv, groups), F32),
        jnp.zeros((local_rows, local_kv, groups, head_size), F32),
    )
    (row_max, denominator, summed), unused = lax.scan(
        advance, start, (kv_blocks, valid_blocks, starts)
    )
    return row_max, denominator, summed / denominator[..., None]


def attend_backward(
    head_queries, kv_piece, valid_row, query_place, place, row_max, denominator, exact, head_grad
):
    local_rows, local_kv, groups, head_size = head_queries.shape
    score_scale = head_size ** (-0.5)
    grad_summed = (head_grad / denominator[..., None]).astype(BF)
    shift_term = -jnp.sum(head_grad * exact, axis=-1) / denominator
    total = kv_piece.shape[0]
    fold = math.gcd(total, 1024)
    number = total // fold
    kv_blocks = kv_piece.reshape(number, fold, local_kv, 2 * head_size)
    valid_blocks = valid_row.reshape(number, fold)
    starts = jnp.arange(number, dtype=jnp.int32) * fold

    def step(grad_q, block):
        kv_block, valid_block, first_row = block
        key_rows = kv_block[..., :head_size]
        value_rows = kv_block[..., head_size:]
        key_place = place(first_row + jnp.arange(fold, dtype=jnp.int32))
        masked, visible = score_block(
            head_queries, key_rows, query_place, key_place, valid_block, score_scale
        )
        exp_terms = jnp.where(visible, jnp.exp(masked - row_max[..., None]), 0.0)
        weights = exp_terms.astype(BF)
        products = jnp.einsum(
            "rkgd,jkd->rkgj", grad_summed, value_rows, preferred_element_type=F32
        )
        grad_scores = (exp_terms * (products + shift_term[..., None])).astype(BF)
        grad_q = (
            grad_q
            + jnp.einsum("rkgj,jkd->rkgd", grad_scores, key_rows, preferred_element_type=F32)
            * score_scale
        )
        grad_keys = (
            jnp.einsum("rkgj,rkgd->jkd", grad_scores, head_queries, preferred_element_type=F32)
            * score_scale
        )
        grad_values = jnp.einsum(
            "rkgj,rkgd->jkd", weights, grad_summed, preferred_element_type=F32
        )
        return (grad_q, jnp.concatenate([grad_keys, grad_values], axis=-1))

    grad_q, grad_kv = lax.scan(
        step,
        jnp.zeros((local_rows, local_kv, groups, head_size), F32),
        (kv_blocks, valid_blocks, starts),
    )
    return grad_q, grad_kv.reshape(total, local_kv * 2 * head_size)


def shift(block, count, step):
    return lax.ppermute(block, "seq", [(i, (i + step) % count) for i in range(count)])


def send_out(blocks, count):
    return [blocks[0]] + [shift(blocks[s], count, s) for s in range(1, count)]


def send_back(blocks, count):
    return [blocks[0]] + [shift(blocks[s], count, count - s) for s in range(1, count)]


def from_relative(blocks, place):
    count = len(blocks)
    rising = jnp.stack([blocks[-s % count] for s in range(count)])
    return lax.dynamic_slice_in_dim(
        jnp.concatenate([rising, rising]), count - place, count, 0
    )


def dot(a, b):
    return jnp.dot(a, b, preferred_element_type=F32)


def dot_nt(a, b):
    return lax.dot_general(a, b, (((1,), (1,)), ((), ())), preferred_element_type=F32)


def dot_tn(a, b):
    return lax.dot_general(a, b, (((0,), (0,)), ((), ())), preferred_element_type=F32)


def root(values):
    return lax.rsqrt(jnp.mean(values * values, axis=-1, keepdims=True) + EPSILON)


def root_back(values, factor, grad_scaled):
    inner = jnp.mean(grad_scaled * values, axis=-1, keepdims=True)
    return factor * grad_scaled - values * (factor * factor * factor * inner)


def local(
    tokens,
    teacher,
    valid,
    routes,
    slots,
    gain_attn,
    w_query,
    w_keyval,
    w_out,
    gain_ffn,
    w_router,
    w_gate_up,
    w_down,
):
    seqs = lax.axis_size("seq")
    shards = lax.axis_size("fsdp")
    z = lax.axis_index("seq")
    shard = lax.axis_index("fsdp")
    rows, width = tokens.shape
    groups = HEADS // KVH
    local_kv = KVH // seqs
    q_cols = local_kv * groups * HD
    kv_cols = local_kv * 2 * HD
    local_rows = rows * seqs
    seq_len = local_rows * shards
    experts, part, both = w_gate_up.shape
    units = both // 2
    split = seqs // experts
    piece = units // split
    expert = z // split
    fraction = z % split

    gain_one = gain_attn.astype(F32)[:, None]
    gain_two = gain_ffn.astype(F32)[:, None]
    query_scaled = (w_query.astype(F32) * gain_one).astype(BF)
    keyval_scaled = (w_keyval.astype(F32) * gain_one).astype(BF)
    heads_shard = jnp.concatenate(
        [
            lax.dynamic_slice_in_dim(query_scaled, z * q_cols, q_cols, 1),
            lax.dynamic_slice_in_dim(keyval_scaled, z * kv_cols, kv_cols, 1),
        ],
        axis=1,
    )
    heads_full = lax.all_gather(heads_shard, "fsdp", axis=0, tiled=True)
    out_full = lax.all_gather(w_out, "fsdp", axis=1, tiled=True)
    router_full = lax.all_gather(
        (w_router.astype(F32) * gain_two).astype(BF), "fsdp", axis=0, tiled=True
    )
    gate_up_shard = lax.dynamic_slice(
        w_gate_up.reshape(experts, part, 2, split, piece),
        (expert, 0, 0, fraction, 0),
        (1, part, 2, 1, piece),
    ).reshape(part, 2 * piece)
    gate_up_full = lax.all_gather(
        (gate_up_shard.astype(F32) * gain_two).astype(BF), "fsdp", axis=0, tiled=True
    )
    down_shard = lax.dynamic_slice(
        w_down, (expert, fraction * piece, 0), (1, piece, part)
    ).reshape(piece, part)
    down_full = lax.all_gather(down_shard, "fsdp", axis=1, tiled=True)
    query_full = lax.all_gather(query_scaled, "fsdp", axis=0, tiled=True)
    keyval_full = lax.all_gather(keyval_scaled, "fsdp", axis=0, tiled=True)

    valid_low = valid.astype(BF).reshape(1, rows)
    valid_local = lax.all_gather(valid_low, "seq", axis=0, tiled=True)
    valid_all = lax.all_gather(valid_local, "fsdp", axis=0, tiled=True).reshape(seq_len)
    valid_count = jnp.sum(valid_all.astype(F32))

    token_blocks = send_out([tokens] * seqs, seqs)
    projected = []
    for block in token_blocks:
        values = block.astype(F32)
        projected.append((dot(block, heads_full) * root(values)).astype(BF))
    projected = from_relative(projected, z).reshape(local_rows, q_cols + kv_cols)
    tokens_local = from_relative(token_blocks, z).reshape(local_rows, width)
    head_queries = projected[:, :q_cols].reshape(local_rows, local_kv, groups, HD)
    head_kv = projected[:, q_cols:]
    kv_all = lax.all_gather(head_kv, "fsdp", axis=0, tiled=True)

    def place(index):
        return token_place(index, rows, shards, local_rows)

    query_place = place(shard * local_rows + jnp.arange(local_rows, dtype=jnp.int32))
    row_max, denominator, exact = attend_forward(
        head_queries, kv_all, valid_all, query_place, place
    )
    attended = lax.all_to_all(
        exact.astype(BF).reshape(local_rows, q_cols), "seq", split_axis=0, concat_axis=1, tiled=True
    )

    inputs = tokens.astype(F32)
    residual = inputs + dot(attended, out_full)
    factor_two = root(residual)
    normed_two = (residual * factor_two).astype(BF)
    logits = dot(normed_two, router_full)
    expert_ids = jnp.arange(experts, dtype=jnp.int32)
    picked = (routes[:, :, None] == expert_ids).astype(F32)
    chosen = jnp.sum(picked * logits[:, None, :], axis=-1)
    gating = jax.nn.softmax(chosen, axis=-1)
    owners = ((jnp.arange(seqs, dtype=jnp.int32) + z) % seqs) // split
    to_owner = routes[:, :, None] == owners
    slot_hot = slots[:, :, None] == jnp.arange(CAP, dtype=jnp.int32)
    placed = (to_owner[:, :, :, None] & slot_hot[:, :, None, :]).astype(BF)
    placed = placed.reshape(rows, 2, seqs * CAP)
    dispatch = placed[:, 0] + placed[:, 1]
    placed_pairs = jnp.concatenate([placed[:, 0], placed[:, 1]], axis=0)
    sent_rows = dot_tn(dispatch, normed_two).astype(BF).reshape(seqs, CAP, width)
    expert_rows = jnp.concatenate(send_out([sent_rows[s] for s in range(seqs)], seqs))
    gate_up = dot(expert_rows, gate_up_full)
    gate_part = gate_up[:, :piece]
    up_part = gate_up[:, piece:]
    sigmoid_gate = jax.nn.sigmoid(gate_part)
    hidden = (gate_part * sigmoid_gate * up_part).astype(BF)
    expert_out = dot(hidden, down_full).astype(BF).reshape(seqs, CAP, width)
    returned = jnp.concatenate(send_back([expert_out[s] for s in range(seqs)], seqs))
    selected = dot(placed_pairs, returned).reshape(2, rows, width)
    mixed_exact = residual + gating[:, :1] * selected[0] + gating[:, 1:] * selected[1]
    valid_rows = valid.astype(F32)
    errors = (mixed_exact - teacher.astype(F32)) * valid_rows[:, None]
    squares = lax.psum(jnp.sum(errors * errors), ("seq", "fsdp"))
    loss_value = squares / (width * valid_count)
    loss_scale = width * seq_len // 8
    grad_mixed = errors * (2.0 * loss_scale / (width * valid_count))

    grad_gating = jnp.stack(
        [jnp.sum(selected[0] * grad_mixed, axis=-1), jnp.sum(selected[1] * grad_mixed, axis=-1)],
        axis=1,
    )
    grad_chosen = gating * (grad_gating - jnp.sum(gating * grad_gating, axis=-1, keepdims=True))
    grad_logits = jnp.sum(grad_chosen[:, :, None] * picked, axis=1).astype(BF)
    weighted = jnp.concatenate(
        [(gating[:, :1] * grad_mixed).astype(BF), (gating[:, 1:] * grad_mixed).astype(BF)], axis=0
    )
    sent_grads = dot_tn(placed_pairs, weighted).astype(BF).reshape(seqs, CAP, width)
    grad_expert_out = jnp.concatenate(send_out([sent_grads[s] for s in range(seqs)], seqs))
    grad_down_local = dot_tn(hidden, grad_expert_out).astype(BF)
    grad_hidden = dot_nt(grad_expert_out, down_full)
    grad_gate = grad_hidden * up_part * sigmoid_gate * (1.0 + gate_part * (1.0 - sigmoid_gate))
    grad_up = grad_hidden * gate_part * sigmoid_gate
    grad_gate_up_rows = jnp.concatenate([grad_gate, grad_up], axis=-1).astype(BF)
    grad_rows = dot_nt(grad_gate_up_rows, gate_up_full).astype(BF).reshape(seqs, CAP, width)
    grad_gate_up_local = dot_tn(expert_rows, grad_gate_up_rows).astype(BF)
    grad_returned = jnp.concatenate(send_back([grad_rows[s] for s in range(seqs)], seqs))
    grad_down_shard = lax.psum_scatter(
        grad_down_local, "fsdp", scatter_dimension=1, tiled=True
    )
    grad_gate_up_shard = lax.psum_scatter(
        grad_gate_up_local, "fsdp", scatter_dimension=0, tiled=True
    )
    grad_down = lax.all_gather(grad_down_shard, "seq", axis=0, tiled=False)
    grad_gate_up = lax.all_gather(grad_gate_up_shard, "seq", axis=0, tiled=False)

    grad_normed_two = dot(dispatch, grad_returned) + dot_nt(grad_logits, router_full)
    grad_residual = grad_mixed + root_back(residual, factor_two, grad_normed_two)
    grad_branch = grad_residual.astype(BF)
    grad_attended = dot_nt(grad_branch, out_full).astype(BF)
    head_grad = lax.all_to_all(grad_attended, "seq", split_axis=1, concat_axis=0, tiled=True)
    head_grad = head_grad.reshape(local_rows, local_kv, groups, HD).astype(F32)

    grad_out_local = jnp.concatenate(
        [dot_tn(attended, grad_branch), dot_tn(grad_logits, normed_two)], axis=0
    ).astype(BF)
    grad_out_shard = lax.psum_scatter(grad_out_local, "fsdp", scatter_dimension=1, tiled=True)
    grad_out_sum = lax.psum(grad_out_shard, "seq").astype(F32)
    grad_out = grad_out_sum[: HEADS * HD]
    grad_router_base = grad_out_sum[HEADS * HD :].T

    grad_q, grad_kv = attend_backward(
        head_queries, kv_all, valid_all, query_place, place, row_max, denominator, exact, head_grad
    )
    grad_q = grad_q.reshape(local_rows, q_cols)
    grad_kv_own = lax.psum_scatter(grad_kv.astype(BF), "fsdp", scatter_dimension=0, tiled=True)
    token_grad_q = lax.all_to_all(
        grad_q.astype(BF), "seq", split_axis=0, concat_axis=1, tiled=True
    )
    token_grad_kv = lax.all_to_all(grad_kv_own, "seq", split_axis=0, concat_axis=1, tiled=True)
    factor_local = root(tokens_local.astype(F32))
    grad_heads = jnp.concatenate([grad_q, grad_kv_own.astype(F32)], axis=1) * factor_local
    grad_heads_local = dot_tn(tokens_local, grad_heads.astype(BF)).astype(BF)
    grad_heads_shard = lax.psum_scatter(
        grad_heads_local, "fsdp", scatter_dimension=0, tiled=True
    )
    grad_heads_all = lax.all_gather(grad_heads_shard, "seq", axis=0, tiled=False).astype(F32)
    grad_query_base = jnp.concatenate([grad_heads_all[s, :, :q_cols] for s in range(seqs)], axis=1)
    grad_keyval_base = jnp.concatenate([grad_heads_all[s, :, q_cols:] for s in range(seqs)], axis=1)
    grad_normed = dot_nt(token_grad_q, query_full) + dot_nt(token_grad_kv, keyval_full)
    grad_tokens = grad_residual + root_back(inputs, root(inputs), grad_normed)

    grad_gain_attn = jnp.sum(w_query.astype(F32) * grad_query_base, axis=1) + jnp.sum(
        w_keyval.astype(F32) * grad_keyval_base, axis=1
    )
    grad_down = grad_down.reshape(experts, units, part).astype(F32)
    grad_gate_up = (
        grad_gate_up.reshape(experts, split, part, 2, piece)
        .transpose(0, 2, 3, 1, 4)
        .reshape(experts, part, both)
        .astype(F32)
    )
    grad_gain_ffn = jnp.sum(w_gate_up.astype(F32) * grad_gate_up, axis=(0, 2)) + jnp.sum(
        w_router.astype(F32) * grad_router_base, axis=1
    )
    return (
        mixed_exact.astype(BF),
        loss_value,
        grad_tokens,
        grad_gain_attn,
        grad_query_base * gain_one,
        grad_keyval_base * gain_one,
        grad_out,
        grad_gain_ffn,
        grad_router_base * gain_two,
        grad_gate_up * gain_two,
        grad_down,
    )


def solution(mesh):
    return jax.shard_map(
        local,
        mesh=mesh,
        in_specs=(
            P(("seq", "fsdp"), None),
            P(("seq", "fsdp"), None),
            P(("seq", "fsdp")),
            P(("seq", "fsdp"), None),
            P(("seq", "fsdp"), None),
            P("fsdp"),
            P("fsdp", None),
            P("fsdp", None),
            P(None, "fsdp"),
            P("fsdp"),
            P("fsdp", None),
            P(None, "fsdp", None),
            P(None, None, "fsdp"),
        ),
        out_specs=(
            P(("seq", "fsdp"), None),
            P(),
            P(("seq", "fsdp"), None),
            P("fsdp"),
            P("fsdp", None),
            P("fsdp", None),
            P(None, "fsdp"),
            P("fsdp"),
            P("fsdp", None),
            P(None, "fsdp", None),
            P(None, None, "fsdp"),
        ),
        check_vma=False,
    )
```

```python
import functools

import jax
import jax.numpy as jnp
from jax import lax
from jax.experimental import pallas as pl
from jax.experimental.pallas import tpu as pltpu
from jax.sharding import PartitionSpec as P

HEADS = 24
KVH = 8
HD = 64
CAP = 96
EPSILON = 1e-06
FLOOR_SCORE = -1e30
BF = jnp.bfloat16
F32 = jnp.float32


def dot(a, b):
    return jnp.dot(a, b, preferred_element_type=F32)


def dot_nt(a, b):
    return lax.dot_general(a, b, (((1,), (1,)), ((), ())), preferred_element_type=F32)


def dot_tn(a, b):
    return lax.dot_general(a, b, (((0,), (0,)), ((), ())), preferred_element_type=F32)


def own_mask(valid_row, rows):
    i = lax.broadcasted_iota(jnp.int32, (rows, rows), 0)
    j = lax.broadcasted_iota(jnp.int32, (rows, rows), 1)
    return jnp.where(j == i, 0.0, jnp.where(j < i, valid_row, FLOOR_SCORE))


def key_chunk(kv_refs, zk, rows, g):
    return jnp.concatenate(
        [ref[pl.ds(zk * rows, rows), pl.ds(g * 2 * HD, 2 * HD)] for ref in kv_refs], axis=0
    )


def forward_kernel(shards, seqs, rows, local_kv, groups, *refs):
    kv_refs = refs[:shards]
    q_ref, bias_ref, low_ref, exact_ref, lse_ref, acc_ref, max_ref = refs[shards:]
    zq = pl.program_id(0)
    stack = groups * rows
    zeros = jnp.zeros((rows, HD), BF)
    half = lax.broadcasted_iota(jnp.int32, (1, 2 * HD), 1) < HD

    def queries(g):
        parts = []
        for h in range(groups):
            start = (g * groups + h) * HD
            parts.append(jnp.concatenate([q_ref[:, start : start + HD], zeros], axis=1))
        return jnp.concatenate(parts, axis=0)

    def chunk(g, zk, scores):
        first = scores is None
        keys = key_chunk(kv_refs, zk, rows, g)
        raw = dot_nt(queries(g), keys)
        if first:
            row = bias_ref[seqs + zk]
            mask = own_mask(row[:, :rows], rows)
            mask = jnp.concatenate([mask] * groups, axis=0)
            masked = jnp.concatenate([raw[:, :rows] + mask, raw[:, rows:] + row[:, rows:]], axis=1)
            new_max = jnp.max(masked, axis=1, keepdims=True)
        else:
            masked = raw + bias_ref[zk]
            new_max = jnp.maximum(max_ref[g][:, :1], jnp.max(masked, axis=1, keepdims=True))
        terms = jnp.exp(masked - new_max).astype(BF)
        ones_values = jnp.where(half, jnp.ones_like(keys), keys)
        part = dot(terms, ones_values)
        if first:
            acc_ref[g] = part
        else:
            acc_ref[g] = acc_ref[g] * jnp.exp(max_ref[g][:, :1] - new_max) + part
        max_ref[g] = jnp.broadcast_to(new_max, (stack, 2 * HD))

    for g in range(local_kv):
        chunk(g, zq, None)

    @pl.loop(0, zq)
    def _(zk):
        for g in range(local_kv):
            chunk(g, zk, True)

    exact_parts, lse_parts = [], []
    for g in range(local_kv):
        acc = acc_ref[g]
        total = acc[:, :HD]
        exact = acc[:, HD:] / total
        lse = max_ref[g][:, :HD] + jnp.log(total)
        for h in range(groups):
            exact_parts.append(exact[h * rows : (h + 1) * rows])
            lse_parts.append(lse[h * rows : (h + 1) * rows])
    exact = jnp.concatenate(exact_parts, axis=1)
    exact_ref[...] = exact
    low_ref[...] = exact.astype(BF)
    lse_ref[...] = jnp.concatenate(lse_parts, axis=1)


def flash_forward(q, kv_blocks, bias, seqs, rows, local_kv, groups):
    shards = len(kv_blocks)
    q_cols = q.shape[1]
    kv_spec = pl.BlockSpec(kv_blocks[0].shape, lambda i: (0, 0))
    q_spec = pl.BlockSpec((rows, q_cols), lambda i: (i, 0))
    stack = groups * rows
    out = jax.ShapeDtypeStruct((seqs * rows, q_cols), F32)
    return pl.pallas_call(
        functools.partial(forward_kernel, shards, seqs, rows, local_kv, groups),
        grid=(seqs,),
        in_specs=[kv_spec] * shards + [q_spec, pl.BlockSpec(bias.shape, lambda i: (0, 0, 0))],
        out_specs=[q_spec] * 3,
        out_shape=[jax.ShapeDtypeStruct((seqs * rows, q_cols), BF), out, out],
        scratch_shapes=[
            pltpu.VMEM((local_kv, stack, 2 * HD), F32),
            pltpu.VMEM((local_kv, stack, 2 * HD), F32),
        ],
        compiler_params=pltpu.CompilerParams(vmem_limit_bytes=40 * 1024 * 1024),
        cost_estimate=pl.CostEstimate(
            flops=8 * seqs * seqs * shards * rows * rows * local_kv * groups * HD,
            bytes_accessed=8 * 1024 * 1024,
            transcendentals=seqs * seqs * shards * rows * rows * local_kv * groups // 2,
        ),
    )(*kv_blocks, q, bias)


def backward_kernel(shards, seqs, rows, local_kv, groups, *refs):
    kv_refs = refs[:shards]
    (q_ref, bias_ref, grad_ref, exact_ref, lse_ref, grad_q_ref, near_ref, far_ref,
     pair_ref, pair_t_ref, lse_wide, delta_wide, acc_q, acc_kv) = refs[shards:]
    zk = pl.program_id(0)
    stack = groups * rows
    zeros = jnp.zeros((rows, HD), BF)

    @pl.when(zk == 0)
    def _():
        acc_q[...] = jnp.zeros_like(acc_q)

        @pl.loop(0, seqs)
        def _(zq):
            here = pl.ds(zq * rows, rows)
            for g in range(local_kv):
                tops, bottoms = [], []
                for h in range(groups):
                    cols = slice((g * groups + h) * HD, (g * groups + h + 1) * HD)
                    grad = grad_ref[here, cols]
                    tops.append(jnp.concatenate([q_ref[here, cols], zeros], axis=1))
                    bottoms.append(jnp.concatenate([zeros, grad], axis=1))
                    delta = jnp.sum(grad.astype(F32) * exact_ref[here, cols], axis=1, keepdims=True)
                    part = slice(h * rows, (h + 1) * rows)
                    delta_wide[zq, g, part] = jnp.broadcast_to(delta, (rows, 2 * HD))
                    lse_wide[zq, g, part] = jnp.broadcast_to(
                        lse_ref[here, cols][:, :1], (rows, 2 * HD)
                    )
                pair = jnp.concatenate(tops + bottoms, axis=0)
                pair_ref[zq, g] = pair
                pair_t_ref[zq, g] = pair.astype(F32).T.astype(BF)

    def chunk(g, zq, first):
        keys = key_chunk(kv_refs, zk, rows, g)
        both = dot_nt(pair_ref[zq, g], keys)
        raw, products = both[:stack], both[stack:]
        if first:
            row = bias_ref[seqs + zk]
            mask = own_mask(row[:, :rows], rows)
            mask = jnp.concatenate([mask] * groups, axis=0)
            masked = jnp.concatenate([raw[:, :rows] + mask, raw[:, rows:] + row[:, rows:]], axis=1)
        else:
            masked = raw + bias_ref[zk]
        weights = jnp.exp(masked - lse_wide[zq, g][:, :1])
        grads = (weights * (products - delta_wide[zq, g][:, :1])).astype(BF)
        acc_q[zq, g] += dot(grads, keys)
        part = dot(pair_t_ref[zq, g], jnp.concatenate([grads, weights.astype(BF)], axis=0))
        if first:
            acc_kv[g] = part
        else:
            acc_kv[g] += part

    for g in range(local_kv):
        chunk(g, zk, True)

    @pl.loop(zk + 1, seqs)
    def _(zq):
        for g in range(local_kv):
            chunk(g, zq, False)

    for p in range(shards):
        target = near_ref if p < shards // 2 else far_ref
        block = jnp.concatenate(
            [acc_kv[g, :, p * rows : (p + 1) * rows].T for g in range(local_kv)], axis=1
        )
        target[p % (shards // 2)] = block.astype(BF)

    @pl.when(zk == seqs - 1)
    def _():
        @pl.loop(0, seqs)
        def _(zq):
            parts = []
            for g in range(local_kv):
                total = acc_q[zq, g]
                for h in range(groups):
                    parts.append(total[h * rows : (h + 1) * rows, :HD])
            grad_q_ref[pl.ds(zq * rows, rows), :] = jnp.concatenate(parts, axis=1)


def flash_backward(q, kv_blocks, bias, grad, exact, lse, seqs, rows, local_kv, groups):
    shards = len(kv_blocks)
    q_cols = q.shape[1]
    stack = groups * rows
    kv_cols = 2 * HD * local_kv
    kv_spec = pl.BlockSpec(kv_blocks[0].shape, lambda i: (0, 0))
    whole = pl.BlockSpec((seqs * rows, q_cols), lambda i: (0, 0))
    out_spec = pl.BlockSpec((shards // 2, rows, kv_cols), lambda i: (0, i, 0))
    out = jax.ShapeDtypeStruct((shards // 2, seqs * rows, kv_cols), BF)
    return pl.pallas_call(
        functools.partial(backward_kernel, shards, seqs, rows, local_kv, groups),
        grid=(seqs,),
        in_specs=[kv_spec] * shards
        + [whole, pl.BlockSpec(bias.shape, lambda i: (0, 0, 0)), whole, whole, whole],
        out_specs=[whole, out_spec, out_spec],
        out_shape=[jax.ShapeDtypeStruct((seqs * rows, q_cols), F32), out, out],
        scratch_shapes=[
            pltpu.VMEM((seqs, local_kv, 2 * stack, 2 * HD), BF),
            pltpu.VMEM((seqs, local_kv, 2 * HD, 2 * stack), BF),
            pltpu.VMEM((seqs, local_kv, stack, 2 * HD), F32),
            pltpu.VMEM((seqs, local_kv, stack, 2 * HD), F32),
            pltpu.VMEM((seqs, local_kv, stack, 2 * HD), F32),
            pltpu.VMEM((local_kv, 2 * HD, shards * rows), F32),
        ],
        compiler_params=pltpu.CompilerParams(vmem_limit_bytes=48 * 1024 * 1024),
        cost_estimate=pl.CostEstimate(
            flops=20 * seqs * seqs * shards * rows * rows * local_kv * groups * HD,
            bytes_accessed=12 * 1024 * 1024,
            transcendentals=seqs * seqs * shards * rows * rows * local_kv * groups // 2,
        ),
    )(*kv_blocks, q, bias, grad, exact, lse)


def shift(block, count, step):
    return lax.ppermute(block, "seq", [(i, (i + step) % count) for i in range(count)])


def send_out(blocks, count):
    return [blocks[0]] + [shift(blocks[s], count, s) for s in range(1, count)]


def send_back(blocks, count):
    return [blocks[0]] + [shift(blocks[s], count, count - s) for s in range(1, count)]


def from_relative(blocks, place):
    count = len(blocks)
    rising = jnp.stack([blocks[-s % count] for s in range(count)])
    return lax.dynamic_slice_in_dim(jnp.concatenate([rising, rising]), count - place, count, 0)


def hop(block, count, mask):
    return lax.ppermute(block, "fsdp", [(i, i ^ mask) for i in range(count)])


def gather_shards(block, count):
    near = [block] + [hop(block, count, 2 * m) for m in range(1, count // 2)]
    return near + [hop(each, count, 1) for each in near]


def sum_chips(parts, count):
    total = parts(0)
    for m in range(1, count // 2):
        total = total + hop(parts(m).astype(BF), count, 2 * m).astype(F32)
    return total


def take(array, index, axis):
    return lax.dynamic_index_in_dim(array, index, axis, keepdims=False)


def split_columns(lhs, shard, count):
    tokens, width = lhs.shape
    cut = lhs.reshape(tokens, count // 2, 2, width // count)
    core = shard % 2
    far = take(cut, 1 - core, 2).reshape(tokens, width // 2)
    near = take(cut, core, 2).reshape(tokens, width // 2)
    return far, near


def sum_product(columns, rhs, shard, count):
    far, near = columns
    return sum_parts(dot_tn(far, rhs).astype(BF), dot_tn(near, rhs).astype(BF), shard, count)


def sum_parts(far, near, shard, count):
    there = hop(far, count, 1).reshape(count // 2, -1, far.shape[1])
    here = near.reshape(count // 2, -1, far.shape[1])
    chip = shard // 2

    def parts(m):
        return take(here, chip ^ m, 0).astype(F32) + take(there, chip ^ m, 0).astype(F32)

    return sum_chips(parts, count)


def spread_scalar(value, core, rows):
    high = value.astype(BF)
    low = (value - high.astype(F32)).astype(BF)
    pair = jnp.stack([high, low])
    none = jnp.zeros_like(pair)
    row = jnp.where(core == 0, jnp.concatenate([pair, none]), jnp.concatenate([none, pair]))
    return jnp.broadcast_to(row[None, :], (rows, 4))


def root(values):
    return lax.rsqrt(jnp.mean(values * values, axis=-1, keepdims=True) + EPSILON)


def root_back(values, factor, grad_scaled):
    inner = jnp.mean(grad_scaled * values, axis=-1, keepdims=True)
    return factor * grad_scaled - values * (factor * factor * factor * inner)


def local(
    tokens,
    teacher,
    valid,
    routes,
    slots,
    gain_attn,
    w_query,
    w_keyval,
    w_out,
    gain_ffn,
    w_router,
    w_gate_up,
    w_down,
):
    seqs = lax.axis_size("seq")
    shards = lax.axis_size("fsdp")
    z = lax.axis_index("seq")
    shard = lax.axis_index("fsdp")
    rows, width = tokens.shape
    groups = HEADS // KVH
    local_kv = KVH // seqs
    q_cols = local_kv * groups * HD
    kv_cols = local_kv * 2 * HD
    local_rows = rows * seqs
    seq_len = local_rows * shards
    experts, part, both = w_gate_up.shape
    units = both // 2
    split = seqs // experts
    piece = units // split
    expert = z // split
    fraction = z % split
    scale = HD ** (-0.5)

    gain_one = gain_attn.astype(F32)[:, None]
    gain_two = gain_ffn.astype(F32)[:, None]
    query_scaled = (w_query.astype(F32) * gain_one).astype(BF)
    keyval_scaled = (w_keyval.astype(F32) * gain_one).astype(BF)
    heads_shard = jnp.concatenate(
        [
            lax.dynamic_slice_in_dim(query_scaled, z * q_cols, q_cols, 1),
            lax.dynamic_slice_in_dim(keyval_scaled, z * kv_cols, kv_cols, 1),
        ],
        axis=1,
    )
    heads_full = lax.all_gather(heads_shard, "fsdp", axis=0, tiled=True)
    out_full = lax.all_gather(w_out, "fsdp", axis=1, tiled=True)
    router_full = lax.all_gather(
        (w_router.astype(F32) * gain_two).astype(BF), "fsdp", axis=0, tiled=True
    )
    own_expert = take(w_gate_up, expert, 0)
    gate_shard = lax.dynamic_slice_in_dim(own_expert, fraction * piece, piece, 1)
    up_shard = lax.dynamic_slice_in_dim(own_expert, units + fraction * piece, piece, 1)
    down_shard = lax.dynamic_slice_in_dim(
        take(w_down, expert, 0), fraction * piece, piece, 0
    ).T
    expert_shard = jnp.concatenate(
        [
            (gate_shard.astype(F32) * gain_two).astype(BF),
            (up_shard.astype(F32) * gain_two).astype(BF),
            down_shard,
        ],
        axis=1,
    )
    expert_full = lax.all_gather(expert_shard, "fsdp", axis=0, tiled=True)
    gate_up_full = expert_full[:, : 2 * piece]
    down_full = expert_full[:, 2 * piece :]
    attn_full = lax.all_gather(
        jnp.concatenate([query_scaled, keyval_scaled], axis=1), "fsdp", axis=0, tiled=True
    )

    valid_low = valid.astype(BF).reshape(1, rows)
    token_blocks = send_out([tokens] * seqs, seqs)
    valid_local = from_relative(send_out([valid_low] * seqs, seqs), z)
    projected = []
    for block in token_blocks:
        projected.append(dot(block, heads_full) * root(block.astype(F32)))
    projected = from_relative([each.astype(BF) for each in projected], z)
    projected = projected.reshape(local_rows, q_cols + kv_cols)
    tokens_local = from_relative(token_blocks, z).reshape(local_rows, width)
    factor_local = root(tokens_local.astype(F32))
    head_queries = projected[:, :q_cols] * jnp.asarray(scale, BF)

    valid_rows_kv = local_rows // kv_cols
    payload = jnp.concatenate(
        [
            projected[:, q_cols:],
            valid_local.reshape(valid_rows_kv, kv_cols),
            jnp.zeros((16 - valid_rows_kv, kv_cols), BF),
        ],
        axis=0,
    )
    kv_blocks = gather_shards(payload, shards)
    order = jnp.asarray(
        [2 * m for m in range(shards // 2)] + [2 * m + 1 for m in range(shards // 2)], jnp.int32
    )
    valid_all = jnp.stack(
        [
            each[local_rows : local_rows + valid_rows_kv].reshape(seqs, rows)
            for each in kv_blocks
        ],
        axis=1,
    ).astype(F32)
    valid_count = jnp.sum(valid_all)
    bias = jnp.where(valid_all > 0, 0.0, FLOOR_SCORE)
    earlier = ((order ^ shard) < shard) | (order == 0)
    bias_same = jnp.where(earlier[None, :, None], bias, FLOOR_SCORE)
    bias = jnp.concatenate([bias, bias_same]).reshape(2 * seqs, 1, shards * rows)
    attended_low, exact, lse = flash_forward(
        head_queries, kv_blocks, bias, seqs, rows, local_kv, groups
    )
    attended = lax.all_to_all(attended_low, "seq", split_axis=0, concat_axis=1, tiled=True)

    inputs = tokens.astype(F32)
    residual = inputs + dot(attended, out_full)
    factor_two = root(residual)
    normed_two = (residual * factor_two).astype(BF)
    logits = dot(normed_two, router_full)
    expert_ids = jnp.arange(experts, dtype=jnp.int32)
    picked = (routes[:, :, None] == expert_ids).astype(F32)
    chosen = jnp.sum(picked * logits[:, None, :], axis=-1)
    gating = jax.nn.softmax(chosen, axis=-1)
    owners = ((jnp.arange(seqs, dtype=jnp.int32) + z) % seqs) // split
    to_owner = routes[:, :, None] == owners
    slot_hot = slots[:, :, None] == jnp.arange(CAP, dtype=jnp.int32)
    placed = (to_owner[:, :, :, None] & slot_hot[:, :, None, :]).astype(BF)
    placed = placed.reshape(rows, 2, seqs * CAP)
    dispatch = placed[:, 0] + placed[:, 1]
    placed_pairs = jnp.concatenate([placed[:, 0], placed[:, 1]], axis=0)
    sent_rows = dot_tn(dispatch, normed_two).astype(BF).reshape(seqs, CAP, width)
    expert_rows = jnp.concatenate(send_out([sent_rows[s] for s in range(seqs)], seqs))
    gate_up = dot(expert_rows, gate_up_full)
    gate_part = gate_up[:, :piece]
    up_part = gate_up[:, piece:]
    sigmoid_gate = jax.nn.sigmoid(gate_part)
    hidden = (gate_part * sigmoid_gate * up_part).astype(BF)
    expert_out = dot_nt(hidden, down_full).astype(BF).reshape(seqs, CAP, width)
    returned = jnp.concatenate(send_back([expert_out[s] for s in range(seqs)], seqs))
    selected = dot(placed_pairs, returned).reshape(2, rows, width)
    mixed_exact = residual + gating[:, :1] * selected[0] + gating[:, 1:] * selected[1]
    valid_rows = valid.astype(F32)
    errors = (mixed_exact - teacher.astype(F32)) * valid_rows[:, None]
    squares = jnp.sum(errors * errors)
    loss_scale = width * seq_len // 8
    grad_mixed = errors * (2.0 * loss_scale / (width * valid_count))

    grad_gating = jnp.stack(
        [jnp.sum(selected[0] * grad_mixed, axis=-1), jnp.sum(selected[1] * grad_mixed, axis=-1)],
        axis=1,
    )
    grad_chosen = gating * (grad_gating - jnp.sum(gating * grad_gating, axis=-1, keepdims=True))
    grad_logits = jnp.sum(grad_chosen[:, :, None] * picked, axis=1).astype(BF)
    weighted = jnp.concatenate(
        [(gating[:, :1] * grad_mixed).astype(BF), (gating[:, 1:] * grad_mixed).astype(BF)], axis=0
    )
    sent_grads = dot_tn(placed_pairs, weighted).astype(BF).reshape(seqs, CAP, width)
    grad_expert_out = jnp.concatenate(send_out([sent_grads[s] for s in range(seqs)], seqs))
    grad_hidden = dot(grad_expert_out, down_full)
    grad_gate = grad_hidden * up_part * sigmoid_gate * (1.0 + gate_part * (1.0 - sigmoid_gate))
    grad_up = grad_hidden * gate_part * sigmoid_gate
    grad_gate_up_rows = jnp.concatenate([grad_gate, grad_up], axis=-1).astype(BF)
    grad_rows = dot_nt(grad_gate_up_rows, gate_up_full).astype(BF).reshape(seqs, CAP, width)
    grad_returned = jnp.concatenate(send_back([grad_rows[s] for s in range(seqs)], seqs))
    grad_down_shard = sum_product(
        split_columns(grad_expert_out, shard, shards), hidden, shard, shards
    )
    grad_down = lax.all_gather(grad_down_shard.astype(BF), "seq", axis=0, tiled=False)
    grad_gate_up_shard = sum_product(
        split_columns(expert_rows, shard, shards), grad_gate_up_rows, shard, shards
    )
    grad_gate_up = lax.all_gather(grad_gate_up_shard.astype(BF), "seq", axis=0, tiled=False)

    grad_normed_two = dot(dispatch, grad_returned) + dot_nt(grad_logits, router_full)
    grad_residual = grad_mixed + root_back(residual, factor_two, grad_normed_two)
    grad_branch = grad_residual.astype(BF)
    grad_attended = dot_nt(grad_branch, out_full).astype(BF)
    head_grad = lax.all_to_all(grad_attended, "seq", split_axis=1, concat_axis=0, tiled=True)

    grad_out_part = sum_product(split_columns(grad_branch, shard, shards), attended, shard, shards)
    cut = grad_out_part.astype(BF).reshape(part, seqs, q_cols)
    grad_out_own = jnp.zeros((part, q_cols), F32)
    for each in send_out([take(cut, (z + s) % seqs, 1) for s in range(seqs)], seqs):
        grad_out_own = grad_out_own + each.astype(F32)
    grad_out = from_relative(send_out([grad_out_own.astype(BF)] * seqs, seqs), z)
    grad_out = grad_out.transpose(0, 2, 1).reshape(HEADS * HD, part).astype(F32)

    grad_q, near_kv, far_kv = flash_backward(
        head_queries, kv_blocks, bias, head_grad, exact, lse, seqs, rows, local_kv, groups
    )
    grad_q = grad_q * scale
    there_kv = hop(far_kv, shards, 1)
    grad_kv = sum_chips(lambda m: near_kv[m].astype(F32) + there_kv[m].astype(F32), shards)
    token_grad_q = lax.all_to_all(
        grad_q.astype(BF), "seq", split_axis=0, concat_axis=1, tiled=True
    )
    token_grad_kv = lax.all_to_all(
        grad_kv.astype(BF), "seq", split_axis=0, concat_axis=1, tiled=True
    )
    grad_normed = dot_nt(token_grad_q, attn_full[:, : HEADS * HD]) + dot_nt(
        token_grad_kv, attn_full[:, HEADS * HD :]
    )
    grad_tokens = grad_residual + root_back(inputs, root(inputs), grad_normed)

    token_columns = split_columns(tokens_local, shard, shards)
    normed_columns = split_columns(normed_two, shard, shards)
    query_rhs = (grad_q * factor_local).astype(BF)
    marks = spread_scalar(squares, shard % 2, width // 2)
    grad_query_part = sum_parts(
        *[
            jnp.concatenate(
                [dot_tn(columns, query_rhs).astype(BF), dot_tn(others, grad_logits).astype(BF), marks],
                axis=1,
            )
            for columns, others in zip(token_columns, normed_columns)
        ],
        shard,
        shards,
    )
    grad_keyval_part = sum_product(
        token_columns, (grad_kv * factor_local).astype(BF), shard, shards
    )
    base_cols = q_cols + experts
    plane_squares = jnp.sum(grad_query_part[:, base_cols:], axis=1, keepdims=True)
    plane_high = plane_squares.astype(BF)
    plane_low = (plane_squares - plane_high.astype(F32)).astype(BF)
    grad_query_base = from_relative(
        send_out(
            [jnp.concatenate([grad_query_part[:, :base_cols].astype(BF), plane_high, plane_low], axis=1)]
            * seqs,
            seqs,
        ),
        z,
    ).astype(F32)
    loss_value = jnp.sum(grad_query_base[:, 0, base_cols:]) / (width * valid_count)
    grad_router_base = jnp.sum(grad_query_base[:, :, q_cols:base_cols], axis=0)
    grad_query_base = grad_query_base[:, :, :q_cols].transpose(1, 0, 2).reshape(part, HEADS * HD)
    grad_keyval_base = (
        from_relative(send_out([grad_keyval_part.astype(BF)] * seqs, seqs), z)
        .astype(F32)
        .transpose(1, 0, 2)
        .reshape(part, 2 * KVH * HD)
    )

    grad_gain_attn = jnp.sum(w_query.astype(F32) * grad_query_base, axis=1) + jnp.sum(
        w_keyval.astype(F32) * grad_keyval_base, axis=1
    )
    grad_down = (
        grad_down.reshape(experts, split, part, piece)
        .transpose(0, 1, 3, 2)
        .reshape(experts, units, part)
        .astype(F32)
    )
    grad_gate_up = grad_gate_up.astype(F32)
    if split > 1:
        grad_gate_up = (
            grad_gate_up.reshape(experts, split, part, 2, piece)
            .transpose(0, 2, 3, 1, 4)
            .reshape(experts, part, both)
        )
    grad_gain_ffn = jnp.sum(w_gate_up.astype(F32) * grad_gate_up, axis=(0, 2)) + jnp.sum(
        w_router.astype(F32) * grad_router_base, axis=1
    )
    return (
        mixed_exact.astype(BF),
        loss_value,
        grad_tokens,
        grad_gain_attn,
        grad_query_base * gain_one,
        grad_keyval_base * gain_one,
        grad_out,
        grad_gain_ffn,
        grad_router_base * gain_two,
        grad_gate_up * gain_two,
        grad_down,
    )


def solution(mesh):
    return jax.shard_map(
        local,
        mesh=mesh,
        in_specs=(
            P(("seq", "fsdp"), None),
            P(("seq", "fsdp"), None),
            P(("seq", "fsdp")),
            P(("seq", "fsdp"), None),
            P(("seq", "fsdp"), None),
            P("fsdp"),
            P("fsdp", None),
            P("fsdp", None),
            P(None, "fsdp"),
            P("fsdp"),
            P("fsdp", None),
            P(None, "fsdp", None),
            P(None, None, "fsdp"),
        ),
        out_specs=(
            P(("seq", "fsdp"), None),
            P(),
            P(("seq", "fsdp"), None),
            P("fsdp"),
            P("fsdp", None),
            P("fsdp", None),
            P(None, "fsdp"),
            P("fsdp"),
            P("fsdp", None),
            P(None, "fsdp", None),
            P(None, None, "fsdp"),
        ),
        check_vma=False,
    )
```

```python
import functools

import jax
import jax.numpy as jnp
from jax import lax
from jax.experimental import pallas as pl
from jax.experimental.pallas import tpu as pltpu
from jax.sharding import PartitionSpec as P

HEADS = 24
KVH = 8
HD = 64
CAP = 96
EPSILON = 1e-06
FLOOR_SCORE = -1e30
BF = jnp.bfloat16
F32 = jnp.float32


def dot(a, b):
    return jnp.dot(a, b, preferred_element_type=F32)


def dot_nt(a, b):
    return lax.dot_general(a, b, (((1,), (1,)), ((), ())), preferred_element_type=F32)


def dot_tn(a, b):
    return lax.dot_general(a, b, (((0,), (0,)), ((), ())), preferred_element_type=F32)


def own_mask(valid_row, rows):
    i = lax.broadcasted_iota(jnp.int32, (rows, rows), 0)
    j = lax.broadcasted_iota(jnp.int32, (rows, rows), 1)
    return jnp.where(j == i, 0.0, jnp.where(j < i, valid_row, FLOOR_SCORE))


def key_chunk(kv_refs, zk, rows, g):
    return jnp.concatenate(
        [ref[pl.ds(zk * rows, rows), pl.ds(g * 2 * HD, 2 * HD)] for ref in kv_refs], axis=0
    )


def forward_kernel(shards, seqs, rows, local_kv, groups, *refs):
    kv_refs = refs[:shards]
    q_ref, bias_ref, low_ref, exact_ref, lse_ref, acc_ref, max_ref = refs[shards:]
    zq = pl.program_id(0)
    stack = groups * rows
    zeros = jnp.zeros((rows, HD), BF)
    half = lax.broadcasted_iota(jnp.int32, (1, 2 * HD), 1) < HD

    def queries(g):
        parts = []
        for h in range(groups):
            start = (g * groups + h) * HD
            parts.append(jnp.concatenate([q_ref[:, start : start + HD], zeros], axis=1))
        return jnp.concatenate(parts, axis=0)

    def chunk(g, zk, scores):
        first = scores is None
        keys = key_chunk(kv_refs, zk, rows, g)
        raw = dot_nt(queries(g), keys)
        if first:
            row = bias_ref[seqs + zk]
            mask = own_mask(row[:, :rows], rows)
            mask = jnp.concatenate([mask] * groups, axis=0)
            masked = jnp.concatenate([raw[:, :rows] + mask, raw[:, rows:] + row[:, rows:]], axis=1)
            new_max = jnp.max(masked, axis=1, keepdims=True)
        else:
            masked = raw + bias_ref[zk]
            new_max = jnp.maximum(max_ref[g][:, :1], jnp.max(masked, axis=1, keepdims=True))
        terms = jnp.exp(masked - new_max).astype(BF)
        ones_values = jnp.where(half, jnp.ones_like(keys), keys)
        part = dot(terms, ones_values)
        if first:
            acc_ref[g] = part
        else:
            acc_ref[g] = acc_ref[g] * jnp.exp(max_ref[g][:, :1] - new_max) + part
        max_ref[g] = jnp.broadcast_to(new_max, (stack, 2 * HD))

    for g in range(local_kv):
        chunk(g, zq, None)

    @pl.loop(0, zq)
    def _(zk):
        for g in range(local_kv):
            chunk(g, zk, True)

    exact_parts, lse_parts = [], []
    for g in range(local_kv):
        acc = acc_ref[g]
        total = acc[:, :HD]
        exact = acc[:, HD:] / total
        lse = max_ref[g][:, :HD] + jnp.log(total)
        for h in range(groups):
            exact_parts.append(exact[h * rows : (h + 1) * rows])
            lse_parts.append(lse[h * rows : (h + 1) * rows])
    exact = jnp.concatenate(exact_parts, axis=1)
    exact_ref[...] = exact
    low_ref[...] = exact.astype(BF)
    lse_ref[...] = jnp.concatenate(lse_parts, axis=1)


def flash_forward(q, kv_blocks, bias, seqs, rows, local_kv, groups):
    shards = len(kv_blocks)
    q_cols = q.shape[1]
    kv_spec = pl.BlockSpec(kv_blocks[0].shape, lambda i: (0, 0))
    q_spec = pl.BlockSpec((rows, q_cols), lambda i: (i, 0))
    stack = groups * rows
    out = jax.ShapeDtypeStruct((seqs * rows, q_cols), F32)
    return pl.pallas_call(
        functools.partial(forward_kernel, shards, seqs, rows, local_kv, groups),
        grid=(seqs,),
        in_specs=[kv_spec] * shards + [q_spec, pl.BlockSpec(bias.shape, lambda i: (0, 0, 0))],
        out_specs=[q_spec] * 3,
        out_shape=[jax.ShapeDtypeStruct((seqs * rows, q_cols), BF), out, out],
        scratch_shapes=[
            pltpu.VMEM((local_kv, stack, 2 * HD), F32),
            pltpu.VMEM((local_kv, stack, 2 * HD), F32),
        ],
        compiler_params=pltpu.CompilerParams(vmem_limit_bytes=40 * 1024 * 1024),
        cost_estimate=pl.CostEstimate(
            flops=8 * seqs * seqs * shards * rows * rows * local_kv * groups * HD,
            bytes_accessed=8 * 1024 * 1024,
            transcendentals=seqs * seqs * shards * rows * rows * local_kv * groups // 2,
        ),
    )(*kv_blocks, q, bias)


def backward_kernel(shards, seqs, rows, g, groups, *refs):
    kv_refs = refs[:shards]
    (
        q_ref, bias_ref, grad_ref, exact_ref, lse_ref, grad_q_ref, near_ref, far_ref,
        pair_ref, pair_t_ref, lse_wide, delta_wide, acc_q, acc_kv,
    ) = refs[shards:]
    zk = pl.program_id(0)
    stack = groups * rows
    zeros = jnp.zeros((rows, HD), BF)

    @pl.when(zk == 0)
    def _():
        acc_q[...] = jnp.zeros_like(acc_q)

        @pl.loop(0, seqs)
        def _(zq):
            here = pl.ds(zq * rows, rows)
            tops, bottoms = [], []
            for h in range(groups):
                cols = slice((g * groups + h) * HD, (g * groups + h + 1) * HD)
                grad = grad_ref[here, cols]
                tops.append(jnp.concatenate([q_ref[here, cols], zeros], axis=1))
                bottoms.append(jnp.concatenate([zeros, grad], axis=1))
                delta = jnp.sum(grad.astype(F32) * exact_ref[here, cols], axis=1, keepdims=True)
                part = slice(h * rows, (h + 1) * rows)
                delta_wide[zq, part] = jnp.broadcast_to(delta, (rows, 2 * HD))
                lse_wide[zq, part] = jnp.broadcast_to(lse_ref[here, cols][:, :1], (rows, 2 * HD))
            pair = jnp.concatenate(tops + bottoms, axis=0)
            pair_ref[zq] = pair
            pair_t_ref[zq] = pair.astype(F32).T.astype(BF)

    def chunk(zq, first):
        keys = key_chunk(kv_refs, zk, rows, g)
        both = dot_nt(pair_ref[zq], keys)
        raw, products = both[:stack], both[stack:]
        if first:
            row = bias_ref[seqs + zk]
            mask = own_mask(row[:, :rows], rows)
            mask = jnp.concatenate([mask] * groups, axis=0)
            masked = jnp.concatenate([raw[:, :rows] + mask, raw[:, rows:] + row[:, rows:]], axis=1)
        else:
            masked = raw + bias_ref[zk]
        weights = jnp.exp(masked - lse_wide[zq][:, :1])
        grads = (weights * (products - delta_wide[zq][:, :1])).astype(BF)
        acc_q[zq] += dot(grads, keys)
        part = dot(pair_t_ref[zq], jnp.concatenate([grads, weights.astype(BF)], axis=0))
        if first:
            acc_kv[...] = part
        else:
            acc_kv[...] += part

    chunk(zk, True)

    @pl.loop(zk + 1, seqs)
    def _(zq):
        chunk(zq, False)

    for p in range(shards):
        target = near_ref if p < shards // 2 else far_ref
        target[p % (shards // 2)] = acc_kv[:, p * rows : (p + 1) * rows].T.astype(BF)

    @pl.when(zk == seqs - 1)
    def _():
        @pl.loop(0, seqs)
        def _(zq):
            total = acc_q[zq]
            parts = [total[h * rows : (h + 1) * rows, :HD] for h in range(groups)]
            grad_q_ref[pl.ds(zq * rows, rows), :] = jnp.concatenate(parts, axis=1)


def flash_backward(q, kv_blocks, bias, grad, exact, lse, seqs, rows, g, groups):
    shards = len(kv_blocks)
    q_cols = q.shape[1]
    stack = groups * rows
    kv_spec = pl.BlockSpec(kv_blocks[0].shape, lambda i: (0, 0))
    whole = pl.BlockSpec((seqs * rows, q_cols), lambda i: (0, 0))
    grad_q_shape = (seqs * rows, groups * HD)
    out_spec = pl.BlockSpec((shards // 2, rows, 2 * HD), lambda i: (0, i, 0))
    out = jax.ShapeDtypeStruct((shards // 2, seqs * rows, 2 * HD), BF)
    return pl.pallas_call(
        functools.partial(backward_kernel, shards, seqs, rows, g, groups),
        grid=(seqs,),
        in_specs=[kv_spec] * shards
        + [whole, pl.BlockSpec(bias.shape, lambda i: (0, 0, 0)), whole, whole, whole],
        out_specs=[pl.BlockSpec(grad_q_shape, lambda i: (0, 0)), out_spec, out_spec],
        out_shape=[jax.ShapeDtypeStruct(grad_q_shape, F32), out, out],
        scratch_shapes=[
            pltpu.VMEM((seqs, 2 * stack, 2 * HD), BF),
            pltpu.VMEM((seqs, 2 * HD, 2 * stack), BF),
            pltpu.VMEM((seqs, stack, 2 * HD), F32),
            pltpu.VMEM((seqs, stack, 2 * HD), F32),
            pltpu.VMEM((seqs, stack, 2 * HD), F32),
            pltpu.VMEM((2 * HD, shards * rows), F32),
        ],
        compiler_params=pltpu.CompilerParams(vmem_limit_bytes=40 * 1024 * 1024),
        cost_estimate=pl.CostEstimate(
            flops=40 * seqs * seqs * shards * rows * rows * groups * HD,
            bytes_accessed=8 * 1024 * 1024,
            transcendentals=seqs * seqs * shards * rows * rows * groups // 2,
        ),
    )(*kv_blocks, q, bias, grad, exact, lse)


def shift(block, count, step):
    return lax.ppermute(block, "seq", [(i, (i + step) % count) for i in range(count)])


def send_out(blocks, count):
    return [blocks[0]] + [shift(blocks[s], count, s) for s in range(1, count)]


def send_back(blocks, count):
    return [blocks[0]] + [shift(blocks[s], count, count - s) for s in range(1, count)]


def from_relative(blocks, place):
    count = len(blocks)
    rising = jnp.stack([blocks[-s % count] for s in range(count)])
    return lax.dynamic_slice_in_dim(jnp.concatenate([rising, rising]), count - place, count, 0)


def hop(block, count, mask):
    return lax.ppermute(block, "fsdp", [(i, i ^ mask) for i in range(count)])


def gather_shards(block, count):
    near = [block] + [hop(block, count, 2 * m) for m in range(1, count // 2)]
    return near + [hop(each, count, 1) for each in near]


def send_chips(parts, count):
    return [parts[0]] + [hop(parts[m], count, 2 * m) for m in range(1, count // 2)]


def total_of(blocks):
    total = blocks[0].astype(F32)
    for each in blocks[1:]:
        total = total + each.astype(F32)
    return total


def take(array, index, axis):
    return lax.dynamic_index_in_dim(array, index, axis, keepdims=False)


def pair_halves(product, shard, count):
    width, cols = product.shape
    cut = product.reshape(count // 2, 2, width // count, cols)
    core = shard % 2
    return take(cut, core, 1), hop(take(cut, 1 - core, 1), count, 1)


def pair_sums(halves, shard):
    here, there = halves
    chip = shard // 2
    sums = []
    for m in range(here.shape[0]):
        each = take(here, chip ^ m, 0).astype(F32) + take(there, chip ^ m, 0).astype(F32)
        sums.append(each if m == 0 else each.astype(BF))
    return sums


def sum_rows(product, shard, count):
    return total_of(send_chips(pair_sums(pair_halves(product, shard, count), shard), count))


def spread_scalar(value, core, rows):
    high = value.astype(BF)
    low = (value - high.astype(F32)).astype(BF)
    pair = jnp.stack([high, low])
    none = jnp.zeros_like(pair)
    row = jnp.where(core == 0, jnp.concatenate([pair, none]), jnp.concatenate([none, pair]))
    return jnp.broadcast_to(row[None, :], (rows, 4))


def after(values, *others):
    return lax.optimization_barrier((values, others))[0]


def root(values):
    return lax.rsqrt(jnp.mean(values * values, axis=-1, keepdims=True) + EPSILON)


def root_back(values, factor, grad_scaled):
    inner = jnp.mean(grad_scaled * values, axis=-1, keepdims=True)
    return factor * grad_scaled - values * (factor * factor * factor * inner)


def local(
    tokens,
    teacher,
    valid,
    routes,
    slots,
    gain_attn,
    w_query,
    w_keyval,
    w_out,
    gain_ffn,
    w_router,
    w_gate_up,
    w_down,
):
    seqs = lax.axis_size("seq")
    shards = lax.axis_size("fsdp")
    z = lax.axis_index("seq")
    shard = lax.axis_index("fsdp")
    rows, width = tokens.shape
    groups = HEADS // KVH
    local_kv = KVH // seqs
    q_cols = local_kv * groups * HD
    kv_cols = local_kv * 2 * HD
    local_rows = rows * seqs
    seq_len = local_rows * shards
    experts, part, both = w_gate_up.shape
    units = both // 2
    split = seqs // experts
    piece = units // split
    expert = z // split
    fraction = z % split
    scale = HD ** (-0.5)

    gain_one = gain_attn.astype(F32)[:, None]
    gain_two = gain_ffn.astype(F32)[:, None]
    heads_shard = jnp.concatenate(
        [
            lax.dynamic_slice_in_dim(w_query, z * q_cols, q_cols, 1),
            lax.dynamic_slice_in_dim(w_keyval, z * kv_cols, kv_cols, 1),
        ],
        axis=1,
    )
    heads_shard = (heads_shard.astype(F32) * gain_one).astype(BF)
    heads_full = lax.all_gather(heads_shard, "fsdp", axis=0, tiled=True)
    token_blocks = send_out([tokens] * seqs, seqs)
    late_gate_up, late_down, late_valid = after((w_gate_up, w_down, valid), token_blocks[1])
    out_full = lax.all_gather(w_out, "fsdp", axis=1, tiled=True)
    router_full = lax.all_gather(
        (w_router.astype(F32) * gain_two).astype(BF), "fsdp", axis=0, tiled=True
    )
    own_expert = take(late_gate_up, expert, 0)
    gate_shard = lax.dynamic_slice_in_dim(own_expert, fraction * piece, piece, 1)
    up_shard = lax.dynamic_slice_in_dim(own_expert, units + fraction * piece, piece, 1)
    down_shard = lax.dynamic_slice_in_dim(
        take(late_down, expert, 0), fraction * piece, piece, 0
    ).T
    expert_shard = jnp.concatenate(
        [
            (gate_shard.astype(F32) * gain_two).astype(BF),
            (up_shard.astype(F32) * gain_two).astype(BF),
            down_shard,
        ],
        axis=1,
    )
    expert_full = lax.all_gather(expert_shard, "fsdp", axis=0, tiled=True)
    gate_up_full = expert_full[:, : 2 * piece]
    down_full = expert_full[:, 2 * piece :]
    valid_low = late_valid.astype(BF).reshape(1, rows)
    valid_local = from_relative(send_out([valid_low] * seqs, seqs), z)
    projected = []
    for block in token_blocks:
        projected.append(dot(block, heads_full) * root(block.astype(F32)))
    projected = from_relative([each.astype(BF) for each in projected], z)
    projected = projected.reshape(local_rows, q_cols + kv_cols)
    head_queries = projected[:, :q_cols] * jnp.asarray(scale, BF)

    valid_rows_kv = local_rows // kv_cols
    payload = jnp.concatenate(
        [
            projected[:, q_cols:],
            valid_local.reshape(valid_rows_kv, kv_cols),
            jnp.zeros((16 - valid_rows_kv, kv_cols), BF),
        ],
        axis=0,
    )
    kv_blocks = gather_shards(payload, shards)
    order = jnp.asarray(
        [2 * m for m in range(shards // 2)] + [2 * m + 1 for m in range(shards // 2)], jnp.int32
    )
    valid_all = jnp.stack(
        [
            each[local_rows : local_rows + valid_rows_kv].reshape(seqs, rows)
            for each in kv_blocks
        ],
        axis=1,
    ).astype(F32)
    valid_count = jnp.sum(valid_all)
    bias = jnp.where(valid_all > 0, 0.0, FLOOR_SCORE)
    earlier = ((order ^ shard) < shard) | (order == 0)
    bias_same = jnp.where(earlier[None, :, None], bias, FLOOR_SCORE)
    bias = jnp.concatenate([bias, bias_same]).reshape(2 * seqs, 1, shards * rows)
    attended_low, exact, lse = flash_forward(
        head_queries, kv_blocks, bias, seqs, rows, local_kv, groups
    )
    attended = lax.all_to_all(attended_low, "seq", split_axis=0, concat_axis=1, tiled=True)

    late_query, late_keyval = after((w_query, w_keyval), attended)
    attn_shard = jnp.concatenate([late_query, late_keyval], axis=1)
    attn_full = lax.all_gather(
        (attn_shard.astype(F32) * gain_one).astype(BF), "fsdp", axis=0, tiled=True
    )
    inputs = tokens.astype(F32)
    residual = inputs + dot(attended, out_full)
    factor_two = root(residual)
    normed_two = (residual * factor_two).astype(BF)
    logits = dot(normed_two, router_full)
    expert_ids = jnp.arange(experts, dtype=jnp.int32)
    picked = (routes[:, :, None] == expert_ids).astype(F32)
    chosen = jnp.sum(picked * logits[:, None, :], axis=-1)
    gating = jax.nn.softmax(chosen, axis=-1)
    owners = ((jnp.arange(seqs, dtype=jnp.int32) + z) % seqs) // split
    to_owner = routes[:, :, None] == owners
    slot_hot = slots[:, :, None] == jnp.arange(CAP, dtype=jnp.int32)
    placed = (to_owner[:, :, :, None] & slot_hot[:, :, None, :]).astype(BF)
    placed = placed.reshape(rows, 2, seqs * CAP)
    dispatch = placed[:, 0] + placed[:, 1]
    placed_pairs = jnp.concatenate([placed[:, 0], placed[:, 1]], axis=0)
    sent_rows = dot_tn(dispatch, normed_two).astype(BF).reshape(seqs, CAP, width)
    expert_rows = jnp.concatenate(send_out([sent_rows[s] for s in range(seqs)], seqs))
    gate_up = dot(expert_rows, gate_up_full)
    gate_part = gate_up[:, :piece]
    up_part = gate_up[:, piece:]
    sigmoid_gate = jax.nn.sigmoid(gate_part)
    hidden = (gate_part * sigmoid_gate * up_part).astype(BF)
    expert_out = dot_nt(hidden, down_full).astype(BF).reshape(seqs, CAP, width)
    returned = jnp.concatenate(send_back([expert_out[s] for s in range(seqs)], seqs))
    selected = dot(placed_pairs, returned).reshape(2, rows, width)
    mixed_exact = residual + gating[:, :1] * selected[0] + gating[:, 1:] * selected[1]
    valid_rows = valid.astype(F32)
    errors = (mixed_exact - teacher.astype(F32)) * valid_rows[:, None]
    squares = jnp.sum(errors * errors)
    loss_scale = width * seq_len // 8
    grad_mixed = errors * (2.0 * loss_scale / (width * valid_count))

    grad_gating = jnp.stack(
        [jnp.sum(selected[0] * grad_mixed, axis=-1), jnp.sum(selected[1] * grad_mixed, axis=-1)],
        axis=1,
    )
    grad_chosen = gating * (grad_gating - jnp.sum(gating * grad_gating, axis=-1, keepdims=True))
    grad_logits = jnp.sum(grad_chosen[:, :, None] * picked, axis=1).astype(BF)
    weighted = jnp.concatenate(
        [(gating[:, :1] * grad_mixed).astype(BF), (gating[:, 1:] * grad_mixed).astype(BF)], axis=0
    )
    sent_grads = dot_tn(placed_pairs, weighted).astype(BF).reshape(seqs, CAP, width)
    grad_expert_out = jnp.concatenate(send_out([sent_grads[s] for s in range(seqs)], seqs))
    grad_expert_out = after(grad_expert_out, attn_full)
    grad_hidden = dot(grad_expert_out, down_full)
    grad_gate = grad_hidden * up_part * sigmoid_gate * (1.0 + gate_part * (1.0 - sigmoid_gate))
    grad_up = grad_hidden * gate_part * sigmoid_gate
    grad_gate_up_rows = jnp.concatenate([grad_gate, grad_up], axis=-1).astype(BF)
    grad_rows = dot_nt(grad_gate_up_rows, gate_up_full).astype(BF).reshape(seqs, CAP, width)
    grad_returned = jnp.concatenate(send_back([grad_rows[s] for s in range(seqs)], seqs))
    held_out, held_hidden = after((grad_expert_out, hidden), grad_rows)
    grad_down_sums = pair_sums(
        pair_halves(dot_tn(held_out, held_hidden).astype(BF), shard, shards), shard
    )
    held_rows, held_gate_up = after((expert_rows, grad_gate_up_rows), grad_rows)
    grad_gate_up_halves = pair_halves(
        dot_tn(held_rows, held_gate_up).astype(BF), shard, shards
    )
    grad_returned = after(grad_returned, grad_down_sums)
    late_blocks = after(token_blocks, sent_grads)
    tokens_local = from_relative(late_blocks, z).reshape(local_rows, width)
    factor_local = root(tokens_local.astype(F32))

    grad_normed_two = dot(dispatch, grad_returned) + dot_nt(grad_logits, router_full)
    grad_residual = grad_mixed + root_back(residual, factor_two, grad_normed_two)
    grad_branch = grad_residual.astype(BF)
    grad_attended = dot_nt(grad_branch, out_full).astype(BF)
    head_grad = lax.all_to_all(grad_attended, "seq", split_axis=1, concat_axis=0, tiled=True)
    grad_down_shard = total_of(send_chips(grad_down_sums, shards)).astype(BF)
    grad_down = lax.all_gather(grad_down_shard, "seq", axis=0, tiled=False)
    grad_gate_up_sums = pair_sums(after(grad_gate_up_halves, grad_attended), shard)
    grad_gate_up_blocks = send_chips(grad_gate_up_sums, shards)

    grad_out_halves = pair_halves(dot_tn(grad_branch, attended).astype(BF), shard, shards)

    grad_q, near, far = [], [], []
    held = after(head_grad, grad_down_shard, grad_gate_up_sums, grad_out_halves)
    for g in range(local_kv):
        part_q, near_kv, far_kv = flash_backward(
            head_queries, kv_blocks, bias, held, exact, lse, seqs, rows, g, groups
        )
        grad_q.append(part_q * scale)
        near.append(near_kv)
        far.append(far_kv)
        if g == 0:
            grad_gate_up_shard = total_of(after(grad_gate_up_blocks, part_q)).astype(BF)
            grad_out_sums = pair_sums(after(grad_out_halves, part_q), shard)
            held = after(head_grad, grad_gate_up_shard, grad_out_sums)
    grad_gate_up = lax.all_gather(grad_gate_up_shard, "seq", axis=0, tiled=False)
    near = jnp.concatenate(near, axis=2)
    there = hop(jnp.concatenate(far, axis=2), shards, 1)
    pairs = [near[m].astype(F32) + there[m].astype(F32) for m in range(shards // 2)]
    pairs = [pairs[0]] + [each.astype(BF) for each in pairs[1:]]
    grad_q = jnp.concatenate(grad_q, axis=1)
    grad_kv = total_of(send_chips(pairs, shards))
    token_grad_q = lax.all_to_all(
        grad_q.astype(BF), "seq", split_axis=0, concat_axis=1, tiled=True
    )
    token_grad_kv = lax.all_to_all(
        grad_kv.astype(BF), "seq", split_axis=0, concat_axis=1, tiled=True
    )
    grad_out_part = total_of(after(send_chips(grad_out_sums, shards), pairs))
    cut = grad_out_part.astype(BF).reshape(part, seqs, q_cols)
    grad_out_own = jnp.zeros((part, q_cols), F32)
    out_parts = send_out([take(cut, (z + s) % seqs, 1) for s in range(seqs)], seqs)
    for each in after(out_parts, grad_kv):
        grad_out_own = grad_out_own + each.astype(F32)
    grad_out = from_relative(send_out([grad_out_own.astype(BF)] * seqs, seqs), z)
    grad_out = grad_out.transpose(0, 2, 1).reshape(HEADS * HD, part).astype(F32)
    grad_normed = dot_nt(token_grad_q, attn_full[:, : HEADS * HD]) + dot_nt(
        token_grad_kv, attn_full[:, HEADS * HD :]
    )
    grad_tokens = grad_residual + root_back(inputs, root(inputs), grad_normed)

    query_rhs = (grad_q * factor_local).astype(BF)
    marks = spread_scalar(squares, shard % 2, width)
    query_product = jnp.concatenate(
        [
            dot_tn(tokens_local, query_rhs).astype(BF),
            dot_tn(normed_two, grad_logits).astype(BF),
            marks,
        ],
        axis=1,
    )
    grad_query_part = sum_rows(after(query_product, pairs), shard, shards)
    keyval_rhs = (grad_kv * factor_local).astype(BF)
    grad_keyval_part = sum_rows(dot_tn(tokens_local, keyval_rhs).astype(BF), shard, shards)
    base_cols = q_cols + experts
    plane_squares = jnp.sum(grad_query_part[:, base_cols:], axis=1, keepdims=True)
    plane_high = plane_squares.astype(BF)
    plane_low = (plane_squares - plane_high.astype(F32)).astype(BF)
    grad_query_base = from_relative(
        send_out(
            [jnp.concatenate([grad_query_part[:, :base_cols].astype(BF), plane_high, plane_low], axis=1)]
            * seqs,
            seqs,
        ),
        z,
    ).astype(F32)
    loss_value = jnp.sum(grad_query_base[:, 0, base_cols:]) / (width * valid_count)
    grad_router_base = jnp.sum(grad_query_base[:, :, q_cols:base_cols], axis=0)
    grad_query_base = grad_query_base[:, :, :q_cols].transpose(1, 0, 2).reshape(part, HEADS * HD)
    grad_keyval_base = (
        from_relative(send_out([grad_keyval_part.astype(BF)] * seqs, seqs), z)
        .astype(F32)
        .transpose(1, 0, 2)
        .reshape(part, 2 * KVH * HD)
    )

    grad_gain_attn = jnp.sum(w_query.astype(F32) * grad_query_base, axis=1) + jnp.sum(
        w_keyval.astype(F32) * grad_keyval_base, axis=1
    )
    grad_down = (
        grad_down.reshape(experts, split, part, piece)
        .transpose(0, 1, 3, 2)
        .reshape(experts, units, part)
        .astype(F32)
    )
    grad_gate_up = grad_gate_up.astype(F32)
    if split > 1:
        grad_gate_up = (
            grad_gate_up.reshape(experts, split, part, 2, piece)
            .transpose(0, 2, 3, 1, 4)
            .reshape(experts, part, both)
        )
    grad_gain_ffn = jnp.sum(w_gate_up.astype(F32) * grad_gate_up, axis=(0, 2)) + jnp.sum(
        w_router.astype(F32) * grad_router_base, axis=1
    )
    return (
        mixed_exact.astype(BF),
        loss_value,
        grad_tokens,
        grad_gain_attn,
        grad_query_base * gain_one,
        grad_keyval_base * gain_one,
        grad_out,
        grad_gain_ffn,
        grad_router_base * gain_two,
        grad_gate_up * gain_two,
        grad_down,
    )


def solution(mesh):
    return jax.shard_map(
        local,
        mesh=mesh,
        in_specs=(
            P(("seq", "fsdp"), None),
            P(("seq", "fsdp"), None),
            P(("seq", "fsdp")),
            P(("seq", "fsdp"), None),
            P(("seq", "fsdp"), None),
            P("fsdp"),
            P("fsdp", None),
            P("fsdp", None),
            P(None, "fsdp"),
            P("fsdp"),
            P("fsdp", None),
            P(None, "fsdp", None),
            P(None, None, "fsdp"),
        ),
        out_specs=(
            P(("seq", "fsdp"), None),
            P(),
            P(("seq", "fsdp"), None),
            P("fsdp"),
            P("fsdp", None),
            P("fsdp", None),
            P(None, "fsdp"),
            P("fsdp"),
            P("fsdp", None),
            P(None, "fsdp", None),
            P(None, None, "fsdp"),
        ),
        check_vma=False,
    )
```

```python
import functools

import jax
import jax.numpy as jnp
from jax import lax
from jax.experimental import pallas as pl
from jax.experimental.pallas import tpu as pltpu
from jax.sharding import PartitionSpec as P

HEADS = 24
KVH = 8
HD = 64
CAP = 96
LANES = 128
EPSILON = 1e-06
FLOOR_SCORE = -1e30
BF = jnp.bfloat16
F32 = jnp.float32


def dot(a, b):
    return jnp.dot(a, b, preferred_element_type=F32)


def dot_nt(a, b):
    return lax.dot_general(a, b, (((1,), (1,)), ((), ())), preferred_element_type=F32)


def dot_tn(a, b):
    return lax.dot_general(a, b, (((0,), (0,)), ((), ())), preferred_element_type=F32)


def own_mask(valid_row, rows):
    i = lax.broadcasted_iota(jnp.int32, (rows, rows), 0)
    j = lax.broadcasted_iota(jnp.int32, (rows, rows), 1)
    return jnp.where(j == i, 0.0, jnp.where(j < i, valid_row, FLOOR_SCORE))


def key_chunk(kv_refs, zk, rows, g):
    return jnp.concatenate(
        [ref[pl.ds(zk * rows, rows), pl.ds(g * 2 * HD, 2 * HD)] for ref in kv_refs], axis=0
    )


def forward_kernel(shards, seqs, rows, local_kv, groups, *refs):
    kv_refs = refs[:shards]
    q_ref, bias_ref, low_ref, exact_ref, lse_ref, acc_ref, max_ref = refs[shards:]
    zq = pl.program_id(0)
    stack = groups * rows
    zeros = jnp.zeros((rows, HD), BF)
    half = lax.broadcasted_iota(jnp.int32, (1, 2 * HD), 1) < HD

    def queries(g):
        parts = []
        for h in range(groups):
            start = (g * groups + h) * HD
            parts.append(jnp.concatenate([q_ref[:, start : start + HD], zeros], axis=1))
        return jnp.concatenate(parts, axis=0)

    def chunk(g, zk, scores):
        first = scores is None
        keys = key_chunk(kv_refs, zk, rows, g)
        raw = dot_nt(queries(g), keys)
        if first:
            row = bias_ref[seqs + zk]
            mask = own_mask(row[:, :rows], rows)
            mask = jnp.concatenate([mask] * groups, axis=0)
            masked = jnp.concatenate([raw[:, :rows] + mask, raw[:, rows:] + row[:, rows:]], axis=1)
            new_max = jnp.max(masked, axis=1, keepdims=True)
        else:
            masked = raw + bias_ref[zk]
            new_max = jnp.maximum(max_ref[g][:, :1], jnp.max(masked, axis=1, keepdims=True))
        terms = jnp.exp(masked - new_max).astype(BF)
        ones_values = jnp.where(half, jnp.ones_like(keys), keys)
        part = dot(terms, ones_values)
        if first:
            acc_ref[g] = part
        else:
            acc_ref[g] = acc_ref[g] * jnp.exp(max_ref[g][:, :1] - new_max) + part
        max_ref[g] = jnp.broadcast_to(new_max, (stack, 2 * HD))

    for g in range(local_kv):
        chunk(g, zq, None)

    @pl.loop(0, zq)
    def _(zk):
        for g in range(local_kv):
            chunk(g, zk, True)

    exact_parts, lse_parts = [], []
    for g in range(local_kv):
        acc = acc_ref[g]
        total = acc[:, :HD]
        exact = acc[:, HD:] / total
        lse = max_ref[g][:, :HD] + jnp.log(total)
        for h in range(groups):
            exact_parts.append(exact[h * rows : (h + 1) * rows])
            lse_parts.append(lse[h * rows : (h + 1) * rows])
    exact = jnp.concatenate(exact_parts, axis=1)
    exact_ref[...] = exact
    low_ref[...] = exact.astype(BF)
    lse_ref[...] = jnp.concatenate(lse_parts, axis=1)


def flash_forward(q, kv_blocks, bias, seqs, rows, local_kv, groups):
    shards = len(kv_blocks)
    q_cols = q.shape[1]
    kv_spec = pl.BlockSpec(kv_blocks[0].shape, lambda i: (0, 0))
    q_spec = pl.BlockSpec((rows, q_cols), lambda i: (i, 0))
    stack = groups * rows
    out = jax.ShapeDtypeStruct((seqs * rows, q_cols), F32)
    return pl.pallas_call(
        functools.partial(forward_kernel, shards, seqs, rows, local_kv, groups),
        grid=(seqs,),
        in_specs=[kv_spec] * shards + [q_spec, pl.BlockSpec(bias.shape, lambda i: (0, 0, 0))],
        out_specs=[q_spec] * 3,
        out_shape=[jax.ShapeDtypeStruct((seqs * rows, q_cols), BF), out, out],
        scratch_shapes=[
            pltpu.VMEM((local_kv, stack, 2 * HD), F32),
            pltpu.VMEM((local_kv, stack, 2 * HD), F32),
        ],
        compiler_params=pltpu.CompilerParams(vmem_limit_bytes=60 * 1024 * 1024),
        cost_estimate=pl.CostEstimate(
            flops=8 * seqs * seqs * shards * rows * rows * local_kv * groups * HD,
            bytes_accessed=8 * 1024 * 1024,
            transcendentals=seqs * seqs * shards * rows * rows * local_kv * groups // 2,
        ),
    )(*kv_blocks, q, bias)


def backward_kernel(shards, seqs, rows, g, groups, *refs):
    kv_refs = refs[:shards]
    (
        q_ref, bias_ref, grad_ref, exact_ref, lse_ref, grad_q_ref, near_ref, far_ref,
        pair_ref, pair_t_ref, lse_wide, delta_wide, acc_q, acc_kv,
    ) = refs[shards:]
    zk = pl.program_id(0)
    stack = groups * rows
    zeros = jnp.zeros((rows, HD), BF)

    @pl.when(zk == 0)
    def _():
        acc_q[...] = jnp.zeros_like(acc_q)

        @pl.loop(0, seqs)
        def _(zq):
            here = pl.ds(zq * rows, rows)
            tops, bottoms = [], []
            for h in range(groups):
                cols = slice((g * groups + h) * HD, (g * groups + h + 1) * HD)
                grad = grad_ref[here, cols]
                tops.append(jnp.concatenate([q_ref[here, cols], zeros], axis=1))
                bottoms.append(jnp.concatenate([zeros, grad], axis=1))
                delta = jnp.sum(grad.astype(F32) * exact_ref[here, cols], axis=1, keepdims=True)
                part = slice(h * rows, (h + 1) * rows)
                delta_wide[zq, part] = jnp.broadcast_to(delta, (rows, 2 * HD))
                lse_wide[zq, part] = jnp.broadcast_to(lse_ref[here, cols][:, :1], (rows, 2 * HD))
            pair = jnp.concatenate(tops + bottoms, axis=0)
            pair_ref[zq] = pair
            pair_t_ref[zq] = pair.astype(F32).T.astype(BF)

    def chunk(zq, first):
        keys = key_chunk(kv_refs, zk, rows, g)
        both = dot_nt(pair_ref[zq], keys)
        raw, products = both[:stack], both[stack:]
        if first:
            row = bias_ref[seqs + zk]
            mask = own_mask(row[:, :rows], rows)
            mask = jnp.concatenate([mask] * groups, axis=0)
            masked = jnp.concatenate([raw[:, :rows] + mask, raw[:, rows:] + row[:, rows:]], axis=1)
        else:
            masked = raw + bias_ref[zk]
        weights = jnp.exp(masked - lse_wide[zq][:, :1])
        grads = (weights * (products - delta_wide[zq][:, :1])).astype(BF)
        acc_q[zq] += dot(grads, keys)
        part = dot(pair_t_ref[zq], jnp.concatenate([grads, weights.astype(BF)], axis=0))
        if first:
            acc_kv[...] = part
        else:
            acc_kv[...] += part

    chunk(zk, True)

    @pl.loop(zk + 1, seqs)
    def _(zq):
        chunk(zq, False)

    for p in range(shards):
        target = near_ref if p < shards // 2 else far_ref
        target[p % (shards // 2)] = acc_kv[:, p * rows : (p + 1) * rows].T.astype(BF)

    @pl.when(zk == seqs - 1)
    def _():
        @pl.loop(0, seqs)
        def _(zq):
            total = acc_q[zq]
            parts = [total[h * rows : (h + 1) * rows, :HD] for h in range(groups)]
            grad_q_ref[pl.ds(zq * rows, rows), :] = jnp.concatenate(parts, axis=1)


def flash_backward(q, kv_blocks, bias, grad, exact, lse, seqs, rows, g, groups):
    shards = len(kv_blocks)
    q_cols = q.shape[1]
    stack = groups * rows
    kv_spec = pl.BlockSpec(kv_blocks[0].shape, lambda i: (0, 0))
    whole = pl.BlockSpec((seqs * rows, q_cols), lambda i: (0, 0))
    grad_q_shape = (seqs * rows, groups * HD)
    out_spec = pl.BlockSpec((shards // 2, rows, 2 * HD), lambda i: (0, i, 0))
    out = jax.ShapeDtypeStruct((shards // 2, seqs * rows, 2 * HD), BF)
    return pl.pallas_call(
        functools.partial(backward_kernel, shards, seqs, rows, g, groups),
        grid=(seqs,),
        in_specs=[kv_spec] * shards
        + [whole, pl.BlockSpec(bias.shape, lambda i: (0, 0, 0)), whole, whole, whole],
        out_specs=[pl.BlockSpec(grad_q_shape, lambda i: (0, 0)), out_spec, out_spec],
        out_shape=[jax.ShapeDtypeStruct(grad_q_shape, F32), out, out],
        scratch_shapes=[
            pltpu.VMEM((seqs, 2 * stack, 2 * HD), BF),
            pltpu.VMEM((seqs, 2 * HD, 2 * stack), BF),
            pltpu.VMEM((seqs, stack, 2 * HD), F32),
            pltpu.VMEM((seqs, stack, 2 * HD), F32),
            pltpu.VMEM((seqs, stack, 2 * HD), F32),
            pltpu.VMEM((2 * HD, shards * rows), F32),
        ],
        compiler_params=pltpu.CompilerParams(vmem_limit_bytes=60 * 1024 * 1024),
        cost_estimate=pl.CostEstimate(
            flops=40 * seqs * seqs * shards * rows * rows * groups * HD,
            bytes_accessed=8 * 1024 * 1024,
            transcendentals=seqs * seqs * shards * rows * rows * groups // 2,
        ),
    )(*kv_blocks, q, bias, grad, exact, lse)


def shift(block, count, step):
    return lax.ppermute(block, "seq", [(i, (i + step) % count) for i in range(count)])


def send_out(blocks, count):
    return [blocks[0]] + [shift(blocks[s], count, s) for s in range(1, count)]


def send_back(blocks, count):
    return [blocks[0]] + [shift(blocks[s], count, count - s) for s in range(1, count)]


def relay_step(blocks, count):
    up, down = blocks
    return (
        lax.ppermute(up, "seq", [(i, i + 1) for i in range(count - 1)]),
        lax.ppermute(down, "seq", [(i + 1, i) for i in range(count - 1)]),
    )


def relay_blocks(steps, place):
    count = len(steps)
    return [steps[0][0]] + [
        jnp.where(place >= s, steps[s][0], steps[count - s][1]) for s in range(1, count)
    ]


def from_relative(blocks, place):
    count = len(blocks)
    rising = jnp.stack([blocks[-s % count] for s in range(count)])
    return lax.dynamic_slice_in_dim(jnp.concatenate([rising, rising]), count - place, count, 0)


def hop(block, count, mask):
    return lax.ppermute(block, "fsdp", [(i, i ^ mask) for i in range(count)])


def gather_shards(block, count):
    near = [block] + [hop(block, count, 2 * m) for m in range(1, count // 2)]
    return near + [hop(each, count, 1) for each in near]


def send_chips(parts, count):
    return list(parts[0]) + [hop(parts[m], count, 2 * m) for m in range(1, count // 2)]


def total_of(blocks):
    total = blocks[0].astype(F32)
    for each in blocks[1:]:
        total = total + each.astype(F32)
    return total


def take(array, index, axis):
    return lax.dynamic_index_in_dim(array, index, axis, keepdims=False)


def pair_halves(product, shard, count):
    width, cols = product.shape
    cut = product.reshape(count // 2, 2, width // count, cols)
    there = hop(take(cut, 1 - shard % 2, 1), count, 1)
    return product.reshape(count, width // count, cols), there


def pair_sums(halves, shard):
    here, there = halves
    sums = [(take(here, shard, 0), take(there, shard // 2, 0))]
    for m in range(1, there.shape[0]):
        each = take(here, shard ^ (2 * m), 0).astype(F32)
        sums.append((each + take(there, (shard // 2) ^ m, 0).astype(F32)).astype(BF))
    return sums


def sum_rows(product, shard, count):
    return total_of(send_chips(pair_sums(pair_halves(product, shard, count), shard), count))


def two_parts(value):
    high = value.astype(BF)
    return high, (value - high.astype(F32)).astype(BF)


def after(values, *others):
    return lax.optimization_barrier((values, others))[0]


def root(values):
    return lax.rsqrt(jnp.mean(values * values, axis=-1, keepdims=True) + EPSILON)


def root_back(values, factor, grad_scaled):
    inner = jnp.mean(grad_scaled * values, axis=-1, keepdims=True)
    return factor * grad_scaled - values * (factor * factor * factor * inner)


def place_gate_up(blocks, weight, gain, place, *wait):
    experts, part, both = weight.shape
    count = len(blocks)
    split = count // experts
    if split > 1:
        base = (
            from_relative(blocks, place)
            .reshape(experts, split, part, 2, both // (2 * split))
            .transpose(0, 2, 3, 1, 4)
            .reshape(experts, part, both)
            .astype(F32)
        )
        return base * gain, jnp.sum(weight.astype(F32) * base, axis=(0, 2))
    result = jnp.zeros((experts, part, both), F32)
    blocks = [after(blocks[0], *wait)] + blocks[1:]
    sums = jnp.zeros((part,), F32)
    for s in range(count):
        expert = (place - s) % count
        base = blocks[s].astype(F32)
        result = lax.dynamic_update_index_in_dim(result, base * gain, expert, 0)
        sums = sums + jnp.sum(take(weight, expert, 0).astype(F32) * base, axis=1)
    return result, sums


def place_columns(blocks, place, finish):
    count = len(blocks)
    rows, cols = blocks[0].shape
    result = jnp.zeros((rows, count * cols), F32)
    for s in range(count):
        column = (place - s) % count * cols
        result = lax.dynamic_update_slice(
            result, finish(blocks[s].astype(F32), column), (0, column)
        )
    return result


def columns_of(array, column, cols):
    return lax.dynamic_slice_in_dim(array, column, cols, 1).astype(F32)


def local(
    tokens,
    teacher,
    valid,
    routes,
    slots,
    gain_attn,
    w_query,
    w_keyval,
    w_out,
    gain_ffn,
    w_router,
    w_gate_up,
    w_down,
):
    seqs = lax.axis_size("seq")
    shards = lax.axis_size("fsdp")
    z = lax.axis_index("seq")
    shard = lax.axis_index("fsdp")
    rows, width = tokens.shape
    groups = HEADS // KVH
    local_kv = KVH // seqs
    q_cols = local_kv * groups * HD
    kv_cols = local_kv * 2 * HD
    local_rows = rows * seqs
    seq_len = local_rows * shards
    experts, part, both = w_gate_up.shape
    units = both // 2
    split = seqs // experts
    piece = units // split
    expert = z // split
    fraction = z % split
    scale = HD ** (-0.5)

    gain_one = gain_attn.astype(F32)[:, None]
    gain_two = gain_ffn.astype(F32)[:, None]
    heads_shard = jnp.concatenate(
        [
            lax.dynamic_slice_in_dim(w_query, z * q_cols, q_cols, 1),
            lax.dynamic_slice_in_dim(w_keyval, z * kv_cols, kv_cols, 1),
        ],
        axis=1,
    )
    heads_shard = (heads_shard.astype(F32) * gain_one).astype(BF)
    heads_full = lax.all_gather(heads_shard, "fsdp", axis=0, tiled=True)
    valid_row = jnp.pad(valid.astype(BF).reshape(1, rows), ((0, 7), (0, width - rows)))
    steps = [(jnp.concatenate([tokens, valid_row], axis=0),) * 2]
    for unused in range(seqs - 1):
        steps.append(relay_step(steps[-1], seqs))
    midway = steps[seqs // 2]
    token_blocks = relay_blocks(steps, z)

    valid_local = from_relative([each[rows : rows + 1, :rows] for each in token_blocks], z)
    token_blocks = [each[:rows] for each in token_blocks]
    projected = []
    for block in token_blocks:
        projected.append(dot(block, heads_full) * root(block.astype(F32)))
    projected = from_relative([each.astype(BF) for each in projected], z)
    projected = projected.reshape(local_rows, q_cols + kv_cols)
    head_queries = projected[:, :q_cols] * jnp.asarray(scale, BF)

    valid_rows_kv = local_rows // kv_cols
    payload = jnp.concatenate(
        [
            projected[:, q_cols:],
            valid_local.reshape(valid_rows_kv, kv_cols),
            jnp.zeros((16 - valid_rows_kv, kv_cols), BF),
        ],
        axis=0,
    )
    kv_blocks = gather_shards(payload, shards)
    late_query, late_keyval, late_out, late_router, late_gate_up, late_down = after(
        (w_query, w_keyval, w_out, w_router, w_gate_up, w_down), midway
    )
    out_full = lax.all_gather(w_out, "fsdp", axis=1, tiled=True)
    own_expert = take(late_gate_up, expert, 0)
    gate_shard = lax.dynamic_slice_in_dim(own_expert, fraction * piece, piece, 1)
    up_shard = lax.dynamic_slice_in_dim(own_expert, units + fraction * piece, piece, 1)
    down_shard = lax.dynamic_slice_in_dim(take(late_down, expert, 0), fraction * piece, piece, 0).T
    router_shard = jnp.pad((late_router.astype(F32) * gain_two).astype(BF), ((0, 0), (0, LANES - experts)))
    expert_shard = jnp.concatenate(
        [
            (gate_shard.astype(F32) * gain_two).astype(BF),
            (up_shard.astype(F32) * gain_two).astype(BF),
            down_shard,
            router_shard,
        ],
        axis=1,
    )
    expert_full = lax.all_gather(expert_shard, "fsdp", axis=0, tiled=True)
    gate_up_full = expert_full[:, : 2 * piece]
    down_full = expert_full[:, 2 * piece : 3 * piece]
    router_full = expert_full[:, 3 * piece :]
    attn_shard = jnp.concatenate([late_query, late_keyval], axis=1)
    attn_full = lax.all_gather(
        (attn_shard.astype(F32) * gain_one).astype(BF), "fsdp", axis=0, tiled=True
    )
    order = jnp.asarray(
        [2 * m for m in range(shards // 2)] + [2 * m + 1 for m in range(shards // 2)], jnp.int32
    )
    valid_all = jnp.stack(
        [
            each[local_rows : local_rows + valid_rows_kv].reshape(seqs, rows)
            for each in kv_blocks
        ],
        axis=1,
    ).astype(F32)
    valid_count = jnp.sum(valid_all)
    bias = jnp.where(valid_all > 0, 0.0, FLOOR_SCORE)
    earlier = ((order ^ shard) < shard) | (order == 0)
    bias_same = jnp.where(earlier[None, :, None], bias, FLOOR_SCORE)
    bias = jnp.concatenate([bias, bias_same]).reshape(2 * seqs, 1, shards * rows)
    attended_low, exact, lse = flash_forward(
        head_queries, kv_blocks, bias, seqs, rows, local_kv, groups
    )
    attended = lax.all_to_all(attended_low, "seq", split_axis=0, concat_axis=1, tiled=True)

    inputs = tokens.astype(F32)
    residual = inputs + dot(attended, out_full)
    factor_two = root(residual)
    normed_two = (residual * factor_two).astype(BF)
    logits = dot(normed_two, router_full)[:, :experts]
    expert_ids = jnp.arange(experts, dtype=jnp.int32)
    picked = (routes[:, :, None] == expert_ids).astype(F32)
    chosen = jnp.sum(picked * logits[:, None, :], axis=-1)
    gating = jax.nn.softmax(chosen, axis=-1)
    owners = ((jnp.arange(seqs, dtype=jnp.int32) + z) % seqs) // split
    to_owner = routes[:, :, None] == owners
    slot_hot = slots[:, :, None] == jnp.arange(CAP, dtype=jnp.int32)
    placed = (to_owner[:, :, :, None] & slot_hot[:, :, None, :]).astype(BF)
    placed = placed.reshape(rows, 2, seqs * CAP)
    dispatch = placed[:, 0] + placed[:, 1]
    placed_pairs = jnp.concatenate([placed[:, 0], placed[:, 1]], axis=0)
    sent_rows = dot_tn(dispatch, normed_two).astype(BF).reshape(seqs, CAP, width)
    expert_rows = jnp.concatenate(send_out([sent_rows[s] for s in range(seqs)], seqs))
    gate_up = dot(expert_rows, gate_up_full)
    gate_part = gate_up[:, :piece]
    up_part = gate_up[:, piece:]
    sigmoid_gate = jax.nn.sigmoid(gate_part)
    hidden = (gate_part * sigmoid_gate * up_part).astype(BF)
    expert_out = dot_nt(hidden, down_full).astype(BF).reshape(seqs, CAP, width)
    returned = jnp.concatenate(send_back([expert_out[s] for s in range(seqs)], seqs))
    selected = dot(placed_pairs, returned).reshape(2, rows, width)
    mixed_exact = residual + gating[:, :1] * selected[0] + gating[:, 1:] * selected[1]
    valid_rows = valid.astype(F32)
    errors = (mixed_exact - teacher.astype(F32)) * valid_rows[:, None]
    squares = jnp.sum(errors * errors)
    loss_scale = width * seq_len // 8
    grad_mixed = errors * (2.0 * loss_scale / (width * valid_count))

    grad_gating = jnp.stack(
        [jnp.sum(selected[0] * grad_mixed, axis=-1), jnp.sum(selected[1] * grad_mixed, axis=-1)],
        axis=1,
    )
    grad_chosen = gating * (grad_gating - jnp.sum(gating * grad_gating, axis=-1, keepdims=True))
    grad_logits = jnp.sum(grad_chosen[:, :, None] * picked, axis=1).astype(BF)
    grad_logits = jnp.pad(grad_logits, ((0, 0), (0, LANES - experts)))
    weighted = jnp.concatenate(
        [(gating[:, :1] * grad_mixed).astype(BF), (gating[:, 1:] * grad_mixed).astype(BF)], axis=0
    )
    sent_grads = dot_tn(placed_pairs, weighted).astype(BF).reshape(seqs, CAP, width)
    grad_expert_out = jnp.concatenate(send_out([sent_grads[s] for s in range(seqs)], seqs))
    grad_expert_out = after(grad_expert_out, attn_full)
    grad_hidden = dot(grad_expert_out, down_full)
    grad_gate = grad_hidden * up_part * sigmoid_gate * (1.0 + gate_part * (1.0 - sigmoid_gate))
    grad_up = grad_hidden * gate_part * sigmoid_gate
    grad_gate_up_rows = jnp.concatenate([grad_gate, grad_up], axis=-1).astype(BF)
    grad_rows = dot_nt(grad_gate_up_rows, gate_up_full).astype(BF).reshape(seqs, CAP, width)
    grad_returned = jnp.concatenate(send_back([grad_rows[s] for s in range(seqs)], seqs))
    held_out, held_hidden = after((grad_expert_out, hidden), grad_rows)
    grad_down_sums = pair_sums(
        pair_halves(dot_tn(held_out, held_hidden).astype(BF), shard, shards), shard
    )
    held_rows, held_gate_up = after((expert_rows, grad_gate_up_rows), grad_rows)
    grad_gate_up_halves = pair_halves(
        dot_tn(held_rows, held_gate_up).astype(BF), shard, shards
    )
    grad_gate_up_sums = pair_sums(grad_gate_up_halves, shard)
    grad_returned = after(grad_returned, grad_down_sums, grad_gate_up_sums)
    tokens_local = from_relative(after(token_blocks, grad_rows), z).reshape(local_rows, width)
    factor_local = root(tokens_local.astype(F32))

    grad_normed_two = dot(dispatch, grad_returned) + dot_nt(grad_logits, router_full)
    grad_residual = grad_mixed + root_back(residual, factor_two, grad_normed_two)
    grad_branch = grad_residual.astype(BF)
    grad_attended = dot_nt(grad_branch, out_full).astype(BF)
    head_grad = lax.all_to_all(grad_attended, "seq", split_axis=1, concat_axis=0, tiled=True)
    grad_down_blocks = after(send_chips(grad_down_sums, shards), grad_attended)
    grad_down_shard = total_of(grad_down_blocks).astype(BF)
    grad_down = lax.all_gather(grad_down_shard, "seq", axis=0, tiled=False)
    grad_gate_up_blocks = after(send_chips(grad_gate_up_sums, shards), grad_attended)
    grad_gate_up_steps = [(total_of(grad_gate_up_blocks).astype(BF),) * 2]
    grad_gate_up_steps.append(relay_step(grad_gate_up_steps[0], seqs))

    late_branch = after(grad_branch, grad_attended)
    grad_out_halves = pair_halves(dot_tn(late_branch, attended).astype(BF), shard, shards)
    grad_out_sums = pair_sums(grad_out_halves, shard)

    grad_q, near, far = [], [], []
    held = after(head_grad, grad_down_shard, grad_gate_up_steps[0], grad_out_sums)
    for g in range(local_kv):
        part_q, near_kv, far_kv = flash_backward(
            head_queries, kv_blocks, bias, held, exact, lse, seqs, rows, g, groups
        )
        grad_q.append(part_q * scale)
        near.append(near_kv)
        far.append(far_kv)
        held = after(head_grad, part_q)
    grad_gate_up_steps[-1] = after(grad_gate_up_steps[-1], part_q)
    grad_gate_up_steps.append(relay_step(grad_gate_up_steps[-1], seqs))
    grad_out_blocks = after(send_chips(grad_out_sums, shards), part_q)
    near = jnp.concatenate(near, axis=2)
    there = hop(jnp.concatenate(far, axis=2), shards, 1)
    pairs = [near[m].astype(F32) + there[m].astype(F32) for m in range(shards // 2)]
    pairs = [(near[0], there[0])] + [each.astype(BF) for each in pairs[1:]]
    grad_q = jnp.concatenate(grad_q, axis=1)
    token_grad_q = lax.all_to_all(
        grad_q.astype(BF), "seq", split_axis=0, concat_axis=1, tiled=True
    )
    query_rhs = (grad_q * factor_local).astype(BF)
    high, low = two_parts(squares)
    lane = jnp.arange(LANES, dtype=jnp.int32)[None, :]
    marks = jnp.where(lane == experts + 2 * (shard % 2), high, 0) + jnp.where(
        lane == experts + 1 + 2 * (shard % 2), low, 0
    )
    router_product = dot_tn(normed_two, grad_logits).astype(BF) + marks.astype(BF)
    query_product = jnp.concatenate(
        [dot_tn(tokens_local, query_rhs).astype(BF), router_product], axis=1
    )
    grad_query_sums = pair_sums(pair_halves(after(query_product, pairs), shard, shards), shard)
    grad_kv = total_of(after(send_chips(pairs, shards), grad_query_sums))
    while len(grad_gate_up_steps) < seqs:
        grad_gate_up_steps[-1] = after(grad_gate_up_steps[-1], grad_kv)
        grad_gate_up_steps.append(relay_step(grad_gate_up_steps[-1], seqs))
    token_grad_kv = lax.all_to_all(
        grad_kv.astype(BF), "seq", split_axis=0, concat_axis=1, tiled=True
    )
    keyval_rhs = (grad_kv * factor_local).astype(BF)
    grad_keyval_sums = pair_sums(
        pair_halves(dot_tn(tokens_local, keyval_rhs).astype(BF), shard, shards), shard
    )
    grad_query_part = total_of(after(send_chips(grad_query_sums, shards), grad_keyval_sums))
    base_cols = q_cols + experts
    plane_high, plane_low = two_parts(
        jnp.sum(grad_query_part[:1, base_cols : base_cols + 4], axis=1, keepdims=True)
    )
    lanes = lax.broadcasted_iota(jnp.int32, grad_query_part.shape, 1)
    grad_query_part = jnp.where(
        lanes == base_cols,
        plane_high.astype(F32),
        jnp.where(lanes == base_cols + 1, plane_low.astype(F32), grad_query_part),
    )
    grad_query_blocks = send_out([grad_query_part.astype(BF)] * seqs, seqs)
    grad_out_part = total_of(after(grad_out_blocks, pairs))
    cut = grad_out_part.astype(BF)
    grad_out_own = jnp.zeros((part, q_cols), F32)
    out_parts = send_out(
        [
            lax.dynamic_slice_in_dim(cut, (z + s) % seqs * q_cols, q_cols, 1)
            for s in range(seqs)
        ],
        seqs,
    )
    for each in after(out_parts, grad_kv):
        grad_out_own = grad_out_own + each.astype(F32)
    grad_out = place_columns(
        send_out([grad_out_own.astype(BF)] * seqs, seqs), z, lambda block, column: block
    ).T
    grad_normed = dot_nt(after(token_grad_q, grad_kv), attn_full[:, : HEADS * HD]) + dot_nt(
        token_grad_kv, attn_full[:, HEADS * HD :]
    )
    grad_tokens = grad_residual + root_back(inputs, root(inputs), grad_normed)

    grad_keyval_part = total_of(after(send_chips(grad_keyval_sums, shards), grad_query_part))
    grad_keyval_blocks = send_out([grad_keyval_part.astype(BF)] * seqs, seqs)
    grad_gate_up, grad_gain_ffn = place_gate_up(
        relay_blocks(grad_gate_up_steps, z), w_gate_up, gain_two, z, grad_kv
    )
    grad_keyval_blocks = after(grad_keyval_blocks, grad_gate_up)
    sums = sum(
        jnp.sum(each[:, q_cols : q_cols + LANES].astype(F32).reshape(part, 1, LANES), axis=1)
        for each in grad_query_blocks
    )
    loss_value = jnp.sum(sums[0, experts : experts + 2]) / (width * valid_count)
    grad_router_base = sums[:, :experts]

    gain_parts = []

    def end_query(block, column):
        gain_parts.append(jnp.sum(columns_of(w_query, column, q_cols) * block, axis=1))
        return block * gain_one

    def end_keyval(block, column):
        gain_parts.append(jnp.sum(columns_of(w_keyval, column, kv_cols) * block, axis=1))
        return block * gain_one

    grad_query = place_columns([each[:, :q_cols] for each in grad_query_blocks], z, end_query)
    grad_keyval = place_columns(grad_keyval_blocks, z, end_keyval)
    grad_gain_attn = sum(gain_parts)
    grad_down = (
        after(grad_down, grad_kv).reshape(experts, split, part, piece)
        .transpose(0, 1, 3, 2)
        .reshape(experts, units, part)
        .astype(F32)
    )
    grad_gain_ffn = grad_gain_ffn + jnp.sum(w_router.astype(F32) * grad_router_base, axis=1)
    return (
        mixed_exact.astype(BF),
        loss_value,
        grad_tokens,
        grad_gain_attn,
        grad_query,
        grad_keyval,
        grad_out,
        grad_gain_ffn,
        grad_router_base * gain_two,
        grad_gate_up,
        grad_down,
    )


def solution(mesh):
    return jax.shard_map(
        local,
        mesh=mesh,
        in_specs=(
            P(("seq", "fsdp"), None),
            P(("seq", "fsdp"), None),
            P(("seq", "fsdp")),
            P(("seq", "fsdp"), None),
            P(("seq", "fsdp"), None),
            P("fsdp"),
            P("fsdp", None),
            P("fsdp", None),
            P(None, "fsdp"),
            P("fsdp"),
            P("fsdp", None),
            P(None, "fsdp", None),
            P(None, None, "fsdp"),
        ),
        out_specs=(
            P(("seq", "fsdp"), None),
            P(),
            P(("seq", "fsdp"), None),
            P("fsdp"),
            P("fsdp", None),
            P("fsdp", None),
            P(None, "fsdp"),
            P("fsdp"),
            P("fsdp", None),
            P(None, "fsdp", None),
            P(None, None, "fsdp"),
        ),
        check_vma=False,
    )
```

```python
import functools

import jax
import jax.numpy as jnp
from jax import lax
from jax.experimental import pallas as pl
from jax.experimental.layout import Layout, with_layout_constraint
from jax.experimental.pallas import tpu as pltpu
from jax.sharding import PartitionSpec as P

HEADS = 24
KVH = 8
HD = 64
CAP = 96
LANES = 128
EPSILON = 1e-06
FLOOR_SCORE = -1e30
BF = jnp.bfloat16
F32 = jnp.float32


def dot(a, b):
    return jnp.dot(a, b, preferred_element_type=F32)


def dot_nt(a, b):
    return lax.dot_general(a, b, (((1,), (1,)), ((), ())), preferred_element_type=F32)


def dot_tn(a, b):
    return lax.dot_general(a, b, (((0,), (0,)), ((), ())), preferred_element_type=F32)


def own_mask(valid_row, rows):
    i = lax.broadcasted_iota(jnp.int32, (rows, rows), 0)
    j = lax.broadcasted_iota(jnp.int32, (rows, rows), 1)
    return jnp.where(j == i, 0.0, jnp.where(j < i, valid_row, FLOOR_SCORE))


def key_chunk(kv_refs, zk, rows, g):
    return jnp.concatenate(
        [ref[pl.ds(zk * rows, rows), pl.ds(g * 2 * HD, 2 * HD)] for ref in kv_refs], axis=0
    )


def forward_kernel(shards, seqs, rows, local_kv, groups, *refs):
    kv_refs = refs[:shards]
    q_ref, bias_ref, low_ref, exact_ref, lse_ref, acc_ref, max_ref = refs[shards:]
    zq = pl.program_id(0)
    stack = groups * rows
    zeros = jnp.zeros((rows, HD), BF)
    half = lax.broadcasted_iota(jnp.int32, (1, 2 * HD), 1) < HD

    def queries(g):
        parts = []
        for h in range(groups):
            start = (g * groups + h) * HD
            parts.append(jnp.concatenate([q_ref[:, start : start + HD], zeros], axis=1))
        return jnp.concatenate(parts, axis=0)

    def chunk(g, zk, scores):
        first = scores is None
        keys = key_chunk(kv_refs, zk, rows, g)
        raw = dot_nt(queries(g), keys)
        if first:
            row = bias_ref[seqs + zk]
            mask = own_mask(row[:, :rows], rows)
            mask = jnp.concatenate([mask] * groups, axis=0)
            masked = jnp.concatenate([raw[:, :rows] + mask, raw[:, rows:] + row[:, rows:]], axis=1)
            new_max = jnp.max(masked, axis=1, keepdims=True)
        else:
            masked = raw + bias_ref[zk]
            new_max = jnp.maximum(max_ref[g][:, :1], jnp.max(masked, axis=1, keepdims=True))
        terms = jnp.exp(masked - new_max).astype(BF)
        ones_values = jnp.where(half, jnp.ones_like(keys), keys)
        part = dot(terms, ones_values)
        if first:
            acc_ref[g] = part
        else:
            acc_ref[g] = acc_ref[g] * jnp.exp(max_ref[g][:, :1] - new_max) + part
        max_ref[g] = jnp.broadcast_to(new_max, (stack, 2 * HD))

    for g in range(local_kv):
        chunk(g, zq, None)

    @pl.loop(0, zq)
    def _(zk):
        for g in range(local_kv):
            chunk(g, zk, True)

    exact_parts, lse_parts = [], []
    for g in range(local_kv):
        acc = acc_ref[g]
        total = acc[:, :HD]
        exact = acc[:, HD:] / total
        lse = max_ref[g][:, :HD] + jnp.log(total)
        for h in range(groups):
            exact_parts.append(exact[h * rows : (h + 1) * rows])
            lse_parts.append(lse[h * rows : (h + 1) * rows])
    exact = jnp.concatenate(exact_parts, axis=1)
    exact_ref[...] = exact
    low_ref[...] = exact.astype(BF)
    lse_ref[...] = jnp.concatenate(lse_parts, axis=1)


def flash_forward(q, kv_blocks, bias, seqs, rows, local_kv, groups):
    shards = len(kv_blocks)
    q_cols = q.shape[1]
    kv_spec = pl.BlockSpec(kv_blocks[0].shape, lambda i: (0, 0))
    q_spec = pl.BlockSpec((rows, q_cols), lambda i: (i, 0))
    stack = groups * rows
    out = jax.ShapeDtypeStruct((seqs * rows, q_cols), F32)
    return pl.pallas_call(
        functools.partial(forward_kernel, shards, seqs, rows, local_kv, groups),
        grid=(seqs,),
        in_specs=[kv_spec] * shards + [q_spec, pl.BlockSpec(bias.shape, lambda i: (0, 0, 0))],
        out_specs=[q_spec] * 3,
        out_shape=[jax.ShapeDtypeStruct((seqs * rows, q_cols), BF), out, out],
        scratch_shapes=[
            pltpu.VMEM((local_kv, stack, 2 * HD), F32),
            pltpu.VMEM((local_kv, stack, 2 * HD), F32),
        ],
        compiler_params=pltpu.CompilerParams(vmem_limit_bytes=24 * 1024 * 1024),
        cost_estimate=pl.CostEstimate(
            flops=8 * seqs * seqs * shards * rows * rows * local_kv * groups * HD,
            bytes_accessed=8 * 1024 * 1024,
            transcendentals=seqs * seqs * shards * rows * rows * local_kv * groups // 2,
        ),
    )(*kv_blocks, q, bias)


def backward_kernel(shards, seqs, rows, g, groups, *refs):
    kv_refs = [refs[0].at[p] for p in range(shards)]
    (
        q_ref, bias_ref, grad_ref, exact_ref, lse_ref, grad_q_ref, near_ref, far_ref,
        pair_ref, pair_t_ref, lse_wide, delta_wide, acc_q, acc_kv,
    ) = refs[1:]
    zk = pl.program_id(0)
    stack = groups * rows
    zeros = jnp.zeros((rows, HD), BF)

    @pl.when(zk == 0)
    def _():
        acc_q[...] = jnp.zeros_like(acc_q)

        @pl.loop(0, seqs)
        def _(zq):
            here = pl.ds(zq * rows, rows)
            tops, bottoms = [], []
            for h in range(groups):
                cols = slice((g * groups + h) * HD, (g * groups + h + 1) * HD)
                grad = grad_ref[here, cols]
                tops.append(jnp.concatenate([q_ref[here, cols], zeros], axis=1))
                bottoms.append(jnp.concatenate([zeros, grad], axis=1))
                delta = jnp.sum(grad.astype(F32) * exact_ref[here, cols], axis=1, keepdims=True)
                part = slice(h * rows, (h + 1) * rows)
                delta_wide[zq, part] = jnp.broadcast_to(delta, (rows, 2 * HD))
                lse_wide[zq, part] = jnp.broadcast_to(lse_ref[here, cols][:, :1], (rows, 2 * HD))
            pair = jnp.concatenate(tops + bottoms, axis=0)
            pair_ref[zq] = pair
            pair_t_ref[zq] = pair.astype(F32).T.astype(BF)

    def chunk(zq, first):
        keys = key_chunk(kv_refs, zk, rows, g)
        both = dot_nt(pair_ref[zq], keys)
        raw, products = both[:stack], both[stack:]
        if first:
            row = bias_ref[seqs + zk]
            mask = own_mask(row[:, :rows], rows)
            mask = jnp.concatenate([mask] * groups, axis=0)
            masked = jnp.concatenate([raw[:, :rows] + mask, raw[:, rows:] + row[:, rows:]], axis=1)
        else:
            masked = raw + bias_ref[zk]
        weights = jnp.exp(masked - lse_wide[zq][:, :1])
        grads = (weights * (products - delta_wide[zq][:, :1])).astype(BF)
        acc_q[zq] += dot(grads, keys)
        part = dot(pair_t_ref[zq], jnp.concatenate([grads, weights.astype(BF)], axis=0))
        if first:
            acc_kv[...] = part
        else:
            acc_kv[...] += part

    chunk(zk, True)

    @pl.loop(zk + 1, seqs)
    def _(zq):
        chunk(zq, False)

    for p in range(shards):
        target = near_ref if p < shards // 2 else far_ref
        target[p % (shards // 2)] = acc_kv[:, p * rows : (p + 1) * rows].T.astype(BF)

    @pl.when(zk == seqs - 1)
    def _():
        @pl.loop(0, seqs)
        def _(zq):
            total = acc_q[zq]
            parts = [total[h * rows : (h + 1) * rows, :HD] for h in range(groups)]
            grad_q_ref[pl.ds(zq * rows, rows), :] = jnp.concatenate(parts, axis=1)


def flash_backward(q, kv_all, bias, grad, exact, lse, seqs, rows, g, groups):
    shards = kv_all.shape[0]
    q_cols = q.shape[1]
    stack = groups * rows
    kv_spec = pl.BlockSpec(kv_all.shape, lambda i: (0, 0, 0))
    whole = pl.BlockSpec((seqs * rows, q_cols), lambda i: (0, 0))
    grad_q_shape = (seqs * rows, groups * HD)
    out_spec = pl.BlockSpec((shards // 2, rows, 2 * HD), lambda i: (0, i, 0))
    out = jax.ShapeDtypeStruct((shards // 2, seqs * rows, 2 * HD), BF)
    return pl.pallas_call(
        functools.partial(backward_kernel, shards, seqs, rows, g, groups),
        grid=(seqs,),
        in_specs=[kv_spec]
        + [whole, pl.BlockSpec(bias.shape, lambda i: (0, 0, 0)), whole, whole, whole],
        out_specs=[pl.BlockSpec(grad_q_shape, lambda i: (0, 0)), out_spec, out_spec],
        out_shape=[jax.ShapeDtypeStruct(grad_q_shape, F32), out, out],
        scratch_shapes=[
            pltpu.VMEM((seqs, 2 * stack, 2 * HD), BF),
            pltpu.VMEM((seqs, 2 * HD, 2 * stack), BF),
            pltpu.VMEM((seqs, stack, 2 * HD), F32),
            pltpu.VMEM((seqs, stack, 2 * HD), F32),
            pltpu.VMEM((seqs, stack, 2 * HD), F32),
            pltpu.VMEM((2 * HD, shards * rows), F32),
        ],
        compiler_params=pltpu.CompilerParams(vmem_limit_bytes=28 * 1024 * 1024),
        cost_estimate=pl.CostEstimate(
            flops=40 * seqs * seqs * shards * rows * rows * groups * HD,
            bytes_accessed=8 * 1024 * 1024,
            transcendentals=seqs * seqs * shards * rows * rows * groups // 2,
        ),
    )(kv_all, q, bias, grad, exact, lse)


def shift(block, count, step):
    return lax.ppermute(block, "seq", [(i, (i + step) % count) for i in range(count)])


def send_out(blocks, count):
    return [blocks[0]] + [shift(blocks[s], count, s) for s in range(1, count)]


def send_back(blocks, count):
    return [blocks[0]] + [shift(blocks[s], count, count - s) for s in range(1, count)]


def from_relative(blocks, place):
    count = len(blocks)
    rising = jnp.stack([blocks[-s % count] for s in range(count)])
    return lax.dynamic_slice_in_dim(jnp.concatenate([rising, rising]), count - place, count, 0)


def hop(block, count, mask):
    return lax.ppermute(block, "fsdp", [(i, i ^ mask) for i in range(count)])


def gather_shards(block, count):
    near = [block] + [hop(block, count, 2 * m) for m in range(1, count // 2)]
    return near + [hop(each, count, 1) for each in near]


def send_chips(parts, count):
    return list(parts[0]) + [hop(parts[m], count, 2 * m) for m in range(1, count // 2)]


def total_of(blocks):
    total = blocks[0].astype(F32)
    for each in blocks[1:]:
        total = total + each.astype(F32)
    return total


def take(array, index, axis):
    return lax.dynamic_index_in_dim(array, index, axis, keepdims=False)


def pair_halves(product, shard, count):
    width, cols = product.shape
    cut = product.reshape(count // 2, 2, width // count, cols)
    there = hop(take(cut, 1 - shard % 2, 1), count, 1)
    return product.reshape(count, width // count, cols), there


def pair_sums(halves, shard):
    here, there = halves
    sums = [(take(here, shard, 0), take(there, shard // 2, 0))]
    for m in range(1, there.shape[0]):
        each = take(here, shard ^ (2 * m), 0).astype(F32)
        sums.append((each + take(there, (shard // 2) ^ m, 0).astype(F32)).astype(BF))
    return sums


def sum_rows(product, shard, count):
    return total_of(send_chips(pair_sums(pair_halves(product, shard, count), shard), count))


def two_parts(value):
    high = value.astype(BF)
    return high, (value - high.astype(F32)).astype(BF)


def by_rows(array):
    return with_layout_constraint(array, Layout(major_to_minor=tuple(range(array.ndim))))


def after(values, *others):
    return lax.optimization_barrier((values, others))[0]


def root(values):
    return lax.rsqrt(jnp.mean(values * values, axis=-1, keepdims=True) + EPSILON)


def root_back(values, factor, grad_scaled):
    inner = jnp.mean(grad_scaled * values, axis=-1, keepdims=True)
    return factor * grad_scaled - values * (factor * factor * factor * inner)


def place_gate_up(base, weight, gain):
    experts, part, both = weight.shape
    split = base.shape[0] // experts
    base = base.astype(F32)
    if split > 1:
        base = (
            base.reshape(experts, split, part, 2, both // (2 * split))
            .transpose(0, 2, 3, 1, 4)
            .reshape(experts, part, both)
        )
    return base * gain, jnp.sum(weight.astype(F32) * base, axis=(0, 2))


def place_columns(blocks, place, finish):
    count = len(blocks)
    rows, cols = blocks[0].shape
    result = jnp.zeros((rows, count * cols), F32)
    for s in range(count):
        column = (place - s) % count * cols
        result = lax.dynamic_update_slice(
            result, finish(blocks[s].astype(F32), column), (0, column)
        )
    return result


def columns_of(array, column, cols):
    return lax.dynamic_slice_in_dim(array, column, cols, 1).astype(F32)


def local(
    tokens,
    teacher,
    valid,
    routes,
    slots,
    gain_attn,
    w_query,
    w_keyval,
    w_out,
    gain_ffn,
    w_router,
    w_gate_up,
    w_down,
):
    seqs = lax.axis_size("seq")
    shards = lax.axis_size("fsdp")
    z = lax.axis_index("seq")
    shard = lax.axis_index("fsdp")
    rows, width = tokens.shape
    groups = HEADS // KVH
    local_kv = KVH // seqs
    q_cols = local_kv * groups * HD
    kv_cols = local_kv * 2 * HD
    local_rows = rows * seqs
    seq_len = local_rows * shards
    experts, part, both = w_gate_up.shape
    units = both // 2
    split = seqs // experts
    piece = units // split
    expert = z // split
    fraction = z % split
    scale = HD ** (-0.5)

    gain_one = gain_attn.astype(F32)[:, None]
    gain_two = gain_ffn.astype(F32)[:, None]
    heads_shard = jnp.concatenate(
        [
            lax.dynamic_slice_in_dim(w_query, z * q_cols, q_cols, 1),
            lax.dynamic_slice_in_dim(w_keyval, z * kv_cols, kv_cols, 1),
        ],
        axis=1,
    )
    heads_shard = (heads_shard.astype(F32) * gain_one).astype(BF)
    heads_full = lax.all_gather(heads_shard, "fsdp", axis=0, tiled=True)
    valid_row = jnp.pad(valid.astype(BF).reshape(1, rows), ((0, 7), (0, width - rows)))
    token_blocks = send_out([jnp.concatenate([tokens, valid_row], axis=0)] * seqs, seqs)

    valid_local = from_relative([each[rows : rows + 1, :rows] for each in token_blocks], z)
    token_blocks = [each[:rows] for each in token_blocks]
    projected = []
    for block in token_blocks:
        projected.append(dot(block, heads_full) * root(block.astype(F32)))
    projected = from_relative([each.astype(BF) for each in projected], z)
    projected = projected.reshape(local_rows, q_cols + kv_cols)
    head_queries = projected[:, :q_cols] * jnp.asarray(scale, BF)

    valid_rows_kv = local_rows // kv_cols
    payload = jnp.concatenate(
        [
            projected[:, q_cols:],
            valid_local.reshape(valid_rows_kv, kv_cols),
            jnp.zeros((16 - valid_rows_kv, kv_cols), BF),
        ],
        axis=0,
    )
    kv_blocks = gather_shards(payload, shards)
    late_router, late_gate_up, late_down = after(
        (w_router, w_gate_up, w_down), kv_blocks[: shards // 2]
    )
    out_full = lax.all_gather(w_out, "fsdp", axis=1, tiled=True)
    own_expert = take(late_gate_up, expert, 0)
    gate_shard = lax.dynamic_slice_in_dim(own_expert, fraction * piece, piece, 1)
    up_shard = lax.dynamic_slice_in_dim(own_expert, units + fraction * piece, piece, 1)
    down_shard = lax.dynamic_slice_in_dim(take(late_down, expert, 0), fraction * piece, piece, 0).T
    router_shard = jnp.pad((late_router.astype(F32) * gain_two).astype(BF), ((0, 0), (0, LANES - experts)))
    expert_shard = jnp.concatenate(
        [
            (gate_shard.astype(F32) * gain_two).astype(BF),
            (up_shard.astype(F32) * gain_two).astype(BF),
            down_shard,
            router_shard,
        ],
        axis=1,
    )
    expert_full = lax.all_gather(expert_shard, "fsdp", axis=0, tiled=True)
    gate_up_full = expert_full[:, : 2 * piece]
    down_full = expert_full[:, 2 * piece : 3 * piece]
    router_full = expert_full[:, 3 * piece :]
    order = jnp.asarray(
        [2 * m for m in range(shards // 2)] + [2 * m + 1 for m in range(shards // 2)], jnp.int32
    )
    valid_all = jnp.stack(
        [
            each[local_rows : local_rows + valid_rows_kv].reshape(seqs, rows)
            for each in kv_blocks
        ],
        axis=1,
    ).astype(F32)
    valid_count = jnp.sum(valid_all)
    bias = jnp.where(valid_all > 0, 0.0, FLOOR_SCORE)
    earlier = ((order ^ shard) < shard) | (order == 0)
    bias_same = jnp.where(earlier[None, :, None], bias, FLOOR_SCORE)
    bias = jnp.concatenate([bias, bias_same]).reshape(2 * seqs, 1, shards * rows)
    attended_low, exact, lse = flash_forward(
        head_queries, kv_blocks, bias, seqs, rows, local_kv, groups
    )
    attended = lax.all_to_all(attended_low, "seq", split_axis=0, concat_axis=1, tiled=True)

    inputs = tokens.astype(F32)
    residual = inputs + dot(attended, out_full)
    factor_two = root(residual)
    normed_two = (residual * factor_two).astype(BF)
    logits = dot(normed_two, router_full)[:, :experts]
    expert_ids = jnp.arange(experts, dtype=jnp.int32)
    picked = (routes[:, :, None] == expert_ids).astype(F32)
    chosen = jnp.sum(picked * logits[:, None, :], axis=-1)
    gating = jax.nn.softmax(chosen, axis=-1)
    owners = ((jnp.arange(seqs, dtype=jnp.int32) + z) % seqs) // split
    to_owner = routes[:, :, None] == owners
    slot_hot = slots[:, :, None] == jnp.arange(CAP, dtype=jnp.int32)
    placed = (to_owner[:, :, :, None] & slot_hot[:, :, None, :]).astype(BF)
    placed = placed.reshape(rows, 2, seqs * CAP)
    dispatch = placed[:, 0] + placed[:, 1]
    placed_pairs = jnp.concatenate([placed[:, 0], placed[:, 1]], axis=0)
    sent_rows = dot_tn(dispatch, normed_two).astype(BF).reshape(seqs, CAP, width)
    late_query, late_keyval = after((w_query, w_keyval), sent_rows)
    attn_shard = jnp.concatenate([late_query, late_keyval], axis=1)
    attn_full = lax.all_gather(
        (attn_shard.astype(F32) * gain_one).astype(BF), "fsdp", axis=0, tiled=True
    )
    expert_rows = jnp.concatenate(send_out([sent_rows[s] for s in range(seqs)], seqs))
    gate_up = dot(expert_rows, gate_up_full)
    gate_part = gate_up[:, :piece]
    up_part = gate_up[:, piece:]
    sigmoid_gate = jax.nn.sigmoid(gate_part)
    hidden = (gate_part * sigmoid_gate * up_part).astype(BF)
    expert_out = dot_nt(hidden, down_full).astype(BF).reshape(seqs, CAP, width)
    returned = jnp.concatenate(send_back([expert_out[s] for s in range(seqs)], seqs))
    selected = dot(placed_pairs, returned).reshape(2, rows, width)
    mixed_exact = residual + gating[:, :1] * selected[0] + gating[:, 1:] * selected[1]
    valid_rows = valid.astype(F32)
    errors = (mixed_exact - teacher.astype(F32)) * valid_rows[:, None]
    squares = jnp.sum(errors * errors)
    loss_scale = width * seq_len // 8
    grad_mixed = errors * (2.0 * loss_scale / (width * valid_count))

    grad_gating = jnp.stack(
        [jnp.sum(selected[0] * grad_mixed, axis=-1), jnp.sum(selected[1] * grad_mixed, axis=-1)],
        axis=1,
    )
    grad_chosen = gating * (grad_gating - jnp.sum(gating * grad_gating, axis=-1, keepdims=True))
    grad_logits = jnp.sum(grad_chosen[:, :, None] * picked, axis=1).astype(BF)
    grad_logits = jnp.pad(grad_logits, ((0, 0), (0, LANES - experts)))
    weighted = jnp.concatenate(
        [(gating[:, :1] * grad_mixed).astype(BF), (gating[:, 1:] * grad_mixed).astype(BF)], axis=0
    )
    sent_grads = dot_tn(placed_pairs, weighted).astype(BF).reshape(seqs, CAP, width)
    grad_expert_out = jnp.concatenate(send_out([sent_grads[s] for s in range(seqs)], seqs))
    grad_expert_out = after(grad_expert_out, attn_full)
    grad_hidden = dot(grad_expert_out, down_full)
    grad_gate = grad_hidden * up_part * sigmoid_gate * (1.0 + gate_part * (1.0 - sigmoid_gate))
    grad_up = grad_hidden * gate_part * sigmoid_gate
    grad_gate_up_rows = jnp.concatenate([grad_gate, grad_up], axis=-1).astype(BF)
    grad_rows = dot_nt(grad_gate_up_rows, gate_up_full).astype(BF).reshape(seqs, CAP, width)
    grad_returned = jnp.concatenate(send_back([grad_rows[s] for s in range(seqs)], seqs))
    held_out, held_hidden = after((grad_expert_out, hidden), grad_rows)
    grad_down_sums = pair_sums(
        pair_halves(dot_tn(held_out, held_hidden).astype(BF), shard, shards), shard
    )
    held_rows, held_gate_up = after((expert_rows, grad_gate_up_rows), grad_rows)
    grad_gate_up_halves = pair_halves(
        dot_tn(held_rows, held_gate_up).astype(BF), shard, shards
    )
    grad_returned = after(grad_returned, grad_down_sums)
    kv_all = jnp.stack(after(kv_blocks, grad_rows))
    tokens_local = from_relative(after(token_blocks, grad_rows), z).reshape(local_rows, width)
    factor_local = root(tokens_local.astype(F32))
    ride_rows = jnp.concatenate([normed_two, jnp.ones((16, width), BF)], axis=0)
    product_rows = jnp.concatenate([tokens_local, ride_rows], axis=0)

    grad_normed_two = dot(dispatch, grad_returned) + dot_nt(grad_logits, router_full)
    grad_residual = grad_mixed + root_back(residual, factor_two, grad_normed_two)
    grad_branch = grad_residual.astype(BF)
    grad_attended = dot_nt(grad_branch, out_full).astype(BF)
    head_grad = lax.all_to_all(grad_attended, "seq", split_axis=1, concat_axis=0, tiled=True)
    grad_gate_up_sums = pair_sums(after(grad_gate_up_halves, grad_attended), shard)
    grad_gate_up_blocks = send_chips(grad_gate_up_sums, shards)
    grad_down_blocks = after(send_chips(grad_down_sums, shards), head_grad)
    grad_down_shard = total_of(grad_down_blocks).astype(BF)
    grad_down = lax.all_gather(grad_down_shard, "seq", axis=0, tiled=False)

    late_branch = after(grad_branch, head_grad)
    grad_out_halves = pair_halves(dot_tn(late_branch, attended).astype(BF), shard, shards)

    grad_q, near, far = [], [], []
    held = after(head_grad, grad_down_shard, grad_gate_up_sums, grad_out_halves)
    for g in range(local_kv):
        part_q, near_kv, far_kv = flash_backward(
            head_queries, kv_all, bias, held, exact, lse, seqs, rows, g, groups
        )
        grad_q.append(part_q * scale)
        near.append(near_kv)
        far.append(far_kv)
        if g == 0:
            grad_gate_up_shard = total_of(after(grad_gate_up_blocks, part_q)).astype(BF)
            grad_out_sums = pair_sums(after(grad_out_halves, part_q), shard)
            held = after(head_grad, grad_gate_up_shard, grad_out_sums)
    grad_gate_up_all = lax.all_gather(grad_gate_up_shard, "seq", axis=0, tiled=False)
    grad_out_blocks = after(send_chips(grad_out_sums, shards), part_q)
    near = jnp.concatenate(near, axis=2)
    there = hop(jnp.concatenate(far, axis=2), shards, 1)
    pairs = [near[m].astype(F32) + there[m].astype(F32) for m in range(shards // 2)]
    pairs = [(near[0], there[0])] + [each.astype(BF) for each in pairs[1:]]
    grad_q = jnp.concatenate(grad_q, axis=1)
    token_grad_q = lax.all_to_all(
        grad_q.astype(BF), "seq", split_axis=0, concat_axis=1, tiled=True
    )
    query_rhs = (grad_q * factor_local).astype(BF)
    high, low = two_parts(squares)
    lane = jnp.arange(LANES, dtype=jnp.int32)[None, :]
    marks = jnp.where(lane == experts + 2 * (shard % 2), high, 0) + jnp.where(
        lane == experts + 1 + 2 * (shard % 2), low, 0
    )
    ride_columns = jnp.concatenate(
        [grad_logits, marks.astype(BF), jnp.zeros((15, LANES), BF)], axis=0
    )
    product_columns = jnp.concatenate(
        [
            jnp.pad(query_rhs, ((0, 0), (0, LANES))),
            jnp.pad(ride_columns, ((0, 0), (q_cols, 0))),
        ],
        axis=0,
    )
    query_product = dot_tn(product_rows, product_columns).astype(BF)
    grad_query_sums = pair_sums(pair_halves(after(query_product, pairs), shard, shards), shard)
    grad_query_sums = [
        tuple(by_rows(part) for part in each) if isinstance(each, tuple) else by_rows(each)
        for each in grad_query_sums
    ]
    grad_kv = total_of(after(send_chips(pairs, shards), grad_query_sums))
    token_grad_kv = lax.all_to_all(
        grad_kv.astype(BF), "seq", split_axis=0, concat_axis=1, tiled=True
    )
    keyval_rhs = (grad_kv * factor_local).astype(BF)
    grad_keyval_sums = pair_sums(
        pair_halves(dot_tn(tokens_local, keyval_rhs).astype(BF), shard, shards), shard
    )
    grad_query_part = total_of(after(send_chips(grad_query_sums, shards), grad_keyval_sums))
    base_cols = q_cols + experts
    plane_high, plane_low = two_parts(
        jnp.sum(grad_query_part[:1, base_cols : base_cols + 4], axis=1, keepdims=True)
    )
    lanes = lax.broadcasted_iota(jnp.int32, grad_query_part.shape, 1)
    grad_query_part = jnp.where(
        lanes == base_cols,
        plane_high.astype(F32),
        jnp.where(lanes == base_cols + 1, plane_low.astype(F32), grad_query_part),
    )
    grad_query_blocks = send_out([by_rows(grad_query_part.astype(BF))] * seqs, seqs)
    grad_query_blocks = [by_rows(each) for each in grad_query_blocks]
    grad_out_part = total_of(after(grad_out_blocks, pairs))
    cut = grad_out_part.astype(BF)
    grad_out_own = jnp.zeros((part, q_cols), F32)
    out_parts = send_out(
        [
            lax.dynamic_slice_in_dim(cut, (z + s) % seqs * q_cols, q_cols, 1)
            for s in range(seqs)
        ],
        seqs,
    )
    for each in after(out_parts, grad_kv):
        grad_out_own = grad_out_own + each.astype(F32)
    grad_out = place_columns(
        send_out([grad_out_own.astype(BF)] * seqs, seqs), z, lambda block, column: block
    ).T
    grad_normed = dot_nt(after(token_grad_q, grad_kv), attn_full[:, : HEADS * HD]) + dot_nt(
        token_grad_kv, attn_full[:, HEADS * HD :]
    )
    grad_tokens = grad_residual + root_back(inputs, root(inputs), grad_normed)

    grad_keyval_part = total_of(after(send_chips(grad_keyval_sums, shards), grad_query_part))
    grad_keyval_blocks = send_out([grad_keyval_part.astype(BF)] * seqs, seqs)
    grad_gate_up, grad_gain_ffn = place_gate_up(grad_gate_up_all, w_gate_up, gain_two)
    grad_keyval_blocks = after(grad_keyval_blocks, grad_gate_up)
    sums = sum(
        jnp.sum(each[:, q_cols : q_cols + LANES].astype(F32).reshape(part, 1, LANES), axis=1)
        for each in grad_query_blocks
    )
    loss_value = jnp.sum(sums[0, experts : experts + 2]) / (width * valid_count)
    grad_router_base = sums[:, :experts]

    gain_parts = []

    def end_query(block, column):
        gain_parts.append(jnp.sum(columns_of(w_query, column, q_cols) * block, axis=1))
        return block * gain_one

    def end_keyval(block, column):
        gain_parts.append(jnp.sum(columns_of(w_keyval, column, kv_cols) * block, axis=1))
        return block * gain_one

    grad_query = place_columns([each[:, :q_cols] for each in grad_query_blocks], z, end_query)
    grad_keyval = place_columns(grad_keyval_blocks, z, end_keyval)
    grad_gain_attn = sum(gain_parts)
    grad_down = (
        after(grad_down, grad_kv).reshape(experts, split, part, piece)
        .transpose(0, 1, 3, 2)
        .reshape(experts, units, part)
        .astype(F32)
    )
    grad_gain_ffn = grad_gain_ffn + jnp.sum(w_router.astype(F32) * grad_router_base, axis=1)
    return (
        mixed_exact.astype(BF),
        loss_value,
        grad_tokens,
        grad_gain_attn,
        grad_query,
        grad_keyval,
        grad_out,
        grad_gain_ffn,
        grad_router_base * gain_two,
        grad_gate_up,
        grad_down,
    )


def solution(mesh):
    return jax.shard_map(
        local,
        mesh=mesh,
        in_specs=(
            P(("seq", "fsdp"), None),
            P(("seq", "fsdp"), None),
            P(("seq", "fsdp")),
            P(("seq", "fsdp"), None),
            P(("seq", "fsdp"), None),
            P("fsdp"),
            P("fsdp", None),
            P("fsdp", None),
            P(None, "fsdp"),
            P("fsdp"),
            P("fsdp", None),
            P(None, "fsdp", None),
            P(None, None, "fsdp"),
        ),
        out_specs=(
            P(("seq", "fsdp"), None),
            P(),
            P(("seq", "fsdp"), None),
            P("fsdp"),
            P("fsdp", None),
            P("fsdp", None),
            P(None, "fsdp"),
            P("fsdp"),
            P("fsdp", None),
            P(None, "fsdp", None),
            P(None, None, "fsdp"),
        ),
        check_vma=False,
    )
```

```python
import functools

import jax
import jax.numpy as jnp
from jax import lax
from jax.experimental import pallas as pl
from jax.experimental.layout import Layout, with_layout_constraint
from jax.experimental.pallas import tpu as pltpu
from jax.sharding import PartitionSpec as P

HEADS = 24
KVH = 8
HD = 64
CAP = 96
LANES = 128
EPSILON = 1e-06
FLOOR_SCORE = -1e30
BF = jnp.bfloat16
F32 = jnp.float32


def dot(a, b):
    return jnp.dot(a, b, preferred_element_type=F32)


def dot_nt(a, b):
    return lax.dot_general(a, b, (((1,), (1,)), ((), ())), preferred_element_type=F32)


def dot_tn(a, b):
    return lax.dot_general(a, b, (((0,), (0,)), ((), ())), preferred_element_type=F32)


def own_mask(valid_row, rows):
    i = lax.broadcasted_iota(jnp.int32, (rows, rows), 0)
    j = lax.broadcasted_iota(jnp.int32, (rows, rows), 1)
    return jnp.where(j == i, 0.0, jnp.where(j < i, valid_row, FLOOR_SCORE))


def key_chunk(kv_refs, zk, rows, g):
    return jnp.concatenate(
        [ref[pl.ds(zk * rows, rows), pl.ds(g * 2 * HD, 2 * HD)] for ref in kv_refs], axis=0
    )


def forward_kernel(shards, seqs, rows, local_kv, groups, *refs):
    kv_refs = refs[:shards]
    q_ref, bias_ref, low_ref, exact_ref, lse_ref, acc_ref, max_ref = refs[shards:]
    zq = pl.program_id(0)
    stack = groups * rows
    zeros = jnp.zeros((rows, HD), BF)
    half = lax.broadcasted_iota(jnp.int32, (1, 2 * HD), 1) < HD

    def queries(g):
        parts = []
        for h in range(groups):
            start = (g * groups + h) * HD
            parts.append(jnp.concatenate([q_ref[:, start : start + HD], zeros], axis=1))
        return jnp.concatenate(parts, axis=0)

    def chunk(g, zk, scores):
        first = scores is None
        keys = key_chunk(kv_refs, zk, rows, g)
        raw = dot_nt(queries(g), keys)
        if first:
            row = bias_ref[seqs + zk]
            mask = own_mask(row[:, :rows], rows)
            mask = jnp.concatenate([mask] * groups, axis=0)
            masked = jnp.concatenate([raw[:, :rows] + mask, raw[:, rows:] + row[:, rows:]], axis=1)
            new_max = jnp.max(masked, axis=1, keepdims=True)
        else:
            masked = raw + bias_ref[zk]
            new_max = jnp.maximum(max_ref[g][:, :1], jnp.max(masked, axis=1, keepdims=True))
        terms = jnp.exp(masked - new_max).astype(BF)
        ones_values = jnp.where(half, jnp.ones_like(keys), keys)
        part = dot(terms, ones_values)
        if first:
            acc_ref[g] = part
        else:
            acc_ref[g] = acc_ref[g] * jnp.exp(max_ref[g][:, :1] - new_max) + part
        max_ref[g] = jnp.broadcast_to(new_max, (stack, 2 * HD))

    for g in range(local_kv):
        chunk(g, zq, None)

    @pl.loop(0, zq)
    def _(zk):
        for g in range(local_kv):
            chunk(g, zk, True)

    exact_parts, lse_parts = [], []
    for g in range(local_kv):
        acc = acc_ref[g]
        total = acc[:, :HD]
        exact = acc[:, HD:] / total
        lse = max_ref[g][:, :HD] + jnp.log(total)
        for h in range(groups):
            exact_parts.append(exact[h * rows : (h + 1) * rows])
            lse_parts.append(lse[h * rows : (h + 1) * rows])
    exact = jnp.concatenate(exact_parts, axis=1)
    exact_ref[...] = exact
    low_ref[...] = exact.astype(BF)
    lse_ref[...] = jnp.concatenate(lse_parts, axis=1)


def flash_forward(q, kv_blocks, bias, seqs, rows, local_kv, groups):
    shards = len(kv_blocks)
    q_cols = q.shape[1]
    kv_spec = pl.BlockSpec(kv_blocks[0].shape, lambda i: (0, 0))
    q_spec = pl.BlockSpec((rows, q_cols), lambda i: (i, 0))
    stack = groups * rows
    out = jax.ShapeDtypeStruct((seqs * rows, q_cols), F32)
    return pl.pallas_call(
        functools.partial(forward_kernel, shards, seqs, rows, local_kv, groups),
        grid=(seqs,),
        in_specs=[kv_spec] * shards + [q_spec, pl.BlockSpec(bias.shape, lambda i: (0, 0, 0))],
        out_specs=[q_spec] * 3,
        out_shape=[jax.ShapeDtypeStruct((seqs * rows, q_cols), BF), out, out],
        scratch_shapes=[
            pltpu.VMEM((local_kv, stack, 2 * HD), F32),
            pltpu.VMEM((local_kv, stack, 2 * HD), F32),
        ],
        compiler_params=pltpu.CompilerParams(vmem_limit_bytes=24 * 1024 * 1024),
        cost_estimate=pl.CostEstimate(
            flops=0,
            bytes_accessed=0,
            transcendentals=0,
        ),
    )(*kv_blocks, q, bias)


def backward_kernel(shards, seqs, rows, g, groups, *refs):
    kv_refs = [refs[0].at[p] for p in range(shards)]
    (
        q_ref, bias_ref, grad_ref, exact_ref, lse_ref, grad_q_ref, near_ref, far_ref,
        pair_ref, pair_t_ref, lse_wide, delta_wide, acc_q, acc_kv,
    ) = refs[1:]
    zk = pl.program_id(0)
    stack = groups * rows
    zeros = jnp.zeros((rows, HD), BF)

    @pl.when(zk == 0)
    def _():
        acc_q[...] = jnp.zeros_like(acc_q)

        @pl.loop(0, seqs)
        def _(zq):
            here = pl.ds(zq * rows, rows)
            tops, bottoms = [], []
            for h in range(groups):
                cols = slice((g * groups + h) * HD, (g * groups + h + 1) * HD)
                grad = grad_ref[here, cols]
                tops.append(jnp.concatenate([q_ref[here, cols], zeros], axis=1))
                bottoms.append(jnp.concatenate([zeros, grad], axis=1))
                delta = jnp.sum(grad.astype(F32) * exact_ref[here, cols], axis=1, keepdims=True)
                part = slice(h * rows, (h + 1) * rows)
                delta_wide[zq, part] = jnp.broadcast_to(delta, (rows, 2 * HD))
                lse_wide[zq, part] = jnp.broadcast_to(lse_ref[here, cols][:, :1], (rows, 2 * HD))
            pair = jnp.concatenate(tops + bottoms, axis=0)
            pair_ref[zq] = pair
            pair_t_ref[zq] = pair.astype(F32).T.astype(BF)

    def chunk(zq, first):
        keys = key_chunk(kv_refs, zk, rows, g)
        both = dot_nt(pair_ref[zq], keys)
        raw, products = both[:stack], both[stack:]
        if first:
            row = bias_ref[seqs + zk]
            mask = own_mask(row[:, :rows], rows)
            mask = jnp.concatenate([mask] * groups, axis=0)
            masked = jnp.concatenate([raw[:, :rows] + mask, raw[:, rows:] + row[:, rows:]], axis=1)
        else:
            masked = raw + bias_ref[zk]
        weights = jnp.exp(masked - lse_wide[zq][:, :1])
        grads = (weights * (products - delta_wide[zq][:, :1])).astype(BF)
        acc_q[zq] += dot(grads, keys)
        part = dot(pair_t_ref[zq], jnp.concatenate([grads, weights.astype(BF)], axis=0))
        if first:
            acc_kv[...] = part
        else:
            acc_kv[...] += part

    chunk(zk, True)

    @pl.loop(zk + 1, seqs)
    def _(zq):
        chunk(zq, False)

    for p in range(shards):
        target = near_ref if p < shards // 2 else far_ref
        target[p % (shards // 2)] = acc_kv[:, p * rows : (p + 1) * rows].T.astype(BF)

    @pl.when(zk == seqs - 1)
    def _():
        @pl.loop(0, seqs)
        def _(zq):
            total = acc_q[zq]
            parts = [total[h * rows : (h + 1) * rows, :HD] for h in range(groups)]
            grad_q_ref[pl.ds(zq * rows, rows), :] = jnp.concatenate(parts, axis=1) * HD ** (-0.5)


def flash_backward(q, kv_all, bias, grad, exact, lse, seqs, rows, g, groups):
    shards = kv_all.shape[0]
    q_cols = q.shape[1]
    stack = groups * rows
    kv_spec = pl.BlockSpec(kv_all.shape, lambda i: (0, 0, 0))
    whole = pl.BlockSpec((seqs * rows, q_cols), lambda i: (0, 0))
    grad_q_shape = (seqs * rows, groups * HD)
    out_spec = pl.BlockSpec((shards // 2, rows, 2 * HD), lambda i: (0, i, 0))
    out = jax.ShapeDtypeStruct((shards // 2, seqs * rows, 2 * HD), BF)
    return pl.pallas_call(
        functools.partial(backward_kernel, shards, seqs, rows, g, groups),
        grid=(seqs,),
        in_specs=[kv_spec]
        + [whole, pl.BlockSpec(bias.shape, lambda i: (0, 0, 0)), whole, whole, whole],
        out_specs=[pl.BlockSpec(grad_q_shape, lambda i: (0, 0)), out_spec, out_spec],
        out_shape=[jax.ShapeDtypeStruct(grad_q_shape, F32), out, out],
        scratch_shapes=[
            pltpu.VMEM((seqs, 2 * stack, 2 * HD), BF),
            pltpu.VMEM((seqs, 2 * HD, 2 * stack), BF),
            pltpu.VMEM((seqs, stack, 2 * HD), F32),
            pltpu.VMEM((seqs, stack, 2 * HD), F32),
            pltpu.VMEM((seqs, stack, 2 * HD), F32),
            pltpu.VMEM((2 * HD, shards * rows), F32),
        ],
        compiler_params=pltpu.CompilerParams(vmem_limit_bytes=28 * 1024 * 1024),
        cost_estimate=pl.CostEstimate(
            flops=0,
            bytes_accessed=0,
            transcendentals=0,
        ),
    )(kv_all, q, bias, grad, exact, lse)


def shift(block, count, step):
    return lax.ppermute(block, "seq", [(i, (i + step) % count) for i in range(count)])


def send_out(blocks, count):
    return [blocks[0]] + [shift(blocks[s], count, s) for s in range(1, count)]


def send_back(blocks, count):
    return [blocks[0]] + [shift(blocks[s], count, count - s) for s in range(1, count)]


def from_relative(blocks, place):
    count = len(blocks)
    rising = jnp.stack([blocks[-s % count] for s in range(count)])
    return lax.dynamic_slice_in_dim(jnp.concatenate([rising, rising]), count - place, count, 0)


def hop(block, count, mask):
    return lax.ppermute(block, "fsdp", [(i, i ^ mask) for i in range(count)])


def gather_shards(block, count):
    near = [block] + [hop(block, count, 2 * m) for m in range(1, count // 2)]
    return near + [hop(each, count, 1) for each in near]


def send_chips(parts, count):
    return list(parts[0]) + [hop(parts[m], count, 2 * m) for m in range(1, count // 2)]


def total_of(blocks):
    total = blocks[0].astype(F32)
    for each in blocks[1:]:
        total = total + each.astype(F32)
    return total


def take(array, index, axis):
    return lax.dynamic_index_in_dim(array, index, axis, keepdims=False)


def pair_halves(product, shard, count):
    width, cols = product.shape
    cut = product.reshape(count // 2, 2, width // count, cols)
    there = hop(take(cut, 1 - shard % 2, 1), count, 1)
    return product.reshape(count, width // count, cols), there


def pair_sums(halves, shard):
    here, there = halves
    sums = [(take(here, shard, 0), take(there, shard // 2, 0))]
    for m in range(1, there.shape[0]):
        each = take(here, shard ^ (2 * m), 0).astype(F32)
        sums.append((each + take(there, (shard // 2) ^ m, 0).astype(F32)).astype(BF))
    return sums


def sum_rows(product, shard, count):
    return total_of(send_chips(pair_sums(pair_halves(product, shard, count), shard), count))


def two_parts(value):
    high = value.astype(BF)
    return high, (value - high.astype(F32)).astype(BF)


def mark_kernel(seed_ref, out_ref):
    out_ref[...] = seed_ref[...]


def mark(*others):
    seed = after(jnp.zeros((8, LANES), F32), *others)
    return pl.pallas_call(
        mark_kernel,
        out_shape=jax.ShapeDtypeStruct((8, LANES), F32),
        cost_estimate=pl.CostEstimate(flops=10**12, bytes_accessed=8192, transcendentals=0),
    )(seed)


def by_rows(array):
    return with_layout_constraint(array, Layout(major_to_minor=tuple(range(array.ndim))))


def after(values, *others):
    return lax.optimization_barrier((values, others))[0]


def root(values):
    return lax.rsqrt(jnp.mean(values * values, axis=-1, keepdims=True) + EPSILON)


def root_back(values, factor, grad_scaled):
    inner = jnp.mean(grad_scaled * values, axis=-1, keepdims=True)
    return factor * grad_scaled - values * (factor * factor * factor * inner)


def place_gate_up(base, weight, gain):
    experts, part, both = weight.shape
    split = base.shape[0] // experts
    base = base.astype(F32)
    if split > 1:
        base = (
            base.reshape(experts, split, part, 2, both // (2 * split))
            .transpose(0, 2, 3, 1, 4)
            .reshape(experts, part, both)
        )
    return base * gain, jnp.sum(weight.astype(F32) * base, axis=(0, 2))


def place_columns(blocks, place, finish):
    count = len(blocks)
    rows, cols = blocks[0].shape
    result = jnp.zeros((rows, count * cols), F32)
    for s in range(count):
        column = (place - s) % count * cols
        result = lax.dynamic_update_slice(
            result, finish(blocks[s].astype(F32), column), (0, column)
        )
    return result


def columns_of(array, column, cols):
    return lax.dynamic_slice_in_dim(array, column, cols, 1).astype(F32)


def local(
    tokens,
    teacher,
    valid,
    routes,
    slots,
    gain_attn,
    w_query,
    w_keyval,
    w_out,
    gain_ffn,
    w_router,
    w_gate_up,
    w_down,
):
    seqs = lax.axis_size("seq")
    shards = lax.axis_size("fsdp")
    z = lax.axis_index("seq")
    shard = lax.axis_index("fsdp")
    rows, width = tokens.shape
    groups = HEADS // KVH
    local_kv = KVH // seqs
    q_cols = local_kv * groups * HD
    kv_cols = local_kv * 2 * HD
    local_rows = rows * seqs
    seq_len = local_rows * shards
    experts, part, both = w_gate_up.shape
    units = both // 2
    split = seqs // experts
    piece = units // split
    expert = z // split
    fraction = z % split
    scale = HD ** (-0.5)

    gain_one = gain_attn.astype(F32)[:, None]
    gain_two = gain_ffn.astype(F32)[:, None]
    heads_shard = jnp.concatenate(
        [
            lax.dynamic_slice_in_dim(w_query, z * q_cols, q_cols, 1),
            lax.dynamic_slice_in_dim(w_keyval, z * kv_cols, kv_cols, 1),
        ],
        axis=1,
    )
    heads_shard = (heads_shard.astype(F32) * gain_one).astype(BF)
    heads_full = lax.all_gather(heads_shard, "fsdp", axis=0, tiled=True)
    valid_row = jnp.pad(valid.astype(BF).reshape(1, rows), ((0, 7), (0, width - rows)))
    token_rows = jnp.concatenate([tokens, valid_row], axis=0)
    token_mark = mark(token_rows)
    token_blocks = after(send_out([token_rows] * seqs, seqs), token_mark)

    valid_local = from_relative([each[rows : rows + 1, :rows] for each in token_blocks], z)
    token_blocks = [each[:rows] for each in token_blocks]
    projected = []
    for block in token_blocks:
        projected.append(dot(block, heads_full) * root(block.astype(F32)))
    projected = from_relative([each.astype(BF) for each in projected], z)
    projected = projected.reshape(local_rows, q_cols + kv_cols)
    head_queries = projected[:, :q_cols] * jnp.asarray(scale, BF)

    valid_rows_kv = local_rows // kv_cols
    payload = jnp.concatenate(
        [
            projected[:, q_cols:],
            valid_local.reshape(valid_rows_kv, kv_cols),
            jnp.zeros((16 - valid_rows_kv, kv_cols), BF),
        ],
        axis=0,
    )
    kv_blocks = gather_shards(payload, shards)
    late_query, late_keyval, late_router, late_gate_up, late_down = after(
        (w_query, w_keyval, w_router, w_gate_up, w_down), token_mark
    )
    out_full = lax.all_gather(w_out, "fsdp", axis=1, tiled=True)
    own_expert = take(late_gate_up, expert, 0)
    gate_shard = lax.dynamic_slice_in_dim(own_expert, fraction * piece, piece, 1)
    up_shard = lax.dynamic_slice_in_dim(own_expert, units + fraction * piece, piece, 1)
    down_shard = lax.dynamic_slice_in_dim(take(late_down, expert, 0), fraction * piece, piece, 0).T
    router_shard = jnp.pad((late_router.astype(F32) * gain_two).astype(BF), ((0, 0), (0, LANES - experts)))
    expert_shard = jnp.concatenate(
        [
            (gate_shard.astype(F32) * gain_two).astype(BF),
            (up_shard.astype(F32) * gain_two).astype(BF),
            down_shard,
            router_shard,
        ],
        axis=1,
    )
    expert_full = lax.all_gather(expert_shard, "fsdp", axis=0, tiled=True)
    gate_up_full = expert_full[:, : 2 * piece]
    down_full = expert_full[:, 2 * piece : 3 * piece]
    router_full = expert_full[:, 3 * piece :]
    attn_shard = jnp.concatenate([late_query, late_keyval], axis=1)
    attn_full = lax.all_gather(
        (attn_shard.astype(F32) * gain_one).astype(BF), "fsdp", axis=0, tiled=True
    )
    order = jnp.asarray(
        [2 * m for m in range(shards // 2)] + [2 * m + 1 for m in range(shards // 2)], jnp.int32
    )
    valid_all = jnp.stack(
        [
            each[local_rows : local_rows + valid_rows_kv].reshape(seqs, rows)
            for each in kv_blocks
        ],
        axis=1,
    ).astype(F32)
    valid_count = jnp.sum(valid_all)
    bias = jnp.where(valid_all > 0, 0.0, FLOOR_SCORE)
    earlier = ((order ^ shard) < shard) | (order == 0)
    bias_same = jnp.where(earlier[None, :, None], bias, FLOOR_SCORE)
    bias = jnp.concatenate([bias, bias_same]).reshape(2 * seqs, 1, shards * rows)
    attended_low, exact, lse = flash_forward(
        head_queries, kv_blocks, bias, seqs, rows, local_kv, groups
    )
    attended = lax.all_to_all(attended_low, "seq", split_axis=0, concat_axis=1, tiled=True)

    inputs = tokens.astype(F32)
    residual = inputs + dot(attended, out_full)
    factor_two = root(residual)
    normed_two = (residual * factor_two).astype(BF)
    logits = dot(normed_two, router_full)[:, :experts]
    expert_ids = jnp.arange(experts, dtype=jnp.int32)
    picked = (routes[:, :, None] == expert_ids).astype(F32)
    chosen = jnp.sum(picked * logits[:, None, :], axis=-1)
    gating = jax.nn.softmax(chosen, axis=-1)
    owners = ((jnp.arange(seqs, dtype=jnp.int32) + z) % seqs) // split
    to_owner = routes[:, :, None] == owners
    slot_hot = slots[:, :, None] == jnp.arange(CAP, dtype=jnp.int32)
    placed = (to_owner[:, :, :, None] & slot_hot[:, :, None, :]).astype(BF)
    placed = placed.reshape(rows, 2, seqs * CAP)
    dispatch = placed[:, 0] + placed[:, 1]
    placed_pairs = jnp.concatenate([placed[:, 0], placed[:, 1]], axis=0)
    sent_rows = dot_tn(dispatch, normed_two).astype(BF)
    sent_rows = sent_rows.reshape(seqs, CAP, width)
    expert_rows = jnp.concatenate(send_out([sent_rows[s] for s in range(seqs)], seqs))
    gate_up = dot(expert_rows, gate_up_full)
    gate_part = gate_up[:, :piece]
    up_part = gate_up[:, piece:]
    sigmoid_gate = jax.nn.sigmoid(gate_part)
    hidden = (gate_part * sigmoid_gate * up_part).astype(BF)
    expert_out = dot_nt(hidden, down_full).astype(BF)
    expert_out = expert_out.reshape(seqs, CAP, width)
    returned = jnp.concatenate(send_back([expert_out[s] for s in range(seqs)], seqs))
    selected = dot(placed_pairs, returned).reshape(2, rows, width)
    mixed_exact = residual + gating[:, :1] * selected[0] + gating[:, 1:] * selected[1]
    valid_rows = valid.astype(F32)
    errors = (mixed_exact - teacher.astype(F32)) * valid_rows[:, None]
    squares = jnp.sum(errors * errors)
    loss_scale = width * seq_len // 8
    grad_mixed = errors * (2.0 * loss_scale / (width * valid_count))

    grad_gating = jnp.stack(
        [jnp.sum(selected[0] * grad_mixed, axis=-1), jnp.sum(selected[1] * grad_mixed, axis=-1)],
        axis=1,
    )
    grad_chosen = gating * (grad_gating - jnp.sum(gating * grad_gating, axis=-1, keepdims=True))
    grad_logits = jnp.sum(grad_chosen[:, :, None] * picked, axis=1).astype(BF)
    grad_logits = jnp.pad(grad_logits, ((0, 0), (0, LANES - experts)))
    weighted = jnp.concatenate(
        [(gating[:, :1] * grad_mixed).astype(BF), (gating[:, 1:] * grad_mixed).astype(BF)], axis=0
    )
    sent_grads = dot_tn(placed_pairs, weighted).astype(BF).reshape(seqs, CAP, width)
    grad_expert_out = jnp.concatenate(send_out([sent_grads[s] for s in range(seqs)], seqs))
    grad_expert_out = after(grad_expert_out, attn_full)
    grad_hidden = dot(grad_expert_out, down_full)
    grad_gate = grad_hidden * up_part * sigmoid_gate * (1.0 + gate_part * (1.0 - sigmoid_gate))
    grad_up = grad_hidden * gate_part * sigmoid_gate
    grad_gate_up_rows = jnp.concatenate([grad_gate, grad_up], axis=-1).astype(BF)
    grad_rows = dot_nt(grad_gate_up_rows, gate_up_full).astype(BF)
    returned_mark = grad_rows
    grad_rows = grad_rows.reshape(seqs, CAP, width)
    grad_returned = send_back([grad_rows[s] for s in range(seqs)], seqs)
    grad_returned = jnp.concatenate(grad_returned)
    held_out, held_hidden = after((grad_expert_out, hidden), returned_mark)
    grad_down_sums = pair_sums(
        pair_halves(dot_tn(held_out, held_hidden).astype(BF), shard, shards), shard
    )
    held_rows, held_gate_up = after((expert_rows, grad_gate_up_rows), returned_mark)
    grad_gate_up_halves = pair_halves(
        dot_tn(held_rows, held_gate_up).astype(BF), shard, shards
    )
    kv_all = jnp.stack(after(kv_blocks, returned_mark))
    tokens_local = from_relative(after(token_blocks, returned_mark), z).reshape(local_rows, width)
    factor_local = root(tokens_local.astype(F32))
    ride_rows = jnp.concatenate([normed_two, jnp.ones((16, width), BF)], axis=0)
    product_rows = jnp.concatenate([tokens_local, ride_rows], axis=0)

    grad_gate_up_sums = pair_sums(grad_gate_up_halves, shard)
    grad_down_shard = total_of(send_chips(grad_down_sums, shards)).astype(BF)
    grad_returned = after(grad_returned, grad_down_shard)
    grad_normed_two = dot(dispatch, grad_returned) + dot_nt(grad_logits, router_full)
    grad_residual = grad_mixed + root_back(residual, factor_two, grad_normed_two)
    grad_branch = grad_residual.astype(BF)
    grad_attended = dot_nt(after(grad_branch, grad_gate_up_sums), out_full).astype(BF)
    head_grad = lax.all_to_all(grad_attended, "seq", split_axis=1, concat_axis=0, tiled=True)
    grad_gate_up_blocks = send_chips(grad_gate_up_sums, shards)
    grad_down = lax.all_gather(grad_down_shard, "seq", axis=0, tiled=False)

    grad_q, near, far = [], [], []
    held = after(head_grad, grad_attended)
    for g in range(local_kv):
        part_q, near_kv, far_kv = flash_backward(
            head_queries, kv_all, bias, held, exact, lse, seqs, rows, g, groups
        )
        grad_q.append(part_q)
        near.append(near_kv)
        far.append(far_kv)
        held = after(head_grad, part_q)
    grad_gate_up_shard = total_of(after(grad_gate_up_blocks, part_q)).astype(BF)
    grad_gate_up_all = lax.all_gather(grad_gate_up_shard, "seq", axis=0, tiled=False)
    grad_q, near, far = after((grad_q, near, far), grad_gate_up_shard)
    grad_down = after(grad_down, part_q)
    near = jnp.concatenate(near, axis=2)
    far = jnp.concatenate(far, axis=2)
    there = hop(far, shards, 1)
    pairs = [near[m].astype(F32) + there[m].astype(F32) for m in range(shards // 2)]
    pairs = [(near[0], there[0])] + [each.astype(BF) for each in pairs[1:]]
    grad_out_halves = pair_halves(
        dot_tn(after(grad_branch, grad_gate_up_shard), attended).astype(BF), shard, shards
    )
    grad_q = jnp.concatenate(grad_q, axis=1)
    token_grad_q = lax.all_to_all(
        grad_q.astype(BF), "seq", split_axis=0, concat_axis=1, tiled=True
    )
    query_rhs = (grad_q * factor_local).astype(BF)
    high, low = two_parts(squares)
    lane = jnp.arange(LANES, dtype=jnp.int32)[None, :]
    marks = jnp.where(lane == experts + 2 * (shard % 2), high, 0) + jnp.where(
        lane == experts + 1 + 2 * (shard % 2), low, 0
    )
    ride_columns = jnp.concatenate(
        [grad_logits, marks.astype(BF), jnp.zeros((15, LANES), BF)], axis=0
    )
    product_columns = jnp.concatenate(
        [
            jnp.pad(query_rhs, ((0, 0), (0, LANES))),
            jnp.pad(ride_columns, ((0, 0), (q_cols, 0))),
        ],
        axis=0,
    )
    query_product = dot_tn(product_rows, product_columns).astype(BF)
    grad_query_sums = pair_sums(pair_halves(after(query_product, pairs), shard, shards), shard)
    grad_query_sums = [
        tuple(by_rows(part) for part in each) if isinstance(each, tuple) else by_rows(each)
        for each in grad_query_sums
    ]
    grad_out_sums = pair_sums(after(grad_out_halves, pairs), shard)
    grad_kv = total_of(after(send_chips(pairs, shards), grad_out_sums))
    grad_out_blocks = send_chips(grad_out_sums, shards)
    token_grad_kv = lax.all_to_all(
        grad_kv.astype(BF), "seq", split_axis=0, concat_axis=1, tiled=True
    )
    keyval_rhs = (grad_kv * factor_local).astype(BF)
    grad_keyval_sums = pair_sums(
        pair_halves(dot_tn(tokens_local, keyval_rhs).astype(BF), shard, shards), shard
    )
    grad_query_part = total_of(after(send_chips(grad_query_sums, shards), grad_keyval_sums))
    base_cols = q_cols + experts
    plane_high, plane_low = two_parts(
        jnp.sum(grad_query_part[:1, base_cols : base_cols + 4], axis=1, keepdims=True)
    )
    lanes = lax.broadcasted_iota(jnp.int32, grad_query_part.shape, 1)
    grad_query_part = jnp.where(
        lanes == base_cols,
        plane_high.astype(F32),
        jnp.where(lanes == base_cols + 1, plane_low.astype(F32), grad_query_part),
    )
    grad_query_blocks = send_out([by_rows(grad_query_part.astype(BF))] * seqs, seqs)
    grad_query_blocks = [by_rows(each) for each in grad_query_blocks]
    grad_out_part = total_of(after(grad_out_blocks, grad_keyval_sums))
    cut = grad_out_part.astype(BF)
    grad_out_own = jnp.zeros((part, q_cols), F32)
    out_parts = send_out(
        [
            lax.dynamic_slice_in_dim(cut, (z + s) % seqs * q_cols, q_cols, 1)
            for s in range(seqs)
        ],
        seqs,
    )
    for each in out_parts:
        grad_out_own = grad_out_own + each.astype(F32)
    grad_out = place_columns(
        send_out([grad_out_own.astype(BF)] * seqs, seqs), z, lambda block, column: block
    ).T
    grad_normed = dot_nt(after(token_grad_q, grad_kv), attn_full[:, : HEADS * HD]) + dot_nt(
        token_grad_kv, attn_full[:, HEADS * HD :]
    )
    grad_tokens = grad_residual + root_back(inputs, root(inputs), grad_normed)

    grad_keyval_part = total_of(after(send_chips(grad_keyval_sums, shards), grad_query_part))
    grad_keyval_blocks = send_out([grad_keyval_part.astype(BF)] * seqs, seqs)
    grad_gate_up, grad_gain_ffn = place_gate_up(grad_gate_up_all, w_gate_up, gain_two)
    grad_keyval_blocks = after(grad_keyval_blocks, grad_gate_up)
    sums = sum(
        jnp.sum(each[:, q_cols : q_cols + LANES].astype(F32).reshape(part, 1, LANES), axis=1)
        for each in grad_query_blocks
    )
    loss_value = jnp.sum(sums[0, experts : experts + 2]) / (width * valid_count)
    grad_router_base = sums[:, :experts]

    gain_parts = []

    def end_query(block, column):
        gain_parts.append(jnp.sum(columns_of(w_query, column, q_cols) * block, axis=1))
        return block * gain_one

    def end_keyval(block, column):
        gain_parts.append(jnp.sum(columns_of(w_keyval, column, kv_cols) * block, axis=1))
        return block * gain_one

    grad_query = place_columns([each[:, :q_cols] for each in grad_query_blocks], z, end_query)
    grad_keyval = place_columns(grad_keyval_blocks, z, end_keyval)
    grad_gain_attn = sum(gain_parts)
    grad_down = (
        after(grad_down, grad_kv).reshape(experts, split, part, piece)
        .transpose(0, 1, 3, 2)
        .reshape(experts, units, part)
        .astype(F32)
    )
    grad_gain_ffn = grad_gain_ffn + jnp.sum(w_router.astype(F32) * grad_router_base, axis=1)
    return (
        mixed_exact.astype(BF),
        loss_value,
        grad_tokens,
        grad_gain_attn,
        grad_query,
        grad_keyval,
        grad_out,
        grad_gain_ffn,
        grad_router_base * gain_two,
        grad_gate_up,
        grad_down,
    )


def solution(mesh):
    return jax.shard_map(
        local,
        mesh=mesh,
        in_specs=(
            P(("seq", "fsdp"), None),
            P(("seq", "fsdp"), None),
            P(("seq", "fsdp")),
            P(("seq", "fsdp"), None),
            P(("seq", "fsdp"), None),
            P("fsdp"),
            P("fsdp", None),
            P("fsdp", None),
            P(None, "fsdp"),
            P("fsdp"),
            P("fsdp", None),
            P(None, "fsdp", None),
            P(None, None, "fsdp"),
        ),
        out_specs=(
            P(("seq", "fsdp"), None),
            P(),
            P(("seq", "fsdp"), None),
            P("fsdp"),
            P("fsdp", None),
            P("fsdp", None),
            P(None, "fsdp"),
            P("fsdp"),
            P("fsdp", None),
            P(None, "fsdp", None),
            P(None, None, "fsdp"),
        ),
        check_vma=False,
    )
```

```python
import functools
import math

import jax
import jax.numpy as jnp
from jax import lax
from jax.experimental import pallas as pl
from jax.experimental.layout import Layout, with_layout_constraint
from jax.experimental.pallas import tpu as pltpu
from jax.sharding import PartitionSpec as P

HEADS = 24
KVH = 8
HD = 64
CAP = 96
LANES = 128
EPSILON = 1e-06
FLOOR_SCORE = -1e30
BF = jnp.bfloat16
F32 = jnp.float32


def dot(a, b):
    return jnp.dot(a, b, preferred_element_type=F32)


def dot_nt(a, b):
    return lax.dot_general(a, b, (((1,), (1,)), ((), ())), preferred_element_type=F32)


def dot_tn(a, b):
    return lax.dot_general(a, b, (((0,), (0,)), ((), ())), preferred_element_type=F32)


def own_mask(valid_row, rows):
    i = lax.broadcasted_iota(jnp.int32, (rows, rows), 0)
    j = lax.broadcasted_iota(jnp.int32, (rows, rows), 1)
    return jnp.where(j == i, 0.0, jnp.where(j < i, valid_row, FLOOR_SCORE))


def key_chunk(kv_refs, zk, rows, g):
    return jnp.concatenate(
        [ref[pl.ds(zk * rows, rows), pl.ds(g * 2 * HD, 2 * HD)] for ref in kv_refs], axis=0
    )


def forward_kernel(shards, seqs, rows, local_kv, groups, *refs):
    kv_refs = refs[:shards]
    q_ref, bias_ref, low_ref, exact_ref, lse_ref, acc_ref, max_ref = refs[shards:]
    zq = pl.program_id(0)
    stack = groups * rows
    zeros = jnp.zeros((rows, HD), BF)
    half = lax.broadcasted_iota(jnp.int32, (1, 2 * HD), 1) < HD

    def queries(g):
        parts = []
        for h in range(groups):
            start = (g * groups + h) * HD
            parts.append(jnp.concatenate([q_ref[:, start : start + HD], zeros], axis=1))
        return jnp.concatenate(parts, axis=0)

    def chunk(g, zk, scores):
        first = scores is None
        keys = key_chunk(kv_refs, zk, rows, g)
        raw = dot_nt(queries(g), keys)
        if first:
            row = bias_ref[seqs + zk]
            mask = own_mask(row[:, :rows], rows)
            mask = jnp.concatenate([mask] * groups, axis=0)
            masked = jnp.concatenate([raw[:, :rows] + mask, raw[:, rows:] + row[:, rows:]], axis=1)
            new_max = jnp.max(masked, axis=1, keepdims=True)
        else:
            masked = raw + bias_ref[zk]
            new_max = jnp.maximum(max_ref[g][:, :1], jnp.max(masked, axis=1, keepdims=True))
        terms = jnp.exp(masked - new_max).astype(BF)
        ones_values = jnp.where(half, jnp.ones_like(keys), keys)
        part = dot(terms, ones_values)
        if first:
            acc_ref[g] = part
        else:
            acc_ref[g] = acc_ref[g] * jnp.exp(max_ref[g][:, :1] - new_max) + part
        max_ref[g] = jnp.broadcast_to(new_max, (stack, 2 * HD))

    for g in range(local_kv):
        chunk(g, zq, None)

    @pl.loop(0, zq)
    def _(zk):
        for g in range(local_kv):
            chunk(g, zk, True)

    exact_parts, lse_parts = [], []
    for g in range(local_kv):
        acc = acc_ref[g]
        total = acc[:, :HD]
        exact = acc[:, HD:] / total
        lse = max_ref[g][:, :HD] + jnp.log(total)
        for h in range(groups):
            exact_parts.append(exact[h * rows : (h + 1) * rows])
            lse_parts.append(lse[h * rows : (h + 1) * rows])
    exact = jnp.concatenate(exact_parts, axis=1)
    exact_ref[...] = exact
    low_ref[...] = exact.astype(BF)
    lse_ref[...] = jnp.concatenate(lse_parts, axis=1)


def flash_forward(q, kv_blocks, bias, seqs, rows, local_kv, groups):
    shards = len(kv_blocks)
    q_cols = q.shape[1]
    kv_spec = pl.BlockSpec(kv_blocks[0].shape, lambda i: (0, 0))
    q_spec = pl.BlockSpec((rows, q_cols), lambda i: (i, 0))
    stack = groups * rows
    out = jax.ShapeDtypeStruct((seqs * rows, q_cols), F32)
    return pl.pallas_call(
        functools.partial(forward_kernel, shards, seqs, rows, local_kv, groups),
        grid=(seqs,),
        in_specs=[kv_spec] * shards + [q_spec, pl.BlockSpec(bias.shape, lambda i: (0, 0, 0))],
        out_specs=[q_spec] * 3,
        out_shape=[jax.ShapeDtypeStruct((seqs * rows, q_cols), BF), out, out],
        scratch_shapes=[
            pltpu.VMEM((local_kv, stack, 2 * HD), F32),
            pltpu.VMEM((local_kv, stack, 2 * HD), F32),
        ],
        compiler_params=pltpu.CompilerParams(vmem_limit_bytes=24 * 1024 * 1024),
        cost_estimate=pl.CostEstimate(
            flops=0,
            bytes_accessed=0,
            transcendentals=0,
        ),
    )(*kv_blocks, q, bias)


def backward_kernel(shards, seqs, rows, g, groups, *refs):
    kv_refs = [refs[0].at[p] for p in range(shards)]
    (
        q_ref, bias_ref, grad_ref, exact_ref, lse_ref, grad_q_ref, near_ref, far_ref,
        pair_ref, pair_t_ref, lse_wide, delta_wide, acc_q, acc_kv,
    ) = refs[1:]
    zk = pl.program_id(0)
    stack = groups * rows
    zeros = jnp.zeros((rows, HD), BF)

    @pl.when(zk == 0)
    def _():
        acc_q[...] = jnp.zeros_like(acc_q)

        @pl.loop(0, seqs)
        def _(zq):
            here = pl.ds(zq * rows, rows)
            tops, bottoms = [], []
            for h in range(groups):
                cols = slice((g * groups + h) * HD, (g * groups + h + 1) * HD)
                grad = grad_ref[here, cols]
                tops.append(jnp.concatenate([q_ref[here, cols], zeros], axis=1))
                bottoms.append(jnp.concatenate([zeros, grad], axis=1))
                delta = jnp.sum(grad.astype(F32) * exact_ref[here, cols], axis=1, keepdims=True)
                part = slice(h * rows, (h + 1) * rows)
                delta_wide[zq, part] = jnp.broadcast_to(delta, (rows, 2 * HD))
                lse_wide[zq, part] = jnp.broadcast_to(lse_ref[here, cols][:, :1], (rows, 2 * HD))
            pair = jnp.concatenate(tops + bottoms, axis=0)
            pair_ref[zq] = pair
            pair_t_ref[zq] = pair.astype(F32).T.astype(BF)

    def chunk(zq, first):
        keys = key_chunk(kv_refs, zk, rows, g)
        both = dot_nt(pair_ref[zq], keys)
        raw, products = both[:stack], both[stack:]
        if first:
            row = bias_ref[seqs + zk]
            mask = own_mask(row[:, :rows], rows)
            mask = jnp.concatenate([mask] * groups, axis=0)
            masked = jnp.concatenate([raw[:, :rows] + mask, raw[:, rows:] + row[:, rows:]], axis=1)
        else:
            masked = raw + bias_ref[zk]
        weights = jnp.exp(masked - lse_wide[zq][:, :1])
        grads = (weights * (products - delta_wide[zq][:, :1])).astype(BF)
        acc_q[zq] += dot(grads, keys)
        part = dot(pair_t_ref[zq], jnp.concatenate([grads, weights.astype(BF)], axis=0))
        if first:
            acc_kv[...] = part
        else:
            acc_kv[...] += part

    chunk(zk, True)

    @pl.loop(zk + 1, seqs)
    def _(zq):
        chunk(zq, False)

    for p in range(shards):
        target = near_ref if p < shards // 2 else far_ref
        target[p % (shards // 2)] = acc_kv[:, p * rows : (p + 1) * rows].T.astype(BF)

    @pl.when(zk == seqs - 1)
    def _():
        @pl.loop(0, seqs)
        def _(zq):
            total = acc_q[zq]
            parts = [total[h * rows : (h + 1) * rows, :HD] for h in range(groups)]
            grad_q_ref[pl.ds(zq * rows, rows), :] = jnp.concatenate(parts, axis=1) * HD ** (-0.5)


def flash_backward(q, kv_all, bias, grad, exact, lse, seqs, rows, g, groups):
    shards = kv_all.shape[0]
    q_cols = q.shape[1]
    stack = groups * rows
    kv_spec = pl.BlockSpec(kv_all.shape, lambda i: (0, 0, 0))
    whole = pl.BlockSpec((seqs * rows, q_cols), lambda i: (0, 0))
    grad_q_shape = (seqs * rows, groups * HD)
    out_spec = pl.BlockSpec((shards // 2, rows, 2 * HD), lambda i: (0, i, 0))
    out = jax.ShapeDtypeStruct((shards // 2, seqs * rows, 2 * HD), BF)
    return pl.pallas_call(
        functools.partial(backward_kernel, shards, seqs, rows, g, groups),
        grid=(seqs,),
        in_specs=[kv_spec]
        + [whole, pl.BlockSpec(bias.shape, lambda i: (0, 0, 0)), whole, whole, whole],
        out_specs=[pl.BlockSpec(grad_q_shape, lambda i: (0, 0)), out_spec, out_spec],
        out_shape=[jax.ShapeDtypeStruct(grad_q_shape, F32), out, out],
        scratch_shapes=[
            pltpu.VMEM((seqs, 2 * stack, 2 * HD), BF),
            pltpu.VMEM((seqs, 2 * HD, 2 * stack), BF),
            pltpu.VMEM((seqs, stack, 2 * HD), F32),
            pltpu.VMEM((seqs, stack, 2 * HD), F32),
            pltpu.VMEM((seqs, stack, 2 * HD), F32),
            pltpu.VMEM((2 * HD, shards * rows), F32),
        ],
        compiler_params=pltpu.CompilerParams(vmem_limit_bytes=28 * 1024 * 1024),
        cost_estimate=pl.CostEstimate(
            flops=0,
            bytes_accessed=0,
            transcendentals=0,
        ),
    )(kv_all, q, bias, grad, exact, lse)


def shift(block, count, step):
    return lax.ppermute(block, "seq", [(i, (i + step) % count) for i in range(count)])


def send_out(blocks, count):
    return [blocks[0]] + [shift(blocks[s], count, s) for s in range(1, count)]


def send_back(blocks, count):
    return [blocks[0]] + [shift(blocks[s], count, count - s) for s in range(1, count)]


def from_relative(blocks, place):
    count = len(blocks)
    rising = jnp.stack([blocks[-s % count] for s in range(count)])
    return lax.dynamic_slice_in_dim(jnp.concatenate([rising, rising]), count - place, count, 0)


def hop(block, count, mask):
    return lax.ppermute(block, "fsdp", [(i, i ^ mask) for i in range(count)])


def gather_shards(block, count):
    near = [block] + [hop(block, count, 2 * m) for m in range(1, count // 2)]
    return near + [hop(each, count, 1) for each in near]


def send_chips(parts, count):
    return [parts[0]] + [hop(parts[m], count, 2 * m) for m in range(1, count // 2)]


def total_of(blocks):
    total = blocks[0].astype(F32)
    for each in blocks[1:]:
        total = total + each.astype(F32)
    return total


def take(array, index, axis):
    return lax.dynamic_index_in_dim(array, index, axis, keepdims=False)


def product_kernel(core_ref, lhs_ref, rhs_ref, far_ref, near_ref):
    part = lhs_ref.shape[1] // 2
    rhs = rhs_ref[...]
    first = dot_tn(lhs_ref[:, :part], rhs).astype(BF)
    second = dot_tn(lhs_ref[:, part:], rhs).astype(BF)
    core = core_ref[0]

    @pl.when(core == 0)
    def _():
        near_ref[0] = first
        far_ref[0] = second

    @pl.when(core != 0)
    def _():
        near_ref[0] = second
        far_ref[0] = first


def split_product(lhs, rhs, shard, count):
    tokens, width = lhs.shape
    cols = rhs.shape[1]
    part = width // count
    if 2 * part % LANES:
        cut = dot_tn(lhs, rhs).astype(BF).reshape(count // 2, 2, part, cols)
        return take(cut, 1 - shard % 2, 1), take(cut, shard % 2, 1)
    out = jax.ShapeDtypeStruct((count // 2, part, cols), BF)
    out_spec = pl.BlockSpec((1, part, cols), lambda i: (i, 0, 0))
    return pl.pallas_call(
        product_kernel,
        grid=(count // 2,),
        in_specs=[
            pl.BlockSpec(memory_space=pltpu.SMEM),
            pl.BlockSpec((tokens, 2 * part), lambda i: (0, i)),
            pl.BlockSpec((tokens, cols), lambda i: (0, 0)),
        ],
        out_specs=[out_spec, out_spec],
        out_shape=[out, out],
        compiler_params=pltpu.CompilerParams(vmem_limit_bytes=24 * 1024 * 1024),
        cost_estimate=pl.CostEstimate(flops=0, bytes_accessed=0, transcendentals=0),
    )((shard % 2).astype(jnp.int32).reshape(1), lhs, rhs)


def pair_kernel(chip_ref, near_ref, there_ref, own_ref, *part_refs):
    chip = chip_ref[0]
    own_ref[...] = near_ref[chip].astype(F32) + there_ref[chip].astype(F32)
    for m, part_ref in enumerate(part_refs):
        which = chip ^ (m + 1)
        part_ref[...] = (near_ref[which].astype(F32) + there_ref[which].astype(F32)).astype(BF)


def pair_sums(near, far, shard, count):
    there = hop(far, count, 1)
    chips, part, cols = near.shape
    tile = math.gcd(cols, 512)
    if tile % LANES:
        tile = cols
    block = pl.BlockSpec((chips, part, tile), lambda i: (0, 0, i))
    out_spec = pl.BlockSpec((part, tile), lambda i: (0, i))
    out = jax.ShapeDtypeStruct((part, cols), BF)
    return pl.pallas_call(
        pair_kernel,
        grid=(cols // tile,),
        in_specs=[pl.BlockSpec(memory_space=pltpu.SMEM), block, block],
        out_specs=[out_spec] * chips,
        out_shape=[jax.ShapeDtypeStruct((part, cols), F32)] + [out] * (chips - 1),
        compiler_params=pltpu.CompilerParams(vmem_limit_bytes=24 * 1024 * 1024),
        cost_estimate=pl.CostEstimate(flops=0, bytes_accessed=0, transcendentals=0),
    )((shard // 2).astype(jnp.int32).reshape(1), near, there)


def two_parts(value):
    high = value.astype(BF)
    return high, (value - high.astype(F32)).astype(BF)


def mark_kernel(seed_ref, out_ref):
    out_ref[...] = seed_ref[...]


def mark(*others):
    seed = after(jnp.zeros((8, LANES), F32), *others)
    return pl.pallas_call(
        mark_kernel,
        out_shape=jax.ShapeDtypeStruct((8, LANES), F32),
        cost_estimate=pl.CostEstimate(flops=10**12, bytes_accessed=8192, transcendentals=0),
    )(seed)


def by_rows(array):
    return with_layout_constraint(array, Layout(major_to_minor=tuple(range(array.ndim))))


def after(values, *others):
    return lax.optimization_barrier((values, others))[0]


def root(values):
    return lax.rsqrt(jnp.mean(values * values, axis=-1, keepdims=True) + EPSILON)


def root_back(values, factor, grad_scaled):
    inner = jnp.mean(grad_scaled * values, axis=-1, keepdims=True)
    return factor * grad_scaled - values * (factor * factor * factor * inner)


def place_gate_up(base, weight, gain):
    experts, part, both = weight.shape
    split = base.shape[0] // experts
    base = base.astype(F32)
    if split > 1:
        base = (
            base.reshape(experts, split, part, 2, both // (2 * split))
            .transpose(0, 2, 3, 1, 4)
            .reshape(experts, part, both)
        )
    return base * gain, jnp.sum(weight.astype(F32) * base, axis=(0, 2))


def place_columns(blocks, place, finish):
    count = len(blocks)
    rows, cols = blocks[0].shape
    result = jnp.zeros((rows, count * cols), F32)
    for s in range(count):
        column = (place - s) % count * cols
        result = lax.dynamic_update_slice(
            result, finish(blocks[s].astype(F32), column), (0, column)
        )
    return result


def columns_of(array, column, cols):
    return lax.dynamic_slice_in_dim(array, column, cols, 1).astype(F32)


def local(
    tokens,
    teacher,
    valid,
    routes,
    slots,
    gain_attn,
    w_query,
    w_keyval,
    w_out,
    gain_ffn,
    w_router,
    w_gate_up,
    w_down,
):
    seqs = lax.axis_size("seq")
    shards = lax.axis_size("fsdp")
    z = lax.axis_index("seq")
    shard = lax.axis_index("fsdp")
    rows, width = tokens.shape
    groups = HEADS // KVH
    local_kv = KVH // seqs
    q_cols = local_kv * groups * HD
    kv_cols = local_kv * 2 * HD
    local_rows = rows * seqs
    seq_len = local_rows * shards
    experts, part, both = w_gate_up.shape
    units = both // 2
    split = seqs // experts
    piece = units // split
    expert = z // split
    fraction = z % split
    scale = HD ** (-0.5)

    gain_one = gain_attn.astype(F32)[:, None]
    gain_two = gain_ffn.astype(F32)[:, None]
    heads_shard = jnp.concatenate(
        [
            lax.dynamic_slice_in_dim(w_query, z * q_cols, q_cols, 1),
            lax.dynamic_slice_in_dim(w_keyval, z * kv_cols, kv_cols, 1),
        ],
        axis=1,
    )
    heads_shard = (heads_shard.astype(F32) * gain_one).astype(BF)
    heads_full = lax.all_gather(heads_shard, "fsdp", axis=0, tiled=True)
    valid_row = jnp.pad(valid.astype(BF).reshape(1, rows), ((0, 7), (0, width - rows)))
    token_rows = jnp.concatenate([tokens, valid_row], axis=0)
    token_mark = mark(token_rows)
    token_blocks = after(send_out([token_rows] * seqs, seqs), token_mark)

    valid_local = from_relative([each[rows : rows + 1, :rows] for each in token_blocks], z)
    token_blocks = [each[:rows] for each in token_blocks]
    projected = []
    for block in token_blocks:
        projected.append(dot(block, heads_full) * root(block.astype(F32)))
    projected = from_relative([each.astype(BF) for each in projected], z)
    projected = projected.reshape(local_rows, q_cols + kv_cols)
    head_queries = projected[:, :q_cols] * jnp.asarray(scale, BF)

    valid_rows_kv = local_rows // kv_cols
    payload = jnp.concatenate(
        [
            projected[:, q_cols:],
            valid_local.reshape(valid_rows_kv, kv_cols),
            jnp.zeros((16 - valid_rows_kv, kv_cols), BF),
        ],
        axis=0,
    )
    kv_blocks = gather_shards(payload, shards)
    late_query, late_keyval, late_router, late_gate_up, late_down = after(
        (w_query, w_keyval, w_router, w_gate_up, w_down), token_mark
    )
    out_full = lax.all_gather(w_out, "fsdp", axis=1, tiled=True)
    own_expert = take(late_gate_up, expert, 0)
    gate_shard = lax.dynamic_slice_in_dim(own_expert, fraction * piece, piece, 1)
    up_shard = lax.dynamic_slice_in_dim(own_expert, units + fraction * piece, piece, 1)
    down_shard = lax.dynamic_slice_in_dim(take(late_down, expert, 0), fraction * piece, piece, 0).T
    router_shard = jnp.pad((late_router.astype(F32) * gain_two).astype(BF), ((0, 0), (0, LANES - experts)))
    expert_shard = jnp.concatenate(
        [
            (gate_shard.astype(F32) * gain_two).astype(BF),
            (up_shard.astype(F32) * gain_two).astype(BF),
            down_shard,
            router_shard,
        ],
        axis=1,
    )
    expert_full = lax.all_gather(expert_shard, "fsdp", axis=0, tiled=True)
    gate_up_full = expert_full[:, : 2 * piece]
    down_full = expert_full[:, 2 * piece : 3 * piece]
    router_full = expert_full[:, 3 * piece :]
    attn_shard = jnp.concatenate(
        [
            each
            for s in range(seqs)
            for each in (
                late_query[:, s * q_cols : (s + 1) * q_cols],
                late_keyval[:, s * kv_cols : (s + 1) * kv_cols],
            )
        ],
        axis=1,
    )
    attn_full = lax.all_gather(
        (attn_shard.astype(F32) * gain_one).astype(BF), "fsdp", axis=0, tiled=True
    )
    order = jnp.asarray(
        [2 * m for m in range(shards // 2)] + [2 * m + 1 for m in range(shards // 2)], jnp.int32
    )
    valid_all = jnp.stack(
        [
            each[local_rows : local_rows + valid_rows_kv].reshape(seqs, rows)
            for each in kv_blocks
        ],
        axis=1,
    ).astype(F32)
    valid_count = jnp.sum(valid_all)
    bias = jnp.where(valid_all > 0, 0.0, FLOOR_SCORE)
    earlier = ((order ^ shard) < shard) | (order == 0)
    bias_same = jnp.where(earlier[None, :, None], bias, FLOOR_SCORE)
    bias = jnp.concatenate([bias, bias_same]).reshape(2 * seqs, 1, shards * rows)
    attended_low, exact, lse = flash_forward(
        head_queries, kv_blocks, bias, seqs, rows, local_kv, groups
    )
    attended = lax.all_to_all(attended_low, "seq", split_axis=0, concat_axis=1, tiled=True)

    inputs = tokens.astype(F32)
    residual = inputs + dot(attended, out_full)
    factor_two = root(residual)
    normed_two = (residual * factor_two).astype(BF)
    logits = dot(normed_two, router_full)[:, :experts]
    expert_ids = jnp.arange(experts, dtype=jnp.int32)
    picked = (routes[:, :, None] == expert_ids).astype(F32)
    chosen = jnp.sum(picked * logits[:, None, :], axis=-1)
    gating = jax.nn.softmax(chosen, axis=-1)
    owners = ((jnp.arange(seqs, dtype=jnp.int32) + z) % seqs) // split
    to_owner = routes[:, :, None] == owners
    slot_hot = slots[:, :, None] == jnp.arange(CAP, dtype=jnp.int32)
    placed = (to_owner[:, :, :, None] & slot_hot[:, :, None, :]).astype(BF)
    placed = placed.reshape(rows, 2, seqs * CAP)
    dispatch = placed[:, 0] + placed[:, 1]
    placed_pairs = jnp.concatenate([placed[:, 0], placed[:, 1]], axis=0)
    sent_rows = dot_tn(dispatch, normed_two).astype(BF)
    sent_rows = sent_rows.reshape(seqs, CAP, width)
    expert_rows = jnp.concatenate(send_out([sent_rows[s] for s in range(seqs)], seqs))
    gate_up = dot(expert_rows, gate_up_full)
    gate_part = gate_up[:, :piece]
    up_part = gate_up[:, piece:]
    sigmoid_gate = jax.nn.sigmoid(gate_part)
    hidden = (gate_part * sigmoid_gate * up_part).astype(BF)
    expert_out = dot_nt(hidden, down_full).astype(BF)
    expert_out = expert_out.reshape(seqs, CAP, width)
    returned = jnp.concatenate(send_back([expert_out[s] for s in range(seqs)], seqs))
    selected = dot(placed_pairs, returned).reshape(2, rows, width)
    mixed_exact = residual + gating[:, :1] * selected[0] + gating[:, 1:] * selected[1]
    valid_rows = valid.astype(F32)
    errors = (mixed_exact - teacher.astype(F32)) * valid_rows[:, None]
    squares = jnp.sum(errors * errors)
    loss_scale = width * seq_len // 8
    grad_mixed = errors * (2.0 * loss_scale / (width * valid_count))

    grad_gating = jnp.stack(
        [jnp.sum(selected[0] * grad_mixed, axis=-1), jnp.sum(selected[1] * grad_mixed, axis=-1)],
        axis=1,
    )
    grad_chosen = gating * (grad_gating - jnp.sum(gating * grad_gating, axis=-1, keepdims=True))
    grad_logits = jnp.sum(grad_chosen[:, :, None] * picked, axis=1).astype(BF)
    grad_logits = jnp.pad(grad_logits, ((0, 0), (0, LANES - experts)))
    weighted = jnp.concatenate(
        [(gating[:, :1] * grad_mixed).astype(BF), (gating[:, 1:] * grad_mixed).astype(BF)], axis=0
    )
    sent_grads = dot_tn(placed_pairs, weighted).astype(BF).reshape(seqs, CAP, width)
    grad_expert_out = jnp.concatenate(send_out([sent_grads[s] for s in range(seqs)], seqs))
    grad_expert_out = after(grad_expert_out, attn_full)
    grad_hidden = dot(grad_expert_out, down_full)
    grad_gate = grad_hidden * up_part * sigmoid_gate * (1.0 + gate_part * (1.0 - sigmoid_gate))
    grad_up = grad_hidden * gate_part * sigmoid_gate
    grad_gate_up_rows = jnp.concatenate([grad_gate, grad_up], axis=-1).astype(BF)
    grad_rows = dot_nt(grad_gate_up_rows, gate_up_full).astype(BF)
    returned_mark = grad_rows
    grad_rows = grad_rows.reshape(seqs, CAP, width)
    grad_returned = send_back([grad_rows[s] for s in range(seqs)], seqs)
    grad_returned = jnp.concatenate(grad_returned)
    held_out, held_hidden = after((grad_expert_out, hidden), returned_mark)
    down_far, down_near = split_product(held_out, held_hidden, shard, shards)
    held_rows, held_gate_up = after((expert_rows, grad_gate_up_rows), returned_mark)
    gate_up_far, gate_up_near = split_product(held_rows, held_gate_up, shard, shards)
    grad_down_sums = pair_sums(down_near, down_far, shard, shards)
    kv_all = jnp.stack(after(kv_blocks, returned_mark))
    tokens_local = from_relative(after(token_blocks, returned_mark), z).reshape(local_rows, width)
    factor_local = root(tokens_local.astype(F32))
    ride_rows = jnp.concatenate([normed_two, jnp.ones((16, width), BF)], axis=0)
    product_rows = jnp.concatenate([tokens_local, ride_rows], axis=0)

    grad_gate_up_sums = pair_sums(gate_up_near, gate_up_far, shard, shards)
    grad_down_shard = total_of(send_chips(grad_down_sums, shards)).astype(BF)
    grad_returned = after(grad_returned, grad_down_shard, product_rows)
    grad_normed_two = dot(dispatch, grad_returned) + dot_nt(grad_logits, router_full)
    grad_residual = grad_mixed + root_back(residual, factor_two, grad_normed_two)
    grad_branch = grad_residual.astype(BF)
    grad_attended = dot_nt(after(grad_branch, grad_gate_up_sums), out_full).astype(BF)
    head_grad = lax.all_to_all(grad_attended, "seq", split_axis=1, concat_axis=0, tiled=True)
    grad_gate_up_blocks = send_chips(grad_gate_up_sums, shards)
    grad_down = lax.all_gather(grad_down_shard, "seq", axis=0, tiled=False)

    grad_q, near, far = [], [], []
    held = after(head_grad, grad_attended)
    for g in range(local_kv):
        part_q, near_kv, far_kv = flash_backward(
            head_queries, kv_all, bias, held, exact, lse, seqs, rows, g, groups
        )
        grad_q.append(part_q)
        near.append(near_kv)
        far.append(far_kv)
        held = after(head_grad, part_q)
    grad_gate_up_blocks = after(grad_gate_up_blocks, grad_down, part_q)
    grad_gate_up_shard = total_of(grad_gate_up_blocks).astype(BF)
    grad_gate_up_all = lax.all_gather(grad_gate_up_shard, "seq", axis=0, tiled=False)
    grad_q, near, far = after((grad_q, near, far), grad_gate_up_shard)
    grad_down = after(grad_down, part_q)
    grad_q = jnp.concatenate(grad_q, axis=1)
    near = jnp.concatenate(near, axis=2)
    far = jnp.concatenate(far, axis=2)
    there = hop(far, shards, 1)
    pairs = [near[m].astype(F32) + there[m].astype(F32) for m in range(shards // 2)]
    pairs = [pairs[0]] + [each.astype(BF) for each in pairs[1:]]
    out_far, out_near = split_product(
        after(grad_branch, grad_gate_up_shard), attended, shard, shards
    )
    out_sums = pair_sums(out_near, after(out_far, pairs), shard, shards)
    out_blocks = send_chips(out_sums, shards)
    grad_kv = total_of(after(send_chips(pairs, shards), out_sums))
    grad_heads = jnp.concatenate([grad_q, grad_kv], axis=1)
    token_grads = lax.all_to_all(
        grad_heads.astype(BF), "seq", split_axis=0, concat_axis=1, tiled=True
    )

    high, low = two_parts(squares)
    lane = jnp.arange(LANES, dtype=jnp.int32)[None, :]
    marks = jnp.where(lane == experts + 2 * (shard % 2), high, 0) + jnp.where(
        lane == experts + 1 + 2 * (shard % 2), low, 0
    )
    ride_columns = jnp.concatenate(
        [grad_logits, marks.astype(BF), jnp.zeros((15, LANES), BF)], axis=0
    )
    head_cols = q_cols + kv_cols
    product_columns = jnp.concatenate(
        [
            jnp.pad((grad_heads * factor_local).astype(BF), ((0, 0), (0, LANES))),
            jnp.pad(ride_columns, ((0, 0), (head_cols, 0))),
        ],
        axis=0,
    )
    head_far, head_near = split_product(product_rows, product_columns, shard, shards)
    head_sums = pair_sums(head_near, head_far, shard, shards)
    out_part = total_of(after(out_blocks, head_sums)).astype(BF)
    out_parts = lax.all_to_all(
        out_part.reshape(part, seqs, q_cols), "seq", split_axis=1, concat_axis=1, tiled=True
    )
    grad_normed = dot_nt(token_grads, attn_full)
    grad_tokens = grad_residual + root_back(inputs, root(inputs), grad_normed)
    head_part = total_of(send_chips(head_sums, shards))
    base_cols = head_cols + experts
    plane_high, plane_low = two_parts(
        jnp.sum(head_part[:1, base_cols : base_cols + 4], axis=1, keepdims=True)
    )
    lanes = lax.broadcasted_iota(jnp.int32, head_part.shape, 1)
    head_part = jnp.where(
        lanes == base_cols,
        plane_high.astype(F32),
        jnp.where(lanes == base_cols + 1, plane_low.astype(F32), head_part),
    )
    out_own = jnp.sum(out_parts.astype(F32), axis=1)
    final_part = by_rows(jnp.concatenate([head_part, out_own], axis=1).astype(BF))
    final_blocks = [by_rows(each) for each in send_out([final_part] * seqs, seqs)]
    grad_gate_up, grad_gain_ffn = place_gate_up(
        after(grad_gate_up_all, final_part), w_gate_up, gain_two
    )
    final_blocks = after(final_blocks, grad_gate_up)
    sums = sum(each[:, head_cols : head_cols + LANES].astype(F32) for each in final_blocks)
    loss_value = jnp.sum(sums[0, experts : experts + 2]) / (width * valid_count)
    grad_router_base = sums[:, :experts]

    gain_parts = []

    def end_query(block, column):
        gain_parts.append(jnp.sum(columns_of(w_query, column, q_cols) * block, axis=1))
        return block * gain_one

    def end_keyval(block, column):
        gain_parts.append(jnp.sum(columns_of(w_keyval, column, kv_cols) * block, axis=1))
        return block * gain_one

    grad_query = place_columns([each[:, :q_cols] for each in final_blocks], z, end_query)
    grad_keyval = place_columns([each[:, q_cols:head_cols] for each in final_blocks], z, end_keyval)
    grad_out = place_columns(
        [each[:, head_cols + LANES :] for each in final_blocks], z, lambda block, column: block
    ).T
    grad_gain_attn = sum(gain_parts)
    grad_down = (
        after(grad_down, final_part).reshape(experts, split, part, piece)
        .transpose(0, 1, 3, 2)
        .reshape(experts, units, part)
        .astype(F32)
    )
    grad_gain_ffn = grad_gain_ffn + jnp.sum(w_router.astype(F32) * grad_router_base, axis=1)
    return (
        mixed_exact.astype(BF),
        loss_value,
        grad_tokens,
        grad_gain_attn,
        grad_query,
        grad_keyval,
        grad_out,
        grad_gain_ffn,
        grad_router_base * gain_two,
        grad_gate_up,
        grad_down,
    )


def solution(mesh):
    return jax.shard_map(
        local,
        mesh=mesh,
        in_specs=(
            P(("seq", "fsdp"), None),
            P(("seq", "fsdp"), None),
            P(("seq", "fsdp")),
            P(("seq", "fsdp"), None),
            P(("seq", "fsdp"), None),
            P("fsdp"),
            P("fsdp", None),
            P("fsdp", None),
            P(None, "fsdp"),
            P("fsdp"),
            P("fsdp", None),
            P(None, "fsdp", None),
            P(None, None, "fsdp"),
        ),
        out_specs=(
            P(("seq", "fsdp"), None),
            P(),
            P(("seq", "fsdp"), None),
            P("fsdp"),
            P("fsdp", None),
            P("fsdp", None),
            P(None, "fsdp"),
            P("fsdp"),
            P("fsdp", None),
            P(None, "fsdp", None),
            P(None, None, "fsdp"),
        ),
        check_vma=False,
    )
```

```python
import functools
import math

import jax
import jax.numpy as jnp
from jax import lax
from jax.experimental import pallas as pl
from jax.experimental.layout import Layout, with_layout_constraint
from jax.experimental.pallas import tpu as pltpu
from jax.sharding import PartitionSpec as P

HEADS = 24
KVH = 8
HD = 64
CAP = 96
LANES = 128
EPSILON = 1e-06
FLOOR_SCORE = -1e30
BF = jnp.bfloat16
F32 = jnp.float32


def dot(a, b):
    return jnp.dot(a, b, preferred_element_type=F32)


def dot_nt(a, b):
    return lax.dot_general(a, b, (((1,), (1,)), ((), ())), preferred_element_type=F32)


def dot_tn(a, b):
    return lax.dot_general(a, b, (((0,), (0,)), ((), ())), preferred_element_type=F32)


def own_mask(valid_row, rows):
    i = lax.broadcasted_iota(jnp.int32, (rows, rows), 0)
    j = lax.broadcasted_iota(jnp.int32, (rows, rows), 1)
    return jnp.where(j == i, 0.0, jnp.where(j < i, valid_row, FLOOR_SCORE))


def key_chunk(kv_refs, zk, rows, g):
    return jnp.concatenate(
        [ref[pl.ds(zk * rows, rows), pl.ds(g * 2 * HD, 2 * HD)] for ref in kv_refs], axis=0
    )


def forward_kernel(shards, seqs, rows, local_kv, groups, *refs):
    kv_refs = refs[:shards]
    q_ref, bias_ref, low_ref, exact_ref, lse_ref, acc_ref, max_ref = refs[shards:]
    zq = pl.program_id(0)
    stack = groups * rows
    zeros = jnp.zeros((rows, HD), BF)
    half = lax.broadcasted_iota(jnp.int32, (1, 2 * HD), 1) < HD

    def queries(g):
        parts = []
        for h in range(groups):
            start = (g * groups + h) * HD
            parts.append(jnp.concatenate([q_ref[:, start : start + HD], zeros], axis=1))
        return jnp.concatenate(parts, axis=0)

    def chunk(g, zk, scores):
        first = scores is None
        keys = key_chunk(kv_refs, zk, rows, g)
        raw = dot_nt(queries(g), keys)
        if first:
            row = bias_ref[seqs + zk]
            mask = own_mask(row[:, :rows], rows)
            mask = jnp.concatenate([mask] * groups, axis=0)
            masked = jnp.concatenate([raw[:, :rows] + mask, raw[:, rows:] + row[:, rows:]], axis=1)
            new_max = jnp.max(masked, axis=1, keepdims=True)
        else:
            masked = raw + bias_ref[zk]
            new_max = jnp.maximum(max_ref[g][:, :1], jnp.max(masked, axis=1, keepdims=True))
        terms = jnp.exp(masked - new_max).astype(BF)
        ones_values = jnp.where(half, jnp.ones_like(keys), keys)
        part = dot(terms, ones_values)
        if first:
            acc_ref[g] = part
        else:
            acc_ref[g] = acc_ref[g] * jnp.exp(max_ref[g][:, :1] - new_max) + part
        max_ref[g] = jnp.broadcast_to(new_max, (stack, 2 * HD))

    for g in range(local_kv):
        chunk(g, zq, None)

    @pl.loop(0, zq)
    def _(zk):
        for g in range(local_kv):
            chunk(g, zk, True)

    exact_parts, lse_parts = [], []
    for g in range(local_kv):
        acc = acc_ref[g]
        total = acc[:, :HD]
        exact = acc[:, HD:] / total
        lse = max_ref[g][:, :HD] + jnp.log(total)
        for h in range(groups):
            exact_parts.append(exact[h * rows : (h + 1) * rows])
            lse_parts.append(lse[h * rows : (h + 1) * rows])
    exact = jnp.concatenate(exact_parts, axis=1)
    exact_ref[...] = exact
    low_ref[...] = exact.astype(BF)
    lse_ref[...] = jnp.concatenate(lse_parts, axis=1)


def flash_forward(q, kv_blocks, bias, seqs, rows, local_kv, groups):
    shards = len(kv_blocks)
    q_cols = q.shape[1]
    kv_spec = pl.BlockSpec(kv_blocks[0].shape, lambda i: (0, 0))
    q_spec = pl.BlockSpec((rows, q_cols), lambda i: (i, 0))
    stack = groups * rows
    out = jax.ShapeDtypeStruct((seqs * rows, q_cols), F32)
    return pl.pallas_call(
        functools.partial(forward_kernel, shards, seqs, rows, local_kv, groups),
        grid=(seqs,),
        in_specs=[kv_spec] * shards + [q_spec, pl.BlockSpec(bias.shape, lambda i: (0, 0, 0))],
        out_specs=[q_spec] * 3,
        out_shape=[jax.ShapeDtypeStruct((seqs * rows, q_cols), BF), out, out],
        scratch_shapes=[
            pltpu.VMEM((local_kv, stack, 2 * HD), F32),
            pltpu.VMEM((local_kv, stack, 2 * HD), F32),
        ],
        compiler_params=pltpu.CompilerParams(vmem_limit_bytes=24 * 1024 * 1024),
        cost_estimate=pl.CostEstimate(
            flops=0,
            bytes_accessed=0,
            transcendentals=0,
        ),
    )(*kv_blocks, q, bias)


def backward_kernel(shards, seqs, rows, g, groups, *refs):
    kv_refs = [refs[0].at[p] for p in range(shards)]
    (
        q_ref, bias_ref, grad_ref, exact_ref, lse_ref, grad_q_ref, near_ref, far_ref,
        pair_ref, pair_t_ref, lse_wide, delta_wide, acc_q, acc_kv,
    ) = refs[1:]
    zk = pl.program_id(0)
    stack = groups * rows
    zeros = jnp.zeros((rows, HD), BF)

    @pl.when(zk == 0)
    def _():
        acc_q[...] = jnp.zeros_like(acc_q)

        @pl.loop(0, seqs)
        def _(zq):
            here = pl.ds(zq * rows, rows)
            tops, bottoms = [], []
            for h in range(groups):
                cols = slice((g * groups + h) * HD, (g * groups + h + 1) * HD)
                grad = grad_ref[here, cols]
                tops.append(jnp.concatenate([q_ref[here, cols], zeros], axis=1))
                bottoms.append(jnp.concatenate([zeros, grad], axis=1))
                delta = jnp.sum(grad.astype(F32) * exact_ref[here, cols], axis=1, keepdims=True)
                part = slice(h * rows, (h + 1) * rows)
                delta_wide[zq, part] = jnp.broadcast_to(delta, (rows, 2 * HD))
                lse_wide[zq, part] = jnp.broadcast_to(lse_ref[here, cols][:, :1], (rows, 2 * HD))
            pair = jnp.concatenate(tops + bottoms, axis=0)
            pair_ref[zq] = pair
            pair_t_ref[zq] = pair.astype(F32).T.astype(BF)

    def chunk(zq, first):
        keys = key_chunk(kv_refs, zk, rows, g)
        both = dot_nt(pair_ref[zq], keys)
        raw, products = both[:stack], both[stack:]
        if first:
            row = bias_ref[seqs + zk]
            mask = own_mask(row[:, :rows], rows)
            mask = jnp.concatenate([mask] * groups, axis=0)
            masked = jnp.concatenate([raw[:, :rows] + mask, raw[:, rows:] + row[:, rows:]], axis=1)
        else:
            masked = raw + bias_ref[zk]
        weights = jnp.exp(masked - lse_wide[zq][:, :1])
        grads = (weights * (products - delta_wide[zq][:, :1])).astype(BF)
        acc_q[zq] += dot(grads, keys)
        part = dot(pair_t_ref[zq], jnp.concatenate([grads, weights.astype(BF)], axis=0))
        if first:
            acc_kv[...] = part
        else:
            acc_kv[...] += part

    chunk(zk, True)

    @pl.loop(zk + 1, seqs)
    def _(zq):
        chunk(zq, False)

    for p in range(shards):
        target = near_ref if p < shards // 2 else far_ref
        target[p % (shards // 2)] = acc_kv[:, p * rows : (p + 1) * rows].T.astype(BF)

    @pl.when(zk == seqs - 1)
    def _():
        @pl.loop(0, seqs)
        def _(zq):
            total = acc_q[zq]
            parts = [total[h * rows : (h + 1) * rows, :HD] for h in range(groups)]
            grad_q_ref[pl.ds(zq * rows, rows), :] = jnp.concatenate(parts, axis=1) * HD ** (-0.5)


def flash_backward(q, kv_all, bias, grad, exact, lse, seqs, rows, g, groups):
    shards = kv_all.shape[0]
    q_cols = q.shape[1]
    stack = groups * rows
    kv_spec = pl.BlockSpec(kv_all.shape, lambda i: (0, 0, 0))
    whole = pl.BlockSpec((seqs * rows, q_cols), lambda i: (0, 0))
    grad_q_shape = (seqs * rows, groups * HD)
    out_spec = pl.BlockSpec((shards // 2, rows, 2 * HD), lambda i: (0, i, 0))
    out = jax.ShapeDtypeStruct((shards // 2, seqs * rows, 2 * HD), BF)
    return pl.pallas_call(
        functools.partial(backward_kernel, shards, seqs, rows, g, groups),
        grid=(seqs,),
        in_specs=[kv_spec]
        + [whole, pl.BlockSpec(bias.shape, lambda i: (0, 0, 0)), whole, whole, whole],
        out_specs=[pl.BlockSpec(grad_q_shape, lambda i: (0, 0)), out_spec, out_spec],
        out_shape=[jax.ShapeDtypeStruct(grad_q_shape, F32), out, out],
        scratch_shapes=[
            pltpu.VMEM((seqs, 2 * stack, 2 * HD), BF),
            pltpu.VMEM((seqs, 2 * HD, 2 * stack), BF),
            pltpu.VMEM((seqs, stack, 2 * HD), F32),
            pltpu.VMEM((seqs, stack, 2 * HD), F32),
            pltpu.VMEM((seqs, stack, 2 * HD), F32),
            pltpu.VMEM((2 * HD, shards * rows), F32),
        ],
        compiler_params=pltpu.CompilerParams(vmem_limit_bytes=28 * 1024 * 1024),
        cost_estimate=pl.CostEstimate(
            flops=0,
            bytes_accessed=0,
            transcendentals=0,
        ),
    )(kv_all, q, bias, grad, exact, lse)


def shift(block, count, step):
    return lax.ppermute(block, "seq", [(i, (i + step) % count) for i in range(count)])


def send_out(blocks, count):
    return [blocks[0]] + [shift(blocks[s], count, s) for s in range(1, count)]


def send_back(blocks, count):
    return [blocks[0]] + [shift(blocks[s], count, count - s) for s in range(1, count)]


def from_relative(blocks, place):
    count = len(blocks)
    rising = jnp.stack([blocks[-s % count] for s in range(count)])
    return lax.dynamic_slice_in_dim(jnp.concatenate([rising, rising]), count - place, count, 0)


def hop(block, count, mask):
    return lax.ppermute(block, "fsdp", [(i, i ^ mask) for i in range(count)])


def gather_shards(block, count):
    near = [block] + [hop(block, count, 2 * m) for m in range(1, count // 2)]
    return near + [hop(each, count, 1) for each in near]


def send_chips(parts, count):
    return [parts[0]] + [hop(parts[m], count, 2 * m) for m in range(1, count // 2)]


def total_of(blocks):
    total = blocks[0].astype(F32)
    for each in blocks[1:]:
        total = total + each.astype(F32)
    return total


def take(array, index, axis):
    return lax.dynamic_index_in_dim(array, index, axis, keepdims=False)


def product_kernel(core_ref, lhs_ref, rhs_ref, far_ref, near_ref):
    part = lhs_ref.shape[1] // 2
    rhs = rhs_ref[...]
    first = dot_tn(lhs_ref[:, :part], rhs).astype(BF)
    second = dot_tn(lhs_ref[:, part:], rhs).astype(BF)
    core = core_ref[0]

    @pl.when(core == 0)
    def _():
        near_ref[0] = first
        far_ref[0] = second

    @pl.when(core != 0)
    def _():
        near_ref[0] = second
        far_ref[0] = first


def split_product(lhs, rhs, shard, count):
    tokens, width = lhs.shape
    cols = rhs.shape[1]
    part = width // count
    if 2 * part % LANES:
        cut = dot_tn(lhs, rhs).astype(BF).reshape(count // 2, 2, part, cols)
        return take(cut, 1 - shard % 2, 1), take(cut, shard % 2, 1)
    out = jax.ShapeDtypeStruct((count // 2, part, cols), BF)
    out_spec = pl.BlockSpec((1, part, cols), lambda i: (i, 0, 0))
    return pl.pallas_call(
        product_kernel,
        grid=(count // 2,),
        in_specs=[
            pl.BlockSpec(memory_space=pltpu.SMEM),
            pl.BlockSpec((tokens, 2 * part), lambda i: (0, i)),
            pl.BlockSpec((tokens, cols), lambda i: (0, 0)),
        ],
        out_specs=[out_spec, out_spec],
        out_shape=[out, out],
        compiler_params=pltpu.CompilerParams(vmem_limit_bytes=24 * 1024 * 1024),
        cost_estimate=pl.CostEstimate(flops=0, bytes_accessed=0, transcendentals=0),
    )((shard % 2).astype(jnp.int32).reshape(1), lhs, rhs)


def pair_kernel(chip_ref, near_ref, there_ref, own_ref, *part_refs):
    chip = chip_ref[0]
    own_ref[...] = near_ref[chip].astype(F32) + there_ref[chip].astype(F32)
    for m, part_ref in enumerate(part_refs):
        which = chip ^ (m + 1)
        part_ref[...] = (near_ref[which].astype(F32) + there_ref[which].astype(F32)).astype(BF)


def pair_sums(near, far, shard, count):
    there = hop(far, count, 1)
    chips, part, cols = near.shape
    tile = math.gcd(cols, 512)
    if tile % LANES:
        tile = cols
    block = pl.BlockSpec((chips, part, tile), lambda i: (0, 0, i))
    out_spec = pl.BlockSpec((part, tile), lambda i: (0, i))
    out = jax.ShapeDtypeStruct((part, cols), BF)
    return pl.pallas_call(
        pair_kernel,
        grid=(cols // tile,),
        in_specs=[pl.BlockSpec(memory_space=pltpu.SMEM), block, block],
        out_specs=[out_spec] * chips,
        out_shape=[jax.ShapeDtypeStruct((part, cols), F32)] + [out] * (chips - 1),
        compiler_params=pltpu.CompilerParams(vmem_limit_bytes=24 * 1024 * 1024),
        cost_estimate=pl.CostEstimate(flops=0, bytes_accessed=0, transcendentals=0),
    )((shard // 2).astype(jnp.int32).reshape(1), near, there)


def two_parts(value):
    high = value.astype(BF)
    return high, (value - high.astype(F32)).astype(BF)


def mark_kernel(seed_ref, out_ref):
    out_ref[...] = seed_ref[...]


def mark(*others):
    seed = after(jnp.zeros((8, LANES), F32), *others)
    return pl.pallas_call(
        mark_kernel,
        out_shape=jax.ShapeDtypeStruct((8, LANES), F32),
        cost_estimate=pl.CostEstimate(flops=10**12, bytes_accessed=8192, transcendentals=0),
    )(seed)


def by_rows(array):
    return with_layout_constraint(array, Layout(major_to_minor=tuple(range(array.ndim))))


def after(values, *others):
    return lax.optimization_barrier((values, others))[0]


def root(values):
    return lax.rsqrt(jnp.mean(values * values, axis=-1, keepdims=True) + EPSILON)


def root_back(values, factor, grad_scaled):
    inner = jnp.mean(grad_scaled * values, axis=-1, keepdims=True)
    return factor * grad_scaled - values * (factor * factor * factor * inner)


def place_gate_up(base, weight, gain):
    experts, part, both = weight.shape
    split = base.shape[0] // experts
    base = base.astype(F32)
    if split > 1:
        base = (
            base.reshape(experts, split, part, 2, both // (2 * split))
            .transpose(0, 2, 3, 1, 4)
            .reshape(experts, part, both)
        )
    return base * gain, jnp.sum(weight.astype(F32) * base, axis=(0, 2))


def place_kernel(count, q_cols, kv_cols, place_ref, *refs):
    blocks = refs[:count]
    w_query_ref, w_keyval_ref, gain_ref, query_ref, keyval_ref, out_ref, base_ref, sums_ref = refs[
        count:
    ]
    gain = gain_ref[...]
    base = jnp.zeros_like(gain)
    sums = jnp.zeros(sums_ref.shape, F32)
    for s in range(count):
        owner = lax.rem(place_ref[0] + (count - s), count)
        q_at = pl.ds(pl.multiple_of(owner * q_cols, LANES), q_cols)
        kv_at = pl.ds(pl.multiple_of(owner * kv_cols, LANES), kv_cols)
        query = blocks[s][:, :q_cols].astype(F32)
        keyval = blocks[s][:, q_cols : q_cols + kv_cols].astype(F32)
        start = q_cols + kv_cols
        sums = sums + blocks[s][:, start : start + LANES].astype(F32)
        out_ref[:, q_at] = blocks[s][:, start + LANES :].astype(F32)
        base = base + jnp.sum(w_query_ref[:, q_at].astype(F32) * query, axis=1, keepdims=True)
        base = base + jnp.sum(w_keyval_ref[:, kv_at].astype(F32) * keyval, axis=1, keepdims=True)
        query_ref[:, q_at] = query * gain
        keyval_ref[:, kv_at] = keyval * gain
    base_ref[...] = jnp.broadcast_to(base, base_ref.shape)
    sums_ref[...] = sums


def place_heads(blocks, place, w_query, w_keyval, gain, q_cols, kv_cols):
    count = len(blocks)
    part = w_query.shape[0]
    start = q_cols + kv_cols
    if q_cols % LANES == 0 and kv_cols % LANES == 0:
        wide = jax.ShapeDtypeStruct((part, count * q_cols), F32)
        narrow = jax.ShapeDtypeStruct((part, count * kv_cols), F32)
        lanes = jax.ShapeDtypeStruct((part, LANES), F32)
        in_vmem = pl.BlockSpec(memory_space=pltpu.VMEM)
        query, keyval, out, base, sums = pl.pallas_call(
            functools.partial(place_kernel, count, q_cols, kv_cols),
            in_specs=[pl.BlockSpec(memory_space=pltpu.SMEM)] + [in_vmem] * (count + 3),
            out_specs=[in_vmem] * 5,
            out_shape=[wide, narrow, wide, lanes, lanes],
            compiler_params=pltpu.CompilerParams(vmem_limit_bytes=24 * 1024 * 1024),
            cost_estimate=pl.CostEstimate(flops=0, bytes_accessed=0, transcendentals=0),
        )(place.astype(jnp.int32).reshape(1), *blocks, w_query, w_keyval, gain)
        return query, keyval, out, base[:, 0], sums
    blocks = from_relative(blocks, place).astype(F32)

    def columns(begin, end):
        return blocks[:, :, begin:end].transpose(1, 0, 2).reshape(part, count * (end - begin))

    query, keyval = columns(0, q_cols), columns(q_cols, start)
    base = jnp.sum(w_query.astype(F32) * query, axis=1) + jnp.sum(
        w_keyval.astype(F32) * keyval, axis=1
    )
    sums = jnp.sum(blocks[:, :, start : start + LANES], axis=0)
    out = columns(start + LANES, start + LANES + q_cols)
    return query * gain, keyval * gain, out, base, sums


def local(
    tokens,
    teacher,
    valid,
    routes,
    slots,
    gain_attn,
    w_query,
    w_keyval,
    w_out,
    gain_ffn,
    w_router,
    w_gate_up,
    w_down,
):
    seqs = lax.axis_size("seq")
    shards = lax.axis_size("fsdp")
    z = lax.axis_index("seq")
    shard = lax.axis_index("fsdp")
    rows, width = tokens.shape
    groups = HEADS // KVH
    local_kv = KVH // seqs
    q_cols = local_kv * groups * HD
    kv_cols = local_kv * 2 * HD
    local_rows = rows * seqs
    seq_len = local_rows * shards
    experts, part, both = w_gate_up.shape
    units = both // 2
    split = seqs // experts
    piece = units // split
    expert = z // split
    fraction = z % split
    scale = HD ** (-0.5)

    gain_one = gain_attn.astype(F32)[:, None]
    gain_two = gain_ffn.astype(F32)[:, None]
    heads_shard = jnp.concatenate(
        [
            lax.dynamic_slice_in_dim(w_query, z * q_cols, q_cols, 1),
            lax.dynamic_slice_in_dim(w_keyval, z * kv_cols, kv_cols, 1),
        ],
        axis=1,
    )
    heads_shard = (heads_shard.astype(F32) * gain_one).astype(BF)
    heads_full = lax.all_gather(heads_shard, "fsdp", axis=0, tiled=True)
    valid_row = jnp.pad(valid.astype(BF).reshape(1, rows), ((0, 7), (0, width - rows)))
    token_rows = jnp.concatenate([tokens, valid_row], axis=0)
    token_mark = mark(token_rows)
    token_blocks = after(send_out([token_rows] * seqs, seqs), token_mark)

    valid_local = from_relative([each[rows : rows + 1, :rows] for each in token_blocks], z)
    token_blocks = [each[:rows] for each in token_blocks]
    projected = []
    for block in token_blocks:
        projected.append(dot(block, heads_full) * root(block.astype(F32)))
    projected = from_relative([each.astype(BF) for each in projected], z)
    projected = projected.reshape(local_rows, q_cols + kv_cols)
    head_queries = projected[:, :q_cols] * jnp.asarray(scale, BF)

    valid_rows_kv = local_rows // kv_cols
    payload = jnp.concatenate(
        [
            projected[:, q_cols:],
            valid_local.reshape(valid_rows_kv, kv_cols),
            jnp.zeros((16 - valid_rows_kv, kv_cols), BF),
        ],
        axis=0,
    )
    kv_blocks = gather_shards(payload, shards)
    late_query, late_keyval, late_router, late_gate_up, late_down = after(
        (w_query, w_keyval, w_router, w_gate_up, w_down), token_mark
    )
    out_full = lax.all_gather(w_out, "fsdp", axis=1, tiled=True)
    own_expert = take(late_gate_up, expert, 0)
    gate_shard = lax.dynamic_slice_in_dim(own_expert, fraction * piece, piece, 1)
    up_shard = lax.dynamic_slice_in_dim(own_expert, units + fraction * piece, piece, 1)
    down_shard = lax.dynamic_slice_in_dim(take(late_down, expert, 0), fraction * piece, piece, 0).T
    router_shard = jnp.pad((late_router.astype(F32) * gain_two).astype(BF), ((0, 0), (0, LANES - experts)))
    expert_shard = jnp.concatenate(
        [
            (gate_shard.astype(F32) * gain_two).astype(BF),
            (up_shard.astype(F32) * gain_two).astype(BF),
            down_shard,
            router_shard,
        ],
        axis=1,
    )
    expert_full = lax.all_gather(expert_shard, "fsdp", axis=0, tiled=True)
    gate_up_full = expert_full[:, : 2 * piece]
    down_full = expert_full[:, 2 * piece : 3 * piece]
    router_full = expert_full[:, 3 * piece :]
    attn_shard = jnp.concatenate(
        [
            each
            for s in range(seqs)
            for each in (
                late_query[:, s * q_cols : (s + 1) * q_cols],
                late_keyval[:, s * kv_cols : (s + 1) * kv_cols],
            )
        ],
        axis=1,
    )
    attn_full = lax.all_gather(
        (attn_shard.astype(F32) * gain_one).astype(BF), "fsdp", axis=0, tiled=True
    )
    order = jnp.asarray(
        [2 * m for m in range(shards // 2)] + [2 * m + 1 for m in range(shards // 2)], jnp.int32
    )
    valid_all = jnp.stack(
        [
            each[local_rows : local_rows + valid_rows_kv].reshape(seqs, rows)
            for each in kv_blocks
        ],
        axis=1,
    ).astype(F32)
    valid_count = jnp.sum(valid_all)
    bias = jnp.where(valid_all > 0, 0.0, FLOOR_SCORE)
    earlier = ((order ^ shard) < shard) | (order == 0)
    bias_same = jnp.where(earlier[None, :, None], bias, FLOOR_SCORE)
    bias = jnp.concatenate([bias, bias_same]).reshape(2 * seqs, 1, shards * rows)
    attended_low, exact, lse = flash_forward(
        head_queries, kv_blocks, bias, seqs, rows, local_kv, groups
    )
    attended = lax.all_to_all(attended_low, "seq", split_axis=0, concat_axis=1, tiled=True)

    inputs = tokens.astype(F32)
    residual = inputs + dot(attended, out_full)
    factor_two = root(residual)
    normed_two = (residual * factor_two).astype(BF)
    logits = dot(normed_two, router_full)[:, :experts]
    expert_ids = jnp.arange(experts, dtype=jnp.int32)
    picked = (routes[:, :, None] == expert_ids).astype(F32)
    chosen = jnp.sum(picked * logits[:, None, :], axis=-1)
    gating = jax.nn.softmax(chosen, axis=-1)
    owners = ((jnp.arange(seqs, dtype=jnp.int32) + z) % seqs) // split
    to_owner = routes[:, :, None] == owners
    slot_hot = slots[:, :, None] == jnp.arange(CAP, dtype=jnp.int32)
    placed = (to_owner[:, :, :, None] & slot_hot[:, :, None, :]).astype(BF)
    placed = placed.reshape(rows, 2, seqs * CAP)
    dispatch = placed[:, 0] + placed[:, 1]
    placed_pairs = jnp.concatenate([placed[:, 0], placed[:, 1]], axis=0)
    sent_rows = dot_tn(dispatch, normed_two).astype(BF)
    sent_rows = sent_rows.reshape(seqs, CAP, width)
    expert_rows = jnp.concatenate(send_out([sent_rows[s] for s in range(seqs)], seqs))
    gate_up = dot(expert_rows, gate_up_full)
    gate_part = gate_up[:, :piece]
    up_part = gate_up[:, piece:]
    sigmoid_gate = jax.nn.sigmoid(gate_part)
    hidden = (gate_part * sigmoid_gate * up_part).astype(BF)
    expert_out = dot_nt(hidden, down_full).astype(BF)
    expert_out = expert_out.reshape(seqs, CAP, width)
    returned = jnp.concatenate(send_back([expert_out[s] for s in range(seqs)], seqs))
    selected = dot(placed_pairs, returned).reshape(2, rows, width)
    mixed_exact = residual + gating[:, :1] * selected[0] + gating[:, 1:] * selected[1]
    valid_rows = valid.astype(F32)
    errors = (mixed_exact - teacher.astype(F32)) * valid_rows[:, None]
    squares = jnp.sum(errors * errors)
    loss_scale = width * seq_len // 8
    grad_mixed = errors * (2.0 * loss_scale / (width * valid_count))

    grad_gating = jnp.stack(
        [jnp.sum(selected[0] * grad_mixed, axis=-1), jnp.sum(selected[1] * grad_mixed, axis=-1)],
        axis=1,
    )
    grad_chosen = gating * (grad_gating - jnp.sum(gating * grad_gating, axis=-1, keepdims=True))
    grad_logits = jnp.sum(grad_chosen[:, :, None] * picked, axis=1).astype(BF)
    grad_logits = jnp.pad(grad_logits, ((0, 0), (0, LANES - experts)))
    weighted = jnp.concatenate(
        [(gating[:, :1] * grad_mixed).astype(BF), (gating[:, 1:] * grad_mixed).astype(BF)], axis=0
    )
    sent_grads = dot_tn(placed_pairs, weighted).astype(BF).reshape(seqs, CAP, width)
    grad_expert_out = jnp.concatenate(send_out([sent_grads[s] for s in range(seqs)], seqs))
    grad_expert_out = after(grad_expert_out, attn_full)
    grad_hidden = dot(grad_expert_out, down_full)
    grad_gate = grad_hidden * up_part * sigmoid_gate * (1.0 + gate_part * (1.0 - sigmoid_gate))
    grad_up = grad_hidden * gate_part * sigmoid_gate
    grad_gate_up_rows = jnp.concatenate([grad_gate, grad_up], axis=-1).astype(BF)
    grad_rows = dot_nt(grad_gate_up_rows, gate_up_full).astype(BF)
    returned_mark = grad_rows
    grad_rows = grad_rows.reshape(seqs, CAP, width)
    grad_returned = send_back([grad_rows[s] for s in range(seqs)], seqs)
    grad_returned = jnp.concatenate(grad_returned)
    held_out, held_hidden = after((grad_expert_out, hidden), returned_mark)
    down_far, down_near = split_product(held_out, held_hidden, shard, shards)
    held_rows, held_gate_up = after((expert_rows, grad_gate_up_rows), returned_mark)
    gate_up_far, gate_up_near = split_product(held_rows, held_gate_up, shard, shards)
    grad_down_sums = pair_sums(down_near, down_far, shard, shards)
    kv_all = jnp.stack(after(kv_blocks, returned_mark))
    tokens_local = from_relative(after(token_blocks, returned_mark), z).reshape(local_rows, width)
    factor_local = root(tokens_local.astype(F32))
    ride_rows = jnp.concatenate([normed_two, jnp.ones((16, width), BF)], axis=0)
    product_rows = jnp.concatenate([tokens_local, ride_rows], axis=0)

    grad_gate_up_sums = pair_sums(gate_up_near, gate_up_far, shard, shards)
    grad_down_blocks = send_chips(grad_down_sums, shards)
    grad_returned = after(grad_returned, grad_down_sums, product_rows)
    grad_normed_two = dot(dispatch, grad_returned) + dot_nt(grad_logits, router_full)
    grad_residual = grad_mixed + root_back(residual, factor_two, grad_normed_two)
    grad_branch = grad_residual.astype(BF)
    grad_attended = dot_nt(after(grad_branch, grad_gate_up_sums), out_full).astype(BF)
    head_grad = lax.all_to_all(grad_attended, "seq", split_axis=1, concat_axis=0, tiled=True)
    grad_gate_up_blocks = send_chips(grad_gate_up_sums, shards)
    grad_down_shard = total_of(after(grad_down_blocks, head_grad)).astype(BF)
    grad_down = lax.all_gather(grad_down_shard, "seq", axis=0, tiled=False)

    grad_q, near, far = [], [], []
    held = after(head_grad, grad_attended)
    for g in range(local_kv):
        part_q, near_kv, far_kv = flash_backward(
            head_queries, kv_all, bias, held, exact, lse, seqs, rows, g, groups
        )
        grad_q.append(part_q)
        near.append(near_kv)
        far.append(far_kv)
        held = after(head_grad, part_q)
    grad_gate_up_blocks = after(grad_gate_up_blocks, grad_down, part_q)
    grad_gate_up_shard = total_of(grad_gate_up_blocks).astype(BF)
    grad_gate_up_all = lax.all_gather(grad_gate_up_shard, "seq", axis=0, tiled=False)
    grad_q, near, far = after((grad_q, near, far), grad_gate_up_shard)
    grad_down = after(grad_down, part_q)
    grad_q = jnp.concatenate(grad_q, axis=1)
    near = jnp.concatenate(near, axis=2)
    far = jnp.concatenate(far, axis=2)
    there = hop(far, shards, 1)
    pairs = [near[m].astype(F32) + there[m].astype(F32) for m in range(shards // 2)]
    pairs = [pairs[0]] + [each.astype(BF) for each in pairs[1:]]
    out_far, out_near = split_product(
        after(grad_branch, grad_gate_up_shard), attended, shard, shards
    )
    out_sums = pair_sums(out_near, after(out_far, pairs), shard, shards)
    out_blocks = send_chips(out_sums, shards)
    grad_kv = total_of(after(send_chips(pairs, shards), out_sums))
    grad_heads = jnp.concatenate([grad_q, grad_kv], axis=1)
    token_grads = lax.all_to_all(
        grad_heads.astype(BF), "seq", split_axis=0, concat_axis=1, tiled=True
    )

    high, low = two_parts(squares)
    lane = jnp.arange(LANES, dtype=jnp.int32)[None, :]
    marks = jnp.where(lane == experts + 2 * (shard % 2), high, 0) + jnp.where(
        lane == experts + 1 + 2 * (shard % 2), low, 0
    )
    ride_columns = jnp.concatenate(
        [grad_logits, marks.astype(BF), jnp.zeros((15, LANES), BF)], axis=0
    )
    head_cols = q_cols + kv_cols
    product_columns = jnp.concatenate(
        [
            jnp.pad((grad_heads * factor_local).astype(BF), ((0, 0), (0, LANES))),
            jnp.pad(ride_columns, ((0, 0), (head_cols, 0))),
        ],
        axis=0,
    )
    head_far, head_near = split_product(product_rows, product_columns, shard, shards)
    head_sums = pair_sums(head_near, head_far, shard, shards)
    out_part = total_of(after(out_blocks, head_sums)).astype(BF)
    out_parts = lax.all_to_all(
        out_part.reshape(part, seqs, q_cols), "seq", split_axis=1, concat_axis=1, tiled=True
    )
    head_part = total_of(send_chips(head_sums, shards))
    grad_normed = dot_nt(after(token_grads, head_part), attn_full)
    grad_tokens = grad_residual + root_back(inputs, root(inputs), grad_normed)
    base_cols = head_cols + experts
    plane_high, plane_low = two_parts(
        jnp.sum(head_part[:1, base_cols : base_cols + 4], axis=1, keepdims=True)
    )
    lanes = lax.broadcasted_iota(jnp.int32, head_part.shape, 1)
    head_part = jnp.where(
        lanes == base_cols,
        plane_high.astype(F32),
        jnp.where(lanes == base_cols + 1, plane_low.astype(F32), head_part),
    )
    out_own = jnp.sum(out_parts.astype(F32), axis=1)
    final_part = by_rows(jnp.concatenate([head_part, out_own], axis=1).astype(BF))
    final_blocks = [by_rows(each) for each in send_out([final_part] * seqs, seqs)]
    grad_gate_up, grad_gain_ffn = place_gate_up(
        after(grad_gate_up_all, final_part), w_gate_up, gain_two
    )
    final_blocks = after(final_blocks, grad_gate_up)
    grad_query, grad_keyval, grad_out, grad_gain_attn, sums = place_heads(
        final_blocks, z, w_query, w_keyval, gain_one, q_cols, kv_cols
    )
    loss_value = jnp.sum(sums[0, experts : experts + 2]) / (width * valid_count)
    grad_router_base = sums[:, :experts]
    grad_down = (
        after(grad_down, final_part).reshape(experts, split, part, piece)
        .transpose(0, 1, 3, 2)
        .reshape(experts, units, part)
        .astype(F32)
    )
    grad_gain_ffn = grad_gain_ffn + jnp.sum(w_router.astype(F32) * grad_router_base, axis=1)
    return (
        mixed_exact.astype(BF),
        loss_value,
        grad_tokens,
        grad_gain_attn,
        grad_query,
        grad_keyval,
        grad_out.T,
        grad_gain_ffn,
        grad_router_base * gain_two,
        grad_gate_up,
        grad_down,
    )


def solution(mesh):
    return jax.shard_map(
        local,
        mesh=mesh,
        in_specs=(
            P(("seq", "fsdp"), None),
            P(("seq", "fsdp"), None),
            P(("seq", "fsdp")),
            P(("seq", "fsdp"), None),
            P(("seq", "fsdp"), None),
            P("fsdp"),
            P("fsdp", None),
            P("fsdp", None),
            P(None, "fsdp"),
            P("fsdp"),
            P("fsdp", None),
            P(None, "fsdp", None),
            P(None, None, "fsdp"),
        ),
        out_specs=(
            P(("seq", "fsdp"), None),
            P(),
            P(("seq", "fsdp"), None),
            P("fsdp"),
            P("fsdp", None),
            P("fsdp", None),
            P(None, "fsdp"),
            P("fsdp"),
            P("fsdp", None),
            P(None, "fsdp", None),
            P(None, None, "fsdp"),
        ),
        check_vma=False,
    )
```

```python
import functools
import math

import jax
import jax.numpy as jnp
from jax import lax
from jax.experimental import pallas as pl
from jax.experimental.layout import Layout, with_layout_constraint
from jax.experimental.pallas import tpu as pltpu
from jax.sharding import PartitionSpec as P

HEADS = 24
KVH = 8
HD = 64
CAP = 96
LANES = 128
EPSILON = 1e-06
FLOOR_SCORE = -1e30
BF = jnp.bfloat16
F32 = jnp.float32


def dot(a, b):
    return jnp.dot(a, b, preferred_element_type=F32)


def dot_nt(a, b):
    return lax.dot_general(a, b, (((1,), (1,)), ((), ())), preferred_element_type=F32)


def dot_tn(a, b):
    return lax.dot_general(a, b, (((0,), (0,)), ((), ())), preferred_element_type=F32)


def own_mask(valid_row, rows):
    i = lax.broadcasted_iota(jnp.int32, (rows, rows), 0)
    j = lax.broadcasted_iota(jnp.int32, (rows, rows), 1)
    return jnp.where(j == i, 0.0, jnp.where(j < i, valid_row, FLOOR_SCORE))


def key_chunk(kv_refs, zk, rows, g):
    return jnp.concatenate(
        [ref[pl.ds(zk * rows, rows), pl.ds(g * 2 * HD, 2 * HD)] for ref in kv_refs], axis=0
    )


def forward_kernel(shards, seqs, rows, local_kv, groups, *refs):
    kv_refs = refs[:shards]
    q_ref, bias_ref, low_ref, exact_ref, lse_ref, all_ref, acc_ref, max_ref = refs[shards:]
    zq = pl.program_id(0)
    stack = groups * rows
    zeros = jnp.zeros((rows, HD), BF)
    half = lax.broadcasted_iota(jnp.int32, (1, 2 * HD), 1) < HD

    def queries(g):
        parts = []
        for h in range(groups):
            start = (g * groups + h) * HD
            parts.append(jnp.concatenate([q_ref[:, start : start + HD], zeros], axis=1))
        return jnp.concatenate(parts, axis=0)

    def chunk(g, zk, scores):
        first = scores is None
        keys = key_chunk(kv_refs, zk, rows, g)
        raw = dot_nt(queries(g), keys)
        if first:
            row = bias_ref[seqs + zk]
            mask = own_mask(row[:, :rows], rows)
            mask = jnp.concatenate([mask] * groups, axis=0)
            masked = jnp.concatenate([raw[:, :rows] + mask, raw[:, rows:] + row[:, rows:]], axis=1)
            new_max = jnp.max(masked, axis=1, keepdims=True)
        else:
            masked = raw + bias_ref[zk]
            new_max = jnp.maximum(max_ref[g][:, :1], jnp.max(masked, axis=1, keepdims=True))
        terms = jnp.exp(masked - new_max).astype(BF)
        ones_values = jnp.where(half, jnp.ones_like(keys), keys)
        part = dot(terms, ones_values)
        if first:
            acc_ref[g] = part
        else:
            acc_ref[g] = acc_ref[g] * jnp.exp(max_ref[g][:, :1] - new_max) + part
        max_ref[g] = jnp.broadcast_to(new_max, (stack, 2 * HD))

    @pl.when(zq == 0)
    def _():
        for p in range(shards):
            all_ref[p] = kv_refs[p][...]

    for g in range(local_kv):
        chunk(g, zq, None)

    @pl.loop(0, zq)
    def _(zk):
        for g in range(local_kv):
            chunk(g, zk, True)

    exact_parts, lse_parts = [], []
    for g in range(local_kv):
        acc = acc_ref[g]
        total = acc[:, :HD]
        exact = acc[:, HD:] / total
        lse = max_ref[g][:, :HD] + jnp.log(total)
        for h in range(groups):
            exact_parts.append(exact[h * rows : (h + 1) * rows])
            lse_parts.append(lse[h * rows : (h + 1) * rows])
    exact = jnp.concatenate(exact_parts, axis=1)
    exact_ref[...] = exact
    low_ref[...] = exact.astype(BF)
    lse_ref[...] = jnp.concatenate(lse_parts, axis=1)


def flash_forward(q, kv_blocks, bias, seqs, rows, local_kv, groups):
    shards = len(kv_blocks)
    q_cols = q.shape[1]
    kv_spec = pl.BlockSpec(kv_blocks[0].shape, lambda i: (0, 0))
    q_spec = pl.BlockSpec((rows, q_cols), lambda i: (i, 0))
    stack = groups * rows
    all_shape = (shards,) + kv_blocks[0].shape
    out = jax.ShapeDtypeStruct((seqs * rows, q_cols), F32)
    return pl.pallas_call(
        functools.partial(forward_kernel, shards, seqs, rows, local_kv, groups),
        grid=(seqs,),
        in_specs=[kv_spec] * shards + [q_spec, pl.BlockSpec(bias.shape, lambda i: (0, 0, 0))],
        out_specs=[q_spec] * 3 + [pl.BlockSpec(all_shape, lambda i: (0, 0, 0))],
        out_shape=[
            jax.ShapeDtypeStruct((seqs * rows, q_cols), BF),
            out,
            out,
            jax.ShapeDtypeStruct(all_shape, BF),
        ],
        scratch_shapes=[
            pltpu.VMEM((local_kv, stack, 2 * HD), F32),
            pltpu.VMEM((local_kv, stack, 2 * HD), F32),
        ],
        compiler_params=pltpu.CompilerParams(vmem_limit_bytes=24 * 1024 * 1024),
        cost_estimate=pl.CostEstimate(
            flops=0,
            bytes_accessed=0,
            transcendentals=0,
        ),
    )(*kv_blocks, q, bias)


def backward_kernel(shards, seqs, rows, g, groups, *refs):
    kv_refs = [refs[0].at[p] for p in range(shards)]
    (
        q_ref, bias_ref, grad_ref, exact_ref, lse_ref, grad_q_ref, near_ref, far_ref,
        pair_ref, pair_t_ref, lse_wide, delta_wide, acc_q, acc_kv,
    ) = refs[1:]
    zk = pl.program_id(0)
    stack = groups * rows
    zeros = jnp.zeros((rows, HD), BF)

    @pl.when(zk == 0)
    def _():
        acc_q[...] = jnp.zeros_like(acc_q)

        @pl.loop(0, seqs)
        def _(zq):
            here = pl.ds(zq * rows, rows)
            tops, bottoms = [], []
            for h in range(groups):
                cols = slice((g * groups + h) * HD, (g * groups + h + 1) * HD)
                grad = grad_ref[here, cols]
                tops.append(jnp.concatenate([q_ref[here, cols], zeros], axis=1))
                bottoms.append(jnp.concatenate([zeros, grad], axis=1))
                delta = jnp.sum(grad.astype(F32) * exact_ref[here, cols], axis=1, keepdims=True)
                part = slice(h * rows, (h + 1) * rows)
                delta_wide[zq, part] = jnp.broadcast_to(delta, (rows, 2 * HD))
                lse_wide[zq, part] = jnp.broadcast_to(lse_ref[here, cols][:, :1], (rows, 2 * HD))
            pair = jnp.concatenate(tops + bottoms, axis=0)
            pair_ref[zq] = pair
            pair_t_ref[zq] = pair.astype(F32).T.astype(BF)

    def chunk(zq, first):
        keys = key_chunk(kv_refs, zk, rows, g)
        both = dot_nt(pair_ref[zq], keys)
        raw, products = both[:stack], both[stack:]
        if first:
            row = bias_ref[seqs + zk]
            mask = own_mask(row[:, :rows], rows)
            mask = jnp.concatenate([mask] * groups, axis=0)
            masked = jnp.concatenate([raw[:, :rows] + mask, raw[:, rows:] + row[:, rows:]], axis=1)
        else:
            masked = raw + bias_ref[zk]
        weights = jnp.exp(masked - lse_wide[zq][:, :1])
        grads = (weights * (products - delta_wide[zq][:, :1])).astype(BF)
        acc_q[zq] += dot(grads, keys)
        part = dot(pair_t_ref[zq], jnp.concatenate([grads, weights.astype(BF)], axis=0))
        if first:
            acc_kv[...] = part
        else:
            acc_kv[...] += part

    chunk(zk, True)

    @pl.loop(zk + 1, seqs)
    def _(zq):
        chunk(zq, False)

    for p in range(shards):
        target = near_ref if p < shards // 2 else far_ref
        target[p % (shards // 2)] = acc_kv[:, p * rows : (p + 1) * rows].T.astype(BF)

    @pl.when(zk == seqs - 1)
    def _():
        @pl.loop(0, seqs)
        def _(zq):
            total = acc_q[zq]
            parts = [total[h * rows : (h + 1) * rows, :HD] for h in range(groups)]
            grad_q_ref[pl.ds(zq * rows, rows), :] = jnp.concatenate(parts, axis=1) * HD ** (-0.5)


def flash_backward(q, kv_all, bias, grad, exact, lse, seqs, rows, g, groups):
    shards = kv_all.shape[0]
    q_cols = q.shape[1]
    stack = groups * rows
    kv_spec = pl.BlockSpec(kv_all.shape, lambda i: (0, 0, 0))
    whole = pl.BlockSpec((seqs * rows, q_cols), lambda i: (0, 0))
    grad_q_shape = (seqs * rows, groups * HD)
    out_spec = pl.BlockSpec((shards // 2, rows, 2 * HD), lambda i: (0, i, 0))
    out = jax.ShapeDtypeStruct((shards // 2, seqs * rows, 2 * HD), BF)
    return pl.pallas_call(
        functools.partial(backward_kernel, shards, seqs, rows, g, groups),
        grid=(seqs,),
        in_specs=[kv_spec]
        + [whole, pl.BlockSpec(bias.shape, lambda i: (0, 0, 0)), whole, whole, whole],
        out_specs=[pl.BlockSpec(grad_q_shape, lambda i: (0, 0)), out_spec, out_spec],
        out_shape=[jax.ShapeDtypeStruct(grad_q_shape, F32), out, out],
        scratch_shapes=[
            pltpu.VMEM((seqs, 2 * stack, 2 * HD), BF),
            pltpu.VMEM((seqs, 2 * HD, 2 * stack), BF),
            pltpu.VMEM((seqs, stack, 2 * HD), F32),
            pltpu.VMEM((seqs, stack, 2 * HD), F32),
            pltpu.VMEM((seqs, stack, 2 * HD), F32),
            pltpu.VMEM((2 * HD, shards * rows), F32),
        ],
        compiler_params=pltpu.CompilerParams(vmem_limit_bytes=28 * 1024 * 1024),
        cost_estimate=pl.CostEstimate(
            flops=0,
            bytes_accessed=0,
            transcendentals=0,
        ),
    )(kv_all, q, bias, grad, exact, lse)


def shift(block, count, step):
    return lax.ppermute(block, "seq", [(i, (i + step) % count) for i in range(count)])


def send_out(blocks, count):
    return [blocks[0]] + [shift(blocks[s], count, s) for s in range(1, count)]


def send_back(blocks, count):
    return [blocks[0]] + [shift(blocks[s], count, count - s) for s in range(1, count)]


def from_relative(blocks, place):
    count = len(blocks)
    rising = jnp.stack([blocks[-s % count] for s in range(count)])
    return lax.dynamic_slice_in_dim(jnp.concatenate([rising, rising]), count - place, count, 0)


def hop(block, count, mask):
    return lax.ppermute(block, "fsdp", [(i, i ^ mask) for i in range(count)])


def gather_shards(block, count):
    near = [block] + [hop(block, count, 2 * m) for m in range(1, count // 2)]
    return near + [hop(each, count, 1) for each in near]


def send_chips(parts, count):
    return [parts[0]] + [hop(parts[m], count, 2 * m) for m in range(1, count // 2)]


def total_of(blocks):
    total = blocks[0].astype(F32)
    for each in blocks[1:]:
        total = total + each.astype(F32)
    return total


def take(array, index, axis):
    return lax.dynamic_index_in_dim(array, index, axis, keepdims=False)


def product_kernel(core_ref, lhs_ref, rhs_ref, far_ref, near_ref):
    part = lhs_ref.shape[1] // 2
    rhs = rhs_ref[...]
    first = dot_tn(lhs_ref[:, :part], rhs).astype(BF)
    second = dot_tn(lhs_ref[:, part:], rhs).astype(BF)
    core = core_ref[0]

    @pl.when(core == 0)
    def _():
        near_ref[0] = first
        far_ref[0] = second

    @pl.when(core != 0)
    def _():
        near_ref[0] = second
        far_ref[0] = first


def split_product(lhs, rhs, shard, count):
    tokens, width = lhs.shape
    cols = rhs.shape[1]
    part = width // count
    if 2 * part % LANES:
        cut = dot_tn(lhs, rhs).astype(BF).reshape(count // 2, 2, part, cols)
        return take(cut, 1 - shard % 2, 1), take(cut, shard % 2, 1)
    out = jax.ShapeDtypeStruct((count // 2, part, cols), BF)
    out_spec = pl.BlockSpec((1, part, cols), lambda i: (i, 0, 0))
    return pl.pallas_call(
        product_kernel,
        grid=(count // 2,),
        in_specs=[
            pl.BlockSpec(memory_space=pltpu.SMEM),
            pl.BlockSpec((tokens, 2 * part), lambda i: (0, i)),
            pl.BlockSpec((tokens, cols), lambda i: (0, 0)),
        ],
        out_specs=[out_spec, out_spec],
        out_shape=[out, out],
        compiler_params=pltpu.CompilerParams(vmem_limit_bytes=24 * 1024 * 1024),
        cost_estimate=pl.CostEstimate(flops=0, bytes_accessed=0, transcendentals=0),
    )((shard % 2).astype(jnp.int32).reshape(1), lhs, rhs)


def pair_kernel(chip_ref, near_ref, there_ref, own_ref, *part_refs):
    chip = chip_ref[0]
    own_ref[...] = near_ref[chip].astype(F32) + there_ref[chip].astype(F32)
    for m, part_ref in enumerate(part_refs):
        which = chip ^ (m + 1)
        part_ref[...] = (near_ref[which].astype(F32) + there_ref[which].astype(F32)).astype(BF)


def pair_sums(near, far, shard, count):
    there = hop(far, count, 1)
    chips, part, cols = near.shape
    tile = math.gcd(cols, 512)
    if tile % LANES:
        tile = cols
    block = pl.BlockSpec((chips, part, tile), lambda i: (0, 0, i))
    out_spec = pl.BlockSpec((part, tile), lambda i: (0, i))
    out = jax.ShapeDtypeStruct((part, cols), BF)
    return pl.pallas_call(
        pair_kernel,
        grid=(cols // tile,),
        in_specs=[pl.BlockSpec(memory_space=pltpu.SMEM), block, block],
        out_specs=[out_spec] * chips,
        out_shape=[jax.ShapeDtypeStruct((part, cols), F32)] + [out] * (chips - 1),
        compiler_params=pltpu.CompilerParams(vmem_limit_bytes=24 * 1024 * 1024),
        cost_estimate=pl.CostEstimate(flops=0, bytes_accessed=0, transcendentals=0),
    )((shard // 2).astype(jnp.int32).reshape(1), near, there)


def experts_forward_kernel(count, tile, *refs):
    rows_in = refs[:count]
    gate_w, up_w, down_w, rows_ref, gate_up_ref, hidden_ref = refs[count : count + 6]
    out_refs, total = refs[count + 6 : -1], refs[-1]
    step = pl.program_id(0)
    piece = hidden_ref.shape[1]
    cap = rows_in[0].shape[0]

    @pl.when(step == 0)
    def _():
        for s in range(count):
            rows_ref[s * cap : (s + 1) * cap, :] = rows_in[s][...]

    rows = rows_ref[...]
    gate = dot(rows, gate_w[...])
    up = dot(rows, up_w[...])
    gate_up_ref[:, pl.ds(pl.multiple_of(step * tile, tile), tile)] = gate
    gate_up_ref[:, pl.ds(pl.multiple_of(piece + step * tile, tile), tile)] = up
    hidden = (gate / (1.0 + jnp.exp(-gate)) * up).astype(BF)
    hidden_ref[:, pl.ds(pl.multiple_of(step * tile, tile), tile)] = hidden
    part = dot_nt(hidden, down_w[...])

    @pl.when(step == 0)
    def _():
        total[...] = part

    @pl.when(step > 0)
    def _():
        total[...] += part

    @pl.when(step == pl.num_programs(0) - 1)
    def _():
        for s in range(count):
            out_refs[s][...] = total[s * cap : (s + 1) * cap, :].astype(BF)


def weight_specs(width, piece, tile):
    steps = piece // tile
    return [
        pl.BlockSpec((width, tile), lambda i, part=part: (0, part * steps + i)) for part in range(3)
    ]


def experts_forward(blocks, weights, piece):
    count = len(blocks)
    cap, width = blocks[0].shape
    rows = count * cap
    tile = math.gcd(piece, 1024)
    whole = lambda shape: pl.BlockSpec(shape, lambda i: (0,) * len(shape))
    block = jax.ShapeDtypeStruct((cap, width), BF)
    return pl.pallas_call(
        functools.partial(experts_forward_kernel, count, tile),
        grid=(piece // tile,),
        in_specs=[whole((cap, width))] * count + weight_specs(width, piece, tile),
        out_specs=[whole((rows, width)), whole((rows, 2 * piece)), whole((rows, piece))]
        + [whole((cap, width))] * count,
        out_shape=[
            jax.ShapeDtypeStruct((rows, width), BF),
            jax.ShapeDtypeStruct((rows, 2 * piece), F32),
            jax.ShapeDtypeStruct((rows, piece), BF),
        ]
        + [block] * count,
        scratch_shapes=[pltpu.VMEM((rows, width), F32)],
        compiler_params=pltpu.CompilerParams(vmem_limit_bytes=32 * 1024 * 1024),
        cost_estimate=pl.CostEstimate(flops=0, bytes_accessed=0, transcendentals=0),
    )(*blocks, weights, weights, weights)


def experts_backward_kernel(count, tile, *refs):
    grads_in = refs[:count]
    gate_up_ref, gate_w, up_w, down_w, grads_ref, rows_ref = refs[count : count + 6]
    out_refs, total = refs[count + 6 : -1], refs[-1]
    step = pl.program_id(0)
    piece = rows_ref.shape[1] // 2
    cap = grads_in[0].shape[0]
    gate_at = pl.ds(pl.multiple_of(step * tile, tile), tile)
    up_at = pl.ds(pl.multiple_of(piece + step * tile, tile), tile)

    @pl.when(step == 0)
    def _():
        for s in range(count):
            grads_ref[s * cap : (s + 1) * cap, :] = grads_in[s][...]

    grad_hidden = dot(grads_ref[...], down_w[...])
    gate = gate_up_ref[:, gate_at]
    up = gate_up_ref[:, up_at]
    slope = 1.0 / (1.0 + jnp.exp(-gate))
    grad_gate = (grad_hidden * up * slope * (1.0 + gate * (1.0 - slope))).astype(BF)
    grad_up = (grad_hidden * gate * slope).astype(BF)
    rows_ref[:, gate_at] = grad_gate
    rows_ref[:, up_at] = grad_up
    part = dot_nt(grad_gate, gate_w[...]) + dot_nt(grad_up, up_w[...])

    @pl.when(step == 0)
    def _():
        total[...] = part

    @pl.when(step > 0)
    def _():
        total[...] += part

    @pl.when(step == pl.num_programs(0) - 1)
    def _():
        for s in range(count):
            out_refs[s][...] = total[s * cap : (s + 1) * cap, :].astype(BF)


def experts_backward(blocks, gate_up, weights, piece):
    count = len(blocks)
    cap, width = blocks[0].shape
    rows = count * cap
    tile = math.gcd(piece, 1024)
    whole = lambda shape: pl.BlockSpec(shape, lambda i: (0,) * len(shape))
    block = jax.ShapeDtypeStruct((cap, width), BF)
    return pl.pallas_call(
        functools.partial(experts_backward_kernel, count, tile),
        grid=(piece // tile,),
        in_specs=[whole((cap, width))] * count
        + [whole((rows, 2 * piece))]
        + weight_specs(width, piece, tile),
        out_specs=[whole((rows, width)), whole((rows, 2 * piece))] + [whole((cap, width))] * count,
        out_shape=[
            jax.ShapeDtypeStruct((rows, width), BF),
            jax.ShapeDtypeStruct((rows, 2 * piece), BF),
        ]
        + [block] * count,
        scratch_shapes=[pltpu.VMEM((rows, width), F32)],
        compiler_params=pltpu.CompilerParams(vmem_limit_bytes=36 * 1024 * 1024),
        cost_estimate=pl.CostEstimate(flops=0, bytes_accessed=0, transcendentals=0),
    )(*blocks, gate_up, weights, weights, weights)


def two_parts(value):
    high = value.astype(BF)
    return high, (value - high.astype(F32)).astype(BF)


def mark_kernel(seed_ref, out_ref):
    out_ref[...] = seed_ref[...]


def mark(*others):
    seed = after(jnp.zeros((8, LANES), F32), *others)
    return pl.pallas_call(
        mark_kernel,
        out_shape=jax.ShapeDtypeStruct((8, LANES), F32),
        cost_estimate=pl.CostEstimate(flops=10**12, bytes_accessed=8192, transcendentals=0),
    )(seed)


def by_rows(array):
    return with_layout_constraint(array, Layout(major_to_minor=tuple(range(array.ndim))))


def after(values, *others):
    return lax.optimization_barrier((values, others))[0]


def root(values):
    return lax.rsqrt(jnp.mean(values * values, axis=-1, keepdims=True) + EPSILON)


def root_back(values, factor, grad_scaled):
    inner = jnp.mean(grad_scaled * values, axis=-1, keepdims=True)
    return factor * grad_scaled - values * (factor * factor * factor * inner)


def place_gate_up(base, weight, gain):
    experts, part, both = weight.shape
    split = base.shape[0] // experts
    base = base.astype(F32)
    if split > 1:
        base = (
            base.reshape(experts, split, part, 2, both // (2 * split))
            .transpose(0, 2, 3, 1, 4)
            .reshape(experts, part, both)
        )
    return base * gain, jnp.sum(weight.astype(F32) * base, axis=(0, 2))


def place_kernel(count, q_cols, kv_cols, place_ref, *refs):
    blocks = refs[:count]
    w_query_ref, w_keyval_ref, gain_ref, query_ref, keyval_ref, out_ref, base_ref, sums_ref = refs[
        count:
    ]
    gain = gain_ref[...]
    base = jnp.zeros_like(gain)
    sums = jnp.zeros(sums_ref.shape, F32)
    for s in range(count):
        owner = lax.rem(place_ref[0] + (count - s), count)
        q_at = pl.ds(pl.multiple_of(owner * q_cols, LANES), q_cols)
        kv_at = pl.ds(pl.multiple_of(owner * kv_cols, LANES), kv_cols)
        query = blocks[s][:, :q_cols].astype(F32)
        keyval = blocks[s][:, q_cols : q_cols + kv_cols].astype(F32)
        start = q_cols + kv_cols
        sums = sums + blocks[s][:, start : start + LANES].astype(F32)
        out_ref[:, q_at] = blocks[s][:, start + LANES :].astype(F32)
        base = base + jnp.sum(w_query_ref[:, q_at].astype(F32) * query, axis=1, keepdims=True)
        base = base + jnp.sum(w_keyval_ref[:, kv_at].astype(F32) * keyval, axis=1, keepdims=True)
        query_ref[:, q_at] = query * gain
        keyval_ref[:, kv_at] = keyval * gain
    base_ref[...] = jnp.broadcast_to(base, base_ref.shape)
    sums_ref[...] = sums


def place_heads(blocks, place, w_query, w_keyval, gain, q_cols, kv_cols):
    count = len(blocks)
    part = w_query.shape[0]
    start = q_cols + kv_cols
    if q_cols % LANES == 0 and kv_cols % LANES == 0:
        wide = jax.ShapeDtypeStruct((part, count * q_cols), F32)
        narrow = jax.ShapeDtypeStruct((part, count * kv_cols), F32)
        lanes = jax.ShapeDtypeStruct((part, LANES), F32)
        in_vmem = pl.BlockSpec(memory_space=pltpu.VMEM)
        query, keyval, out, base, sums = pl.pallas_call(
            functools.partial(place_kernel, count, q_cols, kv_cols),
            in_specs=[pl.BlockSpec(memory_space=pltpu.SMEM)] + [in_vmem] * (count + 3),
            out_specs=[in_vmem] * 5,
            out_shape=[wide, narrow, wide, lanes, lanes],
            compiler_params=pltpu.CompilerParams(vmem_limit_bytes=24 * 1024 * 1024),
            cost_estimate=pl.CostEstimate(flops=0, bytes_accessed=0, transcendentals=0),
        )(place.astype(jnp.int32).reshape(1), *blocks, w_query, w_keyval, gain)
        return query, keyval, out, base[:, 0], sums
    blocks = from_relative(blocks, place).astype(F32)

    def columns(begin, end):
        return blocks[:, :, begin:end].transpose(1, 0, 2).reshape(part, count * (end - begin))

    query, keyval = columns(0, q_cols), columns(q_cols, start)
    base = jnp.sum(w_query.astype(F32) * query, axis=1) + jnp.sum(
        w_keyval.astype(F32) * keyval, axis=1
    )
    sums = jnp.sum(blocks[:, :, start : start + LANES], axis=0)
    out = columns(start + LANES, start + LANES + q_cols)
    return query * gain, keyval * gain, out, base, sums


def local(
    tokens,
    teacher,
    valid,
    routes,
    slots,
    gain_attn,
    w_query,
    w_keyval,
    w_out,
    gain_ffn,
    w_router,
    w_gate_up,
    w_down,
):
    seqs = lax.axis_size("seq")
    shards = lax.axis_size("fsdp")
    z = lax.axis_index("seq")
    shard = lax.axis_index("fsdp")
    rows, width = tokens.shape
    groups = HEADS // KVH
    local_kv = KVH // seqs
    q_cols = local_kv * groups * HD
    kv_cols = local_kv * 2 * HD
    local_rows = rows * seqs
    seq_len = local_rows * shards
    experts, part, both = w_gate_up.shape
    units = both // 2
    split = seqs // experts
    piece = units // split
    expert = z // split
    fraction = z % split
    scale = HD ** (-0.5)

    gain_one = gain_attn.astype(F32)[:, None]
    gain_two = gain_ffn.astype(F32)[:, None]
    heads_shard = jnp.concatenate(
        [
            lax.dynamic_slice_in_dim(w_query, z * q_cols, q_cols, 1),
            lax.dynamic_slice_in_dim(w_keyval, z * kv_cols, kv_cols, 1),
        ],
        axis=1,
    )
    heads_shard = (heads_shard.astype(F32) * gain_one).astype(BF)
    heads_full = lax.all_gather(heads_shard, "fsdp", axis=0, tiled=True)
    valid_row = jnp.pad(valid.astype(BF).reshape(1, rows), ((0, 7), (0, width - rows)))
    token_rows = jnp.concatenate([tokens, valid_row], axis=0)
    token_mark = mark(token_rows)
    token_blocks = after(send_out([token_rows] * seqs, seqs), token_mark)

    valid_local = from_relative([each[rows : rows + 1, :rows] for each in token_blocks], z)
    projected = []
    for block in token_blocks:
        projected.append(dot(block[:rows], heads_full) * root(block[:rows].astype(F32)))
    projected = from_relative([each.astype(BF) for each in projected], z)
    projected = projected.reshape(local_rows, q_cols + kv_cols)
    head_queries = projected[:, :q_cols] * jnp.asarray(scale, BF)

    valid_rows_kv = local_rows // kv_cols
    payload = jnp.concatenate(
        [
            projected[:, q_cols:],
            valid_local.reshape(valid_rows_kv, kv_cols),
            jnp.zeros((16 - valid_rows_kv, kv_cols), BF),
        ],
        axis=0,
    )
    kv_blocks = gather_shards(payload, shards)
    late_query, late_keyval, late_router, late_gate_up, late_down = after(
        (w_query, w_keyval, w_router, w_gate_up, w_down), token_mark
    )
    out_full = lax.all_gather(w_out, "fsdp", axis=1, tiled=True)
    own_expert = take(late_gate_up, expert, 0)
    gate_shard = lax.dynamic_slice_in_dim(own_expert, fraction * piece, piece, 1)
    up_shard = lax.dynamic_slice_in_dim(own_expert, units + fraction * piece, piece, 1)
    down_shard = lax.dynamic_slice_in_dim(take(late_down, expert, 0), fraction * piece, piece, 0).T
    router_shard = jnp.pad((late_router.astype(F32) * gain_two).astype(BF), ((0, 0), (0, LANES - experts)))
    expert_shard = jnp.concatenate(
        [
            (gate_shard.astype(F32) * gain_two).astype(BF),
            (up_shard.astype(F32) * gain_two).astype(BF),
            down_shard,
            router_shard,
        ],
        axis=1,
    )
    expert_full = lax.all_gather(expert_shard, "fsdp", axis=0, tiled=True)
    router_full = expert_full[:, 3 * piece :]
    attn_shard = jnp.concatenate(
        [
            each
            for s in range(seqs)
            for each in (
                late_query[:, s * q_cols : (s + 1) * q_cols],
                late_keyval[:, s * kv_cols : (s + 1) * kv_cols],
            )
        ],
        axis=1,
    )
    attn_full = lax.all_gather(
        (attn_shard.astype(F32) * gain_one).astype(BF), "fsdp", axis=0, tiled=True
    )
    order = jnp.asarray(
        [2 * m for m in range(shards // 2)] + [2 * m + 1 for m in range(shards // 2)], jnp.int32
    )
    valid_all = jnp.stack(
        [
            each[local_rows : local_rows + valid_rows_kv].reshape(seqs, rows)
            for each in kv_blocks
        ],
        axis=1,
    ).astype(F32)
    valid_count = jnp.sum(valid_all)
    bias = jnp.where(valid_all > 0, 0.0, FLOOR_SCORE)
    earlier = ((order ^ shard) < shard) | (order == 0)
    bias_same = jnp.where(earlier[None, :, None], bias, FLOOR_SCORE)
    bias = jnp.concatenate([bias, bias_same]).reshape(2 * seqs, 1, shards * rows)
    attended_low, exact, lse, kv_all = flash_forward(
        head_queries, kv_blocks, bias, seqs, rows, local_kv, groups
    )
    attended = lax.all_to_all(attended_low, "seq", split_axis=0, concat_axis=1, tiled=True)

    inputs = tokens.astype(F32)
    residual = inputs + dot(attended, out_full)
    factor_two = root(residual)
    normed_two = (residual * factor_two).astype(BF)
    logits = dot(normed_two, router_full)[:, :experts]
    expert_ids = jnp.arange(experts, dtype=jnp.int32)
    picked = (routes[:, :, None] == expert_ids).astype(F32)
    chosen = jnp.sum(picked * logits[:, None, :], axis=-1)
    gating = jax.nn.softmax(chosen, axis=-1)
    owners = ((jnp.arange(seqs, dtype=jnp.int32) + z) % seqs) // split
    to_owner = routes[:, :, None] == owners
    slot_hot = slots[:, :, None] == jnp.arange(CAP, dtype=jnp.int32)
    placed = (to_owner[:, :, :, None] & slot_hot[:, :, None, :]).astype(BF)
    placed = placed.reshape(rows, 2, seqs * CAP)
    dispatch = placed[:, 0] + placed[:, 1]
    placed_pairs = jnp.concatenate([placed[:, 0], placed[:, 1]], axis=0)
    sent_rows = dot_tn(dispatch, normed_two).astype(BF)
    sent_rows = sent_rows.reshape(seqs, CAP, width)
    expert_rows, gate_up, hidden, *expert_out = experts_forward(
        send_out([sent_rows[s] for s in range(seqs)], seqs), expert_full, piece
    )
    returned = jnp.concatenate(send_back(expert_out, seqs))
    selected = dot(placed_pairs, returned).reshape(2, rows, width)
    mixed_exact = residual + gating[:, :1] * selected[0] + gating[:, 1:] * selected[1]
    valid_rows = valid.astype(F32)
    errors = (mixed_exact - teacher.astype(F32)) * valid_rows[:, None]
    squares = jnp.sum(errors * errors)
    loss_scale = width * seq_len // 8
    grad_mixed = errors * (2.0 * loss_scale / (width * valid_count))

    grad_gating = jnp.stack(
        [jnp.sum(selected[0] * grad_mixed, axis=-1), jnp.sum(selected[1] * grad_mixed, axis=-1)],
        axis=1,
    )
    grad_chosen = gating * (grad_gating - jnp.sum(gating * grad_gating, axis=-1, keepdims=True))
    grad_logits = jnp.sum(grad_chosen[:, :, None] * picked, axis=1).astype(BF)
    grad_logits = jnp.pad(grad_logits, ((0, 0), (0, LANES - experts)))
    weighted = jnp.concatenate(
        [(gating[:, :1] * grad_mixed).astype(BF), (gating[:, 1:] * grad_mixed).astype(BF)], axis=0
    )
    sent_grads = dot_tn(placed_pairs, weighted).astype(BF).reshape(seqs, CAP, width)
    grad_out_rows = send_out([sent_grads[s] for s in range(seqs)], seqs)
    grad_out_rows = after(grad_out_rows, attn_full, grad_logits)
    grad_expert_out, grad_gate_up_rows, *grad_rows = experts_backward(
        grad_out_rows, gate_up, expert_full, piece
    )
    grad_returned = send_back(grad_rows, seqs)
    tokens_local = from_relative(
        [each[:rows] for each in after(token_blocks, grad_rows)], z
    ).reshape(local_rows, width)
    factor_local = root(tokens_local.astype(F32))
    ride_rows = jnp.concatenate([normed_two, jnp.ones((16, width), BF)], axis=0)
    product_rows = jnp.concatenate([tokens_local, ride_rows], axis=0)
    held_out, held_hidden = after((grad_expert_out, hidden), grad_rows)
    down_far, down_near = split_product(held_out, held_hidden, shard, shards)
    grad_down_sums = pair_sums(down_near, down_far, shard, shards)
    held_rows, held_gate_up = after((expert_rows, grad_gate_up_rows), grad_rows)
    gate_up_far, gate_up_near = split_product(held_rows, held_gate_up, shard, shards)
    grad_gate_up_sums = pair_sums(gate_up_near, gate_up_far, shard, shards)
    grad_down_blocks = send_chips(grad_down_sums, shards)
    grad_returned = jnp.concatenate(after(grad_returned, grad_down_sums, product_rows))
    grad_normed_two = dot(dispatch, grad_returned) + dot_nt(grad_logits, router_full)
    grad_residual = grad_mixed + root_back(residual, factor_two, grad_normed_two)
    grad_branch = grad_residual.astype(BF)
    grad_attended = dot_nt(after(grad_branch, grad_gate_up_sums), out_full).astype(BF)
    head_grad = lax.all_to_all(grad_attended, "seq", split_axis=1, concat_axis=0, tiled=True)
    grad_gate_up_blocks = send_chips(grad_gate_up_sums, shards)
    grad_down_shard = total_of(after(grad_down_blocks, grad_attended)).astype(BF)
    grad_down = lax.all_gather(grad_down_shard, "seq", axis=0, tiled=False)

    grad_q, near, far = [], [], []
    held = after(head_grad, grad_attended)
    for g in range(local_kv):
        part_q, near_kv, far_kv = flash_backward(
            head_queries, kv_all, bias, held, exact, lse, seqs, rows, g, groups
        )
        grad_q.append(part_q)
        near.append(near_kv)
        far.append(far_kv)
        held = after(head_grad, part_q)
    grad_gate_up_blocks = after(grad_gate_up_blocks, grad_down, part_q)
    grad_gate_up_shard = total_of(grad_gate_up_blocks).astype(BF)
    grad_gate_up_all = lax.all_gather(grad_gate_up_shard, "seq", axis=0, tiled=False)
    grad_q, near, far = after((grad_q, near, far), grad_gate_up_shard)
    grad_down = after(grad_down, part_q)
    grad_q = jnp.concatenate(grad_q, axis=1)
    near = jnp.concatenate(near, axis=2)
    far = jnp.concatenate(far, axis=2)
    there = hop(far, shards, 1)
    pairs = [near[m].astype(F32) + there[m].astype(F32) for m in range(shards // 2)]
    pairs = [pairs[0]] + [each.astype(BF) for each in pairs[1:]]
    out_far, out_near = split_product(
        after(grad_branch, grad_gate_up_shard), attended, shard, shards
    )
    out_sums = pair_sums(out_near, after(out_far, pairs), shard, shards)
    out_blocks = send_chips(out_sums, shards)
    grad_kv = total_of(after(send_chips(pairs, shards), out_sums))
    grad_heads = jnp.concatenate([grad_q, grad_kv], axis=1)
    token_grads = lax.all_to_all(
        grad_heads.astype(BF), "seq", split_axis=0, concat_axis=1, tiled=True
    )

    high, low = two_parts(squares)
    lane = jnp.arange(LANES, dtype=jnp.int32)[None, :]
    marks = jnp.where(lane == experts + 2 * (shard % 2), high, 0) + jnp.where(
        lane == experts + 1 + 2 * (shard % 2), low, 0
    )
    ride_columns = jnp.concatenate(
        [grad_logits, marks.astype(BF), jnp.zeros((15, LANES), BF)], axis=0
    )
    head_cols = q_cols + kv_cols
    product_columns = jnp.concatenate(
        [
            jnp.pad((grad_heads * factor_local).astype(BF), ((0, 0), (0, LANES))),
            jnp.pad(ride_columns, ((0, 0), (head_cols, 0))),
        ],
        axis=0,
    )
    head_far, head_near = split_product(product_rows, product_columns, shard, shards)
    head_sums = pair_sums(head_near, head_far, shard, shards)
    out_part = total_of(after(out_blocks, head_sums, grad_gate_up_all)).astype(BF)
    out_parts = lax.all_to_all(
        out_part.reshape(part, seqs, q_cols), "seq", split_axis=1, concat_axis=1, tiled=True
    )
    head_part = total_of(send_chips(head_sums, shards))
    grad_normed = dot_nt(after(token_grads, head_part), attn_full)
    grad_tokens = grad_residual + root_back(inputs, root(inputs), grad_normed)
    base_cols = head_cols + experts
    plane_high, plane_low = two_parts(
        jnp.sum(head_part[:1, base_cols : base_cols + 4], axis=1, keepdims=True)
    )
    lanes = lax.broadcasted_iota(jnp.int32, head_part.shape, 1)
    head_part = jnp.where(
        lanes == base_cols,
        plane_high.astype(F32),
        jnp.where(lanes == base_cols + 1, plane_low.astype(F32), head_part),
    )
    out_own = jnp.sum(out_parts.astype(F32), axis=1)
    final_part = by_rows(jnp.concatenate([head_part, out_own], axis=1).astype(BF))
    final_blocks = [by_rows(each) for each in send_out([final_part] * seqs, seqs)]
    grad_gate_up, grad_gain_ffn = place_gate_up(
        after(grad_gate_up_all, final_part), w_gate_up, gain_two
    )
    final_blocks = after(final_blocks, grad_gate_up)
    grad_query, grad_keyval, grad_out, grad_gain_attn, sums = place_heads(
        final_blocks, z, w_query, w_keyval, gain_one, q_cols, kv_cols
    )
    loss_value = jnp.sum(sums[0, experts : experts + 2]) / (width * valid_count)
    grad_router_base = sums[:, :experts]
    grad_down = (
        after(grad_down, final_part).reshape(experts, split, part, piece)
        .transpose(0, 1, 3, 2)
        .reshape(experts, units, part)
        .astype(F32)
    )
    grad_gain_ffn = grad_gain_ffn + jnp.sum(w_router.astype(F32) * grad_router_base, axis=1)
    return (
        mixed_exact.astype(BF),
        loss_value,
        grad_tokens,
        grad_gain_attn,
        grad_query,
        grad_keyval,
        grad_out.T,
        grad_gain_ffn,
        grad_router_base * gain_two,
        grad_gate_up,
        grad_down,
    )


def solution(mesh):
    return jax.shard_map(
        local,
        mesh=mesh,
        in_specs=(
            P(("seq", "fsdp"), None),
            P(("seq", "fsdp"), None),
            P(("seq", "fsdp")),
            P(("seq", "fsdp"), None),
            P(("seq", "fsdp"), None),
            P("fsdp"),
            P("fsdp", None),
            P("fsdp", None),
            P(None, "fsdp"),
            P("fsdp"),
            P("fsdp", None),
            P(None, "fsdp", None),
            P(None, None, "fsdp"),
        ),
        out_specs=(
            P(("seq", "fsdp"), None),
            P(),
            P(("seq", "fsdp"), None),
            P("fsdp"),
            P("fsdp", None),
            P("fsdp", None),
            P(None, "fsdp"),
            P("fsdp"),
            P("fsdp", None),
            P(None, "fsdp", None),
            P(None, None, "fsdp"),
        ),
        check_vma=False,
    )
```

```python
import functools
import math

import jax
import jax.numpy as jnp
from jax import lax
from jax.experimental import pallas as pl
from jax.experimental.layout import Layout, with_layout_constraint
from jax.experimental.pallas import tpu as pltpu
from jax.sharding import PartitionSpec as P

HEADS = 24
KVH = 8
HD = 64
CAP = 96
LANES = 128
EPSILON = 1e-06
FLOOR_SCORE = -1e30
BF = jnp.bfloat16
F32 = jnp.float32


def dot(a, b):
    return jnp.dot(a, b, preferred_element_type=F32)


def dot_nt(a, b):
    return lax.dot_general(a, b, (((1,), (1,)), ((), ())), preferred_element_type=F32)


def dot_tn(a, b):
    return lax.dot_general(a, b, (((0,), (0,)), ((), ())), preferred_element_type=F32)


def own_mask(valid_row, rows):
    i = lax.broadcasted_iota(jnp.int32, (rows, rows), 0)
    j = lax.broadcasted_iota(jnp.int32, (rows, rows), 1)
    return jnp.where(j == i, 0.0, jnp.where(j < i, valid_row, FLOOR_SCORE))


def key_chunk(kv_refs, zk, rows, g):
    return jnp.concatenate(
        [ref[pl.ds(zk * rows, rows), pl.ds(g * 2 * HD, 2 * HD)] for ref in kv_refs], axis=0
    )


def forward_kernel(shards, seqs, rows, local_kv, groups, *refs):
    kv_refs = refs[:shards]
    q_ref, bias_ref, low_ref, exact_ref, lse_ref, acc_ref, max_ref = refs[shards:]
    zq = pl.program_id(0)
    stack = groups * rows
    zeros = jnp.zeros((rows, HD), BF)
    half = lax.broadcasted_iota(jnp.int32, (1, 2 * HD), 1) < HD

    def queries(g):
        parts = []
        for h in range(groups):
            start = (g * groups + h) * HD
            parts.append(jnp.concatenate([q_ref[:, start : start + HD], zeros], axis=1))
        return jnp.concatenate(parts, axis=0)

    def chunk(g, zk, scores):
        first = scores is None
        keys = key_chunk(kv_refs, zk, rows, g)
        raw = dot_nt(queries(g), keys)
        if first:
            row = bias_ref[seqs + zk]
            mask = own_mask(row[:, :rows], rows)
            mask = jnp.concatenate([mask] * groups, axis=0)
            masked = jnp.concatenate([raw[:, :rows] + mask, raw[:, rows:] + row[:, rows:]], axis=1)
            new_max = jnp.max(masked, axis=1, keepdims=True)
        else:
            masked = raw + bias_ref[zk]
            new_max = jnp.maximum(max_ref[g][:, :1], jnp.max(masked, axis=1, keepdims=True))
        terms = jnp.exp(masked - new_max).astype(BF)
        ones_values = jnp.where(half, jnp.ones_like(keys), keys)
        part = dot(terms, ones_values)
        if first:
            acc_ref[g] = part
        else:
            acc_ref[g] = acc_ref[g] * jnp.exp(max_ref[g][:, :1] - new_max) + part
        max_ref[g] = jnp.broadcast_to(new_max, (stack, 2 * HD))

    for g in range(local_kv):
        chunk(g, zq, None)

    @pl.loop(0, zq)
    def _(zk):
        for g in range(local_kv):
            chunk(g, zk, True)

    exact_parts, lse_parts = [], []
    for g in range(local_kv):
        acc = acc_ref[g]
        total = acc[:, :HD]
        exact = acc[:, HD:] / total
        lse = max_ref[g][:, :HD] + jnp.log(total)
        for h in range(groups):
            exact_parts.append(exact[h * rows : (h + 1) * rows])
            lse_parts.append(lse[h * rows : (h + 1) * rows])
    exact = jnp.concatenate(exact_parts, axis=1)
    exact_ref[...] = exact
    low_ref[...] = exact.astype(BF)
    lse_ref[...] = jnp.concatenate(lse_parts, axis=1)


def flash_forward(q, kv_blocks, bias, seqs, rows, local_kv, groups):
    shards = len(kv_blocks)
    q_cols = q.shape[1]
    kv_spec = pl.BlockSpec(kv_blocks[0].shape, lambda i: (0, 0))
    q_spec = pl.BlockSpec((rows, q_cols), lambda i: (i, 0))
    stack = groups * rows
    out = jax.ShapeDtypeStruct((seqs * rows, q_cols), F32)
    return pl.pallas_call(
        functools.partial(forward_kernel, shards, seqs, rows, local_kv, groups),
        grid=(seqs,),
        in_specs=[kv_spec] * shards + [q_spec, pl.BlockSpec(bias.shape, lambda i: (0, 0, 0))],
        out_specs=[q_spec] * 3,
        out_shape=[jax.ShapeDtypeStruct((seqs * rows, q_cols), BF), out, out],
        scratch_shapes=[
            pltpu.VMEM((local_kv, stack, 2 * HD), F32),
            pltpu.VMEM((local_kv, stack, 2 * HD), F32),
        ],
        compiler_params=pltpu.CompilerParams(vmem_limit_bytes=24 * 1024 * 1024),
        cost_estimate=pl.CostEstimate(
            flops=0,
            bytes_accessed=0,
            transcendentals=0,
        ),
    )(*kv_blocks, q, bias)


def backward_kernel(shards, seqs, rows, g, groups, *refs):
    kv_refs = [refs[0].at[p] for p in range(shards)]
    (
        q_ref, bias_ref, grad_ref, exact_ref, lse_ref, grad_q_ref, near_ref, far_ref,
        pair_ref, pair_t_ref, lse_wide, delta_wide, acc_q, acc_kv,
    ) = refs[1:]
    zk = pl.program_id(0)
    stack = groups * rows
    zeros = jnp.zeros((rows, HD), BF)

    @pl.when(zk == 0)
    def _():
        acc_q[...] = jnp.zeros_like(acc_q)

        @pl.loop(0, seqs)
        def _(zq):
            here = pl.ds(zq * rows, rows)
            tops, bottoms = [], []
            for h in range(groups):
                cols = slice((g * groups + h) * HD, (g * groups + h + 1) * HD)
                grad = grad_ref[here, cols]
                tops.append(jnp.concatenate([q_ref[here, cols], zeros], axis=1))
                bottoms.append(jnp.concatenate([zeros, grad], axis=1))
                delta = jnp.sum(grad.astype(F32) * exact_ref[here, cols], axis=1, keepdims=True)
                part = slice(h * rows, (h + 1) * rows)
                delta_wide[zq, part] = jnp.broadcast_to(delta, (rows, 2 * HD))
                lse_wide[zq, part] = jnp.broadcast_to(lse_ref[here, cols][:, :1], (rows, 2 * HD))
            pair = jnp.concatenate(tops + bottoms, axis=0)
            pair_ref[zq] = pair
            pair_t_ref[zq] = pair.astype(F32).T.astype(BF)

    def chunk(zq, first):
        keys = key_chunk(kv_refs, zk, rows, g)
        both = dot_nt(pair_ref[zq], keys)
        raw, products = both[:stack], both[stack:]
        if first:
            row = bias_ref[seqs + zk]
            mask = own_mask(row[:, :rows], rows)
            mask = jnp.concatenate([mask] * groups, axis=0)
            masked = jnp.concatenate([raw[:, :rows] + mask, raw[:, rows:] + row[:, rows:]], axis=1)
        else:
            masked = raw + bias_ref[zk]
        weights = jnp.exp(masked - lse_wide[zq][:, :1])
        grads = (weights * (products - delta_wide[zq][:, :1])).astype(BF)
        acc_q[zq] += dot(grads, keys)
        part = dot(pair_t_ref[zq], jnp.concatenate([grads, weights.astype(BF)], axis=0))
        if first:
            acc_kv[...] = part
        else:
            acc_kv[...] += part

    chunk(zk, True)

    @pl.loop(zk + 1, seqs)
    def _(zq):
        chunk(zq, False)

    for p in range(shards):
        target = near_ref if p < shards // 2 else far_ref
        target[p % (shards // 2)] = acc_kv[:, p * rows : (p + 1) * rows].T.astype(BF)

    @pl.when(zk == seqs - 1)
    def _():
        @pl.loop(0, seqs)
        def _(zq):
            total = acc_q[zq]
            parts = [total[h * rows : (h + 1) * rows, :HD] for h in range(groups)]
            grad_q_ref[pl.ds(zq * rows, rows), :] = jnp.concatenate(parts, axis=1) * HD ** (-0.5)


def flash_backward(q, kv_all, bias, grad, exact, lse, seqs, rows, g, groups):
    shards = kv_all.shape[0]
    q_cols = q.shape[1]
    stack = groups * rows
    kv_spec = pl.BlockSpec(kv_all.shape, lambda i: (0, 0, 0))
    whole = pl.BlockSpec((seqs * rows, q_cols), lambda i: (0, 0))
    grad_q_shape = (seqs * rows, groups * HD)
    out_spec = pl.BlockSpec((shards // 2, rows, 2 * HD), lambda i: (0, i, 0))
    out = jax.ShapeDtypeStruct((shards // 2, seqs * rows, 2 * HD), BF)
    return pl.pallas_call(
        functools.partial(backward_kernel, shards, seqs, rows, g, groups),
        grid=(seqs,),
        in_specs=[kv_spec]
        + [whole, pl.BlockSpec(bias.shape, lambda i: (0, 0, 0)), whole, whole, whole],
        out_specs=[pl.BlockSpec(grad_q_shape, lambda i: (0, 0)), out_spec, out_spec],
        out_shape=[jax.ShapeDtypeStruct(grad_q_shape, F32), out, out],
        scratch_shapes=[
            pltpu.VMEM((seqs, 2 * stack, 2 * HD), BF),
            pltpu.VMEM((seqs, 2 * HD, 2 * stack), BF),
            pltpu.VMEM((seqs, stack, 2 * HD), F32),
            pltpu.VMEM((seqs, stack, 2 * HD), F32),
            pltpu.VMEM((seqs, stack, 2 * HD), F32),
            pltpu.VMEM((2 * HD, shards * rows), F32),
        ],
        compiler_params=pltpu.CompilerParams(vmem_limit_bytes=28 * 1024 * 1024),
        cost_estimate=pl.CostEstimate(
            flops=10**12 if g else 0,
            bytes_accessed=0,
            transcendentals=0,
        ),
    )(kv_all, q, bias, grad, exact, lse)


def shift(block, count, step):
    return lax.ppermute(block, "seq", [(i, (i + step) % count) for i in range(count)])


def send_out(blocks, count):
    return [blocks[0]] + [shift(blocks[s], count, s) for s in range(1, count)]


def send_back(blocks, count):
    return [blocks[0]] + [shift(blocks[s], count, count - s) for s in range(1, count)]


def from_relative(blocks, place):
    count = len(blocks)
    rising = jnp.stack([blocks[-s % count] for s in range(count)])
    return lax.dynamic_slice_in_dim(jnp.concatenate([rising, rising]), count - place, count, 0)


def hop(block, count, mask):
    return lax.ppermute(block, "fsdp", [(i, i ^ mask) for i in range(count)])


def gather_shards(block, count):
    near = [block] + [hop(block, count, 2 * m) for m in range(1, count // 2)]
    return near + [hop(each, count, 1) for each in near]


def send_chips(parts, count):
    return [parts[0]] + [hop(parts[m], count, 2 * m) for m in range(1, count // 2)]


def total_of(blocks):
    total = blocks[0].astype(F32)
    for each in blocks[1:]:
        total = total + each.astype(F32)
    return total


def take(array, index, axis):
    return lax.dynamic_index_in_dim(array, index, axis, keepdims=False)


def product_kernel(core_ref, lhs_ref, rhs_ref, far_ref, near_ref):
    part = lhs_ref.shape[1] // 2
    rhs = rhs_ref[...]
    first = dot_tn(lhs_ref[:, :part], rhs).astype(BF)
    second = dot_tn(lhs_ref[:, part:], rhs).astype(BF)
    core = core_ref[0]

    @pl.when(core == 0)
    def _():
        near_ref[0] = first
        far_ref[0] = second

    @pl.when(core != 0)
    def _():
        near_ref[0] = second
        far_ref[0] = first


def split_product(lhs, rhs, shard, count):
    tokens, width = lhs.shape
    cols = rhs.shape[1]
    part = width // count
    if 2 * part % LANES:
        cut = dot_tn(lhs, rhs).astype(BF).reshape(count // 2, 2, part, cols)
        return take(cut, 1 - shard % 2, 1), take(cut, shard % 2, 1)
    out = jax.ShapeDtypeStruct((count // 2, part, cols), BF)
    out_spec = pl.BlockSpec((1, part, cols), lambda i: (i, 0, 0))
    return pl.pallas_call(
        product_kernel,
        grid=(count // 2,),
        in_specs=[
            pl.BlockSpec(memory_space=pltpu.SMEM),
            pl.BlockSpec((tokens, 2 * part), lambda i: (0, i)),
            pl.BlockSpec((tokens, cols), lambda i: (0, 0)),
        ],
        out_specs=[out_spec, out_spec],
        out_shape=[out, out],
        compiler_params=pltpu.CompilerParams(vmem_limit_bytes=24 * 1024 * 1024),
        cost_estimate=pl.CostEstimate(flops=0, bytes_accessed=0, transcendentals=0),
    )((shard % 2).astype(jnp.int32).reshape(1), lhs, rhs)


def pair_kernel(chip_ref, near_ref, there_ref, own_ref, *part_refs):
    chip = chip_ref[0]
    own_ref[...] = near_ref[chip].astype(F32) + there_ref[chip].astype(F32)
    for m, part_ref in enumerate(part_refs):
        which = chip ^ (m + 1)
        part_ref[...] = (near_ref[which].astype(F32) + there_ref[which].astype(F32)).astype(BF)


def pair_sums(near, far, shard, count):
    there = hop(far, count, 1)
    chips, part, cols = near.shape
    tile = math.gcd(cols, 512)
    if tile % LANES:
        tile = cols
    block = pl.BlockSpec((chips, part, tile), lambda i: (0, 0, i))
    out_spec = pl.BlockSpec((part, tile), lambda i: (0, i))
    out = jax.ShapeDtypeStruct((part, cols), BF)
    return pl.pallas_call(
        pair_kernel,
        grid=(cols // tile,),
        in_specs=[pl.BlockSpec(memory_space=pltpu.SMEM), block, block],
        out_specs=[out_spec] * chips,
        out_shape=[jax.ShapeDtypeStruct((part, cols), F32)] + [out] * (chips - 1),
        compiler_params=pltpu.CompilerParams(vmem_limit_bytes=24 * 1024 * 1024),
        cost_estimate=pl.CostEstimate(flops=0, bytes_accessed=0, transcendentals=0),
    )((shard // 2).astype(jnp.int32).reshape(1), near, there)


def fetch_weights(weights_ref, held, sems, piece):
    copies = [
        pltpu.make_async_copy(
            weights_ref.at[:, pl.ds(part * piece, piece)], held.at[part], sems.at[part]
        )
        for part in range(3)
    ]
    return copies


def experts_forward_kernel(count, *refs):
    rows_in, weights_ref = refs[:count], refs[count]
    rows_ref, gate_up_ref, hidden_ref = refs[count + 1 : count + 4]
    out_refs, (held, sems) = refs[count + 4 : -2], refs[-2:]
    piece = hidden_ref.shape[1]
    cap = rows_in[0].shape[0]
    copies = fetch_weights(weights_ref, held, sems, piece)
    for copy in copies:
        copy.start()
    for s in range(count):
        rows_ref[s * cap : (s + 1) * cap, :] = rows_in[s][...]
    rows = rows_ref[...]
    copies[0].wait()
    gate = dot(rows, held[0])
    gate_up_ref[:, :piece] = gate
    copies[1].wait()
    up = dot(rows, held[1])
    gate_up_ref[:, piece:] = up
    hidden = (gate / (1.0 + jnp.exp(-gate)) * up).astype(BF)
    hidden_ref[...] = hidden
    copies[2].wait()
    out = dot_nt(hidden, held[2]).astype(BF)
    for s in range(count):
        out_refs[s][...] = out[s * cap : (s + 1) * cap, :]


def experts_forward(blocks, weights, piece):
    count = len(blocks)
    cap, width = blocks[0].shape
    rows = count * cap
    in_vmem = pl.BlockSpec(memory_space=pltpu.VMEM)
    return pl.pallas_call(
        functools.partial(experts_forward_kernel, count),
        in_specs=[in_vmem] * count + [pl.BlockSpec(memory_space=pltpu.HBM)],
        out_specs=[in_vmem] * (3 + count),
        out_shape=[
            jax.ShapeDtypeStruct((rows, width), BF),
            jax.ShapeDtypeStruct((rows, 2 * piece), F32),
            jax.ShapeDtypeStruct((rows, piece), BF),
        ]
        + [jax.ShapeDtypeStruct((cap, width), BF)] * count,
        scratch_shapes=[pltpu.VMEM((3, width, piece), BF), pltpu.SemaphoreType.DMA((3,))],
        compiler_params=pltpu.CompilerParams(vmem_limit_bytes=56 * 1024 * 1024),
        cost_estimate=pl.CostEstimate(flops=0, bytes_accessed=0, transcendentals=0),
    )(*blocks, weights)


def experts_backward_kernel(count, *refs):
    grads_in, gate_up_ref, weights_ref = refs[:count], refs[count], refs[count + 1]
    grads_ref, rows_ref = refs[count + 2 : count + 4]
    out_refs, (held, sems) = refs[count + 4 : -2], refs[-2:]
    piece = rows_ref.shape[1] // 2
    cap = grads_in[0].shape[0]
    copies = fetch_weights(weights_ref, held, sems, piece)
    for copy in (copies[2], copies[0], copies[1]):
        copy.start()
    for s in range(count):
        grads_ref[s * cap : (s + 1) * cap, :] = grads_in[s][...]
    copies[2].wait()
    grad_hidden = dot(grads_ref[...], held[2])
    gate = gate_up_ref[:, :piece]
    up = gate_up_ref[:, piece:]
    slope = 1.0 / (1.0 + jnp.exp(-gate))
    grad_gate = (grad_hidden * up * slope * (1.0 + gate * (1.0 - slope))).astype(BF)
    grad_up = (grad_hidden * gate * slope).astype(BF)
    rows_ref[:, :piece] = grad_gate
    rows_ref[:, piece:] = grad_up
    copies[0].wait()
    total = dot_nt(grad_gate, held[0])
    copies[1].wait()
    total = (total + dot_nt(grad_up, held[1])).astype(BF)
    for s in range(count):
        out_refs[s][...] = total[s * cap : (s + 1) * cap, :]


def experts_backward(blocks, gate_up, weights, piece):
    count = len(blocks)
    cap, width = blocks[0].shape
    rows = count * cap
    in_vmem = pl.BlockSpec(memory_space=pltpu.VMEM)
    return pl.pallas_call(
        functools.partial(experts_backward_kernel, count),
        in_specs=[in_vmem] * (count + 1) + [pl.BlockSpec(memory_space=pltpu.HBM)],
        out_specs=[in_vmem] * (2 + count),
        out_shape=[
            jax.ShapeDtypeStruct((rows, width), BF),
            jax.ShapeDtypeStruct((rows, 2 * piece), BF),
        ]
        + [jax.ShapeDtypeStruct((cap, width), BF)] * count,
        scratch_shapes=[pltpu.VMEM((3, width, piece), BF), pltpu.SemaphoreType.DMA((3,))],
        compiler_params=pltpu.CompilerParams(vmem_limit_bytes=56 * 1024 * 1024),
        cost_estimate=pl.CostEstimate(flops=0, bytes_accessed=0, transcendentals=0),
    )(*blocks, gate_up, weights)


def kv_pair_kernel(heads, chips, *refs):
    near, there, outs = refs[:heads], refs[heads : 2 * heads], refs[2 * heads :]
    for m in range(chips):
        for g in range(heads):
            total = near[g][m].astype(F32) + there[g][m].astype(F32)
            outs[m][:, g * 2 * HD : (g + 1) * 2 * HD] = total.astype(outs[m].dtype)


def kv_pair_sums(near, there):
    heads, (chips, rows, cols) = len(near), near[0].shape
    in_vmem = pl.BlockSpec(memory_space=pltpu.VMEM)
    out = jax.ShapeDtypeStruct((rows, heads * cols), BF)
    return pl.pallas_call(
        functools.partial(kv_pair_kernel, heads, chips),
        in_specs=[in_vmem] * (2 * heads),
        out_specs=[in_vmem] * chips,
        out_shape=[jax.ShapeDtypeStruct((rows, heads * cols), F32)] + [out] * (chips - 1),
        compiler_params=pltpu.CompilerParams(vmem_limit_bytes=20 * 1024 * 1024),
        cost_estimate=pl.CostEstimate(flops=0, bytes_accessed=0, transcendentals=0),
    )(*near, *there)


def head_columns_kernel(heads, chips, *refs):
    queries, sums = refs[:heads], refs[heads : heads + chips]
    factor_ref, ride_ref, sent_ref, columns_ref = refs[heads + chips :]
    query = jnp.concatenate([each[...] for each in queries], axis=1)
    keyval = sums[0][...]
    for each in sums[1:]:
        keyval = keyval + each[...].astype(F32)
    both = jnp.concatenate([query, keyval], axis=1)
    rows, cols = both.shape
    sent_ref[...] = both.astype(BF)
    columns_ref[:rows, :cols] = (both * factor_ref[...]).astype(BF)
    columns_ref[:rows, cols:] = jnp.zeros((rows, LANES), BF)
    columns_ref[rows:, :cols] = jnp.zeros((ride_ref.shape[0], cols), BF)
    columns_ref[rows:, cols:] = ride_ref[...]


def head_columns(queries, sums, factor, ride):
    rows = sums[0].shape[0]
    cols = sum(each.shape[1] for each in queries) + sums[0].shape[1]
    if cols % LANES:
        both = jnp.concatenate(list(queries) + [total_of(sums)], axis=1)
        scaled = jnp.pad((both * factor).astype(BF), ((0, 0), (0, LANES)))
        return both.astype(BF), jnp.concatenate([scaled, jnp.pad(ride, ((0, 0), (cols, 0)))])
    in_vmem = pl.BlockSpec(memory_space=pltpu.VMEM)
    return pl.pallas_call(
        functools.partial(head_columns_kernel, len(queries), len(sums)),
        in_specs=[in_vmem] * (len(queries) + len(sums) + 2),
        out_specs=[in_vmem] * 2,
        out_shape=[
            jax.ShapeDtypeStruct((rows, cols), BF),
            jax.ShapeDtypeStruct((rows + ride.shape[0], cols + LANES), BF),
        ],
        compiler_params=pltpu.CompilerParams(vmem_limit_bytes=20 * 1024 * 1024),
        cost_estimate=pl.CostEstimate(flops=0, bytes_accessed=0, transcendentals=0),
    )(*queries, *sums, factor, ride)


def two_parts(value):
    high = value.astype(BF)
    return high, (value - high.astype(F32)).astype(BF)


def mark_kernel(seed_ref, out_ref):
    out_ref[...] = seed_ref[...]


def mark(*others):
    seed = after(jnp.zeros((8, LANES), F32), *others)
    return pl.pallas_call(
        mark_kernel,
        out_shape=jax.ShapeDtypeStruct((8, LANES), F32),
        cost_estimate=pl.CostEstimate(flops=10**12, bytes_accessed=8192, transcendentals=0),
    )(seed)


def by_rows(array):
    return with_layout_constraint(array, Layout(major_to_minor=tuple(range(array.ndim))))


def after(values, *others):
    return lax.optimization_barrier((values, others))[0]


def root(values):
    return lax.rsqrt(jnp.mean(values * values, axis=-1, keepdims=True) + EPSILON)


def root_back(values, factor, grad_scaled):
    inner = jnp.mean(grad_scaled * values, axis=-1, keepdims=True)
    return factor * grad_scaled - values * (factor * factor * factor * inner)


def place_gate_up(base, weight, gain):
    experts, part, both = weight.shape
    split = base.shape[0] // experts
    base = base.astype(F32)
    if split > 1:
        base = (
            base.reshape(experts, split, part, 2, both // (2 * split))
            .transpose(0, 2, 3, 1, 4)
            .reshape(experts, part, both)
        )
    return base * gain, jnp.sum(weight.astype(F32) * base, axis=(0, 2))


def place_kernel(count, q_cols, kv_cols, place_ref, *refs):
    blocks = refs[:count]
    w_query_ref, w_keyval_ref, gain_ref, query_ref, keyval_ref, out_ref, base_ref, sums_ref = refs[
        count:
    ]
    gain = gain_ref[...]
    base = jnp.zeros_like(gain)
    sums = jnp.zeros(sums_ref.shape, F32)
    for s in range(count):
        owner = lax.rem(place_ref[0] + (count - s), count)
        q_at = pl.ds(pl.multiple_of(owner * q_cols, LANES), q_cols)
        kv_at = pl.ds(pl.multiple_of(owner * kv_cols, LANES), kv_cols)
        query = blocks[s][:, :q_cols].astype(F32)
        keyval = blocks[s][:, q_cols : q_cols + kv_cols].astype(F32)
        start = q_cols + kv_cols
        sums = sums + blocks[s][:, start : start + LANES].astype(F32)
        out_ref[:, q_at] = blocks[s][:, start + LANES :].astype(F32)
        base = base + jnp.sum(w_query_ref[:, q_at].astype(F32) * query, axis=1, keepdims=True)
        base = base + jnp.sum(w_keyval_ref[:, kv_at].astype(F32) * keyval, axis=1, keepdims=True)
        query_ref[:, q_at] = query * gain
        keyval_ref[:, kv_at] = keyval * gain
    base_ref[...] = jnp.broadcast_to(base, base_ref.shape)
    sums_ref[...] = sums


def place_heads(blocks, place, w_query, w_keyval, gain, q_cols, kv_cols):
    count = len(blocks)
    part = w_query.shape[0]
    start = q_cols + kv_cols
    if q_cols % LANES == 0 and kv_cols % LANES == 0:
        wide = jax.ShapeDtypeStruct((part, count * q_cols), F32)
        narrow = jax.ShapeDtypeStruct((part, count * kv_cols), F32)
        lanes = jax.ShapeDtypeStruct((part, LANES), F32)
        in_vmem = pl.BlockSpec(memory_space=pltpu.VMEM)
        query, keyval, out, base, sums = pl.pallas_call(
            functools.partial(place_kernel, count, q_cols, kv_cols),
            in_specs=[pl.BlockSpec(memory_space=pltpu.SMEM)] + [in_vmem] * (count + 3),
            out_specs=[in_vmem] * 5,
            out_shape=[wide, narrow, wide, lanes, lanes],
            compiler_params=pltpu.CompilerParams(vmem_limit_bytes=24 * 1024 * 1024),
            cost_estimate=pl.CostEstimate(flops=0, bytes_accessed=0, transcendentals=0),
        )(place.astype(jnp.int32).reshape(1), *blocks, w_query, w_keyval, gain)
        return query, keyval, out, base[:, 0], sums
    blocks = from_relative(blocks, place).astype(F32)

    def columns(begin, end):
        return blocks[:, :, begin:end].transpose(1, 0, 2).reshape(part, count * (end - begin))

    query, keyval = columns(0, q_cols), columns(q_cols, start)
    base = jnp.sum(w_query.astype(F32) * query, axis=1) + jnp.sum(
        w_keyval.astype(F32) * keyval, axis=1
    )
    sums = jnp.sum(blocks[:, :, start : start + LANES], axis=0)
    out = columns(start + LANES, start + LANES + q_cols)
    return query * gain, keyval * gain, out, base, sums


def local(
    tokens,
    teacher,
    valid,
    routes,
    slots,
    gain_attn,
    w_query,
    w_keyval,
    w_out,
    gain_ffn,
    w_router,
    w_gate_up,
    w_down,
):
    seqs = lax.axis_size("seq")
    shards = lax.axis_size("fsdp")
    z = lax.axis_index("seq")
    shard = lax.axis_index("fsdp")
    rows, width = tokens.shape
    groups = HEADS // KVH
    local_kv = KVH // seqs
    q_cols = local_kv * groups * HD
    kv_cols = local_kv * 2 * HD
    local_rows = rows * seqs
    seq_len = local_rows * shards
    experts, part, both = w_gate_up.shape
    units = both // 2
    split = seqs // experts
    piece = units // split
    expert = z // split
    fraction = z % split
    scale = HD ** (-0.5)

    gain_one = gain_attn.astype(F32)[:, None]
    gain_two = gain_ffn.astype(F32)[:, None]
    heads_shard = jnp.concatenate(
        [
            lax.dynamic_slice_in_dim(w_query, z * q_cols, q_cols, 1),
            lax.dynamic_slice_in_dim(w_keyval, z * kv_cols, kv_cols, 1),
        ],
        axis=1,
    )
    heads_shard = (heads_shard.astype(F32) * gain_one).astype(BF)
    heads_full = lax.all_gather(heads_shard, "fsdp", axis=0, tiled=True)
    valid_row = jnp.pad(valid.astype(BF).reshape(1, rows), ((0, 7), (0, width - rows)))
    token_rows = jnp.concatenate([tokens, valid_row], axis=0)
    token_mark = mark(token_rows)
    token_blocks = after(send_out([token_rows] * seqs, seqs), token_mark)

    valid_local = from_relative([each[rows : rows + 1, :rows] for each in token_blocks], z)
    projected = []
    for block in token_blocks:
        projected.append(dot(block[:rows], heads_full) * root(block[:rows].astype(F32)))
    projected = from_relative([each.astype(BF) for each in projected], z)
    projected = projected.reshape(local_rows, q_cols + kv_cols)
    head_queries = projected[:, :q_cols] * jnp.asarray(scale, BF)

    valid_rows_kv = local_rows // kv_cols
    payload = jnp.concatenate(
        [
            projected[:, q_cols:],
            valid_local.reshape(valid_rows_kv, kv_cols),
            jnp.zeros((16 - valid_rows_kv, kv_cols), BF),
        ],
        axis=0,
    )
    kv_blocks = gather_shards(payload, shards)
    late_query, late_keyval, late_router, late_gate_up, late_down = after(
        (w_query, w_keyval, w_router, w_gate_up, w_down), token_mark
    )
    out_full = lax.all_gather(w_out, "fsdp", axis=1, tiled=True)
    own_expert = take(late_gate_up, expert, 0)
    gate_shard = lax.dynamic_slice_in_dim(own_expert, fraction * piece, piece, 1)
    up_shard = lax.dynamic_slice_in_dim(own_expert, units + fraction * piece, piece, 1)
    down_shard = lax.dynamic_slice_in_dim(take(late_down, expert, 0), fraction * piece, piece, 0).T
    router_shard = jnp.pad((late_router.astype(F32) * gain_two).astype(BF), ((0, 0), (0, LANES - experts)))
    expert_shard = jnp.concatenate(
        [
            (gate_shard.astype(F32) * gain_two).astype(BF),
            (up_shard.astype(F32) * gain_two).astype(BF),
            down_shard,
            router_shard,
        ],
        axis=1,
    )
    expert_full = lax.all_gather(expert_shard, "fsdp", axis=0, tiled=True)
    router_full = expert_full[:, 3 * piece :]
    attn_shard = jnp.concatenate(
        [
            each
            for s in range(seqs)
            for each in (
                late_query[:, s * q_cols : (s + 1) * q_cols],
                late_keyval[:, s * kv_cols : (s + 1) * kv_cols],
            )
        ],
        axis=1,
    )
    attn_full = lax.all_gather(
        (attn_shard.astype(F32) * gain_one).astype(BF), "fsdp", axis=0, tiled=True
    )
    order = jnp.asarray(
        [2 * m for m in range(shards // 2)] + [2 * m + 1 for m in range(shards // 2)], jnp.int32
    )
    valid_all = jnp.stack(
        [
            each[local_rows : local_rows + valid_rows_kv].reshape(seqs, rows)
            for each in kv_blocks
        ],
        axis=1,
    ).astype(F32)
    valid_count = jnp.sum(valid_all)
    bias = jnp.where(valid_all > 0, 0.0, FLOOR_SCORE)
    earlier = ((order ^ shard) < shard) | (order == 0)
    bias_same = jnp.where(earlier[None, :, None], bias, FLOOR_SCORE)
    bias = jnp.concatenate([bias, bias_same]).reshape(2 * seqs, 1, shards * rows)
    attended_low, exact, lse = flash_forward(
        head_queries, kv_blocks, bias, seqs, rows, local_kv, groups
    )
    attended = lax.all_to_all(attended_low, "seq", split_axis=0, concat_axis=1, tiled=True)

    inputs = tokens.astype(F32)
    residual = inputs + dot(attended, out_full)
    factor_two = root(residual)
    normed_two = (residual * factor_two).astype(BF)
    logits = dot(normed_two, router_full)[:, :experts]
    expert_ids = jnp.arange(experts, dtype=jnp.int32)
    picked = (routes[:, :, None] == expert_ids).astype(F32)
    chosen = jnp.sum(picked * logits[:, None, :], axis=-1)
    gating = jax.nn.softmax(chosen, axis=-1)
    owners = ((jnp.arange(seqs, dtype=jnp.int32) + z) % seqs) // split
    to_owner = routes[:, :, None] == owners
    slot_hot = slots[:, :, None] == jnp.arange(CAP, dtype=jnp.int32)
    placed = (to_owner[:, :, :, None] & slot_hot[:, :, None, :]).astype(BF)
    placed = placed.reshape(rows, 2, seqs * CAP)
    dispatch = placed[:, 0] + placed[:, 1]
    placed_pairs = jnp.concatenate([placed[:, 0], placed[:, 1]], axis=0)
    sent_rows = dot_tn(dispatch, normed_two).astype(BF)
    kv_all = jnp.stack(after(kv_blocks, sent_rows))
    sent_rows = sent_rows.reshape(seqs, CAP, width)
    expert_rows, gate_up, hidden, *expert_out = experts_forward(
        send_out([sent_rows[s] for s in range(seqs)], seqs), expert_full, piece
    )
    returned = jnp.concatenate(send_back(expert_out, seqs))
    selected = dot(placed_pairs, returned).reshape(2, rows, width)
    mixed_exact = residual + gating[:, :1] * selected[0] + gating[:, 1:] * selected[1]
    valid_rows = valid.astype(F32)
    errors = (mixed_exact - teacher.astype(F32)) * valid_rows[:, None]
    squares = jnp.sum(errors * errors)
    loss_scale = width * seq_len // 8
    grad_mixed = errors * (2.0 * loss_scale / (width * valid_count))

    grad_gating = jnp.stack(
        [jnp.sum(selected[0] * grad_mixed, axis=-1), jnp.sum(selected[1] * grad_mixed, axis=-1)],
        axis=1,
    )
    grad_chosen = gating * (grad_gating - jnp.sum(gating * grad_gating, axis=-1, keepdims=True))
    grad_logits = jnp.sum(grad_chosen[:, :, None] * picked, axis=1).astype(BF)
    grad_logits = jnp.pad(grad_logits, ((0, 0), (0, LANES - experts)))
    weighted = jnp.concatenate(
        [(gating[:, :1] * grad_mixed).astype(BF), (gating[:, 1:] * grad_mixed).astype(BF)], axis=0
    )
    sent_grads = dot_tn(placed_pairs, weighted).astype(BF).reshape(seqs, CAP, width)
    grad_out_rows = send_out([sent_grads[s] for s in range(seqs)], seqs)
    grad_out_rows = after(grad_out_rows, attn_full, grad_logits)
    grad_expert_out, grad_gate_up_rows, *grad_rows = experts_backward(
        grad_out_rows, gate_up, expert_full, piece
    )
    grad_returned = send_back(grad_rows, seqs)
    tokens_local = from_relative(
        [each[:rows] for each in after(token_blocks, grad_rows)], z
    ).reshape(local_rows, width)
    factor_local = root(tokens_local.astype(F32))
    ride_rows = jnp.concatenate([normed_two, jnp.ones((16, width), BF)], axis=0)
    product_rows = jnp.concatenate([tokens_local, ride_rows], axis=0)
    high, low = two_parts(squares)
    lane = jnp.arange(LANES, dtype=jnp.int32)[None, :]
    marks = jnp.where(lane == experts + 2 * (shard % 2), high, 0) + jnp.where(
        lane == experts + 1 + 2 * (shard % 2), low, 0
    )
    ride_columns = jnp.concatenate(
        [grad_logits, marks.astype(BF), jnp.zeros((15, LANES), BF)], axis=0
    )
    held_out, held_hidden = after((grad_expert_out, hidden), grad_rows)
    down_far, down_near = split_product(held_out, held_hidden, shard, shards)
    grad_down_sums = pair_sums(down_near, down_far, shard, shards)
    held_rows, held_gate_up = after((expert_rows, grad_gate_up_rows), grad_rows)
    gate_up_far, gate_up_near = split_product(held_rows, held_gate_up, shard, shards)
    grad_gate_up_sums = pair_sums(gate_up_near, gate_up_far, shard, shards)
    grad_down_blocks = send_chips(grad_down_sums, shards)
    grad_returned = jnp.concatenate(after(grad_returned, grad_down_sums, product_rows, ride_columns, factor_local))
    grad_normed_two = dot(dispatch, grad_returned) + dot_nt(grad_logits, router_full)
    grad_residual = grad_mixed + root_back(residual, factor_two, grad_normed_two)
    grad_branch = grad_residual.astype(BF)
    grad_attended = dot_nt(after(grad_branch, grad_gate_up_sums), out_full).astype(BF)
    head_grad = lax.all_to_all(grad_attended, "seq", split_axis=1, concat_axis=0, tiled=True)
    grad_gate_up_blocks = send_chips(grad_gate_up_sums, shards)
    grad_down_shard = total_of(after(grad_down_blocks, grad_attended)).astype(BF)
    grad_down = lax.all_gather(grad_down_shard, "seq", axis=0, tiled=False)

    grad_q, near, far = [], [], []
    held = after(head_grad, grad_attended)
    for g in range(local_kv):
        part_q, near_kv, far_kv = flash_backward(
            head_queries, kv_all, bias, held, exact, lse, seqs, rows, g, groups
        )
        if g == 0:
            grad_gate_up_blocks = after(grad_gate_up_blocks, grad_down, part_q)
            grad_gate_up_shard = total_of(grad_gate_up_blocks).astype(BF)
            grad_gate_up_all = lax.all_gather(grad_gate_up_shard, "seq", axis=0, tiled=False)
        grad_q.append(part_q)
        near.append(near_kv)
        far.append(far_kv)
        held = after(head_grad, grad_gate_up_shard)
    grad_gate_up_all = after(grad_gate_up_all, part_q)
    pairs = kv_pair_sums(near, [hop(each, shards, 1) for each in far])
    out_far, out_near = split_product(
        after(grad_branch, part_q), attended, shard, shards
    )
    out_sums = pair_sums(out_near, after(out_far, pairs), shard, shards)
    out_blocks = send_chips(out_sums, shards)
    sent_grads, product_columns = head_columns(
        grad_q, after(send_chips(pairs, shards), out_sums), factor_local, ride_columns
    )
    token_grads = lax.all_to_all(sent_grads, "seq", split_axis=0, concat_axis=1, tiled=True)

    head_cols = q_cols + kv_cols
    head_far, head_near = split_product(product_rows, product_columns, shard, shards)
    head_sums = pair_sums(head_near, head_far, shard, shards)
    out_part = total_of(after(out_blocks, head_sums)).astype(BF)
    out_parts = lax.all_to_all(
        out_part.reshape(part, seqs, q_cols), "seq", split_axis=1, concat_axis=1, tiled=True
    )
    head_part = total_of(send_chips(head_sums, shards))
    grad_normed = dot_nt(after(token_grads, head_part), attn_full)
    grad_tokens = grad_residual + root_back(inputs, root(inputs), grad_normed)
    base_cols = head_cols + experts
    plane_high, plane_low = two_parts(
        jnp.sum(head_part[:1, base_cols : base_cols + 4], axis=1, keepdims=True)
    )
    lanes = lax.broadcasted_iota(jnp.int32, head_part.shape, 1)
    head_part = jnp.where(
        lanes == base_cols,
        plane_high.astype(F32),
        jnp.where(lanes == base_cols + 1, plane_low.astype(F32), head_part),
    )
    out_own = jnp.sum(out_parts.astype(F32), axis=1)
    final_part = jnp.concatenate([head_part, out_own], axis=1).astype(BF)
    final_part = by_rows(after(final_part, grad_gate_up_all))
    final_blocks = [by_rows(each) for each in send_out([final_part] * seqs, seqs)]
    grad_gate_up, grad_gain_ffn = place_gate_up(
        after(grad_gate_up_all, final_part), w_gate_up, gain_two
    )
    final_blocks = after(final_blocks, grad_gate_up)
    grad_query, grad_keyval, grad_out, grad_gain_attn, sums = place_heads(
        final_blocks, z, w_query, w_keyval, gain_one, q_cols, kv_cols
    )
    loss_value = jnp.sum(sums[0, experts : experts + 2]) / (width * valid_count)
    grad_router_base = sums[:, :experts]
    grad_down = (
        after(grad_down, final_part).reshape(experts, split, part, piece)
        .transpose(0, 1, 3, 2)
        .reshape(experts, units, part)
        .astype(F32)
    )
    grad_gain_ffn = grad_gain_ffn + jnp.sum(w_router.astype(F32) * grad_router_base, axis=1)
    return (
        mixed_exact.astype(BF),
        loss_value,
        grad_tokens,
        grad_gain_attn,
        grad_query,
        grad_keyval,
        grad_out.T,
        grad_gain_ffn,
        grad_router_base * gain_two,
        grad_gate_up,
        grad_down,
    )


def solution(mesh):
    return jax.shard_map(
        local,
        mesh=mesh,
        in_specs=(
            P(("seq", "fsdp"), None),
            P(("seq", "fsdp"), None),
            P(("seq", "fsdp")),
            P(("seq", "fsdp"), None),
            P(("seq", "fsdp"), None),
            P("fsdp"),
            P("fsdp", None),
            P("fsdp", None),
            P(None, "fsdp"),
            P("fsdp"),
            P("fsdp", None),
            P(None, "fsdp", None),
            P(None, None, "fsdp"),
        ),
        out_specs=(
            P(("seq", "fsdp"), None),
            P(),
            P(("seq", "fsdp"), None),
            P("fsdp"),
            P("fsdp", None),
            P("fsdp", None),
            P(None, "fsdp"),
            P("fsdp"),
            P("fsdp", None),
            P(None, "fsdp", None),
            P(None, None, "fsdp"),
        ),
        check_vma=False,
    )
```

```python
import functools
import math

import jax
import jax.numpy as jnp
from jax import lax
from jax.experimental import pallas as pl
from jax.experimental.layout import Layout, with_layout_constraint
from jax.experimental.pallas import tpu as pltpu
from jax.sharding import PartitionSpec as P

HEADS = 24
KVH = 8
HD = 64
CAP = 96
LANES = 128
EPSILON = 1e-06
FLOOR_SCORE = -1e30
BF = jnp.bfloat16
F32 = jnp.float32


def dot(a, b):
    return jnp.dot(a, b, preferred_element_type=F32)


def dot_nt(a, b):
    return lax.dot_general(a, b, (((1,), (1,)), ((), ())), preferred_element_type=F32)


def dot_tn(a, b):
    return lax.dot_general(a, b, (((0,), (0,)), ((), ())), preferred_element_type=F32)


def own_mask(valid_row, rows):
    i = lax.broadcasted_iota(jnp.int32, (rows, rows), 0)
    j = lax.broadcasted_iota(jnp.int32, (rows, rows), 1)
    return jnp.where(j == i, 0.0, jnp.where(j < i, valid_row, FLOOR_SCORE))


def key_chunk(kv_refs, zk, rows, g):
    return jnp.concatenate(
        [ref[pl.ds(zk * rows, rows), pl.ds(g * 2 * HD, 2 * HD)] for ref in kv_refs], axis=0
    )


def forward_kernel(shards, seqs, rows, local_kv, groups, *refs):
    kv_refs = refs[:shards]
    q_ref, bias_ref, low_ref, exact_ref, lse_ref, acc_ref, max_ref = refs[shards:]
    zq = pl.program_id(0)
    stack = groups * rows
    zeros = jnp.zeros((rows, HD), BF)
    half = lax.broadcasted_iota(jnp.int32, (1, 2 * HD), 1) < HD

    def queries(g):
        parts = []
        for h in range(groups):
            start = (g * groups + h) * HD
            parts.append(jnp.concatenate([q_ref[:, start : start + HD], zeros], axis=1))
        return jnp.concatenate(parts, axis=0)

    def chunk(g, zk, scores):
        first = scores is None
        keys = key_chunk(kv_refs, zk, rows, g)
        raw = dot_nt(queries(g), keys)
        if first:
            row = bias_ref[seqs + zk]
            mask = own_mask(row[:, :rows], rows)
            mask = jnp.concatenate([mask] * groups, axis=0)
            masked = jnp.concatenate([raw[:, :rows] + mask, raw[:, rows:] + row[:, rows:]], axis=1)
            new_max = jnp.max(masked, axis=1, keepdims=True)
        else:
            masked = raw + bias_ref[zk]
            new_max = jnp.maximum(max_ref[g][:, :1], jnp.max(masked, axis=1, keepdims=True))
        terms = jnp.exp(masked - new_max).astype(BF)
        ones_values = jnp.where(half, jnp.ones_like(keys), keys)
        part = dot(terms, ones_values)
        if first:
            acc_ref[g] = part
        else:
            acc_ref[g] = acc_ref[g] * jnp.exp(max_ref[g][:, :1] - new_max) + part
        max_ref[g] = jnp.broadcast_to(new_max, (stack, 2 * HD))

    for g in range(local_kv):
        chunk(g, zq, None)

    @pl.loop(0, zq)
    def _(zk):
        for g in range(local_kv):
            chunk(g, zk, True)

    exact_parts, lse_parts = [], []
    for g in range(local_kv):
        acc = acc_ref[g]
        total = acc[:, :HD]
        exact = acc[:, HD:] / total
        lse = max_ref[g][:, :HD] + jnp.log(total)
        for h in range(groups):
            exact_parts.append(exact[h * rows : (h + 1) * rows])
            lse_parts.append(lse[h * rows : (h + 1) * rows])
    exact = jnp.concatenate(exact_parts, axis=1)
    exact_ref[...] = exact
    low_ref[...] = exact.astype(BF)
    lse_ref[...] = jnp.concatenate(lse_parts, axis=1)


def flash_forward(q, kv_blocks, bias, seqs, rows, local_kv, groups):
    shards = len(kv_blocks)
    q_cols = q.shape[1]
    kv_spec = pl.BlockSpec(kv_blocks[0].shape, lambda i: (0, 0))
    q_spec = pl.BlockSpec((rows, q_cols), lambda i: (i, 0))
    stack = groups * rows
    out = jax.ShapeDtypeStruct((seqs * rows, q_cols), F32)
    return pl.pallas_call(
        functools.partial(forward_kernel, shards, seqs, rows, local_kv, groups),
        grid=(seqs,),
        in_specs=[kv_spec] * shards + [q_spec, pl.BlockSpec(bias.shape, lambda i: (0, 0, 0))],
        out_specs=[q_spec] * 3,
        out_shape=[jax.ShapeDtypeStruct((seqs * rows, q_cols), BF), out, out],
        scratch_shapes=[
            pltpu.VMEM((local_kv, stack, 2 * HD), F32),
            pltpu.VMEM((local_kv, stack, 2 * HD), F32),
        ],
        compiler_params=pltpu.CompilerParams(vmem_limit_bytes=24 * 1024 * 1024),
        cost_estimate=pl.CostEstimate(
            flops=0,
            bytes_accessed=0,
            transcendentals=0,
        ),
    )(*kv_blocks, q, bias)


def backward_kernel(shards, seqs, rows, g, groups, *refs):
    kv_refs = [refs[0].at[p] for p in range(shards)]
    (
        q_ref, bias_ref, grad_ref, exact_ref, lse_ref, grad_q_ref, near_ref, far_ref,
        pair_ref, pair_t_ref, lse_wide, delta_wide, acc_q, acc_kv,
    ) = refs[1:]
    zk = pl.program_id(0)
    stack = groups * rows
    zeros = jnp.zeros((rows, HD), BF)

    @pl.when(zk == 0)
    def _():
        acc_q[...] = jnp.zeros_like(acc_q)

        @pl.loop(0, seqs)
        def _(zq):
            here = pl.ds(zq * rows, rows)
            tops, bottoms = [], []
            for h in range(groups):
                cols = slice((g * groups + h) * HD, (g * groups + h + 1) * HD)
                grad = grad_ref[here, cols]
                tops.append(jnp.concatenate([q_ref[here, cols], zeros], axis=1))
                bottoms.append(jnp.concatenate([zeros, grad], axis=1))
                delta = jnp.sum(grad.astype(F32) * exact_ref[here, cols], axis=1, keepdims=True)
                part = slice(h * rows, (h + 1) * rows)
                delta_wide[zq, part] = jnp.broadcast_to(delta, (rows, 2 * HD))
                lse_wide[zq, part] = jnp.broadcast_to(lse_ref[here, cols][:, :1], (rows, 2 * HD))
            pair = jnp.concatenate(tops + bottoms, axis=0)
            pair_ref[zq] = pair
            pair_t_ref[zq] = pair.astype(F32).T.astype(BF)

    def chunk(zq, first):
        keys = key_chunk(kv_refs, zk, rows, g)
        both = dot_nt(pair_ref[zq], keys)
        raw, products = both[:stack], both[stack:]
        if first:
            row = bias_ref[seqs + zk]
            mask = own_mask(row[:, :rows], rows)
            mask = jnp.concatenate([mask] * groups, axis=0)
            masked = jnp.concatenate([raw[:, :rows] + mask, raw[:, rows:] + row[:, rows:]], axis=1)
        else:
            masked = raw + bias_ref[zk]
        weights = jnp.exp(masked - lse_wide[zq][:, :1])
        grads = (weights * (products - delta_wide[zq][:, :1])).astype(BF)
        acc_q[zq] += dot(grads, keys)
        part = dot(pair_t_ref[zq], jnp.concatenate([grads, weights.astype(BF)], axis=0))
        if first:
            acc_kv[...] = part
        else:
            acc_kv[...] += part

    chunk(zk, True)

    @pl.loop(zk + 1, seqs)
    def _(zq):
        chunk(zq, False)

    for p in range(shards):
        target = near_ref if p < shards // 2 else far_ref
        target[p % (shards // 2)] = acc_kv[:, p * rows : (p + 1) * rows].T.astype(BF)

    @pl.when(zk == seqs - 1)
    def _():
        @pl.loop(0, seqs)
        def _(zq):
            total = acc_q[zq]
            parts = [total[h * rows : (h + 1) * rows, :HD] for h in range(groups)]
            grad_q_ref[pl.ds(zq * rows, rows), :] = jnp.concatenate(parts, axis=1) * HD ** (-0.5)


def flash_backward(q, kv_all, bias, grad, exact, lse, seqs, rows, g, groups):
    shards = kv_all.shape[0]
    q_cols = q.shape[1]
    stack = groups * rows
    kv_spec = pl.BlockSpec(kv_all.shape, lambda i: (0, 0, 0))
    whole = pl.BlockSpec((seqs * rows, q_cols), lambda i: (0, 0))
    grad_q_shape = (seqs * rows, groups * HD)
    out_spec = pl.BlockSpec((shards // 2, rows, 2 * HD), lambda i: (0, i, 0))
    out = jax.ShapeDtypeStruct((shards // 2, seqs * rows, 2 * HD), BF)
    return pl.pallas_call(
        functools.partial(backward_kernel, shards, seqs, rows, g, groups),
        grid=(seqs,),
        in_specs=[kv_spec]
        + [whole, pl.BlockSpec(bias.shape, lambda i: (0, 0, 0)), whole, whole, whole],
        out_specs=[pl.BlockSpec(grad_q_shape, lambda i: (0, 0)), out_spec, out_spec],
        out_shape=[jax.ShapeDtypeStruct(grad_q_shape, F32), out, out],
        scratch_shapes=[
            pltpu.VMEM((seqs, 2 * stack, 2 * HD), BF),
            pltpu.VMEM((seqs, 2 * HD, 2 * stack), BF),
            pltpu.VMEM((seqs, stack, 2 * HD), F32),
            pltpu.VMEM((seqs, stack, 2 * HD), F32),
            pltpu.VMEM((seqs, stack, 2 * HD), F32),
            pltpu.VMEM((2 * HD, shards * rows), F32),
        ],
        compiler_params=pltpu.CompilerParams(vmem_limit_bytes=28 * 1024 * 1024),
        cost_estimate=pl.CostEstimate(
            flops=10**12,
            bytes_accessed=0,
            transcendentals=0,
        ),
    )(kv_all, q, bias, grad, exact, lse)


def shift(block, count, step):
    return lax.ppermute(block, "seq", [(i, (i + step) % count) for i in range(count)])


def send_out(blocks, count):
    return [blocks[0]] + [shift(blocks[s], count, s) for s in range(1, count)]


def send_back(blocks, count):
    return [blocks[0]] + [shift(blocks[s], count, count - s) for s in range(1, count)]


def relay_step(blocks, count):
    up, down = blocks
    return (
        lax.ppermute(up, "seq", [(i, i + 1) for i in range(count - 1)]),
        lax.ppermute(down, "seq", [(i + 1, i) for i in range(count - 1)]),
    )


def from_relative(blocks, place):
    count = len(blocks)
    rising = jnp.stack([blocks[-s % count] for s in range(count)])
    return lax.dynamic_slice_in_dim(jnp.concatenate([rising, rising]), count - place, count, 0)


def hop(block, count, mask):
    return lax.ppermute(block, "fsdp", [(i, i ^ mask) for i in range(count)])


def gather_shards(block, count):
    near = [block] + [hop(block, count, 2 * m) for m in range(1, count // 2)]
    return near + [hop(each, count, 1) for each in near]


def send_chips(parts, count):
    return [parts[0]] + [hop(parts[m], count, 2 * m) for m in range(1, count // 2)]


def total_of(blocks):
    total = blocks[0].astype(F32)
    for each in blocks[1:]:
        total = total + each.astype(F32)
    return total


def take(array, index, axis):
    return lax.dynamic_index_in_dim(array, index, axis, keepdims=False)


def product_kernel(core_ref, lhs_ref, rhs_ref, far_ref, near_ref):
    part = lhs_ref.shape[1] // 2
    rhs = rhs_ref[...]
    first = dot_tn(lhs_ref[:, :part], rhs).astype(BF)
    second = dot_tn(lhs_ref[:, part:], rhs).astype(BF)
    core = core_ref[0]

    @pl.when(core == 0)
    def _():
        near_ref[0] = first
        far_ref[0] = second

    @pl.when(core != 0)
    def _():
        near_ref[0] = second
        far_ref[0] = first


def split_product(lhs, rhs, shard, count):
    tokens, width = lhs.shape
    cols = rhs.shape[1]
    part = width // count
    if 2 * part % LANES:
        cut = dot_tn(lhs, rhs).astype(BF).reshape(count // 2, 2, part, cols)
        return take(cut, 1 - shard % 2, 1), take(cut, shard % 2, 1)
    out = jax.ShapeDtypeStruct((count // 2, part, cols), BF)
    out_spec = pl.BlockSpec((1, part, cols), lambda i: (i, 0, 0))
    return pl.pallas_call(
        product_kernel,
        grid=(count // 2,),
        in_specs=[
            pl.BlockSpec(memory_space=pltpu.SMEM),
            pl.BlockSpec((tokens, 2 * part), lambda i: (0, i)),
            pl.BlockSpec((tokens, cols), lambda i: (0, 0)),
        ],
        out_specs=[out_spec, out_spec],
        out_shape=[out, out],
        compiler_params=pltpu.CompilerParams(vmem_limit_bytes=24 * 1024 * 1024),
        cost_estimate=pl.CostEstimate(flops=0, bytes_accessed=0, transcendentals=0),
    )((shard % 2).astype(jnp.int32).reshape(1), lhs, rhs)


def pair_kernel(chip_ref, near_ref, there_ref, own_ref, *part_refs):
    chip = chip_ref[0]
    own_ref[...] = near_ref[chip].astype(F32) + there_ref[chip].astype(F32)
    for m, part_ref in enumerate(part_refs):
        which = chip ^ (m + 1)
        part_ref[...] = (near_ref[which].astype(F32) + there_ref[which].astype(F32)).astype(BF)


def pair_sums(near, there, shard):
    chips, part, cols = near.shape
    tile = math.gcd(cols, 512)
    if tile % LANES:
        tile = cols
    block = pl.BlockSpec((chips, part, tile), lambda i: (0, 0, i))
    out_spec = pl.BlockSpec((part, tile), lambda i: (0, i))
    out = jax.ShapeDtypeStruct((part, cols), BF)
    return pl.pallas_call(
        pair_kernel,
        grid=(cols // tile,),
        in_specs=[pl.BlockSpec(memory_space=pltpu.SMEM), block, block],
        out_specs=[out_spec] * chips,
        out_shape=[jax.ShapeDtypeStruct((part, cols), F32)] + [out] * (chips - 1),
        compiler_params=pltpu.CompilerParams(vmem_limit_bytes=24 * 1024 * 1024),
        cost_estimate=pl.CostEstimate(flops=0, bytes_accessed=0, transcendentals=0),
    )((shard // 2).astype(jnp.int32).reshape(1), near, there)


def fetch_weights(weights_ref, held, sems, piece):
    copies = [
        pltpu.make_async_copy(
            weights_ref.at[:, pl.ds(part * piece, piece)], held.at[part], sems.at[part]
        )
        for part in range(3)
    ]
    return copies


def experts_forward_kernel(count, *refs):
    rows_in, weights_ref = refs[:count], refs[count]
    rows_ref, gate_up_ref, hidden_ref = refs[count + 1 : count + 4]
    out_refs, (held, sems) = refs[count + 4 : -2], refs[-2:]
    piece = hidden_ref.shape[1]
    cap = rows_in[0].shape[0]
    copies = fetch_weights(weights_ref, held, sems, piece)
    for copy in copies:
        copy.start()
    for s in range(count):
        rows_ref[s * cap : (s + 1) * cap, :] = rows_in[s][...]
    rows = rows_ref[...]
    copies[0].wait()
    gate = dot(rows, held[0])
    gate_up_ref[:, :piece] = gate
    copies[1].wait()
    up = dot(rows, held[1])
    gate_up_ref[:, piece:] = up
    hidden = (gate / (1.0 + jnp.exp(-gate)) * up).astype(BF)
    hidden_ref[...] = hidden
    copies[2].wait()
    out = dot_nt(hidden, held[2]).astype(BF)
    for s in range(count):
        out_refs[s][...] = out[s * cap : (s + 1) * cap, :]


def experts_forward(blocks, weights, piece):
    count = len(blocks)
    cap, width = blocks[0].shape
    rows = count * cap
    in_vmem = pl.BlockSpec(memory_space=pltpu.VMEM)
    return pl.pallas_call(
        functools.partial(experts_forward_kernel, count),
        in_specs=[in_vmem] * count + [pl.BlockSpec(memory_space=pltpu.HBM)],
        out_specs=[in_vmem] * (3 + count),
        out_shape=[
            jax.ShapeDtypeStruct((rows, width), BF),
            jax.ShapeDtypeStruct((rows, 2 * piece), F32),
            jax.ShapeDtypeStruct((rows, piece), BF),
        ]
        + [jax.ShapeDtypeStruct((cap, width), BF)] * count,
        scratch_shapes=[pltpu.VMEM((3, width, piece), BF), pltpu.SemaphoreType.DMA((3,))],
        compiler_params=pltpu.CompilerParams(vmem_limit_bytes=56 * 1024 * 1024),
        cost_estimate=pl.CostEstimate(flops=0, bytes_accessed=0, transcendentals=0),
    )(*blocks, weights)


def experts_backward_kernel(count, *refs):
    grads_in, gate_up_ref, weights_ref = refs[:count], refs[count], refs[count + 1]
    grads_ref, rows_ref = refs[count + 2 : count + 4]
    out_refs, (held, sems) = refs[count + 4 : -2], refs[-2:]
    piece = rows_ref.shape[1] // 2
    cap = grads_in[0].shape[0]
    copies = fetch_weights(weights_ref, held, sems, piece)
    for copy in (copies[2], copies[0], copies[1]):
        copy.start()
    for s in range(count):
        grads_ref[s * cap : (s + 1) * cap, :] = grads_in[s][...]
    copies[2].wait()
    grad_hidden = dot(grads_ref[...], held[2])
    gate = gate_up_ref[:, :piece]
    up = gate_up_ref[:, piece:]
    slope = 1.0 / (1.0 + jnp.exp(-gate))
    grad_gate = (grad_hidden * up * slope * (1.0 + gate * (1.0 - slope))).astype(BF)
    grad_up = (grad_hidden * gate * slope).astype(BF)
    rows_ref[:, :piece] = grad_gate
    rows_ref[:, piece:] = grad_up
    copies[0].wait()
    total = dot_nt(grad_gate, held[0])
    copies[1].wait()
    total = (total + dot_nt(grad_up, held[1])).astype(BF)
    for s in range(count):
        out_refs[s][...] = total[s * cap : (s + 1) * cap, :]


def experts_backward(blocks, gate_up, weights, piece):
    count = len(blocks)
    cap, width = blocks[0].shape
    rows = count * cap
    in_vmem = pl.BlockSpec(memory_space=pltpu.VMEM)
    return pl.pallas_call(
        functools.partial(experts_backward_kernel, count),
        in_specs=[in_vmem] * (count + 1) + [pl.BlockSpec(memory_space=pltpu.HBM)],
        out_specs=[in_vmem] * (2 + count),
        out_shape=[
            jax.ShapeDtypeStruct((rows, width), BF),
            jax.ShapeDtypeStruct((rows, 2 * piece), BF),
        ]
        + [jax.ShapeDtypeStruct((cap, width), BF)] * count,
        scratch_shapes=[pltpu.VMEM((3, width, piece), BF), pltpu.SemaphoreType.DMA((3,))],
        compiler_params=pltpu.CompilerParams(vmem_limit_bytes=56 * 1024 * 1024),
        cost_estimate=pl.CostEstimate(flops=0, bytes_accessed=0, transcendentals=0),
    )(*blocks, gate_up, weights)


def kv_pair_kernel(heads, chips, *refs):
    near, there, outs = refs[:heads], refs[heads : 2 * heads], refs[2 * heads :]
    for m in range(chips):
        for g in range(heads):
            total = near[g][m].astype(F32) + there[g][m].astype(F32)
            outs[m][:, g * 2 * HD : (g + 1) * 2 * HD] = total.astype(outs[m].dtype)


def kv_pair_sums(near, there):
    heads, (chips, rows, cols) = len(near), near[0].shape
    in_vmem = pl.BlockSpec(memory_space=pltpu.VMEM)
    out = jax.ShapeDtypeStruct((rows, heads * cols), BF)
    return pl.pallas_call(
        functools.partial(kv_pair_kernel, heads, chips),
        in_specs=[in_vmem] * (2 * heads),
        out_specs=[in_vmem] * chips,
        out_shape=[jax.ShapeDtypeStruct((rows, heads * cols), F32)] + [out] * (chips - 1),
        compiler_params=pltpu.CompilerParams(vmem_limit_bytes=20 * 1024 * 1024),
        cost_estimate=pl.CostEstimate(flops=0, bytes_accessed=0, transcendentals=0),
    )(*near, *there)


def head_columns_kernel(heads, chips, *refs):
    queries, sums = refs[:heads], refs[heads : heads + chips]
    factor_ref, ride_ref, sent_ref, columns_ref = refs[heads + chips :]
    query = jnp.concatenate([each[...] for each in queries], axis=1)
    keyval = sums[0][...]
    for each in sums[1:]:
        keyval = keyval + each[...].astype(F32)
    both = jnp.concatenate([query, keyval], axis=1)
    rows, cols = both.shape
    sent_ref[...] = both.astype(BF)
    columns_ref[:rows, :cols] = (both * factor_ref[...]).astype(BF)
    columns_ref[:rows, cols:] = jnp.zeros((rows, LANES), BF)
    columns_ref[rows:, :cols] = jnp.zeros((ride_ref.shape[0], cols), BF)
    columns_ref[rows:, cols:] = ride_ref[...]


def head_columns(queries, sums, factor, ride):
    rows = sums[0].shape[0]
    cols = sum(each.shape[1] for each in queries) + sums[0].shape[1]
    if cols % LANES:
        both = jnp.concatenate(list(queries) + [total_of(sums)], axis=1)
        scaled = jnp.pad((both * factor).astype(BF), ((0, 0), (0, LANES)))
        return both.astype(BF), jnp.concatenate([scaled, jnp.pad(ride, ((0, 0), (cols, 0)))])
    in_vmem = pl.BlockSpec(memory_space=pltpu.VMEM)
    return pl.pallas_call(
        functools.partial(head_columns_kernel, len(queries), len(sums)),
        in_specs=[in_vmem] * (len(queries) + len(sums) + 2),
        out_specs=[in_vmem] * 2,
        out_shape=[
            jax.ShapeDtypeStruct((rows, cols), BF),
            jax.ShapeDtypeStruct((rows + ride.shape[0], cols + LANES), BF),
        ],
        compiler_params=pltpu.CompilerParams(vmem_limit_bytes=20 * 1024 * 1024),
        cost_estimate=pl.CostEstimate(flops=0, bytes_accessed=0, transcendentals=0),
    )(*queries, *sums, factor, ride)


def two_parts(value):
    high = value.astype(BF)
    return high, (value - high.astype(F32)).astype(BF)


def mark_kernel(seed_ref, out_ref):
    out_ref[...] = seed_ref[...]


def mark(*others):
    seed = after(jnp.zeros((8, LANES), F32), *others)
    return pl.pallas_call(
        mark_kernel,
        out_shape=jax.ShapeDtypeStruct((8, LANES), F32),
        cost_estimate=pl.CostEstimate(flops=10**12, bytes_accessed=8192, transcendentals=0),
    )(seed)


def by_rows(array):
    return with_layout_constraint(array, Layout(major_to_minor=tuple(range(array.ndim))))


def after(values, *others):
    return lax.optimization_barrier((values, others))[0]


def root(values):
    return lax.rsqrt(jnp.mean(values * values, axis=-1, keepdims=True) + EPSILON)


def root_back(values, factor, grad_scaled):
    inner = jnp.mean(grad_scaled * values, axis=-1, keepdims=True)
    return factor * grad_scaled - values * (factor * factor * factor * inner)


def place_gate_up_kernel(count, place_ref, *refs):
    blocks = refs[: 2 * count - 1]
    weight_ref, gain_ref, out_ref, sums_ref, base = refs[2 * count - 1 :]
    offset = place_ref[0] - pl.program_id(1)

    for s in range(2 * count - 1):

        @pl.when(offset == (s if s < count else count - 1 - s))
        def _(s=s):
            base[...] = blocks[s][...].astype(F32)

    @pl.when((pl.program_id(0) == 0) & (pl.program_id(1) == 0))
    def _():
        sums_ref[...] = jnp.zeros_like(sums_ref)

    values = base[...]
    out_ref[0] = values * gain_ref[...]
    product = jnp.sum(weight_ref[0].astype(F32) * values, axis=1, keepdims=True)
    sums_ref[...] += jnp.broadcast_to(product, sums_ref.shape)


def place_gate_up(steps, weight, gain, place):
    experts, part, both = weight.shape
    count = len(steps)
    split = count // experts
    if split == 1:
        tile = math.gcd(both, 1024)
        blocks = [steps[0][0]] + [each[0] for each in steps[1:]] + [each[1] for each in steps[1:]]
        block = pl.BlockSpec((part, tile), lambda t, e: (0, t))
        out, sums = pl.pallas_call(
            functools.partial(place_gate_up_kernel, count),
            grid=(both // tile, experts),
            in_specs=[pl.BlockSpec(memory_space=pltpu.SMEM)]
            + [block] * len(blocks)
            + [
                pl.BlockSpec((1, part, tile), lambda t, e: (e, 0, t)),
                pl.BlockSpec((part, 1), lambda t, e: (0, 0)),
            ],
            out_specs=[
                pl.BlockSpec((1, part, tile), lambda t, e: (e, 0, t)),
                pl.BlockSpec((part, LANES), lambda t, e: (0, 0)),
            ],
            out_shape=[
                jax.ShapeDtypeStruct(weight.shape, F32),
                jax.ShapeDtypeStruct((part, LANES), F32),
            ],
            scratch_shapes=[pltpu.VMEM((part, tile), F32)],
            compiler_params=pltpu.CompilerParams(vmem_limit_bytes=28 * 1024 * 1024),
            cost_estimate=pl.CostEstimate(flops=0, bytes_accessed=0, transcendentals=0),
        )(place.astype(jnp.int32).reshape(1), *blocks, weight, gain)
        return out, sums[:, 0]
    blocks = [steps[0][0]] + [
        jnp.where(place >= s, steps[s][0], steps[count - s][1]) for s in range(1, count)
    ]
    base = (
        from_relative(blocks, place)
        .reshape(experts, split, part, 2, both // (2 * split))
        .transpose(0, 2, 3, 1, 4)
        .reshape(experts, part, both)
        .astype(F32)
    )
    return base * gain, jnp.sum(weight.astype(F32) * base, axis=(0, 2))


def place_kernel(count, q_cols, kv_cols, place_ref, *refs):
    blocks, outs = refs[:count], refs[count : 2 * count]
    w_query_ref, w_keyval_ref, gain_ref, query_ref, keyval_ref, out_ref, base_ref, sums_ref = refs[
        2 * count :
    ]
    gain = gain_ref[...]
    base = jnp.zeros_like(gain)
    sums = jnp.zeros(sums_ref.shape, F32)
    for s in range(count):
        owner = lax.rem(place_ref[0] + (count - s), count)
        q_at = pl.ds(pl.multiple_of(owner * q_cols, LANES), q_cols)
        kv_at = pl.ds(pl.multiple_of(owner * kv_cols, LANES), kv_cols)
        query = blocks[s][:, :q_cols].astype(F32)
        keyval = blocks[s][:, q_cols : q_cols + kv_cols].astype(F32)
        start = q_cols + kv_cols
        sums = sums + blocks[s][:, start : start + LANES].astype(F32)
        out_ref[:, q_at] = outs[s][...].astype(F32)
        base = base + jnp.sum(w_query_ref[:, q_at].astype(F32) * query, axis=1, keepdims=True)
        base = base + jnp.sum(w_keyval_ref[:, kv_at].astype(F32) * keyval, axis=1, keepdims=True)
        query_ref[:, q_at] = query * gain
        keyval_ref[:, kv_at] = keyval * gain
    base_ref[...] = jnp.broadcast_to(base, base_ref.shape)
    sums_ref[...] = sums


def place_heads(blocks, outs, place, w_query, w_keyval, gain, q_cols, kv_cols):
    count = len(blocks)
    part = w_query.shape[0]
    start = q_cols + kv_cols
    if q_cols % LANES == 0 and kv_cols % LANES == 0:
        wide = jax.ShapeDtypeStruct((part, count * q_cols), F32)
        narrow = jax.ShapeDtypeStruct((part, count * kv_cols), F32)
        lanes = jax.ShapeDtypeStruct((part, LANES), F32)
        in_vmem = pl.BlockSpec(memory_space=pltpu.VMEM)
        query, keyval, out, base, sums = pl.pallas_call(
            functools.partial(place_kernel, count, q_cols, kv_cols),
            in_specs=[pl.BlockSpec(memory_space=pltpu.SMEM)] + [in_vmem] * (2 * count + 3),
            out_specs=[in_vmem] * 5,
            out_shape=[wide, narrow, wide, lanes, lanes],
            compiler_params=pltpu.CompilerParams(vmem_limit_bytes=24 * 1024 * 1024),
            cost_estimate=pl.CostEstimate(flops=0, bytes_accessed=0, transcendentals=0),
        )(place.astype(jnp.int32).reshape(1), *blocks, *outs, w_query, w_keyval, gain)
        return query, keyval, out, base[:, 0], sums
    blocks = from_relative(blocks, place).astype(F32)
    outs = from_relative(outs, place).astype(F32)

    def columns(begin, end):
        return blocks[:, :, begin:end].transpose(1, 0, 2).reshape(part, count * (end - begin))

    query, keyval = columns(0, q_cols), columns(q_cols, start)
    base = jnp.sum(w_query.astype(F32) * query, axis=1) + jnp.sum(
        w_keyval.astype(F32) * keyval, axis=1
    )
    sums = jnp.sum(blocks[:, :, start : start + LANES], axis=0)
    out = outs.transpose(1, 0, 2).reshape(part, count * q_cols)
    return query * gain, keyval * gain, out, base, sums


def local(
    tokens,
    teacher,
    valid,
    routes,
    slots,
    gain_attn,
    w_query,
    w_keyval,
    w_out,
    gain_ffn,
    w_router,
    w_gate_up,
    w_down,
):
    seqs = lax.axis_size("seq")
    shards = lax.axis_size("fsdp")
    z = lax.axis_index("seq")
    shard = lax.axis_index("fsdp")
    rows, width = tokens.shape
    groups = HEADS // KVH
    local_kv = KVH // seqs
    q_cols = local_kv * groups * HD
    kv_cols = local_kv * 2 * HD
    local_rows = rows * seqs
    seq_len = local_rows * shards
    experts, part, both = w_gate_up.shape
    units = both // 2
    split = seqs // experts
    piece = units // split
    expert = z // split
    fraction = z % split
    scale = HD ** (-0.5)

    gain_one = gain_attn.astype(F32)[:, None]
    gain_two = gain_ffn.astype(F32)[:, None]
    heads_shard = jnp.concatenate(
        [
            lax.dynamic_slice_in_dim(w_query, z * q_cols, q_cols, 1),
            lax.dynamic_slice_in_dim(w_keyval, z * kv_cols, kv_cols, 1),
        ],
        axis=1,
    )
    heads_shard = (heads_shard.astype(F32) * gain_one).astype(BF)
    heads_full = lax.all_gather(heads_shard, "fsdp", axis=0, tiled=True)
    valid_row = jnp.pad(valid.astype(BF).reshape(1, rows), ((0, 7), (0, width - rows)))
    token_rows = jnp.concatenate([tokens, valid_row], axis=0)
    token_mark = mark(token_rows)
    token_blocks = after(send_out([token_rows] * seqs, seqs), token_mark)

    valid_local = from_relative([each[rows : rows + 1, :rows] for each in token_blocks], z)
    projected = []
    for block in token_blocks:
        projected.append(dot(block[:rows], heads_full) * root(block[:rows].astype(F32)))
    projected = from_relative([each.astype(BF) for each in projected], z)
    projected = projected.reshape(local_rows, q_cols + kv_cols)
    head_queries = projected[:, :q_cols] * jnp.asarray(scale, BF)

    valid_rows_kv = local_rows // kv_cols
    payload = jnp.concatenate(
        [
            projected[:, q_cols:],
            valid_local.reshape(valid_rows_kv, kv_cols),
            jnp.zeros((16 - valid_rows_kv, kv_cols), BF),
        ],
        axis=0,
    )
    kv_blocks = gather_shards(payload, shards)
    late_query, late_keyval, late_router, late_gate_up, late_down = after(
        (w_query, w_keyval, w_router, w_gate_up, w_down), token_mark
    )
    out_full = lax.all_gather(w_out, "fsdp", axis=1, tiled=True)
    own_expert = take(late_gate_up, expert, 0)
    gate_shard = lax.dynamic_slice_in_dim(own_expert, fraction * piece, piece, 1)
    up_shard = lax.dynamic_slice_in_dim(own_expert, units + fraction * piece, piece, 1)
    down_shard = lax.dynamic_slice_in_dim(take(late_down, expert, 0), fraction * piece, piece, 0).T
    router_shard = jnp.pad((late_router.astype(F32) * gain_two).astype(BF), ((0, 0), (0, LANES - experts)))
    expert_shard = jnp.concatenate(
        [
            (gate_shard.astype(F32) * gain_two).astype(BF),
            (up_shard.astype(F32) * gain_two).astype(BF),
            down_shard,
            router_shard,
        ],
        axis=1,
    )
    expert_full = lax.all_gather(expert_shard, "fsdp", axis=0, tiled=True)
    router_full = expert_full[:, 3 * piece :]
    attn_shard = jnp.concatenate(
        [
            each
            for s in range(seqs)
            for each in (
                late_query[:, s * q_cols : (s + 1) * q_cols],
                late_keyval[:, s * kv_cols : (s + 1) * kv_cols],
            )
        ],
        axis=1,
    )
    attn_full = lax.all_gather(
        (attn_shard.astype(F32) * gain_one).astype(BF), "fsdp", axis=0, tiled=True
    )
    order = jnp.asarray(
        [2 * m for m in range(shards // 2)] + [2 * m + 1 for m in range(shards // 2)], jnp.int32
    )
    valid_all = jnp.stack(
        [
            each[local_rows : local_rows + valid_rows_kv].reshape(seqs, rows)
            for each in kv_blocks
        ],
        axis=1,
    ).astype(F32)
    valid_count = jnp.sum(valid_all)
    bias = jnp.where(valid_all > 0, 0.0, FLOOR_SCORE)
    earlier = ((order ^ shard) < shard) | (order == 0)
    bias_same = jnp.where(earlier[None, :, None], bias, FLOOR_SCORE)
    bias = jnp.concatenate([bias, bias_same]).reshape(2 * seqs, 1, shards * rows)
    attended_low, exact, lse = flash_forward(
        head_queries, kv_blocks, bias, seqs, rows, local_kv, groups
    )
    attended = lax.all_to_all(attended_low, "seq", split_axis=0, concat_axis=1, tiled=True)

    inputs = tokens.astype(F32)
    residual = inputs + dot(attended, out_full)
    factor_two = root(residual)
    normed_two = (residual * factor_two).astype(BF)
    logits = dot(normed_two, router_full)[:, :experts]
    expert_ids = jnp.arange(experts, dtype=jnp.int32)
    picked = (routes[:, :, None] == expert_ids).astype(F32)
    chosen = jnp.sum(picked * logits[:, None, :], axis=-1)
    gating = jax.nn.softmax(chosen, axis=-1)
    owners = ((jnp.arange(seqs, dtype=jnp.int32) + z) % seqs) // split
    to_owner = routes[:, :, None] == owners
    slot_hot = slots[:, :, None] == jnp.arange(CAP, dtype=jnp.int32)
    placed = (to_owner[:, :, :, None] & slot_hot[:, :, None, :]).astype(BF)
    placed = placed.reshape(rows, 2, seqs * CAP)
    dispatch = placed[:, 0] + placed[:, 1]
    placed_pairs = jnp.concatenate([placed[:, 0], placed[:, 1]], axis=0)
    sent_rows = dot_tn(dispatch, normed_two).astype(BF)
    kv_all = jnp.stack(after(kv_blocks, sent_rows))
    sent_rows = sent_rows.reshape(seqs, CAP, width)
    expert_rows, gate_up, hidden, *expert_out = experts_forward(
        send_out([sent_rows[s] for s in range(seqs)], seqs), expert_full, piece
    )
    returned = jnp.concatenate(after(send_back(expert_out, seqs), kv_all))
    selected = dot(placed_pairs, returned).reshape(2, rows, width)
    mixed_exact = residual + gating[:, :1] * selected[0] + gating[:, 1:] * selected[1]
    valid_rows = valid.astype(F32)
    errors = (mixed_exact - teacher.astype(F32)) * valid_rows[:, None]
    squares = jnp.sum(errors * errors)
    loss_scale = width * seq_len // 8
    grad_mixed = errors * (2.0 * loss_scale / (width * valid_count))

    grad_gating = jnp.stack(
        [jnp.sum(selected[0] * grad_mixed, axis=-1), jnp.sum(selected[1] * grad_mixed, axis=-1)],
        axis=1,
    )
    grad_chosen = gating * (grad_gating - jnp.sum(gating * grad_gating, axis=-1, keepdims=True))
    grad_logits = jnp.sum(grad_chosen[:, :, None] * picked, axis=1).astype(BF)
    grad_logits = jnp.pad(grad_logits, ((0, 0), (0, LANES - experts)))
    weighted = jnp.concatenate(
        [(gating[:, :1] * grad_mixed).astype(BF), (gating[:, 1:] * grad_mixed).astype(BF)], axis=0
    )
    sent_grads = dot_tn(placed_pairs, weighted).astype(BF).reshape(seqs, CAP, width)
    grad_out_rows = send_out([sent_grads[s] for s in range(seqs)], seqs)
    grad_out_rows = after(grad_out_rows, attn_full, grad_logits)
    grad_expert_out, grad_gate_up_rows, *grad_rows = experts_backward(
        grad_out_rows, gate_up, expert_full, piece
    )
    grad_returned = send_back(grad_rows, seqs)
    tokens_local = from_relative(
        [each[:rows] for each in after(token_blocks, grad_rows)], z
    ).reshape(local_rows, width)
    factor_local = root(tokens_local.astype(F32))
    ride_rows = jnp.concatenate([normed_two, jnp.ones((16, width), BF)], axis=0)
    product_rows = jnp.concatenate([tokens_local, ride_rows], axis=0)
    high, low = two_parts(squares)
    lane = jnp.arange(LANES, dtype=jnp.int32)[None, :]
    marks = jnp.where(lane == experts + 2 * (shard % 2), high, 0) + jnp.where(
        lane == experts + 1 + 2 * (shard % 2), low, 0
    )
    ride_columns = jnp.concatenate(
        [grad_logits, marks.astype(BF), jnp.zeros((15, LANES), BF)], axis=0
    )
    held_out, held_hidden = after((grad_expert_out, hidden), grad_rows)
    down_far, down_near = split_product(held_out, held_hidden, shard, shards)
    grad_down_sums = pair_sums(down_near, hop(down_far, shards, 1), shard)
    held_rows, held_gate_up = after((expert_rows, grad_gate_up_rows), grad_rows)
    gate_up_far, gate_up_near = split_product(held_rows, held_gate_up, shard, shards)
    grad_gate_up_sums = pair_sums(gate_up_near, hop(gate_up_far, shards, 1), shard)
    grad_down_blocks = send_chips(grad_down_sums, shards)
    grad_returned = jnp.concatenate(after(grad_returned, grad_down_sums, product_rows, ride_columns, factor_local))
    grad_normed_two = dot(dispatch, grad_returned) + dot_nt(grad_logits, router_full)
    grad_residual = grad_mixed + root_back(residual, factor_two, grad_normed_two)
    grad_branch = grad_residual.astype(BF)
    grad_attended = dot_nt(after(grad_branch, grad_gate_up_sums), out_full).astype(BF)
    head_grad = lax.all_to_all(grad_attended, "seq", split_axis=1, concat_axis=0, tiled=True)
    grad_gate_up_blocks = send_chips(grad_gate_up_sums, shards)
    grad_down_shard = total_of(after(grad_down_blocks, grad_attended)).astype(BF)
    grad_down = lax.all_gather(grad_down_shard, "seq", axis=0, tiled=False)

    out_far, out_near = split_product(
        after(grad_branch, grad_attended), attended, shard, shards
    )
    grad_q, near, far = [], [], []
    held = after(head_grad, grad_down_shard)
    for g in range(local_kv):
        part_q, near_kv, far_kv = flash_backward(
            head_queries, kv_all, bias, held, exact, lse, seqs, rows, g, groups
        )
        if g == 0:
            grad_gate_up_blocks = after(grad_gate_up_blocks, grad_down, part_q)
            grad_gate_up_shard = total_of(grad_gate_up_blocks).astype(BF)
            steps = [(grad_gate_up_shard, grad_gate_up_shard)]
            steps.append(relay_step(steps[0], seqs))
            out_there = hop(after(out_far, head_grad), shards, 1)
        grad_q.append(part_q)
        near.append(near_kv)
        far.append(far_kv)
        held = after(head_grad, grad_gate_up_shard, out_there)
    steps[1] = after(steps[1], part_q)
    steps.append(relay_step(steps[1], seqs))
    far = after(far, steps[1])
    pairs = kv_pair_sums(near, [hop(each, shards, 1) for each in far])
    out_sums = pair_sums(out_near, after(out_there, pairs), shard)
    sent_grads, product_columns = head_columns(
        grad_q, after(send_chips(pairs, shards), out_sums, steps[2]), factor_local, ride_columns
    )
    steps[2] = after(steps[2], product_columns)
    while len(steps) < seqs:
        steps.append(relay_step(steps[-1], seqs))
    token_grads = lax.all_to_all(sent_grads, "seq", split_axis=0, concat_axis=1, tiled=True)

    head_cols = q_cols + kv_cols
    head_far, head_near = split_product(product_rows, product_columns, shard, shards)
    head_sums = pair_sums(head_near, hop(head_far, shards, 1), shard)
    out_part = total_of(
        after(send_chips(after(out_sums, product_columns), shards), head_sums)
    ).astype(BF)
    out_parts = lax.all_to_all(
        out_part.reshape(part, seqs, q_cols), "seq", split_axis=1, concat_axis=1, tiled=True
    )
    out_own = by_rows(jnp.sum(out_parts.astype(F32), axis=1).astype(BF))
    out_last = [by_rows(each) for each in send_out([out_own] * seqs, seqs)]
    head_part = total_of(after(send_chips(head_sums, shards), steps[3]))
    grad_normed = dot_nt(after(token_grads, head_part), attn_full)
    grad_tokens = grad_residual + root_back(inputs, root(inputs), grad_normed)
    base_cols = head_cols + experts
    plane_high, plane_low = two_parts(
        jnp.sum(head_part[:1, base_cols : base_cols + 4], axis=1, keepdims=True)
    )
    lanes = lax.broadcasted_iota(jnp.int32, head_part.shape, 1)
    head_part = jnp.where(
        lanes == base_cols,
        plane_high.astype(F32),
        jnp.where(lanes == base_cols + 1, plane_low.astype(F32), head_part),
    )
    head_part = by_rows(head_part.astype(BF))
    head_last = [by_rows(each) for each in send_out([head_part] * seqs, seqs)]
    grad_gate_up, grad_gain_ffn = place_gate_up(after(steps, head_part), w_gate_up, gain_two, z)
    head_last, out_last = after((head_last, out_last), grad_gate_up)
    grad_query, grad_keyval, grad_out, grad_gain_attn, sums = place_heads(
        head_last, out_last, z, w_query, w_keyval, gain_one, q_cols, kv_cols
    )
    loss_value = jnp.sum(sums[0, experts : experts + 2]) / (width * valid_count)
    grad_router_base = sums[:, :experts]
    grad_down = (
        after(grad_down, head_part).reshape(experts, split, part, piece)
        .transpose(0, 1, 3, 2)
        .reshape(experts, units, part)
        .astype(F32)
    )
    grad_gain_ffn = grad_gain_ffn + jnp.sum(w_router.astype(F32) * grad_router_base, axis=1)
    return (
        mixed_exact.astype(BF),
        loss_value,
        grad_tokens,
        grad_gain_attn,
        grad_query,
        grad_keyval,
        grad_out.T,
        grad_gain_ffn,
        grad_router_base * gain_two,
        grad_gate_up,
        grad_down,
    )


def solution(mesh):
    return jax.shard_map(
        local,
        mesh=mesh,
        in_specs=(
            P(("seq", "fsdp"), None),
            P(("seq", "fsdp"), None),
            P(("seq", "fsdp")),
            P(("seq", "fsdp"), None),
            P(("seq", "fsdp"), None),
            P("fsdp"),
            P("fsdp", None),
            P("fsdp", None),
            P(None, "fsdp"),
            P("fsdp"),
            P("fsdp", None),
            P(None, "fsdp", None),
            P(None, None, "fsdp"),
        ),
        out_specs=(
            P(("seq", "fsdp"), None),
            P(),
            P(("seq", "fsdp"), None),
            P("fsdp"),
            P("fsdp", None),
            P("fsdp", None),
            P(None, "fsdp"),
            P("fsdp"),
            P("fsdp", None),
            P(None, "fsdp", None),
            P(None, None, "fsdp"),
        ),
        check_vma=False,
    )
```

```python
import functools
import math

import jax
import jax.numpy as jnp
from jax import lax
from jax.experimental import pallas as pl
from jax.experimental.layout import Layout, with_layout_constraint
from jax.experimental.pallas import tpu as pltpu
from jax.sharding import PartitionSpec as P

HEADS = 24
KVH = 8
HD = 64
CAP = 96
LANES = 128
EPSILON = 1e-06
FLOOR_SCORE = -1e30
BF = jnp.bfloat16
F32 = jnp.float32


def dot(a, b):
    return jnp.dot(a, b, preferred_element_type=F32)


def dot_nt(a, b):
    return lax.dot_general(a, b, (((1,), (1,)), ((), ())), preferred_element_type=F32)


def dot_tn(a, b):
    return lax.dot_general(a, b, (((0,), (0,)), ((), ())), preferred_element_type=F32)


def own_mask(valid_row, rows):
    i = lax.broadcasted_iota(jnp.int32, (rows, rows), 0)
    j = lax.broadcasted_iota(jnp.int32, (rows, rows), 1)
    return jnp.where(j == i, 0.0, jnp.where(j < i, valid_row, FLOOR_SCORE))


def key_chunk(kv_refs, zk, rows, g):
    return jnp.concatenate(
        [ref[pl.ds(zk * rows, rows), pl.ds(g * 2 * HD, 2 * HD)] for ref in kv_refs], axis=0
    )


def forward_kernel(shards, seqs, rows, local_kv, groups, *refs):
    kv_refs = refs[:shards]
    q_ref, bias_ref, low_ref, exact_ref, lse_ref, acc_ref, max_ref = refs[shards:]
    zq = pl.program_id(0)
    stack = groups * rows
    zeros = jnp.zeros((rows, HD), BF)
    half = lax.broadcasted_iota(jnp.int32, (1, 2 * HD), 1) < HD

    def queries(g):
        parts = []
        for h in range(groups):
            start = (g * groups + h) * HD
            parts.append(jnp.concatenate([q_ref[:, start : start + HD], zeros], axis=1))
        return jnp.concatenate(parts, axis=0)

    def chunk(g, zk, scores):
        first = scores is None
        keys = key_chunk(kv_refs, zk, rows, g)
        raw = dot_nt(queries(g), keys)
        if first:
            row = bias_ref[seqs + zk]
            mask = own_mask(row[:, :rows], rows)
            mask = jnp.concatenate([mask] * groups, axis=0)
            masked = jnp.concatenate([raw[:, :rows] + mask, raw[:, rows:] + row[:, rows:]], axis=1)
            new_max = jnp.max(masked, axis=1, keepdims=True)
        else:
            masked = raw + bias_ref[zk]
            new_max = jnp.maximum(max_ref[g][:, :1], jnp.max(masked, axis=1, keepdims=True))
        terms = jnp.exp(masked - new_max).astype(BF)
        ones_values = jnp.where(half, jnp.ones_like(keys), keys)
        part = dot(terms, ones_values)
        if first:
            acc_ref[g] = part
        else:
            acc_ref[g] = acc_ref[g] * jnp.exp(max_ref[g][:, :1] - new_max) + part
        max_ref[g] = jnp.broadcast_to(new_max, (stack, 2 * HD))

    for g in range(local_kv):
        chunk(g, zq, None)

    @pl.loop(0, zq)
    def _(zk):
        for g in range(local_kv):
            chunk(g, zk, True)

    exact_parts, lse_parts = [], []
    for g in range(local_kv):
        acc = acc_ref[g]
        total = acc[:, :HD]
        exact = acc[:, HD:] / total
        lse = max_ref[g][:, :HD] + jnp.log(total)
        for h in range(groups):
            exact_parts.append(exact[h * rows : (h + 1) * rows])
            lse_parts.append(lse[h * rows : (h + 1) * rows])
    exact = jnp.concatenate(exact_parts, axis=1)
    exact_ref[...] = exact
    low_ref[...] = exact.astype(BF)
    lse_ref[...] = jnp.concatenate(lse_parts, axis=1)


def flash_forward(q, kv_blocks, bias, seqs, rows, local_kv, groups):
    shards = len(kv_blocks)
    q_cols = q.shape[1]
    kv_spec = pl.BlockSpec(kv_blocks[0].shape, lambda i: (0, 0))
    q_spec = pl.BlockSpec((rows, q_cols), lambda i: (i, 0))
    stack = groups * rows
    out = jax.ShapeDtypeStruct((seqs * rows, q_cols), F32)
    return pl.pallas_call(
        functools.partial(forward_kernel, shards, seqs, rows, local_kv, groups),
        grid=(seqs,),
        in_specs=[kv_spec] * shards + [q_spec, pl.BlockSpec(bias.shape, lambda i: (0, 0, 0))],
        out_specs=[q_spec] * 3,
        out_shape=[jax.ShapeDtypeStruct((seqs * rows, q_cols), BF), out, out],
        scratch_shapes=[
            pltpu.VMEM((local_kv, stack, 2 * HD), F32),
            pltpu.VMEM((local_kv, stack, 2 * HD), F32),
        ],
        compiler_params=pltpu.CompilerParams(vmem_limit_bytes=24 * 1024 * 1024),
        cost_estimate=pl.CostEstimate(
            flops=0,
            bytes_accessed=0,
            transcendentals=0,
        ),
    )(*kv_blocks, q, bias)


def backward_kernel(shards, seqs, rows, g, groups, *refs):
    kv_refs = [refs[0].at[p] for p in range(shards)]
    (
        q_ref, bias_ref, grad_ref, exact_ref, lse_ref, grad_q_ref, near_ref, far_ref,
        pair_ref, pair_t_ref, lse_wide, delta_wide, acc_q, acc_kv,
    ) = refs[1:]
    zk = pl.program_id(0)
    stack = groups * rows
    zeros = jnp.zeros((rows, HD), BF)

    @pl.when(zk == 0)
    def _():
        acc_q[...] = jnp.zeros_like(acc_q)

        @pl.loop(0, seqs)
        def _(zq):
            here = pl.ds(zq * rows, rows)
            tops, bottoms = [], []
            for h in range(groups):
                cols = slice((g * groups + h) * HD, (g * groups + h + 1) * HD)
                grad = grad_ref[here, cols]
                tops.append(jnp.concatenate([q_ref[here, cols], zeros], axis=1))
                bottoms.append(jnp.concatenate([zeros, grad], axis=1))
                delta = jnp.sum(grad.astype(F32) * exact_ref[here, cols], axis=1, keepdims=True)
                part = slice(h * rows, (h + 1) * rows)
                delta_wide[zq, part] = jnp.broadcast_to(delta, (rows, 2 * HD))
                lse_wide[zq, part] = jnp.broadcast_to(lse_ref[here, cols][:, :1], (rows, 2 * HD))
            pair = jnp.concatenate(tops + bottoms, axis=0)
            pair_ref[zq] = pair
            pair_t_ref[zq] = pair.astype(F32).T.astype(BF)

    def chunk(zq, first):
        keys = key_chunk(kv_refs, zk, rows, g)
        both = dot_nt(pair_ref[zq], keys)
        raw, products = both[:stack], both[stack:]
        if first:
            row = bias_ref[seqs + zk]
            mask = own_mask(row[:, :rows], rows)
            mask = jnp.concatenate([mask] * groups, axis=0)
            masked = jnp.concatenate([raw[:, :rows] + mask, raw[:, rows:] + row[:, rows:]], axis=1)
        else:
            masked = raw + bias_ref[zk]
        weights = jnp.exp(masked - lse_wide[zq][:, :1])
        grads = (weights * (products - delta_wide[zq][:, :1])).astype(BF)
        acc_q[zq] += dot(grads, keys)
        part = dot(pair_t_ref[zq], jnp.concatenate([grads, weights.astype(BF)], axis=0))
        if first:
            acc_kv[...] = part
        else:
            acc_kv[...] += part

    chunk(zk, True)

    @pl.loop(zk + 1, seqs)
    def _(zq):
        chunk(zq, False)

    for p in range(shards):
        target = near_ref if p < shards // 2 else far_ref
        target[p % (shards // 2)] = acc_kv[:, p * rows : (p + 1) * rows].T.astype(BF)

    @pl.when(zk == seqs - 1)
    def _():
        @pl.loop(0, seqs)
        def _(zq):
            total = acc_q[zq]
            parts = [total[h * rows : (h + 1) * rows, :HD] for h in range(groups)]
            grad_q_ref[pl.ds(zq * rows, rows), :] = jnp.concatenate(parts, axis=1) * HD ** (-0.5)


def flash_backward(q, kv_all, bias, grad, exact, lse, seqs, rows, g, groups):
    shards = kv_all.shape[0]
    q_cols = q.shape[1]
    stack = groups * rows
    kv_spec = pl.BlockSpec(kv_all.shape, lambda i: (0, 0, 0))
    whole = pl.BlockSpec((seqs * rows, q_cols), lambda i: (0, 0))
    grad_q_shape = (seqs * rows, groups * HD)
    out_spec = pl.BlockSpec((shards // 2, rows, 2 * HD), lambda i: (0, i, 0))
    out = jax.ShapeDtypeStruct((shards // 2, seqs * rows, 2 * HD), BF)
    return pl.pallas_call(
        functools.partial(backward_kernel, shards, seqs, rows, g, groups),
        grid=(seqs,),
        in_specs=[kv_spec]
        + [whole, pl.BlockSpec(bias.shape, lambda i: (0, 0, 0)), whole, whole, whole],
        out_specs=[pl.BlockSpec(grad_q_shape, lambda i: (0, 0)), out_spec, out_spec],
        out_shape=[jax.ShapeDtypeStruct(grad_q_shape, F32), out, out],
        scratch_shapes=[
            pltpu.VMEM((seqs, 2 * stack, 2 * HD), BF),
            pltpu.VMEM((seqs, 2 * HD, 2 * stack), BF),
            pltpu.VMEM((seqs, stack, 2 * HD), F32),
            pltpu.VMEM((seqs, stack, 2 * HD), F32),
            pltpu.VMEM((seqs, stack, 2 * HD), F32),
            pltpu.VMEM((2 * HD, shards * rows), F32),
        ],
        compiler_params=pltpu.CompilerParams(vmem_limit_bytes=28 * 1024 * 1024),
        cost_estimate=pl.CostEstimate(
            flops=0 if g else 10**12,
            bytes_accessed=0,
            transcendentals=0,
        ),
    )(kv_all, q, bias, grad, exact, lse)


def shift(block, count, step):
    return lax.ppermute(block, "seq", [(i, (i + step) % count) for i in range(count)])


def send_out(blocks, count):
    return [blocks[0]] + [shift(blocks[s], count, s) for s in range(1, count)]


def send_back(blocks, count):
    return [blocks[0]] + [shift(blocks[s], count, count - s) for s in range(1, count)]


def relay_step(blocks, count):
    up, down = blocks
    return (
        lax.ppermute(up, "seq", [(i, i + 1) for i in range(count - 1)]),
        lax.ppermute(down, "seq", [(i + 1, i) for i in range(count - 1)]),
    )


def from_relative(blocks, place):
    count = len(blocks)
    rising = jnp.stack([blocks[-s % count] for s in range(count)])
    return lax.dynamic_slice_in_dim(jnp.concatenate([rising, rising]), count - place, count, 0)


def hop(block, count, mask):
    return lax.ppermute(block, "fsdp", [(i, i ^ mask) for i in range(count)])


def gather_shards(block, count):
    near = [block] + [hop(block, count, 2 * m) for m in range(1, count // 2)]
    return near + [hop(each, count, 1) for each in near]


def send_chips(parts, count):
    return [parts[0]] + [hop(parts[m], count, 2 * m) for m in range(1, count // 2)]


def total_of(blocks):
    total = blocks[0].astype(F32)
    for each in blocks[1:]:
        total = total + each.astype(F32)
    return total


def take(array, index, axis):
    return lax.dynamic_index_in_dim(array, index, axis, keepdims=False)


def product_kernel(core_ref, lhs_ref, rhs_ref, far_ref, near_ref):
    part = lhs_ref.shape[1] // 2
    rhs = rhs_ref[...]
    first = dot_tn(lhs_ref[:, :part], rhs).astype(BF)
    second = dot_tn(lhs_ref[:, part:], rhs).astype(BF)
    core = core_ref[0]

    @pl.when(core == 0)
    def _():
        near_ref[0] = first
        far_ref[0] = second

    @pl.when(core != 0)
    def _():
        near_ref[0] = second
        far_ref[0] = first


def split_product(lhs, rhs, shard, count):
    tokens, width = lhs.shape
    cols = rhs.shape[1]
    part = width // count
    if 2 * part % LANES:
        cut = dot_tn(lhs, rhs).astype(BF).reshape(count // 2, 2, part, cols)
        return take(cut, 1 - shard % 2, 1), take(cut, shard % 2, 1)
    out = jax.ShapeDtypeStruct((count // 2, part, cols), BF)
    out_spec = pl.BlockSpec((1, part, cols), lambda i: (i, 0, 0))
    return pl.pallas_call(
        product_kernel,
        grid=(count // 2,),
        in_specs=[
            pl.BlockSpec(memory_space=pltpu.SMEM),
            pl.BlockSpec((tokens, 2 * part), lambda i: (0, i)),
            pl.BlockSpec((tokens, cols), lambda i: (0, 0)),
        ],
        out_specs=[out_spec, out_spec],
        out_shape=[out, out],
        compiler_params=pltpu.CompilerParams(vmem_limit_bytes=24 * 1024 * 1024),
        cost_estimate=pl.CostEstimate(flops=0, bytes_accessed=0, transcendentals=0),
    )((shard % 2).astype(jnp.int32).reshape(1), lhs, rhs)


def pair_kernel(chip_ref, near_ref, there_ref, own_ref, *part_refs):
    chip = chip_ref[0]
    own_ref[...] = near_ref[chip].astype(F32) + there_ref[chip].astype(F32)
    for m, part_ref in enumerate(part_refs):
        which = chip ^ (m + 1)
        part_ref[...] = (near_ref[which].astype(F32) + there_ref[which].astype(F32)).astype(BF)


def pair_sums(near, there, shard):
    chips, part, cols = near.shape
    tile = math.gcd(cols, 512)
    if tile % LANES:
        tile = cols
    block = pl.BlockSpec((chips, part, tile), lambda i: (0, 0, i))
    out_spec = pl.BlockSpec((part, tile), lambda i: (0, i))
    out = jax.ShapeDtypeStruct((part, cols), BF)
    return pl.pallas_call(
        pair_kernel,
        grid=(cols // tile,),
        in_specs=[pl.BlockSpec(memory_space=pltpu.SMEM), block, block],
        out_specs=[out_spec] * chips,
        out_shape=[jax.ShapeDtypeStruct((part, cols), F32)] + [out] * (chips - 1),
        compiler_params=pltpu.CompilerParams(vmem_limit_bytes=24 * 1024 * 1024),
        cost_estimate=pl.CostEstimate(flops=0, bytes_accessed=0, transcendentals=0),
    )((shard // 2).astype(jnp.int32).reshape(1), near, there)


def fetch_weights(weights_ref, held, sems, piece):
    copies = [
        pltpu.make_async_copy(
            weights_ref.at[:, pl.ds(part * piece, piece)], held.at[part], sems.at[part]
        )
        for part in range(3)
    ]
    return copies


def experts_forward_kernel(count, *refs):
    rows_in, weights_ref = refs[:count], refs[count]
    rows_ref, gate_up_ref, hidden_ref = refs[count + 1 : count + 4]
    out_refs, (held, sems) = refs[count + 4 : -2], refs[-2:]
    piece = hidden_ref.shape[1]
    cap = rows_in[0].shape[0]
    copies = fetch_weights(weights_ref, held, sems, piece)
    for copy in copies:
        copy.start()
    for s in range(count):
        rows_ref[s * cap : (s + 1) * cap, :] = rows_in[s][...]
    rows = rows_ref[...]
    copies[0].wait()
    gate = dot(rows, held[0])
    gate_up_ref[:, :piece] = gate
    copies[1].wait()
    up = dot(rows, held[1])
    gate_up_ref[:, piece:] = up
    hidden = (gate / (1.0 + jnp.exp(-gate)) * up).astype(BF)
    hidden_ref[...] = hidden
    copies[2].wait()
    out = dot_nt(hidden, held[2]).astype(BF)
    for s in range(count):
        out_refs[s][...] = out[s * cap : (s + 1) * cap, :]


def experts_forward(blocks, weights, piece):
    count = len(blocks)
    cap, width = blocks[0].shape
    rows = count * cap
    in_vmem = pl.BlockSpec(memory_space=pltpu.VMEM)
    return pl.pallas_call(
        functools.partial(experts_forward_kernel, count),
        in_specs=[in_vmem] * count + [pl.BlockSpec(memory_space=pltpu.HBM)],
        out_specs=[in_vmem] * (3 + count),
        out_shape=[
            jax.ShapeDtypeStruct((rows, width), BF),
            jax.ShapeDtypeStruct((rows, 2 * piece), F32),
            jax.ShapeDtypeStruct((rows, piece), BF),
        ]
        + [jax.ShapeDtypeStruct((cap, width), BF)] * count,
        scratch_shapes=[pltpu.VMEM((3, width, piece), BF), pltpu.SemaphoreType.DMA((3,))],
        compiler_params=pltpu.CompilerParams(vmem_limit_bytes=56 * 1024 * 1024),
        cost_estimate=pl.CostEstimate(flops=0, bytes_accessed=0, transcendentals=0),
    )(*blocks, weights)


def experts_backward_kernel(count, *refs):
    grads_in, gate_up_ref, weights_ref = refs[:count], refs[count], refs[count + 1]
    grads_ref, rows_ref = refs[count + 2 : count + 4]
    out_refs, (held, sems) = refs[count + 4 : -2], refs[-2:]
    piece = rows_ref.shape[1] // 2
    cap = grads_in[0].shape[0]
    copies = fetch_weights(weights_ref, held, sems, piece)
    for copy in (copies[2], copies[0], copies[1]):
        copy.start()
    for s in range(count):
        grads_ref[s * cap : (s + 1) * cap, :] = grads_in[s][...]
    copies[2].wait()
    grad_hidden = dot(grads_ref[...], held[2])
    gate = gate_up_ref[:, :piece]
    up = gate_up_ref[:, piece:]
    slope = 1.0 / (1.0 + jnp.exp(-gate))
    grad_gate = (grad_hidden * up * slope * (1.0 + gate * (1.0 - slope))).astype(BF)
    grad_up = (grad_hidden * gate * slope).astype(BF)
    rows_ref[:, :piece] = grad_gate
    rows_ref[:, piece:] = grad_up
    copies[0].wait()
    total = dot_nt(grad_gate, held[0])
    copies[1].wait()
    total = (total + dot_nt(grad_up, held[1])).astype(BF)
    for s in range(count):
        out_refs[s][...] = total[s * cap : (s + 1) * cap, :]


def experts_backward(blocks, gate_up, weights, piece):
    count = len(blocks)
    cap, width = blocks[0].shape
    rows = count * cap
    in_vmem = pl.BlockSpec(memory_space=pltpu.VMEM)
    return pl.pallas_call(
        functools.partial(experts_backward_kernel, count),
        in_specs=[in_vmem] * (count + 1) + [pl.BlockSpec(memory_space=pltpu.HBM)],
        out_specs=[in_vmem] * (2 + count),
        out_shape=[
            jax.ShapeDtypeStruct((rows, width), BF),
            jax.ShapeDtypeStruct((rows, 2 * piece), BF),
        ]
        + [jax.ShapeDtypeStruct((cap, width), BF)] * count,
        scratch_shapes=[pltpu.VMEM((3, width, piece), BF), pltpu.SemaphoreType.DMA((3,))],
        compiler_params=pltpu.CompilerParams(vmem_limit_bytes=56 * 1024 * 1024),
        cost_estimate=pl.CostEstimate(flops=0, bytes_accessed=0, transcendentals=0),
    )(*blocks, gate_up, weights)


def kv_pair_kernel(heads, chips, *refs):
    near, there, outs = refs[:heads], refs[heads : 2 * heads], refs[2 * heads :]
    for m in range(chips):
        for g in range(heads):
            total = near[g][m].astype(F32) + there[g][m].astype(F32)
            outs[m][:, g * 2 * HD : (g + 1) * 2 * HD] = total.astype(outs[m].dtype)


def kv_pair_sums(near, there):
    heads, (chips, rows, cols) = len(near), near[0].shape
    in_vmem = pl.BlockSpec(memory_space=pltpu.VMEM)
    out = jax.ShapeDtypeStruct((rows, heads * cols), BF)
    return pl.pallas_call(
        functools.partial(kv_pair_kernel, heads, chips),
        in_specs=[in_vmem] * (2 * heads),
        out_specs=[in_vmem] * chips,
        out_shape=[jax.ShapeDtypeStruct((rows, heads * cols), F32)] + [out] * (chips - 1),
        compiler_params=pltpu.CompilerParams(vmem_limit_bytes=20 * 1024 * 1024),
        cost_estimate=pl.CostEstimate(flops=0, bytes_accessed=0, transcendentals=0),
    )(*near, *there)


def head_columns_kernel(heads, chips, *refs):
    queries, sums = refs[:heads], refs[heads : heads + chips]
    factor_ref, ride_ref, sent_ref, columns_ref = refs[heads + chips :]
    query = jnp.concatenate([each[...] for each in queries], axis=1)
    keyval = sums[0][...]
    for each in sums[1:]:
        keyval = keyval + each[...].astype(F32)
    both = jnp.concatenate([query, keyval], axis=1)
    rows, cols = both.shape
    sent_ref[...] = both.astype(BF)
    columns_ref[:rows, :cols] = (both * factor_ref[...]).astype(BF)
    columns_ref[:rows, cols:] = jnp.zeros((rows, LANES), BF)
    columns_ref[rows:, :cols] = jnp.zeros((ride_ref.shape[0], cols), BF)
    columns_ref[rows:, cols:] = ride_ref[...]


def head_columns(queries, sums, factor, ride):
    rows = sums[0].shape[0]
    cols = sum(each.shape[1] for each in queries) + sums[0].shape[1]
    if cols % LANES:
        both = jnp.concatenate(list(queries) + [total_of(sums)], axis=1)
        scaled = jnp.pad((both * factor).astype(BF), ((0, 0), (0, LANES)))
        return both.astype(BF), jnp.concatenate([scaled, jnp.pad(ride, ((0, 0), (cols, 0)))])
    in_vmem = pl.BlockSpec(memory_space=pltpu.VMEM)
    return pl.pallas_call(
        functools.partial(head_columns_kernel, len(queries), len(sums)),
        in_specs=[in_vmem] * (len(queries) + len(sums) + 2),
        out_specs=[in_vmem] * 2,
        out_shape=[
            jax.ShapeDtypeStruct((rows, cols), BF),
            jax.ShapeDtypeStruct((rows + ride.shape[0], cols + LANES), BF),
        ],
        compiler_params=pltpu.CompilerParams(vmem_limit_bytes=20 * 1024 * 1024),
        cost_estimate=pl.CostEstimate(flops=0, bytes_accessed=0, transcendentals=0),
    )(*queries, *sums, factor, ride)


def two_parts(value):
    high = value.astype(BF)
    return high, (value - high.astype(F32)).astype(BF)


def mark_kernel(seed_ref, out_ref):
    out_ref[...] = seed_ref[...]


def mark(*others):
    seed = after(jnp.zeros((8, LANES), F32), *others)
    return pl.pallas_call(
        mark_kernel,
        out_shape=jax.ShapeDtypeStruct((8, LANES), F32),
        cost_estimate=pl.CostEstimate(flops=10**12, bytes_accessed=8192, transcendentals=0),
    )(seed)


def by_rows(array):
    return with_layout_constraint(array, Layout(major_to_minor=tuple(range(array.ndim))))


def after(values, *others):
    return lax.optimization_barrier((values, others))[0]


def root(values):
    return lax.rsqrt(jnp.mean(values * values, axis=-1, keepdims=True) + EPSILON)


def root_back(values, factor, grad_scaled):
    inner = jnp.mean(grad_scaled * values, axis=-1, keepdims=True)
    return factor * grad_scaled - values * (factor * factor * factor * inner)


def place_gate_up_kernel(count, place_ref, *refs):
    blocks = refs[: 2 * count - 1]
    weight_ref, gain_ref, out_ref, sums_ref, base = refs[2 * count - 1 :]
    offset = place_ref[0] - pl.program_id(1)

    for s in range(2 * count - 1):

        @pl.when(offset == (s if s < count else count - 1 - s))
        def _(s=s):
            base[...] = blocks[s][...].astype(F32)

    @pl.when((pl.program_id(0) == 0) & (pl.program_id(1) == 0))
    def _():
        sums_ref[...] = jnp.zeros_like(sums_ref)

    values = base[...]
    out_ref[0] = values * gain_ref[...]
    product = jnp.sum(weight_ref[0].astype(F32) * values, axis=1, keepdims=True)
    sums_ref[...] += jnp.broadcast_to(product, sums_ref.shape)


def place_gate_up(steps, weight, gain, place):
    experts, part, both = weight.shape
    count = len(steps)
    split = count // experts
    if split == 1:
        tile = math.gcd(both, 1024)
        blocks = [steps[0][0]] + [each[0] for each in steps[1:]] + [each[1] for each in steps[1:]]
        block = pl.BlockSpec((part, tile), lambda t, e: (0, t))
        out, sums = pl.pallas_call(
            functools.partial(place_gate_up_kernel, count),
            grid=(both // tile, experts),
            in_specs=[pl.BlockSpec(memory_space=pltpu.SMEM)]
            + [block] * len(blocks)
            + [
                pl.BlockSpec((1, part, tile), lambda t, e: (e, 0, t)),
                pl.BlockSpec((part, 1), lambda t, e: (0, 0)),
            ],
            out_specs=[
                pl.BlockSpec((1, part, tile), lambda t, e: (e, 0, t)),
                pl.BlockSpec((part, LANES), lambda t, e: (0, 0)),
            ],
            out_shape=[
                jax.ShapeDtypeStruct(weight.shape, F32),
                jax.ShapeDtypeStruct((part, LANES), F32),
            ],
            scratch_shapes=[pltpu.VMEM((part, tile), F32)],
            compiler_params=pltpu.CompilerParams(vmem_limit_bytes=28 * 1024 * 1024),
            cost_estimate=pl.CostEstimate(flops=0, bytes_accessed=0, transcendentals=0),
        )(place.astype(jnp.int32).reshape(1), *blocks, weight, gain)
        return out, sums[:, 0]
    blocks = [steps[0][0]] + [
        jnp.where(place >= s, steps[s][0], steps[count - s][1]) for s in range(1, count)
    ]
    base = (
        from_relative(blocks, place)
        .reshape(experts, split, part, 2, both // (2 * split))
        .transpose(0, 2, 3, 1, 4)
        .reshape(experts, part, both)
        .astype(F32)
    )
    return base * gain, jnp.sum(weight.astype(F32) * base, axis=(0, 2))


def place_kernel(count, q_cols, kv_cols, place_ref, *refs):
    blocks = refs[:count]
    w_query_ref, w_keyval_ref, gain_ref, query_ref, keyval_ref, out_ref, base_ref, sums_ref = refs[
        count:
    ]
    gain = gain_ref[...]
    base = jnp.zeros_like(gain)
    sums = jnp.zeros(sums_ref.shape, F32)
    for s in range(count):
        owner = lax.rem(place_ref[0] + (count - s), count)
        q_at = pl.ds(pl.multiple_of(owner * q_cols, LANES), q_cols)
        kv_at = pl.ds(pl.multiple_of(owner * kv_cols, LANES), kv_cols)
        query = blocks[s][:, :q_cols].astype(F32)
        keyval = blocks[s][:, q_cols : q_cols + kv_cols].astype(F32)
        start = q_cols + kv_cols
        sums = sums + blocks[s][:, start : start + LANES].astype(F32)
        out_ref[:, q_at] = blocks[s][:, start + LANES :].astype(F32)
        base = base + jnp.sum(w_query_ref[:, q_at].astype(F32) * query, axis=1, keepdims=True)
        base = base + jnp.sum(w_keyval_ref[:, kv_at].astype(F32) * keyval, axis=1, keepdims=True)
        query_ref[:, q_at] = query * gain
        keyval_ref[:, kv_at] = keyval * gain
    base_ref[...] = jnp.broadcast_to(base, base_ref.shape)
    sums_ref[...] = sums


def place_heads(blocks, place, w_query, w_keyval, gain, q_cols, kv_cols):
    count = len(blocks)
    part = w_query.shape[0]
    start = q_cols + kv_cols
    if q_cols % LANES == 0 and kv_cols % LANES == 0:
        wide = jax.ShapeDtypeStruct((part, count * q_cols), F32)
        narrow = jax.ShapeDtypeStruct((part, count * kv_cols), F32)
        lanes = jax.ShapeDtypeStruct((part, LANES), F32)
        in_vmem = pl.BlockSpec(memory_space=pltpu.VMEM)
        query, keyval, out, base, sums = pl.pallas_call(
            functools.partial(place_kernel, count, q_cols, kv_cols),
            in_specs=[pl.BlockSpec(memory_space=pltpu.SMEM)] + [in_vmem] * (count + 3),
            out_specs=[in_vmem] * 5,
            out_shape=[wide, narrow, wide, lanes, lanes],
            compiler_params=pltpu.CompilerParams(vmem_limit_bytes=24 * 1024 * 1024),
            cost_estimate=pl.CostEstimate(flops=0, bytes_accessed=0, transcendentals=0),
        )(place.astype(jnp.int32).reshape(1), *blocks, w_query, w_keyval, gain)
        return query, keyval, out, base[:, 0], sums
    blocks = from_relative(blocks, place).astype(F32)

    def columns(begin, end):
        return blocks[:, :, begin:end].transpose(1, 0, 2).reshape(part, count * (end - begin))

    query, keyval = columns(0, q_cols), columns(q_cols, start)
    base = jnp.sum(w_query.astype(F32) * query, axis=1) + jnp.sum(
        w_keyval.astype(F32) * keyval, axis=1
    )
    sums = jnp.sum(blocks[:, :, start : start + LANES], axis=0)
    out = columns(start + LANES, start + LANES + q_cols)
    return query * gain, keyval * gain, out, base, sums


def local(
    tokens,
    teacher,
    valid,
    routes,
    slots,
    gain_attn,
    w_query,
    w_keyval,
    w_out,
    gain_ffn,
    w_router,
    w_gate_up,
    w_down,
):
    seqs = lax.axis_size("seq")
    shards = lax.axis_size("fsdp")
    z = lax.axis_index("seq")
    shard = lax.axis_index("fsdp")
    rows, width = tokens.shape
    groups = HEADS // KVH
    local_kv = KVH // seqs
    q_cols = local_kv * groups * HD
    kv_cols = local_kv * 2 * HD
    local_rows = rows * seqs
    seq_len = local_rows * shards
    experts, part, both = w_gate_up.shape
    units = both // 2
    split = seqs // experts
    piece = units // split
    expert = z // split
    fraction = z % split
    scale = HD ** (-0.5)

    gain_one = gain_attn.astype(F32)[:, None]
    gain_two = gain_ffn.astype(F32)[:, None]
    heads_shard = jnp.concatenate(
        [
            lax.dynamic_slice_in_dim(w_query, z * q_cols, q_cols, 1),
            lax.dynamic_slice_in_dim(w_keyval, z * kv_cols, kv_cols, 1),
        ],
        axis=1,
    )
    heads_shard = (heads_shard.astype(F32) * gain_one).astype(BF)
    heads_full = lax.all_gather(heads_shard, "fsdp", axis=0, tiled=True)
    valid_row = jnp.pad(valid.astype(BF).reshape(1, rows), ((0, 7), (0, width - rows)))
    token_rows = jnp.concatenate([tokens, valid_row], axis=0)
    token_mark = mark(token_rows)
    token_blocks = after(send_out([token_rows] * seqs, seqs), token_mark)

    valid_local = from_relative([each[rows : rows + 1, :rows] for each in token_blocks], z)
    projected = []
    for block in token_blocks:
        projected.append(dot(block[:rows], heads_full) * root(block[:rows].astype(F32)))
    projected = from_relative([each.astype(BF) for each in projected], z)
    projected = projected.reshape(local_rows, q_cols + kv_cols)
    head_queries = projected[:, :q_cols] * jnp.asarray(scale, BF)

    valid_rows_kv = local_rows // kv_cols
    payload = jnp.concatenate(
        [
            projected[:, q_cols:],
            valid_local.reshape(valid_rows_kv, kv_cols),
            jnp.zeros((16 - valid_rows_kv, kv_cols), BF),
        ],
        axis=0,
    )
    kv_blocks = gather_shards(payload, shards)
    late_query, late_keyval, late_router, late_gate_up, late_down = after(
        (w_query, w_keyval, w_router, w_gate_up, w_down), token_mark
    )
    out_full = lax.all_gather(w_out, "fsdp", axis=1, tiled=True)
    own_expert = take(late_gate_up, expert, 0)
    gate_shard = lax.dynamic_slice_in_dim(own_expert, fraction * piece, piece, 1)
    up_shard = lax.dynamic_slice_in_dim(own_expert, units + fraction * piece, piece, 1)
    down_shard = lax.dynamic_slice_in_dim(take(late_down, expert, 0), fraction * piece, piece, 0).T
    router_shard = jnp.pad((late_router.astype(F32) * gain_two).astype(BF), ((0, 0), (0, LANES - experts)))
    expert_shard = jnp.concatenate(
        [
            (gate_shard.astype(F32) * gain_two).astype(BF),
            (up_shard.astype(F32) * gain_two).astype(BF),
            down_shard,
            router_shard,
        ],
        axis=1,
    )
    expert_full = lax.all_gather(expert_shard, "fsdp", axis=0, tiled=True)
    router_full = expert_full[:, 3 * piece :]
    attn_shard = jnp.concatenate(
        [
            each
            for s in range(seqs)
            for each in (
                late_query[:, s * q_cols : (s + 1) * q_cols],
                late_keyval[:, s * kv_cols : (s + 1) * kv_cols],
            )
        ],
        axis=1,
    )
    attn_full = lax.all_gather(
        (attn_shard.astype(F32) * gain_one).astype(BF), "fsdp", axis=0, tiled=True
    )
    order = jnp.asarray(
        [2 * m for m in range(shards // 2)] + [2 * m + 1 for m in range(shards // 2)], jnp.int32
    )
    valid_all = jnp.stack(
        [
            each[local_rows : local_rows + valid_rows_kv].reshape(seqs, rows)
            for each in kv_blocks
        ],
        axis=1,
    ).astype(F32)
    valid_count = jnp.sum(valid_all)
    bias = jnp.where(valid_all > 0, 0.0, FLOOR_SCORE)
    earlier = ((order ^ shard) < shard) | (order == 0)
    bias_same = jnp.where(earlier[None, :, None], bias, FLOOR_SCORE)
    bias = jnp.concatenate([bias, bias_same]).reshape(2 * seqs, 1, shards * rows)
    attended_low, exact, lse = flash_forward(
        head_queries, kv_blocks, bias, seqs, rows, local_kv, groups
    )
    attended = lax.all_to_all(attended_low, "seq", split_axis=0, concat_axis=1, tiled=True)

    inputs = tokens.astype(F32)
    residual = inputs + dot(attended, out_full)
    factor_two = root(residual)
    normed_two = (residual * factor_two).astype(BF)
    logits = dot(normed_two, router_full)[:, :experts]
    expert_ids = jnp.arange(experts, dtype=jnp.int32)
    picked = (routes[:, :, None] == expert_ids).astype(F32)
    chosen = jnp.sum(picked * logits[:, None, :], axis=-1)
    gating = jax.nn.softmax(chosen, axis=-1)
    owners = ((jnp.arange(seqs, dtype=jnp.int32) + z) % seqs) // split
    to_owner = routes[:, :, None] == owners
    slot_hot = slots[:, :, None] == jnp.arange(CAP, dtype=jnp.int32)
    placed = (to_owner[:, :, :, None] & slot_hot[:, :, None, :]).astype(BF)
    placed = placed.reshape(rows, 2, seqs * CAP)
    dispatch = placed[:, 0] + placed[:, 1]
    placed_pairs = jnp.concatenate([placed[:, 0], placed[:, 1]], axis=0)
    sent_rows = dot_tn(dispatch, normed_two).astype(BF)
    kv_all = jnp.stack(after(kv_blocks, sent_rows))
    sent_rows = sent_rows.reshape(seqs, CAP, width)
    expert_rows, gate_up, hidden, *expert_out = experts_forward(
        send_out([sent_rows[s] for s in range(seqs)], seqs), expert_full, piece
    )
    returned = jnp.concatenate(after(send_back(expert_out, seqs), kv_all))
    selected = dot(placed_pairs, returned).reshape(2, rows, width)
    mixed_exact = residual + gating[:, :1] * selected[0] + gating[:, 1:] * selected[1]
    valid_rows = valid.astype(F32)
    errors = (mixed_exact - teacher.astype(F32)) * valid_rows[:, None]
    squares = jnp.sum(errors * errors)
    loss_scale = width * seq_len // 8
    grad_mixed = errors * (2.0 * loss_scale / (width * valid_count))

    grad_gating = jnp.stack(
        [jnp.sum(selected[0] * grad_mixed, axis=-1), jnp.sum(selected[1] * grad_mixed, axis=-1)],
        axis=1,
    )
    grad_chosen = gating * (grad_gating - jnp.sum(gating * grad_gating, axis=-1, keepdims=True))
    grad_logits = jnp.sum(grad_chosen[:, :, None] * picked, axis=1).astype(BF)
    grad_logits = jnp.pad(grad_logits, ((0, 0), (0, LANES - experts)))
    weighted = jnp.concatenate(
        [(gating[:, :1] * grad_mixed).astype(BF), (gating[:, 1:] * grad_mixed).astype(BF)], axis=0
    )
    sent_grads = dot_tn(placed_pairs, weighted).astype(BF).reshape(seqs, CAP, width)
    grad_out_rows = send_out([sent_grads[s] for s in range(seqs)], seqs)
    grad_out_rows = after(grad_out_rows, attn_full, grad_logits)
    grad_expert_out, grad_gate_up_rows, *grad_rows = experts_backward(
        grad_out_rows, gate_up, expert_full, piece
    )
    grad_returned = send_back(grad_rows, seqs)
    tokens_local = from_relative(
        [each[:rows] for each in after(token_blocks, grad_rows)], z
    ).reshape(local_rows, width)
    factor_local = root(tokens_local.astype(F32))
    ride_rows = jnp.concatenate([normed_two, jnp.ones((16, width), BF)], axis=0)
    product_rows = jnp.concatenate([tokens_local, ride_rows], axis=0)
    high, low = two_parts(squares)
    lane = jnp.arange(LANES, dtype=jnp.int32)[None, :]
    marks = jnp.where(lane == experts + 2 * (shard % 2), high, 0) + jnp.where(
        lane == experts + 1 + 2 * (shard % 2), low, 0
    )
    ride_columns = jnp.concatenate(
        [grad_logits, marks.astype(BF), jnp.zeros((15, LANES), BF)], axis=0
    )
    held_out, held_hidden = after((grad_expert_out, hidden), grad_rows)
    down_far, down_near = split_product(held_out, held_hidden, shard, shards)
    grad_down_sums = pair_sums(down_near, hop(down_far, shards, 1), shard)
    held_rows, held_gate_up = after((expert_rows, grad_gate_up_rows), grad_rows)
    gate_up_far, gate_up_near = split_product(held_rows, held_gate_up, shard, shards)
    grad_gate_up_sums = pair_sums(gate_up_near, hop(gate_up_far, shards, 1), shard)
    grad_down_blocks = send_chips(grad_down_sums, shards)
    grad_returned = jnp.concatenate(after(grad_returned, grad_down_sums, product_rows, ride_columns, factor_local))
    grad_normed_two = dot(dispatch, grad_returned) + dot_nt(grad_logits, router_full)
    grad_residual = grad_mixed + root_back(residual, factor_two, grad_normed_two)
    grad_branch = grad_residual.astype(BF)
    grad_attended = dot_nt(after(grad_branch, grad_gate_up_sums), out_full).astype(BF)
    head_grad = lax.all_to_all(grad_attended, "seq", split_axis=1, concat_axis=0, tiled=True)
    grad_gate_up_blocks = send_chips(grad_gate_up_sums, shards)
    grad_down_shard = total_of(after(grad_down_blocks, grad_attended)).astype(BF)
    grad_down = lax.all_gather(grad_down_shard, "seq", axis=0, tiled=False)

    out_far, out_near = split_product(
        after(grad_branch, grad_attended), attended, shard, shards
    )
    grad_q, near, far = [], [], []
    held = after(head_grad, grad_down_shard)
    for g in range(local_kv):
        part_q, near_kv, far_kv = flash_backward(
            head_queries, kv_all, bias, held, exact, lse, seqs, rows, g, groups
        )
        if g == 0:
            grad_gate_up_blocks = after(grad_gate_up_blocks, part_q)
            grad_gate_up_shard = total_of(grad_gate_up_blocks).astype(BF)
            steps = [(grad_gate_up_shard, grad_gate_up_shard)]
            steps.append(relay_step(steps[0], seqs))
            out_there = hop(after(out_far, head_grad), shards, 1)
        grad_q.append(part_q)
        near.append(near_kv)
        far.append(far_kv)
        held = after(head_grad, grad_gate_up_shard, out_there)
    steps[1] = after(steps[1], part_q)
    steps.append(relay_step(steps[1], seqs))
    far = after(far, steps[1], grad_down)
    pairs = kv_pair_sums(near, [hop(each, shards, 1) for each in far])
    out_sums = pair_sums(out_near, after(out_there, pairs), shard)
    sent_grads, product_columns = head_columns(
        grad_q, after(send_chips(pairs, shards), out_sums, steps[2]), factor_local, ride_columns
    )
    steps[2] = after(steps[2], product_columns)
    while len(steps) < seqs:
        steps.append(relay_step(steps[-1], seqs))
    token_grads = lax.all_to_all(sent_grads, "seq", split_axis=0, concat_axis=1, tiled=True)

    head_cols = q_cols + kv_cols
    head_far, head_near = split_product(product_rows, product_columns, shard, shards)
    head_sums = pair_sums(head_near, hop(head_far, shards, 1), shard)
    out_part = total_of(
        after(send_chips(after(out_sums, product_columns), shards), head_sums)
    ).astype(BF)
    out_parts = lax.all_to_all(
        out_part.reshape(part, seqs, q_cols), "seq", split_axis=1, concat_axis=1, tiled=True
    )
    head_blocks = send_chips(head_sums, shards)
    head_part = total_of(after(head_blocks, steps[3]))
    grad_normed = dot_nt(after(token_grads, head_part), attn_full)
    grad_tokens = grad_residual + root_back(inputs, root(inputs), grad_normed)
    base_cols = head_cols + experts
    plane_high, plane_low = two_parts(
        jnp.sum(head_part[:1, base_cols : base_cols + 4], axis=1, keepdims=True)
    )
    lanes = lax.broadcasted_iota(jnp.int32, head_part.shape, 1)
    head_part = jnp.where(
        lanes == base_cols,
        plane_high.astype(F32),
        jnp.where(lanes == base_cols + 1, plane_low.astype(F32), head_part),
    )
    out_own = jnp.sum(out_parts.astype(F32), axis=1)
    head_part = by_rows(jnp.concatenate([head_part, out_own], axis=1).astype(BF))
    head_last = [by_rows(each) for each in send_out([head_part] * seqs, seqs)]
    grad_gate_up, grad_gain_ffn = place_gate_up(after(steps, head_part), w_gate_up, gain_two, z)
    head_last = after(head_last, grad_gate_up)
    grad_query, grad_keyval, grad_out, grad_gain_attn, sums = place_heads(
        head_last, z, w_query, w_keyval, gain_one, q_cols, kv_cols
    )
    loss_value = jnp.sum(sums[0, experts : experts + 2]) / (width * valid_count)
    grad_router_base = sums[:, :experts]
    grad_down = (
        after(grad_down, head_part).reshape(experts, split, part, piece)
        .transpose(0, 1, 3, 2)
        .reshape(experts, units, part)
        .astype(F32)
    )
    grad_gain_ffn = grad_gain_ffn + jnp.sum(w_router.astype(F32) * grad_router_base, axis=1)
    return (
        mixed_exact.astype(BF),
        loss_value,
        grad_tokens,
        grad_gain_attn,
        grad_query,
        grad_keyval,
        grad_out.T,
        grad_gain_ffn,
        grad_router_base * gain_two,
        grad_gate_up,
        grad_down,
    )


def solution(mesh):
    return jax.shard_map(
        local,
        mesh=mesh,
        in_specs=(
            P(("seq", "fsdp"), None),
            P(("seq", "fsdp"), None),
            P(("seq", "fsdp")),
            P(("seq", "fsdp"), None),
            P(("seq", "fsdp"), None),
            P("fsdp"),
            P("fsdp", None),
            P("fsdp", None),
            P(None, "fsdp"),
            P("fsdp"),
            P("fsdp", None),
            P(None, "fsdp", None),
            P(None, None, "fsdp"),
        ),
        out_specs=(
            P(("seq", "fsdp"), None),
            P(),
            P(("seq", "fsdp"), None),
            P("fsdp"),
            P("fsdp", None),
            P("fsdp", None),
            P(None, "fsdp"),
            P("fsdp"),
            P("fsdp", None),
            P(None, "fsdp", None),
            P(None, None, "fsdp"),
        ),
        check_vma=False,
    )
```

```python
import functools
import math

import jax
import jax.numpy as jnp
from jax import lax
from jax.experimental import pallas as pl
from jax.experimental.layout import Layout, with_layout_constraint
from jax.experimental.pallas import tpu as pltpu
from jax.sharding import PartitionSpec as P

HEADS = 24
KVH = 8
HD = 64
CAP = 96
LANES = 128
EPSILON = 1e-06
FLOOR_SCORE = -1e30
BF = jnp.bfloat16
F32 = jnp.float32


def dot(a, b):
    return jnp.dot(a, b, preferred_element_type=F32)


def dot_nt(a, b):
    return lax.dot_general(a, b, (((1,), (1,)), ((), ())), preferred_element_type=F32)


def dot_tn(a, b):
    return lax.dot_general(a, b, (((0,), (0,)), ((), ())), preferred_element_type=F32)


def own_mask(valid_row, rows):
    i = lax.broadcasted_iota(jnp.int32, (rows, rows), 0)
    j = lax.broadcasted_iota(jnp.int32, (rows, rows), 1)
    return jnp.where(j == i, 0.0, jnp.where(j < i, valid_row, FLOOR_SCORE))


def key_chunk(kv_refs, zk, rows, g):
    return jnp.concatenate(
        [ref[pl.ds(zk * rows, rows), pl.ds(g * 2 * HD, 2 * HD)] for ref in kv_refs], axis=0
    )


def forward_kernel(shards, seqs, rows, local_kv, groups, *refs):
    kv_refs = refs[:shards]
    q_ref, bias_ref, low_ref, exact_ref, lse_ref, acc_ref, max_ref = refs[shards:]
    zq = pl.program_id(0)
    stack = groups * rows
    zeros = jnp.zeros((rows, HD), BF)
    half = lax.broadcasted_iota(jnp.int32, (1, 2 * HD), 1) < HD

    def queries(g):
        parts = []
        for h in range(groups):
            start = (g * groups + h) * HD
            parts.append(jnp.concatenate([q_ref[:, start : start + HD], zeros], axis=1))
        return jnp.concatenate(parts, axis=0)

    def chunk(g, zk, scores):
        first = scores is None
        keys = key_chunk(kv_refs, zk, rows, g)
        raw = dot_nt(queries(g), keys)
        if first:
            row = bias_ref[seqs + zk]
            mask = own_mask(row[:, :rows], rows)
            mask = jnp.concatenate([mask] * groups, axis=0)
            masked = jnp.concatenate([raw[:, :rows] + mask, raw[:, rows:] + row[:, rows:]], axis=1)
            new_max = jnp.max(masked, axis=1, keepdims=True)
        else:
            masked = raw + bias_ref[zk]
            new_max = jnp.maximum(max_ref[g][:, :1], jnp.max(masked, axis=1, keepdims=True))
        terms = jnp.exp(masked - new_max).astype(BF)
        ones_values = jnp.where(half, jnp.ones_like(keys), keys)
        part = dot(terms, ones_values)
        if first:
            acc_ref[g] = part
        else:
            acc_ref[g] = acc_ref[g] * jnp.exp(max_ref[g][:, :1] - new_max) + part
        max_ref[g] = jnp.broadcast_to(new_max, (stack, 2 * HD))

    for g in range(local_kv):
        chunk(g, zq, None)

    @pl.loop(0, zq)
    def _(zk):
        for g in range(local_kv):
            chunk(g, zk, True)

    exact_parts, lse_parts = [], []
    for g in range(local_kv):
        acc = acc_ref[g]
        total = acc[:, :HD]
        exact = acc[:, HD:] / total
        lse = max_ref[g][:, :HD] + jnp.log(total)
        for h in range(groups):
            exact_parts.append(exact[h * rows : (h + 1) * rows])
            lse_parts.append(lse[h * rows : (h + 1) * rows])
    exact = jnp.concatenate(exact_parts, axis=1)
    exact_ref[...] = exact
    low_ref[...] = exact.astype(BF)
    lse_ref[...] = jnp.concatenate(lse_parts, axis=1)


def flash_forward(q, kv_blocks, bias, seqs, rows, local_kv, groups):
    shards = len(kv_blocks)
    q_cols = q.shape[1]
    kv_spec = pl.BlockSpec(kv_blocks[0].shape, lambda i: (0, 0))
    q_spec = pl.BlockSpec((rows, q_cols), lambda i: (i, 0))
    stack = groups * rows
    out = jax.ShapeDtypeStruct((seqs * rows, q_cols), F32)
    return pl.pallas_call(
        functools.partial(forward_kernel, shards, seqs, rows, local_kv, groups),
        grid=(seqs,),
        in_specs=[kv_spec] * shards + [q_spec, pl.BlockSpec(bias.shape, lambda i: (0, 0, 0))],
        out_specs=[q_spec] * 3,
        out_shape=[jax.ShapeDtypeStruct((seqs * rows, q_cols), BF), out, out],
        scratch_shapes=[
            pltpu.VMEM((local_kv, stack, 2 * HD), F32),
            pltpu.VMEM((local_kv, stack, 2 * HD), F32),
        ],
        compiler_params=pltpu.CompilerParams(vmem_limit_bytes=24 * 1024 * 1024),
        cost_estimate=pl.CostEstimate(
            flops=0,
            bytes_accessed=0,
            transcendentals=0,
        ),
    )(*kv_blocks, q, bias)


def backward_kernel(shards, seqs, rows, g, groups, *refs):
    kv_refs = [refs[0].at[p] for p in range(shards)]
    (
        q_ref, bias_ref, grad_ref, exact_ref, lse_ref, grad_q_ref, near_ref, far_ref,
        pair_ref, pair_t_ref, lse_wide, delta_wide, acc_q, acc_kv,
    ) = refs[1:]
    zk = pl.program_id(0)
    stack = groups * rows
    zeros = jnp.zeros((rows, HD), BF)

    @pl.when(zk == 0)
    def _():
        acc_q[...] = jnp.zeros_like(acc_q)

        @pl.loop(0, seqs)
        def _(zq):
            here = pl.ds(zq * rows, rows)
            tops, bottoms = [], []
            for h in range(groups):
                cols = slice((g * groups + h) * HD, (g * groups + h + 1) * HD)
                grad = grad_ref[here, cols]
                tops.append(jnp.concatenate([q_ref[here, cols], zeros], axis=1))
                bottoms.append(jnp.concatenate([zeros, grad], axis=1))
                delta = jnp.sum(grad.astype(F32) * exact_ref[here, cols], axis=1, keepdims=True)
                part = slice(h * rows, (h + 1) * rows)
                delta_wide[zq, part] = jnp.broadcast_to(delta, (rows, 2 * HD))
                lse_wide[zq, part] = jnp.broadcast_to(lse_ref[here, cols][:, :1], (rows, 2 * HD))
            pair = jnp.concatenate(tops + bottoms, axis=0)
            pair_ref[zq] = pair
            pair_t_ref[zq] = pair.astype(F32).T.astype(BF)

    def chunk(zq, first):
        keys = key_chunk(kv_refs, zk, rows, g)
        both = dot_nt(pair_ref[zq], keys)
        raw, products = both[:stack], both[stack:]
        if first:
            row = bias_ref[seqs + zk]
            mask = own_mask(row[:, :rows], rows)
            mask = jnp.concatenate([mask] * groups, axis=0)
            masked = jnp.concatenate([raw[:, :rows] + mask, raw[:, rows:] + row[:, rows:]], axis=1)
        else:
            masked = raw + bias_ref[zk]
        weights = jnp.exp(masked - lse_wide[zq][:, :1])
        grads = (weights * (products - delta_wide[zq][:, :1])).astype(BF)
        acc_q[zq] += dot(grads, keys)
        part = dot(pair_t_ref[zq], jnp.concatenate([grads, weights.astype(BF)], axis=0))
        if first:
            acc_kv[...] = part
        else:
            acc_kv[...] += part

    chunk(zk, True)

    @pl.loop(zk + 1, seqs)
    def _(zq):
        chunk(zq, False)

    for p in range(shards):
        target = near_ref if p < shards // 2 else far_ref
        target[p % (shards // 2)] = acc_kv[:, p * rows : (p + 1) * rows].T.astype(BF)

    @pl.when(zk == seqs - 1)
    def _():
        @pl.loop(0, seqs)
        def _(zq):
            total = acc_q[zq]
            parts = [total[h * rows : (h + 1) * rows, :HD] for h in range(groups)]
            grad_q_ref[pl.ds(zq * rows, rows), :] = jnp.concatenate(parts, axis=1) * HD ** (-0.5)


def flash_backward(q, kv_all, bias, grad, exact, lse, seqs, rows, g, groups):
    shards = kv_all.shape[0]
    q_cols = q.shape[1]
    stack = groups * rows
    kv_spec = pl.BlockSpec(kv_all.shape, lambda i: (0, 0, 0))
    whole = pl.BlockSpec((seqs * rows, q_cols), lambda i: (0, 0))
    grad_q_shape = (seqs * rows, groups * HD)
    out_spec = pl.BlockSpec((shards // 2, rows, 2 * HD), lambda i: (0, i, 0))
    out = jax.ShapeDtypeStruct((shards // 2, seqs * rows, 2 * HD), BF)
    return pl.pallas_call(
        functools.partial(backward_kernel, shards, seqs, rows, g, groups),
        grid=(seqs,),
        in_specs=[kv_spec]
        + [whole, pl.BlockSpec(bias.shape, lambda i: (0, 0, 0)), whole, whole, whole],
        out_specs=[pl.BlockSpec(grad_q_shape, lambda i: (0, 0)), out_spec, out_spec],
        out_shape=[jax.ShapeDtypeStruct(grad_q_shape, F32), out, out],
        scratch_shapes=[
            pltpu.VMEM((seqs, 2 * stack, 2 * HD), BF),
            pltpu.VMEM((seqs, 2 * HD, 2 * stack), BF),
            pltpu.VMEM((seqs, stack, 2 * HD), F32),
            pltpu.VMEM((seqs, stack, 2 * HD), F32),
            pltpu.VMEM((seqs, stack, 2 * HD), F32),
            pltpu.VMEM((2 * HD, shards * rows), F32),
        ],
        compiler_params=pltpu.CompilerParams(vmem_limit_bytes=28 * 1024 * 1024),
        cost_estimate=pl.CostEstimate(
            flops=0 if g else 10**12,
            bytes_accessed=0,
            transcendentals=0,
        ),
    )(kv_all, q, bias, grad, exact, lse)


def shift(block, count, step):
    return lax.ppermute(block, "seq", [(i, (i + step) % count) for i in range(count)])


def send_out(blocks, count):
    return [blocks[0]] + [shift(blocks[s], count, s) for s in range(1, count)]


def send_back(blocks, count):
    return [blocks[0]] + [shift(blocks[s], count, count - s) for s in range(1, count)]


def relay_step(blocks, count):
    up, down = blocks
    return (
        lax.ppermute(up, "seq", [(i, i + 1) for i in range(count - 1)]),
        lax.ppermute(down, "seq", [(i + 1, i) for i in range(count - 1)]),
    )


def from_relative(blocks, place):
    count = len(blocks)
    rising = jnp.stack([blocks[-s % count] for s in range(count)])
    return lax.dynamic_slice_in_dim(jnp.concatenate([rising, rising]), count - place, count, 0)


def hop(block, count, mask):
    return lax.ppermute(block, "fsdp", [(i, i ^ mask) for i in range(count)])


def gather_shards(block, count):
    near = [block] + [hop(block, count, 2 * m) for m in range(1, count // 2)]
    return near + [hop(each, count, 1) for each in near]


def send_chips(parts, count):
    return [parts[0]] + [hop(parts[m], count, 2 * m) for m in range(1, count // 2)]


def total_of(blocks):
    total = blocks[0].astype(F32)
    for each in blocks[1:]:
        total = total + each.astype(F32)
    return total


def take(array, index, axis):
    return lax.dynamic_index_in_dim(array, index, axis, keepdims=False)


def product_kernel(core_ref, lhs_ref, rhs_ref, far_ref, near_ref):
    part = lhs_ref.shape[1] // 2
    rhs = rhs_ref[...]
    first = dot_tn(lhs_ref[:, :part], rhs).astype(BF)
    second = dot_tn(lhs_ref[:, part:], rhs).astype(BF)
    core = core_ref[0]

    @pl.when(core == 0)
    def _():
        near_ref[0] = first
        far_ref[0] = second

    @pl.when(core != 0)
    def _():
        near_ref[0] = second
        far_ref[0] = first


def split_product(lhs, rhs, shard, count):
    tokens, width = lhs.shape
    cols = rhs.shape[1]
    part = width // count
    if 2 * part % LANES:
        cut = dot_tn(lhs, rhs).astype(BF).reshape(count // 2, 2, part, cols)
        return take(cut, 1 - shard % 2, 1), take(cut, shard % 2, 1)
    out = jax.ShapeDtypeStruct((count // 2, part, cols), BF)
    out_spec = pl.BlockSpec((1, part, cols), lambda i: (i, 0, 0))
    return pl.pallas_call(
        product_kernel,
        grid=(count // 2,),
        in_specs=[
            pl.BlockSpec(memory_space=pltpu.SMEM),
            pl.BlockSpec((tokens, 2 * part), lambda i: (0, i)),
            pl.BlockSpec((tokens, cols), lambda i: (0, 0)),
        ],
        out_specs=[out_spec, out_spec],
        out_shape=[out, out],
        compiler_params=pltpu.CompilerParams(vmem_limit_bytes=24 * 1024 * 1024),
        cost_estimate=pl.CostEstimate(flops=0, bytes_accessed=0, transcendentals=0),
    )((shard % 2).astype(jnp.int32).reshape(1), lhs, rhs)


def pair_kernel(chip_ref, near_ref, there_ref, own_ref, *part_refs):
    chip = chip_ref[0]
    own_ref[...] = near_ref[chip].astype(F32) + there_ref[chip].astype(F32)
    for m, part_ref in enumerate(part_refs):
        which = chip ^ (m + 1)
        part_ref[...] = (near_ref[which].astype(F32) + there_ref[which].astype(F32)).astype(BF)


def pair_sums(near, there, shard):
    chips, part, cols = near.shape
    tile = math.gcd(cols, 512)
    if tile % LANES:
        tile = cols
    block = pl.BlockSpec((chips, part, tile), lambda i: (0, 0, i))
    out_spec = pl.BlockSpec((part, tile), lambda i: (0, i))
    out = jax.ShapeDtypeStruct((part, cols), BF)
    return pl.pallas_call(
        pair_kernel,
        grid=(cols // tile,),
        in_specs=[pl.BlockSpec(memory_space=pltpu.SMEM), block, block],
        out_specs=[out_spec] * chips,
        out_shape=[jax.ShapeDtypeStruct((part, cols), F32)] + [out] * (chips - 1),
        compiler_params=pltpu.CompilerParams(vmem_limit_bytes=24 * 1024 * 1024),
        cost_estimate=pl.CostEstimate(flops=0, bytes_accessed=0, transcendentals=0),
    )((shard // 2).astype(jnp.int32).reshape(1), near, there)


def fetch_weights(weights_ref, held, sems, piece):
    copies = [
        pltpu.make_async_copy(
            weights_ref.at[:, pl.ds(part * piece, piece)], held.at[part], sems.at[part]
        )
        for part in range(3)
    ]
    return copies


def experts_forward_kernel(count, *refs):
    rows_in, weights_ref = refs[:count], refs[count]
    rows_ref, gate_up_ref, hidden_ref = refs[count + 1 : count + 4]
    out_refs, (held, sems) = refs[count + 4 : -2], refs[-2:]
    piece = hidden_ref.shape[1]
    cap = rows_in[0].shape[0]
    copies = fetch_weights(weights_ref, held, sems, piece)
    for copy in copies:
        copy.start()
    for s in range(count):
        rows_ref[s * cap : (s + 1) * cap, :] = rows_in[s][...]
    rows = rows_ref[...]
    copies[0].wait()
    gate = dot(rows, held[0])
    gate_up_ref[:, :piece] = gate
    copies[1].wait()
    up = dot(rows, held[1])
    gate_up_ref[:, piece:] = up
    hidden = (gate / (1.0 + jnp.exp(-gate)) * up).astype(BF)
    hidden_ref[...] = hidden
    copies[2].wait()
    out = dot_nt(hidden, held[2]).astype(BF)
    for s in range(count):
        out_refs[s][...] = out[s * cap : (s + 1) * cap, :]


def experts_forward(blocks, weights, piece):
    count = len(blocks)
    cap, width = blocks[0].shape
    rows = count * cap
    in_vmem = pl.BlockSpec(memory_space=pltpu.VMEM)
    return pl.pallas_call(
        functools.partial(experts_forward_kernel, count),
        in_specs=[in_vmem] * count + [pl.BlockSpec(memory_space=pltpu.HBM)],
        out_specs=[in_vmem] * (3 + count),
        out_shape=[
            jax.ShapeDtypeStruct((rows, width), BF),
            jax.ShapeDtypeStruct((rows, 2 * piece), F32),
            jax.ShapeDtypeStruct((rows, piece), BF),
        ]
        + [jax.ShapeDtypeStruct((cap, width), BF)] * count,
        scratch_shapes=[pltpu.VMEM((3, width, piece), BF), pltpu.SemaphoreType.DMA((3,))],
        compiler_params=pltpu.CompilerParams(vmem_limit_bytes=56 * 1024 * 1024),
        cost_estimate=pl.CostEstimate(flops=0, bytes_accessed=0, transcendentals=0),
    )(*blocks, weights)


def experts_backward_kernel(count, *refs):
    grads_in, gate_up_ref, weights_ref = refs[:count], refs[count], refs[count + 1]
    grads_ref, rows_ref = refs[count + 2 : count + 4]
    out_refs, (held, sems) = refs[count + 4 : -2], refs[-2:]
    piece = rows_ref.shape[1] // 2
    cap = grads_in[0].shape[0]
    copies = fetch_weights(weights_ref, held, sems, piece)
    for copy in (copies[2], copies[0], copies[1]):
        copy.start()
    for s in range(count):
        grads_ref[s * cap : (s + 1) * cap, :] = grads_in[s][...]
    copies[2].wait()
    grad_hidden = dot(grads_ref[...], held[2])
    gate = gate_up_ref[:, :piece]
    up = gate_up_ref[:, piece:]
    slope = 1.0 / (1.0 + jnp.exp(-gate))
    grad_gate = (grad_hidden * up * slope * (1.0 + gate * (1.0 - slope))).astype(BF)
    grad_up = (grad_hidden * gate * slope).astype(BF)
    rows_ref[:, :piece] = grad_gate
    rows_ref[:, piece:] = grad_up
    copies[0].wait()
    total = dot_nt(grad_gate, held[0])
    copies[1].wait()
    total = (total + dot_nt(grad_up, held[1])).astype(BF)
    for s in range(count):
        out_refs[s][...] = total[s * cap : (s + 1) * cap, :]


def experts_backward(blocks, gate_up, weights, piece):
    count = len(blocks)
    cap, width = blocks[0].shape
    rows = count * cap
    in_vmem = pl.BlockSpec(memory_space=pltpu.VMEM)
    return pl.pallas_call(
        functools.partial(experts_backward_kernel, count),
        in_specs=[in_vmem] * (count + 1) + [pl.BlockSpec(memory_space=pltpu.HBM)],
        out_specs=[in_vmem] * (2 + count),
        out_shape=[
            jax.ShapeDtypeStruct((rows, width), BF),
            jax.ShapeDtypeStruct((rows, 2 * piece), BF),
        ]
        + [jax.ShapeDtypeStruct((cap, width), BF)] * count,
        scratch_shapes=[pltpu.VMEM((3, width, piece), BF), pltpu.SemaphoreType.DMA((3,))],
        compiler_params=pltpu.CompilerParams(vmem_limit_bytes=56 * 1024 * 1024),
        cost_estimate=pl.CostEstimate(flops=0, bytes_accessed=0, transcendentals=0),
    )(*blocks, gate_up, weights)


def kv_pair_kernel(heads, chips, *refs):
    near, there, outs = refs[:heads], refs[heads : 2 * heads], refs[2 * heads :]
    for m in range(chips):
        for g in range(heads):
            total = near[g][m].astype(F32) + there[g][m].astype(F32)
            outs[m][:, g * 2 * HD : (g + 1) * 2 * HD] = total.astype(outs[m].dtype)


def kv_pair_sums(near, there):
    heads, (chips, rows, cols) = len(near), near[0].shape
    in_vmem = pl.BlockSpec(memory_space=pltpu.VMEM)
    out = jax.ShapeDtypeStruct((rows, heads * cols), BF)
    return pl.pallas_call(
        functools.partial(kv_pair_kernel, heads, chips),
        in_specs=[in_vmem] * (2 * heads),
        out_specs=[in_vmem] * chips,
        out_shape=[jax.ShapeDtypeStruct((rows, heads * cols), F32)] + [out] * (chips - 1),
        compiler_params=pltpu.CompilerParams(vmem_limit_bytes=20 * 1024 * 1024),
        cost_estimate=pl.CostEstimate(flops=0, bytes_accessed=0, transcendentals=0),
    )(*near, *there)


def head_columns_kernel(heads, chips, *refs):
    queries, sums = refs[:heads], refs[heads : heads + chips]
    factor_ref, ride_ref, sent_ref, columns_ref = refs[heads + chips :]
    query = jnp.concatenate([each[...] for each in queries], axis=1)
    keyval = sums[0][...]
    for each in sums[1:]:
        keyval = keyval + each[...].astype(F32)
    both = jnp.concatenate([query, keyval], axis=1)
    rows, cols = both.shape
    sent_ref[...] = both.astype(BF)
    columns_ref[:rows, :cols] = (both * factor_ref[...]).astype(BF)
    columns_ref[:rows, cols:] = jnp.zeros((rows, LANES), BF)
    columns_ref[rows:, :cols] = jnp.zeros((ride_ref.shape[0], cols), BF)
    columns_ref[rows:, cols:] = ride_ref[...]


def head_columns(queries, sums, factor, ride):
    rows = sums[0].shape[0]
    cols = sum(each.shape[1] for each in queries) + sums[0].shape[1]
    if cols % LANES:
        both = jnp.concatenate(list(queries) + [total_of(sums)], axis=1)
        scaled = jnp.pad((both * factor).astype(BF), ((0, 0), (0, LANES)))
        return both.astype(BF), jnp.concatenate([scaled, jnp.pad(ride, ((0, 0), (cols, 0)))])
    in_vmem = pl.BlockSpec(memory_space=pltpu.VMEM)
    return pl.pallas_call(
        functools.partial(head_columns_kernel, len(queries), len(sums)),
        in_specs=[in_vmem] * (len(queries) + len(sums) + 2),
        out_specs=[in_vmem] * 2,
        out_shape=[
            jax.ShapeDtypeStruct((rows, cols), BF),
            jax.ShapeDtypeStruct((rows + ride.shape[0], cols + LANES), BF),
        ],
        compiler_params=pltpu.CompilerParams(vmem_limit_bytes=20 * 1024 * 1024),
        cost_estimate=pl.CostEstimate(flops=0, bytes_accessed=0, transcendentals=0),
    )(*queries, *sums, factor, ride)


def two_parts(value):
    high = value.astype(BF)
    return high, (value - high.astype(F32)).astype(BF)


def mark_kernel(seed_ref, out_ref):
    out_ref[...] = seed_ref[...]


def mark(*others):
    seed = after(jnp.zeros((8, LANES), F32), *others)
    return pl.pallas_call(
        mark_kernel,
        out_shape=jax.ShapeDtypeStruct((8, LANES), F32),
        cost_estimate=pl.CostEstimate(flops=10**12, bytes_accessed=8192, transcendentals=0),
    )(seed)


def by_rows(array):
    return with_layout_constraint(array, Layout(major_to_minor=tuple(range(array.ndim))))


def after(values, *others):
    return lax.optimization_barrier((values, others))[0]


def root(values):
    return lax.rsqrt(jnp.mean(values * values, axis=-1, keepdims=True) + EPSILON)


def root_back(values, factor, grad_scaled):
    inner = jnp.mean(grad_scaled * values, axis=-1, keepdims=True)
    return factor * grad_scaled - values * (factor * factor * factor * inner)


def place_gate_up_kernel(count, place_ref, *refs):
    blocks = refs[: 2 * count - 1]
    weight_ref, gain_ref, out_ref, sums_ref, base = refs[2 * count - 1 :]
    offset = place_ref[0] - pl.program_id(1)

    for s in range(2 * count - 1):

        @pl.when(offset == (s if s < count else count - 1 - s))
        def _(s=s):
            base[...] = blocks[s][...].astype(F32)

    @pl.when((pl.program_id(0) == 0) & (pl.program_id(1) == 0))
    def _():
        sums_ref[...] = jnp.zeros_like(sums_ref)

    values = base[...]
    out_ref[0] = values * gain_ref[...]
    product = jnp.sum(weight_ref[0].astype(F32) * values, axis=1, keepdims=True)
    sums_ref[...] += jnp.broadcast_to(product, sums_ref.shape)


def place_gate_up(steps, weight, gain, place):
    experts, part, both = weight.shape
    count = len(steps)
    split = count // experts
    if split == 1:
        tile = math.gcd(both, 1024)
        blocks = [steps[0][0]] + [each[0] for each in steps[1:]] + [each[1] for each in steps[1:]]
        block = pl.BlockSpec((part, tile), lambda t, e: (0, t))
        out, sums = pl.pallas_call(
            functools.partial(place_gate_up_kernel, count),
            grid=(both // tile, experts),
            in_specs=[pl.BlockSpec(memory_space=pltpu.SMEM)]
            + [block] * len(blocks)
            + [
                pl.BlockSpec((1, part, tile), lambda t, e: (e, 0, t)),
                pl.BlockSpec((part, 1), lambda t, e: (0, 0)),
            ],
            out_specs=[
                pl.BlockSpec((1, part, tile), lambda t, e: (e, 0, t)),
                pl.BlockSpec((part, LANES), lambda t, e: (0, 0)),
            ],
            out_shape=[
                jax.ShapeDtypeStruct(weight.shape, F32),
                jax.ShapeDtypeStruct((part, LANES), F32),
            ],
            scratch_shapes=[pltpu.VMEM((part, tile), F32)],
            compiler_params=pltpu.CompilerParams(vmem_limit_bytes=28 * 1024 * 1024),
            cost_estimate=pl.CostEstimate(flops=0, bytes_accessed=0, transcendentals=0),
        )(place.astype(jnp.int32).reshape(1), *blocks, weight, gain)
        return out, sums[:, 0]
    blocks = [steps[0][0]] + [
        jnp.where(place >= s, steps[s][0], steps[count - s][1]) for s in range(1, count)
    ]
    base = (
        from_relative(blocks, place)
        .reshape(experts, split, part, 2, both // (2 * split))
        .transpose(0, 2, 3, 1, 4)
        .reshape(experts, part, both)
        .astype(F32)
    )
    return base * gain, jnp.sum(weight.astype(F32) * base, axis=(0, 2))


def place_kernel(count, q_cols, kv_cols, place_ref, *refs):
    blocks, outs = refs[:count], refs[count : 2 * count]
    w_query_ref, w_keyval_ref, gain_ref, query_ref, keyval_ref, out_ref, base_ref, sums_ref = refs[
        2 * count :
    ]
    gain = gain_ref[...]
    base = jnp.zeros_like(gain)
    sums = jnp.zeros(sums_ref.shape, F32)
    for s in range(count):
        owner = lax.rem(place_ref[0] + (count - s), count)
        q_at = pl.ds(pl.multiple_of(owner * q_cols, LANES), q_cols)
        kv_at = pl.ds(pl.multiple_of(owner * kv_cols, LANES), kv_cols)
        query = blocks[s][:, :q_cols].astype(F32)
        keyval = blocks[s][:, q_cols : q_cols + kv_cols].astype(F32)
        start = q_cols + kv_cols
        sums = sums + blocks[s][:, start : start + LANES].astype(F32)
        out_ref[:, q_at] = outs[s][...].astype(F32)
        base = base + jnp.sum(w_query_ref[:, q_at].astype(F32) * query, axis=1, keepdims=True)
        base = base + jnp.sum(w_keyval_ref[:, kv_at].astype(F32) * keyval, axis=1, keepdims=True)
        query_ref[:, q_at] = query * gain
        keyval_ref[:, kv_at] = keyval * gain
    base_ref[...] = jnp.broadcast_to(base, base_ref.shape)
    sums_ref[...] = sums


def place_heads(blocks, outs, place, w_query, w_keyval, gain, q_cols, kv_cols):
    count = len(blocks)
    part = w_query.shape[0]
    start = q_cols + kv_cols
    if q_cols % LANES == 0 and kv_cols % LANES == 0:
        wide = jax.ShapeDtypeStruct((part, count * q_cols), F32)
        narrow = jax.ShapeDtypeStruct((part, count * kv_cols), F32)
        lanes = jax.ShapeDtypeStruct((part, LANES), F32)
        in_vmem = pl.BlockSpec(memory_space=pltpu.VMEM)
        query, keyval, out, base, sums = pl.pallas_call(
            functools.partial(place_kernel, count, q_cols, kv_cols),
            in_specs=[pl.BlockSpec(memory_space=pltpu.SMEM)] + [in_vmem] * (2 * count + 3),
            out_specs=[in_vmem] * 5,
            out_shape=[wide, narrow, wide, lanes, lanes],
            compiler_params=pltpu.CompilerParams(vmem_limit_bytes=24 * 1024 * 1024),
            cost_estimate=pl.CostEstimate(flops=0, bytes_accessed=0, transcendentals=0),
        )(place.astype(jnp.int32).reshape(1), *blocks, *outs, w_query, w_keyval, gain)
        return query, keyval, out, base[:, 0], sums
    blocks = from_relative(blocks, place).astype(F32)
    outs = from_relative(outs, place).astype(F32)

    def columns(begin, end):
        return blocks[:, :, begin:end].transpose(1, 0, 2).reshape(part, count * (end - begin))

    query, keyval = columns(0, q_cols), columns(q_cols, start)
    base = jnp.sum(w_query.astype(F32) * query, axis=1) + jnp.sum(
        w_keyval.astype(F32) * keyval, axis=1
    )
    sums = jnp.sum(blocks[:, :, start : start + LANES], axis=0)
    out = outs.transpose(1, 0, 2).reshape(part, count * q_cols)
    return query * gain, keyval * gain, out, base, sums


def local(
    tokens,
    teacher,
    valid,
    routes,
    slots,
    gain_attn,
    w_query,
    w_keyval,
    w_out,
    gain_ffn,
    w_router,
    w_gate_up,
    w_down,
):
    seqs = lax.axis_size("seq")
    shards = lax.axis_size("fsdp")
    z = lax.axis_index("seq")
    shard = lax.axis_index("fsdp")
    rows, width = tokens.shape
    groups = HEADS // KVH
    local_kv = KVH // seqs
    q_cols = local_kv * groups * HD
    kv_cols = local_kv * 2 * HD
    local_rows = rows * seqs
    seq_len = local_rows * shards
    experts, part, both = w_gate_up.shape
    units = both // 2
    split = seqs // experts
    piece = units // split
    expert = z // split
    fraction = z % split
    scale = HD ** (-0.5)

    gain_one = gain_attn.astype(F32)[:, None]
    gain_two = gain_ffn.astype(F32)[:, None]
    heads_shard = jnp.concatenate(
        [
            lax.dynamic_slice_in_dim(w_query, z * q_cols, q_cols, 1),
            lax.dynamic_slice_in_dim(w_keyval, z * kv_cols, kv_cols, 1),
        ],
        axis=1,
    )
    heads_shard = (heads_shard.astype(F32) * gain_one).astype(BF)
    heads_full = lax.all_gather(heads_shard, "fsdp", axis=0, tiled=True)
    valid_row = jnp.pad(valid.astype(BF).reshape(1, rows), ((0, 7), (0, width - rows)))
    token_rows = jnp.concatenate([tokens, valid_row], axis=0)
    token_mark = mark(token_rows)
    token_blocks = after(send_out([token_rows] * seqs, seqs), token_mark)

    valid_local = from_relative([each[rows : rows + 1, :rows] for each in token_blocks], z)
    projected = []
    for block in token_blocks:
        projected.append(dot(block[:rows], heads_full) * root(block[:rows].astype(F32)))
    projected = from_relative([each.astype(BF) for each in projected], z)
    projected = projected.reshape(local_rows, q_cols + kv_cols)
    head_queries = projected[:, :q_cols] * jnp.asarray(scale, BF)

    valid_rows_kv = local_rows // kv_cols
    payload = jnp.concatenate(
        [
            projected[:, q_cols:],
            valid_local.reshape(valid_rows_kv, kv_cols),
            jnp.zeros((16 - valid_rows_kv, kv_cols), BF),
        ],
        axis=0,
    )
    kv_blocks = gather_shards(payload, shards)
    late_query, late_keyval, late_router, late_gate_up, late_down = after(
        (w_query, w_keyval, w_router, w_gate_up, w_down), token_mark
    )
    out_full = lax.all_gather(w_out, "fsdp", axis=1, tiled=True)
    own_expert = take(late_gate_up, expert, 0)
    gate_shard = lax.dynamic_slice_in_dim(own_expert, fraction * piece, piece, 1)
    up_shard = lax.dynamic_slice_in_dim(own_expert, units + fraction * piece, piece, 1)
    down_shard = lax.dynamic_slice_in_dim(take(late_down, expert, 0), fraction * piece, piece, 0).T
    router_shard = jnp.pad((late_router.astype(F32) * gain_two).astype(BF), ((0, 0), (0, LANES - experts)))
    expert_shard = jnp.concatenate(
        [
            (gate_shard.astype(F32) * gain_two).astype(BF),
            (up_shard.astype(F32) * gain_two).astype(BF),
            down_shard,
            router_shard,
        ],
        axis=1,
    )
    expert_full = lax.all_gather(expert_shard, "fsdp", axis=0, tiled=True)
    router_full = expert_full[:, 3 * piece :]
    attn_shard = jnp.concatenate(
        [
            each
            for s in range(seqs)
            for each in (
                late_query[:, s * q_cols : (s + 1) * q_cols],
                late_keyval[:, s * kv_cols : (s + 1) * kv_cols],
            )
        ],
        axis=1,
    )
    attn_full = lax.all_gather(
        (attn_shard.astype(F32) * gain_one).astype(BF), "fsdp", axis=0, tiled=True
    )
    order = jnp.asarray(
        [2 * m for m in range(shards // 2)] + [2 * m + 1 for m in range(shards // 2)], jnp.int32
    )
    valid_all = jnp.stack(
        [
            each[local_rows : local_rows + valid_rows_kv].reshape(seqs, rows)
            for each in kv_blocks
        ],
        axis=1,
    ).astype(F32)
    valid_count = jnp.sum(valid_all)
    bias = jnp.where(valid_all > 0, 0.0, FLOOR_SCORE)
    earlier = ((order ^ shard) < shard) | (order == 0)
    bias_same = jnp.where(earlier[None, :, None], bias, FLOOR_SCORE)
    bias = jnp.concatenate([bias, bias_same]).reshape(2 * seqs, 1, shards * rows)
    attended_low, exact, lse = flash_forward(
        head_queries, kv_blocks, bias, seqs, rows, local_kv, groups
    )
    attended = lax.all_to_all(attended_low, "seq", split_axis=0, concat_axis=1, tiled=True)

    inputs = tokens.astype(F32)
    residual = inputs + dot(attended, out_full)
    factor_two = root(residual)
    normed_two = (residual * factor_two).astype(BF)
    logits = dot(normed_two, router_full)[:, :experts]
    expert_ids = jnp.arange(experts, dtype=jnp.int32)
    picked = (routes[:, :, None] == expert_ids).astype(F32)
    chosen = jnp.sum(picked * logits[:, None, :], axis=-1)
    gating = jax.nn.softmax(chosen, axis=-1)
    owners = ((jnp.arange(seqs, dtype=jnp.int32) + z) % seqs) // split
    to_owner = routes[:, :, None] == owners
    slot_hot = slots[:, :, None] == jnp.arange(CAP, dtype=jnp.int32)
    placed = (to_owner[:, :, :, None] & slot_hot[:, :, None, :]).astype(BF)
    placed = placed.reshape(rows, 2, seqs * CAP)
    dispatch = placed[:, 0] + placed[:, 1]
    placed_pairs = jnp.concatenate([placed[:, 0], placed[:, 1]], axis=0)
    sent_rows = dot_tn(dispatch, normed_two).astype(BF)
    kv_all = jnp.stack(after(kv_blocks, sent_rows))
    sent_rows = sent_rows.reshape(seqs, CAP, width)
    expert_rows, gate_up, hidden, *expert_out = experts_forward(
        send_out([sent_rows[s] for s in range(seqs)], seqs), expert_full, piece
    )
    returned = jnp.concatenate(after(send_back(expert_out, seqs), kv_all))
    selected = dot(placed_pairs, returned).reshape(2, rows, width)
    mixed_exact = residual + gating[:, :1] * selected[0] + gating[:, 1:] * selected[1]
    valid_rows = valid.astype(F32)
    errors = (mixed_exact - teacher.astype(F32)) * valid_rows[:, None]
    squares = jnp.sum(errors * errors)
    loss_scale = width * seq_len // 8
    grad_mixed = errors * (2.0 * loss_scale / (width * valid_count))

    grad_gating = jnp.stack(
        [jnp.sum(selected[0] * grad_mixed, axis=-1), jnp.sum(selected[1] * grad_mixed, axis=-1)],
        axis=1,
    )
    grad_chosen = gating * (grad_gating - jnp.sum(gating * grad_gating, axis=-1, keepdims=True))
    grad_logits = jnp.sum(grad_chosen[:, :, None] * picked, axis=1).astype(BF)
    grad_logits = jnp.pad(grad_logits, ((0, 0), (0, LANES - experts)))
    weighted = jnp.concatenate(
        [(gating[:, :1] * grad_mixed).astype(BF), (gating[:, 1:] * grad_mixed).astype(BF)], axis=0
    )
    sent_grads = dot_tn(placed_pairs, weighted).astype(BF).reshape(seqs, CAP, width)
    grad_out_rows = send_out([sent_grads[s] for s in range(seqs)], seqs)
    grad_out_rows = after(grad_out_rows, attn_full, grad_logits)
    grad_expert_out, grad_gate_up_rows, *grad_rows = experts_backward(
        grad_out_rows, gate_up, expert_full, piece
    )
    grad_returned = send_back(grad_rows, seqs)
    tokens_local = from_relative(
        [each[:rows] for each in after(token_blocks, grad_rows)], z
    ).reshape(local_rows, width)
    factor_local = root(tokens_local.astype(F32))
    ride_rows = jnp.concatenate([normed_two, jnp.ones((16, width), BF)], axis=0)
    product_rows = jnp.concatenate([tokens_local, ride_rows], axis=0)
    high, low = two_parts(squares)
    lane = jnp.arange(LANES, dtype=jnp.int32)[None, :]
    marks = jnp.where(lane == experts + 2 * (shard % 2), high, 0) + jnp.where(
        lane == experts + 1 + 2 * (shard % 2), low, 0
    )
    ride_columns = jnp.concatenate(
        [grad_logits, marks.astype(BF), jnp.zeros((15, LANES), BF)], axis=0
    )
    held_out, held_hidden = after((grad_expert_out, hidden), grad_rows)
    down_far, down_near = split_product(held_out, held_hidden, shard, shards)
    grad_down_sums = pair_sums(down_near, hop(down_far, shards, 1), shard)
    held_rows, held_gate_up = after((expert_rows, grad_gate_up_rows), grad_rows)
    gate_up_far, gate_up_near = split_product(held_rows, held_gate_up, shard, shards)
    grad_gate_up_sums = pair_sums(gate_up_near, hop(gate_up_far, shards, 1), shard)
    grad_down_blocks = send_chips(grad_down_sums, shards)
    grad_returned = jnp.concatenate(after(grad_returned, grad_down_sums, product_rows, ride_columns, factor_local))
    grad_normed_two = dot(dispatch, grad_returned) + dot_nt(grad_logits, router_full)
    grad_residual = grad_mixed + root_back(residual, factor_two, grad_normed_two)
    grad_branch = grad_residual.astype(BF)
    grad_attended = dot_nt(after(grad_branch, grad_gate_up_sums), out_full).astype(BF)
    head_grad = lax.all_to_all(grad_attended, "seq", split_axis=1, concat_axis=0, tiled=True)
    grad_gate_up_blocks = send_chips(grad_gate_up_sums, shards)
    grad_down_shard = total_of(after(grad_down_blocks, grad_attended)).astype(BF)
    grad_down = lax.all_gather(grad_down_shard, "seq", axis=0, tiled=False)

    out_far, out_near = split_product(
        after(grad_branch, grad_attended), attended, shard, shards
    )
    grad_q, near, far = [], [], []
    held = after(head_grad, grad_down_shard)
    for g in range(local_kv):
        part_q, near_kv, far_kv = flash_backward(
            head_queries, kv_all, bias, held, exact, lse, seqs, rows, g, groups
        )
        if g == 0:
            grad_gate_up_blocks = after(grad_gate_up_blocks, part_q)
            grad_gate_up_shard = total_of(grad_gate_up_blocks).astype(BF)
            steps = [(grad_gate_up_shard, grad_gate_up_shard)]
            steps.append(relay_step(steps[0], seqs))
            out_there = hop(after(out_far, head_grad), shards, 1)
        grad_q.append(part_q)
        near.append(near_kv)
        far.append(far_kv)
        held = after(head_grad, grad_gate_up_shard, out_there)
    steps[1] = after(steps[1], part_q)
    steps.append(relay_step(steps[1], seqs))
    far = after(far, steps[1], grad_down)
    pairs = kv_pair_sums(near, [hop(each, shards, 1) for each in far])
    out_sums = pair_sums(out_near, after(out_there, pairs), shard)
    sent_grads, product_columns = head_columns(
        grad_q, after(send_chips(pairs, shards), out_sums, steps[2]), factor_local, ride_columns
    )
    steps[2] = after(steps[2], product_columns)
    while len(steps) < seqs:
        steps.append(relay_step(steps[-1], seqs))
    token_grads = lax.all_to_all(sent_grads, "seq", split_axis=0, concat_axis=1, tiled=True)

    head_cols = q_cols + kv_cols
    head_far, head_near = split_product(product_rows, product_columns, shard, shards)
    head_sums = pair_sums(head_near, hop(head_far, shards, 1), shard)
    out_part = total_of(
        after(send_chips(after(out_sums, product_columns), shards), head_sums)
    ).astype(BF)
    out_parts = lax.all_to_all(
        out_part.reshape(part, seqs, q_cols), "seq", split_axis=1, concat_axis=1, tiled=True
    )
    head_blocks = send_chips(head_sums, shards)
    head_part = total_of(after(head_blocks, steps[3]))
    grad_normed = dot_nt(after(token_grads, head_part, out_parts), attn_full)
    grad_tokens = grad_residual + root_back(inputs, root(inputs), grad_normed)
    base_cols = head_cols + experts
    plane_high, plane_low = two_parts(
        jnp.sum(head_part[:1, base_cols : base_cols + 4], axis=1, keepdims=True)
    )
    lanes = lax.broadcasted_iota(jnp.int32, head_part.shape, 1)
    head_part = jnp.where(
        lanes == base_cols,
        plane_high.astype(F32),
        jnp.where(lanes == base_cols + 1, plane_low.astype(F32), head_part),
    )
    head_part = by_rows(head_part.astype(BF))
    head_last = [by_rows(each) for each in send_out([head_part] * seqs, seqs)]
    out_own = by_rows(jnp.sum(out_parts.astype(F32), axis=1).astype(BF))
    out_last = [by_rows(each) for each in send_out([out_own] * seqs, seqs)]
    grad_gate_up, grad_gain_ffn = place_gate_up(after(steps, head_part), w_gate_up, gain_two, z)
    head_last, out_last = after((head_last, out_last), grad_gate_up)
    grad_query, grad_keyval, grad_out, grad_gain_attn, sums = place_heads(
        head_last, out_last, z, w_query, w_keyval, gain_one, q_cols, kv_cols
    )
    loss_value = jnp.sum(sums[0, experts : experts + 2]) / (width * valid_count)
    grad_router_base = sums[:, :experts]
    grad_down = (
        after(grad_down, head_part).reshape(experts, split, part, piece)
        .transpose(0, 1, 3, 2)
        .reshape(experts, units, part)
        .astype(F32)
    )
    grad_gain_ffn = grad_gain_ffn + jnp.sum(w_router.astype(F32) * grad_router_base, axis=1)
    return (
        mixed_exact.astype(BF),
        loss_value,
        grad_tokens,
        grad_gain_attn,
        grad_query,
        grad_keyval,
        grad_out.T,
        grad_gain_ffn,
        grad_router_base * gain_two,
        grad_gate_up,
        grad_down,
    )


def solution(mesh):
    return jax.shard_map(
        local,
        mesh=mesh,
        in_specs=(
            P(("seq", "fsdp"), None),
            P(("seq", "fsdp"), None),
            P(("seq", "fsdp")),
            P(("seq", "fsdp"), None),
            P(("seq", "fsdp"), None),
            P("fsdp"),
            P("fsdp", None),
            P("fsdp", None),
            P(None, "fsdp"),
            P("fsdp"),
            P("fsdp", None),
            P(None, "fsdp", None),
            P(None, None, "fsdp"),
        ),
        out_specs=(
            P(("seq", "fsdp"), None),
            P(),
            P(("seq", "fsdp"), None),
            P("fsdp"),
            P("fsdp", None),
            P("fsdp", None),
            P(None, "fsdp"),
            P("fsdp"),
            P("fsdp", None),
            P(None, "fsdp", None),
            P(None, None, "fsdp"),
        ),
        check_vma=False,
    )
```

```python
import functools
import math

import jax
import jax.numpy as jnp
from jax import lax
from jax.experimental import pallas as pl
from jax.experimental.layout import Layout, with_layout_constraint
from jax.experimental.pallas import tpu as pltpu
from jax.sharding import PartitionSpec as P

HEADS = 24
KVH = 8
HD = 64
CAP = 96
LANES = 128
EPSILON = 1e-06
FLOOR_SCORE = -1e30
BF = jnp.bfloat16
F32 = jnp.float32


def dot(a, b):
    return jnp.dot(a, b, preferred_element_type=F32)


def dot_nt(a, b):
    return lax.dot_general(a, b, (((1,), (1,)), ((), ())), preferred_element_type=F32)


def dot_tn(a, b):
    return lax.dot_general(a, b, (((0,), (0,)), ((), ())), preferred_element_type=F32)


def own_mask(valid_row, rows):
    i = lax.broadcasted_iota(jnp.int32, (rows, rows), 0)
    j = lax.broadcasted_iota(jnp.int32, (rows, rows), 1)
    return jnp.where(j == i, 0.0, jnp.where(j < i, valid_row, FLOOR_SCORE))


def key_chunk(kv_refs, zk, rows, g):
    return jnp.concatenate(
        [ref[pl.ds(zk * rows, rows), pl.ds(g * 2 * HD, 2 * HD)] for ref in kv_refs], axis=0
    )


def forward_kernel(shards, seqs, rows, local_kv, groups, *refs):
    kv_refs = refs[:shards]
    q_ref, bias_ref, low_ref, exact_ref, lse_ref, acc_ref, max_ref = refs[shards:]
    zq = pl.program_id(0)
    stack = groups * rows
    zeros = jnp.zeros((rows, HD), BF)
    half = lax.broadcasted_iota(jnp.int32, (1, 2 * HD), 1) < HD

    def queries(g):
        parts = []
        for h in range(groups):
            start = (g * groups + h) * HD
            parts.append(jnp.concatenate([q_ref[:, start : start + HD], zeros], axis=1))
        return jnp.concatenate(parts, axis=0)

    def chunk(g, zk, scores):
        first = scores is None
        keys = key_chunk(kv_refs, zk, rows, g)
        raw = dot_nt(queries(g), keys)
        if first:
            row = bias_ref[seqs + zk]
            mask = own_mask(row[:, :rows], rows)
            mask = jnp.concatenate([mask] * groups, axis=0)
            masked = jnp.concatenate([raw[:, :rows] + mask, raw[:, rows:] + row[:, rows:]], axis=1)
            new_max = jnp.max(masked, axis=1, keepdims=True)
        else:
            masked = raw + bias_ref[zk]
            new_max = jnp.maximum(max_ref[g][:, :1], jnp.max(masked, axis=1, keepdims=True))
        terms = jnp.exp(masked - new_max).astype(BF)
        ones_values = jnp.where(half, jnp.ones_like(keys), keys)
        part = dot(terms, ones_values)
        if first:
            acc_ref[g] = part
        else:
            acc_ref[g] = acc_ref[g] * jnp.exp(max_ref[g][:, :1] - new_max) + part
        max_ref[g] = jnp.broadcast_to(new_max, (stack, 2 * HD))

    for g in range(local_kv):
        chunk(g, zq, None)

    @pl.loop(0, zq)
    def _(zk):
        for g in range(local_kv):
            chunk(g, zk, True)

    exact_parts, lse_parts = [], []
    for g in range(local_kv):
        acc = acc_ref[g]
        total = acc[:, :HD]
        exact = acc[:, HD:] / total
        lse = max_ref[g][:, :HD] + jnp.log(total)
        for h in range(groups):
            exact_parts.append(exact[h * rows : (h + 1) * rows])
            lse_parts.append(lse[h * rows : (h + 1) * rows])
    exact = jnp.concatenate(exact_parts, axis=1)
    exact_ref[...] = exact
    low_ref[...] = exact.astype(BF)
    lse_ref[...] = jnp.concatenate(lse_parts, axis=1)


def flash_forward(q, kv_blocks, bias, seqs, rows, local_kv, groups):
    shards = len(kv_blocks)
    q_cols = q.shape[1]
    kv_spec = pl.BlockSpec(kv_blocks[0].shape, lambda i: (0, 0))
    q_spec = pl.BlockSpec((rows, q_cols), lambda i: (i, 0))
    stack = groups * rows
    out = jax.ShapeDtypeStruct((seqs * rows, q_cols), F32)
    return pl.pallas_call(
        functools.partial(forward_kernel, shards, seqs, rows, local_kv, groups),
        grid=(seqs,),
        in_specs=[kv_spec] * shards + [q_spec, pl.BlockSpec(bias.shape, lambda i: (0, 0, 0))],
        out_specs=[q_spec] * 3,
        out_shape=[jax.ShapeDtypeStruct((seqs * rows, q_cols), BF), out, out],
        scratch_shapes=[
            pltpu.VMEM((local_kv, stack, 2 * HD), F32),
            pltpu.VMEM((local_kv, stack, 2 * HD), F32),
        ],
        compiler_params=pltpu.CompilerParams(vmem_limit_bytes=24 * 1024 * 1024),
        cost_estimate=pl.CostEstimate(
            flops=0,
            bytes_accessed=0,
            transcendentals=0,
        ),
    )(*kv_blocks, q, bias)


def backward_kernel(shards, seqs, rows, g, groups, *refs):
    kv_refs = [refs[0].at[p] for p in range(shards)]
    (
        q_ref, bias_ref, grad_ref, exact_ref, lse_ref, grad_q_ref, near_ref, far_ref,
        pair_ref, pair_t_ref, lse_wide, delta_wide, acc_q, acc_kv,
    ) = refs[1:]
    zk = pl.program_id(0)
    stack = groups * rows
    zeros = jnp.zeros((rows, HD), BF)

    @pl.when(zk == 0)
    def _():
        acc_q[...] = jnp.zeros_like(acc_q)

        @pl.loop(0, seqs)
        def _(zq):
            here = pl.ds(zq * rows, rows)
            tops, bottoms = [], []
            for h in range(groups):
                cols = slice((g * groups + h) * HD, (g * groups + h + 1) * HD)
                grad = grad_ref[here, cols]
                tops.append(jnp.concatenate([q_ref[here, cols], zeros], axis=1))
                bottoms.append(jnp.concatenate([zeros, grad], axis=1))
                delta = jnp.sum(grad.astype(F32) * exact_ref[here, cols], axis=1, keepdims=True)
                part = slice(h * rows, (h + 1) * rows)
                delta_wide[zq, part] = jnp.broadcast_to(delta, (rows, 2 * HD))
                lse_wide[zq, part] = jnp.broadcast_to(lse_ref[here, cols][:, :1], (rows, 2 * HD))
            pair = jnp.concatenate(tops + bottoms, axis=0)
            pair_ref[zq] = pair
            pair_t_ref[zq] = pair.astype(F32).T.astype(BF)

    def chunk(zq, first):
        keys = key_chunk(kv_refs, zk, rows, g)
        both = dot_nt(pair_ref[zq], keys)
        raw, products = both[:stack], both[stack:]
        if first:
            row = bias_ref[seqs + zk]
            mask = own_mask(row[:, :rows], rows)
            mask = jnp.concatenate([mask] * groups, axis=0)
            masked = jnp.concatenate([raw[:, :rows] + mask, raw[:, rows:] + row[:, rows:]], axis=1)
        else:
            masked = raw + bias_ref[zk]
        weights = jnp.exp(masked - lse_wide[zq][:, :1])
        grads = (weights * (products - delta_wide[zq][:, :1])).astype(BF)
        acc_q[zq] += dot(grads, keys)
        part = dot(pair_t_ref[zq], jnp.concatenate([grads, weights.astype(BF)], axis=0))
        if first:
            acc_kv[...] = part
        else:
            acc_kv[...] += part

    chunk(zk, True)

    @pl.loop(zk + 1, seqs)
    def _(zq):
        chunk(zq, False)

    for p in range(shards):
        target = near_ref if p < shards // 2 else far_ref
        target[p % (shards // 2)] = acc_kv[:, p * rows : (p + 1) * rows].T.astype(BF)

    @pl.when(zk == seqs - 1)
    def _():
        @pl.loop(0, seqs)
        def _(zq):
            total = acc_q[zq]
            parts = [total[h * rows : (h + 1) * rows, :HD] for h in range(groups)]
            grad_q_ref[pl.ds(zq * rows, rows), :] = jnp.concatenate(parts, axis=1) * HD ** (-0.5)


def flash_backward(q, kv_all, bias, grad, exact, lse, seqs, rows, g, groups):
    shards = kv_all.shape[0]
    q_cols = q.shape[1]
    stack = groups * rows
    kv_spec = pl.BlockSpec(kv_all.shape, lambda i: (0, 0, 0))
    whole = pl.BlockSpec((seqs * rows, q_cols), lambda i: (0, 0))
    grad_q_shape = (seqs * rows, groups * HD)
    out_spec = pl.BlockSpec((shards // 2, rows, 2 * HD), lambda i: (0, i, 0))
    out = jax.ShapeDtypeStruct((shards // 2, seqs * rows, 2 * HD), BF)
    return pl.pallas_call(
        functools.partial(backward_kernel, shards, seqs, rows, g, groups),
        grid=(seqs,),
        in_specs=[kv_spec]
        + [whole, pl.BlockSpec(bias.shape, lambda i: (0, 0, 0)), whole, whole, whole],
        out_specs=[pl.BlockSpec(grad_q_shape, lambda i: (0, 0)), out_spec, out_spec],
        out_shape=[jax.ShapeDtypeStruct(grad_q_shape, F32), out, out],
        scratch_shapes=[
            pltpu.VMEM((seqs, 2 * stack, 2 * HD), BF),
            pltpu.VMEM((seqs, 2 * HD, 2 * stack), BF),
            pltpu.VMEM((seqs, stack, 2 * HD), F32),
            pltpu.VMEM((seqs, stack, 2 * HD), F32),
            pltpu.VMEM((seqs, stack, 2 * HD), F32),
            pltpu.VMEM((2 * HD, shards * rows), F32),
        ],
        compiler_params=pltpu.CompilerParams(vmem_limit_bytes=28 * 1024 * 1024),
        cost_estimate=pl.CostEstimate(
            flops=0 if g else 10**12,
            bytes_accessed=0,
            transcendentals=0,
        ),
    )(kv_all, q, bias, grad, exact, lse)


def shift(block, count, step):
    return lax.ppermute(block, "seq", [(i, (i + step) % count) for i in range(count)])


def send_out(blocks, count):
    return [blocks[0]] + [shift(blocks[s], count, s) for s in range(1, count)]


def send_back(blocks, count):
    return [blocks[0]] + [shift(blocks[s], count, count - s) for s in range(1, count)]


def relay_step(blocks, count):
    up, down = blocks
    return (
        lax.ppermute(up, "seq", [(i, i + 1) for i in range(count - 1)]),
        lax.ppermute(down, "seq", [(i + 1, i) for i in range(count - 1)]),
    )


def from_relative(blocks, place):
    count = len(blocks)
    rising = jnp.stack([blocks[-s % count] for s in range(count)])
    return lax.dynamic_slice_in_dim(jnp.concatenate([rising, rising]), count - place, count, 0)


def hop(block, count, mask):
    return lax.ppermute(block, "fsdp", [(i, i ^ mask) for i in range(count)])


def gather_shards(block, count):
    near = [block] + [hop(block, count, 2 * m) for m in range(1, count // 2)]
    return near + [hop(each, count, 1) for each in near]


def send_chips(parts, count):
    return [parts[0]] + [hop(parts[m], count, 2 * m) for m in range(1, count // 2)]


def total_of(blocks):
    total = blocks[0].astype(F32)
    for each in blocks[1:]:
        total = total + each.astype(F32)
    return total


def take(array, index, axis):
    return lax.dynamic_index_in_dim(array, index, axis, keepdims=False)


def product_kernel(core_ref, lhs_ref, rhs_ref, far_ref, near_ref):
    part = lhs_ref.shape[1] // 2
    rhs = rhs_ref[...]
    first = dot_tn(lhs_ref[:, :part], rhs).astype(BF)
    second = dot_tn(lhs_ref[:, part:], rhs).astype(BF)
    core = core_ref[0]

    @pl.when(core == 0)
    def _():
        near_ref[0] = first
        far_ref[0] = second

    @pl.when(core != 0)
    def _():
        near_ref[0] = second
        far_ref[0] = first


def split_product(lhs, rhs, shard, count):
    tokens, width = lhs.shape
    cols = rhs.shape[1]
    part = width // count
    if 2 * part % LANES:
        cut = dot_tn(lhs, rhs).astype(BF).reshape(count // 2, 2, part, cols)
        return take(cut, 1 - shard % 2, 1), take(cut, shard % 2, 1)
    out = jax.ShapeDtypeStruct((count // 2, part, cols), BF)
    out_spec = pl.BlockSpec((1, part, cols), lambda i: (i, 0, 0))
    return pl.pallas_call(
        product_kernel,
        grid=(count // 2,),
        in_specs=[
            pl.BlockSpec(memory_space=pltpu.SMEM),
            pl.BlockSpec((tokens, 2 * part), lambda i: (0, i)),
            pl.BlockSpec((tokens, cols), lambda i: (0, 0)),
        ],
        out_specs=[out_spec, out_spec],
        out_shape=[out, out],
        compiler_params=pltpu.CompilerParams(vmem_limit_bytes=24 * 1024 * 1024),
        cost_estimate=pl.CostEstimate(flops=0, bytes_accessed=0, transcendentals=0),
    )((shard % 2).astype(jnp.int32).reshape(1), lhs, rhs)


def pair_kernel(chip_ref, near_ref, there_ref, own_ref, *part_refs):
    chip = chip_ref[0]
    own_ref[...] = near_ref[chip].astype(F32) + there_ref[chip].astype(F32)
    for m, part_ref in enumerate(part_refs):
        which = chip ^ (m + 1)
        part_ref[...] = (near_ref[which].astype(F32) + there_ref[which].astype(F32)).astype(BF)


def pair_sums(near, there, shard):
    chips, part, cols = near.shape
    tile = math.gcd(cols, 512)
    if tile % LANES:
        tile = cols
    block = pl.BlockSpec((chips, part, tile), lambda i: (0, 0, i))
    out_spec = pl.BlockSpec((part, tile), lambda i: (0, i))
    out = jax.ShapeDtypeStruct((part, cols), BF)
    return pl.pallas_call(
        pair_kernel,
        grid=(cols // tile,),
        in_specs=[pl.BlockSpec(memory_space=pltpu.SMEM), block, block],
        out_specs=[out_spec] * chips,
        out_shape=[jax.ShapeDtypeStruct((part, cols), F32)] + [out] * (chips - 1),
        compiler_params=pltpu.CompilerParams(vmem_limit_bytes=24 * 1024 * 1024),
        cost_estimate=pl.CostEstimate(flops=0, bytes_accessed=0, transcendentals=0),
    )((shard // 2).astype(jnp.int32).reshape(1), near, there)


def fetch_weights(weights_ref, held, sems, piece):
    copies = [
        pltpu.make_async_copy(
            weights_ref.at[:, pl.ds(part * piece, piece)], held.at[part], sems.at[part]
        )
        for part in range(3)
    ]
    return copies


def experts_forward_kernel(count, *refs):
    rows_in, weights_ref = refs[:count], refs[count]
    rows_ref, gate_up_ref, hidden_ref = refs[count + 1 : count + 4]
    out_refs, (held, sems) = refs[count + 4 : -2], refs[-2:]
    piece = hidden_ref.shape[1]
    cap = rows_in[0].shape[0]
    copies = fetch_weights(weights_ref, held, sems, piece)
    for copy in copies:
        copy.start()
    for s in range(count):
        rows_ref[s * cap : (s + 1) * cap, :] = rows_in[s][...]
    rows = rows_ref[...]
    copies[0].wait()
    gate = dot(rows, held[0])
    gate_up_ref[:, :piece] = gate
    copies[1].wait()
    up = dot(rows, held[1])
    gate_up_ref[:, piece:] = up
    hidden = (gate / (1.0 + jnp.exp(-gate)) * up).astype(BF)
    hidden_ref[...] = hidden
    copies[2].wait()
    out = dot_nt(hidden, held[2]).astype(BF)
    for s in range(count):
        out_refs[s][...] = out[s * cap : (s + 1) * cap, :]


def experts_forward(blocks, weights, piece):
    count = len(blocks)
    cap, width = blocks[0].shape
    rows = count * cap
    in_vmem = pl.BlockSpec(memory_space=pltpu.VMEM)
    return pl.pallas_call(
        functools.partial(experts_forward_kernel, count),
        in_specs=[in_vmem] * count + [pl.BlockSpec(memory_space=pltpu.HBM)],
        out_specs=[in_vmem] * (3 + count),
        out_shape=[
            jax.ShapeDtypeStruct((rows, width), BF),
            jax.ShapeDtypeStruct((rows, 2 * piece), F32),
            jax.ShapeDtypeStruct((rows, piece), BF),
        ]
        + [jax.ShapeDtypeStruct((cap, width), BF)] * count,
        scratch_shapes=[pltpu.VMEM((3, width, piece), BF), pltpu.SemaphoreType.DMA((3,))],
        compiler_params=pltpu.CompilerParams(vmem_limit_bytes=56 * 1024 * 1024),
        cost_estimate=pl.CostEstimate(flops=0, bytes_accessed=0, transcendentals=0),
    )(*blocks, weights)


def experts_backward_kernel(count, *refs):
    grads_in, gate_up_ref, weights_ref = refs[:count], refs[count], refs[count + 1]
    grads_ref, rows_ref = refs[count + 2 : count + 4]
    out_refs, (held, sems) = refs[count + 4 : -2], refs[-2:]
    piece = rows_ref.shape[1] // 2
    cap = grads_in[0].shape[0]
    copies = fetch_weights(weights_ref, held, sems, piece)
    for copy in (copies[2], copies[0], copies[1]):
        copy.start()
    for s in range(count):
        grads_ref[s * cap : (s + 1) * cap, :] = grads_in[s][...]
    copies[2].wait()
    grad_hidden = dot(grads_ref[...], held[2])
    gate = gate_up_ref[:, :piece]
    up = gate_up_ref[:, piece:]
    slope = 1.0 / (1.0 + jnp.exp(-gate))
    grad_gate = (grad_hidden * up * slope * (1.0 + gate * (1.0 - slope))).astype(BF)
    grad_up = (grad_hidden * gate * slope).astype(BF)
    rows_ref[:, :piece] = grad_gate
    rows_ref[:, piece:] = grad_up
    copies[0].wait()
    total = dot_nt(grad_gate, held[0])
    copies[1].wait()
    total = (total + dot_nt(grad_up, held[1])).astype(BF)
    for s in range(count):
        out_refs[s][...] = total[s * cap : (s + 1) * cap, :]


def experts_backward(blocks, gate_up, weights, piece):
    count = len(blocks)
    cap, width = blocks[0].shape
    rows = count * cap
    in_vmem = pl.BlockSpec(memory_space=pltpu.VMEM)
    return pl.pallas_call(
        functools.partial(experts_backward_kernel, count),
        in_specs=[in_vmem] * (count + 1) + [pl.BlockSpec(memory_space=pltpu.HBM)],
        out_specs=[in_vmem] * (2 + count),
        out_shape=[
            jax.ShapeDtypeStruct((rows, width), BF),
            jax.ShapeDtypeStruct((rows, 2 * piece), BF),
        ]
        + [jax.ShapeDtypeStruct((cap, width), BF)] * count,
        scratch_shapes=[pltpu.VMEM((3, width, piece), BF), pltpu.SemaphoreType.DMA((3,))],
        compiler_params=pltpu.CompilerParams(vmem_limit_bytes=56 * 1024 * 1024),
        cost_estimate=pl.CostEstimate(flops=0, bytes_accessed=0, transcendentals=0),
    )(*blocks, gate_up, weights)


def kv_pair_kernel(heads, chips, *refs):
    near, there, outs = refs[:heads], refs[heads : 2 * heads], refs[2 * heads :]
    for m in range(chips):
        for g in range(heads):
            total = near[g][m].astype(F32) + there[g][m].astype(F32)
            outs[m][:, g * 2 * HD : (g + 1) * 2 * HD] = total.astype(outs[m].dtype)


def kv_pair_sums(near, there):
    heads, (chips, rows, cols) = len(near), near[0].shape
    in_vmem = pl.BlockSpec(memory_space=pltpu.VMEM)
    out = jax.ShapeDtypeStruct((rows, heads * cols), BF)
    return pl.pallas_call(
        functools.partial(kv_pair_kernel, heads, chips),
        in_specs=[in_vmem] * (2 * heads),
        out_specs=[in_vmem] * chips,
        out_shape=[jax.ShapeDtypeStruct((rows, heads * cols), F32)] + [out] * (chips - 1),
        compiler_params=pltpu.CompilerParams(vmem_limit_bytes=20 * 1024 * 1024),
        cost_estimate=pl.CostEstimate(flops=0, bytes_accessed=0, transcendentals=0),
    )(*near, *there)


def head_columns_kernel(heads, chips, *refs):
    queries, sums = refs[:heads], refs[heads : heads + chips]
    factor_ref, ride_ref, sent_ref, columns_ref = refs[heads + chips :]
    query = jnp.concatenate([each[...] for each in queries], axis=1)
    keyval = sums[0][...]
    for each in sums[1:]:
        keyval = keyval + each[...].astype(F32)
    both = jnp.concatenate([query, keyval], axis=1)
    rows, cols = both.shape
    sent_ref[...] = both.astype(BF)
    columns_ref[:rows, :cols] = (both * factor_ref[...]).astype(BF)
    columns_ref[:rows, cols:] = jnp.zeros((rows, LANES), BF)
    columns_ref[rows:, :cols] = jnp.zeros((ride_ref.shape[0], cols), BF)
    columns_ref[rows:, cols:] = ride_ref[...]


def head_columns(queries, sums, factor, ride):
    rows = sums[0].shape[0]
    cols = sum(each.shape[1] for each in queries) + sums[0].shape[1]
    if cols % LANES:
        both = jnp.concatenate(list(queries) + [total_of(sums)], axis=1)
        scaled = jnp.pad((both * factor).astype(BF), ((0, 0), (0, LANES)))
        return both.astype(BF), jnp.concatenate([scaled, jnp.pad(ride, ((0, 0), (cols, 0)))])
    in_vmem = pl.BlockSpec(memory_space=pltpu.VMEM)
    return pl.pallas_call(
        functools.partial(head_columns_kernel, len(queries), len(sums)),
        in_specs=[in_vmem] * (len(queries) + len(sums) + 2),
        out_specs=[in_vmem] * 2,
        out_shape=[
            jax.ShapeDtypeStruct((rows, cols), BF),
            jax.ShapeDtypeStruct((rows + ride.shape[0], cols + LANES), BF),
        ],
        compiler_params=pltpu.CompilerParams(vmem_limit_bytes=20 * 1024 * 1024),
        cost_estimate=pl.CostEstimate(flops=0, bytes_accessed=0, transcendentals=0),
    )(*queries, *sums, factor, ride)


def two_parts(value):
    high = value.astype(BF)
    return high, (value - high.astype(F32)).astype(BF)


def mark_kernel(seed_ref, out_ref):
    out_ref[...] = seed_ref[...]


def mark(*others):
    seed = after(jnp.zeros((8, LANES), F32), *others)
    return pl.pallas_call(
        mark_kernel,
        out_shape=jax.ShapeDtypeStruct((8, LANES), F32),
        cost_estimate=pl.CostEstimate(flops=10**12, bytes_accessed=8192, transcendentals=0),
    )(seed)


def by_rows(array):
    return with_layout_constraint(array, Layout(major_to_minor=tuple(range(array.ndim))))


def after(values, *others):
    return lax.optimization_barrier((values, others))[0]


def root(values):
    return lax.rsqrt(jnp.mean(values * values, axis=-1, keepdims=True) + EPSILON)


def root_back(values, factor, grad_scaled):
    inner = jnp.mean(grad_scaled * values, axis=-1, keepdims=True)
    return factor * grad_scaled - values * (factor * factor * factor * inner)


def place_gate_up_kernel(count, place_ref, *refs):
    blocks = refs[: 2 * count - 1]
    weight_ref, gain_ref, out_ref, sums_ref, base = refs[2 * count - 1 :]
    offset = place_ref[0] - pl.program_id(1)

    for s in range(2 * count - 1):

        @pl.when(offset == (s if s < count else count - 1 - s))
        def _(s=s):
            base[...] = blocks[s][...].astype(F32)

    @pl.when((pl.program_id(0) == 0) & (pl.program_id(1) == 0))
    def _():
        sums_ref[...] = jnp.zeros_like(sums_ref)

    values = base[...]
    out_ref[0] = values * gain_ref[...]
    product = jnp.sum(weight_ref[0].astype(F32) * values, axis=1, keepdims=True)
    sums_ref[...] += jnp.broadcast_to(product, sums_ref.shape)


def place_gate_up(steps, weight, gain, place):
    experts, part, both = weight.shape
    count = len(steps)
    split = count // experts
    if split == 1:
        tile = math.gcd(both, 1024)
        blocks = [steps[0][0]] + [each[0] for each in steps[1:]] + [each[1] for each in steps[1:]]
        block = pl.BlockSpec((part, tile), lambda t, e: (0, t))
        out, sums = pl.pallas_call(
            functools.partial(place_gate_up_kernel, count),
            grid=(both // tile, experts),
            in_specs=[pl.BlockSpec(memory_space=pltpu.SMEM)]
            + [block] * len(blocks)
            + [
                pl.BlockSpec((1, part, tile), lambda t, e: (e, 0, t)),
                pl.BlockSpec((part, 1), lambda t, e: (0, 0)),
            ],
            out_specs=[
                pl.BlockSpec((1, part, tile), lambda t, e: (e, 0, t)),
                pl.BlockSpec((part, LANES), lambda t, e: (0, 0)),
            ],
            out_shape=[
                jax.ShapeDtypeStruct(weight.shape, F32),
                jax.ShapeDtypeStruct((part, LANES), F32),
            ],
            scratch_shapes=[pltpu.VMEM((part, tile), F32)],
            compiler_params=pltpu.CompilerParams(vmem_limit_bytes=28 * 1024 * 1024),
            cost_estimate=pl.CostEstimate(flops=0, bytes_accessed=0, transcendentals=0),
        )(place.astype(jnp.int32).reshape(1), *blocks, weight, gain)
        return out, sums[:, 0]
    blocks = [steps[0][0]] + [
        jnp.where(place >= s, steps[s][0], steps[count - s][1]) for s in range(1, count)
    ]
    base = (
        from_relative(blocks, place)
        .reshape(experts, split, part, 2, both // (2 * split))
        .transpose(0, 2, 3, 1, 4)
        .reshape(experts, part, both)
        .astype(F32)
    )
    return base * gain, jnp.sum(weight.astype(F32) * base, axis=(0, 2))


def place_kernel(count, q_cols, kv_cols, place_ref, *refs):
    blocks, outs = refs[:count], refs[count : 2 * count]
    w_query_ref, w_keyval_ref, gain_ref, query_ref, keyval_ref, out_ref, base_ref, sums_ref = refs[
        2 * count :
    ]
    gain = gain_ref[...]
    base = jnp.zeros_like(gain)
    sums = jnp.zeros(sums_ref.shape, F32)
    for s in range(count):
        owner = lax.rem(place_ref[0] + (count - s), count)
        q_at = pl.ds(pl.multiple_of(owner * q_cols, LANES), q_cols)
        kv_at = pl.ds(pl.multiple_of(owner * kv_cols, LANES), kv_cols)
        query = blocks[s][:, :q_cols].astype(F32)
        keyval = blocks[s][:, q_cols : q_cols + kv_cols].astype(F32)
        start = q_cols + kv_cols
        sums = sums + blocks[s][:, start : start + LANES].astype(F32)
        out_ref[:, q_at] = outs[s][...].astype(F32)
        base = base + jnp.sum(w_query_ref[:, q_at].astype(F32) * query, axis=1, keepdims=True)
        base = base + jnp.sum(w_keyval_ref[:, kv_at].astype(F32) * keyval, axis=1, keepdims=True)
        query_ref[:, q_at] = query * gain
        keyval_ref[:, kv_at] = keyval * gain
    base_ref[...] = jnp.broadcast_to(base, base_ref.shape)
    sums_ref[...] = sums


def place_heads(blocks, outs, place, w_query, w_keyval, gain, q_cols, kv_cols):
    count = len(blocks)
    part = w_query.shape[0]
    start = q_cols + kv_cols
    if q_cols % LANES == 0 and kv_cols % LANES == 0:
        wide = jax.ShapeDtypeStruct((part, count * q_cols), F32)
        narrow = jax.ShapeDtypeStruct((part, count * kv_cols), F32)
        lanes = jax.ShapeDtypeStruct((part, LANES), F32)
        in_vmem = pl.BlockSpec(memory_space=pltpu.VMEM)
        query, keyval, out, base, sums = pl.pallas_call(
            functools.partial(place_kernel, count, q_cols, kv_cols),
            in_specs=[pl.BlockSpec(memory_space=pltpu.SMEM)] + [in_vmem] * (2 * count + 3),
            out_specs=[in_vmem] * 5,
            out_shape=[wide, narrow, wide, lanes, lanes],
            compiler_params=pltpu.CompilerParams(vmem_limit_bytes=24 * 1024 * 1024),
            cost_estimate=pl.CostEstimate(flops=0, bytes_accessed=0, transcendentals=0),
        )(place.astype(jnp.int32).reshape(1), *blocks, *outs, w_query, w_keyval, gain)
        return query, keyval, out, base[:, 0], sums
    blocks = from_relative(blocks, place).astype(F32)
    outs = from_relative(outs, place).astype(F32)

    def columns(begin, end):
        return blocks[:, :, begin:end].transpose(1, 0, 2).reshape(part, count * (end - begin))

    query, keyval = columns(0, q_cols), columns(q_cols, start)
    base = jnp.sum(w_query.astype(F32) * query, axis=1) + jnp.sum(
        w_keyval.astype(F32) * keyval, axis=1
    )
    sums = jnp.sum(blocks[:, :, start : start + LANES], axis=0)
    out = outs.transpose(1, 0, 2).reshape(part, count * q_cols)
    return query * gain, keyval * gain, out, base, sums


def local(
    tokens,
    teacher,
    valid,
    routes,
    slots,
    gain_attn,
    w_query,
    w_keyval,
    w_out,
    gain_ffn,
    w_router,
    w_gate_up,
    w_down,
):
    seqs = lax.axis_size("seq")
    shards = lax.axis_size("fsdp")
    z = lax.axis_index("seq")
    shard = lax.axis_index("fsdp")
    rows, width = tokens.shape
    groups = HEADS // KVH
    local_kv = KVH // seqs
    q_cols = local_kv * groups * HD
    kv_cols = local_kv * 2 * HD
    local_rows = rows * seqs
    seq_len = local_rows * shards
    experts, part, both = w_gate_up.shape
    units = both // 2
    split = seqs // experts
    piece = units // split
    expert = z // split
    fraction = z % split
    scale = HD ** (-0.5)

    gain_one = gain_attn.astype(F32)[:, None]
    gain_two = gain_ffn.astype(F32)[:, None]
    heads_shard = jnp.concatenate(
        [
            lax.dynamic_slice_in_dim(w_query, z * q_cols, q_cols, 1),
            lax.dynamic_slice_in_dim(w_keyval, z * kv_cols, kv_cols, 1),
        ],
        axis=1,
    )
    heads_shard = (heads_shard.astype(F32) * gain_one).astype(BF)
    heads_full = lax.all_gather(heads_shard, "fsdp", axis=0, tiled=True)
    valid_row = jnp.pad(valid.astype(BF).reshape(1, rows), ((0, 7), (0, width - rows)))
    token_rows = jnp.concatenate([tokens, valid_row], axis=0)
    token_mark = mark(token_rows)
    token_blocks = after(send_out([token_rows] * seqs, seqs), token_mark)

    valid_local = from_relative([each[rows : rows + 1, :rows] for each in token_blocks], z)
    projected = []
    for block in token_blocks:
        projected.append(dot(block[:rows], heads_full) * root(block[:rows].astype(F32)))
    projected = from_relative([each.astype(BF) for each in projected], z)
    projected = projected.reshape(local_rows, q_cols + kv_cols)
    head_queries = projected[:, :q_cols] * jnp.asarray(scale, BF)

    valid_rows_kv = local_rows // kv_cols
    payload = jnp.concatenate(
        [
            projected[:, q_cols:],
            valid_local.reshape(valid_rows_kv, kv_cols),
            jnp.zeros((16 - valid_rows_kv, kv_cols), BF),
        ],
        axis=0,
    )
    kv_blocks = gather_shards(payload, shards)
    late_query, late_keyval, late_router, late_gate_up, late_down = after(
        (w_query, w_keyval, w_router, w_gate_up, w_down), token_mark
    )
    out_full = lax.all_gather(w_out, "fsdp", axis=1, tiled=True)
    own_expert = take(late_gate_up, expert, 0)
    gate_shard = lax.dynamic_slice_in_dim(own_expert, fraction * piece, piece, 1)
    up_shard = lax.dynamic_slice_in_dim(own_expert, units + fraction * piece, piece, 1)
    down_shard = lax.dynamic_slice_in_dim(take(late_down, expert, 0), fraction * piece, piece, 0).T
    router_shard = jnp.pad((late_router.astype(F32) * gain_two).astype(BF), ((0, 0), (0, LANES - experts)))
    expert_shard = jnp.concatenate(
        [
            (gate_shard.astype(F32) * gain_two).astype(BF),
            (up_shard.astype(F32) * gain_two).astype(BF),
            down_shard,
            router_shard,
        ],
        axis=1,
    )
    expert_full = lax.all_gather(expert_shard, "fsdp", axis=0, tiled=True)
    router_full = expert_full[:, 3 * piece :]
    attn_shard = jnp.concatenate(
        [
            each
            for s in range(seqs)
            for each in (
                late_query[:, s * q_cols : (s + 1) * q_cols],
                late_keyval[:, s * kv_cols : (s + 1) * kv_cols],
            )
        ],
        axis=1,
    )
    attn_full = lax.all_gather(
        (attn_shard.astype(F32) * gain_one).astype(BF), "fsdp", axis=0, tiled=True
    )
    order = jnp.asarray(
        [2 * m for m in range(shards // 2)] + [2 * m + 1 for m in range(shards // 2)], jnp.int32
    )
    valid_all = jnp.stack(
        [
            each[local_rows : local_rows + valid_rows_kv].reshape(seqs, rows)
            for each in kv_blocks
        ],
        axis=1,
    ).astype(F32)
    valid_count = jnp.sum(valid_all)
    bias = jnp.where(valid_all > 0, 0.0, FLOOR_SCORE)
    earlier = ((order ^ shard) < shard) | (order == 0)
    bias_same = jnp.where(earlier[None, :, None], bias, FLOOR_SCORE)
    bias = jnp.concatenate([bias, bias_same]).reshape(2 * seqs, 1, shards * rows)
    attended_low, exact, lse = flash_forward(
        head_queries, kv_blocks, bias, seqs, rows, local_kv, groups
    )
    attended = lax.all_to_all(attended_low, "seq", split_axis=0, concat_axis=1, tiled=True)

    inputs = tokens.astype(F32)
    residual = inputs + dot(attended, out_full)
    factor_two = root(residual)
    normed_two = (residual * factor_two).astype(BF)
    logits = dot(normed_two, router_full)[:, :experts]
    expert_ids = jnp.arange(experts, dtype=jnp.int32)
    picked = (routes[:, :, None] == expert_ids).astype(F32)
    chosen = jnp.sum(picked * logits[:, None, :], axis=-1)
    gating = jax.nn.softmax(chosen, axis=-1)
    owners = ((jnp.arange(seqs, dtype=jnp.int32) + z) % seqs) // split
    to_owner = routes[:, :, None] == owners
    slot_hot = slots[:, :, None] == jnp.arange(CAP, dtype=jnp.int32)
    placed = (to_owner[:, :, :, None] & slot_hot[:, :, None, :]).astype(BF)
    placed = placed.reshape(rows, 2, seqs * CAP)
    dispatch = placed[:, 0] + placed[:, 1]
    placed_pairs = jnp.concatenate([placed[:, 0], placed[:, 1]], axis=0)
    sent_rows = dot_tn(dispatch, normed_two).astype(BF)
    kv_all = jnp.stack(after(kv_blocks, sent_rows))
    sent_rows = sent_rows.reshape(seqs, CAP, width)
    expert_rows, gate_up, hidden, *expert_out = experts_forward(
        send_out([sent_rows[s] for s in range(seqs)], seqs), expert_full, piece
    )
    returned = jnp.concatenate(after(send_back(expert_out, seqs), kv_all))
    selected = dot(placed_pairs, returned).reshape(2, rows, width)
    mixed_exact = residual + gating[:, :1] * selected[0] + gating[:, 1:] * selected[1]
    valid_rows = valid.astype(F32)
    errors = (mixed_exact - teacher.astype(F32)) * valid_rows[:, None]
    squares = jnp.sum(errors * errors)
    loss_scale = width * seq_len // 8
    grad_mixed = errors * (2.0 * loss_scale / (width * valid_count))

    grad_gating = jnp.stack(
        [jnp.sum(selected[0] * grad_mixed, axis=-1), jnp.sum(selected[1] * grad_mixed, axis=-1)],
        axis=1,
    )
    grad_chosen = gating * (grad_gating - jnp.sum(gating * grad_gating, axis=-1, keepdims=True))
    grad_logits = jnp.sum(grad_chosen[:, :, None] * picked, axis=1).astype(BF)
    grad_logits = jnp.pad(grad_logits, ((0, 0), (0, LANES - experts)))
    weighted = jnp.concatenate(
        [(gating[:, :1] * grad_mixed).astype(BF), (gating[:, 1:] * grad_mixed).astype(BF)], axis=0
    )
    sent_grads = dot_tn(placed_pairs, weighted).astype(BF).reshape(seqs, CAP, width)
    grad_out_rows = send_out([sent_grads[s] for s in range(seqs)], seqs)
    grad_out_rows = after(grad_out_rows, attn_full, grad_logits)
    grad_expert_out, grad_gate_up_rows, *grad_rows = experts_backward(
        grad_out_rows, gate_up, expert_full, piece
    )
    grad_returned = send_back(grad_rows, seqs)
    tokens_local = from_relative(
        [each[:rows] for each in after(token_blocks, grad_rows)], z
    ).reshape(local_rows, width)
    factor_local = root(tokens_local.astype(F32))
    ride_rows = jnp.concatenate([normed_two, jnp.ones((16, width), BF)], axis=0)
    product_rows = jnp.concatenate([tokens_local, ride_rows], axis=0)
    high, low = two_parts(squares)
    lane = jnp.arange(LANES, dtype=jnp.int32)[None, :]
    marks = jnp.where(lane == experts + 2 * (shard % 2), high, 0) + jnp.where(
        lane == experts + 1 + 2 * (shard % 2), low, 0
    )
    ride_columns = jnp.concatenate(
        [grad_logits, marks.astype(BF), jnp.zeros((15, LANES), BF)], axis=0
    )
    held_out, held_hidden = after((grad_expert_out, hidden), grad_rows)
    down_far, down_near = split_product(held_out, held_hidden, shard, shards)
    grad_down_sums = pair_sums(down_near, hop(down_far, shards, 1), shard)
    held_rows, held_gate_up = after((expert_rows, grad_gate_up_rows), grad_rows)
    gate_up_far, gate_up_near = split_product(held_rows, held_gate_up, shard, shards)
    grad_gate_up_sums = pair_sums(gate_up_near, hop(gate_up_far, shards, 1), shard)
    grad_down_blocks = send_chips(grad_down_sums, shards)
    grad_returned = jnp.concatenate(after(grad_returned, grad_down_sums, product_rows, ride_columns, factor_local))
    grad_normed_two = dot(dispatch, grad_returned) + dot_nt(grad_logits, router_full)
    grad_residual = grad_mixed + root_back(residual, factor_two, grad_normed_two)
    grad_branch = grad_residual.astype(BF)
    grad_attended = dot_nt(after(grad_branch, grad_gate_up_sums), out_full).astype(BF)
    head_grad = lax.all_to_all(grad_attended, "seq", split_axis=1, concat_axis=0, tiled=True)
    grad_gate_up_blocks = send_chips(grad_gate_up_sums, shards)
    grad_down_shard = total_of(after(grad_down_blocks, grad_attended)).astype(BF)
    grad_down = lax.all_gather(grad_down_shard, "seq", axis=0, tiled=False)

    out_far, out_near = split_product(
        after(grad_branch, grad_attended), attended, shard, shards
    )
    grad_q, near, far = [], [], []
    held = after(head_grad, grad_down_shard)
    for g in range(local_kv):
        part_q, near_kv, far_kv = flash_backward(
            head_queries, kv_all, bias, held, exact, lse, seqs, rows, g, groups
        )
        if g == 0:
            grad_gate_up_blocks = after(grad_gate_up_blocks, part_q)
            grad_gate_up_shard = total_of(grad_gate_up_blocks).astype(BF)
            steps = [(grad_gate_up_shard, grad_gate_up_shard)]
            steps.append(relay_step(steps[0], seqs))
            out_there = hop(after(out_far, head_grad), shards, 1)
        grad_q.append(part_q)
        near.append(near_kv)
        far.append(far_kv)
        held = after(head_grad, grad_gate_up_shard, out_there)
    steps[1] = after(steps[1], part_q)
    steps.append(relay_step(steps[1], seqs))
    far = after(far, steps[1], grad_down)
    pairs = kv_pair_sums(near, [hop(each, shards, 1) for each in far])
    out_sums = pair_sums(out_near, after(out_there, pairs), shard)
    sent_grads, product_columns = head_columns(
        grad_q, after(send_chips(pairs, shards), out_sums, steps[2]), factor_local, ride_columns
    )
    steps[2] = after(steps[2], product_columns)
    while len(steps) < seqs:
        steps.append(relay_step(steps[-1], seqs))
    token_grads = lax.all_to_all(sent_grads, "seq", split_axis=0, concat_axis=1, tiled=True)

    head_cols = q_cols + kv_cols
    head_far, head_near = split_product(product_rows, product_columns, shard, shards)
    head_sums = pair_sums(head_near, hop(head_far, shards, 1), shard)
    head_blocks = send_chips(head_sums, shards)
    head_part = total_of(after(head_blocks, steps[3]))
    grad_normed = dot_nt(after(token_grads, head_part), attn_full)
    grad_tokens = grad_residual + root_back(inputs, root(inputs), grad_normed)
    base_cols = head_cols + experts
    plane_high, plane_low = two_parts(
        jnp.sum(head_part[:1, base_cols : base_cols + 4], axis=1, keepdims=True)
    )
    lanes = lax.broadcasted_iota(jnp.int32, head_part.shape, 1)
    head_part = jnp.where(
        lanes == base_cols,
        plane_high.astype(F32),
        jnp.where(lanes == base_cols + 1, plane_low.astype(F32), head_part),
    )
    head_part = by_rows(head_part.astype(BF))
    head_last = [by_rows(each) for each in send_out([head_part] * seqs, seqs)]
    out_blocks = send_chips(after(out_sums, head_part), shards)
    out_part = total_of(out_blocks).astype(BF)
    out_parts = lax.all_to_all(
        out_part.reshape(part, seqs, q_cols), "seq", split_axis=1, concat_axis=1, tiled=True
    )
    out_own = by_rows(jnp.sum(out_parts.astype(F32), axis=1).astype(BF))
    grad_gate_up, grad_gain_ffn = place_gate_up(after(steps, head_part), w_gate_up, gain_two, z)
    out_own = after(out_own, grad_gate_up)
    out_last = [by_rows(each) for each in send_out([out_own] * seqs, seqs)]
    grad_query, grad_keyval, grad_out, grad_gain_attn, sums = place_heads(
        head_last, out_last, z, w_query, w_keyval, gain_one, q_cols, kv_cols
    )
    loss_value = jnp.sum(sums[0, experts : experts + 2]) / (width * valid_count)
    grad_router_base = sums[:, :experts]
    grad_down = (
        after(grad_down, head_part).reshape(experts, split, part, piece)
        .transpose(0, 1, 3, 2)
        .reshape(experts, units, part)
        .astype(F32)
    )
    grad_gain_ffn = grad_gain_ffn + jnp.sum(w_router.astype(F32) * grad_router_base, axis=1)
    return (
        mixed_exact.astype(BF),
        loss_value,
        grad_tokens,
        grad_gain_attn,
        grad_query,
        grad_keyval,
        grad_out.T,
        grad_gain_ffn,
        grad_router_base * gain_two,
        grad_gate_up,
        grad_down,
    )


def solution(mesh):
    return jax.shard_map(
        local,
        mesh=mesh,
        in_specs=(
            P(("seq", "fsdp"), None),
            P(("seq", "fsdp"), None),
            P(("seq", "fsdp")),
            P(("seq", "fsdp"), None),
            P(("seq", "fsdp"), None),
            P("fsdp"),
            P("fsdp", None),
            P("fsdp", None),
            P(None, "fsdp"),
            P("fsdp"),
            P("fsdp", None),
            P(None, "fsdp", None),
            P(None, None, "fsdp"),
        ),
        out_specs=(
            P(("seq", "fsdp"), None),
            P(),
            P(("seq", "fsdp"), None),
            P("fsdp"),
            P("fsdp", None),
            P("fsdp", None),
            P(None, "fsdp"),
            P("fsdp"),
            P("fsdp", None),
            P(None, "fsdp", None),
            P(None, None, "fsdp"),
        ),
        check_vma=False,
    )
```

```python
import functools
import math

import jax
import jax.numpy as jnp
from jax import lax
from jax.experimental import pallas as pl
from jax.experimental.layout import Layout, with_layout_constraint
from jax.experimental.pallas import tpu as pltpu
from jax.sharding import PartitionSpec as P

HEADS = 24
KVH = 8
HD = 64
CAP = 96
LANES = 128
EPSILON = 1e-06
FLOOR_SCORE = -1e30
BF = jnp.bfloat16
F32 = jnp.float32


def dot(a, b):
    return jnp.dot(a, b, preferred_element_type=F32)


def dot_nt(a, b):
    return lax.dot_general(a, b, (((1,), (1,)), ((), ())), preferred_element_type=F32)


def dot_tn(a, b):
    return lax.dot_general(a, b, (((0,), (0,)), ((), ())), preferred_element_type=F32)


def own_mask(valid_row, rows):
    i = lax.broadcasted_iota(jnp.int32, (rows, rows), 0)
    j = lax.broadcasted_iota(jnp.int32, (rows, rows), 1)
    return jnp.where(j == i, 0.0, jnp.where(j < i, valid_row, FLOOR_SCORE))


def key_chunk(kv_refs, zk, rows, g):
    return jnp.concatenate(
        [ref[pl.ds(zk * rows, rows), pl.ds(g * 2 * HD, 2 * HD)] for ref in kv_refs], axis=0
    )


def forward_kernel(shards, seqs, rows, local_kv, groups, *refs):
    kv_refs = refs[:shards]
    q_ref, bias_ref, low_ref, exact_ref, lse_ref, acc_ref, max_ref = refs[shards:]
    zq = pl.program_id(0)
    stack = groups * rows
    zeros = jnp.zeros((rows, HD), BF)
    half = lax.broadcasted_iota(jnp.int32, (1, 2 * HD), 1) < HD

    def queries(g):
        parts = []
        for h in range(groups):
            start = (g * groups + h) * HD
            parts.append(jnp.concatenate([q_ref[:, start : start + HD], zeros], axis=1))
        return jnp.concatenate(parts, axis=0)

    def chunk(g, zk, scores):
        first = scores is None
        keys = key_chunk(kv_refs, zk, rows, g)
        raw = dot_nt(queries(g), keys)
        if first:
            row = bias_ref[seqs + zk]
            mask = own_mask(row[:, :rows], rows)
            mask = jnp.concatenate([mask] * groups, axis=0)
            masked = jnp.concatenate([raw[:, :rows] + mask, raw[:, rows:] + row[:, rows:]], axis=1)
            new_max = jnp.max(masked, axis=1, keepdims=True)
        else:
            masked = raw + bias_ref[zk]
            new_max = jnp.maximum(max_ref[g][:, :1], jnp.max(masked, axis=1, keepdims=True))
        terms = jnp.exp(masked - new_max).astype(BF)
        ones_values = jnp.where(half, jnp.ones_like(keys), keys)
        part = dot(terms, ones_values)
        if first:
            acc_ref[g] = part
        else:
            acc_ref[g] = acc_ref[g] * jnp.exp(max_ref[g][:, :1] - new_max) + part
        max_ref[g] = jnp.broadcast_to(new_max, (stack, 2 * HD))

    for g in range(local_kv):
        chunk(g, zq, None)

    @pl.loop(0, zq)
    def _(zk):
        for g in range(local_kv):
            chunk(g, zk, True)

    exact_parts, lse_parts = [], []
    for g in range(local_kv):
        acc = acc_ref[g]
        total = acc[:, :HD]
        exact = acc[:, HD:] / total
        lse = max_ref[g][:, :HD] + jnp.log(total)
        for h in range(groups):
            exact_parts.append(exact[h * rows : (h + 1) * rows])
            lse_parts.append(lse[h * rows : (h + 1) * rows])
    exact = jnp.concatenate(exact_parts, axis=1)
    exact_ref[...] = exact
    low_ref[...] = exact.astype(BF)
    lse_ref[...] = jnp.concatenate(lse_parts, axis=1)


def flash_forward(q, kv_blocks, bias, seqs, rows, local_kv, groups):
    shards = len(kv_blocks)
    q_cols = q.shape[1]
    kv_spec = pl.BlockSpec(kv_blocks[0].shape, lambda i: (0, 0))
    q_spec = pl.BlockSpec((rows, q_cols), lambda i: (i, 0))
    stack = groups * rows
    out = jax.ShapeDtypeStruct((seqs * rows, q_cols), F32)
    return pl.pallas_call(
        functools.partial(forward_kernel, shards, seqs, rows, local_kv, groups),
        grid=(seqs,),
        in_specs=[kv_spec] * shards + [q_spec, pl.BlockSpec(bias.shape, lambda i: (0, 0, 0))],
        out_specs=[q_spec] * 3,
        out_shape=[jax.ShapeDtypeStruct((seqs * rows, q_cols), BF), out, out],
        scratch_shapes=[
            pltpu.VMEM((local_kv, stack, 2 * HD), F32),
            pltpu.VMEM((local_kv, stack, 2 * HD), F32),
        ],
        compiler_params=pltpu.CompilerParams(vmem_limit_bytes=24 * 1024 * 1024),
        cost_estimate=pl.CostEstimate(
            flops=0,
            bytes_accessed=0,
            transcendentals=0,
        ),
    )(*kv_blocks, q, bias)


def backward_kernel(shards, seqs, rows, g, groups, *refs):
    kv_refs = [refs[0].at[p] for p in range(shards)]
    (
        q_ref, bias_ref, grad_ref, exact_ref, lse_ref, grad_q_ref, near_ref, far_ref,
        pair_ref, pair_t_ref, lse_wide, delta_wide, acc_q, acc_kv,
    ) = refs[1:]
    zk = pl.program_id(0)
    stack = groups * rows
    zeros = jnp.zeros((rows, HD), BF)

    @pl.when(zk == 0)
    def _():
        acc_q[...] = jnp.zeros_like(acc_q)

        @pl.loop(0, seqs)
        def _(zq):
            here = pl.ds(zq * rows, rows)
            tops, bottoms = [], []
            for h in range(groups):
                cols = slice((g * groups + h) * HD, (g * groups + h + 1) * HD)
                grad = grad_ref[here, cols]
                tops.append(jnp.concatenate([q_ref[here, cols], zeros], axis=1))
                bottoms.append(jnp.concatenate([zeros, grad], axis=1))
                delta = jnp.sum(grad.astype(F32) * exact_ref[here, cols], axis=1, keepdims=True)
                part = slice(h * rows, (h + 1) * rows)
                delta_wide[zq, part] = jnp.broadcast_to(delta, (rows, 2 * HD))
                lse_wide[zq, part] = jnp.broadcast_to(lse_ref[here, cols][:, :1], (rows, 2 * HD))
            pair = jnp.concatenate(tops + bottoms, axis=0)
            pair_ref[zq] = pair
            pair_t_ref[zq] = pair.astype(F32).T.astype(BF)

    def chunk(zq, first):
        keys = key_chunk(kv_refs, zk, rows, g)
        both = dot_nt(pair_ref[zq], keys)
        raw, products = both[:stack], both[stack:]
        if first:
            row = bias_ref[seqs + zk]
            mask = own_mask(row[:, :rows], rows)
            mask = jnp.concatenate([mask] * groups, axis=0)
            masked = jnp.concatenate([raw[:, :rows] + mask, raw[:, rows:] + row[:, rows:]], axis=1)
        else:
            masked = raw + bias_ref[zk]
        weights = jnp.exp(masked - lse_wide[zq][:, :1])
        grads = (weights * (products - delta_wide[zq][:, :1])).astype(BF)
        acc_q[zq] += dot(grads, keys)
        part = dot(pair_t_ref[zq], jnp.concatenate([grads, weights.astype(BF)], axis=0))
        if first:
            acc_kv[...] = part
        else:
            acc_kv[...] += part

    chunk(zk, True)

    @pl.loop(zk + 1, seqs)
    def _(zq):
        chunk(zq, False)

    for p in range(shards):
        target = near_ref if p < shards // 2 else far_ref
        target[p % (shards // 2)] = acc_kv[:, p * rows : (p + 1) * rows].T.astype(BF)

    @pl.when(zk == seqs - 1)
    def _():
        @pl.loop(0, seqs)
        def _(zq):
            total = acc_q[zq]
            parts = [total[h * rows : (h + 1) * rows, :HD] for h in range(groups)]
            grad_q_ref[pl.ds(zq * rows, rows), :] = jnp.concatenate(parts, axis=1) * HD ** (-0.5)


def flash_backward(q, kv_all, bias, grad, exact, lse, seqs, rows, g, groups):
    shards = kv_all.shape[0]
    q_cols = q.shape[1]
    stack = groups * rows
    kv_spec = pl.BlockSpec(kv_all.shape, lambda i: (0, 0, 0))
    whole = pl.BlockSpec((seqs * rows, q_cols), lambda i: (0, 0))
    grad_q_shape = (seqs * rows, groups * HD)
    out_spec = pl.BlockSpec((shards // 2, rows, 2 * HD), lambda i: (0, i, 0))
    out = jax.ShapeDtypeStruct((shards // 2, seqs * rows, 2 * HD), BF)
    return pl.pallas_call(
        functools.partial(backward_kernel, shards, seqs, rows, g, groups),
        grid=(seqs,),
        in_specs=[kv_spec]
        + [whole, pl.BlockSpec(bias.shape, lambda i: (0, 0, 0)), whole, whole, whole],
        out_specs=[pl.BlockSpec(grad_q_shape, lambda i: (0, 0)), out_spec, out_spec],
        out_shape=[jax.ShapeDtypeStruct(grad_q_shape, F32), out, out],
        scratch_shapes=[
            pltpu.VMEM((seqs, 2 * stack, 2 * HD), BF),
            pltpu.VMEM((seqs, 2 * HD, 2 * stack), BF),
            pltpu.VMEM((seqs, stack, 2 * HD), F32),
            pltpu.VMEM((seqs, stack, 2 * HD), F32),
            pltpu.VMEM((seqs, stack, 2 * HD), F32),
            pltpu.VMEM((2 * HD, shards * rows), F32),
        ],
        compiler_params=pltpu.CompilerParams(vmem_limit_bytes=28 * 1024 * 1024),
        cost_estimate=pl.CostEstimate(
            flops=0 if g else 10**12,
            bytes_accessed=0,
            transcendentals=0,
        ),
    )(kv_all, q, bias, grad, exact, lse)


def shift(block, count, step):
    return lax.ppermute(block, "seq", [(i, (i + step) % count) for i in range(count)])


def send_out(blocks, count):
    return [blocks[0]] + [shift(blocks[s], count, s) for s in range(1, count)]


def send_back(blocks, count):
    return [blocks[0]] + [shift(blocks[s], count, count - s) for s in range(1, count)]


def relay_step(blocks, count):
    up, down = blocks
    return (
        lax.ppermute(up, "seq", [(i, i + 1) for i in range(count - 1)]),
        lax.ppermute(down, "seq", [(i + 1, i) for i in range(count - 1)]),
    )


def from_relative(blocks, place):
    count = len(blocks)
    rising = jnp.stack([blocks[-s % count] for s in range(count)])
    return lax.dynamic_slice_in_dim(jnp.concatenate([rising, rising]), count - place, count, 0)


def hop(block, count, mask):
    return lax.ppermute(block, "fsdp", [(i, i ^ mask) for i in range(count)])


def gather_shards(block, count):
    near = [block] + [hop(block, count, 2 * m) for m in range(1, count // 2)]
    return near + [hop(each, count, 1) for each in near]


def send_chips(parts, count):
    return [parts[0]] + [hop(parts[m], count, 2 * m) for m in range(1, count // 2)]


def total_of(blocks):
    total = blocks[0].astype(F32)
    for each in blocks[1:]:
        total = total + each.astype(F32)
    return total


def take(array, index, axis):
    return lax.dynamic_index_in_dim(array, index, axis, keepdims=False)


def product_kernel(core_ref, lhs_ref, rhs_ref, far_ref, near_ref):
    part = lhs_ref.shape[1] // 2
    rhs = rhs_ref[...]
    first = dot_tn(lhs_ref[:, :part], rhs).astype(BF)
    second = dot_tn(lhs_ref[:, part:], rhs).astype(BF)
    core = core_ref[0]

    @pl.when(core == 0)
    def _():
        near_ref[0] = first
        far_ref[0] = second

    @pl.when(core != 0)
    def _():
        near_ref[0] = second
        far_ref[0] = first


def split_product(lhs, rhs, shard, count):
    tokens, width = lhs.shape
    cols = rhs.shape[1]
    part = width // count
    if 2 * part % LANES:
        cut = dot_tn(lhs, rhs).astype(BF).reshape(count // 2, 2, part, cols)
        return take(cut, 1 - shard % 2, 1), take(cut, shard % 2, 1)
    out = jax.ShapeDtypeStruct((count // 2, part, cols), BF)
    out_spec = pl.BlockSpec((1, part, cols), lambda i: (i, 0, 0))
    return pl.pallas_call(
        product_kernel,
        grid=(count // 2,),
        in_specs=[
            pl.BlockSpec(memory_space=pltpu.SMEM),
            pl.BlockSpec((tokens, 2 * part), lambda i: (0, i)),
            pl.BlockSpec((tokens, cols), lambda i: (0, 0)),
        ],
        out_specs=[out_spec, out_spec],
        out_shape=[out, out],
        compiler_params=pltpu.CompilerParams(vmem_limit_bytes=24 * 1024 * 1024),
        cost_estimate=pl.CostEstimate(flops=0, bytes_accessed=0, transcendentals=0),
    )((shard % 2).astype(jnp.int32).reshape(1), lhs, rhs)


def pair_kernel(chip_ref, near_ref, there_ref, own_ref, *part_refs):
    chip = chip_ref[0]
    own_ref[...] = near_ref[chip].astype(F32) + there_ref[chip].astype(F32)
    for m, part_ref in enumerate(part_refs):
        which = chip ^ (m + 1)
        part_ref[...] = (near_ref[which].astype(F32) + there_ref[which].astype(F32)).astype(BF)


def pair_sums(near, there, shard):
    chips, part, cols = near.shape
    tile = math.gcd(cols, 512)
    if tile % LANES:
        tile = cols
    block = pl.BlockSpec((chips, part, tile), lambda i: (0, 0, i))
    out_spec = pl.BlockSpec((part, tile), lambda i: (0, i))
    out = jax.ShapeDtypeStruct((part, cols), BF)
    return pl.pallas_call(
        pair_kernel,
        grid=(cols // tile,),
        in_specs=[pl.BlockSpec(memory_space=pltpu.SMEM), block, block],
        out_specs=[out_spec] * chips,
        out_shape=[jax.ShapeDtypeStruct((part, cols), F32)] + [out] * (chips - 1),
        compiler_params=pltpu.CompilerParams(vmem_limit_bytes=24 * 1024 * 1024),
        cost_estimate=pl.CostEstimate(flops=0, bytes_accessed=0, transcendentals=0),
    )((shard // 2).astype(jnp.int32).reshape(1), near, there)


def fetch_weights(weights_ref, held, sems, piece):
    copies = [
        pltpu.make_async_copy(
            weights_ref.at[:, pl.ds(part * piece, piece)], held.at[part], sems.at[part]
        )
        for part in range(3)
    ]
    return copies


def experts_forward_kernel(count, *refs):
    rows_in, weights_ref = refs[:count], refs[count]
    rows_ref, gate_up_ref, hidden_ref = refs[count + 1 : count + 4]
    out_refs, (held, sems) = refs[count + 4 : -2], refs[-2:]
    piece = hidden_ref.shape[1]
    cap = rows_in[0].shape[0]
    copies = fetch_weights(weights_ref, held, sems, piece)
    for copy in copies:
        copy.start()
    for s in range(count):
        rows_ref[s * cap : (s + 1) * cap, :] = rows_in[s][...]
    rows = rows_ref[...]
    copies[0].wait()
    gate = dot(rows, held[0])
    gate_up_ref[:, :piece] = gate
    copies[1].wait()
    up = dot(rows, held[1])
    gate_up_ref[:, piece:] = up
    hidden = (gate / (1.0 + jnp.exp(-gate)) * up).astype(BF)
    hidden_ref[...] = hidden
    copies[2].wait()
    out = dot_nt(hidden, held[2]).astype(BF)
    for s in range(count):
        out_refs[s][...] = out[s * cap : (s + 1) * cap, :]


def experts_forward(blocks, weights, piece):
    count = len(blocks)
    cap, width = blocks[0].shape
    rows = count * cap
    in_vmem = pl.BlockSpec(memory_space=pltpu.VMEM)
    return pl.pallas_call(
        functools.partial(experts_forward_kernel, count),
        in_specs=[in_vmem] * count + [pl.BlockSpec(memory_space=pltpu.HBM)],
        out_specs=[in_vmem] * (3 + count),
        out_shape=[
            jax.ShapeDtypeStruct((rows, width), BF),
            jax.ShapeDtypeStruct((rows, 2 * piece), F32),
            jax.ShapeDtypeStruct((rows, piece), BF),
        ]
        + [jax.ShapeDtypeStruct((cap, width), BF)] * count,
        scratch_shapes=[pltpu.VMEM((3, width, piece), BF), pltpu.SemaphoreType.DMA((3,))],
        compiler_params=pltpu.CompilerParams(vmem_limit_bytes=56 * 1024 * 1024),
        cost_estimate=pl.CostEstimate(flops=0, bytes_accessed=0, transcendentals=0),
    )(*blocks, weights)


def experts_backward_kernel(count, *refs):
    grads_in, gate_up_ref, weights_ref = refs[:count], refs[count], refs[count + 1]
    grads_ref, rows_ref = refs[count + 2 : count + 4]
    out_refs, (held, sems) = refs[count + 4 : -2], refs[-2:]
    piece = rows_ref.shape[1] // 2
    cap = grads_in[0].shape[0]
    copies = fetch_weights(weights_ref, held, sems, piece)
    for copy in (copies[2], copies[0], copies[1]):
        copy.start()
    for s in range(count):
        grads_ref[s * cap : (s + 1) * cap, :] = grads_in[s][...]
    copies[2].wait()
    grad_hidden = dot(grads_ref[...], held[2])
    gate = gate_up_ref[:, :piece]
    up = gate_up_ref[:, piece:]
    slope = 1.0 / (1.0 + jnp.exp(-gate))
    grad_gate = (grad_hidden * up * slope * (1.0 + gate * (1.0 - slope))).astype(BF)
    grad_up = (grad_hidden * gate * slope).astype(BF)
    rows_ref[:, :piece] = grad_gate
    rows_ref[:, piece:] = grad_up
    copies[0].wait()
    total = dot_nt(grad_gate, held[0])
    copies[1].wait()
    total = (total + dot_nt(grad_up, held[1])).astype(BF)
    for s in range(count):
        out_refs[s][...] = total[s * cap : (s + 1) * cap, :]


def experts_backward(blocks, gate_up, weights, piece):
    count = len(blocks)
    cap, width = blocks[0].shape
    rows = count * cap
    in_vmem = pl.BlockSpec(memory_space=pltpu.VMEM)
    return pl.pallas_call(
        functools.partial(experts_backward_kernel, count),
        in_specs=[in_vmem] * (count + 1) + [pl.BlockSpec(memory_space=pltpu.HBM)],
        out_specs=[in_vmem] * (2 + count),
        out_shape=[
            jax.ShapeDtypeStruct((rows, width), BF),
            jax.ShapeDtypeStruct((rows, 2 * piece), BF),
        ]
        + [jax.ShapeDtypeStruct((cap, width), BF)] * count,
        scratch_shapes=[pltpu.VMEM((3, width, piece), BF), pltpu.SemaphoreType.DMA((3,))],
        compiler_params=pltpu.CompilerParams(vmem_limit_bytes=56 * 1024 * 1024),
        cost_estimate=pl.CostEstimate(flops=0, bytes_accessed=0, transcendentals=0),
    )(*blocks, gate_up, weights)


def kv_pair_kernel(heads, chips, *refs):
    near, there, outs = refs[:heads], refs[heads : 2 * heads], refs[2 * heads :]
    for m in range(chips):
        for g in range(heads):
            total = near[g][m].astype(F32) + there[g][m].astype(F32)
            outs[m][:, g * 2 * HD : (g + 1) * 2 * HD] = total.astype(outs[m].dtype)


def kv_pair_sums(near, there):
    heads, (chips, rows, cols) = len(near), near[0].shape
    in_vmem = pl.BlockSpec(memory_space=pltpu.VMEM)
    out = jax.ShapeDtypeStruct((rows, heads * cols), BF)
    return pl.pallas_call(
        functools.partial(kv_pair_kernel, heads, chips),
        in_specs=[in_vmem] * (2 * heads),
        out_specs=[in_vmem] * chips,
        out_shape=[jax.ShapeDtypeStruct((rows, heads * cols), F32)] + [out] * (chips - 1),
        compiler_params=pltpu.CompilerParams(vmem_limit_bytes=20 * 1024 * 1024),
        cost_estimate=pl.CostEstimate(flops=0, bytes_accessed=0, transcendentals=0),
    )(*near, *there)


def head_columns_kernel(heads, chips, *refs):
    queries, sums = refs[:heads], refs[heads : heads + chips]
    factor_ref, ride_ref, sent_ref, columns_ref = refs[heads + chips :]
    query = jnp.concatenate([each[...] for each in queries], axis=1)
    keyval = sums[0][...]
    for each in sums[1:]:
        keyval = keyval + each[...].astype(F32)
    both = jnp.concatenate([query, keyval], axis=1)
    rows, cols = both.shape
    sent_ref[...] = both.astype(BF)
    columns_ref[:rows, :cols] = (both * factor_ref[...]).astype(BF)
    columns_ref[:rows, cols:] = jnp.zeros((rows, LANES), BF)
    columns_ref[rows:, :cols] = jnp.zeros((ride_ref.shape[0], cols), BF)
    columns_ref[rows:, cols:] = ride_ref[...]


def head_columns(queries, sums, factor, ride):
    rows = sums[0].shape[0]
    cols = sum(each.shape[1] for each in queries) + sums[0].shape[1]
    if cols % LANES:
        both = jnp.concatenate(list(queries) + [total_of(sums)], axis=1)
        scaled = jnp.pad((both * factor).astype(BF), ((0, 0), (0, LANES)))
        return both.astype(BF), jnp.concatenate([scaled, jnp.pad(ride, ((0, 0), (cols, 0)))])
    in_vmem = pl.BlockSpec(memory_space=pltpu.VMEM)
    return pl.pallas_call(
        functools.partial(head_columns_kernel, len(queries), len(sums)),
        in_specs=[in_vmem] * (len(queries) + len(sums) + 2),
        out_specs=[in_vmem] * 2,
        out_shape=[
            jax.ShapeDtypeStruct((rows, cols), BF),
            jax.ShapeDtypeStruct((rows + ride.shape[0], cols + LANES), BF),
        ],
        compiler_params=pltpu.CompilerParams(vmem_limit_bytes=20 * 1024 * 1024),
        cost_estimate=pl.CostEstimate(flops=0, bytes_accessed=0, transcendentals=0),
    )(*queries, *sums, factor, ride)


def two_parts(value):
    high = value.astype(BF)
    return high, (value - high.astype(F32)).astype(BF)


def mark_kernel(seed_ref, out_ref):
    out_ref[...] = seed_ref[...]


def mark(*others):
    seed = after(jnp.zeros((8, LANES), F32), *others)
    return pl.pallas_call(
        mark_kernel,
        out_shape=jax.ShapeDtypeStruct((8, LANES), F32),
        cost_estimate=pl.CostEstimate(flops=10**12, bytes_accessed=8192, transcendentals=0),
    )(seed)


def by_rows(array):
    return with_layout_constraint(array, Layout(major_to_minor=tuple(range(array.ndim))))


def after(values, *others):
    return lax.optimization_barrier((values, others))[0]


def root(values):
    return lax.rsqrt(jnp.mean(values * values, axis=-1, keepdims=True) + EPSILON)


def root_back(values, factor, grad_scaled):
    inner = jnp.mean(grad_scaled * values, axis=-1, keepdims=True)
    return factor * grad_scaled - values * (factor * factor * factor * inner)


def place_gate_up_kernel(count, place_ref, *refs):
    blocks = refs[: 2 * count - 1]
    weight_ref, gain_ref, out_ref, sums_ref, base = refs[2 * count - 1 :]
    offset = place_ref[0] - pl.program_id(1)

    for s in range(2 * count - 1):

        @pl.when(offset == (s if s < count else count - 1 - s))
        def _(s=s):
            base[...] = blocks[s][...].astype(F32)

    @pl.when((pl.program_id(0) == 0) & (pl.program_id(1) == 0))
    def _():
        sums_ref[...] = jnp.zeros_like(sums_ref)

    values = base[...]
    out_ref[0] = values * gain_ref[...]
    product = jnp.sum(weight_ref[0].astype(F32) * values, axis=1, keepdims=True)
    sums_ref[...] += jnp.broadcast_to(product, sums_ref.shape)


def place_gate_up(steps, weight, gain, place):
    experts, part, both = weight.shape
    count = len(steps)
    split = count // experts
    if split == 1:
        tile = math.gcd(both, 1024)
        blocks = [steps[0][0]] + [each[0] for each in steps[1:]] + [each[1] for each in steps[1:]]
        block = pl.BlockSpec((part, tile), lambda t, e: (0, t))
        out, sums = pl.pallas_call(
            functools.partial(place_gate_up_kernel, count),
            grid=(both // tile, experts),
            in_specs=[pl.BlockSpec(memory_space=pltpu.SMEM)]
            + [block] * len(blocks)
            + [
                pl.BlockSpec((1, part, tile), lambda t, e: (e, 0, t)),
                pl.BlockSpec((part, 1), lambda t, e: (0, 0)),
            ],
            out_specs=[
                pl.BlockSpec((1, part, tile), lambda t, e: (e, 0, t)),
                pl.BlockSpec((part, LANES), lambda t, e: (0, 0)),
            ],
            out_shape=[
                jax.ShapeDtypeStruct(weight.shape, F32),
                jax.ShapeDtypeStruct((part, LANES), F32),
            ],
            scratch_shapes=[pltpu.VMEM((part, tile), F32)],
            compiler_params=pltpu.CompilerParams(vmem_limit_bytes=28 * 1024 * 1024),
            cost_estimate=pl.CostEstimate(flops=0, bytes_accessed=0, transcendentals=0),
        )(place.astype(jnp.int32).reshape(1), *blocks, weight, gain)
        return out, sums[:, 0]
    blocks = [steps[0][0]] + [
        jnp.where(place >= s, steps[s][0], steps[count - s][1]) for s in range(1, count)
    ]
    base = (
        from_relative(blocks, place)
        .reshape(experts, split, part, 2, both // (2 * split))
        .transpose(0, 2, 3, 1, 4)
        .reshape(experts, part, both)
        .astype(F32)
    )
    return base * gain, jnp.sum(weight.astype(F32) * base, axis=(0, 2))


def place_kernel(count, q_cols, kv_cols, place_ref, *refs):
    blocks = refs[:count]
    w_query_ref, w_keyval_ref, gain_ref, query_ref, keyval_ref, out_ref, base_ref, sums_ref = refs[
        count:
    ]
    gain = gain_ref[...]
    base = jnp.zeros_like(gain)
    sums = jnp.zeros(sums_ref.shape, F32)
    for s in range(count):
        owner = lax.rem(place_ref[0] + (count - s), count)
        q_at = pl.ds(pl.multiple_of(owner * q_cols, LANES), q_cols)
        kv_at = pl.ds(pl.multiple_of(owner * kv_cols, LANES), kv_cols)
        query = blocks[s][:, :q_cols].astype(F32)
        keyval = blocks[s][:, q_cols : q_cols + kv_cols].astype(F32)
        start = q_cols + kv_cols
        sums = sums + blocks[s][:, start : start + LANES].astype(F32)
        out_ref[:, q_at] = blocks[s][:, start + LANES :].astype(F32)
        base = base + jnp.sum(w_query_ref[:, q_at].astype(F32) * query, axis=1, keepdims=True)
        base = base + jnp.sum(w_keyval_ref[:, kv_at].astype(F32) * keyval, axis=1, keepdims=True)
        query_ref[:, q_at] = query * gain
        keyval_ref[:, kv_at] = keyval * gain
    base_ref[...] = jnp.broadcast_to(base, base_ref.shape)
    sums_ref[...] = sums


def place_heads(blocks, place, w_query, w_keyval, gain, q_cols, kv_cols):
    count = len(blocks)
    part = w_query.shape[0]
    start = q_cols + kv_cols
    if q_cols % LANES == 0 and kv_cols % LANES == 0:
        wide = jax.ShapeDtypeStruct((part, count * q_cols), F32)
        narrow = jax.ShapeDtypeStruct((part, count * kv_cols), F32)
        lanes = jax.ShapeDtypeStruct((part, LANES), F32)
        in_vmem = pl.BlockSpec(memory_space=pltpu.VMEM)
        query, keyval, out, base, sums = pl.pallas_call(
            functools.partial(place_kernel, count, q_cols, kv_cols),
            in_specs=[pl.BlockSpec(memory_space=pltpu.SMEM)] + [in_vmem] * (count + 3),
            out_specs=[in_vmem] * 5,
            out_shape=[wide, narrow, wide, lanes, lanes],
            compiler_params=pltpu.CompilerParams(vmem_limit_bytes=24 * 1024 * 1024),
            cost_estimate=pl.CostEstimate(flops=0, bytes_accessed=0, transcendentals=0),
        )(place.astype(jnp.int32).reshape(1), *blocks, w_query, w_keyval, gain)
        return query, keyval, out, base[:, 0], sums
    blocks = from_relative(blocks, place).astype(F32)

    def columns(begin, end):
        return blocks[:, :, begin:end].transpose(1, 0, 2).reshape(part, count * (end - begin))

    query, keyval = columns(0, q_cols), columns(q_cols, start)
    base = jnp.sum(w_query.astype(F32) * query, axis=1) + jnp.sum(
        w_keyval.astype(F32) * keyval, axis=1
    )
    sums = jnp.sum(blocks[:, :, start : start + LANES], axis=0)
    out = columns(start + LANES, start + LANES + q_cols)
    return query * gain, keyval * gain, out, base, sums


def local(
    tokens,
    teacher,
    valid,
    routes,
    slots,
    gain_attn,
    w_query,
    w_keyval,
    w_out,
    gain_ffn,
    w_router,
    w_gate_up,
    w_down,
):
    seqs = lax.axis_size("seq")
    shards = lax.axis_size("fsdp")
    z = lax.axis_index("seq")
    shard = lax.axis_index("fsdp")
    rows, width = tokens.shape
    groups = HEADS // KVH
    local_kv = KVH // seqs
    q_cols = local_kv * groups * HD
    kv_cols = local_kv * 2 * HD
    local_rows = rows * seqs
    seq_len = local_rows * shards
    experts, part, both = w_gate_up.shape
    units = both // 2
    split = seqs // experts
    piece = units // split
    expert = z // split
    fraction = z % split
    scale = HD ** (-0.5)

    gain_one = gain_attn.astype(F32)[:, None]
    gain_two = gain_ffn.astype(F32)[:, None]
    heads_shard = jnp.concatenate(
        [
            lax.dynamic_slice_in_dim(w_query, z * q_cols, q_cols, 1),
            lax.dynamic_slice_in_dim(w_keyval, z * kv_cols, kv_cols, 1),
        ],
        axis=1,
    )
    heads_shard = (heads_shard.astype(F32) * gain_one).astype(BF)
    heads_full = lax.all_gather(heads_shard, "fsdp", axis=0, tiled=True)
    valid_row = jnp.pad(valid.astype(BF).reshape(1, rows), ((0, 7), (0, width - rows)))
    token_rows = jnp.concatenate([tokens, valid_row], axis=0)
    token_mark = mark(token_rows)
    token_blocks = after(send_out([token_rows] * seqs, seqs), token_mark)

    valid_local = from_relative([each[rows : rows + 1, :rows] for each in token_blocks], z)
    projected = []
    for block in token_blocks:
        projected.append(dot(block[:rows], heads_full) * root(block[:rows].astype(F32)))
    projected = from_relative([each.astype(BF) for each in projected], z)
    projected = projected.reshape(local_rows, q_cols + kv_cols)
    head_queries = projected[:, :q_cols] * jnp.asarray(scale, BF)

    valid_rows_kv = local_rows // kv_cols
    payload = jnp.concatenate(
        [
            projected[:, q_cols:],
            valid_local.reshape(valid_rows_kv, kv_cols),
            jnp.zeros((16 - valid_rows_kv, kv_cols), BF),
        ],
        axis=0,
    )
    kv_blocks = gather_shards(payload, shards)
    late_query, late_keyval, late_router, late_gate_up, late_down = after(
        (w_query, w_keyval, w_router, w_gate_up, w_down), token_mark
    )
    out_full = lax.all_gather(w_out, "fsdp", axis=1, tiled=True)
    own_expert = take(late_gate_up, expert, 0)
    gate_shard = lax.dynamic_slice_in_dim(own_expert, fraction * piece, piece, 1)
    up_shard = lax.dynamic_slice_in_dim(own_expert, units + fraction * piece, piece, 1)
    down_shard = lax.dynamic_slice_in_dim(take(late_down, expert, 0), fraction * piece, piece, 0).T
    router_shard = jnp.pad((late_router.astype(F32) * gain_two).astype(BF), ((0, 0), (0, LANES - experts)))
    expert_shard = jnp.concatenate(
        [
            (gate_shard.astype(F32) * gain_two).astype(BF),
            (up_shard.astype(F32) * gain_two).astype(BF),
            down_shard,
            router_shard,
        ],
        axis=1,
    )
    expert_full = lax.all_gather(expert_shard, "fsdp", axis=0, tiled=True)
    router_full = expert_full[:, 3 * piece :]
    attn_shard = jnp.concatenate(
        [
            each
            for s in range(seqs)
            for each in (
                late_query[:, s * q_cols : (s + 1) * q_cols],
                late_keyval[:, s * kv_cols : (s + 1) * kv_cols],
            )
        ],
        axis=1,
    )
    attn_full = lax.all_gather(
        (attn_shard.astype(F32) * gain_one).astype(BF), "fsdp", axis=0, tiled=True
    )
    order = jnp.asarray(
        [2 * m for m in range(shards // 2)] + [2 * m + 1 for m in range(shards // 2)], jnp.int32
    )
    valid_all = jnp.stack(
        [
            each[local_rows : local_rows + valid_rows_kv].reshape(seqs, rows)
            for each in kv_blocks
        ],
        axis=1,
    ).astype(F32)
    valid_count = jnp.sum(valid_all)
    bias = jnp.where(valid_all > 0, 0.0, FLOOR_SCORE)
    earlier = ((order ^ shard) < shard) | (order == 0)
    bias_same = jnp.where(earlier[None, :, None], bias, FLOOR_SCORE)
    bias = jnp.concatenate([bias, bias_same]).reshape(2 * seqs, 1, shards * rows)
    attended_low, exact, lse = flash_forward(
        head_queries, kv_blocks, bias, seqs, rows, local_kv, groups
    )
    attended = lax.all_to_all(attended_low, "seq", split_axis=0, concat_axis=1, tiled=True)

    inputs = tokens.astype(F32)
    residual = inputs + dot(attended, out_full)
    factor_two = root(residual)
    normed_two = (residual * factor_two).astype(BF)
    logits = dot(normed_two, router_full)[:, :experts]
    expert_ids = jnp.arange(experts, dtype=jnp.int32)
    picked = (routes[:, :, None] == expert_ids).astype(F32)
    chosen = jnp.sum(picked * logits[:, None, :], axis=-1)
    gating = jax.nn.softmax(chosen, axis=-1)
    owners = ((jnp.arange(seqs, dtype=jnp.int32) + z) % seqs) // split
    to_owner = routes[:, :, None] == owners
    slot_hot = slots[:, :, None] == jnp.arange(CAP, dtype=jnp.int32)
    placed = (to_owner[:, :, :, None] & slot_hot[:, :, None, :]).astype(BF)
    placed = placed.reshape(rows, 2, seqs * CAP)
    dispatch = placed[:, 0] + placed[:, 1]
    placed_pairs = jnp.concatenate([placed[:, 0], placed[:, 1]], axis=0)
    sent_rows = dot_tn(dispatch, normed_two).astype(BF)
    kv_all = jnp.stack(after(kv_blocks, sent_rows))
    sent_rows = sent_rows.reshape(seqs, CAP, width)
    expert_rows, gate_up, hidden, *expert_out = experts_forward(
        send_out([sent_rows[s] for s in range(seqs)], seqs), expert_full, piece
    )
    returned = jnp.concatenate(after(send_back(expert_out, seqs), kv_all))
    selected = dot(placed_pairs, returned).reshape(2, rows, width)
    mixed_exact = residual + gating[:, :1] * selected[0] + gating[:, 1:] * selected[1]
    valid_rows = valid.astype(F32)
    errors = (mixed_exact - teacher.astype(F32)) * valid_rows[:, None]
    squares = jnp.sum(errors * errors)
    loss_scale = width * seq_len // 8
    grad_mixed = errors * (2.0 * loss_scale / (width * valid_count))

    grad_gating = jnp.stack(
        [jnp.sum(selected[0] * grad_mixed, axis=-1), jnp.sum(selected[1] * grad_mixed, axis=-1)],
        axis=1,
    )
    grad_chosen = gating * (grad_gating - jnp.sum(gating * grad_gating, axis=-1, keepdims=True))
    grad_logits = jnp.sum(grad_chosen[:, :, None] * picked, axis=1).astype(BF)
    grad_logits = jnp.pad(grad_logits, ((0, 0), (0, LANES - experts)))
    weighted = jnp.concatenate(
        [(gating[:, :1] * grad_mixed).astype(BF), (gating[:, 1:] * grad_mixed).astype(BF)], axis=0
    )
    sent_grads = dot_tn(placed_pairs, weighted).astype(BF).reshape(seqs, CAP, width)
    grad_out_rows = send_out([sent_grads[s] for s in range(seqs)], seqs)
    grad_out_rows = after(grad_out_rows, attn_full, grad_logits)
    grad_expert_out, grad_gate_up_rows, *grad_rows = experts_backward(
        grad_out_rows, gate_up, expert_full, piece
    )
    grad_returned = send_back(grad_rows, seqs)
    tokens_local = from_relative(
        [each[:rows] for each in after(token_blocks, grad_rows)], z
    ).reshape(local_rows, width)
    factor_local = root(tokens_local.astype(F32))
    ride_rows = jnp.concatenate([normed_two, jnp.ones((16, width), BF)], axis=0)
    product_rows = jnp.concatenate([tokens_local, ride_rows], axis=0)
    high, low = two_parts(squares)
    lane = jnp.arange(LANES, dtype=jnp.int32)[None, :]
    marks = jnp.where(lane == experts + 2 * (shard % 2), high, 0) + jnp.where(
        lane == experts + 1 + 2 * (shard % 2), low, 0
    )
    ride_columns = jnp.concatenate(
        [grad_logits, marks.astype(BF), jnp.zeros((15, LANES), BF)], axis=0
    )
    held_out, held_hidden = after((grad_expert_out, hidden), grad_rows)
    down_far, down_near = split_product(held_out, held_hidden, shard, shards)
    grad_down_sums = pair_sums(down_near, hop(down_far, shards, 1), shard)
    held_rows, held_gate_up = after((expert_rows, grad_gate_up_rows), grad_rows)
    gate_up_far, gate_up_near = split_product(held_rows, held_gate_up, shard, shards)
    grad_gate_up_sums = pair_sums(gate_up_near, hop(gate_up_far, shards, 1), shard)
    grad_down_blocks = send_chips(grad_down_sums, shards)
    grad_returned = jnp.concatenate(after(grad_returned, grad_down_sums, product_rows, ride_columns, factor_local))
    grad_normed_two = dot(dispatch, grad_returned) + dot_nt(grad_logits, router_full)
    grad_residual = grad_mixed + root_back(residual, factor_two, grad_normed_two)
    grad_branch = grad_residual.astype(BF)
    grad_attended = dot_nt(after(grad_branch, grad_gate_up_sums), out_full).astype(BF)
    head_grad = lax.all_to_all(grad_attended, "seq", split_axis=1, concat_axis=0, tiled=True)
    grad_gate_up_blocks = send_chips(grad_gate_up_sums, shards)
    grad_down_shard = total_of(after(grad_down_blocks, grad_attended)).astype(BF)
    grad_down = lax.all_gather(grad_down_shard, "seq", axis=0, tiled=False)

    out_far, out_near = split_product(
        after(grad_branch, grad_attended), attended, shard, shards
    )
    grad_q, near, far = [], [], []
    held = after(head_grad, grad_down_shard)
    for g in range(local_kv):
        part_q, near_kv, far_kv = flash_backward(
            head_queries, kv_all, bias, held, exact, lse, seqs, rows, g, groups
        )
        if g == 0:
            grad_gate_up_blocks = after(grad_gate_up_blocks, part_q)
            grad_gate_up_shard = total_of(grad_gate_up_blocks).astype(BF)
            steps = [(grad_gate_up_shard, grad_gate_up_shard)]
            steps.append(relay_step(steps[0], seqs))
            out_there = hop(after(out_far, head_grad), shards, 1)
        grad_q.append(part_q)
        near.append(near_kv)
        far.append(far_kv)
        if g == 0:
            out_sums = pair_sums(out_near, out_there, shard)
        held = after(head_grad, grad_gate_up_shard, out_sums)
    steps[1] = after(steps[1], part_q)
    steps.append(relay_step(steps[1], seqs))
    out_blocks = after(send_chips(out_sums, shards), part_q)
    far = after(far, steps[1], grad_down, out_blocks)
    pairs = kv_pair_sums(near, [hop(each, shards, 1) for each in far])
    out_part = total_of(after(out_blocks, pairs)).astype(BF)
    out_parts = lax.all_to_all(
        out_part.reshape(part, seqs, q_cols), "seq", split_axis=1, concat_axis=1, tiled=True
    )
    sent_grads, product_columns = head_columns(
        grad_q, after(send_chips(pairs, shards), out_part, steps[2]), factor_local, ride_columns
    )
    steps[2] = after(steps[2], product_columns)
    while len(steps) < seqs:
        steps.append(relay_step(steps[-1], seqs))
    token_grads = lax.all_to_all(sent_grads, "seq", split_axis=0, concat_axis=1, tiled=True)

    head_cols = q_cols + kv_cols
    head_far, head_near = split_product(product_rows, product_columns, shard, shards)
    head_sums = pair_sums(head_near, hop(head_far, shards, 1), shard)
    head_blocks = send_chips(head_sums, shards)
    head_part = total_of(after(head_blocks, steps[3]))
    grad_normed = dot_nt(after(token_grads, head_part), attn_full)
    grad_tokens = grad_residual + root_back(inputs, root(inputs), grad_normed)
    base_cols = head_cols + experts
    plane_high, plane_low = two_parts(
        jnp.sum(head_part[:1, base_cols : base_cols + 4], axis=1, keepdims=True)
    )
    lanes = lax.broadcasted_iota(jnp.int32, head_part.shape, 1)
    head_part = jnp.where(
        lanes == base_cols,
        plane_high.astype(F32),
        jnp.where(lanes == base_cols + 1, plane_low.astype(F32), head_part),
    )
    out_own = jnp.sum(out_parts.astype(F32), axis=1)
    head_part = by_rows(jnp.concatenate([head_part, out_own], axis=1).astype(BF))
    head_last = [by_rows(each) for each in send_out([head_part] * seqs, seqs)]
    grad_gate_up, grad_gain_ffn = place_gate_up(after(steps, head_part), w_gate_up, gain_two, z)
    head_last = after(head_last, grad_gate_up)
    grad_query, grad_keyval, grad_out, grad_gain_attn, sums = place_heads(
        head_last, z, w_query, w_keyval, gain_one, q_cols, kv_cols
    )
    loss_value = jnp.sum(sums[0, experts : experts + 2]) / (width * valid_count)
    grad_router_base = sums[:, :experts]
    grad_down = (
        after(grad_down, head_part).reshape(experts, split, part, piece)
        .transpose(0, 1, 3, 2)
        .reshape(experts, units, part)
        .astype(F32)
    )
    grad_gain_ffn = grad_gain_ffn + jnp.sum(w_router.astype(F32) * grad_router_base, axis=1)
    return (
        mixed_exact.astype(BF),
        loss_value,
        grad_tokens,
        grad_gain_attn,
        grad_query,
        grad_keyval,
        grad_out.T,
        grad_gain_ffn,
        grad_router_base * gain_two,
        grad_gate_up,
        grad_down,
    )


def solution(mesh):
    return jax.shard_map(
        local,
        mesh=mesh,
        in_specs=(
            P(("seq", "fsdp"), None),
            P(("seq", "fsdp"), None),
            P(("seq", "fsdp")),
            P(("seq", "fsdp"), None),
            P(("seq", "fsdp"), None),
            P("fsdp"),
            P("fsdp", None),
            P("fsdp", None),
            P(None, "fsdp"),
            P("fsdp"),
            P("fsdp", None),
            P(None, "fsdp", None),
            P(None, None, "fsdp"),
        ),
        out_specs=(
            P(("seq", "fsdp"), None),
            P(),
            P(("seq", "fsdp"), None),
            P("fsdp"),
            P("fsdp", None),
            P("fsdp", None),
            P(None, "fsdp"),
            P("fsdp"),
            P("fsdp", None),
            P(None, "fsdp", None),
            P(None, None, "fsdp"),
        ),
        check_vma=False,
    )
```

```python
import functools
import math

import jax
import jax.numpy as jnp
from jax import lax
from jax.experimental import pallas as pl
from jax.experimental.layout import Layout, with_layout_constraint
from jax.experimental.pallas import tpu as pltpu
from jax.sharding import PartitionSpec as P

HEADS = 24
KVH = 8
HD = 64
CAP = 96
LANES = 128
EPSILON = 1e-06
FLOOR_SCORE = -1e30
BF = jnp.bfloat16
F32 = jnp.float32


def dot(a, b):
    return jnp.dot(a, b, preferred_element_type=F32)


def dot_nt(a, b):
    return lax.dot_general(a, b, (((1,), (1,)), ((), ())), preferred_element_type=F32)


def dot_tn(a, b):
    return lax.dot_general(a, b, (((0,), (0,)), ((), ())), preferred_element_type=F32)


def own_mask(valid_row, rows):
    i = lax.broadcasted_iota(jnp.int32, (rows, rows), 0)
    j = lax.broadcasted_iota(jnp.int32, (rows, rows), 1)
    return jnp.where(j == i, 0.0, jnp.where(j < i, valid_row, FLOOR_SCORE))


def key_chunk(kv_refs, zk, rows, g):
    return jnp.concatenate(
        [ref[pl.ds(zk * rows, rows), pl.ds(g * 2 * HD, 2 * HD)] for ref in kv_refs], axis=0
    )


def forward_kernel(shards, seqs, rows, local_kv, groups, *refs):
    kv_refs = refs[:shards]
    q_ref, bias_ref, low_ref, exact_ref, lse_ref, acc_ref, max_ref = refs[shards:]
    zq = pl.program_id(0)
    stack = groups * rows
    zeros = jnp.zeros((rows, HD), BF)
    half = lax.broadcasted_iota(jnp.int32, (1, 2 * HD), 1) < HD

    def queries(g):
        parts = []
        for h in range(groups):
            start = (g * groups + h) * HD
            parts.append(jnp.concatenate([q_ref[:, start : start + HD], zeros], axis=1))
        return jnp.concatenate(parts, axis=0)

    def chunk(g, zk, scores):
        first = scores is None
        keys = key_chunk(kv_refs, zk, rows, g)
        raw = dot_nt(queries(g), keys)
        if first:
            row = bias_ref[seqs + zk]
            mask = own_mask(row[:, :rows], rows)
            mask = jnp.concatenate([mask] * groups, axis=0)
            masked = jnp.concatenate([raw[:, :rows] + mask, raw[:, rows:] + row[:, rows:]], axis=1)
            new_max = jnp.max(masked, axis=1, keepdims=True)
        else:
            masked = raw + bias_ref[zk]
            new_max = jnp.maximum(max_ref[g][:, :1], jnp.max(masked, axis=1, keepdims=True))
        terms = jnp.exp(masked - new_max).astype(BF)
        ones_values = jnp.where(half, jnp.ones_like(keys), keys)
        part = dot(terms, ones_values)
        if first:
            acc_ref[g] = part
        else:
            acc_ref[g] = acc_ref[g] * jnp.exp(max_ref[g][:, :1] - new_max) + part
        max_ref[g] = jnp.broadcast_to(new_max, (stack, 2 * HD))

    for g in range(local_kv):
        chunk(g, zq, None)

    @pl.loop(0, zq)
    def _(zk):
        for g in range(local_kv):
            chunk(g, zk, True)

    exact_parts, lse_parts = [], []
    for g in range(local_kv):
        acc = acc_ref[g]
        total = acc[:, :HD]
        exact = acc[:, HD:] / total
        lse = max_ref[g][:, :HD] + jnp.log(total)
        for h in range(groups):
            exact_parts.append(exact[h * rows : (h + 1) * rows])
            lse_parts.append(lse[h * rows : (h + 1) * rows])
    exact = jnp.concatenate(exact_parts, axis=1)
    exact_ref[...] = exact
    low_ref[...] = exact.astype(BF)
    lse_ref[...] = jnp.concatenate(lse_parts, axis=1)


def flash_forward(q, kv_blocks, bias, seqs, rows, local_kv, groups):
    shards = len(kv_blocks)
    q_cols = q.shape[1]
    kv_spec = pl.BlockSpec(kv_blocks[0].shape, lambda i: (0, 0))
    q_spec = pl.BlockSpec((rows, q_cols), lambda i: (i, 0))
    stack = groups * rows
    out = jax.ShapeDtypeStruct((seqs * rows, q_cols), F32)
    return pl.pallas_call(
        functools.partial(forward_kernel, shards, seqs, rows, local_kv, groups),
        grid=(seqs,),
        in_specs=[kv_spec] * shards + [q_spec, pl.BlockSpec(bias.shape, lambda i: (0, 0, 0))],
        out_specs=[q_spec] * 3,
        out_shape=[jax.ShapeDtypeStruct((seqs * rows, q_cols), BF), out, out],
        scratch_shapes=[
            pltpu.VMEM((local_kv, stack, 2 * HD), F32),
            pltpu.VMEM((local_kv, stack, 2 * HD), F32),
        ],
        compiler_params=pltpu.CompilerParams(vmem_limit_bytes=20 * 1024 * 1024),
        cost_estimate=pl.CostEstimate(
            flops=0,
            bytes_accessed=0,
            transcendentals=0,
        ),
    )(*kv_blocks, q, bias)


def backward_kernel(shards, seqs, rows, g, groups, *refs):
    kv_refs = [refs[0].at[p] for p in range(shards)]
    (
        q_ref, bias_ref, grad_ref, exact_ref, lse_ref, grad_q_ref, near_ref, far_ref,
        pair_ref, pair_t_ref, lse_wide, delta_wide, acc_q, acc_kv,
    ) = refs[1:]
    zk = pl.program_id(0)
    stack = groups * rows
    zeros = jnp.zeros((rows, HD), BF)

    @pl.when(zk == 0)
    def _():
        acc_q[...] = jnp.zeros_like(acc_q)

        @pl.loop(0, seqs)
        def _(zq):
            here = pl.ds(zq * rows, rows)
            tops, bottoms = [], []
            for h in range(groups):
                cols = slice((g * groups + h) * HD, (g * groups + h + 1) * HD)
                grad = grad_ref[here, cols]
                tops.append(jnp.concatenate([q_ref[here, cols], zeros], axis=1))
                bottoms.append(jnp.concatenate([zeros, grad], axis=1))
                delta = jnp.sum(grad.astype(F32) * exact_ref[here, cols], axis=1, keepdims=True)
                part = slice(h * rows, (h + 1) * rows)
                delta_wide[zq, part] = jnp.broadcast_to(delta, (rows, 2 * HD))
                lse_wide[zq, part] = jnp.broadcast_to(lse_ref[here, cols][:, :1], (rows, 2 * HD))
            pair = jnp.concatenate(tops + bottoms, axis=0)
            pair_ref[zq] = pair
            pair_t_ref[zq] = pair.astype(F32).T.astype(BF)

    def chunk(zq, first):
        keys = key_chunk(kv_refs, zk, rows, g)
        both = dot_nt(pair_ref[zq], keys)
        raw, products = both[:stack], both[stack:]
        if first:
            row = bias_ref[seqs + zk]
            mask = own_mask(row[:, :rows], rows)
            mask = jnp.concatenate([mask] * groups, axis=0)
            masked = jnp.concatenate([raw[:, :rows] + mask, raw[:, rows:] + row[:, rows:]], axis=1)
        else:
            masked = raw + bias_ref[zk]
        weights = jnp.exp(masked - lse_wide[zq][:, :1])
        grads = (weights * (products - delta_wide[zq][:, :1])).astype(BF)
        acc_q[zq] += dot(grads, keys)
        part = dot(pair_t_ref[zq], jnp.concatenate([grads, weights.astype(BF)], axis=0))
        if first:
            acc_kv[...] = part
        else:
            acc_kv[...] += part

    chunk(zk, True)

    @pl.loop(zk + 1, seqs)
    def _(zq):
        chunk(zq, False)

    for p in range(shards):
        target = near_ref if p < shards // 2 else far_ref
        target[p % (shards // 2)] = acc_kv[:, p * rows : (p + 1) * rows].T.astype(BF)

    @pl.when(zk == seqs - 1)
    def _():
        @pl.loop(0, seqs)
        def _(zq):
            total = acc_q[zq]
            parts = [total[h * rows : (h + 1) * rows, :HD] for h in range(groups)]
            grad_q_ref[pl.ds(zq * rows, rows), :] = jnp.concatenate(parts, axis=1) * HD ** (-0.5)


def flash_backward(q, kv_all, bias, grad, exact, lse, seqs, rows, g, groups):
    shards = kv_all.shape[0]
    q_cols = q.shape[1]
    stack = groups * rows
    kv_spec = pl.BlockSpec(kv_all.shape, lambda i: (0, 0, 0))
    whole = pl.BlockSpec((seqs * rows, q_cols), lambda i: (0, 0))
    grad_q_shape = (seqs * rows, groups * HD)
    out_spec = pl.BlockSpec((shards // 2, rows, 2 * HD), lambda i: (0, i, 0))
    out = jax.ShapeDtypeStruct((shards // 2, seqs * rows, 2 * HD), BF)
    return pl.pallas_call(
        functools.partial(backward_kernel, shards, seqs, rows, g, groups),
        grid=(seqs,),
        in_specs=[kv_spec]
        + [whole, pl.BlockSpec(bias.shape, lambda i: (0, 0, 0)), whole, whole, whole],
        out_specs=[pl.BlockSpec(grad_q_shape, lambda i: (0, 0)), out_spec, out_spec],
        out_shape=[jax.ShapeDtypeStruct(grad_q_shape, F32), out, out],
        scratch_shapes=[
            pltpu.VMEM((seqs, 2 * stack, 2 * HD), BF),
            pltpu.VMEM((seqs, 2 * HD, 2 * stack), BF),
            pltpu.VMEM((seqs, stack, 2 * HD), F32),
            pltpu.VMEM((seqs, stack, 2 * HD), F32),
            pltpu.VMEM((seqs, stack, 2 * HD), F32),
            pltpu.VMEM((2 * HD, shards * rows), F32),
        ],
        compiler_params=pltpu.CompilerParams(vmem_limit_bytes=26 * 1024 * 1024),
        cost_estimate=pl.CostEstimate(
            flops=0 if g else 10**12,
            bytes_accessed=0,
            transcendentals=0,
        ),
    )(kv_all, q, bias, grad, exact, lse)


def shift(block, count, step):
    return lax.ppermute(block, "seq", [(i, (i + step) % count) for i in range(count)])


def send_out(blocks, count):
    return [blocks[0]] + [shift(blocks[s], count, s) for s in range(1, count)]


def send_back(blocks, count):
    return [blocks[0]] + [shift(blocks[s], count, count - s) for s in range(1, count)]


def relay_step(blocks, count):
    up, down = blocks
    return (
        lax.ppermute(up, "seq", [(i, i + 1) for i in range(count - 1)]),
        lax.ppermute(down, "seq", [(i + 1, i) for i in range(count - 1)]),
    )


def from_relative(blocks, place):
    count = len(blocks)
    rising = jnp.stack([blocks[-s % count] for s in range(count)])
    return lax.dynamic_slice_in_dim(jnp.concatenate([rising, rising]), count - place, count, 0)


def hop(block, count, mask):
    return lax.ppermute(block, "fsdp", [(i, i ^ mask) for i in range(count)])


def gather_shards(block, count):
    near = [block] + [hop(block, count, 2 * m) for m in range(1, count // 2)]
    return near + [hop(each, count, 1) for each in near]


def send_chips(parts, count):
    return [parts[0]] + [hop(parts[m], count, 2 * m) for m in range(1, count // 2)]


def total_of(blocks):
    total = blocks[0].astype(F32)
    for each in blocks[1:]:
        total = total + each.astype(F32)
    return total


def take(array, index, axis):
    return lax.dynamic_index_in_dim(array, index, axis, keepdims=False)


def product_kernel(core_ref, lhs_ref, rhs_ref, far_ref, near_ref):
    part = lhs_ref.shape[1] // 2
    rhs = rhs_ref[...]
    first = dot_tn(lhs_ref[:, :part], rhs).astype(BF)
    second = dot_tn(lhs_ref[:, part:], rhs).astype(BF)
    core = core_ref[0]

    @pl.when(core == 0)
    def _():
        near_ref[0] = first
        far_ref[0] = second

    @pl.when(core != 0)
    def _():
        near_ref[0] = second
        far_ref[0] = first


def split_product(lhs, rhs, shard, count):
    tokens, width = lhs.shape
    cols = rhs.shape[1]
    part = width // count
    if 2 * part % LANES:
        cut = dot_tn(lhs, rhs).astype(BF).reshape(count // 2, 2, part, cols)
        return take(cut, 1 - shard % 2, 1), take(cut, shard % 2, 1)
    out = jax.ShapeDtypeStruct((count // 2, part, cols), BF)
    out_spec = pl.BlockSpec((1, part, cols), lambda i: (i, 0, 0))
    return pl.pallas_call(
        product_kernel,
        grid=(count // 2,),
        in_specs=[
            pl.BlockSpec(memory_space=pltpu.SMEM),
            pl.BlockSpec((tokens, 2 * part), lambda i: (0, i)),
            pl.BlockSpec((tokens, cols), lambda i: (0, 0)),
        ],
        out_specs=[out_spec, out_spec],
        out_shape=[out, out],
        compiler_params=pltpu.CompilerParams(vmem_limit_bytes=16 * 1024 * 1024),
        cost_estimate=pl.CostEstimate(flops=0, bytes_accessed=0, transcendentals=0),
    )((shard % 2).astype(jnp.int32).reshape(1), lhs, rhs)


def pair_kernel(chip_ref, near_ref, there_ref, own_ref, *part_refs):
    chip = chip_ref[0]
    own_ref[...] = near_ref[chip].astype(F32) + there_ref[chip].astype(F32)
    for m, part_ref in enumerate(part_refs):
        which = chip ^ (m + 1)
        part_ref[...] = (near_ref[which].astype(F32) + there_ref[which].astype(F32)).astype(BF)


def pair_sums(near, there, shard):
    chips, part, cols = near.shape
    tile = math.gcd(cols, 512)
    if tile % LANES:
        tile = cols
    block = pl.BlockSpec((chips, part, tile), lambda i: (0, 0, i))
    out_spec = pl.BlockSpec((part, tile), lambda i: (0, i))
    out = jax.ShapeDtypeStruct((part, cols), BF)
    return pl.pallas_call(
        pair_kernel,
        grid=(cols // tile,),
        in_specs=[pl.BlockSpec(memory_space=pltpu.SMEM), block, block],
        out_specs=[out_spec] * chips,
        out_shape=[jax.ShapeDtypeStruct((part, cols), F32)] + [out] * (chips - 1),
        compiler_params=pltpu.CompilerParams(vmem_limit_bytes=12 * 1024 * 1024),
        cost_estimate=pl.CostEstimate(flops=0, bytes_accessed=0, transcendentals=0),
    )((shard // 2).astype(jnp.int32).reshape(1), near, there)


def fetch_weights(weights_ref, held, sems, piece):
    copies = [
        pltpu.make_async_copy(
            weights_ref.at[:, pl.ds(part * piece, piece)], held.at[part], sems.at[part]
        )
        for part in range(3)
    ]
    return copies


def experts_forward_kernel(count, *refs):
    rows_in, weights_ref = refs[:count], refs[count]
    rows_ref, gate_up_ref, hidden_ref = refs[count + 1 : count + 4]
    out_refs, (held, sems) = refs[count + 4 : -2], refs[-2:]
    piece = hidden_ref.shape[1]
    cap = rows_in[0].shape[0]
    copies = fetch_weights(weights_ref, held, sems, piece)
    for copy in copies:
        copy.start()
    for s in range(count):
        rows_ref[s * cap : (s + 1) * cap, :] = rows_in[s][...]
    rows = rows_ref[...]
    copies[0].wait()
    gate = dot(rows, held[0])
    gate_up_ref[:, :piece] = gate
    copies[1].wait()
    up = dot(rows, held[1])
    gate_up_ref[:, piece:] = up
    hidden = (gate / (1.0 + jnp.exp(-gate)) * up).astype(BF)
    hidden_ref[...] = hidden
    copies[2].wait()
    out = dot_nt(hidden, held[2]).astype(BF)
    for s in range(count):
        out_refs[s][...] = out[s * cap : (s + 1) * cap, :]


def experts_forward(blocks, weights, piece):
    count = len(blocks)
    cap, width = blocks[0].shape
    rows = count * cap
    in_vmem = pl.BlockSpec(memory_space=pltpu.VMEM)
    return pl.pallas_call(
        functools.partial(experts_forward_kernel, count),
        in_specs=[in_vmem] * count + [pl.BlockSpec(memory_space=pltpu.HBM)],
        out_specs=[in_vmem] * (3 + count),
        out_shape=[
            jax.ShapeDtypeStruct((rows, width), BF),
            jax.ShapeDtypeStruct((rows, 2 * piece), F32),
            jax.ShapeDtypeStruct((rows, piece), BF),
        ]
        + [jax.ShapeDtypeStruct((cap, width), BF)] * count,
        scratch_shapes=[pltpu.VMEM((3, width, piece), BF), pltpu.SemaphoreType.DMA((3,))],
        compiler_params=pltpu.CompilerParams(vmem_limit_bytes=56 * 1024 * 1024),
        cost_estimate=pl.CostEstimate(flops=0, bytes_accessed=0, transcendentals=0),
    )(*blocks, weights)


def experts_backward_kernel(count, *refs):
    grads_in, gate_up_ref, weights_ref = refs[:count], refs[count], refs[count + 1]
    grads_ref, rows_ref = refs[count + 2 : count + 4]
    out_refs, (held, sems) = refs[count + 4 : -2], refs[-2:]
    piece = rows_ref.shape[1] // 2
    cap = grads_in[0].shape[0]
    copies = fetch_weights(weights_ref, held, sems, piece)
    for copy in (copies[2], copies[0], copies[1]):
        copy.start()
    for s in range(count):
        grads_ref[s * cap : (s + 1) * cap, :] = grads_in[s][...]
    copies[2].wait()
    grad_hidden = dot(grads_ref[...], held[2])
    gate = gate_up_ref[:, :piece]
    up = gate_up_ref[:, piece:]
    slope = 1.0 / (1.0 + jnp.exp(-gate))
    grad_gate = (grad_hidden * up * slope * (1.0 + gate * (1.0 - slope))).astype(BF)
    grad_up = (grad_hidden * gate * slope).astype(BF)
    rows_ref[:, :piece] = grad_gate
    rows_ref[:, piece:] = grad_up
    copies[0].wait()
    total = dot_nt(grad_gate, held[0])
    copies[1].wait()
    total = (total + dot_nt(grad_up, held[1])).astype(BF)
    for s in range(count):
        out_refs[s][...] = total[s * cap : (s + 1) * cap, :]


def experts_backward(blocks, gate_up, weights, piece):
    count = len(blocks)
    cap, width = blocks[0].shape
    rows = count * cap
    in_vmem = pl.BlockSpec(memory_space=pltpu.VMEM)
    return pl.pallas_call(
        functools.partial(experts_backward_kernel, count),
        in_specs=[in_vmem] * (count + 1) + [pl.BlockSpec(memory_space=pltpu.HBM)],
        out_specs=[in_vmem] * (2 + count),
        out_shape=[
            jax.ShapeDtypeStruct((rows, width), BF),
            jax.ShapeDtypeStruct((rows, 2 * piece), BF),
        ]
        + [jax.ShapeDtypeStruct((cap, width), BF)] * count,
        scratch_shapes=[pltpu.VMEM((3, width, piece), BF), pltpu.SemaphoreType.DMA((3,))],
        compiler_params=pltpu.CompilerParams(vmem_limit_bytes=56 * 1024 * 1024),
        cost_estimate=pl.CostEstimate(flops=0, bytes_accessed=0, transcendentals=0),
    )(*blocks, gate_up, weights)


def kv_pair_kernel(heads, chips, *refs):
    near, there, outs = refs[:heads], refs[heads : 2 * heads], refs[2 * heads :]
    for m in range(chips):
        for g in range(heads):
            total = near[g][m].astype(F32) + there[g][m].astype(F32)
            outs[m][:, g * 2 * HD : (g + 1) * 2 * HD] = total.astype(outs[m].dtype)


def kv_pair_sums(near, there):
    heads, (chips, rows, cols) = len(near), near[0].shape
    in_vmem = pl.BlockSpec(memory_space=pltpu.VMEM)
    out = jax.ShapeDtypeStruct((rows, heads * cols), BF)
    return pl.pallas_call(
        functools.partial(kv_pair_kernel, heads, chips),
        in_specs=[in_vmem] * (2 * heads),
        out_specs=[in_vmem] * chips,
        out_shape=[jax.ShapeDtypeStruct((rows, heads * cols), F32)] + [out] * (chips - 1),
        compiler_params=pltpu.CompilerParams(vmem_limit_bytes=10 * 1024 * 1024),
        cost_estimate=pl.CostEstimate(flops=0, bytes_accessed=0, transcendentals=0),
    )(*near, *there)


def head_columns_kernel(heads, chips, *refs):
    queries, sums = refs[:heads], refs[heads : heads + chips]
    factor_ref, ride_ref, sent_ref, columns_ref = refs[heads + chips :]
    query = jnp.concatenate([each[...] for each in queries], axis=1)
    keyval = sums[0][...]
    for each in sums[1:]:
        keyval = keyval + each[...].astype(F32)
    both = jnp.concatenate([query, keyval], axis=1)
    rows, cols = both.shape
    sent_ref[...] = both.astype(BF)
    columns_ref[:rows, :cols] = (both * factor_ref[...]).astype(BF)
    columns_ref[:rows, cols:] = jnp.zeros((rows, LANES), BF)
    columns_ref[rows:, :cols] = jnp.zeros((ride_ref.shape[0], cols), BF)
    columns_ref[rows:, cols:] = ride_ref[...]


def head_columns(queries, sums, factor, ride):
    rows = sums[0].shape[0]
    cols = sum(each.shape[1] for each in queries) + sums[0].shape[1]
    if cols % LANES:
        both = jnp.concatenate(list(queries) + [total_of(sums)], axis=1)
        scaled = jnp.pad((both * factor).astype(BF), ((0, 0), (0, LANES)))
        return both.astype(BF), jnp.concatenate([scaled, jnp.pad(ride, ((0, 0), (cols, 0)))])
    in_vmem = pl.BlockSpec(memory_space=pltpu.VMEM)
    return pl.pallas_call(
        functools.partial(head_columns_kernel, len(queries), len(sums)),
        in_specs=[in_vmem] * (len(queries) + len(sums) + 2),
        out_specs=[in_vmem] * 2,
        out_shape=[
            jax.ShapeDtypeStruct((rows, cols), BF),
            jax.ShapeDtypeStruct((rows + ride.shape[0], cols + LANES), BF),
        ],
        compiler_params=pltpu.CompilerParams(vmem_limit_bytes=14 * 1024 * 1024),
        cost_estimate=pl.CostEstimate(flops=0, bytes_accessed=0, transcendentals=0),
    )(*queries, *sums, factor, ride)


def two_parts(value):
    high = value.astype(BF)
    return high, (value - high.astype(F32)).astype(BF)


def mark_kernel(seed_ref, out_ref):
    out_ref[...] = seed_ref[...]


def mark(*others):
    seed = after(jnp.zeros((8, LANES), F32), *others)
    return pl.pallas_call(
        mark_kernel,
        out_shape=jax.ShapeDtypeStruct((8, LANES), F32),
        cost_estimate=pl.CostEstimate(flops=10**12, bytes_accessed=8192, transcendentals=0),
    )(seed)


def by_rows(array):
    return with_layout_constraint(array, Layout(major_to_minor=tuple(range(array.ndim))))


def after(values, *others):
    return lax.optimization_barrier((values, others))[0]


def root(values):
    return lax.rsqrt(jnp.mean(values * values, axis=-1, keepdims=True) + EPSILON)


def root_back(values, factor, grad_scaled):
    inner = jnp.mean(grad_scaled * values, axis=-1, keepdims=True)
    return factor * grad_scaled - values * (factor * factor * factor * inner)


def place_gate_up_kernel(count, place_ref, *refs):
    blocks = refs[: 2 * count - 1]
    weight_ref, gain_ref, out_ref, sums_ref, base = refs[2 * count - 1 :]
    offset = place_ref[0] - pl.program_id(1)

    for s in range(2 * count - 1):

        @pl.when(offset == (s if s < count else count - 1 - s))
        def _(s=s):
            base[...] = blocks[s][...].astype(F32)

    @pl.when((pl.program_id(0) == 0) & (pl.program_id(1) == 0))
    def _():
        sums_ref[...] = jnp.zeros_like(sums_ref)

    values = base[...]
    out_ref[0] = values * gain_ref[...]
    product = jnp.sum(weight_ref[0].astype(F32) * values, axis=1, keepdims=True)
    sums_ref[...] += jnp.broadcast_to(product, sums_ref.shape)


def place_gate_up(steps, weight, gain, place):
    experts, part, both = weight.shape
    count = len(steps)
    split = count // experts
    if split == 1:
        tile = math.gcd(both, 1024)
        blocks = [steps[0][0]] + [each[0] for each in steps[1:]] + [each[1] for each in steps[1:]]
        block = pl.BlockSpec((part, tile), lambda t, e: (0, t))
        out, sums = pl.pallas_call(
            functools.partial(place_gate_up_kernel, count),
            grid=(both // tile, experts),
            in_specs=[pl.BlockSpec(memory_space=pltpu.SMEM)]
            + [block] * len(blocks)
            + [
                pl.BlockSpec((1, part, tile), lambda t, e: (e, 0, t)),
                pl.BlockSpec((part, 1), lambda t, e: (0, 0)),
            ],
            out_specs=[
                pl.BlockSpec((1, part, tile), lambda t, e: (e, 0, t)),
                pl.BlockSpec((part, LANES), lambda t, e: (0, 0)),
            ],
            out_shape=[
                jax.ShapeDtypeStruct(weight.shape, F32),
                jax.ShapeDtypeStruct((part, LANES), F32),
            ],
            scratch_shapes=[pltpu.VMEM((part, tile), F32)],
            compiler_params=pltpu.CompilerParams(vmem_limit_bytes=18 * 1024 * 1024),
            cost_estimate=pl.CostEstimate(flops=0, bytes_accessed=0, transcendentals=0),
        )(place.astype(jnp.int32).reshape(1), *blocks, weight, gain)
        return out, sums[:, 0]
    blocks = [steps[0][0]] + [
        jnp.where(place >= s, steps[s][0], steps[count - s][1]) for s in range(1, count)
    ]
    base = (
        from_relative(blocks, place)
        .reshape(experts, split, part, 2, both // (2 * split))
        .transpose(0, 2, 3, 1, 4)
        .reshape(experts, part, both)
        .astype(F32)
    )
    return base * gain, jnp.sum(weight.astype(F32) * base, axis=(0, 2))


def place_kernel(count, q_cols, kv_cols, place_ref, *refs):
    blocks, outs = refs[:count], refs[count : 2 * count]
    w_query_ref, w_keyval_ref, gain_ref, query_ref, keyval_ref, out_ref, base_ref, sums_ref = refs[
        2 * count :
    ]
    gain = gain_ref[...]
    base = jnp.zeros_like(gain)
    sums = jnp.zeros(sums_ref.shape, F32)
    for s in range(count):
        owner = lax.rem(place_ref[0] + (count - s), count)
        q_at = pl.ds(pl.multiple_of(owner * q_cols, LANES), q_cols)
        kv_at = pl.ds(pl.multiple_of(owner * kv_cols, LANES), kv_cols)
        query = blocks[s][:, :q_cols].astype(F32)
        keyval = blocks[s][:, q_cols : q_cols + kv_cols].astype(F32)
        start = q_cols + kv_cols
        sums = sums + blocks[s][:, start : start + LANES].astype(F32)
        out_ref[:, q_at] = outs[s][...].astype(F32)
        base = base + jnp.sum(w_query_ref[:, q_at].astype(F32) * query, axis=1, keepdims=True)
        base = base + jnp.sum(w_keyval_ref[:, kv_at].astype(F32) * keyval, axis=1, keepdims=True)
        query_ref[:, q_at] = query * gain
        keyval_ref[:, kv_at] = keyval * gain
    base_ref[...] = jnp.broadcast_to(base, base_ref.shape)
    sums_ref[...] = sums


def place_heads(blocks, outs, place, w_query, w_keyval, gain, q_cols, kv_cols):
    count = len(blocks)
    part = w_query.shape[0]
    start = q_cols + kv_cols
    if q_cols % LANES == 0 and kv_cols % LANES == 0:
        wide = jax.ShapeDtypeStruct((part, count * q_cols), F32)
        narrow = jax.ShapeDtypeStruct((part, count * kv_cols), F32)
        lanes = jax.ShapeDtypeStruct((part, LANES), F32)
        in_vmem = pl.BlockSpec(memory_space=pltpu.VMEM)
        query, keyval, out, base, sums = pl.pallas_call(
            functools.partial(place_kernel, count, q_cols, kv_cols),
            in_specs=[pl.BlockSpec(memory_space=pltpu.SMEM)] + [in_vmem] * (2 * count + 3),
            out_specs=[in_vmem] * 5,
            out_shape=[wide, narrow, wide, lanes, lanes],
            compiler_params=pltpu.CompilerParams(vmem_limit_bytes=16 * 1024 * 1024),
            cost_estimate=pl.CostEstimate(flops=0, bytes_accessed=0, transcendentals=0),
        )(place.astype(jnp.int32).reshape(1), *blocks, *outs, w_query, w_keyval, gain)
        return query, keyval, out, base[:, 0], sums
    blocks = from_relative(blocks, place).astype(F32)
    outs = from_relative(outs, place).astype(F32)

    def columns(begin, end):
        return blocks[:, :, begin:end].transpose(1, 0, 2).reshape(part, count * (end - begin))

    query, keyval = columns(0, q_cols), columns(q_cols, start)
    base = jnp.sum(w_query.astype(F32) * query, axis=1) + jnp.sum(
        w_keyval.astype(F32) * keyval, axis=1
    )
    sums = jnp.sum(blocks[:, :, start : start + LANES], axis=0)
    out = outs.transpose(1, 0, 2).reshape(part, count * q_cols)
    return query * gain, keyval * gain, out, base, sums


def local(
    tokens,
    teacher,
    valid,
    routes,
    slots,
    gain_attn,
    w_query,
    w_keyval,
    w_out,
    gain_ffn,
    w_router,
    w_gate_up,
    w_down,
):
    seqs = lax.axis_size("seq")
    shards = lax.axis_size("fsdp")
    z = lax.axis_index("seq")
    shard = lax.axis_index("fsdp")
    rows, width = tokens.shape
    groups = HEADS // KVH
    local_kv = KVH // seqs
    q_cols = local_kv * groups * HD
    kv_cols = local_kv * 2 * HD
    local_rows = rows * seqs
    seq_len = local_rows * shards
    experts, part, both = w_gate_up.shape
    units = both // 2
    split = seqs // experts
    piece = units // split
    expert = z // split
    fraction = z % split
    scale = HD ** (-0.5)

    gain_one = gain_attn.astype(F32)[:, None]
    gain_two = gain_ffn.astype(F32)[:, None]
    heads_shard = jnp.concatenate(
        [
            lax.dynamic_slice_in_dim(w_query, z * q_cols, q_cols, 1),
            lax.dynamic_slice_in_dim(w_keyval, z * kv_cols, kv_cols, 1),
        ],
        axis=1,
    )
    heads_shard = (heads_shard.astype(F32) * gain_one).astype(BF)
    heads_full = lax.all_gather(heads_shard, "fsdp", axis=0, tiled=True)
    valid_row = jnp.pad(valid.astype(BF).reshape(1, rows), ((0, 7), (0, width - rows)))
    token_rows = jnp.concatenate([tokens, valid_row], axis=0)
    token_mark = mark(token_rows)
    token_blocks = after(send_out([token_rows] * seqs, seqs), token_mark)

    valid_local = from_relative([each[rows : rows + 1, :rows] for each in token_blocks], z)
    projected = []
    for block in token_blocks:
        projected.append(dot(block[:rows], heads_full) * root(block[:rows].astype(F32)))
    projected = from_relative([each.astype(BF) for each in projected], z)
    projected = projected.reshape(local_rows, q_cols + kv_cols)
    head_queries = projected[:, :q_cols] * jnp.asarray(scale, BF)

    valid_rows_kv = local_rows // kv_cols
    payload = jnp.concatenate(
        [
            projected[:, q_cols:],
            valid_local.reshape(valid_rows_kv, kv_cols),
            jnp.zeros((16 - valid_rows_kv, kv_cols), BF),
        ],
        axis=0,
    )
    kv_blocks = gather_shards(payload, shards)
    late_query, late_keyval, late_router, late_gate_up, late_down = after(
        (w_query, w_keyval, w_router, w_gate_up, w_down), token_mark
    )
    out_full = lax.all_gather(w_out, "fsdp", axis=1, tiled=True)
    own_expert = take(late_gate_up, expert, 0)
    gate_shard = lax.dynamic_slice_in_dim(own_expert, fraction * piece, piece, 1)
    up_shard = lax.dynamic_slice_in_dim(own_expert, units + fraction * piece, piece, 1)
    down_shard = lax.dynamic_slice_in_dim(take(late_down, expert, 0), fraction * piece, piece, 0).T
    router_shard = jnp.pad((late_router.astype(F32) * gain_two).astype(BF), ((0, 0), (0, LANES - experts)))
    expert_shard = jnp.concatenate(
        [
            (gate_shard.astype(F32) * gain_two).astype(BF),
            (up_shard.astype(F32) * gain_two).astype(BF),
            down_shard,
            router_shard,
        ],
        axis=1,
    )
    expert_full = lax.all_gather(expert_shard, "fsdp", axis=0, tiled=True)
    router_full = expert_full[:, 3 * piece :]
    attn_shard = jnp.concatenate(
        [
            each
            for s in range(seqs)
            for each in (
                late_query[:, s * q_cols : (s + 1) * q_cols],
                late_keyval[:, s * kv_cols : (s + 1) * kv_cols],
            )
        ],
        axis=1,
    )
    attn_full = lax.all_gather(
        (attn_shard.astype(F32) * gain_one).astype(BF), "fsdp", axis=0, tiled=True
    )
    order = jnp.asarray(
        [2 * m for m in range(shards // 2)] + [2 * m + 1 for m in range(shards // 2)], jnp.int32
    )
    valid_all = jnp.stack(
        [
            each[local_rows : local_rows + valid_rows_kv].reshape(seqs, rows)
            for each in kv_blocks
        ],
        axis=1,
    ).astype(F32)
    valid_count = jnp.sum(valid_all)
    bias = jnp.where(valid_all > 0, 0.0, FLOOR_SCORE)
    earlier = ((order ^ shard) < shard) | (order == 0)
    bias_same = jnp.where(earlier[None, :, None], bias, FLOOR_SCORE)
    bias = jnp.concatenate([bias, bias_same]).reshape(2 * seqs, 1, shards * rows)
    attended_low, exact, lse = flash_forward(
        head_queries, kv_blocks, bias, seqs, rows, local_kv, groups
    )
    attended = lax.all_to_all(attended_low, "seq", split_axis=0, concat_axis=1, tiled=True)

    inputs = tokens.astype(F32)
    residual = inputs + dot(attended, out_full)
    factor_two = root(residual)
    normed_two = (residual * factor_two).astype(BF)
    logits = dot(normed_two, router_full)[:, :experts]
    expert_ids = jnp.arange(experts, dtype=jnp.int32)
    picked = (routes[:, :, None] == expert_ids).astype(F32)
    chosen = jnp.sum(picked * logits[:, None, :], axis=-1)
    gating = jax.nn.softmax(chosen, axis=-1)
    owners = ((jnp.arange(seqs, dtype=jnp.int32) + z) % seqs) // split
    to_owner = routes[:, :, None] == owners
    slot_hot = slots[:, :, None] == jnp.arange(CAP, dtype=jnp.int32)
    placed = (to_owner[:, :, :, None] & slot_hot[:, :, None, :]).astype(BF)
    placed = placed.reshape(rows, 2, seqs * CAP)
    dispatch = placed[:, 0] + placed[:, 1]
    placed_pairs = jnp.concatenate([placed[:, 0], placed[:, 1]], axis=0)
    sent_rows = dot_tn(dispatch, normed_two).astype(BF)
    kv_all = jnp.stack(after(kv_blocks, sent_rows))
    sent_rows = sent_rows.reshape(seqs, CAP, width)
    expert_rows, gate_up, hidden, *expert_out = experts_forward(
        send_out([sent_rows[s] for s in range(seqs)], seqs), expert_full, piece
    )
    returned = jnp.concatenate(after(send_back(expert_out, seqs), kv_all))
    selected = dot(placed_pairs, returned).reshape(2, rows, width)
    mixed_exact = residual + gating[:, :1] * selected[0] + gating[:, 1:] * selected[1]
    valid_rows = valid.astype(F32)
    errors = (mixed_exact - teacher.astype(F32)) * valid_rows[:, None]
    squares = jnp.sum(errors * errors)
    loss_scale = width * seq_len // 8
    grad_mixed = errors * (2.0 * loss_scale / (width * valid_count))

    grad_gating = jnp.stack(
        [jnp.sum(selected[0] * grad_mixed, axis=-1), jnp.sum(selected[1] * grad_mixed, axis=-1)],
        axis=1,
    )
    grad_chosen = gating * (grad_gating - jnp.sum(gating * grad_gating, axis=-1, keepdims=True))
    grad_logits = jnp.sum(grad_chosen[:, :, None] * picked, axis=1).astype(BF)
    grad_logits = jnp.pad(grad_logits, ((0, 0), (0, LANES - experts)))
    weighted = jnp.concatenate(
        [(gating[:, :1] * grad_mixed).astype(BF), (gating[:, 1:] * grad_mixed).astype(BF)], axis=0
    )
    sent_grads = dot_tn(placed_pairs, weighted).astype(BF).reshape(seqs, CAP, width)
    grad_out_rows = send_out([sent_grads[s] for s in range(seqs)], seqs)
    grad_out_rows = after(grad_out_rows, attn_full, grad_logits)
    grad_expert_out, grad_gate_up_rows, *grad_rows = experts_backward(
        grad_out_rows, gate_up, expert_full, piece
    )
    grad_returned = send_back(grad_rows, seqs)
    tokens_local = from_relative(
        [each[:rows] for each in after(token_blocks, grad_rows)], z
    ).reshape(local_rows, width)
    factor_local = root(tokens_local.astype(F32))
    ride_rows = jnp.concatenate([normed_two, jnp.ones((16, width), BF)], axis=0)
    product_rows = jnp.concatenate([tokens_local, ride_rows], axis=0)
    high, low = two_parts(squares)
    lane = jnp.arange(LANES, dtype=jnp.int32)[None, :]
    marks = jnp.where(lane == experts + 2 * (shard % 2), high, 0) + jnp.where(
        lane == experts + 1 + 2 * (shard % 2), low, 0
    )
    ride_columns = jnp.concatenate(
        [grad_logits, marks.astype(BF), jnp.zeros((15, LANES), BF)], axis=0
    )
    held_out, held_hidden = after((grad_expert_out, hidden), grad_rows)
    down_far, down_near = split_product(held_out, held_hidden, shard, shards)
    grad_down_sums = pair_sums(down_near, hop(down_far, shards, 1), shard)
    held_rows, held_gate_up = after((expert_rows, grad_gate_up_rows), grad_rows)
    gate_up_far, gate_up_near = split_product(held_rows, held_gate_up, shard, shards)
    grad_gate_up_sums = pair_sums(gate_up_near, hop(gate_up_far, shards, 1), shard)
    grad_down_blocks = send_chips(grad_down_sums, shards)
    grad_returned = jnp.concatenate(after(grad_returned, grad_down_sums, product_rows, ride_columns, factor_local))
    grad_normed_two = dot(dispatch, grad_returned) + dot_nt(grad_logits, router_full)
    grad_residual = grad_mixed + root_back(residual, factor_two, grad_normed_two)
    grad_branch = grad_residual.astype(BF)
    grad_attended = dot_nt(after(grad_branch, grad_gate_up_sums), out_full).astype(BF)
    head_grad = lax.all_to_all(grad_attended, "seq", split_axis=1, concat_axis=0, tiled=True)
    grad_gate_up_blocks = send_chips(grad_gate_up_sums, shards)
    grad_down_shard = total_of(after(grad_down_blocks, grad_attended)).astype(BF)
    grad_down = lax.all_gather(grad_down_shard, "seq", axis=0, tiled=False)

    out_far, out_near = split_product(
        after(grad_branch, grad_attended), attended, shard, shards
    )
    grad_q, near, far = [], [], []
    held = after(head_grad, grad_down_shard)
    for g in range(local_kv):
        part_q, near_kv, far_kv = flash_backward(
            head_queries, kv_all, bias, held, exact, lse, seqs, rows, g, groups
        )
        if g == 0:
            grad_gate_up_blocks = after(grad_gate_up_blocks, part_q)
            grad_gate_up_shard = total_of(grad_gate_up_blocks).astype(BF)
            steps = [(grad_gate_up_shard, grad_gate_up_shard)]
            steps.append(relay_step(steps[0], seqs))
            out_there = hop(after(out_far, head_grad), shards, 1)
        grad_q.append(part_q)
        near.append(near_kv)
        far.append(far_kv)
        held = after(head_grad, grad_gate_up_shard, out_there)
    steps[1] = after(steps[1], part_q)
    steps.append(relay_step(steps[1], seqs))
    far = after(far, steps[1], grad_down)
    pairs = kv_pair_sums(near, [hop(each, shards, 1) for each in far])
    out_sums = pair_sums(out_near, after(out_there, pairs), shard)
    sent_grads, product_columns = head_columns(
        grad_q, after(send_chips(pairs, shards), out_sums, steps[2]), factor_local, ride_columns
    )
    steps[2] = after(steps[2], product_columns)
    while len(steps) < seqs:
        steps.append(relay_step(steps[-1], seqs))
    token_grads = lax.all_to_all(sent_grads, "seq", split_axis=0, concat_axis=1, tiled=True)

    head_cols = q_cols + kv_cols
    head_far, head_near = split_product(product_rows, product_columns, shard, shards)
    head_sums = pair_sums(head_near, hop(head_far, shards, 1), shard)
    head_blocks = send_chips(head_sums, shards)
    head_part = total_of(after(head_blocks, steps[3]))
    grad_normed = dot_nt(after(token_grads, head_part), attn_full)
    grad_tokens = grad_residual + root_back(inputs, root(inputs), grad_normed)
    base_cols = head_cols + experts
    plane_high, plane_low = two_parts(
        jnp.sum(head_part[:1, base_cols : base_cols + 4], axis=1, keepdims=True)
    )
    lanes = lax.broadcasted_iota(jnp.int32, head_part.shape, 1)
    head_part = jnp.where(
        lanes == base_cols,
        plane_high.astype(F32),
        jnp.where(lanes == base_cols + 1, plane_low.astype(F32), head_part),
    )
    head_part = by_rows(head_part.astype(BF))
    head_last = [by_rows(each) for each in send_out([head_part] * seqs, seqs)]
    out_blocks = send_chips(after(out_sums, head_part), shards)
    out_part = total_of(out_blocks).astype(BF)
    out_parts = lax.all_to_all(
        out_part.reshape(part, seqs, q_cols), "seq", split_axis=1, concat_axis=1, tiled=True
    )
    out_own = by_rows(jnp.sum(out_parts.astype(F32), axis=1).astype(BF))
    out_last = [by_rows(each) for each in send_out([out_own] * seqs, seqs)]
    grad_gate_up, grad_gain_ffn = place_gate_up(
        after(steps, out_last[1]), w_gate_up, gain_two, z
    )
    grad_query, grad_keyval, grad_out, grad_gain_attn, sums = place_heads(
        head_last, out_last, z, w_query, w_keyval, gain_one, q_cols, kv_cols
    )
    loss_value = jnp.sum(sums[0, experts : experts + 2]) / (width * valid_count)
    grad_router_base = sums[:, :experts]
    grad_down = (
        after(grad_down, head_part).reshape(experts, split, part, piece)
        .transpose(0, 1, 3, 2)
        .reshape(experts, units, part)
        .astype(F32)
    )
    grad_gain_ffn = grad_gain_ffn + jnp.sum(w_router.astype(F32) * grad_router_base, axis=1)
    return (
        mixed_exact.astype(BF),
        loss_value,
        grad_tokens,
        grad_gain_attn,
        grad_query,
        grad_keyval,
        grad_out.T,
        grad_gain_ffn,
        grad_router_base * gain_two,
        grad_gate_up,
        grad_down,
    )


def solution(mesh):
    return jax.shard_map(
        local,
        mesh=mesh,
        in_specs=(
            P(("seq", "fsdp"), None),
            P(("seq", "fsdp"), None),
            P(("seq", "fsdp")),
            P(("seq", "fsdp"), None),
            P(("seq", "fsdp"), None),
            P("fsdp"),
            P("fsdp", None),
            P("fsdp", None),
            P(None, "fsdp"),
            P("fsdp"),
            P("fsdp", None),
            P(None, "fsdp", None),
            P(None, None, "fsdp"),
        ),
        out_specs=(
            P(("seq", "fsdp"), None),
            P(),
            P(("seq", "fsdp"), None),
            P("fsdp"),
            P("fsdp", None),
            P("fsdp", None),
            P(None, "fsdp"),
            P("fsdp"),
            P("fsdp", None),
            P(None, "fsdp", None),
            P(None, None, "fsdp"),
        ),
        check_vma=False,
    )
```

```python
import functools
import math

import jax
import jax.numpy as jnp
from jax import lax
from jax.experimental import pallas as pl
from jax.experimental.layout import Layout, with_layout_constraint
from jax.experimental.pallas import tpu as pltpu
from jax.sharding import PartitionSpec as P

HEADS = 24
KVH = 8
HD = 64
CAP = 96
LANES = 128
EPSILON = 1e-06
FLOOR_SCORE = -1e30
BF = jnp.bfloat16
F32 = jnp.float32


def dot(a, b):
    return jnp.dot(a, b, preferred_element_type=F32)


def dot_nt(a, b):
    return lax.dot_general(a, b, (((1,), (1,)), ((), ())), preferred_element_type=F32)


def dot_tn(a, b):
    return lax.dot_general(a, b, (((0,), (0,)), ((), ())), preferred_element_type=F32)


def own_mask(valid_row, rows):
    i = lax.broadcasted_iota(jnp.int32, (rows, rows), 0)
    j = lax.broadcasted_iota(jnp.int32, (rows, rows), 1)
    return jnp.where(j == i, 0.0, jnp.where(j < i, valid_row, FLOOR_SCORE))


def key_chunk(kv_refs, zk, rows, g):
    return jnp.concatenate(
        [ref[pl.ds(zk * rows, rows), pl.ds(g * 2 * HD, 2 * HD)] for ref in kv_refs], axis=0
    )


def forward_kernel(shards, seqs, rows, local_kv, groups, *refs):
    kv_refs = refs[:shards]
    q_ref, bias_ref, low_ref, exact_ref, lse_ref, acc_ref, max_ref = refs[shards:]
    zq = pl.program_id(0)
    stack = groups * rows
    zeros = jnp.zeros((rows, HD), BF)
    half = lax.broadcasted_iota(jnp.int32, (1, 2 * HD), 1) < HD

    def queries(g):
        parts = []
        for h in range(groups):
            start = (g * groups + h) * HD
            parts.append(jnp.concatenate([q_ref[:, start : start + HD], zeros], axis=1))
        return jnp.concatenate(parts, axis=0)

    def chunk(g, zk, scores):
        first = scores is None
        keys = key_chunk(kv_refs, zk, rows, g)
        raw = dot_nt(queries(g), keys)
        if first:
            row = bias_ref[seqs + zk]
            mask = own_mask(row[:, :rows], rows)
            mask = jnp.concatenate([mask] * groups, axis=0)
            masked = jnp.concatenate([raw[:, :rows] + mask, raw[:, rows:] + row[:, rows:]], axis=1)
            new_max = jnp.max(masked, axis=1, keepdims=True)
        else:
            masked = raw + bias_ref[zk]
            new_max = jnp.maximum(max_ref[g][:, :1], jnp.max(masked, axis=1, keepdims=True))
        terms = jnp.exp(masked - new_max).astype(BF)
        ones_values = jnp.where(half, jnp.ones_like(keys), keys)
        part = dot(terms, ones_values)
        if first:
            acc_ref[g] = part
        else:
            acc_ref[g] = acc_ref[g] * jnp.exp(max_ref[g][:, :1] - new_max) + part
        max_ref[g] = jnp.broadcast_to(new_max, (stack, 2 * HD))

    for g in range(local_kv):
        chunk(g, zq, None)

    @pl.loop(0, zq)
    def _(zk):
        for g in range(local_kv):
            chunk(g, zk, True)

    exact_parts, lse_parts = [], []
    for g in range(local_kv):
        acc = acc_ref[g]
        total = acc[:, :HD]
        exact = acc[:, HD:] / total
        lse = max_ref[g][:, :HD] + jnp.log(total)
        for h in range(groups):
            exact_parts.append(exact[h * rows : (h + 1) * rows])
            lse_parts.append(lse[h * rows : (h + 1) * rows])
    exact = jnp.concatenate(exact_parts, axis=1)
    exact_ref[...] = exact
    low_ref[...] = exact.astype(BF)
    lse_ref[...] = jnp.concatenate(lse_parts, axis=1)


def flash_forward(q, kv_blocks, bias, seqs, rows, local_kv, groups):
    shards = len(kv_blocks)
    q_cols = q.shape[1]
    kv_spec = pl.BlockSpec(kv_blocks[0].shape, lambda i: (0, 0))
    q_spec = pl.BlockSpec((rows, q_cols), lambda i: (i, 0))
    stack = groups * rows
    out = jax.ShapeDtypeStruct((seqs * rows, q_cols), F32)
    return pl.pallas_call(
        functools.partial(forward_kernel, shards, seqs, rows, local_kv, groups),
        grid=(seqs,),
        in_specs=[kv_spec] * shards + [q_spec, pl.BlockSpec(bias.shape, lambda i: (0, 0, 0))],
        out_specs=[q_spec] * 3,
        out_shape=[jax.ShapeDtypeStruct((seqs * rows, q_cols), BF), out, out],
        scratch_shapes=[
            pltpu.VMEM((local_kv, stack, 2 * HD), F32),
            pltpu.VMEM((local_kv, stack, 2 * HD), F32),
        ],
        compiler_params=pltpu.CompilerParams(vmem_limit_bytes=24 * 1024 * 1024),
        cost_estimate=pl.CostEstimate(
            flops=0,
            bytes_accessed=0,
            transcendentals=0,
        ),
    )(*kv_blocks, q, bias)


def backward_kernel(shards, seqs, rows, g, groups, *refs):
    kv_refs = [refs[0].at[p] for p in range(shards)]
    (
        q_ref, bias_ref, grad_ref, exact_ref, lse_ref, grad_q_ref, near_ref, far_ref,
        pair_ref, pair_t_ref, lse_wide, delta_wide, acc_q, acc_kv,
    ) = refs[1:]
    zk = pl.program_id(0)
    stack = groups * rows
    zeros = jnp.zeros((rows, HD), BF)

    @pl.when(zk == 0)
    def _():
        acc_q[...] = jnp.zeros_like(acc_q)

        @pl.loop(0, seqs)
        def _(zq):
            here = pl.ds(zq * rows, rows)
            tops, bottoms = [], []
            for h in range(groups):
                cols = slice((g * groups + h) * HD, (g * groups + h + 1) * HD)
                grad = grad_ref[here, cols]
                tops.append(jnp.concatenate([q_ref[here, cols], zeros], axis=1))
                bottoms.append(jnp.concatenate([zeros, grad], axis=1))
                delta = jnp.sum(grad.astype(F32) * exact_ref[here, cols], axis=1, keepdims=True)
                part = slice(h * rows, (h + 1) * rows)
                delta_wide[zq, part] = jnp.broadcast_to(delta, (rows, 2 * HD))
                lse_wide[zq, part] = jnp.broadcast_to(lse_ref[here, cols][:, :1], (rows, 2 * HD))
            pair = jnp.concatenate(tops + bottoms, axis=0)
            pair_ref[zq] = pair
            pair_t_ref[zq] = pair.astype(F32).T.astype(BF)

    def chunk(zq, first):
        keys = key_chunk(kv_refs, zk, rows, g)
        both = dot_nt(pair_ref[zq], keys)
        raw, products = both[:stack], both[stack:]
        if first:
            row = bias_ref[seqs + zk]
            mask = own_mask(row[:, :rows], rows)
            mask = jnp.concatenate([mask] * groups, axis=0)
            masked = jnp.concatenate([raw[:, :rows] + mask, raw[:, rows:] + row[:, rows:]], axis=1)
        else:
            masked = raw + bias_ref[zk]
        weights = jnp.exp(masked - lse_wide[zq][:, :1])
        grads = (weights * (products - delta_wide[zq][:, :1])).astype(BF)
        acc_q[zq] += dot(grads, keys)
        part = dot(pair_t_ref[zq], jnp.concatenate([grads, weights.astype(BF)], axis=0))
        if first:
            acc_kv[...] = part
        else:
            acc_kv[...] += part

    chunk(zk, True)

    @pl.loop(zk + 1, seqs)
    def _(zq):
        chunk(zq, False)

    for p in range(shards):
        target = near_ref if p < shards // 2 else far_ref
        target[p % (shards // 2)] = acc_kv[:, p * rows : (p + 1) * rows].T.astype(BF)

    @pl.when(zk == seqs - 1)
    def _():
        @pl.loop(0, seqs)
        def _(zq):
            total = acc_q[zq]
            parts = [total[h * rows : (h + 1) * rows, :HD] for h in range(groups)]
            grad_q_ref[pl.ds(zq * rows, rows), :] = jnp.concatenate(parts, axis=1) * HD ** (-0.5)


def flash_backward(q, kv_all, bias, grad, exact, lse, seqs, rows, g, groups):
    shards = kv_all.shape[0]
    q_cols = q.shape[1]
    stack = groups * rows
    kv_spec = pl.BlockSpec(kv_all.shape, lambda i: (0, 0, 0))
    whole = pl.BlockSpec((seqs * rows, q_cols), lambda i: (0, 0))
    grad_q_shape = (seqs * rows, groups * HD)
    out_spec = pl.BlockSpec((shards // 2, rows, 2 * HD), lambda i: (0, i, 0))
    out = jax.ShapeDtypeStruct((shards // 2, seqs * rows, 2 * HD), BF)
    return pl.pallas_call(
        functools.partial(backward_kernel, shards, seqs, rows, g, groups),
        grid=(seqs,),
        in_specs=[kv_spec]
        + [whole, pl.BlockSpec(bias.shape, lambda i: (0, 0, 0)), whole, whole, whole],
        out_specs=[pl.BlockSpec(grad_q_shape, lambda i: (0, 0)), out_spec, out_spec],
        out_shape=[jax.ShapeDtypeStruct(grad_q_shape, F32), out, out],
        scratch_shapes=[
            pltpu.VMEM((seqs, 2 * stack, 2 * HD), BF),
            pltpu.VMEM((seqs, 2 * HD, 2 * stack), BF),
            pltpu.VMEM((seqs, stack, 2 * HD), F32),
            pltpu.VMEM((seqs, stack, 2 * HD), F32),
            pltpu.VMEM((seqs, stack, 2 * HD), F32),
            pltpu.VMEM((2 * HD, shards * rows), F32),
        ],
        compiler_params=pltpu.CompilerParams(vmem_limit_bytes=28 * 1024 * 1024),
        cost_estimate=pl.CostEstimate(
            flops=0 if g else 10**12,
            bytes_accessed=0,
            transcendentals=0,
        ),
    )(kv_all, q, bias, grad, exact, lse)


def shift(block, count, step):
    return lax.ppermute(block, "seq", [(i, (i + step) % count) for i in range(count)])


def send_out(blocks, count):
    return [blocks[0]] + [shift(blocks[s], count, s) for s in range(1, count)]


def send_back(blocks, count):
    return [blocks[0]] + [shift(blocks[s], count, count - s) for s in range(1, count)]


def relay_step(blocks, count):
    up, down = blocks
    return (
        lax.ppermute(up, "seq", [(i, i + 1) for i in range(count - 1)]),
        lax.ppermute(down, "seq", [(i + 1, i) for i in range(count - 1)]),
    )


def from_relative(blocks, place):
    count = len(blocks)
    rising = jnp.stack([blocks[-s % count] for s in range(count)])
    return lax.dynamic_slice_in_dim(jnp.concatenate([rising, rising]), count - place, count, 0)


def hop(block, count, mask):
    return lax.ppermute(block, "fsdp", [(i, i ^ mask) for i in range(count)])


def gather_shards(block, count):
    near = [block] + [hop(block, count, 2 * m) for m in range(1, count // 2)]
    return near + [hop(each, count, 1) for each in near]


def send_chips(parts, count):
    return [parts[0]] + [hop(parts[m], count, 2 * m) for m in range(1, count // 2)]


def total_of(blocks):
    total = blocks[0].astype(F32)
    for each in blocks[1:]:
        total = total + each.astype(F32)
    return total


def take(array, index, axis):
    return lax.dynamic_index_in_dim(array, index, axis, keepdims=False)


def product_kernel(core_ref, lhs_ref, rhs_ref, far_ref, near_ref):
    part = lhs_ref.shape[1] // 2
    rhs = rhs_ref[...]
    first = dot_tn(lhs_ref[:, :part], rhs).astype(BF)
    second = dot_tn(lhs_ref[:, part:], rhs).astype(BF)
    core = core_ref[0]

    @pl.when(core == 0)
    def _():
        near_ref[0] = first
        far_ref[0] = second

    @pl.when(core != 0)
    def _():
        near_ref[0] = second
        far_ref[0] = first


def split_product(lhs, rhs, shard, count):
    tokens, width = lhs.shape
    cols = rhs.shape[1]
    part = width // count
    if 2 * part % LANES:
        cut = dot_tn(lhs, rhs).astype(BF).reshape(count // 2, 2, part, cols)
        return take(cut, 1 - shard % 2, 1), take(cut, shard % 2, 1)
    out = jax.ShapeDtypeStruct((count // 2, part, cols), BF)
    out_spec = pl.BlockSpec((1, part, cols), lambda i: (i, 0, 0))
    return pl.pallas_call(
        product_kernel,
        grid=(count // 2,),
        in_specs=[
            pl.BlockSpec(memory_space=pltpu.SMEM),
            pl.BlockSpec((tokens, 2 * part), lambda i: (0, i)),
            pl.BlockSpec((tokens, cols), lambda i: (0, 0)),
        ],
        out_specs=[out_spec, out_spec],
        out_shape=[out, out],
        compiler_params=pltpu.CompilerParams(vmem_limit_bytes=24 * 1024 * 1024),
        cost_estimate=pl.CostEstimate(flops=0, bytes_accessed=0, transcendentals=0),
    )((shard % 2).astype(jnp.int32).reshape(1), lhs, rhs)


def pair_kernel(chip_ref, near_ref, there_ref, own_ref, *part_refs):
    chip = chip_ref[0]
    own_ref[...] = near_ref[chip].astype(F32) + there_ref[chip].astype(F32)
    for m, part_ref in enumerate(part_refs):
        which = chip ^ (m + 1)
        part_ref[...] = (near_ref[which].astype(F32) + there_ref[which].astype(F32)).astype(BF)


def pair_sums(near, there, shard):
    chips, part, cols = near.shape
    tile = math.gcd(cols, 512)
    if tile % LANES:
        tile = cols
    block = pl.BlockSpec((chips, part, tile), lambda i: (0, 0, i))
    out_spec = pl.BlockSpec((part, tile), lambda i: (0, i))
    out = jax.ShapeDtypeStruct((part, cols), BF)
    return pl.pallas_call(
        pair_kernel,
        grid=(cols // tile,),
        in_specs=[pl.BlockSpec(memory_space=pltpu.SMEM), block, block],
        out_specs=[out_spec] * chips,
        out_shape=[jax.ShapeDtypeStruct((part, cols), F32)] + [out] * (chips - 1),
        compiler_params=pltpu.CompilerParams(vmem_limit_bytes=24 * 1024 * 1024),
        cost_estimate=pl.CostEstimate(flops=0, bytes_accessed=0, transcendentals=0),
    )((shard // 2).astype(jnp.int32).reshape(1), near, there)


def fetch_weights(weights_ref, held, sems, piece):
    copies = [
        pltpu.make_async_copy(
            weights_ref.at[:, pl.ds(part * piece, piece)], held.at[part], sems.at[part]
        )
        for part in range(3)
    ]
    return copies


def experts_forward_kernel(count, *refs):
    rows_in, weights_ref = refs[:count], refs[count]
    rows_ref, gate_up_ref, hidden_ref = refs[count + 1 : count + 4]
    out_refs, (held, sems) = refs[count + 4 : -2], refs[-2:]
    piece = hidden_ref.shape[1]
    cap = rows_in[0].shape[0]
    copies = fetch_weights(weights_ref, held, sems, piece)
    for copy in copies:
        copy.start()
    for s in range(count):
        rows_ref[s * cap : (s + 1) * cap, :] = rows_in[s][...]
    rows = rows_ref[...]
    copies[0].wait()
    gate = dot(rows, held[0])
    gate_up_ref[:, :piece] = gate
    copies[1].wait()
    up = dot(rows, held[1])
    gate_up_ref[:, piece:] = up
    hidden = (gate / (1.0 + jnp.exp(-gate)) * up).astype(BF)
    hidden_ref[...] = hidden
    copies[2].wait()
    out = dot_nt(hidden, held[2]).astype(BF)
    for s in range(count):
        out_refs[s][...] = out[s * cap : (s + 1) * cap, :]


def experts_forward(blocks, weights, piece):
    count = len(blocks)
    cap, width = blocks[0].shape
    rows = count * cap
    in_vmem = pl.BlockSpec(memory_space=pltpu.VMEM)
    return pl.pallas_call(
        functools.partial(experts_forward_kernel, count),
        in_specs=[in_vmem] * count + [pl.BlockSpec(memory_space=pltpu.HBM)],
        out_specs=[in_vmem] * (3 + count),
        out_shape=[
            jax.ShapeDtypeStruct((rows, width), BF),
            jax.ShapeDtypeStruct((rows, 2 * piece), F32),
            jax.ShapeDtypeStruct((rows, piece), BF),
        ]
        + [jax.ShapeDtypeStruct((cap, width), BF)] * count,
        scratch_shapes=[pltpu.VMEM((3, width, piece), BF), pltpu.SemaphoreType.DMA((3,))],
        compiler_params=pltpu.CompilerParams(vmem_limit_bytes=56 * 1024 * 1024),
        cost_estimate=pl.CostEstimate(flops=0, bytes_accessed=0, transcendentals=0),
    )(*blocks, weights)


def experts_backward_kernel(count, *refs):
    grads_in, gate_up_ref, weights_ref = refs[:count], refs[count], refs[count + 1]
    grads_ref, rows_ref = refs[count + 2 : count + 4]
    out_refs, (held, sems) = refs[count + 4 : -2], refs[-2:]
    piece = rows_ref.shape[1] // 2
    cap = grads_in[0].shape[0]
    copies = fetch_weights(weights_ref, held, sems, piece)
    for copy in (copies[2], copies[0], copies[1]):
        copy.start()
    for s in range(count):
        grads_ref[s * cap : (s + 1) * cap, :] = grads_in[s][...]
    copies[2].wait()
    grad_hidden = dot(grads_ref[...], held[2])
    gate = gate_up_ref[:, :piece]
    up = gate_up_ref[:, piece:]
    slope = 1.0 / (1.0 + jnp.exp(-gate))
    grad_gate = (grad_hidden * up * slope * (1.0 + gate * (1.0 - slope))).astype(BF)
    grad_up = (grad_hidden * gate * slope).astype(BF)
    rows_ref[:, :piece] = grad_gate
    rows_ref[:, piece:] = grad_up
    copies[0].wait()
    total = dot_nt(grad_gate, held[0])
    copies[1].wait()
    total = (total + dot_nt(grad_up, held[1])).astype(BF)
    for s in range(count):
        out_refs[s][...] = total[s * cap : (s + 1) * cap, :]


def experts_backward(blocks, gate_up, weights, piece):
    count = len(blocks)
    cap, width = blocks[0].shape
    rows = count * cap
    in_vmem = pl.BlockSpec(memory_space=pltpu.VMEM)
    return pl.pallas_call(
        functools.partial(experts_backward_kernel, count),
        in_specs=[in_vmem] * (count + 1) + [pl.BlockSpec(memory_space=pltpu.HBM)],
        out_specs=[in_vmem] * (2 + count),
        out_shape=[
            jax.ShapeDtypeStruct((rows, width), BF),
            jax.ShapeDtypeStruct((rows, 2 * piece), BF),
        ]
        + [jax.ShapeDtypeStruct((cap, width), BF)] * count,
        scratch_shapes=[pltpu.VMEM((3, width, piece), BF), pltpu.SemaphoreType.DMA((3,))],
        compiler_params=pltpu.CompilerParams(vmem_limit_bytes=56 * 1024 * 1024),
        cost_estimate=pl.CostEstimate(flops=0, bytes_accessed=0, transcendentals=0),
    )(*blocks, gate_up, weights)


def kv_pair_kernel(heads, chips, *refs):
    near, there, outs = refs[:heads], refs[heads : 2 * heads], refs[2 * heads :]
    for m in range(chips):
        for g in range(heads):
            total = near[g][m].astype(F32) + there[g][m].astype(F32)
            outs[m][:, g * 2 * HD : (g + 1) * 2 * HD] = total.astype(outs[m].dtype)


def kv_pair_sums(near, there):
    heads, (chips, rows, cols) = len(near), near[0].shape
    in_vmem = pl.BlockSpec(memory_space=pltpu.VMEM)
    out = jax.ShapeDtypeStruct((rows, heads * cols), BF)
    return pl.pallas_call(
        functools.partial(kv_pair_kernel, heads, chips),
        in_specs=[in_vmem] * (2 * heads),
        out_specs=[in_vmem] * chips,
        out_shape=[jax.ShapeDtypeStruct((rows, heads * cols), F32)] + [out] * (chips - 1),
        compiler_params=pltpu.CompilerParams(vmem_limit_bytes=20 * 1024 * 1024),
        cost_estimate=pl.CostEstimate(flops=0, bytes_accessed=0, transcendentals=0),
    )(*near, *there)


def head_columns_kernel(heads, chips, *refs):
    queries, sums = refs[:heads], refs[heads : heads + chips]
    factor_ref, ride_ref, sent_ref, columns_ref = refs[heads + chips :]
    query = jnp.concatenate([each[...] for each in queries], axis=1)
    keyval = sums[0][...]
    for each in sums[1:]:
        keyval = keyval + each[...].astype(F32)
    both = jnp.concatenate([query, keyval], axis=1)
    rows, cols = both.shape
    sent_ref[...] = both.astype(BF)
    columns_ref[:rows, :cols] = (both * factor_ref[...]).astype(BF)
    columns_ref[:rows, cols:] = jnp.zeros((rows, LANES), BF)
    columns_ref[rows:, :cols] = jnp.zeros((ride_ref.shape[0], cols), BF)
    columns_ref[rows:, cols:] = ride_ref[...]


def head_columns(queries, sums, factor, ride):
    rows = sums[0].shape[0]
    cols = sum(each.shape[1] for each in queries) + sums[0].shape[1]
    if cols % LANES:
        both = jnp.concatenate(list(queries) + [total_of(sums)], axis=1)
        scaled = jnp.pad((both * factor).astype(BF), ((0, 0), (0, LANES)))
        return both.astype(BF), jnp.concatenate([scaled, jnp.pad(ride, ((0, 0), (cols, 0)))])
    in_vmem = pl.BlockSpec(memory_space=pltpu.VMEM)
    return pl.pallas_call(
        functools.partial(head_columns_kernel, len(queries), len(sums)),
        in_specs=[in_vmem] * (len(queries) + len(sums) + 2),
        out_specs=[in_vmem] * 2,
        out_shape=[
            jax.ShapeDtypeStruct((rows, cols), BF),
            jax.ShapeDtypeStruct((rows + ride.shape[0], cols + LANES), BF),
        ],
        compiler_params=pltpu.CompilerParams(vmem_limit_bytes=20 * 1024 * 1024),
        cost_estimate=pl.CostEstimate(flops=0, bytes_accessed=0, transcendentals=0),
    )(*queries, *sums, factor, ride)


def two_parts(value):
    high = value.astype(BF)
    return high, (value - high.astype(F32)).astype(BF)


def mark_kernel(seed_ref, out_ref):
    out_ref[...] = seed_ref[...]


def mark(*others):
    seed = after(jnp.zeros((8, LANES), F32), *others)
    return pl.pallas_call(
        mark_kernel,
        out_shape=jax.ShapeDtypeStruct((8, LANES), F32),
        cost_estimate=pl.CostEstimate(flops=10**12, bytes_accessed=8192, transcendentals=0),
    )(seed)


def by_rows(array):
    return with_layout_constraint(array, Layout(major_to_minor=tuple(range(array.ndim))))


def after(values, *others):
    return lax.optimization_barrier((values, others))[0]


def root(values):
    return lax.rsqrt(jnp.mean(values * values, axis=-1, keepdims=True) + EPSILON)


def root_back(values, factor, grad_scaled):
    inner = jnp.mean(grad_scaled * values, axis=-1, keepdims=True)
    return factor * grad_scaled - values * (factor * factor * factor * inner)


def place_gate_up_kernel(count, place_ref, *refs):
    blocks = refs[: 2 * count - 1]
    weight_ref, gain_ref, out_ref, sums_ref, base = refs[2 * count - 1 :]
    offset = place_ref[0] - pl.program_id(1)

    for s in range(2 * count - 1):

        @pl.when(offset == (s if s < count else count - 1 - s))
        def _(s=s):
            base[...] = blocks[s][...].astype(F32)

    @pl.when((pl.program_id(0) == 0) & (pl.program_id(1) == 0))
    def _():
        sums_ref[...] = jnp.zeros_like(sums_ref)

    values = base[...]
    out_ref[0] = values * gain_ref[...]
    product = jnp.sum(weight_ref[0].astype(F32) * values, axis=1, keepdims=True)
    sums_ref[...] += jnp.broadcast_to(product, sums_ref.shape)


def place_gate_up(steps, weight, gain, place):
    experts, part, both = weight.shape
    count = len(steps)
    split = count // experts
    if split == 1:
        tile = math.gcd(both, 1024)
        blocks = [steps[0][0]] + [each[0] for each in steps[1:]] + [each[1] for each in steps[1:]]
        block = pl.BlockSpec((part, tile), lambda t, e: (0, t))
        out, sums = pl.pallas_call(
            functools.partial(place_gate_up_kernel, count),
            grid=(both // tile, experts),
            in_specs=[pl.BlockSpec(memory_space=pltpu.SMEM)]
            + [block] * len(blocks)
            + [
                pl.BlockSpec((1, part, tile), lambda t, e: (e, 0, t)),
                pl.BlockSpec((part, 1), lambda t, e: (0, 0)),
            ],
            out_specs=[
                pl.BlockSpec((1, part, tile), lambda t, e: (e, 0, t)),
                pl.BlockSpec((part, LANES), lambda t, e: (0, 0)),
            ],
            out_shape=[
                jax.ShapeDtypeStruct(weight.shape, F32),
                jax.ShapeDtypeStruct((part, LANES), F32),
            ],
            scratch_shapes=[pltpu.VMEM((part, tile), F32)],
            compiler_params=pltpu.CompilerParams(vmem_limit_bytes=28 * 1024 * 1024),
            cost_estimate=pl.CostEstimate(flops=0, bytes_accessed=0, transcendentals=0),
        )(place.astype(jnp.int32).reshape(1), *blocks, weight, gain)
        return out, sums[:, 0]
    blocks = [steps[0][0]] + [
        jnp.where(place >= s, steps[s][0], steps[count - s][1]) for s in range(1, count)
    ]
    base = (
        from_relative(blocks, place)
        .reshape(experts, split, part, 2, both // (2 * split))
        .transpose(0, 2, 3, 1, 4)
        .reshape(experts, part, both)
        .astype(F32)
    )
    return base * gain, jnp.sum(weight.astype(F32) * base, axis=(0, 2))


def place_kernel(count, q_cols, kv_cols, place_ref, *refs):
    blocks = refs[:count]
    w_query_ref, w_keyval_ref, gain_ref, query_ref, keyval_ref, out_ref, base_ref, sums_ref = refs[
        count:
    ]
    gain = gain_ref[...]
    base = jnp.zeros_like(gain)
    sums = jnp.zeros(sums_ref.shape, F32)
    for s in range(count):
        owner = lax.rem(place_ref[0] + (count - s), count)
        q_at = pl.ds(pl.multiple_of(owner * q_cols, LANES), q_cols)
        kv_at = pl.ds(pl.multiple_of(owner * kv_cols, LANES), kv_cols)
        query = blocks[s][:, :q_cols].astype(F32)
        keyval = blocks[s][:, q_cols : q_cols + kv_cols].astype(F32)
        start = q_cols + kv_cols
        sums = sums + blocks[s][:, start : start + LANES].astype(F32)
        out_ref[:, q_at] = blocks[s][:, start + LANES :].astype(F32)
        base = base + jnp.sum(w_query_ref[:, q_at].astype(F32) * query, axis=1, keepdims=True)
        base = base + jnp.sum(w_keyval_ref[:, kv_at].astype(F32) * keyval, axis=1, keepdims=True)
        query_ref[:, q_at] = query * gain
        keyval_ref[:, kv_at] = keyval * gain
    base_ref[...] = jnp.broadcast_to(base, base_ref.shape)
    sums_ref[...] = sums


def place_heads(blocks, place, w_query, w_keyval, gain, q_cols, kv_cols):
    count = len(blocks)
    part = w_query.shape[0]
    start = q_cols + kv_cols
    if q_cols % LANES == 0 and kv_cols % LANES == 0:
        wide = jax.ShapeDtypeStruct((part, count * q_cols), F32)
        narrow = jax.ShapeDtypeStruct((part, count * kv_cols), F32)
        lanes = jax.ShapeDtypeStruct((part, LANES), F32)
        in_vmem = pl.BlockSpec(memory_space=pltpu.VMEM)
        query, keyval, out, base, sums = pl.pallas_call(
            functools.partial(place_kernel, count, q_cols, kv_cols),
            in_specs=[pl.BlockSpec(memory_space=pltpu.SMEM)] + [in_vmem] * (count + 3),
            out_specs=[in_vmem] * 5,
            out_shape=[wide, narrow, wide, lanes, lanes],
            compiler_params=pltpu.CompilerParams(vmem_limit_bytes=24 * 1024 * 1024),
            cost_estimate=pl.CostEstimate(flops=0, bytes_accessed=0, transcendentals=0),
        )(place.astype(jnp.int32).reshape(1), *blocks, w_query, w_keyval, gain)
        return query, keyval, out, base[:, 0], sums
    blocks = from_relative(blocks, place).astype(F32)

    def columns(begin, end):
        return blocks[:, :, begin:end].transpose(1, 0, 2).reshape(part, count * (end - begin))

    query, keyval = columns(0, q_cols), columns(q_cols, start)
    base = jnp.sum(w_query.astype(F32) * query, axis=1) + jnp.sum(
        w_keyval.astype(F32) * keyval, axis=1
    )
    sums = jnp.sum(blocks[:, :, start : start + LANES], axis=0)
    out = columns(start + LANES, start + LANES + q_cols)
    return query * gain, keyval * gain, out, base, sums


def local(
    tokens,
    teacher,
    valid,
    routes,
    slots,
    gain_attn,
    w_query,
    w_keyval,
    w_out,
    gain_ffn,
    w_router,
    w_gate_up,
    w_down,
):
    seqs = lax.axis_size("seq")
    shards = lax.axis_size("fsdp")
    z = lax.axis_index("seq")
    shard = lax.axis_index("fsdp")
    rows, width = tokens.shape
    groups = HEADS // KVH
    local_kv = KVH // seqs
    q_cols = local_kv * groups * HD
    kv_cols = local_kv * 2 * HD
    local_rows = rows * seqs
    seq_len = local_rows * shards
    experts, part, both = w_gate_up.shape
    units = both // 2
    split = seqs // experts
    piece = units // split
    expert = z // split
    fraction = z % split
    scale = HD ** (-0.5)

    gain_one = gain_attn.astype(F32)[:, None]
    gain_two = gain_ffn.astype(F32)[:, None]
    heads_shard = jnp.concatenate(
        [
            lax.dynamic_slice_in_dim(w_query, z * q_cols, q_cols, 1),
            lax.dynamic_slice_in_dim(w_keyval, z * kv_cols, kv_cols, 1),
        ],
        axis=1,
    )
    heads_shard = (heads_shard.astype(F32) * gain_one).astype(BF)
    heads_full = lax.all_gather(heads_shard, "fsdp", axis=0, tiled=True)
    valid_row = jnp.pad(valid.astype(BF).reshape(1, rows), ((0, 7), (0, width - rows)))
    token_rows = jnp.concatenate([tokens, valid_row], axis=0)
    token_mark = mark(token_rows)
    token_blocks = after(send_out([token_rows] * seqs, seqs), token_mark)

    valid_local = from_relative([each[rows : rows + 1, :rows] for each in token_blocks], z)
    projected = []
    for block in token_blocks:
        projected.append(dot(block[:rows], heads_full) * root(block[:rows].astype(F32)))
    projected = from_relative([each.astype(BF) for each in projected], z)
    projected = projected.reshape(local_rows, q_cols + kv_cols)
    head_queries = projected[:, :q_cols] * jnp.asarray(scale, BF)

    valid_rows_kv = local_rows // kv_cols
    payload = jnp.concatenate(
        [
            projected[:, q_cols:],
            valid_local.reshape(valid_rows_kv, kv_cols),
            jnp.zeros((16 - valid_rows_kv, kv_cols), BF),
        ],
        axis=0,
    )
    kv_blocks = gather_shards(payload, shards)
    late_query, late_keyval, late_router, late_gate_up, late_down = after(
        (w_query, w_keyval, w_router, w_gate_up, w_down), token_mark
    )
    out_full = lax.all_gather(w_out, "fsdp", axis=1, tiled=True)
    own_expert = take(late_gate_up, expert, 0)
    gate_shard = lax.dynamic_slice_in_dim(own_expert, fraction * piece, piece, 1)
    up_shard = lax.dynamic_slice_in_dim(own_expert, units + fraction * piece, piece, 1)
    down_shard = lax.dynamic_slice_in_dim(take(late_down, expert, 0), fraction * piece, piece, 0).T
    router_shard = jnp.pad((late_router.astype(F32) * gain_two).astype(BF), ((0, 0), (0, LANES - experts)))
    expert_shard = jnp.concatenate(
        [
            (gate_shard.astype(F32) * gain_two).astype(BF),
            (up_shard.astype(F32) * gain_two).astype(BF),
            down_shard,
            router_shard,
        ],
        axis=1,
    )
    expert_full = lax.all_gather(expert_shard, "fsdp", axis=0, tiled=True)
    router_full = expert_full[:, 3 * piece :]
    attn_shard = jnp.concatenate(
        [
            each
            for s in range(seqs)
            for each in (
                late_query[:, s * q_cols : (s + 1) * q_cols],
                late_keyval[:, s * kv_cols : (s + 1) * kv_cols],
            )
        ],
        axis=1,
    )
    attn_full = lax.all_gather(
        (attn_shard.astype(F32) * gain_one).astype(BF), "fsdp", axis=0, tiled=True
    )
    order = jnp.asarray(
        [2 * m for m in range(shards // 2)] + [2 * m + 1 for m in range(shards // 2)], jnp.int32
    )
    valid_all = jnp.stack(
        [
            each[local_rows : local_rows + valid_rows_kv].reshape(seqs, rows)
            for each in kv_blocks
        ],
        axis=1,
    ).astype(F32)
    valid_count = jnp.sum(valid_all)
    bias = jnp.where(valid_all > 0, 0.0, FLOOR_SCORE)
    earlier = ((order ^ shard) < shard) | (order == 0)
    bias_same = jnp.where(earlier[None, :, None], bias, FLOOR_SCORE)
    bias = jnp.concatenate([bias, bias_same]).reshape(2 * seqs, 1, shards * rows)
    attended_low, exact, lse = flash_forward(
        head_queries, kv_blocks, bias, seqs, rows, local_kv, groups
    )
    attended = lax.all_to_all(attended_low, "seq", split_axis=0, concat_axis=1, tiled=True)

    inputs = tokens.astype(F32)
    residual = inputs + dot(attended, out_full)
    factor_two = root(residual)
    normed_two = (residual * factor_two).astype(BF)
    logits = dot(normed_two, router_full)[:, :experts]
    expert_ids = jnp.arange(experts, dtype=jnp.int32)
    picked = (routes[:, :, None] == expert_ids).astype(F32)
    chosen = jnp.sum(picked * logits[:, None, :], axis=-1)
    gating = jax.nn.softmax(chosen, axis=-1)
    owners = ((jnp.arange(seqs, dtype=jnp.int32) + z) % seqs) // split
    to_owner = routes[:, :, None] == owners
    slot_hot = slots[:, :, None] == jnp.arange(CAP, dtype=jnp.int32)
    placed = (to_owner[:, :, :, None] & slot_hot[:, :, None, :]).astype(BF)
    placed = placed.reshape(rows, 2, seqs * CAP)
    dispatch = placed[:, 0] + placed[:, 1]
    placed_pairs = jnp.concatenate([placed[:, 0], placed[:, 1]], axis=0)
    sent_rows = dot_tn(dispatch, normed_two).astype(BF)
    kv_all = jnp.stack(after(kv_blocks, sent_rows))
    sent_rows = sent_rows.reshape(seqs, CAP, width)
    expert_rows, gate_up, hidden, *expert_out = experts_forward(
        send_out([sent_rows[s] for s in range(seqs)], seqs), expert_full, piece
    )
    returned = jnp.concatenate(after(send_back(expert_out, seqs), kv_all))
    selected = dot(placed_pairs, returned).reshape(2, rows, width)
    mixed_exact = residual + gating[:, :1] * selected[0] + gating[:, 1:] * selected[1]
    valid_rows = valid.astype(F32)
    errors = (mixed_exact - teacher.astype(F32)) * valid_rows[:, None]
    squares = jnp.sum(errors * errors)
    loss_scale = width * seq_len // 8
    grad_mixed = errors * (2.0 * loss_scale / (width * valid_count))

    grad_gating = jnp.stack(
        [jnp.sum(selected[0] * grad_mixed, axis=-1), jnp.sum(selected[1] * grad_mixed, axis=-1)],
        axis=1,
    )
    grad_chosen = gating * (grad_gating - jnp.sum(gating * grad_gating, axis=-1, keepdims=True))
    grad_logits = jnp.sum(grad_chosen[:, :, None] * picked, axis=1).astype(BF)
    grad_logits = jnp.pad(grad_logits, ((0, 0), (0, LANES - experts)))
    weighted = jnp.concatenate(
        [(gating[:, :1] * grad_mixed).astype(BF), (gating[:, 1:] * grad_mixed).astype(BF)], axis=0
    )
    sent_grads = dot_tn(placed_pairs, weighted).astype(BF).reshape(seqs, CAP, width)
    grad_out_rows = send_out([sent_grads[s] for s in range(seqs)], seqs)
    grad_out_rows = after(grad_out_rows, attn_full, grad_logits)
    grad_expert_out, grad_gate_up_rows, *grad_rows = experts_backward(
        grad_out_rows, gate_up, expert_full, piece
    )
    grad_returned = send_back(grad_rows, seqs)
    tokens_local = from_relative(
        [each[:rows] for each in after(token_blocks, grad_rows)], z
    ).reshape(local_rows, width)
    factor_local = root(tokens_local.astype(F32))
    ride_rows = jnp.concatenate([normed_two, jnp.ones((16, width), BF)], axis=0)
    product_rows = jnp.concatenate([tokens_local, ride_rows], axis=0)
    high, low = two_parts(squares)
    lane = jnp.arange(LANES, dtype=jnp.int32)[None, :]
    marks = jnp.where(lane == experts + 2 * (shard % 2), high, 0) + jnp.where(
        lane == experts + 1 + 2 * (shard % 2), low, 0
    )
    ride_columns = jnp.concatenate(
        [grad_logits, marks.astype(BF), jnp.zeros((15, LANES), BF)], axis=0
    )
    held_out, held_hidden = after((grad_expert_out, hidden), grad_rows)
    down_far, down_near = split_product(held_out, held_hidden, shard, shards)
    grad_down_sums = pair_sums(down_near, hop(down_far, shards, 1), shard)
    held_rows, held_gate_up = after((expert_rows, grad_gate_up_rows), grad_rows)
    gate_up_far, gate_up_near = split_product(held_rows, held_gate_up, shard, shards)
    grad_gate_up_sums = pair_sums(gate_up_near, hop(gate_up_far, shards, 1), shard)
    grad_down_blocks = send_chips(grad_down_sums, shards)
    grad_returned = jnp.concatenate(after(grad_returned, grad_down_sums, product_rows, ride_columns, factor_local))
    grad_normed_two = dot(dispatch, grad_returned) + dot_nt(grad_logits, router_full)
    grad_residual = grad_mixed + root_back(residual, factor_two, grad_normed_two)
    grad_branch = grad_residual.astype(BF)
    grad_attended = dot_nt(after(grad_branch, grad_gate_up_sums), out_full).astype(BF)
    head_grad = lax.all_to_all(grad_attended, "seq", split_axis=1, concat_axis=0, tiled=True)
    grad_gate_up_blocks = send_chips(grad_gate_up_sums, shards)
    grad_down_shard = total_of(after(grad_down_blocks, grad_attended)).astype(BF)
    grad_down = lax.all_gather(grad_down_shard, "seq", axis=0, tiled=False)

    out_far, out_near = split_product(
        after(grad_branch, grad_attended), attended, shard, shards
    )
    grad_q, near, far = [], [], []
    held = after(head_grad, grad_down_shard)
    for g in range(local_kv):
        part_q, near_kv, far_kv = flash_backward(
            head_queries, kv_all, bias, held, exact, lse, seqs, rows, g, groups
        )
        if g == 0:
            grad_gate_up_blocks = after(grad_gate_up_blocks, part_q)
            grad_gate_up_shard = total_of(grad_gate_up_blocks).astype(BF)
            steps = [(grad_gate_up_shard, grad_gate_up_shard)]
            steps.append(relay_step(steps[0], seqs))
            out_there = hop(after(out_far, head_grad), shards, 1)
        grad_q.append(part_q)
        near.append(near_kv)
        far.append(far_kv)
        if g == 0:
            out_sums = pair_sums(out_near, out_there, shard)
        held = after(head_grad, grad_gate_up_shard, out_sums)
    steps[1] = after(steps[1], part_q)
    steps.append(relay_step(steps[1], seqs))
    out_blocks = after(send_chips(out_sums, shards), part_q)
    far = after(far, steps[1], grad_down, out_blocks)
    pairs = kv_pair_sums(near, [hop(each, shards, 1) for each in far])
    out_part = total_of(after(out_blocks, pairs)).astype(BF)
    out_parts = lax.all_to_all(
        out_part.reshape(part, seqs, q_cols), "seq", split_axis=1, concat_axis=1, tiled=True
    )
    sent_grads, product_columns = head_columns(
        grad_q, after(send_chips(pairs, shards), out_part, steps[2]), factor_local, ride_columns
    )
    steps[2] = after(steps[2], product_columns)
    while len(steps) < seqs:
        steps.append(relay_step(steps[-1], seqs))
    token_grads = lax.all_to_all(sent_grads, "seq", split_axis=0, concat_axis=1, tiled=True)

    head_cols = q_cols + kv_cols
    head_far, head_near = split_product(
        product_rows, after(product_columns, out_parts), shard, shards
    )
    head_sums = pair_sums(head_near, hop(head_far, shards, 1), shard)
    head_blocks = send_chips(head_sums, shards)
    head_part = total_of(after(head_blocks, steps[3], token_grads))
    grad_normed = dot_nt(after(token_grads, head_part), attn_full)
    grad_tokens = grad_residual + root_back(inputs, root(inputs), grad_normed)
    base_cols = head_cols + experts
    plane_high, plane_low = two_parts(
        jnp.sum(head_part[:1, base_cols : base_cols + 4], axis=1, keepdims=True)
    )
    lanes = lax.broadcasted_iota(jnp.int32, head_part.shape, 1)
    head_part = jnp.where(
        lanes == base_cols,
        plane_high.astype(F32),
        jnp.where(lanes == base_cols + 1, plane_low.astype(F32), head_part),
    )
    out_own = jnp.sum(out_parts.astype(F32), axis=1)
    head_part = by_rows(jnp.concatenate([head_part, out_own], axis=1).astype(BF))
    head_last = [by_rows(each) for each in send_out([head_part] * seqs, seqs)]
    grad_gate_up, grad_gain_ffn = place_gate_up(after(steps, head_part), w_gate_up, gain_two, z)
    head_last = after(head_last, grad_gate_up)
    grad_query, grad_keyval, grad_out, grad_gain_attn, sums = place_heads(
        head_last, z, w_query, w_keyval, gain_one, q_cols, kv_cols
    )
    loss_value = jnp.sum(sums[0, experts : experts + 2]) / (width * valid_count)
    grad_router_base = sums[:, :experts]
    grad_down = (
        after(grad_down, head_part).reshape(experts, split, part, piece)
        .transpose(0, 1, 3, 2)
        .reshape(experts, units, part)
        .astype(F32)
    )
    grad_gain_ffn = grad_gain_ffn + jnp.sum(w_router.astype(F32) * grad_router_base, axis=1)
    return (
        mixed_exact.astype(BF),
        loss_value,
        grad_tokens,
        grad_gain_attn,
        grad_query,
        grad_keyval,
        grad_out.T,
        grad_gain_ffn,
        grad_router_base * gain_two,
        grad_gate_up,
        grad_down,
    )


def solution(mesh):
    return jax.shard_map(
        local,
        mesh=mesh,
        in_specs=(
            P(("seq", "fsdp"), None),
            P(("seq", "fsdp"), None),
            P(("seq", "fsdp")),
            P(("seq", "fsdp"), None),
            P(("seq", "fsdp"), None),
            P("fsdp"),
            P("fsdp", None),
            P("fsdp", None),
            P(None, "fsdp"),
            P("fsdp"),
            P("fsdp", None),
            P(None, "fsdp", None),
            P(None, None, "fsdp"),
        ),
        out_specs=(
            P(("seq", "fsdp"), None),
            P(),
            P(("seq", "fsdp"), None),
            P("fsdp"),
            P("fsdp", None),
            P("fsdp", None),
            P(None, "fsdp"),
            P("fsdp"),
            P("fsdp", None),
            P(None, "fsdp", None),
            P(None, None, "fsdp"),
        ),
        check_vma=False,
    )
```

```python
import functools
import math

import jax
import jax.numpy as jnp
from jax import lax
from jax.experimental import pallas as pl
from jax.experimental.layout import Layout, with_layout_constraint
from jax.experimental.pallas import tpu as pltpu
from jax.sharding import PartitionSpec as P

HEADS = 24
KVH = 8
HD = 64
CAP = 96
LANES = 128
EPSILON = 1e-06
FLOOR_SCORE = -1e30
BF = jnp.bfloat16
F32 = jnp.float32


def dot(a, b):
    return jnp.dot(a, b, preferred_element_type=F32)


def dot_nt(a, b):
    return lax.dot_general(a, b, (((1,), (1,)), ((), ())), preferred_element_type=F32)


def dot_tn(a, b):
    return lax.dot_general(a, b, (((0,), (0,)), ((), ())), preferred_element_type=F32)


def own_mask(valid_row, rows):
    i = lax.broadcasted_iota(jnp.int32, (rows, rows), 0)
    j = lax.broadcasted_iota(jnp.int32, (rows, rows), 1)
    return jnp.where(j == i, 0.0, jnp.where(j < i, valid_row, FLOOR_SCORE))


def key_chunk(kv_refs, zk, rows, g):
    return jnp.concatenate(
        [ref[pl.ds(zk * rows, rows), pl.ds(g * 2 * HD, 2 * HD)] for ref in kv_refs], axis=0
    )


def forward_kernel(shards, seqs, rows, local_kv, groups, *refs):
    kv_refs = refs[:shards]
    q_ref, bias_ref, low_ref, exact_ref, lse_ref, acc_ref, max_ref = refs[shards:]
    zq = pl.program_id(0)
    stack = groups * rows
    zeros = jnp.zeros((rows, HD), BF)
    half = lax.broadcasted_iota(jnp.int32, (1, 2 * HD), 1) < HD

    def queries(g):
        parts = []
        for h in range(groups):
            start = (g * groups + h) * HD
            parts.append(jnp.concatenate([q_ref[:, start : start + HD], zeros], axis=1))
        return jnp.concatenate(parts, axis=0)

    def chunk(g, zk, scores):
        first = scores is None
        keys = key_chunk(kv_refs, zk, rows, g)
        raw = dot_nt(queries(g), keys)
        if first:
            row = bias_ref[seqs + zk]
            mask = own_mask(row[:, :rows], rows)
            mask = jnp.concatenate([mask] * groups, axis=0)
            masked = jnp.concatenate([raw[:, :rows] + mask, raw[:, rows:] + row[:, rows:]], axis=1)
            new_max = jnp.max(masked, axis=1, keepdims=True)
        else:
            masked = raw + bias_ref[zk]
            new_max = jnp.maximum(max_ref[g][:, :1], jnp.max(masked, axis=1, keepdims=True))
        terms = jnp.exp(masked - new_max).astype(BF)
        ones_values = jnp.where(half, jnp.ones_like(keys), keys)
        part = dot(terms, ones_values)
        if first:
            acc_ref[g] = part
        else:
            acc_ref[g] = acc_ref[g] * jnp.exp(max_ref[g][:, :1] - new_max) + part
        max_ref[g] = jnp.broadcast_to(new_max, (stack, 2 * HD))

    for g in range(local_kv):
        chunk(g, zq, None)

    @pl.loop(0, zq)
    def _(zk):
        for g in range(local_kv):
            chunk(g, zk, True)

    exact_parts, lse_parts = [], []
    for g in range(local_kv):
        acc = acc_ref[g]
        total = acc[:, :HD]
        exact = acc[:, HD:] / total
        lse = max_ref[g][:, :HD] + jnp.log(total)
        for h in range(groups):
            exact_parts.append(exact[h * rows : (h + 1) * rows])
            lse_parts.append(lse[h * rows : (h + 1) * rows])
    exact = jnp.concatenate(exact_parts, axis=1)
    exact_ref[...] = exact
    low_ref[...] = exact.astype(BF)
    lse_ref[...] = jnp.concatenate(lse_parts, axis=1)


def flash_forward(q, kv_blocks, bias, seqs, rows, local_kv, groups):
    shards = len(kv_blocks)
    q_cols = q.shape[1]
    kv_spec = pl.BlockSpec(kv_blocks[0].shape, lambda i: (0, 0))
    q_spec = pl.BlockSpec((rows, q_cols), lambda i: (i, 0))
    stack = groups * rows
    out = jax.ShapeDtypeStruct((seqs * rows, q_cols), F32)
    return pl.pallas_call(
        functools.partial(forward_kernel, shards, seqs, rows, local_kv, groups),
        grid=(seqs,),
        in_specs=[kv_spec] * shards + [q_spec, pl.BlockSpec(bias.shape, lambda i: (0, 0, 0))],
        out_specs=[q_spec] * 3,
        out_shape=[jax.ShapeDtypeStruct((seqs * rows, q_cols), BF), out, out],
        scratch_shapes=[
            pltpu.VMEM((local_kv, stack, 2 * HD), F32),
            pltpu.VMEM((local_kv, stack, 2 * HD), F32),
        ],
        compiler_params=pltpu.CompilerParams(vmem_limit_bytes=24 * 1024 * 1024),
        cost_estimate=pl.CostEstimate(
            flops=0,
            bytes_accessed=0,
            transcendentals=0,
        ),
    )(*kv_blocks, q, bias)


def backward_kernel(shards, seqs, rows, g, groups, *refs):
    kv_refs = [refs[0].at[p] for p in range(shards)]
    (
        q_ref, bias_ref, grad_ref, exact_ref, lse_ref, grad_q_ref, near_ref, far_ref,
        pair_ref, pair_t_ref, lse_wide, delta_wide, acc_q, acc_kv,
    ) = refs[1:]
    zk = pl.program_id(0)
    stack = groups * rows
    zeros = jnp.zeros((rows, HD), BF)

    @pl.when(zk == 0)
    def _():
        acc_q[...] = jnp.zeros_like(acc_q)

        @pl.loop(0, seqs)
        def _(zq):
            here = pl.ds(zq * rows, rows)
            tops, bottoms = [], []
            for h in range(groups):
                cols = slice((g * groups + h) * HD, (g * groups + h + 1) * HD)
                grad = grad_ref[here, cols]
                tops.append(jnp.concatenate([q_ref[here, cols], zeros], axis=1))
                bottoms.append(jnp.concatenate([zeros, grad], axis=1))
                delta = jnp.sum(grad.astype(F32) * exact_ref[here, cols], axis=1, keepdims=True)
                part = slice(h * rows, (h + 1) * rows)
                delta_wide[zq, part] = jnp.broadcast_to(delta, (rows, 2 * HD))
                lse_wide[zq, part] = jnp.broadcast_to(lse_ref[here, cols][:, :1], (rows, 2 * HD))
            pair = jnp.concatenate(tops + bottoms, axis=0)
            pair_ref[zq] = pair
            pair_t_ref[zq] = pair.astype(F32).T.astype(BF)

    def chunk(zq, first):
        keys = key_chunk(kv_refs, zk, rows, g)
        both = dot_nt(pair_ref[zq], keys)
        raw, products = both[:stack], both[stack:]
        if first:
            row = bias_ref[seqs + zk]
            mask = own_mask(row[:, :rows], rows)
            mask = jnp.concatenate([mask] * groups, axis=0)
            masked = jnp.concatenate([raw[:, :rows] + mask, raw[:, rows:] + row[:, rows:]], axis=1)
        else:
            masked = raw + bias_ref[zk]
        weights = jnp.exp(masked - lse_wide[zq][:, :1])
        grads = (weights * (products - delta_wide[zq][:, :1])).astype(BF)
        acc_q[zq] += dot(grads, keys)
        part = dot(pair_t_ref[zq], jnp.concatenate([grads, weights.astype(BF)], axis=0))
        if first:
            acc_kv[...] = part
        else:
            acc_kv[...] += part

    chunk(zk, True)

    @pl.loop(zk + 1, seqs)
    def _(zq):
        chunk(zq, False)

    for p in range(shards):
        target = near_ref if p < shards // 2 else far_ref
        target[p % (shards // 2)] = acc_kv[:, p * rows : (p + 1) * rows].T.astype(BF)

    @pl.when(zk == seqs - 1)
    def _():
        @pl.loop(0, seqs)
        def _(zq):
            total = acc_q[zq]
            parts = [total[h * rows : (h + 1) * rows, :HD] for h in range(groups)]
            grad_q_ref[pl.ds(zq * rows, rows), :] = jnp.concatenate(parts, axis=1) * HD ** (-0.5)


def flash_backward(q, kv_all, bias, grad, exact, lse, seqs, rows, g, groups):
    shards = kv_all.shape[0]
    q_cols = q.shape[1]
    stack = groups * rows
    kv_spec = pl.BlockSpec(kv_all.shape, lambda i: (0, 0, 0))
    whole = pl.BlockSpec((seqs * rows, q_cols), lambda i: (0, 0))
    grad_q_shape = (seqs * rows, groups * HD)
    out_spec = pl.BlockSpec((shards // 2, rows, 2 * HD), lambda i: (0, i, 0))
    out = jax.ShapeDtypeStruct((shards // 2, seqs * rows, 2 * HD), BF)
    return pl.pallas_call(
        functools.partial(backward_kernel, shards, seqs, rows, g, groups),
        grid=(seqs,),
        in_specs=[kv_spec]
        + [whole, pl.BlockSpec(bias.shape, lambda i: (0, 0, 0)), whole, whole, whole],
        out_specs=[pl.BlockSpec(grad_q_shape, lambda i: (0, 0)), out_spec, out_spec],
        out_shape=[jax.ShapeDtypeStruct(grad_q_shape, F32), out, out],
        scratch_shapes=[
            pltpu.VMEM((seqs, 2 * stack, 2 * HD), BF),
            pltpu.VMEM((seqs, 2 * HD, 2 * stack), BF),
            pltpu.VMEM((seqs, stack, 2 * HD), F32),
            pltpu.VMEM((seqs, stack, 2 * HD), F32),
            pltpu.VMEM((seqs, stack, 2 * HD), F32),
            pltpu.VMEM((2 * HD, shards * rows), F32),
        ],
        compiler_params=pltpu.CompilerParams(vmem_limit_bytes=28 * 1024 * 1024),
        cost_estimate=pl.CostEstimate(
            flops=0 if g else 10**12,
            bytes_accessed=0,
            transcendentals=0,
        ),
    )(kv_all, q, bias, grad, exact, lse)


def shift(block, count, step):
    return lax.ppermute(block, "seq", [(i, (i + step) % count) for i in range(count)])


def send_out(blocks, count):
    return [blocks[0]] + [shift(blocks[s], count, s) for s in range(1, count)]


def send_back(blocks, count):
    return [blocks[0]] + [shift(blocks[s], count, count - s) for s in range(1, count)]


def relay_step(blocks, count):
    up, down = blocks
    return (
        lax.ppermute(up, "seq", [(i, i + 1) for i in range(count - 1)]),
        lax.ppermute(down, "seq", [(i + 1, i) for i in range(count - 1)]),
    )


def from_relative(blocks, place):
    count = len(blocks)
    rising = jnp.stack([blocks[-s % count] for s in range(count)])
    return lax.dynamic_slice_in_dim(jnp.concatenate([rising, rising]), count - place, count, 0)


def hop(block, count, mask):
    return lax.ppermute(block, "fsdp", [(i, i ^ mask) for i in range(count)])


def gather_shards(block, count):
    near = [block] + [hop(block, count, 2 * m) for m in range(1, count // 2)]
    return near + [hop(each, count, 1) for each in near]


def send_chips(parts, count):
    return [parts[0]] + [hop(parts[m], count, 2 * m) for m in range(1, count // 2)]


def total_of(blocks):
    total = blocks[0].astype(F32)
    for each in blocks[1:]:
        total = total + each.astype(F32)
    return total


def take(array, index, axis):
    return lax.dynamic_index_in_dim(array, index, axis, keepdims=False)


def product_kernel(core_ref, lhs_ref, rhs_ref, far_ref, near_ref):
    part = lhs_ref.shape[1] // 2
    rhs = rhs_ref[...]
    first = dot_tn(lhs_ref[:, :part], rhs).astype(BF)
    second = dot_tn(lhs_ref[:, part:], rhs).astype(BF)
    core = core_ref[0]

    @pl.when(core == 0)
    def _():
        near_ref[0] = first
        far_ref[0] = second

    @pl.when(core != 0)
    def _():
        near_ref[0] = second
        far_ref[0] = first


def split_product(lhs, rhs, shard, count):
    tokens, width = lhs.shape
    cols = rhs.shape[1]
    part = width // count
    if 2 * part % LANES:
        cut = dot_tn(lhs, rhs).astype(BF).reshape(count // 2, 2, part, cols)
        return take(cut, 1 - shard % 2, 1), take(cut, shard % 2, 1)
    out = jax.ShapeDtypeStruct((count // 2, part, cols), BF)
    out_spec = pl.BlockSpec((1, part, cols), lambda i: (i, 0, 0))
    return pl.pallas_call(
        product_kernel,
        grid=(count // 2,),
        in_specs=[
            pl.BlockSpec(memory_space=pltpu.SMEM),
            pl.BlockSpec((tokens, 2 * part), lambda i: (0, i)),
            pl.BlockSpec((tokens, cols), lambda i: (0, 0)),
        ],
        out_specs=[out_spec, out_spec],
        out_shape=[out, out],
        compiler_params=pltpu.CompilerParams(vmem_limit_bytes=24 * 1024 * 1024),
        cost_estimate=pl.CostEstimate(flops=0, bytes_accessed=0, transcendentals=0),
    )((shard % 2).astype(jnp.int32).reshape(1), lhs, rhs)


def pair_kernel(chip_ref, near_ref, there_ref, own_ref, *part_refs):
    chip = chip_ref[0]
    own_ref[...] = near_ref[chip].astype(F32) + there_ref[chip].astype(F32)
    for m, part_ref in enumerate(part_refs):
        which = chip ^ (m + 1)
        part_ref[...] = (near_ref[which].astype(F32) + there_ref[which].astype(F32)).astype(BF)


def pair_sums(near, there, shard):
    chips, part, cols = near.shape
    tile = math.gcd(cols, 512)
    if tile % LANES:
        tile = cols
    block = pl.BlockSpec((chips, part, tile), lambda i: (0, 0, i))
    out_spec = pl.BlockSpec((part, tile), lambda i: (0, i))
    out = jax.ShapeDtypeStruct((part, cols), BF)
    return pl.pallas_call(
        pair_kernel,
        grid=(cols // tile,),
        in_specs=[pl.BlockSpec(memory_space=pltpu.SMEM), block, block],
        out_specs=[out_spec] * chips,
        out_shape=[jax.ShapeDtypeStruct((part, cols), F32)] + [out] * (chips - 1),
        compiler_params=pltpu.CompilerParams(vmem_limit_bytes=24 * 1024 * 1024),
        cost_estimate=pl.CostEstimate(flops=0, bytes_accessed=0, transcendentals=0),
    )((shard // 2).astype(jnp.int32).reshape(1), near, there)


def fetch_weights(weights_ref, held, sems, piece):
    copies = [
        pltpu.make_async_copy(
            weights_ref.at[:, pl.ds(part * piece, piece)], held.at[part], sems.at[part]
        )
        for part in range(3)
    ]
    return copies


def experts_forward_kernel(count, *refs):
    rows_in, weights_ref = refs[:count], refs[count]
    rows_ref, gate_up_ref, hidden_ref = refs[count + 1 : count + 4]
    out_refs, (held, sems) = refs[count + 4 : -2], refs[-2:]
    piece = hidden_ref.shape[1]
    cap = rows_in[0].shape[0]
    copies = fetch_weights(weights_ref, held, sems, piece)
    for copy in copies:
        copy.start()
    for s in range(count):
        rows_ref[s * cap : (s + 1) * cap, :] = rows_in[s][...]
    rows = rows_ref[...]
    copies[0].wait()
    gate = dot(rows, held[0])
    gate_up_ref[:, :piece] = gate
    copies[1].wait()
    up = dot(rows, held[1])
    gate_up_ref[:, piece:] = up
    hidden = (gate / (1.0 + jnp.exp(-gate)) * up).astype(BF)
    hidden_ref[...] = hidden
    copies[2].wait()
    out = dot_nt(hidden, held[2]).astype(BF)
    for s in range(count):
        out_refs[s][...] = out[s * cap : (s + 1) * cap, :]


def experts_forward(blocks, weights, piece):
    count = len(blocks)
    cap, width = blocks[0].shape
    rows = count * cap
    in_vmem = pl.BlockSpec(memory_space=pltpu.VMEM)
    return pl.pallas_call(
        functools.partial(experts_forward_kernel, count),
        in_specs=[in_vmem] * count + [pl.BlockSpec(memory_space=pltpu.HBM)],
        out_specs=[in_vmem] * (3 + count),
        out_shape=[
            jax.ShapeDtypeStruct((rows, width), BF),
            jax.ShapeDtypeStruct((rows, 2 * piece), F32),
            jax.ShapeDtypeStruct((rows, piece), BF),
        ]
        + [jax.ShapeDtypeStruct((cap, width), BF)] * count,
        scratch_shapes=[pltpu.VMEM((3, width, piece), BF), pltpu.SemaphoreType.DMA((3,))],
        compiler_params=pltpu.CompilerParams(vmem_limit_bytes=56 * 1024 * 1024),
        cost_estimate=pl.CostEstimate(flops=0, bytes_accessed=0, transcendentals=0),
    )(*blocks, weights)


def experts_backward_kernel(count, *refs):
    grads_in, gate_up_ref, weights_ref = refs[:count], refs[count], refs[count + 1]
    grads_ref, rows_ref = refs[count + 2 : count + 4]
    out_refs, (held, sems) = refs[count + 4 : -2], refs[-2:]
    piece = rows_ref.shape[1] // 2
    cap = grads_in[0].shape[0]
    copies = fetch_weights(weights_ref, held, sems, piece)
    for copy in (copies[2], copies[0], copies[1]):
        copy.start()
    for s in range(count):
        grads_ref[s * cap : (s + 1) * cap, :] = grads_in[s][...]
    copies[2].wait()
    grad_hidden = dot(grads_ref[...], held[2])
    gate = gate_up_ref[:, :piece]
    up = gate_up_ref[:, piece:]
    slope = 1.0 / (1.0 + jnp.exp(-gate))
    grad_gate = (grad_hidden * up * slope * (1.0 + gate * (1.0 - slope))).astype(BF)
    grad_up = (grad_hidden * gate * slope).astype(BF)
    rows_ref[:, :piece] = grad_gate
    rows_ref[:, piece:] = grad_up
    copies[0].wait()
    total = dot_nt(grad_gate, held[0])
    copies[1].wait()
    total = (total + dot_nt(grad_up, held[1])).astype(BF)
    for s in range(count):
        out_refs[s][...] = total[s * cap : (s + 1) * cap, :]


def experts_backward(blocks, gate_up, weights, piece):
    count = len(blocks)
    cap, width = blocks[0].shape
    rows = count * cap
    in_vmem = pl.BlockSpec(memory_space=pltpu.VMEM)
    return pl.pallas_call(
        functools.partial(experts_backward_kernel, count),
        in_specs=[in_vmem] * (count + 1) + [pl.BlockSpec(memory_space=pltpu.HBM)],
        out_specs=[in_vmem] * (2 + count),
        out_shape=[
            jax.ShapeDtypeStruct((rows, width), BF),
            jax.ShapeDtypeStruct((rows, 2 * piece), BF),
        ]
        + [jax.ShapeDtypeStruct((cap, width), BF)] * count,
        scratch_shapes=[pltpu.VMEM((3, width, piece), BF), pltpu.SemaphoreType.DMA((3,))],
        compiler_params=pltpu.CompilerParams(vmem_limit_bytes=56 * 1024 * 1024),
        cost_estimate=pl.CostEstimate(flops=0, bytes_accessed=0, transcendentals=0),
    )(*blocks, gate_up, weights)


def kv_pair_kernel(heads, chips, *refs):
    near, there, outs = refs[:heads], refs[heads : 2 * heads], refs[2 * heads :]
    for m in range(chips):
        for g in range(heads):
            total = near[g][m].astype(F32) + there[g][m].astype(F32)
            outs[m][:, g * 2 * HD : (g + 1) * 2 * HD] = total.astype(outs[m].dtype)


def kv_pair_sums(near, there):
    heads, (chips, rows, cols) = len(near), near[0].shape
    in_vmem = pl.BlockSpec(memory_space=pltpu.VMEM)
    out = jax.ShapeDtypeStruct((rows, heads * cols), BF)
    return pl.pallas_call(
        functools.partial(kv_pair_kernel, heads, chips),
        in_specs=[in_vmem] * (2 * heads),
        out_specs=[in_vmem] * chips,
        out_shape=[jax.ShapeDtypeStruct((rows, heads * cols), F32)] + [out] * (chips - 1),
        compiler_params=pltpu.CompilerParams(vmem_limit_bytes=20 * 1024 * 1024),
        cost_estimate=pl.CostEstimate(flops=0, bytes_accessed=0, transcendentals=0),
    )(*near, *there)


def head_columns_kernel(heads, chips, *refs):
    queries, sums = refs[:heads], refs[heads : heads + chips]
    factor_ref, ride_ref, sent_ref, columns_ref = refs[heads + chips :]
    query = jnp.concatenate([each[...] for each in queries], axis=1)
    keyval = sums[0][...]
    for each in sums[1:]:
        keyval = keyval + each[...].astype(F32)
    both = jnp.concatenate([query, keyval], axis=1)
    rows, cols = both.shape
    sent_ref[...] = both.astype(BF)
    columns_ref[:rows, :cols] = (both * factor_ref[...]).astype(BF)
    columns_ref[:rows, cols:] = jnp.zeros((rows, LANES), BF)
    columns_ref[rows:, :cols] = jnp.zeros((ride_ref.shape[0], cols), BF)
    columns_ref[rows:, cols:] = ride_ref[...]


def head_columns(queries, sums, factor, ride):
    rows = sums[0].shape[0]
    cols = sum(each.shape[1] for each in queries) + sums[0].shape[1]
    if cols % LANES:
        both = jnp.concatenate(list(queries) + [total_of(sums)], axis=1)
        scaled = jnp.pad((both * factor).astype(BF), ((0, 0), (0, LANES)))
        return both.astype(BF), jnp.concatenate([scaled, jnp.pad(ride, ((0, 0), (cols, 0)))])
    in_vmem = pl.BlockSpec(memory_space=pltpu.VMEM)
    return pl.pallas_call(
        functools.partial(head_columns_kernel, len(queries), len(sums)),
        in_specs=[in_vmem] * (len(queries) + len(sums) + 2),
        out_specs=[in_vmem] * 2,
        out_shape=[
            jax.ShapeDtypeStruct((rows, cols), BF),
            jax.ShapeDtypeStruct((rows + ride.shape[0], cols + LANES), BF),
        ],
        compiler_params=pltpu.CompilerParams(vmem_limit_bytes=20 * 1024 * 1024),
        cost_estimate=pl.CostEstimate(flops=0, bytes_accessed=0, transcendentals=0),
    )(*queries, *sums, factor, ride)


def two_parts(value):
    high = value.astype(BF)
    return high, (value - high.astype(F32)).astype(BF)


def mark_kernel(seed_ref, out_ref):
    out_ref[...] = seed_ref[...]


def mark(*others):
    seed = after(jnp.zeros((8, LANES), F32), *others)
    return pl.pallas_call(
        mark_kernel,
        out_shape=jax.ShapeDtypeStruct((8, LANES), F32),
        cost_estimate=pl.CostEstimate(flops=10**12, bytes_accessed=8192, transcendentals=0),
    )(seed)


def by_rows(array):
    return with_layout_constraint(array, Layout(major_to_minor=tuple(range(array.ndim))))


def after(values, *others):
    return lax.optimization_barrier((values, others))[0]


def root(values):
    return lax.rsqrt(jnp.mean(values * values, axis=-1, keepdims=True) + EPSILON)


def root_back(values, factor, grad_scaled):
    inner = jnp.mean(grad_scaled * values, axis=-1, keepdims=True)
    return factor * grad_scaled - values * (factor * factor * factor * inner)


def place_gate_up_kernel(count, place_ref, *refs):
    blocks = refs[: 2 * count - 1]
    weight_ref, gain_ref, out_ref, sums_ref, base = refs[2 * count - 1 :]
    offset = place_ref[0] - pl.program_id(1)

    for s in range(2 * count - 1):

        @pl.when(offset == (s if s < count else count - 1 - s))
        def _(s=s):
            base[...] = blocks[s][...].astype(F32)

    @pl.when((pl.program_id(0) == 0) & (pl.program_id(1) == 0))
    def _():
        sums_ref[...] = jnp.zeros_like(sums_ref)

    values = base[...]
    out_ref[0] = values * gain_ref[...]
    product = jnp.sum(weight_ref[0].astype(F32) * values, axis=1, keepdims=True)
    sums_ref[...] += jnp.broadcast_to(product, sums_ref.shape)


def place_gate_up(steps, weight, gain, place):
    experts, part, both = weight.shape
    count = len(steps)
    split = count // experts
    if split == 1:
        tile = math.gcd(both, 1024)
        blocks = [steps[0][0]] + [each[0] for each in steps[1:]] + [each[1] for each in steps[1:]]
        block = pl.BlockSpec((part, tile), lambda t, e: (0, t))
        out, sums = pl.pallas_call(
            functools.partial(place_gate_up_kernel, count),
            grid=(both // tile, experts),
            in_specs=[pl.BlockSpec(memory_space=pltpu.SMEM)]
            + [block] * len(blocks)
            + [
                pl.BlockSpec((1, part, tile), lambda t, e: (e, 0, t)),
                pl.BlockSpec((part, 1), lambda t, e: (0, 0)),
            ],
            out_specs=[
                pl.BlockSpec((1, part, tile), lambda t, e: (e, 0, t)),
                pl.BlockSpec((part, LANES), lambda t, e: (0, 0)),
            ],
            out_shape=[
                jax.ShapeDtypeStruct(weight.shape, F32),
                jax.ShapeDtypeStruct((part, LANES), F32),
            ],
            scratch_shapes=[pltpu.VMEM((part, tile), F32)],
            compiler_params=pltpu.CompilerParams(vmem_limit_bytes=28 * 1024 * 1024),
            cost_estimate=pl.CostEstimate(flops=0, bytes_accessed=0, transcendentals=0),
        )(place.astype(jnp.int32).reshape(1), *blocks, weight, gain)
        return out, sums[:, 0]
    blocks = [steps[0][0]] + [
        jnp.where(place >= s, steps[s][0], steps[count - s][1]) for s in range(1, count)
    ]
    base = (
        from_relative(blocks, place)
        .reshape(experts, split, part, 2, both // (2 * split))
        .transpose(0, 2, 3, 1, 4)
        .reshape(experts, part, both)
        .astype(F32)
    )
    return base * gain, jnp.sum(weight.astype(F32) * base, axis=(0, 2))


def place_kernel(count, q_cols, kv_cols, place_ref, *refs):
    blocks, outs = refs[:count], refs[count : 2 * count]
    w_query_ref, w_keyval_ref, gain_ref, query_ref, keyval_ref, out_ref, base_ref, sums_ref = refs[
        2 * count :
    ]
    gain = gain_ref[...]
    base = jnp.zeros_like(gain)
    sums = jnp.zeros(sums_ref.shape, F32)
    for s in range(count):
        owner = lax.rem(place_ref[0] + (count - s), count)
        q_at = pl.ds(pl.multiple_of(owner * q_cols, LANES), q_cols)
        kv_at = pl.ds(pl.multiple_of(owner * kv_cols, LANES), kv_cols)
        query = blocks[s][:, :q_cols].astype(F32)
        keyval = blocks[s][:, q_cols : q_cols + kv_cols].astype(F32)
        start = q_cols + kv_cols
        sums = sums + blocks[s][:, start : start + LANES].astype(F32)
        out_ref[:, q_at] = outs[s][...].astype(F32)
        base = base + jnp.sum(w_query_ref[:, q_at].astype(F32) * query, axis=1, keepdims=True)
        base = base + jnp.sum(w_keyval_ref[:, kv_at].astype(F32) * keyval, axis=1, keepdims=True)
        query_ref[:, q_at] = query * gain
        keyval_ref[:, kv_at] = keyval * gain
    base_ref[...] = jnp.broadcast_to(base, base_ref.shape)
    sums_ref[...] = sums


def place_heads(blocks, outs, place, w_query, w_keyval, gain, q_cols, kv_cols):
    count = len(blocks)
    part = w_query.shape[0]
    start = q_cols + kv_cols
    if q_cols % LANES == 0 and kv_cols % LANES == 0:
        wide = jax.ShapeDtypeStruct((part, count * q_cols), F32)
        narrow = jax.ShapeDtypeStruct((part, count * kv_cols), F32)
        lanes = jax.ShapeDtypeStruct((part, LANES), F32)
        in_vmem = pl.BlockSpec(memory_space=pltpu.VMEM)
        query, keyval, out, base, sums = pl.pallas_call(
            functools.partial(place_kernel, count, q_cols, kv_cols),
            in_specs=[pl.BlockSpec(memory_space=pltpu.SMEM)] + [in_vmem] * (2 * count + 3),
            out_specs=[in_vmem] * 5,
            out_shape=[wide, narrow, wide, lanes, lanes],
            compiler_params=pltpu.CompilerParams(vmem_limit_bytes=24 * 1024 * 1024),
            cost_estimate=pl.CostEstimate(flops=0, bytes_accessed=0, transcendentals=0),
        )(place.astype(jnp.int32).reshape(1), *blocks, *outs, w_query, w_keyval, gain)
        return query, keyval, out, base[:, 0], sums
    blocks = from_relative(blocks, place).astype(F32)
    outs = from_relative(outs, place).astype(F32)

    def columns(begin, end):
        return blocks[:, :, begin:end].transpose(1, 0, 2).reshape(part, count * (end - begin))

    query, keyval = columns(0, q_cols), columns(q_cols, start)
    base = jnp.sum(w_query.astype(F32) * query, axis=1) + jnp.sum(
        w_keyval.astype(F32) * keyval, axis=1
    )
    sums = jnp.sum(blocks[:, :, start : start + LANES], axis=0)
    out = outs.transpose(1, 0, 2).reshape(part, count * q_cols)
    return query * gain, keyval * gain, out, base, sums


def local(
    tokens,
    teacher,
    valid,
    routes,
    slots,
    gain_attn,
    w_query,
    w_keyval,
    w_out,
    gain_ffn,
    w_router,
    w_gate_up,
    w_down,
):
    seqs = lax.axis_size("seq")
    shards = lax.axis_size("fsdp")
    z = lax.axis_index("seq")
    shard = lax.axis_index("fsdp")
    rows, width = tokens.shape
    groups = HEADS // KVH
    local_kv = KVH // seqs
    q_cols = local_kv * groups * HD
    kv_cols = local_kv * 2 * HD
    local_rows = rows * seqs
    seq_len = local_rows * shards
    experts, part, both = w_gate_up.shape
    units = both // 2
    split = seqs // experts
    piece = units // split
    expert = z // split
    fraction = z % split
    scale = HD ** (-0.5)

    gain_one = gain_attn.astype(F32)[:, None]
    gain_two = gain_ffn.astype(F32)[:, None]
    heads_shard = jnp.concatenate(
        [
            lax.dynamic_slice_in_dim(w_query, z * q_cols, q_cols, 1),
            lax.dynamic_slice_in_dim(w_keyval, z * kv_cols, kv_cols, 1),
        ],
        axis=1,
    )
    heads_shard = (heads_shard.astype(F32) * gain_one).astype(BF)
    heads_full = lax.all_gather(heads_shard, "fsdp", axis=0, tiled=True)
    valid_row = jnp.pad(valid.astype(BF).reshape(1, rows), ((0, 7), (0, width - rows)))
    token_rows = jnp.concatenate([tokens, valid_row], axis=0)
    token_mark = mark(token_rows)
    token_blocks = after(send_out([token_rows] * seqs, seqs), token_mark)

    valid_local = from_relative([each[rows : rows + 1, :rows] for each in token_blocks], z)
    projected = []
    for block in token_blocks:
        projected.append(dot(block[:rows], heads_full) * root(block[:rows].astype(F32)))
    projected = from_relative([each.astype(BF) for each in projected], z)
    projected = projected.reshape(local_rows, q_cols + kv_cols)
    head_queries = projected[:, :q_cols] * jnp.asarray(scale, BF)

    valid_rows_kv = local_rows // kv_cols
    payload = jnp.concatenate(
        [
            projected[:, q_cols:],
            valid_local.reshape(valid_rows_kv, kv_cols),
            jnp.zeros((16 - valid_rows_kv, kv_cols), BF),
        ],
        axis=0,
    )
    kv_blocks = gather_shards(payload, shards)
    late_query, late_keyval, late_router, late_gate_up, late_down = after(
        (w_query, w_keyval, w_router, w_gate_up, w_down), token_mark
    )
    out_full = lax.all_gather(w_out, "fsdp", axis=1, tiled=True)
    own_expert = take(late_gate_up, expert, 0)
    gate_shard = lax.dynamic_slice_in_dim(own_expert, fraction * piece, piece, 1)
    up_shard = lax.dynamic_slice_in_dim(own_expert, units + fraction * piece, piece, 1)
    down_shard = lax.dynamic_slice_in_dim(take(late_down, expert, 0), fraction * piece, piece, 0).T
    router_shard = jnp.pad((late_router.astype(F32) * gain_two).astype(BF), ((0, 0), (0, LANES - experts)))
    expert_shard = jnp.concatenate(
        [
            (gate_shard.astype(F32) * gain_two).astype(BF),
            (up_shard.astype(F32) * gain_two).astype(BF),
            down_shard,
            router_shard,
        ],
        axis=1,
    )
    expert_full = lax.all_gather(expert_shard, "fsdp", axis=0, tiled=True)
    router_full = expert_full[:, 3 * piece :]
    attn_shard = jnp.concatenate(
        [
            each
            for s in range(seqs)
            for each in (
                late_query[:, s * q_cols : (s + 1) * q_cols],
                late_keyval[:, s * kv_cols : (s + 1) * kv_cols],
            )
        ],
        axis=1,
    )
    attn_full = lax.all_gather(
        (attn_shard.astype(F32) * gain_one).astype(BF), "fsdp", axis=0, tiled=True
    )
    order = jnp.asarray(
        [2 * m for m in range(shards // 2)] + [2 * m + 1 for m in range(shards // 2)], jnp.int32
    )
    valid_all = jnp.stack(
        [
            each[local_rows : local_rows + valid_rows_kv].reshape(seqs, rows)
            for each in kv_blocks
        ],
        axis=1,
    ).astype(F32)
    valid_count = jnp.sum(valid_all)
    bias = jnp.where(valid_all > 0, 0.0, FLOOR_SCORE)
    earlier = ((order ^ shard) < shard) | (order == 0)
    bias_same = jnp.where(earlier[None, :, None], bias, FLOOR_SCORE)
    bias = jnp.concatenate([bias, bias_same]).reshape(2 * seqs, 1, shards * rows)
    attended_low, exact, lse = flash_forward(
        head_queries, kv_blocks, bias, seqs, rows, local_kv, groups
    )
    attended = lax.all_to_all(attended_low, "seq", split_axis=0, concat_axis=1, tiled=True)

    inputs = tokens.astype(F32)
    residual = inputs + dot(attended, out_full)
    factor_two = root(residual)
    normed_two = (residual * factor_two).astype(BF)
    logits = dot(normed_two, router_full)[:, :experts]
    expert_ids = jnp.arange(experts, dtype=jnp.int32)
    picked = (routes[:, :, None] == expert_ids).astype(F32)
    chosen = jnp.sum(picked * logits[:, None, :], axis=-1)
    gating = jax.nn.softmax(chosen, axis=-1)
    owners = ((jnp.arange(seqs, dtype=jnp.int32) + z) % seqs) // split
    to_owner = routes[:, :, None] == owners
    slot_hot = slots[:, :, None] == jnp.arange(CAP, dtype=jnp.int32)
    placed = (to_owner[:, :, :, None] & slot_hot[:, :, None, :]).astype(BF)
    placed = placed.reshape(rows, 2, seqs * CAP)
    dispatch = placed[:, 0] + placed[:, 1]
    placed_pairs = jnp.concatenate([placed[:, 0], placed[:, 1]], axis=0)
    sent_rows = dot_tn(dispatch, normed_two).astype(BF)
    kv_all = jnp.stack(after(kv_blocks, sent_rows))
    sent_rows = sent_rows.reshape(seqs, CAP, width)
    expert_rows, gate_up, hidden, *expert_out = experts_forward(
        send_out([sent_rows[s] for s in range(seqs)], seqs), expert_full, piece
    )
    returned = jnp.concatenate(after(send_back(expert_out, seqs), kv_all))
    selected = dot(placed_pairs, returned).reshape(2, rows, width)
    mixed_exact = residual + gating[:, :1] * selected[0] + gating[:, 1:] * selected[1]
    valid_rows = valid.astype(F32)
    errors = (mixed_exact - teacher.astype(F32)) * valid_rows[:, None]
    squares = jnp.sum(errors * errors)
    loss_scale = width * seq_len // 8
    grad_mixed = errors * (2.0 * loss_scale / (width * valid_count))

    grad_gating = jnp.stack(
        [jnp.sum(selected[0] * grad_mixed, axis=-1), jnp.sum(selected[1] * grad_mixed, axis=-1)],
        axis=1,
    )
    grad_chosen = gating * (grad_gating - jnp.sum(gating * grad_gating, axis=-1, keepdims=True))
    grad_logits = jnp.sum(grad_chosen[:, :, None] * picked, axis=1).astype(BF)
    grad_logits = jnp.pad(grad_logits, ((0, 0), (0, LANES - experts)))
    weighted = jnp.concatenate(
        [(gating[:, :1] * grad_mixed).astype(BF), (gating[:, 1:] * grad_mixed).astype(BF)], axis=0
    )
    sent_grads = dot_tn(placed_pairs, weighted).astype(BF).reshape(seqs, CAP, width)
    grad_out_rows = send_out([sent_grads[s] for s in range(seqs)], seqs)
    grad_out_rows = after(grad_out_rows, attn_full, grad_logits)
    grad_expert_out, grad_gate_up_rows, *grad_rows = experts_backward(
        grad_out_rows, gate_up, expert_full, piece
    )
    grad_returned = send_back(grad_rows, seqs)
    tokens_local = from_relative(
        [each[:rows] for each in after(token_blocks, grad_rows)], z
    ).reshape(local_rows, width)
    factor_local = root(tokens_local.astype(F32))
    ride_rows = jnp.concatenate([normed_two, jnp.ones((16, width), BF)], axis=0)
    product_rows = jnp.concatenate([tokens_local, ride_rows], axis=0)
    high, low = two_parts(squares)
    lane = jnp.arange(LANES, dtype=jnp.int32)[None, :]
    marks = jnp.where(lane == experts + 2 * (shard % 2), high, 0) + jnp.where(
        lane == experts + 1 + 2 * (shard % 2), low, 0
    )
    ride_columns = jnp.concatenate(
        [grad_logits, marks.astype(BF), jnp.zeros((15, LANES), BF)], axis=0
    )
    held_out, held_hidden = after((grad_expert_out, hidden), grad_rows)
    down_far, down_near = split_product(held_out, held_hidden, shard, shards)
    grad_down_sums = pair_sums(down_near, hop(down_far, shards, 1), shard)
    held_rows, held_gate_up = after((expert_rows, grad_gate_up_rows), grad_rows)
    gate_up_far, gate_up_near = split_product(held_rows, held_gate_up, shard, shards)
    grad_gate_up_sums = pair_sums(gate_up_near, hop(gate_up_far, shards, 1), shard)
    grad_down_blocks = send_chips(grad_down_sums, shards)
    grad_returned = jnp.concatenate(after(grad_returned, grad_down_sums, product_rows, ride_columns, factor_local))
    grad_normed_two = dot(dispatch, grad_returned) + dot_nt(grad_logits, router_full)
    grad_residual = grad_mixed + root_back(residual, factor_two, grad_normed_two)
    grad_branch = grad_residual.astype(BF)
    grad_attended = dot_nt(after(grad_branch, grad_gate_up_sums), out_full).astype(BF)
    head_grad = lax.all_to_all(grad_attended, "seq", split_axis=1, concat_axis=0, tiled=True)
    grad_gate_up_blocks = send_chips(grad_gate_up_sums, shards)
    grad_down_shard = total_of(after(grad_down_blocks, grad_attended)).astype(BF)
    grad_down = lax.all_gather(grad_down_shard, "seq", axis=0, tiled=False)

    out_far, out_near = split_product(
        after(grad_branch, grad_attended), attended, shard, shards
    )
    grad_q, near, far = [], [], []
    held = after(head_grad, grad_down_shard)
    for g in range(local_kv):
        part_q, near_kv, far_kv = flash_backward(
            head_queries, kv_all, bias, held, exact, lse, seqs, rows, g, groups
        )
        if g == 0:
            grad_gate_up_blocks = after(grad_gate_up_blocks, part_q)
            grad_gate_up_shard = total_of(grad_gate_up_blocks).astype(BF)
            steps = [(grad_gate_up_shard, grad_gate_up_shard)]
            steps.append(relay_step(steps[0], seqs))
            out_there = hop(after(out_far, head_grad), shards, 1)
        grad_q.append(part_q)
        near.append(near_kv)
        far.append(far_kv)
        held = after(head_grad, grad_gate_up_shard, out_there)
    steps[1] = after(steps[1], part_q)
    steps.append(relay_step(steps[1], seqs))
    far = after(far, steps[1], grad_down)
    pairs = kv_pair_sums(near, [hop(each, shards, 1) for each in far])
    out_pair = out_near.astype(F32) + after(out_there, pairs).astype(F32)
    out_sums = lax.all_to_all(
        out_pair.astype(BF),
        "fsdp",
        split_axis=0,
        concat_axis=0,
        tiled=True,
        axis_index_groups=[list(range(core, shards, 2)) for core in range(2)],
    )
    sent_grads, product_columns = head_columns(
        grad_q, after(send_chips(pairs, shards), out_pair, steps[2]), factor_local, ride_columns
    )
    steps[2] = after(steps[2], product_columns)
    while len(steps) < seqs:
        steps.append(relay_step(steps[-1], seqs))
    token_grads = lax.all_to_all(sent_grads, "seq", split_axis=0, concat_axis=1, tiled=True)

    head_cols = q_cols + kv_cols
    head_far, head_near = split_product(product_rows, product_columns, shard, shards)
    head_sums = pair_sums(head_near, hop(head_far, shards, 1), shard)
    head_blocks = send_chips(head_sums, shards)
    head_part = total_of(after(head_blocks, steps[3]))
    grad_normed = dot_nt(after(token_grads, head_part), attn_full)
    grad_tokens = grad_residual + root_back(inputs, root(inputs), grad_normed)
    base_cols = head_cols + experts
    plane_high, plane_low = two_parts(
        jnp.sum(head_part[:1, base_cols : base_cols + 4], axis=1, keepdims=True)
    )
    lanes = lax.broadcasted_iota(jnp.int32, head_part.shape, 1)
    head_part = jnp.where(
        lanes == base_cols,
        plane_high.astype(F32),
        jnp.where(lanes == base_cols + 1, plane_low.astype(F32), head_part),
    )
    head_part = by_rows(head_part.astype(BF))
    head_last = [by_rows(each) for each in send_out([head_part] * seqs, seqs)]
    out_part = jnp.sum(after(out_sums, head_sums).astype(F32), axis=0).astype(BF)
    out_parts = lax.all_to_all(
        out_part.reshape(part, seqs, q_cols), "seq", split_axis=1, concat_axis=1, tiled=True
    )
    out_own = by_rows(jnp.sum(out_parts.astype(F32), axis=1).astype(BF))
    grad_gate_up, grad_gain_ffn = place_gate_up(after(steps, head_part), w_gate_up, gain_two, z)
    out_own = after(out_own, grad_gate_up)
    out_last = [by_rows(each) for each in send_out([out_own] * seqs, seqs)]
    grad_query, grad_keyval, grad_out, grad_gain_attn, sums = place_heads(
        head_last, out_last, z, w_query, w_keyval, gain_one, q_cols, kv_cols
    )
    loss_value = jnp.sum(sums[0, experts : experts + 2]) / (width * valid_count)
    grad_router_base = sums[:, :experts]
    grad_down = (
        after(grad_down, head_part).reshape(experts, split, part, piece)
        .transpose(0, 1, 3, 2)
        .reshape(experts, units, part)
        .astype(F32)
    )
    grad_gain_ffn = grad_gain_ffn + jnp.sum(w_router.astype(F32) * grad_router_base, axis=1)
    return (
        mixed_exact.astype(BF),
        loss_value,
        grad_tokens,
        grad_gain_attn,
        grad_query,
        grad_keyval,
        grad_out.T,
        grad_gain_ffn,
        grad_router_base * gain_two,
        grad_gate_up,
        grad_down,
    )


def solution(mesh):
    return jax.shard_map(
        local,
        mesh=mesh,
        in_specs=(
            P(("seq", "fsdp"), None),
            P(("seq", "fsdp"), None),
            P(("seq", "fsdp")),
            P(("seq", "fsdp"), None),
            P(("seq", "fsdp"), None),
            P("fsdp"),
            P("fsdp", None),
            P("fsdp", None),
            P(None, "fsdp"),
            P("fsdp"),
            P("fsdp", None),
            P(None, "fsdp", None),
            P(None, None, "fsdp"),
        ),
        out_specs=(
            P(("seq", "fsdp"), None),
            P(),
            P(("seq", "fsdp"), None),
            P("fsdp"),
            P("fsdp", None),
            P("fsdp", None),
            P(None, "fsdp"),
            P("fsdp"),
            P("fsdp", None),
            P(None, "fsdp", None),
            P(None, None, "fsdp"),
        ),
        check_vma=False,
    )
```

```python
import functools
import math

import jax
import jax.numpy as jnp
from jax import lax
from jax.experimental import pallas as pl
from jax.experimental.layout import Layout, with_layout_constraint
from jax.experimental.pallas import tpu as pltpu
from jax.sharding import PartitionSpec as P

HEADS = 24
KVH = 8
HD = 64
CAP = 96
LANES = 128
EPSILON = 1e-06
FLOOR_SCORE = -1e30
BF = jnp.bfloat16
F32 = jnp.float32


def dot(a, b):
    return jnp.dot(a, b, preferred_element_type=F32)


def dot_nt(a, b):
    return lax.dot_general(a, b, (((1,), (1,)), ((), ())), preferred_element_type=F32)


def dot_tn(a, b):
    return lax.dot_general(a, b, (((0,), (0,)), ((), ())), preferred_element_type=F32)


def own_mask(valid_row, rows):
    i = lax.broadcasted_iota(jnp.int32, (rows, rows), 0)
    j = lax.broadcasted_iota(jnp.int32, (rows, rows), 1)
    return jnp.where(j == i, 0.0, jnp.where(j < i, valid_row, FLOOR_SCORE))


def key_chunk(kv_refs, zk, rows, g):
    return jnp.concatenate(
        [ref[pl.ds(zk * rows, rows), pl.ds(g * 2 * HD, 2 * HD)] for ref in kv_refs], axis=0
    )


def forward_kernel(shards, seqs, rows, local_kv, groups, *refs):
    kv_refs = refs[:shards]
    q_ref, bias_ref, low_ref, lse_ref, acc_ref, max_ref = refs[shards:]
    zq = pl.program_id(0)
    stack = groups * rows
    zeros = jnp.zeros((rows, HD), BF)
    half = lax.broadcasted_iota(jnp.int32, (1, 2 * HD), 1) < HD

    def queries(g):
        parts = []
        for h in range(groups):
            start = (g * groups + h) * HD
            parts.append(jnp.concatenate([q_ref[:, start : start + HD], zeros], axis=1))
        return jnp.concatenate(parts, axis=0)

    def chunk(g, zk, scores):
        first = scores is None
        keys = key_chunk(kv_refs, zk, rows, g)
        raw = dot_nt(queries(g), keys)
        if first:
            row = bias_ref[seqs + zk]
            mask = own_mask(row[:, :rows], rows)
            mask = jnp.concatenate([mask] * groups, axis=0)
            masked = jnp.concatenate([raw[:, :rows] + mask, raw[:, rows:] + row[:, rows:]], axis=1)
            new_max = jnp.max(masked, axis=1, keepdims=True)
        else:
            masked = raw + bias_ref[zk]
            new_max = jnp.maximum(max_ref[g][:, :1], jnp.max(masked, axis=1, keepdims=True))
        terms = jnp.exp(masked - new_max).astype(BF)
        ones_values = jnp.where(half, jnp.ones_like(keys), keys)
        part = dot(terms, ones_values)
        if first:
            acc_ref[g] = part
        else:
            acc_ref[g] = acc_ref[g] * jnp.exp(max_ref[g][:, :1] - new_max) + part
        max_ref[g] = jnp.broadcast_to(new_max, (stack, 2 * HD))

    for g in range(local_kv):
        chunk(g, zq, None)

    @pl.loop(0, zq)
    def _(zk):
        for g in range(local_kv):
            chunk(g, zk, True)

    exact_parts, lse_parts = [], []
    for g in range(local_kv):
        acc = acc_ref[g]
        total = acc[:, :HD]
        exact = acc[:, HD:] / total
        lse = max_ref[g][:, :HD] + jnp.log(total)
        for h in range(groups):
            exact_parts.append(exact[h * rows : (h + 1) * rows])
            lse_parts.append(lse[h * rows : (h + 1) * rows])
    low_ref[...] = jnp.concatenate(exact_parts, axis=1).astype(BF)
    lse_ref[...] = jnp.concatenate(lse_parts, axis=1)


def flash_forward(q, kv_blocks, bias, seqs, rows, local_kv, groups):
    shards = len(kv_blocks)
    q_cols = q.shape[1]
    kv_spec = pl.BlockSpec(kv_blocks[0].shape, lambda i: (0, 0))
    q_spec = pl.BlockSpec((rows, q_cols), lambda i: (i, 0))
    stack = groups * rows
    out = jax.ShapeDtypeStruct((seqs * rows, q_cols), F32)
    return pl.pallas_call(
        functools.partial(forward_kernel, shards, seqs, rows, local_kv, groups),
        grid=(seqs,),
        in_specs=[kv_spec] * shards + [q_spec, pl.BlockSpec(bias.shape, lambda i: (0, 0, 0))],
        out_specs=[q_spec] * 2,
        out_shape=[jax.ShapeDtypeStruct((seqs * rows, q_cols), BF), out],
        scratch_shapes=[
            pltpu.VMEM((local_kv, stack, 2 * HD), F32),
            pltpu.VMEM((local_kv, stack, 2 * HD), F32),
        ],
        compiler_params=pltpu.CompilerParams(vmem_limit_bytes=24 * 1024 * 1024),
        cost_estimate=pl.CostEstimate(
            flops=0,
            bytes_accessed=0,
            transcendentals=0,
        ),
    )(*kv_blocks, q, bias)


def backward_kernel(shards, seqs, rows, g, groups, *refs):
    kv_refs = [refs[0].at[p] for p in range(shards)]
    (
        q_ref, bias_ref, grad_ref, low_ref, lse_ref, grad_q_ref, near_ref, far_ref,
        pair_ref, pair_t_ref, lse_wide, delta_wide, acc_q, acc_kv,
    ) = refs[1:]
    zk = pl.program_id(0)
    stack = groups * rows
    zeros = jnp.zeros((rows, HD), BF)

    @pl.when(zk == 0)
    def _():
        acc_q[...] = jnp.zeros_like(acc_q)

        @pl.loop(0, seqs)
        def _(zq):
            here = pl.ds(zq * rows, rows)
            tops, bottoms = [], []
            for h in range(groups):
                cols = slice((g * groups + h) * HD, (g * groups + h + 1) * HD)
                grad = grad_ref[here, cols]
                tops.append(jnp.concatenate([q_ref[here, cols], zeros], axis=1))
                bottoms.append(jnp.concatenate([zeros, grad], axis=1))
                delta = jnp.sum(grad.astype(F32) * low_ref[here, cols].astype(F32), axis=1, keepdims=True)
                part = slice(h * rows, (h + 1) * rows)
                delta_wide[zq, part] = jnp.broadcast_to(delta, (rows, 2 * HD))
                lse_wide[zq, part] = jnp.broadcast_to(lse_ref[here, cols][:, :1], (rows, 2 * HD))
            pair = jnp.concatenate(tops + bottoms, axis=0)
            pair_ref[zq] = pair
            pair_t_ref[zq] = pair.astype(F32).T.astype(BF)

    def chunk(zq, first):
        keys = key_chunk(kv_refs, zk, rows, g)
        both = dot_nt(pair_ref[zq], keys)
        raw, products = both[:stack], both[stack:]
        if first:
            row = bias_ref[seqs + zk]
            mask = own_mask(row[:, :rows], rows)
            mask = jnp.concatenate([mask] * groups, axis=0)
            masked = jnp.concatenate([raw[:, :rows] + mask, raw[:, rows:] + row[:, rows:]], axis=1)
        else:
            masked = raw + bias_ref[zk]
        weights = jnp.exp(masked - lse_wide[zq][:, :1])
        grads = (weights * (products - delta_wide[zq][:, :1])).astype(BF)
        acc_q[zq] += dot(grads, keys)
        part = dot(pair_t_ref[zq], jnp.concatenate([grads, weights.astype(BF)], axis=0))
        if first:
            acc_kv[...] = part
        else:
            acc_kv[...] += part

    chunk(zk, True)

    @pl.loop(zk + 1, seqs)
    def _(zq):
        chunk(zq, False)

    for p in range(shards):
        target = near_ref if p < shards // 2 else far_ref
        target[p % (shards // 2)] = acc_kv[:, p * rows : (p + 1) * rows].T.astype(BF)

    @pl.when(zk == seqs - 1)
    def _():
        @pl.loop(0, seqs)
        def _(zq):
            total = acc_q[zq]
            parts = [total[h * rows : (h + 1) * rows, :HD] for h in range(groups)]
            grad_q_ref[pl.ds(zq * rows, rows), :] = jnp.concatenate(parts, axis=1) * HD ** (-0.5)


def flash_backward(q, kv_all, bias, grad, low, lse, seqs, rows, g, groups):
    shards = kv_all.shape[0]
    q_cols = q.shape[1]
    stack = groups * rows
    kv_spec = pl.BlockSpec(kv_all.shape, lambda i: (0, 0, 0))
    whole = pl.BlockSpec((seqs * rows, q_cols), lambda i: (0, 0))
    grad_q_shape = (seqs * rows, groups * HD)
    out_spec = pl.BlockSpec((shards // 2, rows, 2 * HD), lambda i: (0, i, 0))
    out = jax.ShapeDtypeStruct((shards // 2, seqs * rows, 2 * HD), BF)
    return pl.pallas_call(
        functools.partial(backward_kernel, shards, seqs, rows, g, groups),
        grid=(seqs,),
        in_specs=[kv_spec]
        + [whole, pl.BlockSpec(bias.shape, lambda i: (0, 0, 0)), whole, whole, whole],
        out_specs=[pl.BlockSpec(grad_q_shape, lambda i: (0, 0)), out_spec, out_spec],
        out_shape=[jax.ShapeDtypeStruct(grad_q_shape, F32), out, out],
        scratch_shapes=[
            pltpu.VMEM((seqs, 2 * stack, 2 * HD), BF),
            pltpu.VMEM((seqs, 2 * HD, 2 * stack), BF),
            pltpu.VMEM((seqs, stack, 2 * HD), F32),
            pltpu.VMEM((seqs, stack, 2 * HD), F32),
            pltpu.VMEM((seqs, stack, 2 * HD), F32),
            pltpu.VMEM((2 * HD, shards * rows), F32),
        ],
        compiler_params=pltpu.CompilerParams(vmem_limit_bytes=28 * 1024 * 1024),
        cost_estimate=pl.CostEstimate(
            flops=0 if g else 10**12,
            bytes_accessed=0,
            transcendentals=0,
        ),
    )(kv_all, q, bias, grad, low, lse)


def shift(block, count, step):
    return lax.ppermute(block, "seq", [(i, (i + step) % count) for i in range(count)])


def send_out(blocks, count):
    return [blocks[0]] + [shift(blocks[s], count, s) for s in range(1, count)]


def send_back(blocks, count):
    return [blocks[0]] + [shift(blocks[s], count, count - s) for s in range(1, count)]


def relay_step(blocks, count):
    up, down = blocks
    return (
        lax.ppermute(up, "seq", [(i, i + 1) for i in range(count - 1)]),
        lax.ppermute(down, "seq", [(i + 1, i) for i in range(count - 1)]),
    )


def from_relative(blocks, place):
    count = len(blocks)
    rising = jnp.stack([blocks[-s % count] for s in range(count)])
    return lax.dynamic_slice_in_dim(jnp.concatenate([rising, rising]), count - place, count, 0)


def hop(block, count, mask):
    return lax.ppermute(block, "fsdp", [(i, i ^ mask) for i in range(count)])


def gather_shards(block, count):
    near = [block] + [hop(block, count, 2 * m) for m in range(1, count // 2)]
    return near + [hop(each, count, 1) for each in near]


def send_chips(parts, count):
    return [parts[0]] + [hop(parts[m], count, 2 * m) for m in range(1, count // 2)]


def total_of(blocks):
    total = blocks[0].astype(F32)
    for each in blocks[1:]:
        total = total + each.astype(F32)
    return total


def take(array, index, axis):
    return lax.dynamic_index_in_dim(array, index, axis, keepdims=False)


def product_kernel(core_ref, lhs_ref, rhs_ref, far_ref, near_ref):
    part = lhs_ref.shape[1] // 2
    rhs = rhs_ref[...]
    first = dot_tn(lhs_ref[:, :part], rhs).astype(BF)
    second = dot_tn(lhs_ref[:, part:], rhs).astype(BF)
    core = core_ref[0]

    @pl.when(core == 0)
    def _():
        near_ref[0] = first
        far_ref[0] = second

    @pl.when(core != 0)
    def _():
        near_ref[0] = second
        far_ref[0] = first


def split_product(lhs, rhs, shard, count):
    tokens, width = lhs.shape
    cols = rhs.shape[1]
    part = width // count
    if 2 * part % LANES:
        cut = dot_tn(lhs, rhs).astype(BF).reshape(count // 2, 2, part, cols)
        return take(cut, 1 - shard % 2, 1), take(cut, shard % 2, 1)
    out = jax.ShapeDtypeStruct((count // 2, part, cols), BF)
    out_spec = pl.BlockSpec((1, part, cols), lambda i: (i, 0, 0))
    return pl.pallas_call(
        product_kernel,
        grid=(count // 2,),
        in_specs=[
            pl.BlockSpec(memory_space=pltpu.SMEM),
            pl.BlockSpec((tokens, 2 * part), lambda i: (0, i)),
            pl.BlockSpec((tokens, cols), lambda i: (0, 0)),
        ],
        out_specs=[out_spec, out_spec],
        out_shape=[out, out],
        compiler_params=pltpu.CompilerParams(vmem_limit_bytes=24 * 1024 * 1024),
        cost_estimate=pl.CostEstimate(flops=0, bytes_accessed=0, transcendentals=0),
    )((shard % 2).astype(jnp.int32).reshape(1), lhs, rhs)


def pair_kernel(chip_ref, near_ref, there_ref, own_ref, *part_refs):
    chip = chip_ref[0]
    own_ref[...] = near_ref[chip].astype(F32) + there_ref[chip].astype(F32)
    for m, part_ref in enumerate(part_refs):
        which = chip ^ (m + 1)
        part_ref[...] = (near_ref[which].astype(F32) + there_ref[which].astype(F32)).astype(BF)


def pair_sums(near, there, shard):
    chips, part, cols = near.shape
    tile = math.gcd(cols, 512)
    if tile % LANES:
        tile = cols
    block = pl.BlockSpec((chips, part, tile), lambda i: (0, 0, i))
    out_spec = pl.BlockSpec((part, tile), lambda i: (0, i))
    out = jax.ShapeDtypeStruct((part, cols), BF)
    return pl.pallas_call(
        pair_kernel,
        grid=(cols // tile,),
        in_specs=[pl.BlockSpec(memory_space=pltpu.SMEM), block, block],
        out_specs=[out_spec] * chips,
        out_shape=[jax.ShapeDtypeStruct((part, cols), F32)] + [out] * (chips - 1),
        compiler_params=pltpu.CompilerParams(vmem_limit_bytes=24 * 1024 * 1024),
        cost_estimate=pl.CostEstimate(flops=0, bytes_accessed=0, transcendentals=0),
    )((shard // 2).astype(jnp.int32).reshape(1), near, there)


def fetch_weights(weights_ref, held, sems, piece):
    copies = [
        pltpu.make_async_copy(
            weights_ref.at[:, pl.ds(part * piece, piece)], held.at[part], sems.at[part]
        )
        for part in range(3)
    ]
    return copies


def experts_forward_kernel(count, *refs):
    rows_in, weights_ref = refs[:count], refs[count]
    rows_ref, gate_up_ref, hidden_ref = refs[count + 1 : count + 4]
    out_refs, (held, sems) = refs[count + 4 : -2], refs[-2:]
    piece = hidden_ref.shape[1]
    cap = rows_in[0].shape[0]
    copies = fetch_weights(weights_ref, held, sems, piece)
    for copy in copies:
        copy.start()
    for s in range(count):
        rows_ref[s * cap : (s + 1) * cap, :] = rows_in[s][...]
    rows = rows_ref[...]
    copies[0].wait()
    gate = dot(rows, held[0])
    gate_up_ref[:, :piece] = gate
    copies[1].wait()
    up = dot(rows, held[1])
    gate_up_ref[:, piece:] = up
    hidden = (gate / (1.0 + jnp.exp(-gate)) * up).astype(BF)
    hidden_ref[...] = hidden
    copies[2].wait()
    out = dot_nt(hidden, held[2]).astype(BF)
    for s in range(count):
        out_refs[s][...] = out[s * cap : (s + 1) * cap, :]


def experts_forward(blocks, weights, piece):
    count = len(blocks)
    cap, width = blocks[0].shape
    rows = count * cap
    in_vmem = pl.BlockSpec(memory_space=pltpu.VMEM)
    return pl.pallas_call(
        functools.partial(experts_forward_kernel, count),
        in_specs=[in_vmem] * count + [pl.BlockSpec(memory_space=pltpu.HBM)],
        out_specs=[in_vmem] * (3 + count),
        out_shape=[
            jax.ShapeDtypeStruct((rows, width), BF),
            jax.ShapeDtypeStruct((rows, 2 * piece), F32),
            jax.ShapeDtypeStruct((rows, piece), BF),
        ]
        + [jax.ShapeDtypeStruct((cap, width), BF)] * count,
        scratch_shapes=[pltpu.VMEM((3, width, piece), BF), pltpu.SemaphoreType.DMA((3,))],
        compiler_params=pltpu.CompilerParams(vmem_limit_bytes=56 * 1024 * 1024),
        cost_estimate=pl.CostEstimate(flops=0, bytes_accessed=0, transcendentals=0),
    )(*blocks, weights)


def experts_backward_kernel(count, *refs):
    grads_in, gate_up_ref, weights_ref = refs[:count], refs[count], refs[count + 1]
    grads_ref, rows_ref = refs[count + 2 : count + 4]
    out_refs, (held, sems) = refs[count + 4 : -2], refs[-2:]
    piece = rows_ref.shape[1] // 2
    cap = grads_in[0].shape[0]
    copies = fetch_weights(weights_ref, held, sems, piece)
    for copy in (copies[2], copies[0], copies[1]):
        copy.start()
    for s in range(count):
        grads_ref[s * cap : (s + 1) * cap, :] = grads_in[s][...]
    copies[2].wait()
    grad_hidden = dot(grads_ref[...], held[2])
    gate = gate_up_ref[:, :piece]
    up = gate_up_ref[:, piece:]
    slope = 1.0 / (1.0 + jnp.exp(-gate))
    grad_gate = (grad_hidden * up * slope * (1.0 + gate * (1.0 - slope))).astype(BF)
    grad_up = (grad_hidden * gate * slope).astype(BF)
    rows_ref[:, :piece] = grad_gate
    rows_ref[:, piece:] = grad_up
    copies[0].wait()
    total = dot_nt(grad_gate, held[0])
    copies[1].wait()
    total = (total + dot_nt(grad_up, held[1])).astype(BF)
    for s in range(count):
        out_refs[s][...] = total[s * cap : (s + 1) * cap, :]


def experts_backward(blocks, gate_up, weights, piece):
    count = len(blocks)
    cap, width = blocks[0].shape
    rows = count * cap
    in_vmem = pl.BlockSpec(memory_space=pltpu.VMEM)
    return pl.pallas_call(
        functools.partial(experts_backward_kernel, count),
        in_specs=[in_vmem] * (count + 1) + [pl.BlockSpec(memory_space=pltpu.HBM)],
        out_specs=[in_vmem] * (2 + count),
        out_shape=[
            jax.ShapeDtypeStruct((rows, width), BF),
            jax.ShapeDtypeStruct((rows, 2 * piece), BF),
        ]
        + [jax.ShapeDtypeStruct((cap, width), BF)] * count,
        scratch_shapes=[pltpu.VMEM((3, width, piece), BF), pltpu.SemaphoreType.DMA((3,))],
        compiler_params=pltpu.CompilerParams(vmem_limit_bytes=56 * 1024 * 1024),
        cost_estimate=pl.CostEstimate(flops=0, bytes_accessed=0, transcendentals=0),
    )(*blocks, gate_up, weights)


def kv_pair_kernel(heads, chips, *refs):
    near, there, outs = refs[:heads], refs[heads : 2 * heads], refs[2 * heads :]
    for m in range(chips):
        for g in range(heads):
            total = near[g][m].astype(F32) + there[g][m].astype(F32)
            outs[m][:, g * 2 * HD : (g + 1) * 2 * HD] = total.astype(outs[m].dtype)


def kv_pair_sums(near, there):
    heads, (chips, rows, cols) = len(near), near[0].shape
    in_vmem = pl.BlockSpec(memory_space=pltpu.VMEM)
    out = jax.ShapeDtypeStruct((rows, heads * cols), BF)
    return pl.pallas_call(
        functools.partial(kv_pair_kernel, heads, chips),
        in_specs=[in_vmem] * (2 * heads),
        out_specs=[in_vmem] * chips,
        out_shape=[jax.ShapeDtypeStruct((rows, heads * cols), F32)] + [out] * (chips - 1),
        compiler_params=pltpu.CompilerParams(vmem_limit_bytes=20 * 1024 * 1024),
        cost_estimate=pl.CostEstimate(flops=0, bytes_accessed=0, transcendentals=0),
    )(*near, *there)


def head_columns_kernel(heads, chips, *refs):
    queries, sums = refs[:heads], refs[heads : heads + chips]
    factor_ref, ride_ref, sent_ref, columns_ref = refs[heads + chips :]
    query = jnp.concatenate([each[...] for each in queries], axis=1)
    keyval = sums[0][...]
    for each in sums[1:]:
        keyval = keyval + each[...].astype(F32)
    both = jnp.concatenate([query, keyval], axis=1)
    rows, cols = both.shape
    sent_ref[...] = both.astype(BF)
    columns_ref[:rows, :cols] = (both * factor_ref[...]).astype(BF)
    columns_ref[:rows, cols:] = jnp.zeros((rows, LANES), BF)
    columns_ref[rows:, :cols] = jnp.zeros((ride_ref.shape[0], cols), BF)
    columns_ref[rows:, cols:] = ride_ref[...]


def head_columns(queries, sums, factor, ride):
    rows = sums[0].shape[0]
    cols = sum(each.shape[1] for each in queries) + sums[0].shape[1]
    if cols % LANES:
        both = jnp.concatenate(list(queries) + [total_of(sums)], axis=1)
        scaled = jnp.pad((both * factor).astype(BF), ((0, 0), (0, LANES)))
        return both.astype(BF), jnp.concatenate([scaled, jnp.pad(ride, ((0, 0), (cols, 0)))])
    in_vmem = pl.BlockSpec(memory_space=pltpu.VMEM)
    return pl.pallas_call(
        functools.partial(head_columns_kernel, len(queries), len(sums)),
        in_specs=[in_vmem] * (len(queries) + len(sums) + 2),
        out_specs=[in_vmem] * 2,
        out_shape=[
            jax.ShapeDtypeStruct((rows, cols), BF),
            jax.ShapeDtypeStruct((rows + ride.shape[0], cols + LANES), BF),
        ],
        compiler_params=pltpu.CompilerParams(vmem_limit_bytes=20 * 1024 * 1024),
        cost_estimate=pl.CostEstimate(flops=0, bytes_accessed=0, transcendentals=0),
    )(*queries, *sums, factor, ride)


def two_parts(value):
    high = value.astype(BF)
    return high, (value - high.astype(F32)).astype(BF)


def mark_kernel(seed_ref, out_ref):
    out_ref[...] = seed_ref[...]


def mark(*others):
    seed = after(jnp.zeros((8, LANES), F32), *others)
    return pl.pallas_call(
        mark_kernel,
        out_shape=jax.ShapeDtypeStruct((8, LANES), F32),
        cost_estimate=pl.CostEstimate(flops=10**12, bytes_accessed=8192, transcendentals=0),
    )(seed)


def by_rows(array):
    return with_layout_constraint(array, Layout(major_to_minor=tuple(range(array.ndim))))


def after(values, *others):
    return lax.optimization_barrier((values, others))[0]


def root(values):
    return lax.rsqrt(jnp.mean(values * values, axis=-1, keepdims=True) + EPSILON)


def root_back(values, factor, grad_scaled):
    inner = jnp.mean(grad_scaled * values, axis=-1, keepdims=True)
    return factor * grad_scaled - values * (factor * factor * factor * inner)


def place_gate_up_kernel(count, place_ref, *refs):
    blocks = refs[: 2 * count - 1]
    weight_ref, gain_ref, out_ref, sums_ref, base = refs[2 * count - 1 :]
    offset = place_ref[0] - pl.program_id(1)

    for s in range(2 * count - 1):

        @pl.when(offset == (s if s < count else count - 1 - s))
        def _(s=s):
            base[...] = blocks[s][...].astype(F32)

    @pl.when((pl.program_id(0) == 0) & (pl.program_id(1) == 0))
    def _():
        sums_ref[...] = jnp.zeros_like(sums_ref)

    values = base[...]
    out_ref[0] = values * gain_ref[...]
    product = jnp.sum(weight_ref[0].astype(F32) * values, axis=1, keepdims=True)
    sums_ref[...] += jnp.broadcast_to(product, sums_ref.shape)


def place_gate_up(steps, weight, gain, place):
    experts, part, both = weight.shape
    count = len(steps)
    split = count // experts
    if split == 1:
        tile = math.gcd(both, 1024)
        blocks = [steps[0][0]] + [each[0] for each in steps[1:]] + [each[1] for each in steps[1:]]
        block = pl.BlockSpec((part, tile), lambda t, e: (0, t))
        out, sums = pl.pallas_call(
            functools.partial(place_gate_up_kernel, count),
            grid=(both // tile, experts),
            in_specs=[pl.BlockSpec(memory_space=pltpu.SMEM)]
            + [block] * len(blocks)
            + [
                pl.BlockSpec((1, part, tile), lambda t, e: (e, 0, t)),
                pl.BlockSpec((part, 1), lambda t, e: (0, 0)),
            ],
            out_specs=[
                pl.BlockSpec((1, part, tile), lambda t, e: (e, 0, t)),
                pl.BlockSpec((part, LANES), lambda t, e: (0, 0)),
            ],
            out_shape=[
                jax.ShapeDtypeStruct(weight.shape, F32),
                jax.ShapeDtypeStruct((part, LANES), F32),
            ],
            scratch_shapes=[pltpu.VMEM((part, tile), F32)],
            compiler_params=pltpu.CompilerParams(vmem_limit_bytes=28 * 1024 * 1024),
            cost_estimate=pl.CostEstimate(flops=0, bytes_accessed=0, transcendentals=0),
        )(place.astype(jnp.int32).reshape(1), *blocks, weight, gain)
        return out, sums[:, 0]
    blocks = [steps[0][0]] + [
        jnp.where(place >= s, steps[s][0], steps[count - s][1]) for s in range(1, count)
    ]
    base = (
        from_relative(blocks, place)
        .reshape(experts, split, part, 2, both // (2 * split))
        .transpose(0, 2, 3, 1, 4)
        .reshape(experts, part, both)
        .astype(F32)
    )
    return base * gain, jnp.sum(weight.astype(F32) * base, axis=(0, 2))


def place_kernel(count, q_cols, kv_cols, place_ref, *refs):
    blocks, outs = refs[:count], refs[count : 2 * count]
    w_query_ref, w_keyval_ref, gain_ref, query_ref, keyval_ref, out_ref, base_ref, sums_ref = refs[
        2 * count :
    ]
    gain = gain_ref[...]
    base = jnp.zeros_like(gain)
    sums = jnp.zeros(sums_ref.shape, F32)
    for s in range(count):
        owner = lax.rem(place_ref[0] + (count - s), count)
        q_at = pl.ds(pl.multiple_of(owner * q_cols, LANES), q_cols)
        kv_at = pl.ds(pl.multiple_of(owner * kv_cols, LANES), kv_cols)
        query = blocks[s][:, :q_cols].astype(F32)
        keyval = blocks[s][:, q_cols : q_cols + kv_cols].astype(F32)
        start = q_cols + kv_cols
        sums = sums + blocks[s][:, start : start + LANES].astype(F32)
        out_ref[:, q_at] = outs[s][...].astype(F32)
        base = base + jnp.sum(w_query_ref[:, q_at].astype(F32) * query, axis=1, keepdims=True)
        base = base + jnp.sum(w_keyval_ref[:, kv_at].astype(F32) * keyval, axis=1, keepdims=True)
        query_ref[:, q_at] = query * gain
        keyval_ref[:, kv_at] = keyval * gain
    base_ref[...] = jnp.broadcast_to(base, base_ref.shape)
    sums_ref[...] = sums


def place_heads(blocks, outs, place, w_query, w_keyval, gain, q_cols, kv_cols):
    count = len(blocks)
    part = w_query.shape[0]
    start = q_cols + kv_cols
    if q_cols % LANES == 0 and kv_cols % LANES == 0:
        wide = jax.ShapeDtypeStruct((part, count * q_cols), F32)
        narrow = jax.ShapeDtypeStruct((part, count * kv_cols), F32)
        lanes = jax.ShapeDtypeStruct((part, LANES), F32)
        in_vmem = pl.BlockSpec(memory_space=pltpu.VMEM)
        query, keyval, out, base, sums = pl.pallas_call(
            functools.partial(place_kernel, count, q_cols, kv_cols),
            in_specs=[pl.BlockSpec(memory_space=pltpu.SMEM)] + [in_vmem] * (2 * count + 3),
            out_specs=[in_vmem] * 5,
            out_shape=[wide, narrow, wide, lanes, lanes],
            compiler_params=pltpu.CompilerParams(vmem_limit_bytes=24 * 1024 * 1024),
            cost_estimate=pl.CostEstimate(flops=0, bytes_accessed=0, transcendentals=0),
        )(place.astype(jnp.int32).reshape(1), *blocks, *outs, w_query, w_keyval, gain)
        return query, keyval, out, base[:, 0], sums
    blocks = from_relative(blocks, place).astype(F32)
    outs = from_relative(outs, place).astype(F32)

    def columns(begin, end):
        return blocks[:, :, begin:end].transpose(1, 0, 2).reshape(part, count * (end - begin))

    query, keyval = columns(0, q_cols), columns(q_cols, start)
    base = jnp.sum(w_query.astype(F32) * query, axis=1) + jnp.sum(
        w_keyval.astype(F32) * keyval, axis=1
    )
    sums = jnp.sum(blocks[:, :, start : start + LANES], axis=0)
    out = outs.transpose(1, 0, 2).reshape(part, count * q_cols)
    return query * gain, keyval * gain, out, base, sums


def local(
    tokens,
    teacher,
    valid,
    routes,
    slots,
    gain_attn,
    w_query,
    w_keyval,
    w_out,
    gain_ffn,
    w_router,
    w_gate_up,
    w_down,
):
    seqs = lax.axis_size("seq")
    shards = lax.axis_size("fsdp")
    z = lax.axis_index("seq")
    shard = lax.axis_index("fsdp")
    rows, width = tokens.shape
    groups = HEADS // KVH
    local_kv = KVH // seqs
    q_cols = local_kv * groups * HD
    kv_cols = local_kv * 2 * HD
    local_rows = rows * seqs
    seq_len = local_rows * shards
    experts, part, both = w_gate_up.shape
    units = both // 2
    split = seqs // experts
    piece = units // split
    expert = z // split
    fraction = z % split
    scale = HD ** (-0.5)

    gain_one = gain_attn.astype(F32)[:, None]
    gain_two = gain_ffn.astype(F32)[:, None]
    heads_shard = jnp.concatenate(
        [
            lax.dynamic_slice_in_dim(w_query, z * q_cols, q_cols, 1),
            lax.dynamic_slice_in_dim(w_keyval, z * kv_cols, kv_cols, 1),
        ],
        axis=1,
    )
    heads_shard = (heads_shard.astype(F32) * gain_one).astype(BF)
    heads_full = lax.all_gather(heads_shard, "fsdp", axis=0, tiled=True)
    valid_row = jnp.pad(valid.astype(BF).reshape(1, rows), ((0, 7), (0, width - rows)))
    token_rows = jnp.concatenate([tokens, valid_row], axis=0)
    token_mark = mark(token_rows)
    token_blocks = after(send_out([token_rows] * seqs, seqs), token_mark)

    valid_local = from_relative([each[rows : rows + 1, :rows] for each in token_blocks], z)
    projected = []
    for block in token_blocks:
        projected.append(dot(block[:rows], heads_full) * root(block[:rows].astype(F32)))
    projected = from_relative([each.astype(BF) for each in projected], z)
    projected = projected.reshape(local_rows, q_cols + kv_cols)
    head_queries = projected[:, :q_cols] * jnp.asarray(scale, BF)

    valid_rows_kv = local_rows // kv_cols
    payload = jnp.concatenate(
        [
            projected[:, q_cols:],
            valid_local.reshape(valid_rows_kv, kv_cols),
            jnp.zeros((16 - valid_rows_kv, kv_cols), BF),
        ],
        axis=0,
    )
    kv_blocks = gather_shards(payload, shards)
    late_query, late_keyval, late_router, late_gate_up, late_down = after(
        (w_query, w_keyval, w_router, w_gate_up, w_down), token_mark
    )
    out_full = lax.all_gather(w_out, "fsdp", axis=1, tiled=True)
    own_expert = take(late_gate_up, expert, 0)
    gate_shard = lax.dynamic_slice_in_dim(own_expert, fraction * piece, piece, 1)
    up_shard = lax.dynamic_slice_in_dim(own_expert, units + fraction * piece, piece, 1)
    down_shard = lax.dynamic_slice_in_dim(take(late_down, expert, 0), fraction * piece, piece, 0).T
    router_shard = jnp.pad((late_router.astype(F32) * gain_two).astype(BF), ((0, 0), (0, LANES - experts)))
    expert_shard = jnp.concatenate(
        [
            (gate_shard.astype(F32) * gain_two).astype(BF),
            (up_shard.astype(F32) * gain_two).astype(BF),
            down_shard,
            router_shard,
        ],
        axis=1,
    )
    expert_full = lax.all_gather(expert_shard, "fsdp", axis=0, tiled=True)
    router_full = expert_full[:, 3 * piece :]
    attn_shard = jnp.concatenate(
        [
            each
            for s in range(seqs)
            for each in (
                late_query[:, s * q_cols : (s + 1) * q_cols],
                late_keyval[:, s * kv_cols : (s + 1) * kv_cols],
            )
        ],
        axis=1,
    )
    attn_full = lax.all_gather(
        (attn_shard.astype(F32) * gain_one).astype(BF), "fsdp", axis=0, tiled=True
    )
    order = jnp.asarray(
        [2 * m for m in range(shards // 2)] + [2 * m + 1 for m in range(shards // 2)], jnp.int32
    )
    valid_all = jnp.stack(
        [
            each[local_rows : local_rows + valid_rows_kv].reshape(seqs, rows)
            for each in kv_blocks
        ],
        axis=1,
    ).astype(F32)
    valid_count = jnp.sum(valid_all)
    bias = jnp.where(valid_all > 0, 0.0, FLOOR_SCORE)
    earlier = ((order ^ shard) < shard) | (order == 0)
    bias_same = jnp.where(earlier[None, :, None], bias, FLOOR_SCORE)
    bias = jnp.concatenate([bias, bias_same]).reshape(2 * seqs, 1, shards * rows)
    attended_low, lse = flash_forward(
        head_queries, kv_blocks, bias, seqs, rows, local_kv, groups
    )
    attended = lax.all_to_all(attended_low, "seq", split_axis=0, concat_axis=1, tiled=True)

    inputs = tokens.astype(F32)
    residual = inputs + dot(attended, out_full)
    factor_two = root(residual)
    normed_two = (residual * factor_two).astype(BF)
    logits = dot(normed_two, router_full)[:, :experts]
    expert_ids = jnp.arange(experts, dtype=jnp.int32)
    picked = (routes[:, :, None] == expert_ids).astype(F32)
    chosen = jnp.sum(picked * logits[:, None, :], axis=-1)
    gating = jax.nn.softmax(chosen, axis=-1)
    owners = ((jnp.arange(seqs, dtype=jnp.int32) + z) % seqs) // split
    to_owner = routes[:, :, None] == owners
    slot_hot = slots[:, :, None] == jnp.arange(CAP, dtype=jnp.int32)
    placed = (to_owner[:, :, :, None] & slot_hot[:, :, None, :]).astype(BF)
    placed = placed.reshape(rows, 2, seqs * CAP)
    dispatch = placed[:, 0] + placed[:, 1]
    placed_pairs = jnp.concatenate([placed[:, 0], placed[:, 1]], axis=0)
    sent_rows = dot_tn(dispatch, normed_two).astype(BF)
    kv_all = jnp.stack(after(kv_blocks, sent_rows))
    sent_rows = sent_rows.reshape(seqs, CAP, width)
    expert_rows, gate_up, hidden, *expert_out = experts_forward(
        send_out([sent_rows[s] for s in range(seqs)], seqs), expert_full, piece
    )
    returned = jnp.concatenate(after(send_back(expert_out, seqs), kv_all))
    selected = dot(placed_pairs, returned).reshape(2, rows, width)
    mixed_exact = residual + gating[:, :1] * selected[0] + gating[:, 1:] * selected[1]
    valid_rows = valid.astype(F32)
    errors = (mixed_exact - teacher.astype(F32)) * valid_rows[:, None]
    squares = jnp.sum(errors * errors)
    loss_scale = width * seq_len // 8
    grad_mixed = errors * (2.0 * loss_scale / (width * valid_count))

    grad_gating = jnp.stack(
        [jnp.sum(selected[0] * grad_mixed, axis=-1), jnp.sum(selected[1] * grad_mixed, axis=-1)],
        axis=1,
    )
    grad_chosen = gating * (grad_gating - jnp.sum(gating * grad_gating, axis=-1, keepdims=True))
    grad_logits = jnp.sum(grad_chosen[:, :, None] * picked, axis=1).astype(BF)
    grad_logits = jnp.pad(grad_logits, ((0, 0), (0, LANES - experts)))
    weighted = jnp.concatenate(
        [(gating[:, :1] * grad_mixed).astype(BF), (gating[:, 1:] * grad_mixed).astype(BF)], axis=0
    )
    sent_grads = dot_tn(placed_pairs, weighted).astype(BF).reshape(seqs, CAP, width)
    grad_out_rows = send_out([sent_grads[s] for s in range(seqs)], seqs)
    grad_out_rows = after(grad_out_rows, attn_full, grad_logits)
    grad_expert_out, grad_gate_up_rows, *grad_rows = experts_backward(
        grad_out_rows, gate_up, expert_full, piece
    )
    grad_returned = send_back(grad_rows, seqs)
    tokens_local = from_relative(
        [each[:rows] for each in after(token_blocks, grad_rows)], z
    ).reshape(local_rows, width)
    factor_local = root(tokens_local.astype(F32))
    ride_rows = jnp.concatenate([normed_two, jnp.ones((16, width), BF)], axis=0)
    product_rows = jnp.concatenate([tokens_local, ride_rows], axis=0)
    high, low = two_parts(squares)
    lane = jnp.arange(LANES, dtype=jnp.int32)[None, :]
    marks = jnp.where(lane == experts + 2 * (shard % 2), high, 0) + jnp.where(
        lane == experts + 1 + 2 * (shard % 2), low, 0
    )
    ride_columns = jnp.concatenate(
        [grad_logits, marks.astype(BF), jnp.zeros((15, LANES), BF)], axis=0
    )
    held_out, held_hidden = after((grad_expert_out, hidden), grad_rows)
    down_far, down_near = split_product(held_out, held_hidden, shard, shards)
    grad_down_sums = pair_sums(down_near, hop(down_far, shards, 1), shard)
    held_rows, held_gate_up = after((expert_rows, grad_gate_up_rows), grad_rows)
    gate_up_far, gate_up_near = split_product(held_rows, held_gate_up, shard, shards)
    grad_gate_up_sums = pair_sums(gate_up_near, hop(gate_up_far, shards, 1), shard)
    grad_down_blocks = send_chips(grad_down_sums, shards)
    grad_returned = jnp.concatenate(after(grad_returned, grad_down_sums, product_rows, ride_columns, factor_local))
    grad_normed_two = dot(dispatch, grad_returned) + dot_nt(grad_logits, router_full)
    grad_residual = grad_mixed + root_back(residual, factor_two, grad_normed_two)
    grad_branch = grad_residual.astype(BF)
    grad_attended = dot_nt(after(grad_branch, grad_gate_up_sums), out_full).astype(BF)
    head_grad = lax.all_to_all(grad_attended, "seq", split_axis=1, concat_axis=0, tiled=True)
    grad_gate_up_blocks = send_chips(grad_gate_up_sums, shards)
    grad_down_shard = total_of(after(grad_down_blocks, grad_attended)).astype(BF)
    grad_down = lax.all_gather(grad_down_shard, "seq", axis=0, tiled=False)

    out_far, out_near = split_product(
        after(grad_branch, grad_attended), attended, shard, shards
    )
    grad_q, near, far = [], [], []
    held = after(head_grad, grad_down_shard)
    for g in range(local_kv):
        part_q, near_kv, far_kv = flash_backward(
            head_queries, kv_all, bias, held, attended_low, lse, seqs, rows, g, groups
        )
        if g == 0:
            grad_gate_up_blocks = after(grad_gate_up_blocks, part_q)
            grad_gate_up_shard = total_of(grad_gate_up_blocks).astype(BF)
            steps = [(grad_gate_up_shard, grad_gate_up_shard)]
            steps.append(relay_step(steps[0], seqs))
            out_there = hop(after(out_far, head_grad), shards, 1)
        grad_q.append(part_q)
        near.append(near_kv)
        far.append(far_kv)
        held = after(head_grad, grad_gate_up_shard, out_there)
    steps[1] = after(steps[1], part_q)
    steps.append(relay_step(steps[1], seqs))
    far = after(far, steps[1], grad_down)
    pairs = kv_pair_sums(near, [hop(each, shards, 1) for each in far])
    out_sums = pair_sums(out_near, after(out_there, pairs), shard)
    sent_grads, product_columns = head_columns(
        grad_q, after(send_chips(pairs, shards), out_sums, steps[2]), factor_local, ride_columns
    )
    steps[2] = after(steps[2], product_columns)
    while len(steps) < seqs:
        steps.append(relay_step(steps[-1], seqs))
    token_grads = lax.all_to_all(sent_grads, "seq", split_axis=0, concat_axis=1, tiled=True)

    head_cols = q_cols + kv_cols
    head_far, head_near = split_product(product_rows, product_columns, shard, shards)
    head_sums = pair_sums(head_near, hop(head_far, shards, 1), shard)
    head_blocks = send_chips(head_sums, shards)
    head_part = total_of(after(head_blocks, steps[3]))
    grad_normed = dot_nt(after(token_grads, head_part), attn_full)
    grad_tokens = grad_residual + root_back(inputs, root(inputs), grad_normed)
    base_cols = head_cols + experts
    plane_high, plane_low = two_parts(
        jnp.sum(head_part[:1, base_cols : base_cols + 4], axis=1, keepdims=True)
    )
    lanes = lax.broadcasted_iota(jnp.int32, head_part.shape, 1)
    head_part = jnp.where(
        lanes == base_cols,
        plane_high.astype(F32),
        jnp.where(lanes == base_cols + 1, plane_low.astype(F32), head_part),
    )
    head_part = by_rows(head_part.astype(BF))
    head_last = [by_rows(each) for each in send_out([head_part] * seqs, seqs)]
    out_blocks = send_chips(after(out_sums, head_part), shards)
    out_part = total_of(out_blocks).astype(BF)
    out_parts = lax.all_to_all(
        out_part.reshape(part, seqs, q_cols), "seq", split_axis=1, concat_axis=1, tiled=True
    )
    out_own = by_rows(jnp.sum(out_parts.astype(F32), axis=1).astype(BF))
    grad_gate_up, grad_gain_ffn = place_gate_up(after(steps, head_part), w_gate_up, gain_two, z)
    out_own = after(out_own, grad_gate_up)
    out_last = [by_rows(each) for each in send_out([out_own] * seqs, seqs)]
    grad_query, grad_keyval, grad_out, grad_gain_attn, sums = place_heads(
        head_last, out_last, z, w_query, w_keyval, gain_one, q_cols, kv_cols
    )
    loss_value = jnp.sum(sums[0, experts : experts + 2]) / (width * valid_count)
    grad_router_base = sums[:, :experts]
    grad_down = (
        after(grad_down, head_part).reshape(experts, split, part, piece)
        .transpose(0, 1, 3, 2)
        .reshape(experts, units, part)
        .astype(F32)
    )
    grad_gain_ffn = grad_gain_ffn + jnp.sum(w_router.astype(F32) * grad_router_base, axis=1)
    return (
        mixed_exact.astype(BF),
        loss_value,
        grad_tokens,
        grad_gain_attn,
        grad_query,
        grad_keyval,
        grad_out.T,
        grad_gain_ffn,
        grad_router_base * gain_two,
        grad_gate_up,
        grad_down,
    )


def solution(mesh):
    return jax.shard_map(
        local,
        mesh=mesh,
        in_specs=(
            P(("seq", "fsdp"), None),
            P(("seq", "fsdp"), None),
            P(("seq", "fsdp")),
            P(("seq", "fsdp"), None),
            P(("seq", "fsdp"), None),
            P("fsdp"),
            P("fsdp", None),
            P("fsdp", None),
            P(None, "fsdp"),
            P("fsdp"),
            P("fsdp", None),
            P(None, "fsdp", None),
            P(None, None, "fsdp"),
        ),
        out_specs=(
            P(("seq", "fsdp"), None),
            P(),
            P(("seq", "fsdp"), None),
            P("fsdp"),
            P("fsdp", None),
            P("fsdp", None),
            P(None, "fsdp"),
            P("fsdp"),
            P("fsdp", None),
            P(None, "fsdp", None),
            P(None, None, "fsdp"),
        ),
        check_vma=False,
    )
```

```python
import functools
import math

import jax
import jax.numpy as jnp
from jax import lax
from jax.experimental import pallas as pl
from jax.experimental.layout import Layout, with_layout_constraint
from jax.experimental.pallas import tpu as pltpu
from jax.sharding import PartitionSpec as P

HEADS = 24
KVH = 8
HD = 64
CAP = 96
LANES = 128
EPSILON = 1e-06
FLOOR_SCORE = -1e30
BF = jnp.bfloat16
F32 = jnp.float32


def dot(a, b):
    return jnp.dot(a, b, preferred_element_type=F32)


def dot_nt(a, b):
    return lax.dot_general(a, b, (((1,), (1,)), ((), ())), preferred_element_type=F32)


def dot_tn(a, b):
    return lax.dot_general(a, b, (((0,), (0,)), ((), ())), preferred_element_type=F32)


def own_mask(valid_row, rows):
    i = lax.broadcasted_iota(jnp.int32, (rows, rows), 0)
    j = lax.broadcasted_iota(jnp.int32, (rows, rows), 1)
    return jnp.where(j == i, 0.0, jnp.where(j < i, valid_row, FLOOR_SCORE))


def key_chunk(kv_refs, zk, rows, g):
    return jnp.concatenate(
        [ref[pl.ds(zk * rows, rows), pl.ds(g * 2 * HD, 2 * HD)] for ref in kv_refs], axis=0
    )


def forward_kernel(shards, seqs, rows, local_kv, groups, *refs):
    kv_refs = refs[:shards]
    q_ref, bias_ref, low_ref, lse_ref, acc_ref, max_ref = refs[shards:]
    zq = pl.program_id(0)
    stack = groups * rows
    zeros = jnp.zeros((rows, HD), BF)
    half = lax.broadcasted_iota(jnp.int32, (1, 2 * HD), 1) < HD

    def queries(g):
        parts = []
        for h in range(groups):
            start = (g * groups + h) * HD
            parts.append(jnp.concatenate([q_ref[:, start : start + HD], zeros], axis=1))
        return jnp.concatenate(parts, axis=0)

    def chunk(g, zk, scores):
        first = scores is None
        keys = key_chunk(kv_refs, zk, rows, g)
        raw = dot_nt(queries(g), keys)
        if first:
            row = bias_ref[seqs + zk]
            mask = own_mask(row[:, :rows], rows)
            mask = jnp.concatenate([mask] * groups, axis=0)
            masked = jnp.concatenate([raw[:, :rows] + mask, raw[:, rows:] + row[:, rows:]], axis=1)
            new_max = jnp.max(masked, axis=1, keepdims=True)
        else:
            masked = raw + bias_ref[zk]
            new_max = jnp.maximum(max_ref[g][:, :1], jnp.max(masked, axis=1, keepdims=True))
        terms = jnp.exp(masked - new_max).astype(BF)
        ones_values = jnp.where(half, jnp.ones_like(keys), keys)
        part = dot(terms, ones_values)
        if first:
            acc_ref[g] = part
        else:
            acc_ref[g] = acc_ref[g] * jnp.exp(max_ref[g][:, :1] - new_max) + part
        max_ref[g] = jnp.broadcast_to(new_max, (stack, 2 * HD))

    for g in range(local_kv):
        chunk(g, zq, None)

    @pl.loop(0, zq)
    def _(zk):
        for g in range(local_kv):
            chunk(g, zk, True)

    exact_parts, lse_parts = [], []
    for g in range(local_kv):
        acc = acc_ref[g]
        total = acc[:, :HD]
        exact = acc[:, HD:] / total
        lse = max_ref[g][:, :HD] + jnp.log(total)
        for h in range(groups):
            exact_parts.append(exact[h * rows : (h + 1) * rows])
            lse_parts.append(lse[h * rows : (h + 1) * rows])
    low_ref[...] = jnp.concatenate(exact_parts, axis=1).astype(BF)
    lse_ref[...] = jnp.concatenate(lse_parts, axis=1)


def flash_forward(q, kv_blocks, bias, seqs, rows, local_kv, groups):
    shards = len(kv_blocks)
    q_cols = q.shape[1]
    kv_spec = pl.BlockSpec(kv_blocks[0].shape, lambda i: (0, 0))
    q_spec = pl.BlockSpec((rows, q_cols), lambda i: (i, 0))
    stack = groups * rows
    out = jax.ShapeDtypeStruct((seqs * rows, q_cols), F32)
    return pl.pallas_call(
        functools.partial(forward_kernel, shards, seqs, rows, local_kv, groups),
        grid=(seqs,),
        in_specs=[kv_spec] * shards + [q_spec, pl.BlockSpec(bias.shape, lambda i: (0, 0, 0))],
        out_specs=[q_spec] * 2,
        out_shape=[jax.ShapeDtypeStruct((seqs * rows, q_cols), BF), out],
        scratch_shapes=[
            pltpu.VMEM((local_kv, stack, 2 * HD), F32),
            pltpu.VMEM((local_kv, stack, 2 * HD), F32),
        ],
        compiler_params=pltpu.CompilerParams(vmem_limit_bytes=24 * 1024 * 1024),
        cost_estimate=pl.CostEstimate(
            flops=0,
            bytes_accessed=0,
            transcendentals=0,
        ),
    )(*kv_blocks, q, bias)


def backward_kernel(shards, seqs, rows, g, groups, *refs):
    kv_refs = [refs[0].at[p] for p in range(shards)]
    (
        q_ref, bias_ref, grad_ref, low_ref, lse_ref, grad_q_ref, near_ref, far_ref,
        pair_ref, pair_t_ref, lse_wide, delta_wide, acc_q, acc_kv,
    ) = refs[1:]
    zk = pl.program_id(0)
    stack = groups * rows
    zeros = jnp.zeros((rows, HD), BF)

    @pl.when(zk == 0)
    def _():
        acc_q[...] = jnp.zeros_like(acc_q)

        @pl.loop(0, seqs)
        def _(zq):
            here = pl.ds(zq * rows, rows)
            tops, bottoms = [], []
            for h in range(groups):
                cols = slice((g * groups + h) * HD, (g * groups + h + 1) * HD)
                grad = grad_ref[here, cols]
                tops.append(jnp.concatenate([q_ref[here, cols], zeros], axis=1))
                bottoms.append(jnp.concatenate([zeros, grad], axis=1))
                delta = jnp.sum(grad.astype(F32) * low_ref[here, cols].astype(F32), axis=1, keepdims=True)
                part = slice(h * rows, (h + 1) * rows)
                delta_wide[zq, part] = jnp.broadcast_to(delta, (rows, 2 * HD))
                lse_wide[zq, part] = jnp.broadcast_to(lse_ref[here, cols][:, :1], (rows, 2 * HD))
            pair = jnp.concatenate(tops + bottoms, axis=0)
            pair_ref[zq] = pair
            pair_t_ref[zq] = pair.astype(F32).T.astype(BF)

    def chunk(zq, first):
        keys = key_chunk(kv_refs, zk, rows, g)
        both = dot_nt(pair_ref[zq], keys)
        raw, products = both[:stack], both[stack:]
        if first:
            row = bias_ref[seqs + zk]
            mask = own_mask(row[:, :rows], rows)
            mask = jnp.concatenate([mask] * groups, axis=0)
            masked = jnp.concatenate([raw[:, :rows] + mask, raw[:, rows:] + row[:, rows:]], axis=1)
        else:
            masked = raw + bias_ref[zk]
        weights = jnp.exp(masked - lse_wide[zq][:, :1])
        grads = (weights * (products - delta_wide[zq][:, :1])).astype(BF)
        acc_q[zq] += dot(grads, keys)
        part = dot(pair_t_ref[zq], jnp.concatenate([grads, weights.astype(BF)], axis=0))
        if first:
            acc_kv[...] = part
        else:
            acc_kv[...] += part

    chunk(zk, True)

    @pl.loop(zk + 1, seqs)
    def _(zq):
        chunk(zq, False)

    for p in range(shards):
        target = near_ref if p < shards // 2 else far_ref
        target[p % (shards // 2)] = acc_kv[:, p * rows : (p + 1) * rows].T.astype(BF)

    @pl.when(zk == seqs - 1)
    def _():
        @pl.loop(0, seqs)
        def _(zq):
            total = acc_q[zq]
            parts = [total[h * rows : (h + 1) * rows, :HD] for h in range(groups)]
            grad_q_ref[pl.ds(zq * rows, rows), :] = jnp.concatenate(parts, axis=1) * HD ** (-0.5)


def flash_backward(q, kv_all, bias, grad, low, lse, seqs, rows, g, groups):
    shards = kv_all.shape[0]
    q_cols = q.shape[1]
    stack = groups * rows
    kv_spec = pl.BlockSpec(kv_all.shape, lambda i: (0, 0, 0))
    whole = pl.BlockSpec((seqs * rows, q_cols), lambda i: (0, 0))
    grad_q_shape = (seqs * rows, groups * HD)
    out_spec = pl.BlockSpec((shards // 2, rows, 2 * HD), lambda i: (0, i, 0))
    out = jax.ShapeDtypeStruct((shards // 2, seqs * rows, 2 * HD), BF)
    return pl.pallas_call(
        functools.partial(backward_kernel, shards, seqs, rows, g, groups),
        grid=(seqs,),
        in_specs=[kv_spec]
        + [whole, pl.BlockSpec(bias.shape, lambda i: (0, 0, 0)), whole, whole, whole],
        out_specs=[pl.BlockSpec(grad_q_shape, lambda i: (0, 0)), out_spec, out_spec],
        out_shape=[jax.ShapeDtypeStruct(grad_q_shape, F32), out, out],
        scratch_shapes=[
            pltpu.VMEM((seqs, 2 * stack, 2 * HD), BF),
            pltpu.VMEM((seqs, 2 * HD, 2 * stack), BF),
            pltpu.VMEM((seqs, stack, 2 * HD), F32),
            pltpu.VMEM((seqs, stack, 2 * HD), F32),
            pltpu.VMEM((seqs, stack, 2 * HD), F32),
            pltpu.VMEM((2 * HD, shards * rows), F32),
        ],
        compiler_params=pltpu.CompilerParams(vmem_limit_bytes=28 * 1024 * 1024),
        cost_estimate=pl.CostEstimate(
            flops=0 if g else 10**12,
            bytes_accessed=0,
            transcendentals=0,
        ),
    )(kv_all, q, bias, grad, low, lse)


def shift(block, count, step):
    return lax.ppermute(block, "seq", [(i, (i + step) % count) for i in range(count)])


def send_out(blocks, count):
    return [blocks[0]] + [shift(blocks[s], count, s) for s in range(1, count)]


def send_back(blocks, count):
    return [blocks[0]] + [shift(blocks[s], count, count - s) for s in range(1, count)]


def relay_step(blocks, count):
    up, down = blocks
    return (
        lax.ppermute(up, "seq", [(i, i + 1) for i in range(count - 1)]),
        lax.ppermute(down, "seq", [(i + 1, i) for i in range(count - 1)]),
    )


def from_relative(blocks, place):
    count = len(blocks)
    rising = jnp.stack([blocks[-s % count] for s in range(count)])
    return lax.dynamic_slice_in_dim(jnp.concatenate([rising, rising]), count - place, count, 0)


def hop(block, count, mask):
    return lax.ppermute(block, "fsdp", [(i, i ^ mask) for i in range(count)])


def gather_shards(block, count):
    near = [block] + [hop(block, count, 2 * m) for m in range(1, count // 2)]
    return near + [hop(each, count, 1) for each in near]


def send_chips(parts, count):
    return [parts[0]] + [hop(parts[m], count, 2 * m) for m in range(1, count // 2)]


def total_of(blocks):
    total = blocks[0].astype(F32)
    for each in blocks[1:]:
        total = total + each.astype(F32)
    return total


def take(array, index, axis):
    return lax.dynamic_index_in_dim(array, index, axis, keepdims=False)


def product_kernel(core_ref, lhs_ref, rhs_ref, far_ref, near_ref):
    part = lhs_ref.shape[1] // 2
    rhs = rhs_ref[...]
    first = dot_tn(lhs_ref[:, :part], rhs).astype(BF)
    second = dot_tn(lhs_ref[:, part:], rhs).astype(BF)
    core = core_ref[0]

    @pl.when(core == 0)
    def _():
        near_ref[0] = first
        far_ref[0] = second

    @pl.when(core != 0)
    def _():
        near_ref[0] = second
        far_ref[0] = first


def split_product(lhs, rhs, shard, count):
    tokens, width = lhs.shape
    cols = rhs.shape[1]
    part = width // count
    if 2 * part % LANES:
        cut = dot_tn(lhs, rhs).astype(BF).reshape(count // 2, 2, part, cols)
        return take(cut, 1 - shard % 2, 1), take(cut, shard % 2, 1)
    out = jax.ShapeDtypeStruct((count // 2, part, cols), BF)
    out_spec = pl.BlockSpec((1, part, cols), lambda i: (i, 0, 0))
    return pl.pallas_call(
        product_kernel,
        grid=(count // 2,),
        in_specs=[
            pl.BlockSpec(memory_space=pltpu.SMEM),
            pl.BlockSpec((tokens, 2 * part), lambda i: (0, i)),
            pl.BlockSpec((tokens, cols), lambda i: (0, 0)),
        ],
        out_specs=[out_spec, out_spec],
        out_shape=[out, out],
        compiler_params=pltpu.CompilerParams(vmem_limit_bytes=24 * 1024 * 1024),
        cost_estimate=pl.CostEstimate(flops=0, bytes_accessed=0, transcendentals=0),
    )((shard % 2).astype(jnp.int32).reshape(1), lhs, rhs)


def pair_kernel(chip_ref, near_ref, there_ref, own_ref, *part_refs):
    chip = chip_ref[0]
    own_ref[...] = near_ref[chip].astype(F32) + there_ref[chip].astype(F32)
    for m, part_ref in enumerate(part_refs):
        which = chip ^ (m + 1)
        part_ref[...] = (near_ref[which].astype(F32) + there_ref[which].astype(F32)).astype(BF)


def pair_sums(near, there, shard):
    chips, part, cols = near.shape
    tile = math.gcd(cols, 512)
    if tile % LANES:
        tile = cols
    block = pl.BlockSpec((chips, part, tile), lambda i: (0, 0, i))
    out_spec = pl.BlockSpec((part, tile), lambda i: (0, i))
    out = jax.ShapeDtypeStruct((part, cols), BF)
    return pl.pallas_call(
        pair_kernel,
        grid=(cols // tile,),
        in_specs=[pl.BlockSpec(memory_space=pltpu.SMEM), block, block],
        out_specs=[out_spec] * chips,
        out_shape=[jax.ShapeDtypeStruct((part, cols), F32)] + [out] * (chips - 1),
        compiler_params=pltpu.CompilerParams(vmem_limit_bytes=24 * 1024 * 1024),
        cost_estimate=pl.CostEstimate(flops=0, bytes_accessed=0, transcendentals=0),
    )((shard // 2).astype(jnp.int32).reshape(1), near, there)


def fetch_weights(weights_ref, held, sems, piece):
    copies = [
        pltpu.make_async_copy(
            weights_ref.at[:, pl.ds(part * piece, piece)], held.at[part], sems.at[part]
        )
        for part in range(3)
    ]
    return copies


def experts_forward_kernel(count, *refs):
    rows_in, weights_ref = refs[:count], refs[count]
    rows_ref, gate_up_ref, hidden_ref = refs[count + 1 : count + 4]
    out_refs, (held, sems) = refs[count + 4 : -2], refs[-2:]
    piece = hidden_ref.shape[1]
    cap = rows_in[0].shape[0]
    copies = fetch_weights(weights_ref, held, sems, piece)
    for copy in copies:
        copy.start()
    for s in range(count):
        rows_ref[s * cap : (s + 1) * cap, :] = rows_in[s][...]
    rows = rows_ref[...]
    copies[0].wait()
    gate = dot(rows, held[0])
    gate_up_ref[:, :piece] = gate
    copies[1].wait()
    up = dot(rows, held[1])
    gate_up_ref[:, piece:] = up
    hidden = (gate / (1.0 + jnp.exp(-gate)) * up).astype(BF)
    hidden_ref[...] = hidden
    copies[2].wait()
    out = dot_nt(hidden, held[2]).astype(BF)
    for s in range(count):
        out_refs[s][...] = out[s * cap : (s + 1) * cap, :]


def experts_forward(blocks, weights, piece):
    count = len(blocks)
    cap, width = blocks[0].shape
    rows = count * cap
    in_vmem = pl.BlockSpec(memory_space=pltpu.VMEM)
    return pl.pallas_call(
        functools.partial(experts_forward_kernel, count),
        in_specs=[in_vmem] * count + [pl.BlockSpec(memory_space=pltpu.HBM)],
        out_specs=[in_vmem] * (3 + count),
        out_shape=[
            jax.ShapeDtypeStruct((rows, width), BF),
            jax.ShapeDtypeStruct((rows, 2 * piece), F32),
            jax.ShapeDtypeStruct((rows, piece), BF),
        ]
        + [jax.ShapeDtypeStruct((cap, width), BF)] * count,
        scratch_shapes=[pltpu.VMEM((3, width, piece), BF), pltpu.SemaphoreType.DMA((3,))],
        compiler_params=pltpu.CompilerParams(vmem_limit_bytes=56 * 1024 * 1024),
        cost_estimate=pl.CostEstimate(flops=0, bytes_accessed=0, transcendentals=0),
    )(*blocks, weights)


def experts_backward_kernel(count, *refs):
    grads_in, gate_up_ref, weights_ref = refs[:count], refs[count], refs[count + 1]
    grads_ref, rows_ref = refs[count + 2 : count + 4]
    out_refs, (held, sems) = refs[count + 4 : -2], refs[-2:]
    piece = rows_ref.shape[1] // 2
    cap = grads_in[0].shape[0]
    copies = fetch_weights(weights_ref, held, sems, piece)
    for copy in (copies[2], copies[0], copies[1]):
        copy.start()
    for s in range(count):
        grads_ref[s * cap : (s + 1) * cap, :] = grads_in[s][...]
    copies[2].wait()
    grad_hidden = dot(grads_ref[...], held[2])
    gate = gate_up_ref[:, :piece]
    up = gate_up_ref[:, piece:]
    slope = 1.0 / (1.0 + jnp.exp(-gate))
    grad_gate = (grad_hidden * up * slope * (1.0 + gate * (1.0 - slope))).astype(BF)
    grad_up = (grad_hidden * gate * slope).astype(BF)
    rows_ref[:, :piece] = grad_gate
    rows_ref[:, piece:] = grad_up
    copies[0].wait()
    total = dot_nt(grad_gate, held[0])
    copies[1].wait()
    total = (total + dot_nt(grad_up, held[1])).astype(BF)
    for s in range(count):
        out_refs[s][...] = total[s * cap : (s + 1) * cap, :]


def experts_backward(blocks, gate_up, weights, piece):
    count = len(blocks)
    cap, width = blocks[0].shape
    rows = count * cap
    in_vmem = pl.BlockSpec(memory_space=pltpu.VMEM)
    return pl.pallas_call(
        functools.partial(experts_backward_kernel, count),
        in_specs=[in_vmem] * (count + 1) + [pl.BlockSpec(memory_space=pltpu.HBM)],
        out_specs=[in_vmem] * (2 + count),
        out_shape=[
            jax.ShapeDtypeStruct((rows, width), BF),
            jax.ShapeDtypeStruct((rows, 2 * piece), BF),
        ]
        + [jax.ShapeDtypeStruct((cap, width), BF)] * count,
        scratch_shapes=[pltpu.VMEM((3, width, piece), BF), pltpu.SemaphoreType.DMA((3,))],
        compiler_params=pltpu.CompilerParams(vmem_limit_bytes=56 * 1024 * 1024),
        cost_estimate=pl.CostEstimate(flops=0, bytes_accessed=0, transcendentals=0),
    )(*blocks, gate_up, weights)


def kv_pair_kernel(heads, chips, *refs):
    near, there, outs = refs[:heads], refs[heads : 2 * heads], refs[2 * heads :]
    for m in range(chips):
        for g in range(heads):
            total = near[g][m].astype(F32) + there[g][m].astype(F32)
            outs[m][:, g * 2 * HD : (g + 1) * 2 * HD] = total.astype(outs[m].dtype)


def kv_pair_sums(near, there):
    heads, (chips, rows, cols) = len(near), near[0].shape
    in_vmem = pl.BlockSpec(memory_space=pltpu.VMEM)
    out = jax.ShapeDtypeStruct((rows, heads * cols), BF)
    return pl.pallas_call(
        functools.partial(kv_pair_kernel, heads, chips),
        in_specs=[in_vmem] * (2 * heads),
        out_specs=[in_vmem] * chips,
        out_shape=[jax.ShapeDtypeStruct((rows, heads * cols), F32)] + [out] * (chips - 1),
        compiler_params=pltpu.CompilerParams(vmem_limit_bytes=20 * 1024 * 1024),
        cost_estimate=pl.CostEstimate(flops=0, bytes_accessed=0, transcendentals=0),
    )(*near, *there)


def head_columns_kernel(heads, chips, *refs):
    queries, sums = refs[:heads], refs[heads : heads + chips]
    factor_ref, ride_ref, sent_ref, columns_ref = refs[heads + chips :]
    query = jnp.concatenate([each[...] for each in queries], axis=1)
    keyval = sums[0][...]
    for each in sums[1:]:
        keyval = keyval + each[...].astype(F32)
    both = jnp.concatenate([query, keyval], axis=1)
    rows, cols = both.shape
    sent_ref[...] = both.astype(BF)
    columns_ref[:rows, :cols] = (both * factor_ref[...]).astype(BF)
    columns_ref[:rows, cols:] = jnp.zeros((rows, LANES), BF)
    columns_ref[rows:, :cols] = jnp.zeros((ride_ref.shape[0], cols), BF)
    columns_ref[rows:, cols:] = ride_ref[...]


def head_columns(queries, sums, factor, ride):
    rows = sums[0].shape[0]
    cols = sum(each.shape[1] for each in queries) + sums[0].shape[1]
    if cols % LANES:
        both = jnp.concatenate(list(queries) + [total_of(sums)], axis=1)
        scaled = jnp.pad((both * factor).astype(BF), ((0, 0), (0, LANES)))
        return both.astype(BF), jnp.concatenate([scaled, jnp.pad(ride, ((0, 0), (cols, 0)))])
    in_vmem = pl.BlockSpec(memory_space=pltpu.VMEM)
    return pl.pallas_call(
        functools.partial(head_columns_kernel, len(queries), len(sums)),
        in_specs=[in_vmem] * (len(queries) + len(sums) + 2),
        out_specs=[in_vmem] * 2,
        out_shape=[
            jax.ShapeDtypeStruct((rows, cols), BF),
            jax.ShapeDtypeStruct((rows + ride.shape[0], cols + LANES), BF),
        ],
        compiler_params=pltpu.CompilerParams(vmem_limit_bytes=20 * 1024 * 1024),
        cost_estimate=pl.CostEstimate(flops=0, bytes_accessed=0, transcendentals=0),
    )(*queries, *sums, factor, ride)


def two_parts(value):
    high = value.astype(BF)
    return high, (value - high.astype(F32)).astype(BF)


def mark_kernel(seed_ref, out_ref):
    out_ref[...] = seed_ref[...]


def mark(*others):
    seed = after(jnp.zeros((8, LANES), F32), *others)
    return pl.pallas_call(
        mark_kernel,
        out_shape=jax.ShapeDtypeStruct((8, LANES), F32),
        cost_estimate=pl.CostEstimate(flops=10**12, bytes_accessed=8192, transcendentals=0),
    )(seed)


def by_rows(array):
    return with_layout_constraint(array, Layout(major_to_minor=tuple(range(array.ndim))))


def after(values, *others):
    return lax.optimization_barrier((values, others))[0]


def root(values):
    return lax.rsqrt(jnp.mean(values * values, axis=-1, keepdims=True) + EPSILON)


def root_back(values, factor, grad_scaled):
    inner = jnp.mean(grad_scaled * values, axis=-1, keepdims=True)
    return factor * grad_scaled - values * (factor * factor * factor * inner)


def place_gate_up_kernel(count, place_ref, *refs):
    blocks = refs[: 2 * count - 1]
    weight_ref, gain_ref, out_ref, sums_ref, base = refs[2 * count - 1 :]
    offset = place_ref[0] - pl.program_id(1)

    for s in range(2 * count - 1):

        @pl.when(offset == (s if s < count else count - 1 - s))
        def _(s=s):
            base[...] = blocks[s][...].astype(F32)

    @pl.when((pl.program_id(0) == 0) & (pl.program_id(1) == 0))
    def _():
        sums_ref[...] = jnp.zeros_like(sums_ref)

    values = base[...]
    out_ref[0] = values * gain_ref[...]
    product = jnp.sum(weight_ref[0].astype(F32) * values, axis=1, keepdims=True)
    sums_ref[...] += jnp.broadcast_to(product, sums_ref.shape)


def place_gate_up(steps, weight, gain, place):
    experts, part, both = weight.shape
    count = len(steps)
    split = count // experts
    if split == 1:
        tile = math.gcd(both, 1024)
        blocks = [steps[0][0]] + [each[0] for each in steps[1:]] + [each[1] for each in steps[1:]]
        block = pl.BlockSpec((part, tile), lambda t, e: (0, t))
        out, sums = pl.pallas_call(
            functools.partial(place_gate_up_kernel, count),
            grid=(both // tile, experts),
            in_specs=[pl.BlockSpec(memory_space=pltpu.SMEM)]
            + [block] * len(blocks)
            + [
                pl.BlockSpec((1, part, tile), lambda t, e: (e, 0, t)),
                pl.BlockSpec((part, 1), lambda t, e: (0, 0)),
            ],
            out_specs=[
                pl.BlockSpec((1, part, tile), lambda t, e: (e, 0, t)),
                pl.BlockSpec((part, LANES), lambda t, e: (0, 0)),
            ],
            out_shape=[
                jax.ShapeDtypeStruct(weight.shape, F32),
                jax.ShapeDtypeStruct((part, LANES), F32),
            ],
            scratch_shapes=[pltpu.VMEM((part, tile), F32)],
            compiler_params=pltpu.CompilerParams(vmem_limit_bytes=28 * 1024 * 1024),
            cost_estimate=pl.CostEstimate(flops=0, bytes_accessed=0, transcendentals=0),
        )(place.astype(jnp.int32).reshape(1), *blocks, weight, gain)
        return out, sums[:, 0]
    blocks = [steps[0][0]] + [
        jnp.where(place >= s, steps[s][0], steps[count - s][1]) for s in range(1, count)
    ]
    base = (
        from_relative(blocks, place)
        .reshape(experts, split, part, 2, both // (2 * split))
        .transpose(0, 2, 3, 1, 4)
        .reshape(experts, part, both)
        .astype(F32)
    )
    return base * gain, jnp.sum(weight.astype(F32) * base, axis=(0, 2))


def place_kernel(count, q_cols, kv_cols, place_ref, *refs):
    blocks, outs = refs[:count], refs[count : 2 * count]
    w_query_ref, w_keyval_ref, gain_ref, query_ref, keyval_ref, out_ref, base_ref, sums_ref = refs[
        2 * count :
    ]
    gain = gain_ref[...]
    base = jnp.zeros_like(gain)
    sums = jnp.zeros(sums_ref.shape, F32)
    for s in range(count):
        owner = lax.rem(place_ref[0] + (count - s), count)
        q_at = pl.ds(pl.multiple_of(owner * q_cols, LANES), q_cols)
        kv_at = pl.ds(pl.multiple_of(owner * kv_cols, LANES), kv_cols)
        query = blocks[s][:, :q_cols].astype(F32)
        keyval = blocks[s][:, q_cols : q_cols + kv_cols].astype(F32)
        start = q_cols + kv_cols
        sums = sums + blocks[s][:, start : start + LANES].astype(F32)
        out_ref[:, q_at] = outs[s][...].astype(F32)
        base = base + jnp.sum(w_query_ref[:, q_at].astype(F32) * query, axis=1, keepdims=True)
        base = base + jnp.sum(w_keyval_ref[:, kv_at].astype(F32) * keyval, axis=1, keepdims=True)
        query_ref[:, q_at] = query * gain
        keyval_ref[:, kv_at] = keyval * gain
    base_ref[...] = jnp.broadcast_to(base, base_ref.shape)
    sums_ref[...] = sums


def place_heads(blocks, outs, place, w_query, w_keyval, gain, q_cols, kv_cols):
    count = len(blocks)
    part = w_query.shape[0]
    start = q_cols + kv_cols
    if q_cols % LANES == 0 and kv_cols % LANES == 0:
        wide = jax.ShapeDtypeStruct((part, count * q_cols), F32)
        narrow = jax.ShapeDtypeStruct((part, count * kv_cols), F32)
        lanes = jax.ShapeDtypeStruct((part, LANES), F32)
        in_vmem = pl.BlockSpec(memory_space=pltpu.VMEM)
        query, keyval, out, base, sums = pl.pallas_call(
            functools.partial(place_kernel, count, q_cols, kv_cols),
            in_specs=[pl.BlockSpec(memory_space=pltpu.SMEM)] + [in_vmem] * (2 * count + 3),
            out_specs=[in_vmem] * 5,
            out_shape=[wide, narrow, wide, lanes, lanes],
            compiler_params=pltpu.CompilerParams(vmem_limit_bytes=24 * 1024 * 1024),
            cost_estimate=pl.CostEstimate(flops=0, bytes_accessed=0, transcendentals=0),
        )(place.astype(jnp.int32).reshape(1), *blocks, *outs, w_query, w_keyval, gain)
        return query, keyval, out, base[:, 0], sums
    blocks = from_relative(blocks, place).astype(F32)
    outs = from_relative(outs, place).astype(F32)

    def columns(begin, end):
        return blocks[:, :, begin:end].transpose(1, 0, 2).reshape(part, count * (end - begin))

    query, keyval = columns(0, q_cols), columns(q_cols, start)
    base = jnp.sum(w_query.astype(F32) * query, axis=1) + jnp.sum(
        w_keyval.astype(F32) * keyval, axis=1
    )
    sums = jnp.sum(blocks[:, :, start : start + LANES], axis=0)
    out = outs.transpose(1, 0, 2).reshape(part, count * q_cols)
    return query * gain, keyval * gain, out, base, sums


def local(
    tokens,
    teacher,
    valid,
    routes,
    slots,
    gain_attn,
    w_query,
    w_keyval,
    w_out,
    gain_ffn,
    w_router,
    w_gate_up,
    w_down,
):
    seqs = lax.axis_size("seq")
    shards = lax.axis_size("fsdp")
    z = lax.axis_index("seq")
    shard = lax.axis_index("fsdp")
    rows, width = tokens.shape
    groups = HEADS // KVH
    local_kv = KVH // seqs
    q_cols = local_kv * groups * HD
    kv_cols = local_kv * 2 * HD
    local_rows = rows * seqs
    seq_len = local_rows * shards
    experts, part, both = w_gate_up.shape
    units = both // 2
    split = seqs // experts
    piece = units // split
    expert = z // split
    fraction = z % split
    scale = HD ** (-0.5)

    gain_one = gain_attn.astype(F32)[:, None]
    gain_two = gain_ffn.astype(F32)[:, None]
    heads_shard = jnp.concatenate(
        [
            lax.dynamic_slice_in_dim(w_query, z * q_cols, q_cols, 1),
            lax.dynamic_slice_in_dim(w_keyval, z * kv_cols, kv_cols, 1),
        ],
        axis=1,
    )
    heads_shard = (heads_shard.astype(F32) * gain_one).astype(BF)
    heads_full = lax.all_gather(heads_shard, "fsdp", axis=0, tiled=True)
    valid_row = jnp.pad(valid.astype(BF).reshape(1, rows), ((0, 7), (0, width - rows)))
    token_rows = jnp.concatenate([tokens, valid_row], axis=0)
    token_mark = mark(token_rows)
    token_blocks = after(send_out([token_rows] * seqs, seqs), token_mark)

    valid_local = from_relative([each[rows : rows + 1, :rows] for each in token_blocks], z)
    projected = []
    for block in token_blocks:
        projected.append(dot(block[:rows], heads_full) * root(block[:rows].astype(F32)))
    projected = from_relative([each.astype(BF) for each in projected], z)
    projected = projected.reshape(local_rows, q_cols + kv_cols)
    head_queries = projected[:, :q_cols] * jnp.asarray(scale, BF)

    valid_rows_kv = local_rows // kv_cols
    payload = jnp.concatenate(
        [
            projected[:, q_cols:],
            valid_local.reshape(valid_rows_kv, kv_cols),
            jnp.zeros((16 - valid_rows_kv, kv_cols), BF),
        ],
        axis=0,
    )
    kv_blocks = gather_shards(payload, shards)
    late_query, late_keyval, late_router, late_gate_up, late_down = after(
        (w_query, w_keyval, w_router, w_gate_up, w_down), token_mark
    )
    out_full = lax.all_gather(w_out, "fsdp", axis=1, tiled=True)
    own_expert = take(late_gate_up, expert, 0)
    gate_shard = lax.dynamic_slice_in_dim(own_expert, fraction * piece, piece, 1)
    up_shard = lax.dynamic_slice_in_dim(own_expert, units + fraction * piece, piece, 1)
    down_shard = lax.dynamic_slice_in_dim(take(late_down, expert, 0), fraction * piece, piece, 0).T
    router_shard = jnp.pad((late_router.astype(F32) * gain_two).astype(BF), ((0, 0), (0, LANES - experts)))
    expert_shard = jnp.concatenate(
        [
            (gate_shard.astype(F32) * gain_two).astype(BF),
            (up_shard.astype(F32) * gain_two).astype(BF),
            down_shard,
            router_shard,
        ],
        axis=1,
    )
    expert_full = lax.all_gather(expert_shard, "fsdp", axis=0, tiled=True)
    router_full = expert_full[:, 3 * piece :]
    attn_shard = jnp.concatenate(
        [
            each
            for s in range(seqs)
            for each in (
                late_query[:, s * q_cols : (s + 1) * q_cols],
                late_keyval[:, s * kv_cols : (s + 1) * kv_cols],
            )
        ],
        axis=1,
    )
    attn_full = lax.all_gather(
        (attn_shard.astype(F32) * gain_one).astype(BF), "fsdp", axis=0, tiled=True
    )
    order = jnp.asarray(
        [2 * m for m in range(shards // 2)] + [2 * m + 1 for m in range(shards // 2)], jnp.int32
    )
    valid_all = jnp.stack(
        [
            each[local_rows : local_rows + valid_rows_kv].reshape(seqs, rows)
            for each in kv_blocks
        ],
        axis=1,
    ).astype(F32)
    valid_count = jnp.sum(valid_all)
    bias = jnp.where(valid_all > 0, 0.0, FLOOR_SCORE)
    earlier = ((order ^ shard) < shard) | (order == 0)
    bias_same = jnp.where(earlier[None, :, None], bias, FLOOR_SCORE)
    bias = jnp.concatenate([bias, bias_same]).reshape(2 * seqs, 1, shards * rows)
    attended_low, lse = flash_forward(
        head_queries, kv_blocks, bias, seqs, rows, local_kv, groups
    )
    attended = lax.all_to_all(attended_low, "seq", split_axis=0, concat_axis=1, tiled=True)

    inputs = tokens.astype(F32)
    residual = inputs + dot(attended, out_full)
    factor_two = root(residual)
    normed_two = (residual * factor_two).astype(BF)
    logits = dot(normed_two, router_full)[:, :experts]
    expert_ids = jnp.arange(experts, dtype=jnp.int32)
    picked = (routes[:, :, None] == expert_ids).astype(F32)
    chosen = jnp.sum(picked * logits[:, None, :], axis=-1)
    gating = jax.nn.softmax(chosen, axis=-1)
    owners = ((jnp.arange(seqs, dtype=jnp.int32) + z) % seqs) // split
    to_owner = routes[:, :, None] == owners
    slot_hot = slots[:, :, None] == jnp.arange(CAP, dtype=jnp.int32)
    placed = (to_owner[:, :, :, None] & slot_hot[:, :, None, :]).astype(BF)
    placed = placed.reshape(rows, 2, seqs * CAP)
    dispatch = placed[:, 0] + placed[:, 1]
    placed_pairs = jnp.concatenate([placed[:, 0], placed[:, 1]], axis=0)
    sent_rows = dot_tn(dispatch, normed_two).astype(BF)
    kv_all = jnp.stack(after(kv_blocks, sent_rows))
    sent_rows = sent_rows.reshape(seqs, CAP, width)
    expert_rows, gate_up, hidden, *expert_out = experts_forward(
        send_out([sent_rows[s] for s in range(seqs)], seqs), expert_full, piece
    )
    returned = jnp.concatenate(after(send_back(expert_out, seqs), kv_all))
    selected = dot(placed_pairs, returned).reshape(2, rows, width)
    mixed_exact = residual + gating[:, :1] * selected[0] + gating[:, 1:] * selected[1]
    valid_rows = valid.astype(F32)
    errors = (mixed_exact - teacher.astype(F32)) * valid_rows[:, None]
    squares = jnp.sum(errors * errors)
    loss_scale = width * seq_len // 8
    grad_mixed = errors * (2.0 * loss_scale / (width * valid_count))

    grad_gating = jnp.stack(
        [jnp.sum(selected[0] * grad_mixed, axis=-1), jnp.sum(selected[1] * grad_mixed, axis=-1)],
        axis=1,
    )
    grad_chosen = gating * (grad_gating - jnp.sum(gating * grad_gating, axis=-1, keepdims=True))
    grad_logits = jnp.sum(grad_chosen[:, :, None] * picked, axis=1).astype(BF)
    grad_logits = jnp.pad(grad_logits, ((0, 0), (0, LANES - experts)))
    weighted = jnp.concatenate(
        [(gating[:, :1] * grad_mixed).astype(BF), (gating[:, 1:] * grad_mixed).astype(BF)], axis=0
    )
    sent_grads = dot_tn(placed_pairs, weighted).astype(BF).reshape(seqs, CAP, width)
    grad_out_rows = send_out([sent_grads[s] for s in range(seqs)], seqs)
    grad_out_rows = after(grad_out_rows, attn_full, grad_logits)
    grad_expert_out, grad_gate_up_rows, *grad_rows = experts_backward(
        grad_out_rows, gate_up, expert_full, piece
    )
    grad_returned = send_back(grad_rows, seqs)
    tokens_local = from_relative(
        [each[:rows] for each in after(token_blocks, grad_rows)], z
    ).reshape(local_rows, width)
    factor_local = root(tokens_local.astype(F32))
    ride_rows = jnp.concatenate([normed_two, jnp.ones((16, width), BF)], axis=0)
    product_rows = jnp.concatenate([tokens_local, ride_rows], axis=0)
    high, low = two_parts(squares)
    lane = jnp.arange(LANES, dtype=jnp.int32)[None, :]
    marks = jnp.where(lane == experts + 2 * (shard % 2), high, 0) + jnp.where(
        lane == experts + 1 + 2 * (shard % 2), low, 0
    )
    ride_columns = jnp.concatenate(
        [grad_logits, marks.astype(BF), jnp.zeros((15, LANES), BF)], axis=0
    )
    held_out, held_hidden = after((grad_expert_out, hidden), grad_rows)
    down_far, down_near = split_product(held_out, held_hidden, shard, shards)
    grad_down_sums = pair_sums(down_near, hop(down_far, shards, 1), shard)
    held_rows, held_gate_up = after((expert_rows, grad_gate_up_rows), grad_rows)
    gate_up_far, gate_up_near = split_product(held_rows, held_gate_up, shard, shards)
    grad_gate_up_sums = pair_sums(gate_up_near, hop(gate_up_far, shards, 1), shard)
    grad_down_blocks = send_chips(grad_down_sums, shards)
    grad_returned = jnp.concatenate(after(grad_returned, grad_down_sums, product_rows, ride_columns, factor_local))
    grad_normed_two = dot(dispatch, grad_returned) + dot_nt(grad_logits, router_full)
    grad_residual = grad_mixed + root_back(residual, factor_two, grad_normed_two)
    grad_branch = grad_residual.astype(BF)
    grad_attended = dot_nt(after(grad_branch, grad_gate_up_sums), out_full).astype(BF)
    head_grad = lax.all_to_all(grad_attended, "seq", split_axis=1, concat_axis=0, tiled=True)
    grad_gate_up_blocks = send_chips(grad_gate_up_sums, shards)
    grad_down_shard = total_of(after(grad_down_blocks, grad_attended)).astype(BF)
    grad_down = lax.all_gather(grad_down_shard, "seq", axis=0, tiled=False)

    out_far, out_near = split_product(
        after(grad_branch, grad_attended), attended, shard, shards
    )
    grad_q, near, far = [], [], []
    held = after(head_grad, grad_down_shard)
    for g in range(local_kv):
        part_q, near_kv, far_kv = flash_backward(
            head_queries, kv_all, bias, held, attended_low, lse, seqs, rows, g, groups
        )
        if g == 0:
            grad_gate_up_blocks = after(grad_gate_up_blocks, part_q)
            grad_gate_up_shard = total_of(grad_gate_up_blocks).astype(BF)
            steps = [(grad_gate_up_shard, grad_gate_up_shard)]
            steps.append(relay_step(steps[0], seqs))
            out_there = hop(after(out_far, head_grad), shards, 1)
        grad_q.append(part_q)
        near.append(near_kv)
        far.append(far_kv)
        held = after(head_grad, grad_gate_up_shard, out_there)
    steps[1] = after(steps[1], part_q)
    steps.append(relay_step(steps[1], seqs))
    far = after(far, steps[1], grad_down)
    pairs = kv_pair_sums(near, [hop(each, shards, 1) for each in far])
    out_sums = pair_sums(out_near, after(out_there, pairs), shard)
    sent_grads, product_columns = head_columns(
        grad_q, after(send_chips(pairs, shards), out_sums, steps[2]), factor_local, ride_columns
    )
    steps[2] = after(steps[2], product_columns)
    while len(steps) < seqs:
        steps.append(relay_step(steps[-1], seqs))
    token_grads = lax.all_to_all(sent_grads, "seq", split_axis=0, concat_axis=1, tiled=True)

    head_cols = q_cols + kv_cols
    head_far, head_near = split_product(product_rows, product_columns, shard, shards)
    head_sums = pair_sums(head_near, hop(head_far, shards, 1), shard)
    head_blocks = send_chips(head_sums, shards)
    head_part = total_of(head_blocks)
    grad_normed = dot_nt(after(token_grads, head_part), attn_full)
    grad_tokens = grad_residual + root_back(inputs, root(inputs), grad_normed)
    base_cols = head_cols + experts
    plane_high, plane_low = two_parts(
        jnp.sum(head_part[:1, base_cols : base_cols + 4], axis=1, keepdims=True)
    )
    lanes = lax.broadcasted_iota(jnp.int32, head_part.shape, 1)
    head_part = jnp.where(
        lanes == base_cols,
        plane_high.astype(F32),
        jnp.where(lanes == base_cols + 1, plane_low.astype(F32), head_part),
    )
    head_part = by_rows(head_part.astype(BF))
    head_last = [by_rows(each) for each in send_out([head_part] * seqs, seqs)]
    out_blocks = send_chips(after(out_sums, head_part, steps[3]), shards)
    out_part = total_of(out_blocks).astype(BF)
    out_parts = lax.all_to_all(
        out_part.reshape(part, seqs, q_cols), "seq", split_axis=1, concat_axis=1, tiled=True
    )
    out_own = by_rows(jnp.sum(out_parts.astype(F32), axis=1).astype(BF))
    grad_gate_up, grad_gain_ffn = place_gate_up(after(steps, head_part), w_gate_up, gain_two, z)
    out_own = after(out_own, grad_gate_up)
    out_last = [by_rows(each) for each in send_out([out_own] * seqs, seqs)]
    grad_query, grad_keyval, grad_out, grad_gain_attn, sums = place_heads(
        head_last, out_last, z, w_query, w_keyval, gain_one, q_cols, kv_cols
    )
    loss_value = jnp.sum(sums[0, experts : experts + 2]) / (width * valid_count)
    grad_router_base = sums[:, :experts]
    grad_down = (
        after(grad_down, head_part).reshape(experts, split, part, piece)
        .transpose(0, 1, 3, 2)
        .reshape(experts, units, part)
        .astype(F32)
    )
    grad_gain_ffn = grad_gain_ffn + jnp.sum(w_router.astype(F32) * grad_router_base, axis=1)
    return (
        mixed_exact.astype(BF),
        loss_value,
        grad_tokens,
        grad_gain_attn,
        grad_query,
        grad_keyval,
        grad_out.T,
        grad_gain_ffn,
        grad_router_base * gain_two,
        grad_gate_up,
        grad_down,
    )


def solution(mesh):
    return jax.shard_map(
        local,
        mesh=mesh,
        in_specs=(
            P(("seq", "fsdp"), None),
            P(("seq", "fsdp"), None),
            P(("seq", "fsdp")),
            P(("seq", "fsdp"), None),
            P(("seq", "fsdp"), None),
            P("fsdp"),
            P("fsdp", None),
            P("fsdp", None),
            P(None, "fsdp"),
            P("fsdp"),
            P("fsdp", None),
            P(None, "fsdp", None),
            P(None, None, "fsdp"),
        ),
        out_specs=(
            P(("seq", "fsdp"), None),
            P(),
            P(("seq", "fsdp"), None),
            P("fsdp"),
            P("fsdp", None),
            P("fsdp", None),
            P(None, "fsdp"),
            P("fsdp"),
            P("fsdp", None),
            P(None, "fsdp", None),
            P(None, None, "fsdp"),
        ),
        check_vma=False,
    )
```

```python
import functools
import math

import jax
import jax.numpy as jnp
from jax import lax
from jax.experimental import pallas as pl
from jax.experimental.layout import Layout, with_layout_constraint
from jax.experimental.pallas import tpu as pltpu
from jax.sharding import PartitionSpec as P

HEADS = 24
KVH = 8
HD = 64
CAP = 96
LANES = 128
EPSILON = 1e-06
FLOOR_SCORE = -1e30
BF = jnp.bfloat16
F32 = jnp.float32


def dot(a, b):
    return jnp.dot(a, b, preferred_element_type=F32)


def dot_nt(a, b):
    return lax.dot_general(a, b, (((1,), (1,)), ((), ())), preferred_element_type=F32)


def dot_tn(a, b):
    return lax.dot_general(a, b, (((0,), (0,)), ((), ())), preferred_element_type=F32)


def own_mask(valid_row, rows):
    i = lax.broadcasted_iota(jnp.int32, (rows, rows), 0)
    j = lax.broadcasted_iota(jnp.int32, (rows, rows), 1)
    return jnp.where(j == i, 0.0, jnp.where(j < i, valid_row, FLOOR_SCORE))


def key_chunk(kv_refs, zk, rows, g):
    return jnp.concatenate(
        [ref[pl.ds(zk * rows, rows), pl.ds(g * 2 * HD, 2 * HD)] for ref in kv_refs], axis=0
    )


def forward_kernel(shards, seqs, rows, local_kv, groups, *refs):
    kv_refs = refs[:shards]
    q_ref, bias_ref, low_ref, lse_ref, acc_ref, max_ref = refs[shards:]
    zq = pl.program_id(0)
    stack = groups * rows
    zeros = jnp.zeros((rows, HD), BF)
    half = lax.broadcasted_iota(jnp.int32, (1, 2 * HD), 1) < HD

    def queries(g):
        parts = []
        for h in range(groups):
            start = (g * groups + h) * HD
            parts.append(jnp.concatenate([q_ref[:, start : start + HD], zeros], axis=1))
        return jnp.concatenate(parts, axis=0)

    def chunk(g, zk, scores):
        first = scores is None
        keys = key_chunk(kv_refs, zk, rows, g)
        raw = dot_nt(queries(g), keys)
        if first:
            row = bias_ref[seqs + zk]
            mask = own_mask(row[:, :rows], rows)
            mask = jnp.concatenate([mask] * groups, axis=0)
            masked = jnp.concatenate([raw[:, :rows] + mask, raw[:, rows:] + row[:, rows:]], axis=1)
            new_max = jnp.max(masked, axis=1, keepdims=True)
        else:
            masked = raw + bias_ref[zk]
            new_max = jnp.maximum(max_ref[g][:, :1], jnp.max(masked, axis=1, keepdims=True))
        terms = jnp.exp(masked - new_max).astype(BF)
        ones_values = jnp.where(half, jnp.ones_like(keys), keys)
        part = dot(terms, ones_values)
        if first:
            acc_ref[g] = part
        else:
            acc_ref[g] = acc_ref[g] * jnp.exp(max_ref[g][:, :1] - new_max) + part
        max_ref[g] = jnp.broadcast_to(new_max, (stack, 2 * HD))

    for g in range(local_kv):
        chunk(g, zq, None)

    @pl.loop(0, zq)
    def _(zk):
        for g in range(local_kv):
            chunk(g, zk, True)

    exact_parts, lse_parts = [], []
    for g in range(local_kv):
        acc = acc_ref[g]
        total = acc[:, :HD]
        exact = acc[:, HD:] / total
        lse = max_ref[g][:, :HD] + jnp.log(total)
        for h in range(groups):
            exact_parts.append(exact[h * rows : (h + 1) * rows])
            lse_parts.append(lse[h * rows : (h + 1) * rows])
    low_ref[...] = jnp.concatenate(exact_parts, axis=1).astype(BF)
    lse_ref[...] = jnp.concatenate(lse_parts, axis=1)


def flash_forward(q, kv_blocks, bias, seqs, rows, local_kv, groups):
    shards = len(kv_blocks)
    q_cols = q.shape[1]
    kv_spec = pl.BlockSpec(kv_blocks[0].shape, lambda i: (0, 0))
    q_spec = pl.BlockSpec((rows, q_cols), lambda i: (i, 0))
    stack = groups * rows
    out = jax.ShapeDtypeStruct((seqs * rows, q_cols), F32)
    return pl.pallas_call(
        functools.partial(forward_kernel, shards, seqs, rows, local_kv, groups),
        grid=(seqs,),
        in_specs=[kv_spec] * shards + [q_spec, pl.BlockSpec(bias.shape, lambda i: (0, 0, 0))],
        out_specs=[q_spec] * 2,
        out_shape=[jax.ShapeDtypeStruct((seqs * rows, q_cols), BF), out],
        scratch_shapes=[
            pltpu.VMEM((local_kv, stack, 2 * HD), F32),
            pltpu.VMEM((local_kv, stack, 2 * HD), F32),
        ],
        compiler_params=pltpu.CompilerParams(vmem_limit_bytes=24 * 1024 * 1024),
        cost_estimate=pl.CostEstimate(
            flops=0,
            bytes_accessed=0,
            transcendentals=0,
        ),
    )(*kv_blocks, q, bias)


def backward_kernel(shards, seqs, rows, g, groups, *refs):
    kv_refs = [refs[0].at[p] for p in range(shards)]
    (
        q_ref, bias_ref, grad_ref, low_ref, lse_ref, grad_q_ref, near_ref, far_ref,
        pair_ref, pair_t_ref, lse_wide, delta_wide, acc_q, acc_kv,
    ) = refs[1:]
    zk = pl.program_id(0)
    stack = groups * rows
    zeros = jnp.zeros((rows, HD), BF)

    @pl.when(zk == 0)
    def _():
        acc_q[...] = jnp.zeros_like(acc_q)

        @pl.loop(0, seqs)
        def _(zq):
            here = pl.ds(zq * rows, rows)
            tops, bottoms = [], []
            for h in range(groups):
                cols = slice((g * groups + h) * HD, (g * groups + h + 1) * HD)
                grad = grad_ref[here, cols]
                tops.append(jnp.concatenate([q_ref[here, cols], zeros], axis=1))
                bottoms.append(jnp.concatenate([zeros, grad], axis=1))
                delta = jnp.sum(grad.astype(F32) * low_ref[here, cols].astype(F32), axis=1, keepdims=True)
                part = slice(h * rows, (h + 1) * rows)
                delta_wide[zq, part] = jnp.broadcast_to(delta, (rows, 2 * HD))
                lse_wide[zq, part] = jnp.broadcast_to(lse_ref[here, cols][:, :1], (rows, 2 * HD))
            pair = jnp.concatenate(tops + bottoms, axis=0)
            pair_ref[zq] = pair
            pair_t_ref[zq] = pair.astype(F32).T.astype(BF)

    def chunk(zq, first):
        keys = key_chunk(kv_refs, zk, rows, g)
        both = dot_nt(pair_ref[zq], keys)
        raw, products = both[:stack], both[stack:]
        if first:
            row = bias_ref[seqs + zk]
            mask = own_mask(row[:, :rows], rows)
            mask = jnp.concatenate([mask] * groups, axis=0)
            masked = jnp.concatenate([raw[:, :rows] + mask, raw[:, rows:] + row[:, rows:]], axis=1)
        else:
            masked = raw + bias_ref[zk]
        weights = jnp.exp(masked - lse_wide[zq][:, :1])
        grads = (weights * (products - delta_wide[zq][:, :1])).astype(BF)
        acc_q[zq] += dot(grads, keys)
        part = dot(pair_t_ref[zq], jnp.concatenate([grads, weights.astype(BF)], axis=0))
        if first:
            acc_kv[...] = part
        else:
            acc_kv[...] += part

    chunk(zk, True)

    @pl.loop(zk + 1, seqs)
    def _(zq):
        chunk(zq, False)

    for p in range(shards):
        target = near_ref if p < shards // 2 else far_ref
        target[p % (shards // 2)] = acc_kv[:, p * rows : (p + 1) * rows].T.astype(BF)

    @pl.when(zk == seqs - 1)
    def _():
        @pl.loop(0, seqs)
        def _(zq):
            total = acc_q[zq]
            parts = [total[h * rows : (h + 1) * rows, :HD] for h in range(groups)]
            grad_q_ref[pl.ds(zq * rows, rows), :] = jnp.concatenate(parts, axis=1) * HD ** (-0.5)


def flash_backward(q, kv_all, bias, grad, low, lse, seqs, rows, g, groups):
    shards = kv_all.shape[0]
    q_cols = q.shape[1]
    stack = groups * rows
    kv_spec = pl.BlockSpec(kv_all.shape, lambda i: (0, 0, 0))
    whole = pl.BlockSpec((seqs * rows, q_cols), lambda i: (0, 0))
    grad_q_shape = (seqs * rows, groups * HD)
    out_spec = pl.BlockSpec((shards // 2, rows, 2 * HD), lambda i: (0, i, 0))
    out = jax.ShapeDtypeStruct((shards // 2, seqs * rows, 2 * HD), BF)
    return pl.pallas_call(
        functools.partial(backward_kernel, shards, seqs, rows, g, groups),
        grid=(seqs,),
        in_specs=[kv_spec]
        + [whole, pl.BlockSpec(bias.shape, lambda i: (0, 0, 0)), whole, whole, whole],
        out_specs=[pl.BlockSpec(grad_q_shape, lambda i: (0, 0)), out_spec, out_spec],
        out_shape=[jax.ShapeDtypeStruct(grad_q_shape, F32), out, out],
        scratch_shapes=[
            pltpu.VMEM((seqs, 2 * stack, 2 * HD), BF),
            pltpu.VMEM((seqs, 2 * HD, 2 * stack), BF),
            pltpu.VMEM((seqs, stack, 2 * HD), F32),
            pltpu.VMEM((seqs, stack, 2 * HD), F32),
            pltpu.VMEM((seqs, stack, 2 * HD), F32),
            pltpu.VMEM((2 * HD, shards * rows), F32),
        ],
        compiler_params=pltpu.CompilerParams(vmem_limit_bytes=28 * 1024 * 1024),
        cost_estimate=pl.CostEstimate(
            flops=0 if g else 10**12,
            bytes_accessed=0,
            transcendentals=0,
        ),
    )(kv_all, q, bias, grad, low, lse)


def shift(block, count, step):
    return lax.ppermute(block, "seq", [(i, (i + step) % count) for i in range(count)])


def send_out(blocks, count):
    return [blocks[0]] + [shift(blocks[s], count, s) for s in range(1, count)]


def send_back(blocks, count):
    return [blocks[0]] + [shift(blocks[s], count, count - s) for s in range(1, count)]


def relay_step(blocks, count):
    up, down = blocks
    return (
        lax.ppermute(up, "seq", [(i, i + 1) for i in range(count - 1)]),
        lax.ppermute(down, "seq", [(i + 1, i) for i in range(count - 1)]),
    )


def from_relative(blocks, place):
    count = len(blocks)
    rising = jnp.stack([blocks[-s % count] for s in range(count)])
    return lax.dynamic_slice_in_dim(jnp.concatenate([rising, rising]), count - place, count, 0)


def hop(block, count, mask):
    return lax.ppermute(block, "fsdp", [(i, i ^ mask) for i in range(count)])


def gather_shards(block, count):
    near = [block] + [hop(block, count, 2 * m) for m in range(1, count // 2)]
    return near + [hop(each, count, 1) for each in near]


def send_chips(parts, count):
    return [parts[0]] + [hop(parts[m], count, 2 * m) for m in range(1, count // 2)]


def total_of(blocks):
    total = blocks[0].astype(F32)
    for each in blocks[1:]:
        total = total + each.astype(F32)
    return total


def take(array, index, axis):
    return lax.dynamic_index_in_dim(array, index, axis, keepdims=False)


def product_kernel(core_ref, lhs_ref, rhs_ref, far_ref, near_ref):
    part = lhs_ref.shape[1] // 2
    rhs = rhs_ref[...]
    first = dot_tn(lhs_ref[:, :part], rhs).astype(BF)
    second = dot_tn(lhs_ref[:, part:], rhs).astype(BF)
    core = core_ref[0]

    @pl.when(core == 0)
    def _():
        near_ref[0] = first
        far_ref[0] = second

    @pl.when(core != 0)
    def _():
        near_ref[0] = second
        far_ref[0] = first


def split_product(lhs, rhs, shard, count):
    tokens, width = lhs.shape
    cols = rhs.shape[1]
    part = width // count
    if 2 * part % LANES:
        cut = dot_tn(lhs, rhs).astype(BF).reshape(count // 2, 2, part, cols)
        return take(cut, 1 - shard % 2, 1), take(cut, shard % 2, 1)
    out = jax.ShapeDtypeStruct((count // 2, part, cols), BF)
    out_spec = pl.BlockSpec((1, part, cols), lambda i: (i, 0, 0))
    return pl.pallas_call(
        product_kernel,
        grid=(count // 2,),
        in_specs=[
            pl.BlockSpec(memory_space=pltpu.SMEM),
            pl.BlockSpec((tokens, 2 * part), lambda i: (0, i)),
            pl.BlockSpec((tokens, cols), lambda i: (0, 0)),
        ],
        out_specs=[out_spec, out_spec],
        out_shape=[out, out],
        compiler_params=pltpu.CompilerParams(vmem_limit_bytes=24 * 1024 * 1024),
        cost_estimate=pl.CostEstimate(flops=0, bytes_accessed=0, transcendentals=0),
    )((shard % 2).astype(jnp.int32).reshape(1), lhs, rhs)


def pair_kernel(chip_ref, near_ref, there_ref, own_ref, *part_refs):
    chip = chip_ref[0]
    own_ref[...] = near_ref[chip].astype(F32) + there_ref[chip].astype(F32)
    for m, part_ref in enumerate(part_refs):
        which = chip ^ (m + 1)
        part_ref[...] = (near_ref[which].astype(F32) + there_ref[which].astype(F32)).astype(BF)


def pair_sums(near, there, shard):
    chips, part, cols = near.shape
    tile = math.gcd(cols, 512)
    if tile % LANES:
        tile = cols
    block = pl.BlockSpec((chips, part, tile), lambda i: (0, 0, i))
    out_spec = pl.BlockSpec((part, tile), lambda i: (0, i))
    out = jax.ShapeDtypeStruct((part, cols), BF)
    return pl.pallas_call(
        pair_kernel,
        grid=(cols // tile,),
        in_specs=[pl.BlockSpec(memory_space=pltpu.SMEM), block, block],
        out_specs=[out_spec] * chips,
        out_shape=[jax.ShapeDtypeStruct((part, cols), F32)] + [out] * (chips - 1),
        compiler_params=pltpu.CompilerParams(vmem_limit_bytes=24 * 1024 * 1024),
        cost_estimate=pl.CostEstimate(flops=0, bytes_accessed=0, transcendentals=0),
    )((shard // 2).astype(jnp.int32).reshape(1), near, there)


def fetch_weights(weights_ref, held, sems, piece):
    copies = [
        pltpu.make_async_copy(
            weights_ref.at[:, pl.ds(part * piece, piece)], held.at[part], sems.at[part]
        )
        for part in range(3)
    ]
    return copies


def experts_forward_kernel(count, *refs):
    rows_in, weights_ref = refs[:count], refs[count]
    rows_ref, gate_up_ref, hidden_ref = refs[count + 1 : count + 4]
    out_refs, (held, sems) = refs[count + 4 : -2], refs[-2:]
    piece = hidden_ref.shape[1]
    cap = rows_in[0].shape[0]
    copies = fetch_weights(weights_ref, held, sems, piece)
    for copy in copies:
        copy.start()
    for s in range(count):
        rows_ref[s * cap : (s + 1) * cap, :] = rows_in[s][...]
    rows = rows_ref[...]
    copies[0].wait()
    gate = dot(rows, held[0])
    gate_up_ref[:, :piece] = gate
    copies[1].wait()
    up = dot(rows, held[1])
    gate_up_ref[:, piece:] = up
    hidden = (gate / (1.0 + jnp.exp(-gate)) * up).astype(BF)
    hidden_ref[...] = hidden
    copies[2].wait()
    out = dot_nt(hidden, held[2]).astype(BF)
    for s in range(count):
        out_refs[s][...] = out[s * cap : (s + 1) * cap, :]


def experts_forward(blocks, weights, piece):
    count = len(blocks)
    cap, width = blocks[0].shape
    rows = count * cap
    in_vmem = pl.BlockSpec(memory_space=pltpu.VMEM)
    return pl.pallas_call(
        functools.partial(experts_forward_kernel, count),
        in_specs=[in_vmem] * count + [pl.BlockSpec(memory_space=pltpu.HBM)],
        out_specs=[in_vmem] * (3 + count),
        out_shape=[
            jax.ShapeDtypeStruct((rows, width), BF),
            jax.ShapeDtypeStruct((rows, 2 * piece), F32),
            jax.ShapeDtypeStruct((rows, piece), BF),
        ]
        + [jax.ShapeDtypeStruct((cap, width), BF)] * count,
        scratch_shapes=[pltpu.VMEM((3, width, piece), BF), pltpu.SemaphoreType.DMA((3,))],
        compiler_params=pltpu.CompilerParams(vmem_limit_bytes=56 * 1024 * 1024),
        cost_estimate=pl.CostEstimate(flops=0, bytes_accessed=0, transcendentals=0),
    )(*blocks, weights)


def experts_backward_kernel(count, *refs):
    grads_in, gate_up_ref, weights_ref = refs[:count], refs[count], refs[count + 1]
    grads_ref, rows_ref = refs[count + 2 : count + 4]
    out_refs, (held, sems) = refs[count + 4 : -2], refs[-2:]
    piece = rows_ref.shape[1] // 2
    cap = grads_in[0].shape[0]
    copies = fetch_weights(weights_ref, held, sems, piece)
    for copy in (copies[2], copies[0], copies[1]):
        copy.start()
    for s in range(count):
        grads_ref[s * cap : (s + 1) * cap, :] = grads_in[s][...]
    copies[2].wait()
    grad_hidden = dot(grads_ref[...], held[2])
    gate = gate_up_ref[:, :piece]
    up = gate_up_ref[:, piece:]
    slope = 1.0 / (1.0 + jnp.exp(-gate))
    grad_gate = (grad_hidden * up * slope * (1.0 + gate * (1.0 - slope))).astype(BF)
    grad_up = (grad_hidden * gate * slope).astype(BF)
    rows_ref[:, :piece] = grad_gate
    rows_ref[:, piece:] = grad_up
    copies[0].wait()
    total = dot_nt(grad_gate, held[0])
    copies[1].wait()
    total = (total + dot_nt(grad_up, held[1])).astype(BF)
    for s in range(count):
        out_refs[s][...] = total[s * cap : (s + 1) * cap, :]


def experts_backward(blocks, gate_up, weights, piece):
    count = len(blocks)
    cap, width = blocks[0].shape
    rows = count * cap
    in_vmem = pl.BlockSpec(memory_space=pltpu.VMEM)
    return pl.pallas_call(
        functools.partial(experts_backward_kernel, count),
        in_specs=[in_vmem] * (count + 1) + [pl.BlockSpec(memory_space=pltpu.HBM)],
        out_specs=[in_vmem] * (2 + count),
        out_shape=[
            jax.ShapeDtypeStruct((rows, width), BF),
            jax.ShapeDtypeStruct((rows, 2 * piece), BF),
        ]
        + [jax.ShapeDtypeStruct((cap, width), BF)] * count,
        scratch_shapes=[pltpu.VMEM((3, width, piece), BF), pltpu.SemaphoreType.DMA((3,))],
        compiler_params=pltpu.CompilerParams(vmem_limit_bytes=56 * 1024 * 1024),
        cost_estimate=pl.CostEstimate(flops=0, bytes_accessed=0, transcendentals=0),
    )(*blocks, gate_up, weights)


def kv_pair_kernel(heads, chips, *refs):
    near, there, outs = refs[:heads], refs[heads : 2 * heads], refs[2 * heads :]
    for m in range(chips):
        for g in range(heads):
            total = near[g][m].astype(F32) + there[g][m].astype(F32)
            outs[m][:, g * 2 * HD : (g + 1) * 2 * HD] = total.astype(outs[m].dtype)


def kv_pair_sums(near, there):
    heads, (chips, rows, cols) = len(near), near[0].shape
    in_vmem = pl.BlockSpec(memory_space=pltpu.VMEM)
    out = jax.ShapeDtypeStruct((rows, heads * cols), BF)
    return pl.pallas_call(
        functools.partial(kv_pair_kernel, heads, chips),
        in_specs=[in_vmem] * (2 * heads),
        out_specs=[in_vmem] * chips,
        out_shape=[jax.ShapeDtypeStruct((rows, heads * cols), F32)] + [out] * (chips - 1),
        compiler_params=pltpu.CompilerParams(vmem_limit_bytes=20 * 1024 * 1024),
        cost_estimate=pl.CostEstimate(flops=0, bytes_accessed=0, transcendentals=0),
    )(*near, *there)


def head_columns_kernel(heads, chips, *refs):
    queries, sums = refs[:heads], refs[heads : heads + chips]
    factor_ref, ride_ref, sent_ref, columns_ref = refs[heads + chips :]
    query = jnp.concatenate([each[...] for each in queries], axis=1)
    keyval = sums[0][...]
    for each in sums[1:]:
        keyval = keyval + each[...].astype(F32)
    both = jnp.concatenate([query, keyval], axis=1)
    rows, cols = both.shape
    sent_ref[...] = both.astype(BF)
    columns_ref[:rows, :cols] = (both * factor_ref[...]).astype(BF)
    columns_ref[:rows, cols:] = jnp.zeros((rows, LANES), BF)
    columns_ref[rows:, :cols] = jnp.zeros((ride_ref.shape[0], cols), BF)
    columns_ref[rows:, cols:] = ride_ref[...]


def head_columns(queries, sums, factor, ride):
    rows = sums[0].shape[0]
    cols = sum(each.shape[1] for each in queries) + sums[0].shape[1]
    if cols % LANES:
        both = jnp.concatenate(list(queries) + [total_of(sums)], axis=1)
        scaled = jnp.pad((both * factor).astype(BF), ((0, 0), (0, LANES)))
        return both.astype(BF), jnp.concatenate([scaled, jnp.pad(ride, ((0, 0), (cols, 0)))])
    in_vmem = pl.BlockSpec(memory_space=pltpu.VMEM)
    return pl.pallas_call(
        functools.partial(head_columns_kernel, len(queries), len(sums)),
        in_specs=[in_vmem] * (len(queries) + len(sums) + 2),
        out_specs=[in_vmem] * 2,
        out_shape=[
            jax.ShapeDtypeStruct((rows, cols), BF),
            jax.ShapeDtypeStruct((rows + ride.shape[0], cols + LANES), BF),
        ],
        compiler_params=pltpu.CompilerParams(vmem_limit_bytes=20 * 1024 * 1024),
        cost_estimate=pl.CostEstimate(flops=0, bytes_accessed=0, transcendentals=0),
    )(*queries, *sums, factor, ride)


def two_parts(value):
    high = value.astype(BF)
    return high, (value - high.astype(F32)).astype(BF)


def mark_kernel(seed_ref, out_ref):
    out_ref[...] = seed_ref[...]


def mark(*others):
    seed = after(jnp.zeros((8, LANES), F32), *others)
    return pl.pallas_call(
        mark_kernel,
        out_shape=jax.ShapeDtypeStruct((8, LANES), F32),
        cost_estimate=pl.CostEstimate(flops=10**12, bytes_accessed=8192, transcendentals=0),
    )(seed)


def by_rows(array):
    return with_layout_constraint(array, Layout(major_to_minor=tuple(range(array.ndim))))


def after(values, *others):
    return lax.optimization_barrier((values, others))[0]


def root(values):
    return lax.rsqrt(jnp.mean(values * values, axis=-1, keepdims=True) + EPSILON)


def root_back(values, factor, grad_scaled):
    inner = jnp.mean(grad_scaled * values, axis=-1, keepdims=True)
    return factor * grad_scaled - values * (factor * factor * factor * inner)


def place_gate_up_kernel(count, place_ref, *refs):
    blocks = refs[: 2 * count - 1]
    weight_ref, gain_ref, out_ref, sums_ref, base = refs[2 * count - 1 :]
    offset = place_ref[0] - pl.program_id(1)

    for s in range(2 * count - 1):

        @pl.when(offset == (s if s < count else count - 1 - s))
        def _(s=s):
            base[...] = blocks[s][...].astype(F32)

    @pl.when((pl.program_id(0) == 0) & (pl.program_id(1) == 0))
    def _():
        sums_ref[...] = jnp.zeros_like(sums_ref)

    values = base[...]
    out_ref[0] = values * gain_ref[...]
    product = jnp.sum(weight_ref[0].astype(F32) * values, axis=1, keepdims=True)
    sums_ref[...] += jnp.broadcast_to(product, sums_ref.shape)


def place_gate_up(steps, weight, gain, place):
    experts, part, both = weight.shape
    count = len(steps)
    split = count // experts
    if split == 1:
        tile = math.gcd(both, 1024)
        blocks = [steps[0][0]] + [each[0] for each in steps[1:]] + [each[1] for each in steps[1:]]
        block = pl.BlockSpec((part, tile), lambda t, e: (0, t))
        out, sums = pl.pallas_call(
            functools.partial(place_gate_up_kernel, count),
            grid=(both // tile, experts),
            in_specs=[pl.BlockSpec(memory_space=pltpu.SMEM)]
            + [block] * len(blocks)
            + [
                pl.BlockSpec((1, part, tile), lambda t, e: (e, 0, t)),
                pl.BlockSpec((part, 1), lambda t, e: (0, 0)),
            ],
            out_specs=[
                pl.BlockSpec((1, part, tile), lambda t, e: (e, 0, t)),
                pl.BlockSpec((part, LANES), lambda t, e: (0, 0)),
            ],
            out_shape=[
                jax.ShapeDtypeStruct(weight.shape, F32),
                jax.ShapeDtypeStruct((part, LANES), F32),
            ],
            scratch_shapes=[pltpu.VMEM((part, tile), F32)],
            compiler_params=pltpu.CompilerParams(vmem_limit_bytes=28 * 1024 * 1024),
            cost_estimate=pl.CostEstimate(flops=0, bytes_accessed=0, transcendentals=0),
        )(place.astype(jnp.int32).reshape(1), *blocks, weight, gain)
        return out, sums[:, 0]
    blocks = [steps[0][0]] + [
        jnp.where(place >= s, steps[s][0], steps[count - s][1]) for s in range(1, count)
    ]
    base = (
        from_relative(blocks, place)
        .reshape(experts, split, part, 2, both // (2 * split))
        .transpose(0, 2, 3, 1, 4)
        .reshape(experts, part, both)
        .astype(F32)
    )
    return base * gain, jnp.sum(weight.astype(F32) * base, axis=(0, 2))


def place_kernel(count, q_cols, kv_cols, place_ref, *refs):
    blocks, outs = refs[:count], refs[count : 2 * count]
    w_query_ref, w_keyval_ref, gain_ref, query_ref, keyval_ref, out_ref, base_ref, sums_ref = refs[
        2 * count :
    ]
    gain = gain_ref[...]
    base = jnp.zeros_like(gain)
    sums = jnp.zeros(sums_ref.shape, F32)
    for s in range(count):
        owner = lax.rem(place_ref[0] + (count - s), count)
        q_at = pl.ds(pl.multiple_of(owner * q_cols, LANES), q_cols)
        kv_at = pl.ds(pl.multiple_of(owner * kv_cols, LANES), kv_cols)
        query = blocks[s][:, :q_cols].astype(F32)
        keyval = blocks[s][:, q_cols : q_cols + kv_cols].astype(F32)
        start = q_cols + kv_cols
        sums = sums + blocks[s][:, start : start + LANES].astype(F32)
        out_ref[:, q_at] = outs[s][...].astype(F32)
        base = base + jnp.sum(w_query_ref[:, q_at].astype(F32) * query, axis=1, keepdims=True)
        base = base + jnp.sum(w_keyval_ref[:, kv_at].astype(F32) * keyval, axis=1, keepdims=True)
        query_ref[:, q_at] = query * gain
        keyval_ref[:, kv_at] = keyval * gain
    base_ref[...] = jnp.broadcast_to(base, base_ref.shape)
    sums_ref[...] = sums


def place_heads(blocks, outs, place, w_query, w_keyval, gain, q_cols, kv_cols):
    count = len(blocks)
    part = w_query.shape[0]
    start = q_cols + kv_cols
    if q_cols % LANES == 0 and kv_cols % LANES == 0:
        wide = jax.ShapeDtypeStruct((part, count * q_cols), F32)
        narrow = jax.ShapeDtypeStruct((part, count * kv_cols), F32)
        lanes = jax.ShapeDtypeStruct((part, LANES), F32)
        in_vmem = pl.BlockSpec(memory_space=pltpu.VMEM)
        query, keyval, out, base, sums = pl.pallas_call(
            functools.partial(place_kernel, count, q_cols, kv_cols),
            in_specs=[pl.BlockSpec(memory_space=pltpu.SMEM)] + [in_vmem] * (2 * count + 3),
            out_specs=[in_vmem] * 5,
            out_shape=[wide, narrow, wide, lanes, lanes],
            compiler_params=pltpu.CompilerParams(vmem_limit_bytes=24 * 1024 * 1024),
            cost_estimate=pl.CostEstimate(flops=0, bytes_accessed=0, transcendentals=0),
        )(place.astype(jnp.int32).reshape(1), *blocks, *outs, w_query, w_keyval, gain)
        return query, keyval, out, base[:, 0], sums
    blocks = from_relative(blocks, place).astype(F32)
    outs = from_relative(outs, place).astype(F32)

    def columns(begin, end):
        return blocks[:, :, begin:end].transpose(1, 0, 2).reshape(part, count * (end - begin))

    query, keyval = columns(0, q_cols), columns(q_cols, start)
    base = jnp.sum(w_query.astype(F32) * query, axis=1) + jnp.sum(
        w_keyval.astype(F32) * keyval, axis=1
    )
    sums = jnp.sum(blocks[:, :, start : start + LANES], axis=0)
    out = outs.transpose(1, 0, 2).reshape(part, count * q_cols)
    return query * gain, keyval * gain, out, base, sums


def local(
    tokens,
    teacher,
    valid,
    routes,
    slots,
    gain_attn,
    w_query,
    w_keyval,
    w_out,
    gain_ffn,
    w_router,
    w_gate_up,
    w_down,
):
    seqs = lax.axis_size("seq")
    shards = lax.axis_size("fsdp")
    z = lax.axis_index("seq")
    shard = lax.axis_index("fsdp")
    rows, width = tokens.shape
    groups = HEADS // KVH
    local_kv = KVH // seqs
    q_cols = local_kv * groups * HD
    kv_cols = local_kv * 2 * HD
    local_rows = rows * seqs
    seq_len = local_rows * shards
    experts, part, both = w_gate_up.shape
    units = both // 2
    split = seqs // experts
    piece = units // split
    expert = z // split
    fraction = z % split
    scale = HD ** (-0.5)

    gain_one = gain_attn.astype(F32)[:, None]
    gain_two = gain_ffn.astype(F32)[:, None]
    heads_shard = jnp.concatenate(
        [
            lax.dynamic_slice_in_dim(w_query, z * q_cols, q_cols, 1),
            lax.dynamic_slice_in_dim(w_keyval, z * kv_cols, kv_cols, 1),
        ],
        axis=1,
    )
    heads_shard = (heads_shard.astype(F32) * gain_one).astype(BF)
    heads_full = lax.all_gather(heads_shard, "fsdp", axis=0, tiled=True)
    valid_row = jnp.pad(valid.astype(BF).reshape(1, rows), ((0, 7), (0, width - rows)))
    token_rows = jnp.concatenate([tokens, valid_row], axis=0)
    token_mark = mark(token_rows)
    token_blocks = after(send_out([token_rows] * seqs, seqs), token_mark)

    valid_local = from_relative([each[rows : rows + 1, :rows] for each in token_blocks], z)
    projected = []
    for block in token_blocks:
        projected.append(dot(block[:rows], heads_full) * root(block[:rows].astype(F32)))
    projected = from_relative([each.astype(BF) for each in projected], z)
    projected = projected.reshape(local_rows, q_cols + kv_cols)
    head_queries = projected[:, :q_cols] * jnp.asarray(scale, BF)

    valid_rows_kv = local_rows // kv_cols
    payload = jnp.concatenate(
        [
            projected[:, q_cols:],
            valid_local.reshape(valid_rows_kv, kv_cols),
            jnp.zeros((16 - valid_rows_kv, kv_cols), BF),
        ],
        axis=0,
    )
    kv_blocks = gather_shards(payload, shards)
    late_query, late_keyval, late_router, late_gate_up, late_down = after(
        (w_query, w_keyval, w_router, w_gate_up, w_down), token_mark
    )
    out_full = lax.all_gather(w_out, "fsdp", axis=1, tiled=True)
    own_expert = take(late_gate_up, expert, 0)
    gate_shard = lax.dynamic_slice_in_dim(own_expert, fraction * piece, piece, 1)
    up_shard = lax.dynamic_slice_in_dim(own_expert, units + fraction * piece, piece, 1)
    down_shard = lax.dynamic_slice_in_dim(take(late_down, expert, 0), fraction * piece, piece, 0).T
    router_shard = jnp.pad((late_router.astype(F32) * gain_two).astype(BF), ((0, 0), (0, LANES - experts)))
    expert_shard = jnp.concatenate(
        [
            (gate_shard.astype(F32) * gain_two).astype(BF),
            (up_shard.astype(F32) * gain_two).astype(BF),
            down_shard,
            router_shard,
        ],
        axis=1,
    )
    expert_full = lax.all_gather(expert_shard, "fsdp", axis=0, tiled=True)
    router_full = expert_full[:, 3 * piece :]
    attn_shard = jnp.concatenate(
        [
            each
            for s in range(seqs)
            for each in (
                late_query[:, s * q_cols : (s + 1) * q_cols],
                late_keyval[:, s * kv_cols : (s + 1) * kv_cols],
            )
        ],
        axis=1,
    )
    attn_full = lax.all_gather(
        (attn_shard.astype(F32) * gain_one).astype(BF), "fsdp", axis=0, tiled=True
    )
    order = jnp.asarray(
        [2 * m for m in range(shards // 2)] + [2 * m + 1 for m in range(shards // 2)], jnp.int32
    )
    valid_all = jnp.stack(
        [
            each[local_rows : local_rows + valid_rows_kv].reshape(seqs, rows)
            for each in kv_blocks
        ],
        axis=1,
    ).astype(F32)
    valid_count = jnp.sum(valid_all)
    bias = jnp.where(valid_all > 0, 0.0, FLOOR_SCORE)
    earlier = ((order ^ shard) < shard) | (order == 0)
    bias_same = jnp.where(earlier[None, :, None], bias, FLOOR_SCORE)
    bias = jnp.concatenate([bias, bias_same]).reshape(2 * seqs, 1, shards * rows)
    attended_low, lse = flash_forward(
        head_queries, kv_blocks, bias, seqs, rows, local_kv, groups
    )
    attended = lax.all_to_all(attended_low, "seq", split_axis=0, concat_axis=1, tiled=True)

    inputs = tokens.astype(F32)
    residual = inputs + dot(attended, out_full)
    factor_two = root(residual)
    normed_two = (residual * factor_two).astype(BF)
    logits = dot(normed_two, router_full)[:, :experts]
    expert_ids = jnp.arange(experts, dtype=jnp.int32)
    picked = (routes[:, :, None] == expert_ids).astype(F32)
    chosen = jnp.sum(picked * logits[:, None, :], axis=-1)
    gating = jax.nn.softmax(chosen, axis=-1)
    owners = ((jnp.arange(seqs, dtype=jnp.int32) + z) % seqs) // split
    to_owner = routes[:, :, None] == owners
    slot_hot = slots[:, :, None] == jnp.arange(CAP, dtype=jnp.int32)
    placed = (to_owner[:, :, :, None] & slot_hot[:, :, None, :]).astype(BF)
    placed = placed.reshape(rows, 2, seqs * CAP)
    dispatch = placed[:, 0] + placed[:, 1]
    placed_pairs = jnp.concatenate([placed[:, 0], placed[:, 1]], axis=0)
    sent_rows = dot_tn(dispatch, normed_two).astype(BF)
    kv_all = jnp.stack(after(kv_blocks, sent_rows))
    sent_rows = sent_rows.reshape(seqs, CAP, width)
    expert_rows, gate_up, hidden, *expert_out = experts_forward(
        send_out([sent_rows[s] for s in range(seqs)], seqs), expert_full, piece
    )
    returned = jnp.concatenate(after(send_back(expert_out, seqs), kv_all))
    selected = dot(placed_pairs, returned).reshape(2, rows, width)
    mixed_exact = residual + gating[:, :1] * selected[0] + gating[:, 1:] * selected[1]
    valid_rows = valid.astype(F32)
    errors = (mixed_exact - teacher.astype(F32)) * valid_rows[:, None]
    squares = jnp.sum(errors * errors)
    loss_scale = width * seq_len // 8
    grad_mixed = errors * (2.0 * loss_scale / (width * valid_count))

    grad_gating = jnp.stack(
        [jnp.sum(selected[0] * grad_mixed, axis=-1), jnp.sum(selected[1] * grad_mixed, axis=-1)],
        axis=1,
    )
    grad_chosen = gating * (grad_gating - jnp.sum(gating * grad_gating, axis=-1, keepdims=True))
    grad_logits = jnp.sum(grad_chosen[:, :, None] * picked, axis=1).astype(BF)
    grad_logits = jnp.pad(grad_logits, ((0, 0), (0, LANES - experts)))
    weighted = jnp.concatenate(
        [(gating[:, :1] * grad_mixed).astype(BF), (gating[:, 1:] * grad_mixed).astype(BF)], axis=0
    )
    sent_grads = dot_tn(placed_pairs, weighted).astype(BF).reshape(seqs, CAP, width)
    grad_out_rows = send_out([sent_grads[s] for s in range(seqs)], seqs)
    grad_out_rows = after(grad_out_rows, attn_full, grad_logits)
    grad_expert_out, grad_gate_up_rows, *grad_rows = experts_backward(
        grad_out_rows, gate_up, expert_full, piece
    )
    grad_returned = send_back(grad_rows, seqs)
    tokens_local = from_relative(
        [each[:rows] for each in after(token_blocks, grad_rows)], z
    ).reshape(local_rows, width)
    factor_local = root(tokens_local.astype(F32))
    ride_rows = jnp.concatenate([normed_two, jnp.ones((16, width), BF)], axis=0)
    product_rows = jnp.concatenate([tokens_local, ride_rows], axis=0)
    high, low = two_parts(squares)
    lane = jnp.arange(LANES, dtype=jnp.int32)[None, :]
    marks = jnp.where(lane == experts + 2 * (shard % 2), high, 0) + jnp.where(
        lane == experts + 1 + 2 * (shard % 2), low, 0
    )
    ride_columns = jnp.concatenate(
        [grad_logits, marks.astype(BF), jnp.zeros((15, LANES), BF)], axis=0
    )
    held_out, held_hidden = after((grad_expert_out, hidden), grad_rows)
    down_far, down_near = split_product(held_out, held_hidden, shard, shards)
    grad_down_sums = pair_sums(down_near, hop(down_far, shards, 1), shard)
    held_rows, held_gate_up = after((expert_rows, grad_gate_up_rows), grad_rows)
    gate_up_far, gate_up_near = split_product(held_rows, held_gate_up, shard, shards)
    grad_gate_up_sums = pair_sums(gate_up_near, hop(gate_up_far, shards, 1), shard)
    grad_down_blocks = send_chips(grad_down_sums, shards)
    grad_returned = jnp.concatenate(after(grad_returned, grad_down_sums, product_rows, ride_columns, factor_local))
    grad_normed_two = dot(dispatch, grad_returned) + dot_nt(grad_logits, router_full)
    grad_residual = grad_mixed + root_back(residual, factor_two, grad_normed_two)
    grad_branch = grad_residual.astype(BF)
    grad_attended = dot_nt(after(grad_branch, grad_gate_up_sums), out_full).astype(BF)
    head_grad = lax.all_to_all(grad_attended, "seq", split_axis=1, concat_axis=0, tiled=True)
    grad_gate_up_blocks = send_chips(grad_gate_up_sums, shards)
    grad_down_shard = total_of(after(grad_down_blocks, grad_attended)).astype(BF)
    grad_down = lax.all_gather(grad_down_shard, "seq", axis=0, tiled=False)

    out_far, out_near = split_product(
        after(grad_branch, grad_attended), attended, shard, shards
    )
    grad_q, near, far = [], [], []
    held = after(head_grad, grad_down_shard)
    for g in range(local_kv):
        part_q, near_kv, far_kv = flash_backward(
            head_queries, kv_all, bias, held, attended_low, lse, seqs, rows, g, groups
        )
        if g == 0:
            grad_gate_up_blocks = after(grad_gate_up_blocks, part_q)
            grad_gate_up_shard = total_of(grad_gate_up_blocks).astype(BF)
            steps = [(grad_gate_up_shard, grad_gate_up_shard)]
            steps.append(relay_step(steps[0], seqs))
            out_there = hop(after(out_far, head_grad), shards, 1)
        grad_q.append(part_q)
        near.append(near_kv)
        far.append(far_kv)
        held = after(head_grad, grad_gate_up_shard, out_there)
    steps[1] = after(steps[1], part_q)
    steps.append(relay_step(steps[1], seqs))
    far = after(far, grad_down)
    pairs = kv_pair_sums(near, [hop(each, shards, 1) for each in far])
    out_sums = pair_sums(out_near, after(out_there, pairs), shard)
    sent_grads, product_columns = head_columns(
        grad_q, after(send_chips(pairs, shards), out_sums, steps[2]), factor_local, ride_columns
    )
    steps[2] = after(steps[2], product_columns)
    while len(steps) < seqs:
        steps.append(relay_step(steps[-1], seqs))
    token_grads = lax.all_to_all(sent_grads, "seq", split_axis=0, concat_axis=1, tiled=True)

    head_cols = q_cols + kv_cols
    head_far, head_near = split_product(product_rows, product_columns, shard, shards)
    head_sums = pair_sums(head_near, hop(head_far, shards, 1), shard)
    head_blocks = send_chips(head_sums, shards)
    head_part = total_of(after(head_blocks, steps[3]))
    grad_normed = dot_nt(after(token_grads, head_part), attn_full)
    grad_tokens = grad_residual + root_back(inputs, root(inputs), grad_normed)
    base_cols = head_cols + experts
    plane_high, plane_low = two_parts(
        jnp.sum(head_part[:1, base_cols : base_cols + 4], axis=1, keepdims=True)
    )
    lanes = lax.broadcasted_iota(jnp.int32, head_part.shape, 1)
    head_part = jnp.where(
        lanes == base_cols,
        plane_high.astype(F32),
        jnp.where(lanes == base_cols + 1, plane_low.astype(F32), head_part),
    )
    head_part = by_rows(head_part.astype(BF))
    head_last = [by_rows(each) for each in send_out([head_part] * seqs, seqs)]
    out_blocks = send_chips(after(out_sums, head_part), shards)
    out_part = total_of(out_blocks).astype(BF)
    out_parts = lax.all_to_all(
        out_part.reshape(part, seqs, q_cols), "seq", split_axis=1, concat_axis=1, tiled=True
    )
    out_own = by_rows(jnp.sum(out_parts.astype(F32), axis=1).astype(BF))
    grad_gate_up, grad_gain_ffn = place_gate_up(after(steps, head_part), w_gate_up, gain_two, z)
    out_own = after(out_own, grad_gate_up)
    out_last = [by_rows(each) for each in send_out([out_own] * seqs, seqs)]
    grad_query, grad_keyval, grad_out, grad_gain_attn, sums = place_heads(
        head_last, out_last, z, w_query, w_keyval, gain_one, q_cols, kv_cols
    )
    loss_value = jnp.sum(sums[0, experts : experts + 2]) / (width * valid_count)
    grad_router_base = sums[:, :experts]
    grad_down = (
        after(grad_down, head_part).reshape(experts, split, part, piece)
        .transpose(0, 1, 3, 2)
        .reshape(experts, units, part)
        .astype(F32)
    )
    grad_gain_ffn = grad_gain_ffn + jnp.sum(w_router.astype(F32) * grad_router_base, axis=1)
    return (
        mixed_exact.astype(BF),
        loss_value,
        grad_tokens,
        grad_gain_attn,
        grad_query,
        grad_keyval,
        grad_out.T,
        grad_gain_ffn,
        grad_router_base * gain_two,
        grad_gate_up,
        grad_down,
    )


def solution(mesh):
    return jax.shard_map(
        local,
        mesh=mesh,
        in_specs=(
            P(("seq", "fsdp"), None),
            P(("seq", "fsdp"), None),
            P(("seq", "fsdp")),
            P(("seq", "fsdp"), None),
            P(("seq", "fsdp"), None),
            P("fsdp"),
            P("fsdp", None),
            P("fsdp", None),
            P(None, "fsdp"),
            P("fsdp"),
            P("fsdp", None),
            P(None, "fsdp", None),
            P(None, None, "fsdp"),
        ),
        out_specs=(
            P(("seq", "fsdp"), None),
            P(),
            P(("seq", "fsdp"), None),
            P("fsdp"),
            P("fsdp", None),
            P("fsdp", None),
            P(None, "fsdp"),
            P("fsdp"),
            P("fsdp", None),
            P(None, "fsdp", None),
            P(None, None, "fsdp"),
        ),
        check_vma=False,
    )
```
